32 devices in a mesh: fsdp: 16 (over z, y, core), tp: 2 (over x).
Axes of the slice: x: 2, y: 2, z: 4, core: 2. Of those that a mesh axis runs over, the one named last changes fastest.
Arguments:
- tokens: bfloat16 [4096, 2048], P(('fsdp', 'tp')), may hold values from -6 to 6
- lengths: int32 [16, 4], P('fsdp'), may hold values from 1 to 192, 256 in all within a row
- routes: int32 [4096, 8], P('fsdp'), may hold values from 0 to 15, all different within a row; in each aligned block of 256 rows (0 to 255, 256 to 511, ...) at most 192 rows name the same one
- deal_order: int32 [16], replicated, may hold values from 0 to 15, each once
- cotangent: bfloat16 [4096, 2048], P(('fsdp', 'tp')), may hold values from -6 to 6
- attn_gain: float32 [2048], replicated, may hold values from 0.1 to 1.9
- query_gain: float32 [128], replicated, may hold values from 0.1 to 1.9
- key_gain: float32 [128], replicated, may hold values from 0.1 to 1.9
- moe_gain: float32 [2048], replicated, may hold values from 0.1 to 1.9
- w_query: bfloat16 [2048, 4096], P('fsdp', 'tp'), may hold values from -0.125 to 0.125
- key_projection_matrix: bfloat16 [2048, 512], P('fsdp', 'tp'), may hold values from -0.125 to 0.125
- value_projection_matrix: bfloat16 [2048, 512], P('fsdp', 'tp'), may hold values from -0.125 to 0.125
- w_out: bfloat16 [4096, 2048], P('tp', 'fsdp'), may hold values from -0.5 to 0.5
- w_router: bfloat16 [2048, 16], replicated, may hold values from -0.0625 to 0.0625
- w_gate: bfloat16 [16, 2048, 768], P('fsdp', None, 'tp'), may hold values from -0.125 to 0.125
- w_up: bfloat16 [16, 2048, 768], P('fsdp', None, 'tp'), may hold values from -0.125 to 0.125
- w_down: bfloat16 [16, 768, 2048], P('fsdp', 'tp'), may hold values from -0.625 to 0.625
Outputs:
- output: bfloat16 [4096, 2048], P(('fsdp', 'tp'))
- grad_input: float32 [4096, 2048], P(('fsdp', 'tp'))
- grad_attn_gain: float32 [2048], replicated
- grad_query_gain: float32 [128], replicated
- grad_key_gain: float32 [128], replicated
- grad_moe_gain: float32 [2048], replicated
- grad_w_query: float32 [2048, 4096], P('fsdp', 'tp')
- grad_w_key: float32 [2048, 512], P('fsdp', 'tp')
- grad_w_value: float32 [2048, 512], P('fsdp', 'tp')
- grad_w_out: float32 [4096, 2048], P('tp', 'fsdp')
- grad_w_router: float32 [2048, 16], replicated
- grad_w_gate: float32 [16, 2048, 768], P('fsdp', None, 'tp')
- grad_w_up: float32 [16, 2048, 768], P('fsdp', None, 'tp')
- grad_w_down: float32 [16, 768, 2048], P('fsdp', 'tp')
The draws below stay inside these ranges and needn't reach their ends.
Inputs may be any that keep to these rules, and one draw needn't show every extreme that they name: `routes`: each row names 8 different experts; within the 256 rows of one token group no expert is named more than 192 times, and in every draw some expert of some group exactly 192 times. Row j lists the lengths of the 4 sequences of token group j in order; each row sums to 256 and its largest entry is exactly 192. `deal_order`: each number appears once.
All inputs are finite; a program needn't handle non-finite values.
Results may differ from the reference program's by a relative error of at most 0.018.
Values may be sent and summed in bfloat16 or wider, within the bound.
A program may use at most 256 MiB of HBM per device.

```python
import math
import jax
import jax.numpy as jnp
import numpy as np
from jax import lax

MODEL_DIMENSION = 2048
QUERY_HEADS = 32
KEY_VALUE_HEADS = 4
HEAD_SIZE = 128
FF = 768
TOPK = 8
SEQ_DEV = 4
GROUP_TOKENS = 256
MAXLEN = 192
TOKENS = 4096
EXPERTS = 16
CAP = 192
N_FSDP = 16
N_TP = 2


def shard_levels(own_key, dims, shards, least, high):
    gain, own = 1.0, jax.random.fold_in(own_key, 6)
    for dim, parts in shards:
        heights = jnp.exp(jax.random.uniform(jax.random.fold_in(own, dim), (parts,), jnp.float32, least / len(shards), high / len(shards)))
        gain = gain * jnp.repeat(heights, dims[dim] // parts).reshape([-1 if axis == dim else 1 for axis in range(len(dims))])
    return gain


def length_profile(count, total, most, lean):
    weights = [(1 << 20) // math.isqrt(grade ** lean) + 1 for grade in range(2, count + 1)]
    spare, holding = total - most - (count - 1), [1] * (count - 1)
    while spare > 0:
        movable = [i for i in range(count - 1) if holding[i] < most]
        mass, left = sum([weights[i] for i in movable]), spare
        for i in movable:
            more = min(most - holding[i], max(1, left * weights[i] // mass), spare)
            holding[i] = holding[i] + more
            spare = spare - more
    return np.array([most] + holding)


def uneven(stream_key, count, total, limit, slope):
    if count == 2:
        one = jax.random.randint(stream_key, (), max(1, total - limit), min(limit, total - 1) + 1)
        return jnp.stack([one, total - one])
    sizes = jnp.asarray(length_profile(count, total, limit, slope), jnp.int32)
    couples = (count - 1) // 2
    source_of, taker = sizes[1:1 + 2 * couples:2], sizes[2:2 + 2 * couples:2]
    room = jnp.minimum(source_of - 1, limit - taker)
    passed = jax.random.randint(jax.random.fold_in(stream_key, 1), (couples,), 0, 1 << 20) % (room + 1)
    sizes = sizes.at[1:1 + 2 * couples:2].set(source_of - passed).at[2:2 + 2 * couples:2].set(taker + passed)
    return sizes[jax.random.permutation(jax.random.fold_in(stream_key, 2), count)]


def assign_block(own_key, own, number, rows, amount, top, reach, lean):
    order = jax.random.permutation(own_key, amount)
    crowded, common = shares(amount, rows * top, reach, lean, True), shares(amount, rows * top, reach, lean, False)
    places = jnp.arange(amount)

    def named(sizes, rotation):
        used = int((sizes > 0).sum())
        fixed = max(1, used // 4)
        passed = fixed + (places - fixed + rotation * (used - fixed)) % max(1, amount - fixed)
        return jnp.zeros((amount,), jnp.int32).at[order[jnp.where(places < fixed, places, passed)]].set(jnp.asarray(sizes, jnp.int32))

    sizes = jnp.where(number % 4 == 0, named(crowded, number // 4), named(common, number - number // 4 - 1))
    mixed = jax.random.permutation(jax.random.fold_in(own, 3), amount)
    source_of, sink = mixed[0:amount // 2 * 2:2], mixed[1:amount // 2 * 2:2]
    margin = jnp.minimum(sizes[source_of] - 1, reach - sizes[sink]) // 2
    margin = jnp.where((source_of == order[0]) | (sink == order[0]) | (sizes[sink] == 0), 0, jnp.maximum(margin, 0))
    passed = jax.random.randint(jax.random.fold_in(own, 4), (amount // 2,), 0, 1 << 20) % (margin + 1)
    sizes = sizes.at[source_of].add(-passed).at[sink].add(passed)
    labels = jnp.searchsorted(jnp.cumsum(sizes), jnp.arange(rows * top), side="right").astype(jnp.int32)
    listing = labels.reshape(top, rows).T
    listing = listing[jax.random.permutation(jax.random.fold_in(own, 1), rows)]
    rotation = jax.random.randint(jax.random.fold_in(own, 2), (rows, 1), 0, top)
    return jnp.take_along_axis(listing, (jnp.arange(top)[None, :] + rotation) % top, axis=1)


def shares(number_of, total, limit, skew, full):
    weights = [(1 << 20) // math.isqrt(standing ** skew) + 1 for standing in range(1, number_of + 1)]
    largest = limit if full else min(limit, max(-(-total // number_of), total * weights[0] // sum(weights)))
    least = 1 if total - largest >= number_of - 1 else 0
    counts, spare = [largest] + [least] * (number_of - 1), total - largest - least * (number_of - 1)
    while spare > 0:
        candidates = [i for i in range(1, number_of) if counts[i] < largest] or [i for i in range(1, number_of) if counts[i] < limit]
        pool, left = sum([weights[i] for i in candidates]), spare
        for i in candidates:
            extra = min(limit - counts[i], max(1, left * weights[i] // pool), spare)
            counts[i] = counts[i] + extra
            spare = spare - extra
    return np.array(counts)


def bell_draw(stream_key, dims, width, most, shards=(), held_as=jnp.bfloat16):
    loudness = shard_levels(stream_key, dims, shards, -0.22, 0.18) if shards else 1.0
    drawn = jax.random.normal(stream_key, dims, jnp.float32) * width * loudness
    return jnp.minimum(jnp.maximum(drawn, -most), most).astype(held_as)


def setup_inputs(seed: int = 0) -> dict:
    arg_keys = jax.random.split(jax.random.key(seed), 18)
    tokens = bell_draw(arg_keys[0], (TOKENS, MODEL_DIMENSION), 1.0, 6.0, ((0, 32),))
    lengths = jax.vmap(lambda own: uneven(own, SEQ_DEV, GROUP_TOKENS, MAXLEN, 1))(jax.random.split(arg_keys[1], N_FSDP)).reshape((N_FSDP, SEQ_DEV)).astype(jnp.int32)
    routes_keys = jax.random.split(jax.random.fold_in(arg_keys[2], 1), TOKENS // GROUP_TOKENS)
    routes_turns = jax.random.permutation(jax.random.fold_in(arg_keys[2], 3), TOKENS // GROUP_TOKENS)
    routes = jax.vmap(lambda own, number: assign_block(jax.random.fold_in(arg_keys[2], 2), own, number, GROUP_TOKENS, EXPERTS, TOPK, CAP, 1))(routes_keys, routes_turns).reshape((TOKENS, TOPK))
    deal_order = jax.random.permutation(arg_keys[3], N_FSDP).astype(jnp.int32)
    cotangent = bell_draw(arg_keys[4], (TOKENS, MODEL_DIMENSION), 1.0, 6.0, ((0, 32),))
    attn_gain = jnp.clip(1.0 + 0.18 * jax.random.normal(arg_keys[5], (MODEL_DIMENSION,), jnp.float32), 0.1, 1.9)
    query_gain = jnp.clip(1.0 + 0.18 * jax.random.normal(arg_keys[6], (HEAD_SIZE,), jnp.float32), 0.1, 1.9)
    key_gain = jnp.clip(1.0 + 0.18 * jax.random.normal(arg_keys[7], (HEAD_SIZE,), jnp.float32), 0.1, 1.9)
    moe_gain = jnp.clip(1.0 + 0.18 * jax.random.normal(arg_keys[8], (MODEL_DIMENSION,), jnp.float32), 0.1, 1.9)
    w_query = bell_draw(arg_keys[9], (MODEL_DIMENSION, QUERY_HEADS * HEAD_SIZE), MODEL_DIMENSION ** -0.5, 0.125, ((0, 16), (1, 2)))
    key_projection_matrix = bell_draw(arg_keys[10], (MODEL_DIMENSION, KEY_VALUE_HEADS * HEAD_SIZE), MODEL_DIMENSION ** -0.5, 0.125, ((0, 16), (1, 2)))
    value_projection_matrix = bell_draw(arg_keys[11], (MODEL_DIMENSION, KEY_VALUE_HEADS * HEAD_SIZE), MODEL_DIMENSION ** -0.5, 0.125, ((0, 16), (1, 2)))
    w_out = bell_draw(arg_keys[12], (QUERY_HEADS * HEAD_SIZE, MODEL_DIMENSION), (QUERY_HEADS * HEAD_SIZE // 32) ** -0.5, 0.5, ((0, 2), (1, 16)))
    w_router = bell_draw(arg_keys[13], (MODEL_DIMENSION, EXPERTS), (4 * MODEL_DIMENSION) ** -0.5, 0.0625)
    w_gate = bell_draw(arg_keys[14], (EXPERTS, MODEL_DIMENSION, FF), MODEL_DIMENSION ** -0.5, 0.125, ((0, 16), (2, 2)))
    w_up = bell_draw(arg_keys[15], (EXPERTS, MODEL_DIMENSION, FF), MODEL_DIMENSION ** -0.5, 0.125, ((0, 16), (2, 2)))
    w_down = bell_draw(arg_keys[16], (EXPERTS, FF, MODEL_DIMENSION), (FF // 8) ** -0.5, 0.625, ((0, 16), (1, 2)))
    return {"tokens": tokens, "lengths": lengths, "routes": routes, "deal_order": deal_order, "cotangent": cotangent, "attn_gain": attn_gain, "query_gain": query_gain, "key_gain": key_gain, "moe_gain": moe_gain, "w_query": w_query, "key_projection_matrix": key_projection_matrix, "value_projection_matrix": value_projection_matrix, "w_out": w_out, "w_router": w_router, "w_gate": w_gate, "w_up": w_up, "w_down": w_down}


epsilon = 1e-06
rope_base = 1000000.0
masked_score = -1e+30
highest_precision = lax.Precision.HIGHEST

@jax.custom_vjp
def lower_precision(v):
    return lax.optimization_barrier(v.astype(jnp.bfloat16)).astype(jnp.float32)

@jax.custom_vjp
def lower_back_cast(v):
    return v

def low_keep(v):
    return (lower_precision(v), None)

def low_pass(kept, grad):
    return (grad,)

def back_keep(v):
    return (v, None)

def back_low(kept, grad):
    return (lower_precision(grad),)
lower_precision.defvjp(low_keep, low_pass)
lower_back_cast.defvjp(back_keep, back_low)

def row_norm(values, gain_vec):
    return values * lax.rsqrt(lax.optimization_barrier(jnp.mean(values * values, axis=-1, keepdims=True)) + epsilon) * gain_vec

def deal_layout(deal_order):
    half_rows = GROUP_TOKENS // N_TP
    slice_rows = half_rows // N_FSDP
    peer_ids = jnp.arange(N_FSDP, dtype=jnp.int32)
    inverse_deal = jnp.zeros((N_FSDP,), jnp.int32).at[deal_order.astype(jnp.int32)].set(peer_ids)
    row_ids = jnp.arange(TOKENS, dtype=jnp.int32)
    group_id = (row_ids // GROUP_TOKENS).astype(jnp.int32)
    within = (row_ids % GROUP_TOKENS).astype(jnp.int32)
    half_id = (within // half_rows).astype(jnp.int32)
    inner_row = (within % half_rows).astype(jnp.int32)
    source = (inner_row // slice_rows).astype(jnp.int32)
    offset = (inner_row % slice_rows).astype(jnp.int32)
    slice_id = inverse_deal[((group_id - source) % N_FSDP).astype(jnp.int32)].astype(jnp.int32)
    input_order = ((source * N_TP + half_id) * half_rows + slice_id * slice_rows + offset).astype(jnp.int32)
    back_order = jnp.zeros((TOKENS,), jnp.int32).at[input_order].set(row_ids)
    return (input_order, back_order)

def seq_layout(seq_lengths, row_count):
    seq_ends = jnp.cumsum(seq_lengths).astype(jnp.int32)
    row_ids = jnp.arange(row_count, dtype=jnp.int32)
    segment = lax.optimization_barrier(jnp.sum((row_ids[:, None] >= seq_ends[None, :]).astype(jnp.int32), axis=1)).astype(jnp.int32)
    seq_starts = (seq_ends - seq_lengths).astype(jnp.int32)
    chosen = segment[:, None] == jnp.arange(seq_lengths.shape[0], dtype=jnp.int32)[None, :]
    position = (row_ids - lax.optimization_barrier(jnp.sum(jnp.where(chosen, seq_starts[None, :], 0), axis=1))).astype(jnp.int32)
    return (segment, position)

def rotary(position, head_width):
    half_width = head_width // 2
    inverse_freq = rope_base ** (-(jnp.arange(half_width, dtype=jnp.float32) * (2.0 / head_width)))
    angles = position.astype(jnp.float32)[:, None] * inverse_freq[None, :]
    return (jnp.cos(angles)[:, None, :], jnp.sin(angles)[:, None, :])

def rotate(values, cosine_table, sine_table):
    half_width = values.shape[-1] // 2
    front_half = values[..., :half_width]
    back_half = values[..., half_width:]
    return jnp.concatenate([front_half * cosine_table - back_half * sine_table, back_half * cosine_table + front_half * sine_table], axis=-1)

def slot_table(route_rows, expert_count, capacity):
    row_count = route_rows.shape[0] * route_rows.shape[1]
    flat_routes = route_rows.reshape(row_count).astype(jnp.int32)
    expert_hits = (flat_routes[:, None] == jnp.arange(expert_count, dtype=jnp.int32)[None, :]).astype(jnp.int32)
    earlier = (jnp.cumsum(expert_hits, axis=0).astype(jnp.int32) - expert_hits).astype(jnp.int32)
    slot_index = lax.optimization_barrier(jnp.sum(earlier * expert_hits, axis=1)).astype(jnp.int32)
    slot_place = (flat_routes * capacity + slot_index).astype(jnp.int32)
    slot_rows = jnp.full((expert_count * capacity,), row_count, jnp.int32)
    slot_rows = slot_rows.at[slot_place].set(jnp.arange(row_count, dtype=jnp.int32))
    return (slot_place, slot_rows.reshape(expert_count, capacity))

def reference(tokens, lengths, routes, deal_order, cotangent, attn_gain, query_gain, key_gain, moe_gain, w_query, key_projection_matrix, value_projection_matrix, w_out, w_router, w_gate, w_up, w_down):
    input_order, back_order = deal_layout(deal_order)
    group_assign = GROUP_TOKENS * TOPK
    route_groups = routes.reshape(N_FSDP, GROUP_TOKENS, TOPK)
    places, tables = jax.vmap(lambda route_rows: slot_table(route_rows, EXPERTS, CAP))(route_groups)
    group_ids = jnp.arange(N_FSDP, dtype=jnp.int32)
    global_pos = (places // CAP * (N_FSDP * CAP) + group_ids[:, None] * CAP + places % CAP).astype(jnp.int32)
    global_pos = global_pos.reshape(TOKENS * TOPK)
    global_rows = jnp.where(tables < group_assign, tables + group_ids[:, None, None] * group_assign, TOKENS * TOPK).astype(jnp.int32)
    global_rows = jnp.transpose(global_rows, (1, 0, 2)).reshape(EXPERTS, N_FSDP * CAP)
    chosen = routes[:, :, None] == jnp.arange(EXPERTS, dtype=jnp.int32)[None, None, :]
    hidden_part = FF // N_TP

    def forward(x_raw, gain_attn, gain_query, gain_key, gain_moe, weight_query, key_weight_cast, value_weight_cast, weight_out, weight_router, weight_gate, weight_up, weight_down):
        x_in = x_raw[input_order]
        normed_input = lower_precision(row_norm(x_in, gain_attn))
        query_pre = lower_back_cast(jnp.dot(normed_input, weight_query, precision=highest_precision)).reshape(N_FSDP, GROUP_TOKENS, QUERY_HEADS, HEAD_SIZE)
        key_before_norm = lower_back_cast(jnp.dot(normed_input, key_weight_cast, precision=highest_precision)).reshape(N_FSDP, GROUP_TOKENS, KEY_VALUE_HEADS, HEAD_SIZE)
        value_every_head = lower_back_cast(lower_precision(jnp.dot(normed_input, value_weight_cast, precision=highest_precision))).reshape(N_FSDP, GROUP_TOKENS, KEY_VALUE_HEADS, HEAD_SIZE)

        def attend(inputs):
            query_block, key_block, value_block, seq_lengths = inputs
            segment, position = seq_layout(seq_lengths, GROUP_TOKENS)
            cosine_table, sine_table = rotary(position, HEAD_SIZE)
            query_rows = lower_precision(rotate(row_norm(query_block, gain_query), cosine_table, sine_table))
            key = lower_precision(rotate(row_norm(key_block, gain_key), cosine_table, sine_table))
            row_ids = jnp.arange(GROUP_TOKENS)
            allowed = (segment[:, None] == segment[None, :]) & (row_ids[None, :] <= row_ids[:, None])
            grouped_rows = query_rows.reshape(GROUP_TOKENS, KEY_VALUE_HEADS, QUERY_HEADS // KEY_VALUE_HEADS, HEAD_SIZE)
            scores = jnp.einsum('qkgd,tkd->kgqt', grouped_rows, key, precision=highest_precision) * HEAD_SIZE ** (-0.5)
            scores = lower_back_cast(scores)
            scores = jnp.where(allowed, scores, masked_score)
            row_peak = lax.optimization_barrier(jnp.max(scores, axis=-1, keepdims=True))
            exponent = jnp.exp(scores - row_peak)
            attn_probs = lower_precision(exponent / lax.optimization_barrier(jnp.sum(exponent, axis=-1, keepdims=True)))
            attn_mixed = jnp.einsum('kgqt,tkd->qkgd', attn_probs, value_block, precision=highest_precision)
            return attn_mixed.reshape(GROUP_TOKENS, QUERY_HEADS * HEAD_SIZE)
        attn_mixed = lax.map(jax.checkpoint(attend), (query_pre, key_before_norm, value_every_head, lengths))
        attn_mixed = lower_back_cast(lower_precision(attn_mixed.reshape(TOKENS, QUERY_HEADS * HEAD_SIZE)))
        residual = x_in + lower_back_cast(jnp.dot(attn_mixed, weight_out, precision=highest_precision))
        moe_in = lower_precision(row_norm(residual, gain_moe))
        logits = lower_back_cast(jnp.dot(moe_in, weight_router, precision=highest_precision))
        selected = lax.optimization_barrier(jnp.sum(jnp.where(chosen, logits[:, None, :], 0.0), axis=-1))
        gate_peak = lax.optimization_barrier(jnp.max(selected, axis=-1, keepdims=True))
        gate_exp = jnp.exp(selected - gate_peak)
        gate_probs = gate_exp / lax.optimization_barrier(jnp.sum(gate_exp, axis=-1, keepdims=True))
        padded = jnp.concatenate([moe_in, jnp.zeros((1, MODEL_DIMENSION), moe_in.dtype)], axis=0)

        def expert(inputs):
            row_index, gate_mat, up_mat, down_mat = inputs
            expert_rows = padded[row_index // TOPK]
            total = jnp.zeros((row_index.shape[0], MODEL_DIMENSION), moe_in.dtype)
            for block_index in range(N_TP):
                hidden_cut = slice(block_index * hidden_part, (block_index + 1) * hidden_part)
                entry = lower_back_cast(expert_rows)
                gate_val = lower_back_cast(jnp.dot(entry, gate_mat[:, hidden_cut], precision=highest_precision))
                up_val = lower_back_cast(jnp.dot(entry, up_mat[:, hidden_cut], precision=highest_precision))
                hidden = lower_precision(jax.nn.silu(gate_val) * up_val)
                total = total + lower_back_cast(lower_precision(jnp.dot(hidden, down_mat[hidden_cut], precision=highest_precision)))
            return total
        expert_out = lax.map(jax.checkpoint(expert), (global_rows, weight_gate, weight_up, weight_down))
        picked = expert_out.reshape(EXPERTS * N_FSDP * CAP, MODEL_DIMENSION)[global_pos].reshape(TOKENS, TOPK, MODEL_DIMENSION)
        grouped_out = residual + lax.optimization_barrier(jnp.sum(gate_probs[:, :, None] * picked, axis=1))
        return grouped_out[back_order]
    floats = (tokens.astype(jnp.float32), attn_gain, query_gain, key_gain, moe_gain, w_query.astype(jnp.float32), key_projection_matrix.astype(jnp.float32), value_projection_matrix.astype(jnp.float32), w_out.astype(jnp.float32), w_router.astype(jnp.float32), w_gate.astype(jnp.float32), w_up.astype(jnp.float32), w_down.astype(jnp.float32))
    result, pullback = jax.vjp(forward, *floats)
    grads = pullback(cotangent.astype(jnp.float32))
    return (result.astype(jnp.bfloat16), grads[0], grads[1], grads[2], grads[3], grads[4], grads[5], grads[6], grads[7], grads[8], grads[9], grads[10], grads[11], grads[12])
```

```python
import jax
import jax.numpy as jnp
from jax import lax
from jax.sharding import Mesh
from jax.sharding import PartitionSpec as P

epsilon = 1e-06
rope_base = 1000000.0
masked_score = -1e30


def row_norm(values, gain_vec):
    factor = lax.rsqrt(jnp.mean(values * values, axis=-1, keepdims=True) + epsilon)
    return (values * factor * gain_vec, factor)


def norm_back(values, factor, gain_vec, upstream):
    scaled = upstream * gain_vec
    inner_term = jnp.mean(scaled * values, axis=-1, keepdims=True)
    return (factor * (scaled - values * (factor * factor) * inner_term), upstream * values * factor)


def seq_layout(seq_lengths, row_count):
    seq_ends = jnp.cumsum(seq_lengths)
    row_ids = jnp.arange(row_count, dtype=jnp.int32)
    segment = jnp.sum((row_ids[:, None] >= seq_ends[None, :]).astype(jnp.int32), axis=1)
    seq_starts = seq_ends - seq_lengths
    chosen = segment[:, None] == jnp.arange(seq_lengths.shape[0], dtype=jnp.int32)[None, :]
    position = row_ids - jnp.sum(jnp.where(chosen, seq_starts[None, :], 0), axis=1)
    return (segment, position)


def rotary(position, head_width):
    half_width = head_width // 2
    inverse_freq = rope_base ** (-(jnp.arange(half_width, dtype=jnp.float32) * (2.0 / head_width)))
    angles = position.astype(jnp.float32)[:, None] * inverse_freq[None, :]
    return (jnp.cos(angles)[:, None, :], jnp.sin(angles)[:, None, :])


def rotate(values, cosine_table, sine_table):
    half_width = values.shape[-1] // 2
    front_half = values[..., :half_width]
    back_half = values[..., half_width:]
    return jnp.concatenate(
        [
            front_half * cosine_table - back_half * sine_table,
            back_half * cosine_table + front_half * sine_table,
        ],
        axis=-1,
    )


def rotate_back(upstream, cosine_table, sine_table):
    half_width = upstream.shape[-1] // 2
    front_half = upstream[..., :half_width]
    back_half = upstream[..., half_width:]
    return jnp.concatenate(
        [
            front_half * cosine_table + back_half * sine_table,
            back_half * cosine_table - front_half * sine_table,
        ],
        axis=-1,
    )


def slot_table(route_rows, expert_count, capacity):
    row_count = route_rows.shape[0] * route_rows.shape[1]
    flat_routes = route_rows.reshape(row_count)
    expert_hits = (
        flat_routes[:, None] == jnp.arange(expert_count, dtype=jnp.int32)[None, :]
    ).astype(jnp.int32)
    earlier = jnp.cumsum(expert_hits, axis=0) - expert_hits
    slot_index = jnp.sum(earlier * expert_hits, axis=1)
    slot_place = flat_routes * capacity + slot_index
    slot_rows = jnp.full((expert_count * capacity,), row_count, jnp.int32)
    slot_rows = slot_rows.at[slot_place].set(jnp.arange(row_count, dtype=jnp.int32))
    return (slot_place, slot_rows.reshape(expert_count, capacity))


def contract_rows(left, right):
    return lax.dot_general(
        left, right, (((0,), (0,)), ((), ())), preferred_element_type=jnp.float32
    )


def contract_last(left, right):
    return lax.dot_general(
        left, right, (((1,), (1,)), ((), ())), preferred_element_type=jnp.float32
    )


def body(
    tokens,
    lengths,
    routes,
    deal_order,
    cotangent,
    attn_gain,
    query_gain,
    key_gain,
    moe_gain,
    w_query,
    key_projection_matrix,
    value_projection_matrix,
    w_out,
    w_router,
    w_gate,
    w_up,
    w_down,
):
    half_rows = tokens.shape[0]
    model_width = tokens.shape[1]
    head_dim = query_gain.shape[0]
    score_scale = head_dim ** (-0.5)
    fsdp_count = lax.axis_size("fsdp")
    tp_count = lax.axis_size("tp")
    fsdp_index = lax.axis_index("fsdp")
    tp_index = lax.axis_index("tp")
    slice_rows = half_rows // fsdp_count
    group_rows = tp_count * half_rows
    own_start = tp_index * half_rows
    peer_ids = jnp.arange(fsdp_count, dtype=jnp.int32)
    wanted = (peer_ids - fsdp_index) % fsdp_count
    send_pick = jnp.sum(
        jnp.where(deal_order[None, :] == wanted[:, None], peer_ids[None, :], 0), axis=1
    )
    back_pick = (deal_order + fsdp_index) % fsdp_count

    def deal_copies(values):
        slices = jnp.take(values.reshape(fsdp_count, slice_rows, model_width), send_pick, axis=0)
        return jnp.broadcast_to(slices[None], (tp_count, fsdp_count, slice_rows, model_width))

    tokens_all, cotangent_all = (
        lax.all_to_all(
            lax.all_to_all(deal_copies(tokens), "tp", split_axis=0, concat_axis=0, tiled=True),
            "fsdp",
            split_axis=1,
            concat_axis=1,
            tiled=True,
        ),
        lax.all_to_all(
            lax.all_to_all(deal_copies(cotangent), "tp", split_axis=0, concat_axis=0, tiled=True),
            "fsdp",
            split_axis=1,
            concat_axis=1,
            tiled=True,
        ),
    )
    tokens_in = tokens_all.reshape(group_rows, model_width).astype(jnp.float32)
    upstream = cotangent_all.reshape(group_rows, model_width).astype(jnp.float32)
    attn_in, attn_factor = row_norm(tokens_in, attn_gain)
    normed_all = attn_in.astype(jnp.bfloat16)
    query_full, key_full, value_full, out_full = (
        lax.all_gather(w_query, "fsdp", axis=0, tiled=True),
        lax.all_gather(key_projection_matrix, "fsdp", axis=0, tiled=True),
        lax.all_gather(value_projection_matrix, "fsdp", axis=0, tiled=True),
        lax.all_gather(w_out, "fsdp", axis=1, tiled=True),
    )
    query_heads = query_full.shape[1] // head_dim
    kv_heads = key_full.shape[1] // head_dim
    group_size = query_heads // kv_heads
    segment, position = seq_layout(lengths[0], group_rows)
    cosine_table, sine_table = rotary(position, head_dim)
    row_ids = jnp.arange(group_rows)
    allowed = (segment[:, None] == segment[None, :]) & (row_ids[None, :] <= row_ids[:, None])
    query_pre = jnp.dot(normed_all, query_full, preferred_element_type=jnp.float32).reshape(
        group_rows, query_heads, head_dim
    )
    query_normed, query_factor = row_norm(query_pre, query_gain)
    query_low = (
        rotate(query_normed, cosine_table, sine_table)
        .astype(jnp.bfloat16)
        .reshape(group_rows, kv_heads, group_size, head_dim)
    )
    key_before_norm = jnp.dot(normed_all, key_full, preferred_element_type=jnp.float32).reshape(
        group_rows, kv_heads, head_dim
    )
    key_normed, key_factor = row_norm(key_before_norm, key_gain)
    key_low = rotate(key_normed, cosine_table, sine_table).astype(jnp.bfloat16)
    value_low = (
        jnp.dot(normed_all, value_full, preferred_element_type=jnp.float32)
        .astype(jnp.bfloat16)
        .reshape(group_rows, kv_heads, head_dim)
    )
    scores = (
        jnp.einsum("qkgd,tkd->kgqt", query_low, key_low, preferred_element_type=jnp.float32)
        * score_scale
    )
    scores = jnp.where(allowed, scores, masked_score)
    row_peak = jnp.max(scores, axis=-1, keepdims=True)
    exponent = jnp.exp(scores - row_peak)
    totals = jnp.sum(exponent, axis=-1, keepdims=True)
    log_total = row_peak + jnp.log(totals)
    attn_probs = (exponent / totals).astype(jnp.bfloat16)
    attn_mixed = jnp.einsum(
        "kgqt,tkd->qkgd", attn_probs, value_low, preferred_element_type=jnp.float32
    )
    mixed_low = attn_mixed.reshape(group_rows, query_heads * head_dim).astype(jnp.bfloat16)
    attn_part = jnp.dot(mixed_low, out_full, preferred_element_type=jnp.float32)
    residual = tokens_in + lax.psum(attn_part, "tp")
    moe_in, moe_factor = row_norm(residual, moe_gain)
    moe_low = moe_in.astype(jnp.bfloat16)
    logits = jnp.dot(moe_low, w_router, preferred_element_type=jnp.float32)
    experts = w_router.shape[1]
    top_count = routes.shape[1]
    chosen = routes[:, :, None] == jnp.arange(experts, dtype=jnp.int32)[None, None, :]
    selected = jnp.sum(jnp.where(chosen, logits[:, None, :], 0.0), axis=-1)
    gate_peak = jnp.max(selected, axis=-1, keepdims=True)
    gate_exp = jnp.exp(selected - gate_peak)
    gate_probs = gate_exp / jnp.sum(gate_exp, axis=-1, keepdims=True)
    capacity = max(2, 3 * group_rows * top_count // (2 * experts))
    slot_place, slot_rows = slot_table(routes, experts, capacity)
    part_cap = capacity // tp_count
    slot_start = tp_index * part_cap
    gate_full, up_full, down_full = (
        lax.all_gather(w_gate, "tp", axis=2, tiled=True),
        lax.all_gather(w_up, "tp", axis=2, tiled=True),
        lax.all_gather(w_down, "tp", axis=1, tiled=True),
    )
    sent_rows = lax.dynamic_slice_in_dim(slot_rows, slot_start, part_cap, 1)
    slot_expert = slot_place // capacity
    slot_offset = slot_place % capacity - slot_start
    in_half = (slot_offset >= 0) & (slot_offset < part_cap)
    local_place = jnp.where(in_half, slot_expert * part_cap + slot_offset, experts * part_cap)
    padded = jnp.concatenate([moe_low, jnp.zeros((1, model_width), jnp.bfloat16)], axis=0)
    arrived = lax.all_to_all(
        padded[sent_rows // top_count], "fsdp", split_axis=0, concat_axis=0, tiled=True
    )
    local_experts = w_gate.shape[0]
    sources = experts // local_experts
    slot_count = sources * part_cap
    ff_part = w_gate.shape[2]

    def to_experts(values):
        return jnp.transpose(
            values.reshape(sources, local_experts, part_cap, model_width), (1, 0, 2, 3)
        ).reshape(local_experts, slot_count, model_width)

    def to_sources(values):
        width = values.shape[-1]
        return jnp.transpose(
            values.reshape(local_experts, sources, part_cap, width), (1, 0, 2, 3)
        ).reshape(experts, part_cap, width)

    def pick_rows(values):
        flat = values.reshape(experts * part_cap, tp_count * model_width)
        flat = jnp.concatenate([flat, jnp.zeros((1, tp_count * model_width), jnp.bfloat16)], axis=0)
        gathered = flat[local_place].reshape(group_rows, top_count, tp_count, model_width)
        return jnp.sum(gathered.astype(jnp.float32), axis=2)

    expert_rows = to_experts(arrived)
    gate_val = jnp.einsum(
        "esd,edf->esf", expert_rows, gate_full, preferred_element_type=jnp.float32
    )
    up_val = jnp.einsum("esd,edf->esf", expert_rows, up_full, preferred_element_type=jnp.float32)
    sigmoid_val = jax.nn.sigmoid(gate_val)
    swish_val = gate_val * sigmoid_val
    hidden_low = (swish_val * up_val).astype(jnp.bfloat16)
    hidden_blocks = hidden_low.reshape(local_experts, slot_count, tp_count, ff_part)
    down_blocks = down_full.reshape(local_experts, tp_count, ff_part, model_width)
    expert_out = (
        jnp.einsum(
            "esbf,ebfd->esbd", hidden_blocks, down_blocks, preferred_element_type=jnp.float32
        )
        .astype(jnp.bfloat16)
        .reshape(local_experts, slot_count, tp_count * model_width)
    )
    returned = lax.all_to_all(
        to_sources(expert_out), "fsdp", split_axis=0, concat_axis=0, tiled=True
    )
    picked = pick_rows(returned)
    moe_part = jnp.sum(gate_probs[:, :, None] * picked, axis=1)
    gate_grad_part = jnp.sum(upstream[:, None, :] * picked, axis=-1)
    weighted = (
        (gate_probs[:, :, None] * upstream[:, None, :])
        .astype(jnp.bfloat16)
        .reshape(group_rows * top_count, model_width)
    )
    weighted = jnp.concatenate([weighted, jnp.zeros((1, model_width), jnp.bfloat16)], axis=0)
    grad_arrived = lax.all_to_all(
        weighted[sent_rows], "fsdp", split_axis=0, concat_axis=0, tiled=True
    )
    grad_slots = to_experts(grad_arrived)
    hidden_grad = jnp.einsum(
        "esd,ebfd->esbf", grad_slots, down_blocks, preferred_element_type=jnp.float32
    ).reshape(local_experts, slot_count, tp_count * ff_part)
    swish_slope = sigmoid_val * (1.0 + gate_val * (1.0 - sigmoid_val))
    gate_val_grad = (hidden_grad * up_val * swish_slope).astype(jnp.bfloat16)
    up_val_grad = (hidden_grad * swish_val).astype(jnp.bfloat16)
    grad_w_down = jnp.einsum(
        "esbf,esd->ebfd", hidden_blocks, grad_slots, preferred_element_type=jnp.float32
    ).reshape(local_experts, tp_count * ff_part, model_width)
    grad_w_gate = jnp.einsum(
        "esd,esf->edf", expert_rows, gate_val_grad, preferred_element_type=jnp.float32
    )
    grad_w_up = jnp.einsum(
        "esd,esf->edf", expert_rows, up_val_grad, preferred_element_type=jnp.float32
    )
    gate_blocks = gate_full.reshape(local_experts, model_width, tp_count, ff_part)
    up_blocks = up_full.reshape(local_experts, model_width, tp_count, ff_part)
    entry_grad = (
        (
            jnp.einsum(
                "esbf,edbf->esbd",
                gate_val_grad.reshape(local_experts, slot_count, tp_count, ff_part),
                gate_blocks,
                preferred_element_type=jnp.float32,
            )
            + jnp.einsum(
                "esbf,edbf->esbd",
                up_val_grad.reshape(local_experts, slot_count, tp_count, ff_part),
                up_blocks,
                preferred_element_type=jnp.float32,
            )
        )
        .astype(jnp.bfloat16)
        .reshape(local_experts, slot_count, tp_count * model_width)
    )
    sent_back = lax.all_to_all(
        to_sources(entry_grad), "fsdp", split_axis=0, concat_axis=0, tiled=True
    )
    expert_grad = jnp.sum(pick_rows(sent_back), axis=1)
    grad_w_gate, grad_w_up, grad_w_down = (
        lax.psum_scatter(
            grad_w_gate.astype(jnp.bfloat16), "tp", scatter_dimension=2, tiled=True
        ).astype(jnp.float32),
        lax.psum_scatter(
            grad_w_up.astype(jnp.bfloat16), "tp", scatter_dimension=2, tiled=True
        ).astype(jnp.float32),
        lax.psum_scatter(
            grad_w_down.astype(jnp.bfloat16), "tp", scatter_dimension=1, tiled=True
        ).astype(jnp.float32),
    )
    moe_grad, gate_grad = (
        lax.psum(expert_grad.astype(jnp.bfloat16), "tp").astype(jnp.float32),
        lax.psum(gate_grad_part.astype(jnp.bfloat16), "tp").astype(jnp.float32),
    )
    gate_inner = jnp.sum(gate_probs * gate_grad, axis=-1, keepdims=True)
    selected_grad = gate_probs * (gate_grad - gate_inner)
    logit_grad = jnp.sum(jnp.where(chosen, selected_grad[:, :, None], 0.0), axis=1).astype(
        jnp.bfloat16
    )
    moe_grad = moe_grad + contract_last(logit_grad, w_router)
    router_grad = contract_rows(
        lax.dynamic_slice_in_dim(moe_low, own_start, half_rows, 0),
        lax.dynamic_slice_in_dim(logit_grad, own_start, half_rows, 0),
    )
    residual_from_norm, moe_gain_terms = norm_back(residual, moe_factor, moe_gain, moe_grad)
    residual_grad = upstream + residual_from_norm
    moe_gain_grad = jnp.sum(
        lax.dynamic_slice_in_dim(moe_gain_terms, own_start, half_rows, 0), axis=0
    )
    residual_low = residual_grad.astype(jnp.bfloat16)
    mixed_grad = (
        contract_last(residual_low, out_full)
        .astype(jnp.bfloat16)
        .reshape(group_rows, kv_heads, group_size, head_dim)
    )
    grad_w_out = contract_rows(mixed_low, residual_low)
    scores = (
        jnp.einsum("qkgd,tkd->kgqt", query_low, key_low, preferred_element_type=jnp.float32)
        * score_scale
    )
    scores = jnp.where(allowed, scores, masked_score)
    probs_full = jnp.exp(scores - log_total)
    prob_grad = jnp.einsum(
        "qkgd,tkd->kgqt", mixed_grad, value_low, preferred_element_type=jnp.float32
    )
    prob_inner = jnp.sum(probs_full * prob_grad, axis=-1, keepdims=True)
    score_grad = (probs_full * (prob_grad - prob_inner)).astype(jnp.bfloat16)
    query_grad = (
        jnp.einsum(
            "kgqt,tkd->qkgd", score_grad, key_low, preferred_element_type=jnp.float32
        ).reshape(group_rows, query_heads, head_dim)
        * score_scale
    )
    key_grad = (
        jnp.einsum("kgqt,qkgd->tkd", score_grad, query_low, preferred_element_type=jnp.float32)
        * score_scale
    )
    value_grad = (
        jnp.einsum(
            "kgqt,qkgd->tkd",
            probs_full.astype(jnp.bfloat16),
            mixed_grad,
            preferred_element_type=jnp.float32,
        )
        .astype(jnp.bfloat16)
        .reshape(group_rows, kv_heads * head_dim)
    )
    query_pre_grad, query_gain_terms = norm_back(
        query_pre, query_factor, query_gain, rotate_back(query_grad, cosine_table, sine_table)
    )
    key_pre_grad, key_gain_terms = norm_back(
        key_before_norm, key_factor, key_gain, rotate_back(key_grad, cosine_table, sine_table)
    )
    query_pre_low = query_pre_grad.astype(jnp.bfloat16).reshape(group_rows, query_heads * head_dim)
    key_pre_low = key_pre_grad.astype(jnp.bfloat16).reshape(group_rows, kv_heads * head_dim)
    grad_w_query = contract_rows(normed_all, query_pre_low)
    grad_w_key = contract_rows(normed_all, key_pre_low)
    grad_w_value = contract_rows(normed_all, value_grad)
    normed_grad = (
        contract_last(query_pre_low, query_full)
        + contract_last(key_pre_low, key_full)
        + contract_last(value_grad, value_full)
    )
    normed_grad_own, moe_own = (
        lax.psum_scatter(
            normed_grad.astype(jnp.bfloat16), "tp", scatter_dimension=0, tiled=True
        ).astype(jnp.float32),
        lax.psum_scatter(
            moe_part.astype(jnp.bfloat16), "tp", scatter_dimension=0, tiled=True
        ).astype(jnp.float32),
    )
    tokens_own = lax.dynamic_slice_in_dim(tokens_in, own_start, half_rows, 0)
    factor_own = lax.dynamic_slice_in_dim(attn_factor, own_start, half_rows, 0)
    tokens_from_norm, attn_gain_terms = norm_back(
        tokens_own, factor_own, attn_gain, normed_grad_own
    )
    grad_group = lax.dynamic_slice_in_dim(residual_grad, own_start, half_rows, 0) + tokens_from_norm
    residual_own = lax.dynamic_slice_in_dim(residual, own_start, half_rows, 0)
    output_group = (residual_own + moe_own).astype(jnp.bfloat16)
    back_output, back_grad = (
        lax.all_to_all(
            output_group.astype(jnp.float32)
            .reshape(fsdp_count, slice_rows, model_width)
            .astype(jnp.bfloat16),
            "fsdp",
            split_axis=0,
            concat_axis=0,
            tiled=True,
        ).astype(jnp.float32),
        lax.all_to_all(
            grad_group.reshape(fsdp_count, slice_rows, model_width).astype(jnp.bfloat16),
            "fsdp",
            split_axis=0,
            concat_axis=0,
            tiled=True,
        ).astype(jnp.float32),
    )
    output = (
        jnp.take(back_output, back_pick, axis=0)
        .reshape(half_rows, model_width)
        .astype(jnp.bfloat16)
    )
    grad_input = jnp.take(back_grad, back_pick, axis=0).reshape(half_rows, model_width)
    grad_w_query, grad_w_key, grad_w_value, grad_w_out = (
        lax.psum_scatter(grad_w_query, "fsdp", scatter_dimension=0, tiled=True),
        lax.psum_scatter(grad_w_key, "fsdp", scatter_dimension=0, tiled=True),
        lax.psum_scatter(grad_w_value, "fsdp", scatter_dimension=0, tiled=True),
        lax.psum_scatter(grad_w_out, "fsdp", scatter_dimension=1, tiled=True),
    )
    grad_attn_gain, grad_query_gain, grad_key_gain, grad_moe_gain, grad_w_router = lax.psum(
        (
            jnp.sum(attn_gain_terms, axis=0),
            jnp.sum(query_gain_terms, axis=(0, 1)),
            jnp.sum(key_gain_terms, axis=(0, 1)),
            moe_gain_grad,
            router_grad,
        ),
        ("fsdp", "tp"),
    )
    return (
        output,
        grad_input,
        grad_attn_gain,
        grad_query_gain,
        grad_key_gain,
        grad_moe_gain,
        grad_w_query,
        grad_w_key,
        grad_w_value,
        grad_w_out,
        grad_w_router,
        grad_w_gate,
        grad_w_up,
        grad_w_down,
    )


def fast_body(
    tokens,
    lengths,
    routes,
    deal_order,
    cotangent,
    attn_gain,
    query_gain,
    key_gain,
    moe_gain,
    w_query,
    key_projection_matrix,
    value_projection_matrix,
    w_out,
    w_router,
    w_gate,
    w_up,
    w_down,
):
    own_rows, model_width = tokens.shape
    head_dim = query_gain.shape[0]
    score_scale = head_dim ** (-0.5)
    chip_count = lax.axis_size("chip")
    core_count = lax.axis_size("core")
    tp_count = lax.axis_size("tp")
    core_index = lax.axis_index("core")
    tp_index = lax.axis_index("tp")
    fsdp_count = chip_count * core_count
    fsdp_index = lax.axis_index("chip") * core_count + core_index
    slice_rows = own_rows // fsdp_count
    group_rows = tp_count * own_rows
    quad_rows = core_count * group_rows
    plane = ("chip", "core")
    quad = ("core", "tp")
    peer_ids = jnp.arange(fsdp_count, dtype=jnp.int32)
    wanted = (peer_ids - fsdp_index) % fsdp_count
    send_pick = jnp.sum(
        jnp.where(deal_order[None, :] == wanted[:, None], peer_ids[None, :], 0), axis=1
    )
    back_pick = (deal_order + fsdp_index) % fsdp_count

    def deal(values):
        slices = jnp.take(values.reshape(fsdp_count, slice_rows, model_width), send_pick, axis=0)
        return lax.all_to_all(slices, plane, split_axis=0, concat_axis=0, tiled=True).reshape(
            own_rows, model_width
        )

    def deal_back(values):
        arrived = lax.all_to_all(
            values.reshape(fsdp_count, slice_rows, model_width),
            plane,
            split_axis=0,
            concat_axis=0,
            tiled=True,
        )
        return jnp.take(arrived, back_pick, axis=0).reshape(own_rows, model_width)

    def quarter_columns(weight):
        rows, width = weight.shape
        mixed = lax.all_to_all(
            weight.reshape(rows, core_count, width // core_count),
            "core",
            split_axis=1,
            concat_axis=0,
            tiled=True,
        ).reshape(core_count * rows, width // core_count)
        return lax.all_gather(mixed, "chip", axis=0, tiled=True)

    def quarter_rows(weight):
        rows, width = weight.shape
        mixed = lax.all_to_all(weight, "core", split_axis=0, concat_axis=1, tiled=True)
        return lax.all_gather(mixed, "chip", axis=1, tiled=True)

    def quarter_columns_back(grad):
        mine = lax.psum_scatter(
            grad.astype(jnp.bfloat16), "chip", scatter_dimension=0, tiled=True
        )
        return lax.all_to_all(mine, "core", split_axis=0, concat_axis=1, tiled=True).astype(
            jnp.float32
        )

    def quarter_rows_back(grad):
        mine = lax.psum_scatter(
            grad.astype(jnp.bfloat16), "chip", scatter_dimension=1, tiled=True
        )
        return lax.all_to_all(mine, "core", split_axis=1, concat_axis=0, tiled=True).astype(
            jnp.float32
        )

    tokens_own = deal(tokens).astype(jnp.float32)
    upstream_low = deal(cotangent)
    upstream_all = lax.all_gather(upstream_low, plane, axis=0, tiled=True)
    upstream = upstream_low.astype(jnp.float32)
    attn_in, attn_factor = row_norm(tokens_own, attn_gain)
    normed = lax.all_gather(attn_in.astype(jnp.bfloat16), quad, axis=0, tiled=True)
    query_part = quarter_columns(w_query)
    key_part = quarter_columns(key_projection_matrix)
    value_part = quarter_columns(value_projection_matrix)
    out_part = quarter_rows(w_out)
    heads = query_part.shape[1] // head_dim
    quad_lengths = lax.all_gather(lengths, "core", axis=0, tiled=True)
    segment, position = jax.vmap(lambda own: seq_layout(own, group_rows))(quad_lengths)
    cosine_table, sine_table = rotary(position.reshape(quad_rows), head_dim)
    row_ids = jnp.arange(group_rows)
    allowed = (segment[:, :, None] == segment[:, None, :]) & (
        row_ids[None, None, :] <= row_ids[None, :, None]
    )
    allowed = allowed[:, None]

    def split_groups(values):
        return values.reshape((core_count, group_rows) + values.shape[1:])

    query_pre = jnp.dot(normed, query_part, preferred_element_type=jnp.float32).reshape(
        quad_rows, heads, head_dim
    )
    query_normed, query_factor = row_norm(query_pre, query_gain)
    query_low = split_groups(rotate(query_normed, cosine_table, sine_table).astype(jnp.bfloat16))
    key_before_norm = jnp.dot(normed, key_part, preferred_element_type=jnp.float32).reshape(
        quad_rows, 1, head_dim
    )
    key_normed, key_factor = row_norm(key_before_norm, key_gain)
    key_low = split_groups(
        rotate(key_normed, cosine_table, sine_table).astype(jnp.bfloat16)[:, 0]
    )
    value_low = split_groups(
        jnp.dot(normed, value_part, preferred_element_type=jnp.float32).astype(jnp.bfloat16)
    )
    scores = (
        jnp.einsum("bqgd,btd->bgqt", query_low, key_low, preferred_element_type=jnp.float32)
        * score_scale
    )
    scores = jnp.where(allowed, scores, masked_score)
    row_peak = jnp.max(scores, axis=-1, keepdims=True)
    exponent = jnp.exp(scores - row_peak)
    probs_full = exponent / jnp.sum(exponent, axis=-1, keepdims=True)
    probs_low = probs_full.astype(jnp.bfloat16)
    mixed_low = (
        jnp.einsum("bgqt,btd->bqgd", probs_low, value_low, preferred_element_type=jnp.float32)
        .reshape(quad_rows, heads * head_dim)
        .astype(jnp.bfloat16)
    )
    attn_out = jnp.dot(mixed_low, out_part, preferred_element_type=jnp.float32)
    residual = tokens_own + lax.psum_scatter(
        attn_out.astype(jnp.bfloat16), quad, scatter_dimension=0, tiled=True
    ).astype(jnp.float32)
    moe_in, moe_factor = row_norm(residual, moe_gain)
    moe_low = moe_in.astype(jnp.bfloat16)
    logits = jnp.dot(moe_low, w_router, preferred_element_type=jnp.float32)
    experts = w_router.shape[1]
    own_routes = lax.dynamic_slice_in_dim(routes, tp_index * own_rows, own_rows, 0)
    chosen = jnp.any(
        own_routes[:, :, None] == jnp.arange(experts, dtype=jnp.int32)[None, None, :], axis=1
    )
    gate_peak = jnp.max(jnp.where(chosen, logits, -jnp.inf), axis=-1, keepdims=True)
    gate_exp = jnp.where(chosen, jnp.exp(jnp.minimum(logits - gate_peak, 0.0)), 0.0)
    gates = gate_exp / jnp.sum(gate_exp, axis=-1, keepdims=True)
    moe_all = lax.all_gather(moe_low, plane, axis=0, tiled=True)
    gate_column = lax.all_to_all(
        gates.T.reshape(experts, 1, own_rows), plane, split_axis=0, concat_axis=0, tiled=True
    ).reshape(fsdp_count * own_rows, 1)
    gate_full = lax.all_gather(w_gate[0], "tp", axis=1, tiled=True)
    up_full = lax.all_gather(w_up[0], "tp", axis=1, tiled=True)
    down_full = lax.all_gather(w_down[0], "tp", axis=0, tiled=True)
    gate_val = jnp.dot(moe_all, gate_full, preferred_element_type=jnp.float32)
    up_val = jnp.dot(moe_all, up_full, preferred_element_type=jnp.float32)
    sigmoid_val = jax.nn.sigmoid(gate_val)
    swish_val = gate_val * sigmoid_val
    hidden_low = (swish_val * up_val).astype(jnp.bfloat16)
    back_hidden = contract_last(upstream_all, down_full)
    gate_grad_column = jnp.sum(hidden_low.astype(jnp.float32) * back_hidden, axis=1)
    hidden_gated = (hidden_low.astype(jnp.float32) * gate_column).astype(jnp.bfloat16)
    moe_out = jnp.dot(hidden_gated, down_full, preferred_element_type=jnp.float32)
    hidden_grad = back_hidden * gate_column
    swish_slope = sigmoid_val * (1.0 + gate_val * (1.0 - sigmoid_val))
    gate_val_grad = (hidden_grad * up_val * swish_slope).astype(jnp.bfloat16)
    up_val_grad = (hidden_grad * swish_val).astype(jnp.bfloat16)
    entry_grad = contract_last(gate_val_grad, gate_full) + contract_last(up_val_grad, up_full)
    grad_w_down = contract_rows(hidden_gated, upstream_all)
    grad_w_gate = contract_rows(moe_all, gate_val_grad)
    grad_w_up = contract_rows(moe_all, up_val_grad)
    entry_own = lax.psum_scatter(
        entry_grad.astype(jnp.bfloat16), plane, scatter_dimension=0, tiled=True
    ).astype(jnp.float32)
    moe_own = lax.psum_scatter(
        moe_out.astype(jnp.bfloat16), plane, scatter_dimension=0, tiled=True
    ).astype(jnp.float32)
    gate_grad = (
        lax.all_to_all(
            gate_grad_column.reshape(experts, 1, own_rows),
            plane,
            split_axis=0,
            concat_axis=0,
            tiled=True,
        )
        .reshape(experts, own_rows)
        .T
    )
    grad_w_gate, grad_w_up, grad_w_down = (
        lax.psum_scatter(
            grad_w_gate.astype(jnp.bfloat16), "tp", scatter_dimension=1, tiled=True
        ).astype(jnp.float32)[None],
        lax.psum_scatter(
            grad_w_up.astype(jnp.bfloat16), "tp", scatter_dimension=1, tiled=True
        ).astype(jnp.float32)[None],
        lax.psum_scatter(
            grad_w_down.astype(jnp.bfloat16), "tp", scatter_dimension=0, tiled=True
        ).astype(jnp.float32)[None],
    )
    gate_inner = jnp.sum(gates * gate_grad, axis=-1, keepdims=True)
    logit_grad = (gates * (gate_grad - gate_inner)).astype(jnp.bfloat16)
    moe_grad = entry_own + contract_last(logit_grad, w_router)
    router_grad = contract_rows(moe_low, logit_grad)
    residual_from_norm, moe_gain_terms = norm_back(residual, moe_factor, moe_gain, moe_grad)
    residual_grad = upstream + residual_from_norm
    residual_low = lax.all_gather(residual_grad.astype(jnp.bfloat16), quad, axis=0, tiled=True)
    mixed_grad = split_groups(
        contract_last(residual_low, out_part)
        .astype(jnp.bfloat16)
        .reshape(quad_rows, heads, head_dim)
    )
    grad_w_out = contract_rows(mixed_low, residual_low)
    prob_grad = jnp.einsum(
        "bqgd,btd->bgqt", mixed_grad, value_low, preferred_element_type=jnp.float32
    )
    prob_inner = jnp.sum(probs_full * prob_grad, axis=-1, keepdims=True)
    score_grad = (probs_full * (prob_grad - prob_inner)).astype(jnp.bfloat16)
    query_grad = (
        jnp.einsum(
            "bgqt,btd->bqgd", score_grad, key_low, preferred_element_type=jnp.float32
        ).reshape(quad_rows, heads, head_dim)
        * score_scale
    )
    key_grad = (
        jnp.einsum("bgqt,bqgd->btd", score_grad, query_low, preferred_element_type=jnp.float32)
        * score_scale
    ).reshape(quad_rows, 1, head_dim)
    value_grad = (
        jnp.einsum("bgqt,bqgd->btd", probs_low, mixed_grad, preferred_element_type=jnp.float32)
        .astype(jnp.bfloat16)
        .reshape(quad_rows, head_dim)
    )
    query_pre_grad, query_gain_terms = norm_back(
        query_pre, query_factor, query_gain, rotate_back(query_grad, cosine_table, sine_table)
    )
    key_pre_grad, key_gain_terms = norm_back(
        key_before_norm, key_factor, key_gain, rotate_back(key_grad, cosine_table, sine_table)
    )
    query_pre_low = query_pre_grad.astype(jnp.bfloat16).reshape(quad_rows, heads * head_dim)
    key_pre_low = key_pre_grad.astype(jnp.bfloat16).reshape(quad_rows, head_dim)
    grad_w_query = contract_rows(normed, query_pre_low)
    grad_w_key = contract_rows(normed, key_pre_low)
    grad_w_value = contract_rows(normed, value_grad)
    normed_grad = (
        contract_last(query_pre_low, query_part)
        + contract_last(key_pre_low, key_part)
        + contract_last(value_grad, value_part)
    )
    normed_grad_own = lax.psum_scatter(
        normed_grad.astype(jnp.bfloat16), quad, scatter_dimension=0, tiled=True
    ).astype(jnp.float32)
    tokens_from_norm, attn_gain_terms = norm_back(
        tokens_own, attn_factor, attn_gain, normed_grad_own
    )
    output = deal_back((residual + moe_own).astype(jnp.bfloat16))
    grad_input = deal_back((residual_grad + tokens_from_norm).astype(jnp.bfloat16)).astype(
        jnp.float32
    )
    grad_attn_gain, grad_query_gain, grad_key_gain, grad_moe_gain, grad_w_router = lax.psum(
        (
            jnp.sum(attn_gain_terms, axis=0),
            jnp.sum(query_gain_terms, axis=(0, 1)),
            jnp.sum(key_gain_terms, axis=(0, 1)),
            jnp.sum(moe_gain_terms, axis=0),
            router_grad,
        ),
        ("chip", "core", "tp"),
    )
    return (
        output,
        grad_input,
        grad_attn_gain,
        grad_query_gain,
        grad_key_gain,
        grad_moe_gain,
        quarter_columns_back(grad_w_query),
        quarter_columns_back(grad_w_key),
        quarter_columns_back(grad_w_value),
        quarter_rows_back(grad_w_out),
        grad_w_router,
        grad_w_gate,
        grad_w_up,
        grad_w_down,
    )


def solution(mesh):
    fsdp_count, tp_count = mesh.shape["fsdp"], mesh.shape["tp"]
    chips = Mesh(mesh.devices.reshape(fsdp_count // 2, 2, tp_count), ("chip", "core", "tp"))
    dense = fsdp_count <= 16
    fsdp = ("chip", "core") if dense else "fsdp"
    every = ("chip", "core", "tp") if dense else ("fsdp", "tp")
    return jax.shard_map(
        fast_body if dense else body,
        mesh=chips if dense else mesh,
        in_specs=(
            P(every, None),
            P(fsdp, None),
            P(fsdp, None),
            P(),
            P(every, None),
            P(),
            P(),
            P(),
            P(),
            P(fsdp, "tp"),
            P(fsdp, "tp"),
            P(fsdp, "tp"),
            P("tp", fsdp),
            P(),
            P(fsdp, None, "tp"),
            P(fsdp, None, "tp"),
            P(fsdp, "tp", None),
        ),
        out_specs=(
            P(every, None),
            P(every, None),
            P(),
            P(),
            P(),
            P(),
            P(fsdp, "tp"),
            P(fsdp, "tp"),
            P(fsdp, "tp"),
            P("tp", fsdp),
            P(),
            P(fsdp, None, "tp"),
            P(fsdp, None, "tp"),
            P(fsdp, "tp", None),
        ),
        check_vma=False,
    )
```

```python
import functools

import jax
import jax.numpy as jnp
from jax import lax
from jax.experimental import pallas as pl
from jax.experimental.pallas import tpu as pltpu
from jax.sharding import Mesh
from jax.sharding import PartitionSpec as P

epsilon = 1e-06
rope_base = 1000000.0
masked_score = -1e30


def row_norm(values, gain_vec):
    factor = lax.rsqrt(jnp.mean(values * values, axis=-1, keepdims=True) + epsilon)
    return (values * factor * gain_vec, factor)


def norm_back(values, factor, gain_vec, upstream):
    scaled = upstream * gain_vec
    inner_term = jnp.mean(scaled * values, axis=-1, keepdims=True)
    return (factor * (scaled - values * (factor * factor) * inner_term), upstream * values * factor)


def seq_layout(seq_lengths, row_count):
    seq_ends = jnp.cumsum(seq_lengths)
    row_ids = jnp.arange(row_count, dtype=jnp.int32)
    segment = jnp.sum((row_ids[:, None] >= seq_ends[None, :]).astype(jnp.int32), axis=1)
    seq_starts = seq_ends - seq_lengths
    chosen = segment[:, None] == jnp.arange(seq_lengths.shape[0], dtype=jnp.int32)[None, :]
    position = row_ids - jnp.sum(jnp.where(chosen, seq_starts[None, :], 0), axis=1)
    return (segment, position)


def rotary(position, head_width):
    half_width = head_width // 2
    inverse_freq = rope_base ** (-(jnp.arange(half_width, dtype=jnp.float32) * (2.0 / head_width)))
    angles = position.astype(jnp.float32)[:, None] * inverse_freq[None, :]
    return (jnp.cos(angles)[:, None, :], jnp.sin(angles)[:, None, :])


def rotate(values, cosine_table, sine_table):
    half_width = values.shape[-1] // 2
    front_half = values[..., :half_width]
    back_half = values[..., half_width:]
    return jnp.concatenate(
        [
            front_half * cosine_table - back_half * sine_table,
            back_half * cosine_table + front_half * sine_table,
        ],
        axis=-1,
    )


def rotate_back(upstream, cosine_table, sine_table):
    half_width = upstream.shape[-1] // 2
    front_half = upstream[..., :half_width]
    back_half = upstream[..., half_width:]
    return jnp.concatenate(
        [
            front_half * cosine_table + back_half * sine_table,
            back_half * cosine_table - front_half * sine_table,
        ],
        axis=-1,
    )


def slot_table(route_rows, expert_count, capacity):
    row_count = route_rows.shape[0] * route_rows.shape[1]
    flat_routes = route_rows.reshape(row_count)
    expert_hits = (
        flat_routes[:, None] == jnp.arange(expert_count, dtype=jnp.int32)[None, :]
    ).astype(jnp.int32)
    earlier = jnp.cumsum(expert_hits, axis=0) - expert_hits
    slot_index = jnp.sum(earlier * expert_hits, axis=1)
    slot_place = flat_routes * capacity + slot_index
    slot_rows = jnp.full((expert_count * capacity,), row_count, jnp.int32)
    slot_rows = slot_rows.at[slot_place].set(jnp.arange(row_count, dtype=jnp.int32))
    return (slot_place, slot_rows.reshape(expert_count, capacity))


def contract_rows(left, right):
    return lax.dot_general(
        left, right, (((0,), (0,)), ((), ())), preferred_element_type=jnp.float32
    )


def contract_last(left, right):
    return lax.dot_general(
        left, right, (((1,), (1,)), ((), ())), preferred_element_type=jnp.float32
    )


def body(
    tokens,
    lengths,
    routes,
    deal_order,
    cotangent,
    attn_gain,
    query_gain,
    key_gain,
    moe_gain,
    w_query,
    key_projection_matrix,
    value_projection_matrix,
    w_out,
    w_router,
    w_gate,
    w_up,
    w_down,
):
    half_rows = tokens.shape[0]
    model_width = tokens.shape[1]
    head_dim = query_gain.shape[0]
    score_scale = head_dim ** (-0.5)
    fsdp_count = lax.axis_size("fsdp")
    tp_count = lax.axis_size("tp")
    fsdp_index = lax.axis_index("fsdp")
    tp_index = lax.axis_index("tp")
    slice_rows = half_rows // fsdp_count
    group_rows = tp_count * half_rows
    own_start = tp_index * half_rows
    peer_ids = jnp.arange(fsdp_count, dtype=jnp.int32)
    wanted = (peer_ids - fsdp_index) % fsdp_count
    send_pick = jnp.sum(
        jnp.where(deal_order[None, :] == wanted[:, None], peer_ids[None, :], 0), axis=1
    )
    back_pick = (deal_order + fsdp_index) % fsdp_count

    def deal_copies(values):
        slices = jnp.take(values.reshape(fsdp_count, slice_rows, model_width), send_pick, axis=0)
        return jnp.broadcast_to(slices[None], (tp_count, fsdp_count, slice_rows, model_width))

    tokens_all, cotangent_all = (
        lax.all_to_all(
            lax.all_to_all(deal_copies(tokens), "tp", split_axis=0, concat_axis=0, tiled=True),
            "fsdp",
            split_axis=1,
            concat_axis=1,
            tiled=True,
        ),
        lax.all_to_all(
            lax.all_to_all(deal_copies(cotangent), "tp", split_axis=0, concat_axis=0, tiled=True),
            "fsdp",
            split_axis=1,
            concat_axis=1,
            tiled=True,
        ),
    )
    tokens_in = tokens_all.reshape(group_rows, model_width).astype(jnp.float32)
    upstream = cotangent_all.reshape(group_rows, model_width).astype(jnp.float32)
    attn_in, attn_factor = row_norm(tokens_in, attn_gain)
    normed_all = attn_in.astype(jnp.bfloat16)
    query_full, key_full, value_full, out_full = (
        lax.all_gather(w_query, "fsdp", axis=0, tiled=True),
        lax.all_gather(key_projection_matrix, "fsdp", axis=0, tiled=True),
        lax.all_gather(value_projection_matrix, "fsdp", axis=0, tiled=True),
        lax.all_gather(w_out, "fsdp", axis=1, tiled=True),
    )
    query_heads = query_full.shape[1] // head_dim
    kv_heads = key_full.shape[1] // head_dim
    group_size = query_heads // kv_heads
    segment, position = seq_layout(lengths[0], group_rows)
    cosine_table, sine_table = rotary(position, head_dim)
    row_ids = jnp.arange(group_rows)
    allowed = (segment[:, None] == segment[None, :]) & (row_ids[None, :] <= row_ids[:, None])
    query_pre = jnp.dot(normed_all, query_full, preferred_element_type=jnp.float32).reshape(
        group_rows, query_heads, head_dim
    )
    query_normed, query_factor = row_norm(query_pre, query_gain)
    query_low = (
        rotate(query_normed, cosine_table, sine_table)
        .astype(jnp.bfloat16)
        .reshape(group_rows, kv_heads, group_size, head_dim)
    )
    key_before_norm = jnp.dot(normed_all, key_full, preferred_element_type=jnp.float32).reshape(
        group_rows, kv_heads, head_dim
    )
    key_normed, key_factor = row_norm(key_before_norm, key_gain)
    key_low = rotate(key_normed, cosine_table, sine_table).astype(jnp.bfloat16)
    value_low = (
        jnp.dot(normed_all, value_full, preferred_element_type=jnp.float32)
        .astype(jnp.bfloat16)
        .reshape(group_rows, kv_heads, head_dim)
    )
    scores = (
        jnp.einsum("qkgd,tkd->kgqt", query_low, key_low, preferred_element_type=jnp.float32)
        * score_scale
    )
    scores = jnp.where(allowed, scores, masked_score)
    row_peak = jnp.max(scores, axis=-1, keepdims=True)
    exponent = jnp.exp(scores - row_peak)
    totals = jnp.sum(exponent, axis=-1, keepdims=True)
    log_total = row_peak + jnp.log(totals)
    attn_probs = (exponent / totals).astype(jnp.bfloat16)
    attn_mixed = jnp.einsum(
        "kgqt,tkd->qkgd", attn_probs, value_low, preferred_element_type=jnp.float32
    )
    mixed_low = attn_mixed.reshape(group_rows, query_heads * head_dim).astype(jnp.bfloat16)
    attn_part = jnp.dot(mixed_low, out_full, preferred_element_type=jnp.float32)
    residual = tokens_in + lax.psum(attn_part, "tp")
    moe_in, moe_factor = row_norm(residual, moe_gain)
    moe_low = moe_in.astype(jnp.bfloat16)
    logits = jnp.dot(moe_low, w_router, preferred_element_type=jnp.float32)
    experts = w_router.shape[1]
    top_count = routes.shape[1]
    chosen = routes[:, :, None] == jnp.arange(experts, dtype=jnp.int32)[None, None, :]
    selected = jnp.sum(jnp.where(chosen, logits[:, None, :], 0.0), axis=-1)
    gate_peak = jnp.max(selected, axis=-1, keepdims=True)
    gate_exp = jnp.exp(selected - gate_peak)
    gate_probs = gate_exp / jnp.sum(gate_exp, axis=-1, keepdims=True)
    capacity = max(2, 3 * group_rows * top_count // (2 * experts))
    slot_place, slot_rows = slot_table(routes, experts, capacity)
    part_cap = capacity // tp_count
    slot_start = tp_index * part_cap
    gate_full, up_full, down_full = (
        lax.all_gather(w_gate, "tp", axis=2, tiled=True),
        lax.all_gather(w_up, "tp", axis=2, tiled=True),
        lax.all_gather(w_down, "tp", axis=1, tiled=True),
    )
    sent_rows = lax.dynamic_slice_in_dim(slot_rows, slot_start, part_cap, 1)
    slot_expert = slot_place // capacity
    slot_offset = slot_place % capacity - slot_start
    in_half = (slot_offset >= 0) & (slot_offset < part_cap)
    local_place = jnp.where(in_half, slot_expert * part_cap + slot_offset, experts * part_cap)
    padded = jnp.concatenate([moe_low, jnp.zeros((1, model_width), jnp.bfloat16)], axis=0)
    arrived = lax.all_to_all(
        padded[sent_rows // top_count], "fsdp", split_axis=0, concat_axis=0, tiled=True
    )
    local_experts = w_gate.shape[0]
    sources = experts // local_experts
    slot_count = sources * part_cap
    ff_part = w_gate.shape[2]

    def to_experts(values):
        return jnp.transpose(
            values.reshape(sources, local_experts, part_cap, model_width), (1, 0, 2, 3)
        ).reshape(local_experts, slot_count, model_width)

    def to_sources(values):
        width = values.shape[-1]
        return jnp.transpose(
            values.reshape(local_experts, sources, part_cap, width), (1, 0, 2, 3)
        ).reshape(experts, part_cap, width)

    def pick_rows(values):
        flat = values.reshape(experts * part_cap, tp_count * model_width)
        flat = jnp.concatenate([flat, jnp.zeros((1, tp_count * model_width), jnp.bfloat16)], axis=0)
        gathered = flat[local_place].reshape(group_rows, top_count, tp_count, model_width)
        return jnp.sum(gathered.astype(jnp.float32), axis=2)

    expert_rows = to_experts(arrived)
    gate_val = jnp.einsum(
        "esd,edf->esf", expert_rows, gate_full, preferred_element_type=jnp.float32
    )
    up_val = jnp.einsum("esd,edf->esf", expert_rows, up_full, preferred_element_type=jnp.float32)
    sigmoid_val = jax.nn.sigmoid(gate_val)
    swish_val = gate_val * sigmoid_val
    hidden_low = (swish_val * up_val).astype(jnp.bfloat16)
    hidden_blocks = hidden_low.reshape(local_experts, slot_count, tp_count, ff_part)
    down_blocks = down_full.reshape(local_experts, tp_count, ff_part, model_width)
    expert_out = (
        jnp.einsum(
            "esbf,ebfd->esbd", hidden_blocks, down_blocks, preferred_element_type=jnp.float32
        )
        .astype(jnp.bfloat16)
        .reshape(local_experts, slot_count, tp_count * model_width)
    )
    returned = lax.all_to_all(
        to_sources(expert_out), "fsdp", split_axis=0, concat_axis=0, tiled=True
    )
    picked = pick_rows(returned)
    moe_part = jnp.sum(gate_probs[:, :, None] * picked, axis=1)
    gate_grad_part = jnp.sum(upstream[:, None, :] * picked, axis=-1)
    weighted = (
        (gate_probs[:, :, None] * upstream[:, None, :])
        .astype(jnp.bfloat16)
        .reshape(group_rows * top_count, model_width)
    )
    weighted = jnp.concatenate([weighted, jnp.zeros((1, model_width), jnp.bfloat16)], axis=0)
    grad_arrived = lax.all_to_all(
        weighted[sent_rows], "fsdp", split_axis=0, concat_axis=0, tiled=True
    )
    grad_slots = to_experts(grad_arrived)
    hidden_grad = jnp.einsum(
        "esd,ebfd->esbf", grad_slots, down_blocks, preferred_element_type=jnp.float32
    ).reshape(local_experts, slot_count, tp_count * ff_part)
    swish_slope = sigmoid_val * (1.0 + gate_val * (1.0 - sigmoid_val))
    gate_val_grad = (hidden_grad * up_val * swish_slope).astype(jnp.bfloat16)
    up_val_grad = (hidden_grad * swish_val).astype(jnp.bfloat16)
    grad_w_down = jnp.einsum(
        "esbf,esd->ebfd", hidden_blocks, grad_slots, preferred_element_type=jnp.float32
    ).reshape(local_experts, tp_count * ff_part, model_width)
    grad_w_gate = jnp.einsum(
        "esd,esf->edf", expert_rows, gate_val_grad, preferred_element_type=jnp.float32
    )
    grad_w_up = jnp.einsum(
        "esd,esf->edf", expert_rows, up_val_grad, preferred_element_type=jnp.float32
    )
    gate_blocks = gate_full.reshape(local_experts, model_width, tp_count, ff_part)
    up_blocks = up_full.reshape(local_experts, model_width, tp_count, ff_part)
    entry_grad = (
        (
            jnp.einsum(
                "esbf,edbf->esbd",
                gate_val_grad.reshape(local_experts, slot_count, tp_count, ff_part),
                gate_blocks,
                preferred_element_type=jnp.float32,
            )
            + jnp.einsum(
                "esbf,edbf->esbd",
                up_val_grad.reshape(local_experts, slot_count, tp_count, ff_part),
                up_blocks,
                preferred_element_type=jnp.float32,
            )
        )
        .astype(jnp.bfloat16)
        .reshape(local_experts, slot_count, tp_count * model_width)
    )
    sent_back = lax.all_to_all(
        to_sources(entry_grad), "fsdp", split_axis=0, concat_axis=0, tiled=True
    )
    expert_grad = jnp.sum(pick_rows(sent_back), axis=1)
    grad_w_gate, grad_w_up, grad_w_down = (
        lax.psum_scatter(
            grad_w_gate.astype(jnp.bfloat16), "tp", scatter_dimension=2, tiled=True
        ).astype(jnp.float32),
        lax.psum_scatter(
            grad_w_up.astype(jnp.bfloat16), "tp", scatter_dimension=2, tiled=True
        ).astype(jnp.float32),
        lax.psum_scatter(
            grad_w_down.astype(jnp.bfloat16), "tp", scatter_dimension=1, tiled=True
        ).astype(jnp.float32),
    )
    moe_grad, gate_grad = (
        lax.psum(expert_grad.astype(jnp.bfloat16), "tp").astype(jnp.float32),
        lax.psum(gate_grad_part.astype(jnp.bfloat16), "tp").astype(jnp.float32),
    )
    gate_inner = jnp.sum(gate_probs * gate_grad, axis=-1, keepdims=True)
    selected_grad = gate_probs * (gate_grad - gate_inner)
    logit_grad = jnp.sum(jnp.where(chosen, selected_grad[:, :, None], 0.0), axis=1).astype(
        jnp.bfloat16
    )
    moe_grad = moe_grad + contract_last(logit_grad, w_router)
    router_grad = contract_rows(
        lax.dynamic_slice_in_dim(moe_low, own_start, half_rows, 0),
        lax.dynamic_slice_in_dim(logit_grad, own_start, half_rows, 0),
    )
    residual_from_norm, moe_gain_terms = norm_back(residual, moe_factor, moe_gain, moe_grad)
    residual_grad = upstream + residual_from_norm
    moe_gain_grad = jnp.sum(
        lax.dynamic_slice_in_dim(moe_gain_terms, own_start, half_rows, 0), axis=0
    )
    residual_low = residual_grad.astype(jnp.bfloat16)
    mixed_grad = (
        contract_last(residual_low, out_full)
        .astype(jnp.bfloat16)
        .reshape(group_rows, kv_heads, group_size, head_dim)
    )
    grad_w_out = contract_rows(mixed_low, residual_low)
    scores = (
        jnp.einsum("qkgd,tkd->kgqt", query_low, key_low, preferred_element_type=jnp.float32)
        * score_scale
    )
    scores = jnp.where(allowed, scores, masked_score)
    probs_full = jnp.exp(scores - log_total)
    prob_grad = jnp.einsum(
        "qkgd,tkd->kgqt", mixed_grad, value_low, preferred_element_type=jnp.float32
    )
    prob_inner = jnp.sum(probs_full * prob_grad, axis=-1, keepdims=True)
    score_grad = (probs_full * (prob_grad - prob_inner)).astype(jnp.bfloat16)
    query_grad = (
        jnp.einsum(
            "kgqt,tkd->qkgd", score_grad, key_low, preferred_element_type=jnp.float32
        ).reshape(group_rows, query_heads, head_dim)
        * score_scale
    )
    key_grad = (
        jnp.einsum("kgqt,qkgd->tkd", score_grad, query_low, preferred_element_type=jnp.float32)
        * score_scale
    )
    value_grad = (
        jnp.einsum(
            "kgqt,qkgd->tkd",
            probs_full.astype(jnp.bfloat16),
            mixed_grad,
            preferred_element_type=jnp.float32,
        )
        .astype(jnp.bfloat16)
        .reshape(group_rows, kv_heads * head_dim)
    )
    query_pre_grad, query_gain_terms = norm_back(
        query_pre, query_factor, query_gain, rotate_back(query_grad, cosine_table, sine_table)
    )
    key_pre_grad, key_gain_terms = norm_back(
        key_before_norm, key_factor, key_gain, rotate_back(key_grad, cosine_table, sine_table)
    )
    query_pre_low = query_pre_grad.astype(jnp.bfloat16).reshape(group_rows, query_heads * head_dim)
    key_pre_low = key_pre_grad.astype(jnp.bfloat16).reshape(group_rows, kv_heads * head_dim)
    grad_w_query = contract_rows(normed_all, query_pre_low)
    grad_w_key = contract_rows(normed_all, key_pre_low)
    grad_w_value = contract_rows(normed_all, value_grad)
    normed_grad = (
        contract_last(query_pre_low, query_full)
        + contract_last(key_pre_low, key_full)
        + contract_last(value_grad, value_full)
    )
    normed_grad_own, moe_own = (
        lax.psum_scatter(
            normed_grad.astype(jnp.bfloat16), "tp", scatter_dimension=0, tiled=True
        ).astype(jnp.float32),
        lax.psum_scatter(
            moe_part.astype(jnp.bfloat16), "tp", scatter_dimension=0, tiled=True
        ).astype(jnp.float32),
    )
    tokens_own = lax.dynamic_slice_in_dim(tokens_in, own_start, half_rows, 0)
    factor_own = lax.dynamic_slice_in_dim(attn_factor, own_start, half_rows, 0)
    tokens_from_norm, attn_gain_terms = norm_back(
        tokens_own, factor_own, attn_gain, normed_grad_own
    )
    grad_group = lax.dynamic_slice_in_dim(residual_grad, own_start, half_rows, 0) + tokens_from_norm
    residual_own = lax.dynamic_slice_in_dim(residual, own_start, half_rows, 0)
    output_group = (residual_own + moe_own).astype(jnp.bfloat16)
    back_output, back_grad = (
        lax.all_to_all(
            output_group.astype(jnp.float32)
            .reshape(fsdp_count, slice_rows, model_width)
            .astype(jnp.bfloat16),
            "fsdp",
            split_axis=0,
            concat_axis=0,
            tiled=True,
        ).astype(jnp.float32),
        lax.all_to_all(
            grad_group.reshape(fsdp_count, slice_rows, model_width).astype(jnp.bfloat16),
            "fsdp",
            split_axis=0,
            concat_axis=0,
            tiled=True,
        ).astype(jnp.float32),
    )
    output = (
        jnp.take(back_output, back_pick, axis=0)
        .reshape(half_rows, model_width)
        .astype(jnp.bfloat16)
    )
    grad_input = jnp.take(back_grad, back_pick, axis=0).reshape(half_rows, model_width)
    grad_w_query, grad_w_key, grad_w_value, grad_w_out = (
        lax.psum_scatter(grad_w_query, "fsdp", scatter_dimension=0, tiled=True),
        lax.psum_scatter(grad_w_key, "fsdp", scatter_dimension=0, tiled=True),
        lax.psum_scatter(grad_w_value, "fsdp", scatter_dimension=0, tiled=True),
        lax.psum_scatter(grad_w_out, "fsdp", scatter_dimension=1, tiled=True),
    )
    grad_attn_gain, grad_query_gain, grad_key_gain, grad_moe_gain, grad_w_router = lax.psum(
        (
            jnp.sum(attn_gain_terms, axis=0),
            jnp.sum(query_gain_terms, axis=(0, 1)),
            jnp.sum(key_gain_terms, axis=(0, 1)),
            moe_gain_grad,
            router_grad,
        ),
        ("fsdp", "tp"),
    )
    return (
        output,
        grad_input,
        grad_attn_gain,
        grad_query_gain,
        grad_key_gain,
        grad_moe_gain,
        grad_w_query,
        grad_w_key,
        grad_w_value,
        grad_w_out,
        grad_w_router,
        grad_w_gate,
        grad_w_up,
        grad_w_down,
    )


def link_cost(microseconds):
    return pl.CostEstimate(flops=0, bytes_accessed=microseconds * 3_000_000, transcendentals=0)


def remote(src, dst, send_sem, recv_sem, target):
    return pltpu.make_async_remote_copy(
        src_ref=src,
        dst_ref=dst,
        send_sem=send_sem,
        recv_sem=recv_sem,
        device_id=target,
        device_id_type=pl.DeviceIdType.MESH,
    )


def greet(targets):
    barrier = pltpu.get_barrier_semaphore()
    for target in targets:
        pl.semaphore_signal(
            barrier, inc=1, device_id=target, device_id_type=pl.DeviceIdType.MESH
        )
    pl.semaphore_wait(barrier, len(targets))


class Place:
    def __init__(self):
        self.chips = lax.axis_size("chip")
        self.levels = self.chips // 2
        self.chip = lax.axis_index("chip")
        self.core = lax.axis_index("core")
        self.tp = lax.axis_index("tp")
        self.level = self.chip // 2
        self.side = self.chip % 2
        self.fsdp = self.chip * 2 + self.core
        self.mate = {"core": 1 - self.core}
        self.across = {"tp": 1 - self.tp}
        self.beside = {"chip": self.level * 2 + 1 - self.side}
        self.above = {"chip": lax.rem(self.chip + 2, self.chips)}
        self.below = {"chip": lax.rem(self.chip + self.chips - 2, self.chips)}

    def member(self, offset):
        count = 2 * self.chips
        index = lax.rem(self.fsdp + offset + count, count)
        return {"chip": index // 2, "core": lax.rem(index, 2)}, index

    def plane_targets(self):
        return [self.member(offset)[0] for offset in range(1, 2 * self.chips)]

    def ring_targets(self):
        return [self.above, self.below, self.beside]


class PlaneGather:
    def __init__(self, place, views, sems):
        self.place, self.views = place, views
        (
            self.up_send,
            self.up_recv,
            self.down_send,
            self.down_recv,
            self.side_send,
            self.side_recv,
        ) = sems

    @staticmethod
    def semaphores(items, levels):
        return [pltpu.SemaphoreType.DMA((items, levels - 1))] * 4 + [
            pltpu.SemaphoreType.DMA((items, 2 * levels - 1))
        ] * 2

    def _up(self, item, step, origin_level):
        view = self.views[item](origin_level * 2 + self.place.side)
        return remote(
            view, view, self.up_send.at[item, step], self.up_recv.at[item, step], self.place.above
        )

    def _down(self, item, step, origin_level):
        view = self.views[item](origin_level * 2 + self.place.side)
        return remote(
            view,
            view,
            self.down_send.at[item, step],
            self.down_recv.at[item, step],
            self.place.below,
        )

    def _side(self, item, slot, origin_level, own_side):
        side = self.place.side if own_side else 1 - self.place.side
        view = self.views[item](origin_level * 2 + side)
        return remote(
            view,
            view,
            self.side_send.at[item, slot],
            self.side_recv.at[item, slot],
            self.place.beside,
        )

    def start(self, item):
        place = self.place
        level, top = place.level, place.levels - 1

        @pl.when(level < top)
        def _():
            self._up(item, 0, level).start()

        @pl.when(level > 0)
        def _():
            self._down(item, 0, level).start()

        self._side(item, 0, level, True).start()

    def step(self, item, step):
        place = self.place
        level, top = place.level, place.levels - 1

        @pl.when(level >= step + 1)
        def _():
            origin = level - 1 - step
            self._up(item, step, origin).wait_recv()
            if step + 1 < top:

                @pl.when(level < top)
                def _():
                    self._up(item, step + 1, origin).start()

            self._side(item, 1 + 2 * step, origin, True).start()

        @pl.when(level + step + 1 <= top)
        def _():
            origin = level + 1 + step
            self._down(item, step, origin).wait_recv()
            if step + 1 < top:

                @pl.when(level > 0)
                def _():
                    self._down(item, step + 1, origin).start()

            self._side(item, 2 + 2 * step, origin, True).start()

    def finish_side(self, item, slot):
        place = self.place
        level, top = place.level, place.levels - 1
        if slot == 0:
            self._side(item, 0, level, False).wait_recv()
        elif slot % 2 == 1:
            step = slot // 2

            @pl.when(level >= step + 1)
            def _():
                self._side(item, slot, level - 1 - step, False).wait_recv()

        else:
            step = slot // 2 - 1

            @pl.when(level + step + 1 <= top)
            def _():
                self._side(item, slot, level + 1 + step, False).wait_recv()

    def drain(self, item):
        place = self.place
        level, top = place.level, place.levels - 1
        self._side(item, 0, level, True).wait_send()
        for step in range(top):

            @pl.when((level < top) & (level >= step))
            def _():
                self._up(item, step, level - step).wait_send()

            @pl.when((level > 0) & (level + step <= top))
            def _():
                self._down(item, step, level + step).wait_send()

            @pl.when(level >= step + 1)
            def _():
                self._side(item, 1 + 2 * step, level - 1 - step, True).wait_send()

            @pl.when(level + step + 1 <= top)
            def _():
                self._side(item, 2 + 2 * step, level + 1 + step, True).wait_send()


def open_kernel(
    slices_ref,
    gain_ref,
    lengths_ref,
    query_ref,
    key_ref,
    value_ref,
    out_ref,
    gate_ref,
    up_ref,
    dealt_ref,
    normed_ref,
    both_lengths_ref,
    query_all,
    key_all,
    value_all,
    out_all,
    gate_all,
    up_all,
    deal_send,
    deal_recv,
    quad_send,
    quad_recv,
    swap_send,
    swap_recv,
    keep_sem,
    pair_send,
    pair_recv,
    pair_keep,
    *ring_sems,
):
    place = Place()
    core, chip = place.core, place.chip
    own_rows = query_ref.shape[0]
    quarter = query_all.shape[2]
    narrow = key_all.shape[2]
    head_rows = out_all.shape[0]
    lanes = out_ref.shape[1]
    members = 2 * place.chips
    greet(place.plane_targets() + [place.across])

    def deal_copy(offset, sending):
        target, index = place.member(offset if sending else -offset)
        return remote(
            slices_ref.at[index],
            dealt_ref.at[place.fsdp if sending else index],
            deal_send.at[offset - 1],
            deal_recv.at[offset - 1],
            target,
        )

    for offset in range(1, members):
        deal_copy(offset, True).start()

    def rows(who):
        return pl.ds(pl.multiple_of(who * own_rows, own_rows), own_rows)

    def columns(who, width):
        return pl.ds(pl.multiple_of(who * width, width), width)

    def spots(who):
        lane_start = pl.multiple_of((2 * chip + core) * lanes, lanes)
        return [
            (query_ref.at[:, columns(who, quarter)], query_all.at[chip, rows(core)]),
            (key_ref.at[:, columns(who, narrow)], key_all.at[chip, rows(core)]),
            (value_ref.at[:, columns(who, narrow)], value_all.at[chip, rows(core)]),
            (
                out_ref.at[pl.ds(pl.multiple_of(who * head_rows, head_rows), head_rows)],
                out_all.at[:, pl.ds(lane_start, lanes)],
            ),
        ]

    def arrivals():
        lane_start = pl.multiple_of((2 * chip + 1 - core) * lanes, lanes)
        return [
            query_all.at[chip, rows(1 - core)],
            key_all.at[chip, rows(1 - core)],
            value_all.at[chip, rows(1 - core)],
            out_all.at[:, pl.ds(lane_start, lanes)],
        ]

    sends = [
        remote(src, dst, swap_send.at[i], swap_recv.at[i], place.mate)
        for i, (src, dst) in enumerate(spots(1 - core))
    ]
    keeps = [
        pltpu.make_async_copy(src, dst, keep_sem.at[i])
        for i, (src, dst) in enumerate(spots(core))
    ]
    mate_lengths = remote(
        lengths_ref, both_lengths_ref.at[core], swap_send.at[4], swap_recv.at[4], place.mate
    )
    own_lengths = pltpu.make_async_copy(lengths_ref, both_lengths_ref.at[core], keep_sem.at[4])
    own_slice = pltpu.make_async_copy(
        slices_ref.at[place.fsdp], dealt_ref.at[place.fsdp], keep_sem.at[5]
    )
    own_slice.start()
    units = gate_ref.shape[1]

    def halves(who):
        at = pl.ds(pl.multiple_of(who * units, units), units)
        return [gate_all.at[:, at], up_all.at[:, at]]

    shards = (gate_ref, up_ref)
    pair_copies = []
    for i, (src, dst) in enumerate(zip(shards, halves(place.tp))):
        pair_copies.append(
            (
                remote(src, dst, pair_send.at[i], pair_recv.at[i], place.across),
                pltpu.make_async_copy(src, dst, pair_keep.at[i]),
            )
        )
    for i in range(4):
        sends[i].start()
        keeps[i].start()
    mate_lengths.start()
    own_lengths.start()

    out_lanes = 2 * lanes
    ring = PlaneGather(
        place,
        [
            lambda who: query_all.at[who],
            lambda who: key_all.at[who],
            lambda who: value_all.at[who],
            lambda who: out_all.at[
                :, pl.ds(pl.multiple_of(who * out_lanes, out_lanes), out_lanes)
            ],
        ],
        ring_sems,
    )
    landed = arrivals()
    for i in range(4):
        keeps[i].wait()
        sends[i].wait_send()
        remote(landed[i], landed[i], swap_send.at[i], swap_recv.at[i], place.mate).wait_recv()
        ring.start(i)

    own_slice.wait()
    for offset in range(1, members):
        deal_copy(offset, False).wait_recv()
    tp = place.tp
    half = slices_ref.shape[1] // 2
    step_rows = 4
    for start in range(0, members, step_rows):
        x = dealt_ref[start : start + step_rows].astype(jnp.float32)[:, :half]
        x = x.reshape(step_rows * half, x.shape[2])
        factor = lax.rsqrt(jnp.mean(x * x, axis=-1, keepdims=True) + epsilon)
        normed_ref[core, tp, start * half : (start + step_rows) * half, :] = (
            x * factor * gain_ref[...]
        ).astype(jnp.bfloat16)
    mine = normed_ref.at[core, tp]
    to_mate = remote(mine, mine, quad_send.at[0], quad_recv.at[0], place.mate)
    to_across = remote(mine, mine, quad_send.at[1], quad_recv.at[1], place.across)
    to_across.start()
    to_mate.start()
    for both in pair_copies:
        both[0].start()
        both[1].start()
    levels = place.levels
    for i in range(4):
        ring.step(i, 0)
    other = normed_ref.at[core, 1 - tp]
    remote(other, other, quad_send.at[1], quad_recv.at[1], place.across).wait_recv()
    passed = remote(other, other, quad_send.at[2], quad_recv.at[2], place.mate)
    passed.start()
    for step in range(1, levels - 1):
        for i in range(4):
            ring.step(i, step)
    for slot in range(2 * levels - 1):
        for i in range(4):
            ring.finish_side(i, slot)
    for i in range(4):
        ring.drain(i)
    for offset in range(1, members):
        deal_copy(offset, True).wait_send()
    to_mate.wait_send()
    to_across.wait_send()
    passed.wait_send()
    for slot, piece in ((0, normed_ref.at[1 - core, tp]), (2, normed_ref.at[1 - core, 1 - tp])):
        remote(piece, piece, quad_send.at[slot], quad_recv.at[slot], place.mate).wait_recv()
    for i, dst in enumerate(halves(1 - place.tp)):
        pair_copies[i][1].wait()
        pair_copies[i][0].wait_send()
        remote(dst, dst, pair_send.at[i], pair_recv.at[i], place.across).wait_recv()
    own_lengths.wait()
    mate_lengths.wait_send()
    theirs = both_lengths_ref.at[1 - core]
    remote(theirs, theirs, swap_send.at[4], swap_recv.at[4], place.mate).wait_recv()


def open_layer(slices, gain_vec, lengths, w_query, w_key, w_value, w_out, w_gate, w_up):
    members, pack, model_width = slices.shape
    chips = members // 2
    own_rows = w_query.shape[0]
    low = jnp.bfloat16
    vmem = pl.BlockSpec(memory_space=pltpu.VMEM)
    anywhere = pl.BlockSpec(memory_space=pl.ANY)
    dma = pltpu.SemaphoreType.DMA
    return pl.pallas_call(
        open_kernel,
        name="open_layer",
        out_shape=[
            jax.ShapeDtypeStruct(slices.shape, low),
            jax.ShapeDtypeStruct((2, 2, own_rows, model_width), low),
            jax.ShapeDtypeStruct((2,) + lengths.shape, jnp.int32),
            jax.ShapeDtypeStruct((chips, 2 * own_rows, w_query.shape[1] // 2), low),
            jax.ShapeDtypeStruct((chips, 2 * own_rows, w_key.shape[1] // 2), low),
            jax.ShapeDtypeStruct((chips, 2 * own_rows, w_value.shape[1] // 2), low),
            jax.ShapeDtypeStruct((w_out.shape[0] // 2, members * w_out.shape[1]), low),
            jax.ShapeDtypeStruct((model_width, 2 * w_gate.shape[1]), low),
            jax.ShapeDtypeStruct((model_width, 2 * w_up.shape[1]), low),
        ],
        in_specs=[vmem, vmem, vmem] + [anywhere] * 6,
        out_specs=[vmem, vmem, vmem] + [anywhere] * 6,
        scratch_shapes=[
            dma((members - 1,)),
            dma((members - 1,)),
            dma((3,)),
            dma((3,)),
            dma((5,)),
            dma((5,)),
            dma((6,)),
            dma((2,)),
            dma((2,)),
            dma((2,)),
        ]
        + PlaneGather.semaphores(4, chips // 2),
        compiler_params=pltpu.CompilerParams(
            collective_id=0, has_side_effects=True, vmem_limit_bytes=40 << 20
        ),
        cost_estimate=link_cost(110),
    )(slices, gain_vec, lengths, w_query, w_key, w_value, w_out, w_gate, w_up)


def quad_share_kernel(own_ref, all_ref, send, recv, keep_sem):
    place = Place()
    core, tp = place.core, place.tp
    greet([place.mate, place.across])
    to_across = remote(own_ref, all_ref.at[core, tp], send.at[1], recv.at[1], place.across)
    to_mate = remote(own_ref, all_ref.at[core, tp], send.at[0], recv.at[0], place.mate)
    to_across.start()
    to_mate.start()
    keep = pltpu.make_async_copy(own_ref, all_ref.at[core, tp], keep_sem)
    keep.start()
    other = all_ref.at[core, 1 - tp]
    remote(other, other, send.at[1], recv.at[1], place.across).wait_recv()
    passed = remote(other, other, send.at[2], recv.at[2], place.mate)
    passed.start()
    keep.wait()
    to_mate.wait_send()
    to_across.wait_send()
    passed.wait_send()
    for slot, piece in ((0, all_ref.at[1 - core, tp]), (2, all_ref.at[1 - core, 1 - tp])):
        remote(piece, piece, send.at[slot], recv.at[slot], place.mate).wait_recv()


def quad_share(own, collective_id):
    vmem = pl.BlockSpec(memory_space=pltpu.VMEM)
    dma = pltpu.SemaphoreType.DMA
    return pl.pallas_call(
        quad_share_kernel,
        name="quad_share",
        out_shape=jax.ShapeDtypeStruct((2, 2) + own.shape, own.dtype),
        in_specs=[vmem],
        out_specs=vmem,
        scratch_shapes=[dma((3,)), dma((3,)), dma],
        compiler_params=pltpu.CompilerParams(
            collective_id=collective_id, has_side_effects=True, vmem_limit_bytes=16 << 20
        ),
        cost_estimate=link_cost(16),
    )(own)


def quad_sum_kernel(parts_ref, sum_ref, near, far, pair, send, recv):
    place = Place()
    core, tp = place.core, place.tp
    greet([place.mate, place.across])
    to_mate = [
        remote(parts_ref.at[1 - core, half], near.at[half], send.at[half], recv.at[half], place.mate)
        for half in (1 - tp, tp)
    ]
    for copy in to_mate:
        copy.start()
    wide = jnp.float32

    def landed(half):
        return remote(near.at[half], near.at[half], send.at[half], recv.at[half], place.mate)

    landed(1 - tp).wait_recv()
    pair[...] = (
        parts_ref[core, 1 - tp].astype(wide) + near[1 - tp].astype(wide)
    ).astype(jnp.bfloat16)
    to_across = remote(pair, far, send.at[2], recv.at[2], place.across)
    to_across.start()
    landed(tp).wait_recv()
    sum_ref[...] = parts_ref[core, tp].astype(wide) + near[tp].astype(wide)
    to_across.wait_recv()
    sum_ref[...] += far[...].astype(wide)
    for copy in to_mate:
        copy.wait_send()
    to_across.wait_send()


def quad_sum(parts, collective_id):
    _, _, rows, width = parts.shape
    vmem = pl.BlockSpec(memory_space=pltpu.VMEM)
    dma = pltpu.SemaphoreType.DMA
    low = jnp.bfloat16
    return pl.pallas_call(
        quad_sum_kernel,
        name="quad_sum",
        out_shape=jax.ShapeDtypeStruct((rows, width), jnp.float32),
        in_specs=[vmem],
        out_specs=vmem,
        scratch_shapes=[
            pltpu.VMEM((2, rows, width), low),
            pltpu.VMEM((rows, width), low),
            pltpu.VMEM((rows, width), low),
            dma((3,)),
            dma((3,)),
        ],
        compiler_params=pltpu.CompilerParams(
            collective_id=collective_id, has_side_effects=True, vmem_limit_bytes=24 << 20
        ),
        cost_estimate=link_cost(16),
    )(parts)


class PlaneSum:
    def __init__(self, place, parts, side_bufs, up_bufs, down_bufs, sems):
        self.place, self.parts = place, parts
        self.side_bufs, self.up_bufs, self.down_bufs = side_bufs, up_bufs, down_bufs
        (
            self.up_send,
            self.up_recv,
            self.down_send,
            self.down_recv,
            self.side_send,
            self.side_recv,
        ) = sems

    @staticmethod
    def semaphores(items, levels):
        return [pltpu.SemaphoreType.DMA((items, levels))] * 6

    def target(self, turn):
        place = self.place
        far, near = place.levels - 1 - turn // 2, turn // 2
        low_half = [far, near][turn % 2]
        high_half = [near, far][turn % 2]
        upper = place.level // (place.levels // 2)
        return low_half * (1 - upper) + high_half * upper

    def _side(self, item, goal):
        return remote(
            self.parts[item](goal * 2 + 1 - self.place.side),
            self.side_bufs[item].at[goal],
            self.side_send.at[item, goal],
            self.side_recv.at[item, goal],
            self.place.beside,
        )

    def _up(self, item, goal):
        source = self.side_bufs[item].at[goal]
        return remote(
            source,
            self.up_bufs[item].at[goal],
            self.up_send.at[item, goal],
            self.up_recv.at[item, goal],
            self.place.above,
        )

    def _down(self, item, goal):
        source = self.side_bufs[item].at[goal]
        return remote(
            source,
            self.down_bufs[item].at[goal],
            self.down_send.at[item, goal],
            self.down_recv.at[item, goal],
            self.place.below,
        )

    def start(self, item, turn):
        self._side(item, self.target(turn)).start()

    def add(self, item, goal, ref):
        held = self.side_bufs[item]
        held[goal] = (held[goal].astype(jnp.float32) + ref.astype(jnp.float32)).astype(held.dtype)

    def turn(self, item, turn):
        place = self.place
        goal = self.target(turn)
        level, top = place.level, place.levels - 1
        self._side(item, goal).wait_recv()
        self.add(item, goal, self.parts[item](goal * 2 + place.side)[...])

        @pl.when(goal > level)
        def _():
            @pl.when(level > 0)
            def _():
                self._up(item, goal).wait_recv()
                self.add(item, goal, self.up_bufs[item][goal])

            self._up(item, goal).start()

        @pl.when(goal < level)
        def _():
            @pl.when(level < top)
            def _():
                self._down(item, goal).wait_recv()
                self.add(item, goal, self.down_bufs[item][goal])

            self._down(item, goal).start()

    def close(self, item):
        place = self.place
        level, top = place.level, place.levels - 1

        @pl.when(level > 0)
        def _():
            self._up(item, level).wait_recv()
            self.add(item, level, self.up_bufs[item][level])

        @pl.when(level < top)
        def _():
            self._down(item, level).wait_recv()
            self.add(item, level, self.down_bufs[item][level])

    def drain(self, item):
        place = self.place
        for turn in range(place.levels):
            goal = self.target(turn)
            self._side(item, goal).wait_send()

            @pl.when(goal > place.level)
            def _():
                self._up(item, goal).wait_send()

            @pl.when(goal < place.level)
            def _():
                self._down(item, goal).wait_send()


def close_kernel(
    slices_ref,
    gain_ref,
    query_ref,
    key_ref,
    value_ref,
    out_ref,
    gate_ref,
    up_ref,
    down_ref,
    dealt_ref,
    gain_sum_ref,
    query_own,
    key_own,
    value_own,
    out_own,
    gate_arrived,
    up_arrived,
    down_arrived,
    gain_near,
    gain_pair,
    gain_parts,
    *rest,
):
    side_bufs, up_bufs, down_bufs = rest[0:4], rest[4:8], rest[8:12]
    deal_send, deal_recv, gain_send, gain_recv, swap_send, swap_recv, keep_sem = rest[12:19]
    pair_send, pair_recv, total_send, total_recv = rest[19:23]
    place = Place()
    core = place.core
    members = 2 * place.chips
    own_rows = query_own.shape[0]
    lanes = out_own.shape[1]
    greet(place.plane_targets() + [place.across])
    blocks = 2 * own_rows

    def by_rows(ref):
        return lambda chip: ref.at[pl.ds(pl.multiple_of(chip * blocks, blocks), blocks)]

    def by_lanes(ref):
        wide = 2 * lanes
        return lambda chip: ref.at[:, pl.ds(pl.multiple_of(chip * wide, wide), wide)]

    sums = PlaneSum(
        place,
        [by_rows(query_ref), by_rows(key_ref), by_rows(value_ref), by_lanes(out_ref)],
        side_bufs,
        up_bufs,
        down_bufs,
        rest[23:],
    )

    def deal_copy(offset, sending):
        target, index = place.member(offset if sending else -offset)
        return remote(
            slices_ref.at[index],
            dealt_ref.at[place.fsdp if sending else index],
            deal_send.at[offset - 1],
            deal_recv.at[offset - 1],
            target,
        )

    def gain_copy(offset, sending):
        target, index = place.member(offset if sending else -offset)
        return remote(
            gain_pair.at[index],
            gain_parts.at[place.fsdp if sending else index],
            gain_send.at[offset],
            gain_recv.at[offset],
            target,
        )

    def total_copy(offset, sending):
        target, index = place.member(offset if sending else -offset)
        piece = gain_sum_ref.at[place.fsdp if sending else index]
        return remote(piece, piece, total_send.at[offset], total_recv.at[offset], target)

    units = gate_arrived.shape[0]
    pair_copies = []
    for i, (src, dst) in enumerate(
        ((gate_ref, gate_arrived), (up_ref, up_arrived), (down_ref, down_arrived))
    ):
        theirs = src.at[pl.ds(pl.multiple_of((1 - place.tp) * units, units), units)]
        pair_copies.append(remote(theirs, dst, pair_send.at[i], pair_recv.at[i], place.across))
    across = remote(gain_ref, gain_near, gain_send.at[0], gain_recv.at[0], place.across)
    across.start()
    across.wait_recv()
    gain_pair[...] = gain_ref[...] + gain_near[...]
    for offset in range(1, members):
        gain_copy(offset, True).start()
    for copy in pair_copies:
        copy.start()
    for item in (3, 0, 1, 2):
        sums.start(item, 0)
    for offset in range(1, members):
        gain_copy(offset, False).wait_recv()
    gain_parts[place.fsdp] = gain_pair[place.fsdp]
    total = gain_parts[0]
    for member in range(1, members):
        total += gain_parts[member]
    gain_sum_ref[place.fsdp] = total
    for offset in range(1, members):
        total_copy(offset, True).start()
    for offset in range(1, members):
        deal_copy(offset, True).start()
    own_slice = pltpu.make_async_copy(
        slices_ref.at[place.fsdp], dealt_ref.at[place.fsdp], keep_sem
    )
    own_slice.start()
    for item in (3, 0, 1, 2):
        sums.start(item, 1)
    for turn in range(place.levels):
        for item in (3, 0, 1, 2):
            sums.turn(item, turn)
            if turn + 2 < place.levels:
                sums.start(item, turn + 2)

    def rows(who):
        return pl.ds(pl.multiple_of(who * own_rows, own_rows), own_rows)

    def columns(who, width):
        return pl.ds(pl.multiple_of(who * width, width), width)

    head_rows = out_ref.shape[0]
    level = place.level
    spots = []
    for held, own in zip(side_bufs[:3], (query_own, key_own, value_own)):
        width = held.shape[2]
        spots.append(
            (
                held.at[level, rows(core)],
                held.at[level, rows(1 - core)],
                own.at[:, columns(core, width)],
                own.at[:, columns(1 - core, width)],
            )
        )
    held = side_bufs[3]
    spots.append(
        (
            held.at[level, :, columns(core, lanes)],
            held.at[level, :, columns(1 - core, lanes)],
            out_own.at[columns(core, head_rows)],
            out_own.at[columns(1 - core, head_rows)],
        )
    )
    keeps, swaps = {}, {}
    for item in (3, 0, 1, 2):
        sums.close(item)
        mine, theirs, here, there = spots[item]
        keeps[item] = pltpu.make_async_copy(mine, here, keep_sem_of(item, swap_send, 4))
        keeps[item].start()
        swaps[item] = remote(
            theirs, here, swap_send.at[item], swap_recv.at[item], place.mate
        )
        swaps[item].start()
    for item in (3, 0, 1, 2):
        keeps[item].wait()
        swaps[item].wait_send()
        _, _, _, there = spots[item]
        remote(there, there, swap_send.at[item], swap_recv.at[item], place.mate).wait_recv()
        sums.drain(item)
    across.wait_send()
    for copy in pair_copies:
        copy.wait()
    own_slice.wait()
    for offset in range(1, members):
        deal_copy(offset, False).wait_recv()
        deal_copy(offset, True).wait_send()
        gain_copy(offset, True).wait_send()
        total_copy(offset, True).wait_send()
        total_copy(offset, False).wait_recv()


def keep_sem_of(item, sems, start):
    return sems.at[start + item]


def close_layer(
    slices, gain_part, query_grad, key_grad, value_grad, out_grad, gate_grad, up_grad, down_grad
):
    members = slices.shape[0]
    levels = members // 4
    own_rows = query_grad.shape[0] // members
    lanes = out_grad.shape[1] // members
    low = jnp.bfloat16
    vmem = pl.BlockSpec(memory_space=pltpu.VMEM)
    anywhere = pl.BlockSpec(memory_space=pl.ANY)
    dma = pltpu.SemaphoreType.DMA
    blocks = [
        (2 * own_rows, query_grad.shape[1]),
        (2 * own_rows, key_grad.shape[1]),
        (2 * own_rows, value_grad.shape[1]),
        (out_grad.shape[0], 2 * lanes),
    ]
    buffers = [pltpu.VMEM((levels,) + block, low) for block in blocks]
    return pl.pallas_call(
        close_kernel,
        name="close_layer",
        out_shape=[
            jax.ShapeDtypeStruct(slices.shape, low),
            jax.ShapeDtypeStruct(gain_part.shape, jnp.float32),
            jax.ShapeDtypeStruct((own_rows, 2 * query_grad.shape[1]), low),
            jax.ShapeDtypeStruct((own_rows, 2 * key_grad.shape[1]), low),
            jax.ShapeDtypeStruct((own_rows, 2 * value_grad.shape[1]), low),
            jax.ShapeDtypeStruct((2 * out_grad.shape[0], lanes), low),
        ]
        + [
            jax.ShapeDtypeStruct((grad.shape[0] // 2, grad.shape[1]), low)
            for grad in (gate_grad, up_grad, down_grad)
        ],
        in_specs=[vmem] * 6 + [anywhere] * 3,
        out_specs=[vmem] * 6 + [anywhere] * 3,
        scratch_shapes=[
            pltpu.VMEM(gain_part.shape, jnp.float32),
            pltpu.VMEM(gain_part.shape, jnp.float32),
            pltpu.VMEM(gain_part.shape, jnp.float32),
        ]
        + buffers * 3
        + [
            dma((members - 1,)),
            dma((members - 1,)),
            dma((members,)),
            dma((members,)),
            dma((8,)),
            dma((4,)),
            dma,
            dma((3,)),
            dma((3,)),
            dma((members,)),
            dma((members,)),
        ]
        + PlaneSum.semaphores(4, levels),
        compiler_params=pltpu.CompilerParams(
            collective_id=1, has_side_effects=True, vmem_limit_bytes=56 << 20
        ),
        cost_estimate=link_cost(130),
    )(
        slices,
        gain_part,
        query_grad,
        key_grad,
        value_grad,
        out_grad,
        gate_grad,
        up_grad,
        down_grad,
    )


class ChainSum:
    def __init__(self, place, parts, side_buf, up_buf, down_buf, sems):
        self.place, self.parts = place, parts
        self.side_buf, self.up_buf, self.down_buf = side_buf, up_buf, down_buf
        (
            self.up_send,
            self.up_recv,
            self.down_send,
            self.down_recv,
            self.side_send,
            self.side_recv,
        ) = sems

    @staticmethod
    def semaphores(levels):
        return [pltpu.SemaphoreType.DMA((levels,))] * 6

    def target(self, turn):
        place = self.place
        far, near = place.levels - 1 - turn // 2, turn // 2
        odd = turn % 2
        low_half = far * (1 - odd) + near * odd
        high_half = near * (1 - odd) + far * odd
        upper = place.level // (place.levels // 2)
        return low_half * (1 - upper) + high_half * upper

    def side(self, goal):
        return remote(
            self.parts.at[goal * 2 + 1 - self.place.side],
            self.side_buf.at[goal],
            self.side_send.at[goal],
            self.side_recv.at[goal],
            self.place.beside,
        )

    def up(self, goal):
        return remote(
            self.side_buf.at[goal],
            self.up_buf.at[goal],
            self.up_send.at[goal],
            self.up_recv.at[goal],
            self.place.above,
        )

    def down(self, goal):
        return remote(
            self.side_buf.at[goal],
            self.down_buf.at[goal],
            self.down_send.at[goal],
            self.down_recv.at[goal],
            self.place.below,
        )

    def add(self, goal, ref, index):
        held = self.side_buf
        total = held[goal].astype(jnp.float32) + ref[index].astype(jnp.float32)
        held[goal] = total.astype(held.dtype)

    def take_side(self, turn):
        place = self.place
        goal = self.target(turn)
        level, top = place.level, place.levels - 1
        self.side(goal).wait_recv()
        self.add(goal, self.parts, goal * 2 + place.side)

        @pl.when((goal > level) & (level == 0))
        def _():
            self.up(goal).start()

        @pl.when((goal < level) & (level == top))
        def _():
            self.down(goal).start()

    def take_chain(self, turn):
        place = self.place
        goal = self.target(turn)
        level, top = place.level, place.levels - 1

        @pl.when((goal > level) & (level > 0))
        def _():
            self.up(goal).wait_recv()
            self.add(goal, self.up_buf, goal)
            self.up(goal).start()

        @pl.when((goal < level) & (level < top))
        def _():
            self.down(goal).wait_recv()
            self.add(goal, self.down_buf, goal)
            self.down(goal).start()

    def close(self):
        place = self.place
        level, top = place.level, place.levels - 1

        @pl.when(level > 0)
        def _():
            self.up(level).wait_recv()
            self.add(level, self.up_buf, level)

        @pl.when(level < top)
        def _():
            self.down(level).wait_recv()
            self.add(level, self.down_buf, level)

    def drain(self):
        place = self.place

        def turn_done(turn, carry):
            goal = self.target(turn)
            self.side(goal).wait_send()

            @pl.when(goal > place.level)
            def _():
                self.up(goal).wait_send()

            @pl.when(goal < place.level)
            def _():
                self.down(goal).wait_send()

            return carry

        lax.fori_loop(0, place.levels, turn_done, 0)


def expert_kernel(
    experts,
    x_own,
    upstream_ref,
    gate_ref,
    up_ref,
    down_ref,
    entry_own,
    out_part,
    gate_grad_ref,
    up_grad_ref,
    down_grad_ref,
    x_all,
    u_all,
    gate_w,
    up_w,
    down_w,
    hidden,
    gate_val_grad,
    up_val_grad,
    scores,
    sums,
    mate_out,
    mate_in,
    side_buf,
    up_buf,
    down_buf,
    staged,
    load_sem,
    store_sem,
    ring_up_send,
    ring_up_recv,
    ring_down_send,
    ring_down_recv,
    ring_side_send,
    ring_side_recv,
    pass_send,
    pass_recv,
    mate_send,
    mate_recv,
    *sum_sems,
):
    place = Place()
    core, chip, level, side = place.core, place.chip, place.level, place.side
    levels, top = place.levels, place.levels - 1
    rows = x_own.shape[0]
    tile = 2 * rows
    width = upstream_ref.shape[1]
    units = down_ref.shape[0]
    wide = jnp.float32
    low = jnp.bfloat16
    loads = [
        pltpu.make_async_copy(x_own, x_all.at[chip, core], load_sem.at[0]),
        pltpu.make_async_copy(gate_ref, gate_w, load_sem.at[1]),
        pltpu.make_async_copy(up_ref, up_w, load_sem.at[2]),
        pltpu.make_async_copy(down_ref, down_w, load_sem.at[3]),
        pltpu.make_async_copy(upstream_ref, u_all, load_sem.at[4]),
    ]
    for load in loads:
        load.start()
    greet(place.ring_targets() + [place.mate])

    def block(origin):
        return x_all.at[origin, core]

    def climb(origin):
        return remote(
            block(origin),
            block(origin),
            ring_up_send.at[origin // 2],
            ring_up_recv.at[origin // 2],
            place.above,
        )

    def sink(origin):
        return remote(
            block(origin),
            block(origin),
            ring_down_send.at[origin // 2],
            ring_down_recv.at[origin // 2],
            place.below,
        )

    def cross(origin):
        return remote(
            block(origin),
            block(origin),
            ring_side_send.at[origin // 2],
            ring_side_recv.at[origin // 2],
            place.beside,
        )

    def hand(origin, whose):
        piece = x_all.at[origin, whose]
        return remote(piece, piece, pass_send.at[origin], pass_recv.at[origin], place.mate)

    loads[0].wait()

    @pl.when(level < top)
    def _():
        climb(chip).start()

    @pl.when(level > 0)
    def _():
        sink(chip).start()

    cross(chip).start()
    hand(chip, core).start()
    for load in loads[1:]:
        load.wait()

    lane = lax.broadcasted_iota(jnp.int32, (128, 128), 0)
    select = (
        (lane == place.fsdp)
        | (lane == place.fsdp + experts)
        | (lane == place.fsdp + 2 * experts)
    ).astype(low)
    cut = 256
    across_lanes = lax.broadcasted_iota(jnp.int32, (tile, 128), 1)

    def forward_tile(origin):
        x = x_all[origin].reshape(tile, x_all.shape[3])
        gate_lanes = jnp.dot(x[:, width:], select, preferred_element_type=wide)
        gate = jnp.concatenate([gate_lanes] * (cut // 128), axis=1)
        x = x[:, :width]
        start = pl.multiple_of(origin * tile, tile)
        u = u_all[pl.ds(start, tile), :]
        score = jnp.zeros((tile, 1), wide)
        for part in range(units // cut):
            lanes = slice(part * cut, (part + 1) * cut)
            gate_val = jnp.dot(x, gate_w[:, lanes], preferred_element_type=wide)
            up_val = jnp.dot(x, up_w[:, lanes], preferred_element_type=wide)
            back = lax.dot_general(
                u, down_w[lanes, :], (((1,), (1,)), ((), ())), preferred_element_type=wide
            )
            sigmoid = 1.0 / (1.0 + jnp.exp(-gate_val))
            swish = gate_val * sigmoid
            out = (swish * up_val).astype(low).astype(wide)
            score += jnp.sum(out * back, axis=1, keepdims=True)
            back = back * gate
            slope = sigmoid * (1.0 + gate_val * (1.0 - sigmoid))
            hidden[pl.ds(start, tile), lanes] = (out * gate).astype(low)
            gate_val_grad[pl.ds(start, tile), lanes] = (back * up_val * slope).astype(low)
            up_val_grad[pl.ds(start, tile), lanes] = (back * swish).astype(low)
        high = score.astype(low).astype(wide)
        packed = jnp.where(
            across_lanes == place.fsdp,
            high,
            jnp.where(across_lanes == place.fsdp + experts, score - high, 0.0),
        )
        scores[origin] = packed.astype(low)

    def gather_step(n, carry):
        step = n - 1
        under, over = level - n, level + n

        @pl.when((n > 0) & (under >= 0))
        def _():
            origin = under * 2 + side
            climb(origin).wait_recv()

            @pl.when(level < top)
            def _():
                climb(origin).start()

            cross(origin).start()
            hand(origin, core).start()

        @pl.when((n > 0) & (over <= top))
        def _():
            origin = over * 2 + side
            sink(origin).wait_recv()

            @pl.when(level > 0)
            def _():
                sink(origin).start()

            cross(origin).start()
            hand(origin, core).start()

        def crossed(origin_level):
            origin = origin_level * 2 + 1 - side
            cross(origin).wait_recv()
            hand(origin, core).start()

        @pl.when((n > 0) & (level - step >= 0))
        def _():
            crossed(level - step)

        @pl.when((n > 1) & (level + step <= top))
        def _():
            crossed(level + step)

        def candidate(which, carried):
            upward = which % 2
            facing = which // 2
            distance = n - 1 + facing
            at = level + distance * (2 * upward - 1)
            origin = at * 2 + side * facing + (1 - side) * (1 - facing)

            @pl.when(
                (at >= 0) & (at <= top) & (distance >= 0) & ((distance > 0) | (upward == 0))
            )
            def _():
                hand(origin, 1 - core).wait_recv()
                forward_tile(origin)

            return carried

        return lax.fori_loop(0, 4, candidate, carry)

    lax.fori_loop(0, levels + 1, gather_step, 0)

    plane_sum = ChainSum(place, sums, side_buf, up_buf, down_buf, sum_sems)

    def to_mate(goal_chip, slot):
        return remote(
            mate_out.at[slot],
            mate_in.at[goal_chip],
            mate_send.at[slot],
            mate_recv.at[goal_chip],
            place.mate,
        )

    def backward_tile(goal_chip, slot, reuse):
        start = pl.multiple_of(goal_chip * tile, tile)
        own_start = pl.multiple_of(goal_chip * tile + core * rows, rows)
        mate_start = pl.multiple_of(goal_chip * tile + (1 - core) * rows, rows)

        @pl.when(reuse)
        def _():
            to_mate(goal_chip, slot).wait_send()

        grads = gate_val_grad[pl.ds(start, tile), :]
        up_grads = up_val_grad[pl.ds(start, tile), :]
        piece = 512
        for first in range(0, width, piece):
            lanes = slice(first, first + piece)
            whole = lax.dot_general(
                grads, gate_w[lanes, :], (((1,), (1,)), ((), ())), preferred_element_type=wide
            ) + lax.dot_general(
                up_grads, up_w[lanes, :], (((1,), (1,)), ((), ())), preferred_element_type=wide
            )
            halves = whole.astype(low).reshape(2, rows, piece)
            sums[goal_chip, :, lanes] = jnp.where(core == 0, halves[0], halves[1])
            mate_out[slot, :, lanes] = jnp.where(core == 0, halves[1], halves[0])
        sums[goal_chip, :, width:] = scores[goal_chip, pl.ds(pl.multiple_of(core * rows, rows), rows)]
        mate_out[slot, :, width:] = scores[
            goal_chip, pl.ds(pl.multiple_of((1 - core) * rows, rows), rows)
        ]
        to_mate(goal_chip, slot).start()

    def joined(goal_chip, slot):
        to_mate(goal_chip, slot).wait_recv()
        sums[goal_chip] = (
            sums[goal_chip].astype(wide) + mate_in[goal_chip].astype(wide)
        ).astype(low)

    def backward_turn(turn, carry):
        goal = plane_sum.target(turn)
        backward_tile(goal * 2 + 1 - side, 0, turn > 0)
        backward_tile(goal * 2 + side, 1, turn > 0)
        joined(goal * 2 + 1 - side, 0)
        plane_sum.side(goal).start()
        joined(goal * 2 + side, 1)
        return carry

    lax.fori_loop(0, levels, backward_turn, 0)

    def store(target, start, slot):
        return pltpu.make_async_copy(
            staged.at[slot], target.at[pl.ds(start, tile)], store_sem.at[slot]
        )

    def output_tile(origin, carry):
        start = pl.multiple_of(origin * tile, tile)
        slot = origin % 2

        @pl.when(origin > 1)
        def _():
            store(out_part, start, slot).wait()

        left = hidden[pl.ds(start, tile), :]
        for first in range(0, width, 512):
            lanes = slice(first, first + 512)
            staged[slot, :, lanes] = jnp.dot(
                left, down_w[:, lanes], preferred_element_type=wide
            ).astype(low)
        store(out_part, start, slot).start()
        return carry

    def weight_grads(left_ref, right, target):
        def chunk(index, carry):
            start = pl.multiple_of(index * tile, tile)
            slot = index % 2
            store(target, start, slot).wait()
            left = left_ref[:, pl.ds(start, tile)]
            for first in range(0, width, 512):
                lanes = slice(first, first + 512)
                staged[slot, :, lanes] = lax.dot_general(
                    left, right(lanes), (((0,), (0,)), ((), ())), preferred_element_type=wide
                ).astype(low)
            store(target, start, slot).start()
            return carry

        lax.fori_loop(0, units // tile, chunk, 0)

    def x_lanes(lanes):
        return x_all[:, :, :, lanes].reshape(u_all.shape[0], 512)

    def u_lanes(lanes):
        return u_all[:, lanes]

    plane_sum.take_side(0)
    lax.fori_loop(0, place.chips, output_tile, 0)
    plane_sum.take_chain(0)
    plane_sum.take_side(1)
    weight_grads(gate_val_grad, x_lanes, gate_grad_ref)
    plane_sum.take_chain(1)
    plane_sum.take_side(2)
    weight_grads(up_val_grad, x_lanes, up_grad_ref)
    plane_sum.take_chain(2)
    plane_sum.take_side(3)
    weight_grads(hidden, u_lanes, down_grad_ref)
    plane_sum.take_chain(3)
    plane_sum.close()
    entry_own[...] = side_buf[level]
    for slot in range(2):
        store(down_grad_ref, 0, slot).wait()
        to_mate(0, slot).wait_send()
    plane_sum.drain()

    def handed(origin, carry):
        hand(origin, core).wait_send()
        return carry

    lax.fori_loop(0, place.chips, handed, 0)

    def sent(at, carry):
        cross(at * 2 + side).wait_send()

        @pl.when((level < top) & (at <= level))
        def _():
            climb(at * 2 + side).wait_send()

        @pl.when((level > 0) & (at >= level))
        def _():
            sink(at * 2 + side).wait_send()

        return carry

    lax.fori_loop(0, levels, sent, 0)


def expert_layer(x_own, upstream_all, gate_all, up_all, down_all, experts):
    rows, span = x_own.shape
    total, width = upstream_all.shape
    units = down_all.shape[0]
    chips = total // (2 * rows)
    levels = chips // 2
    low = jnp.bfloat16
    vmem = pl.BlockSpec(memory_space=pltpu.VMEM)
    anywhere = pl.BlockSpec(memory_space=pl.ANY)
    dma = pltpu.SemaphoreType.DMA
    return pl.pallas_call(
        functools.partial(expert_kernel, experts),
        name="expert_layer",
        out_shape=[
            jax.ShapeDtypeStruct((rows, span), low),
            jax.ShapeDtypeStruct((total, width), low),
            jax.ShapeDtypeStruct((units, width), low),
            jax.ShapeDtypeStruct((units, width), low),
            jax.ShapeDtypeStruct((units, width), low),
        ],
        in_specs=[vmem] + [anywhere] * 4,
        out_specs=[vmem] + [anywhere] * 4,
        scratch_shapes=[
            pltpu.VMEM((chips, 2, rows, span), low),
            pltpu.VMEM((total, width), low),
            pltpu.VMEM((width, units), low),
            pltpu.VMEM((width, units), low),
            pltpu.VMEM((units, width), low),
            pltpu.VMEM((total, units), low),
            pltpu.VMEM((total, units), low),
            pltpu.VMEM((total, units), low),
            pltpu.VMEM((chips, 2 * rows, 128), low),
            pltpu.VMEM((chips, rows, span), low),
            pltpu.VMEM((2, rows, span), low),
            pltpu.VMEM((chips, rows, span), low),
            pltpu.VMEM((levels, rows, span), low),
            pltpu.VMEM((levels, rows, span), low),
            pltpu.VMEM((levels, rows, span), low),
            pltpu.VMEM((2, 2 * rows, width), low),
            dma((5,)),
            dma((2,)),
        ]
        + [dma((levels,))] * 6
        + [dma((chips,)), dma((chips,)), dma((2,)), dma((chips,))]
        + ChainSum.semaphores(levels),
        compiler_params=pltpu.CompilerParams(
            collective_id=5, has_side_effects=True, vmem_limit_bytes=63 << 20
        ),
        cost_estimate=link_cost(125),
    )(x_own, upstream_all, gate_all, up_all, down_all)


def fast_body(
    tokens,
    lengths,
    routes,
    deal_order,
    cotangent,
    attn_gain,
    query_gain,
    key_gain,
    moe_gain,
    w_query,
    key_projection_matrix,
    value_projection_matrix,
    w_out,
    w_router,
    w_gate,
    w_up,
    w_down,
):
    own_rows, model_width = tokens.shape
    head_dim = query_gain.shape[0]
    score_scale = head_dim ** (-0.5)
    chip_count = lax.axis_size("chip")
    core_count = lax.axis_size("core")
    tp_count = lax.axis_size("tp")
    core_index = lax.axis_index("core")
    tp_index = lax.axis_index("tp")
    fsdp_count = chip_count * core_count
    fsdp_index = lax.axis_index("chip") * core_count + core_index
    slice_rows = own_rows // fsdp_count
    group_rows = tp_count * own_rows
    quad_rows = core_count * group_rows
    plane = ("chip", "core")
    quad = ("core", "tp")
    peer_ids = jnp.arange(fsdp_count, dtype=jnp.int32)
    wanted = (peer_ids - fsdp_index) % fsdp_count
    send_pick = jnp.sum(
        jnp.where(deal_order[None, :] == wanted[:, None], peer_ids[None, :], 0), axis=1
    )
    back_pick = (deal_order + fsdp_index) % fsdp_count

    def slices_of(values):
        return values.reshape(fsdp_count, slice_rows, model_width)

    def two_of(dealt):
        return (
            dealt[:, :slice_rows].reshape(own_rows, model_width),
            dealt[:, slice_rows:].reshape(own_rows, model_width),
        )

    outgoing = jnp.take(
        jnp.concatenate([slices_of(tokens), slices_of(cotangent)], axis=1), send_pick, axis=0
    )
    down_full = lax.all_gather(w_down[0], "tp", axis=0, tiled=True)
    padded_lengths = jnp.pad(lengths, ((0, 7), (0, 128 - lengths.shape[1])))
    (
        dealt,
        normed,
        quad_lengths,
        query_part,
        key_part,
        value_part,
        out_part,
        gate_full,
        up_full,
    ) = open_layer(
        outgoing,
        attn_gain[None, :],
        padded_lengths,
        w_query,
        key_projection_matrix,
        value_projection_matrix,
        w_out,
        w_gate[0],
        w_up[0],
    )
    quad_lengths = quad_lengths[:, 0, : lengths.shape[1]]
    normed = normed.reshape(quad_rows, model_width)
    query_part = query_part.reshape(model_width, -1)
    key_part = key_part.reshape(model_width, -1)
    value_part = value_part.reshape(model_width, -1)
    tokens_low, upstream_low = two_of(dealt)
    tokens_own = tokens_low.astype(jnp.float32)
    upstream_all = lax.all_gather(upstream_low, plane, axis=0, tiled=True)
    upstream = upstream_low.astype(jnp.float32)
    attn_factor = row_norm(tokens_own, attn_gain)[1]
    heads = query_part.shape[1] // head_dim
    segment, position = jax.vmap(lambda own: seq_layout(own, group_rows))(quad_lengths)
    cosine_table, sine_table = rotary(position.reshape(quad_rows), head_dim)
    row_ids = jnp.arange(group_rows)
    allowed = (segment[:, :, None] == segment[:, None, :]) & (
        row_ids[None, None, :] <= row_ids[None, :, None]
    )
    allowed = allowed[:, None]

    def by_owner(parts):
        return parts.astype(jnp.bfloat16).reshape(core_count, tp_count, own_rows, model_width)

    def split_groups(values):
        return values.reshape((core_count, group_rows) + values.shape[1:])

    query_pre = jnp.dot(normed, query_part, preferred_element_type=jnp.float32).reshape(
        quad_rows, heads, head_dim
    )
    query_normed, query_factor = row_norm(query_pre, query_gain)
    query_low = split_groups(rotate(query_normed, cosine_table, sine_table).astype(jnp.bfloat16))
    key_before_norm = jnp.dot(normed, key_part, preferred_element_type=jnp.float32).reshape(
        quad_rows, 1, head_dim
    )
    key_normed, key_factor = row_norm(key_before_norm, key_gain)
    key_low = split_groups(
        rotate(key_normed, cosine_table, sine_table).astype(jnp.bfloat16)[:, 0]
    )
    value_low = split_groups(
        jnp.dot(normed, value_part, preferred_element_type=jnp.float32).astype(jnp.bfloat16)
    )
    scores = (
        jnp.einsum("bqgd,btd->bgqt", query_low, key_low, preferred_element_type=jnp.float32)
        * score_scale
    )
    scores = jnp.where(allowed, scores, masked_score)
    row_peak = jnp.max(scores, axis=-1, keepdims=True)
    exponent = jnp.exp(scores - row_peak)
    probs_full = exponent / jnp.sum(exponent, axis=-1, keepdims=True)
    probs_low = probs_full.astype(jnp.bfloat16)
    mixed_low = (
        jnp.einsum("bgqt,btd->bqgd", probs_low, value_low, preferred_element_type=jnp.float32)
        .reshape(quad_rows, heads * head_dim)
        .astype(jnp.bfloat16)
    )
    attn_out = jnp.dot(mixed_low, out_part, preferred_element_type=jnp.float32)
    residual = tokens_own + quad_sum(by_owner(attn_out), 2)
    moe_in, moe_factor = row_norm(residual, moe_gain)
    moe_low = moe_in.astype(jnp.bfloat16)
    logits = jnp.dot(moe_low, w_router, preferred_element_type=jnp.float32)
    experts = w_router.shape[1]
    own_routes = lax.dynamic_slice_in_dim(routes, tp_index * own_rows, own_rows, 0)
    chosen = jnp.any(
        own_routes[:, :, None] == jnp.arange(experts, dtype=jnp.int32)[None, None, :], axis=1
    )
    gate_peak = jnp.max(jnp.where(chosen, logits, -jnp.inf), axis=-1, keepdims=True)
    gate_exp = jnp.where(chosen, jnp.exp(jnp.minimum(logits - gate_peak, 0.0)), 0.0)
    gates = gate_exp / jnp.sum(gate_exp, axis=-1, keepdims=True)
    gate_high = gates.astype(jnp.bfloat16)
    gate_left = gates - gate_high.astype(jnp.float32)
    gate_mid = gate_left.astype(jnp.bfloat16)
    gate_low = (gate_left - gate_mid.astype(jnp.float32)).astype(jnp.bfloat16)
    spare = jnp.zeros((own_rows, 128 - 3 * experts), jnp.bfloat16)
    moe_ext = jnp.concatenate([moe_low, gate_high, gate_mid, gate_low, spare], axis=1)
    entry_ext, moe_out, grad_w_gate, grad_w_up, grad_w_down = expert_layer(
        moe_ext, upstream_all, gate_full, up_full, down_full, experts
    )
    entry_ext = entry_ext.astype(jnp.float32)
    entry_own = entry_ext[:, :model_width]
    gate_grad = (
        entry_ext[:, model_width : model_width + experts]
        + entry_ext[:, model_width + experts : model_width + 2 * experts]
    )
    moe_own = lax.psum_scatter(moe_out, plane, scatter_dimension=0, tiled=True).astype(
        jnp.float32
    )
    gate_inner = jnp.sum(gates * gate_grad, axis=-1, keepdims=True)
    logit_grad = (gates * (gate_grad - gate_inner)).astype(jnp.bfloat16)
    moe_grad = entry_own + contract_last(logit_grad, w_router)
    router_grad = contract_rows(moe_low, logit_grad)
    residual_from_norm, moe_gain_terms = norm_back(residual, moe_factor, moe_gain, moe_grad)
    residual_grad = upstream + residual_from_norm
    residual_low = quad_share(residual_grad.astype(jnp.bfloat16), 3).reshape(
        quad_rows, model_width
    )
    mixed_grad = split_groups(
        contract_last(residual_low, out_part)
        .astype(jnp.bfloat16)
        .reshape(quad_rows, heads, head_dim)
    )
    grad_w_out = contract_rows(mixed_low, residual_low)
    prob_grad = jnp.einsum(
        "bqgd,btd->bgqt", mixed_grad, value_low, preferred_element_type=jnp.float32
    )
    prob_inner = jnp.sum(probs_full * prob_grad, axis=-1, keepdims=True)
    score_grad = (probs_full * (prob_grad - prob_inner)).astype(jnp.bfloat16)
    query_grad = (
        jnp.einsum(
            "bgqt,btd->bqgd", score_grad, key_low, preferred_element_type=jnp.float32
        ).reshape(quad_rows, heads, head_dim)
        * score_scale
    )
    key_grad = (
        jnp.einsum("bgqt,bqgd->btd", score_grad, query_low, preferred_element_type=jnp.float32)
        * score_scale
    ).reshape(quad_rows, 1, head_dim)
    value_grad = (
        jnp.einsum("bgqt,bqgd->btd", probs_low, mixed_grad, preferred_element_type=jnp.float32)
        .astype(jnp.bfloat16)
        .reshape(quad_rows, head_dim)
    )
    query_pre_grad, query_gain_terms = norm_back(
        query_pre, query_factor, query_gain, rotate_back(query_grad, cosine_table, sine_table)
    )
    key_pre_grad, key_gain_terms = norm_back(
        key_before_norm, key_factor, key_gain, rotate_back(key_grad, cosine_table, sine_table)
    )
    query_pre_low = query_pre_grad.astype(jnp.bfloat16).reshape(quad_rows, heads * head_dim)
    key_pre_low = key_pre_grad.astype(jnp.bfloat16).reshape(quad_rows, head_dim)
    grad_w_query = contract_rows(normed, query_pre_low)
    grad_w_key = contract_rows(normed, key_pre_low)
    grad_w_value = contract_rows(normed, value_grad)
    normed_grad = (
        contract_last(query_pre_low, query_part)
        + contract_last(key_pre_low, key_part)
        + contract_last(value_grad, value_part)
    )
    normed_grad_own = quad_sum(by_owner(normed_grad), 4)
    moe_own, normed_grad_own = lax.optimization_barrier((moe_own, normed_grad_own))
    tokens_from_norm, attn_gain_terms = norm_back(
        tokens_own, attn_factor, attn_gain, normed_grad_own
    )
    finished = jnp.concatenate(
        [
            slices_of((residual + moe_own).astype(jnp.bfloat16)),
            slices_of((residual_grad + tokens_from_norm).astype(jnp.bfloat16)),
        ],
        axis=1,
    )
    small = jnp.concatenate(
        [
            jnp.sum(attn_gain_terms, axis=0),
            jnp.sum(moe_gain_terms, axis=0),
            jnp.sum(query_gain_terms, axis=(0, 1)),
            jnp.sum(key_gain_terms, axis=(0, 1)),
            router_grad.reshape(-1),
        ]
    )
    small_rows = -(-small.shape[0] // (fsdp_count * 8 * 128)) * 8
    small = jnp.pad(small, (0, fsdp_count * small_rows * 128 - small.shape[0]))
    (
        returned,
        small,
        grad_w_query,
        grad_w_key,
        grad_w_value,
        grad_w_out,
        gate_arrived,
        up_arrived,
        down_arrived,
    ) = close_layer(
        finished,
        small.reshape(fsdp_count, small_rows, 128),
        grad_w_query.astype(jnp.bfloat16),
        grad_w_key.astype(jnp.bfloat16),
        grad_w_value.astype(jnp.bfloat16),
        grad_w_out.astype(jnp.bfloat16),
        grad_w_gate,
        grad_w_up,
        grad_w_down,
    )

    def pair_sum(parts, arrived):
        mine = lax.dynamic_slice_in_dim(parts, tp_index * arrived.shape[0], arrived.shape[0], 0)
        return mine.astype(jnp.float32) + arrived.astype(jnp.float32)

    output, grad_input = two_of(jnp.take(returned, back_pick, axis=0))
    grad_input = grad_input.astype(jnp.float32)
    bounds = [model_width, 2 * model_width, 2 * model_width + head_dim]
    bounds += [bounds[2] + head_dim, bounds[2] + head_dim + router_grad.size]
    grad_attn_gain, grad_moe_gain, grad_query_gain, grad_key_gain, grad_w_router, _ = jnp.split(
        small.reshape(-1), bounds
    )
    grad_w_router = grad_w_router.reshape(model_width, experts)
    return (
        output,
        grad_input,
        grad_attn_gain,
        grad_query_gain,
        grad_key_gain,
        grad_moe_gain,
        grad_w_query.astype(jnp.float32),
        grad_w_key.astype(jnp.float32),
        grad_w_value.astype(jnp.float32),
        grad_w_out.astype(jnp.float32),
        grad_w_router,
        pair_sum(grad_w_gate, gate_arrived).T[None],
        pair_sum(grad_w_up, up_arrived).T[None],
        pair_sum(grad_w_down, down_arrived)[None],
    )


def solution(mesh):
    fsdp_count, tp_count = mesh.shape["fsdp"], mesh.shape["tp"]
    chips = Mesh(mesh.devices.reshape(fsdp_count // 2, 2, tp_count), ("chip", "core", "tp"))
    dense = fsdp_count <= 16
    fsdp = ("chip", "core") if dense else "fsdp"
    every = ("chip", "core", "tp") if dense else ("fsdp", "tp")
    return jax.shard_map(
        fast_body if dense else body,
        mesh=chips if dense else mesh,
        in_specs=(
            P(every, None),
            P(fsdp, None),
            P(fsdp, None),
            P(),
            P(every, None),
            P(),
            P(),
            P(),
            P(),
            P(fsdp, "tp"),
            P(fsdp, "tp"),
            P(fsdp, "tp"),
            P("tp", fsdp),
            P(),
            P(fsdp, None, "tp"),
            P(fsdp, None, "tp"),
            P(fsdp, "tp", None),
        ),
        out_specs=(
            P(every, None),
            P(every, None),
            P(),
            P(),
            P(),
            P(),
            P(fsdp, "tp"),
            P(fsdp, "tp"),
            P(fsdp, "tp"),
            P("tp", fsdp),
            P(),
            P(fsdp, None, "tp"),
            P(fsdp, None, "tp"),
            P(fsdp, "tp", None),
        ),
        check_vma=False,
    )
```

```python
import functools

import jax
import jax.numpy as jnp
from jax import lax
from jax.experimental import pallas as pl
from jax.experimental.pallas import tpu as pltpu
from jax.sharding import Mesh
from jax.sharding import PartitionSpec as P

epsilon = 1e-06
rope_base = 1000000.0
masked_score = -1e30


def row_norm(values, gain_vec):
    factor = lax.rsqrt(jnp.mean(values * values, axis=-1, keepdims=True) + epsilon)
    return (values * factor * gain_vec, factor)


def norm_back(values, factor, gain_vec, upstream):
    scaled = upstream * gain_vec
    inner_term = jnp.mean(scaled * values, axis=-1, keepdims=True)
    return (factor * (scaled - values * (factor * factor) * inner_term), upstream * values * factor)


def seq_layout(seq_lengths, row_count):
    seq_ends = jnp.cumsum(seq_lengths)
    row_ids = jnp.arange(row_count, dtype=jnp.int32)
    segment = jnp.sum((row_ids[:, None] >= seq_ends[None, :]).astype(jnp.int32), axis=1)
    seq_starts = seq_ends - seq_lengths
    chosen = segment[:, None] == jnp.arange(seq_lengths.shape[0], dtype=jnp.int32)[None, :]
    position = row_ids - jnp.sum(jnp.where(chosen, seq_starts[None, :], 0), axis=1)
    return (segment, position)


def rotary(position, head_width):
    half_width = head_width // 2
    inverse_freq = rope_base ** (-(jnp.arange(half_width, dtype=jnp.float32) * (2.0 / head_width)))
    angles = position.astype(jnp.float32)[:, None] * inverse_freq[None, :]
    return (jnp.cos(angles)[:, None, :], jnp.sin(angles)[:, None, :])


def rotate(values, cosine_table, sine_table):
    half_width = values.shape[-1] // 2
    front_half = values[..., :half_width]
    back_half = values[..., half_width:]
    return jnp.concatenate(
        [
            front_half * cosine_table - back_half * sine_table,
            back_half * cosine_table + front_half * sine_table,
        ],
        axis=-1,
    )


def rotate_back(upstream, cosine_table, sine_table):
    half_width = upstream.shape[-1] // 2
    front_half = upstream[..., :half_width]
    back_half = upstream[..., half_width:]
    return jnp.concatenate(
        [
            front_half * cosine_table + back_half * sine_table,
            back_half * cosine_table - front_half * sine_table,
        ],
        axis=-1,
    )


def slot_table(route_rows, expert_count, capacity):
    row_count = route_rows.shape[0] * route_rows.shape[1]
    flat_routes = route_rows.reshape(row_count)
    expert_hits = (
        flat_routes[:, None] == jnp.arange(expert_count, dtype=jnp.int32)[None, :]
    ).astype(jnp.int32)
    earlier = jnp.cumsum(expert_hits, axis=0) - expert_hits
    slot_index = jnp.sum(earlier * expert_hits, axis=1)
    slot_place = flat_routes * capacity + slot_index
    slot_rows = jnp.full((expert_count * capacity,), row_count, jnp.int32)
    slot_rows = slot_rows.at[slot_place].set(jnp.arange(row_count, dtype=jnp.int32))
    return (slot_place, slot_rows.reshape(expert_count, capacity))


def contract_rows(left, right):
    return lax.dot_general(
        left, right, (((0,), (0,)), ((), ())), preferred_element_type=jnp.float32
    )


def contract_last(left, right):
    return lax.dot_general(
        left, right, (((1,), (1,)), ((), ())), preferred_element_type=jnp.float32
    )


def body(
    tokens,
    lengths,
    routes,
    deal_order,
    cotangent,
    attn_gain,
    query_gain,
    key_gain,
    moe_gain,
    w_query,
    key_projection_matrix,
    value_projection_matrix,
    w_out,
    w_router,
    w_gate,
    w_up,
    w_down,
):
    half_rows = tokens.shape[0]
    model_width = tokens.shape[1]
    head_dim = query_gain.shape[0]
    score_scale = head_dim ** (-0.5)
    fsdp_count = lax.axis_size("fsdp")
    tp_count = lax.axis_size("tp")
    fsdp_index = lax.axis_index("fsdp")
    tp_index = lax.axis_index("tp")
    slice_rows = half_rows // fsdp_count
    group_rows = tp_count * half_rows
    own_start = tp_index * half_rows
    peer_ids = jnp.arange(fsdp_count, dtype=jnp.int32)
    wanted = (peer_ids - fsdp_index) % fsdp_count
    send_pick = jnp.sum(
        jnp.where(deal_order[None, :] == wanted[:, None], peer_ids[None, :], 0), axis=1
    )
    back_pick = (deal_order + fsdp_index) % fsdp_count

    def deal_copies(values):
        slices = jnp.take(values.reshape(fsdp_count, slice_rows, model_width), send_pick, axis=0)
        return jnp.broadcast_to(slices[None], (tp_count, fsdp_count, slice_rows, model_width))

    tokens_all, cotangent_all = (
        lax.all_to_all(
            lax.all_to_all(deal_copies(tokens), "tp", split_axis=0, concat_axis=0, tiled=True),
            "fsdp",
            split_axis=1,
            concat_axis=1,
            tiled=True,
        ),
        lax.all_to_all(
            lax.all_to_all(deal_copies(cotangent), "tp", split_axis=0, concat_axis=0, tiled=True),
            "fsdp",
            split_axis=1,
            concat_axis=1,
            tiled=True,
        ),
    )
    tokens_in = tokens_all.reshape(group_rows, model_width).astype(jnp.float32)
    upstream = cotangent_all.reshape(group_rows, model_width).astype(jnp.float32)
    attn_in, attn_factor = row_norm(tokens_in, attn_gain)
    normed_all = attn_in.astype(jnp.bfloat16)
    query_full, key_full, value_full, out_full = (
        lax.all_gather(w_query, "fsdp", axis=0, tiled=True),
        lax.all_gather(key_projection_matrix, "fsdp", axis=0, tiled=True),
        lax.all_gather(value_projection_matrix, "fsdp", axis=0, tiled=True),
        lax.all_gather(w_out, "fsdp", axis=1, tiled=True),
    )
    query_heads = query_full.shape[1] // head_dim
    kv_heads = key_full.shape[1] // head_dim
    group_size = query_heads // kv_heads
    segment, position = seq_layout(lengths[0], group_rows)
    cosine_table, sine_table = rotary(position, head_dim)
    row_ids = jnp.arange(group_rows)
    allowed = (segment[:, None] == segment[None, :]) & (row_ids[None, :] <= row_ids[:, None])
    query_pre = jnp.dot(normed_all, query_full, preferred_element_type=jnp.float32).reshape(
        group_rows, query_heads, head_dim
    )
    query_normed, query_factor = row_norm(query_pre, query_gain)
    query_low = (
        rotate(query_normed, cosine_table, sine_table)
        .astype(jnp.bfloat16)
        .reshape(group_rows, kv_heads, group_size, head_dim)
    )
    key_before_norm = jnp.dot(normed_all, key_full, preferred_element_type=jnp.float32).reshape(
        group_rows, kv_heads, head_dim
    )
    key_normed, key_factor = row_norm(key_before_norm, key_gain)
    key_low = rotate(key_normed, cosine_table, sine_table).astype(jnp.bfloat16)
    value_low = (
        jnp.dot(normed_all, value_full, preferred_element_type=jnp.float32)
        .astype(jnp.bfloat16)
        .reshape(group_rows, kv_heads, head_dim)
    )
    scores = (
        jnp.einsum("qkgd,tkd->kgqt", query_low, key_low, preferred_element_type=jnp.float32)
        * score_scale
    )
    scores = jnp.where(allowed, scores, masked_score)
    row_peak = jnp.max(scores, axis=-1, keepdims=True)
    exponent = jnp.exp(scores - row_peak)
    totals = jnp.sum(exponent, axis=-1, keepdims=True)
    log_total = row_peak + jnp.log(totals)
    attn_probs = (exponent / totals).astype(jnp.bfloat16)
    attn_mixed = jnp.einsum(
        "kgqt,tkd->qkgd", attn_probs, value_low, preferred_element_type=jnp.float32
    )
    mixed_low = attn_mixed.reshape(group_rows, query_heads * head_dim).astype(jnp.bfloat16)
    attn_part = jnp.dot(mixed_low, out_full, preferred_element_type=jnp.float32)
    residual = tokens_in + lax.psum(attn_part, "tp")
    moe_in, moe_factor = row_norm(residual, moe_gain)
    moe_low = moe_in.astype(jnp.bfloat16)
    logits = jnp.dot(moe_low, w_router, preferred_element_type=jnp.float32)
    experts = w_router.shape[1]
    top_count = routes.shape[1]
    chosen = routes[:, :, None] == jnp.arange(experts, dtype=jnp.int32)[None, None, :]
    selected = jnp.sum(jnp.where(chosen, logits[:, None, :], 0.0), axis=-1)
    gate_peak = jnp.max(selected, axis=-1, keepdims=True)
    gate_exp = jnp.exp(selected - gate_peak)
    gate_probs = gate_exp / jnp.sum(gate_exp, axis=-1, keepdims=True)
    capacity = max(2, 3 * group_rows * top_count // (2 * experts))
    slot_place, slot_rows = slot_table(routes, experts, capacity)
    part_cap = capacity // tp_count
    slot_start = tp_index * part_cap
    gate_full, up_full, down_full = (
        lax.all_gather(w_gate, "tp", axis=2, tiled=True),
        lax.all_gather(w_up, "tp", axis=2, tiled=True),
        lax.all_gather(w_down, "tp", axis=1, tiled=True),
    )
    sent_rows = lax.dynamic_slice_in_dim(slot_rows, slot_start, part_cap, 1)
    slot_expert = slot_place // capacity
    slot_offset = slot_place % capacity - slot_start
    in_half = (slot_offset >= 0) & (slot_offset < part_cap)
    local_place = jnp.where(in_half, slot_expert * part_cap + slot_offset, experts * part_cap)
    padded = jnp.concatenate([moe_low, jnp.zeros((1, model_width), jnp.bfloat16)], axis=0)
    arrived = lax.all_to_all(
        padded[sent_rows // top_count], "fsdp", split_axis=0, concat_axis=0, tiled=True
    )
    local_experts = w_gate.shape[0]
    sources = experts // local_experts
    slot_count = sources * part_cap
    ff_part = w_gate.shape[2]

    def to_experts(values):
        return jnp.transpose(
            values.reshape(sources, local_experts, part_cap, model_width), (1, 0, 2, 3)
        ).reshape(local_experts, slot_count, model_width)

    def to_sources(values):
        width = values.shape[-1]
        return jnp.transpose(
            values.reshape(local_experts, sources, part_cap, width), (1, 0, 2, 3)
        ).reshape(experts, part_cap, width)

    def pick_rows(values):
        flat = values.reshape(experts * part_cap, tp_count * model_width)
        flat = jnp.concatenate([flat, jnp.zeros((1, tp_count * model_width), jnp.bfloat16)], axis=0)
        gathered = flat[local_place].reshape(group_rows, top_count, tp_count, model_width)
        return jnp.sum(gathered.astype(jnp.float32), axis=2)

    expert_rows = to_experts(arrived)
    gate_val = jnp.einsum(
        "esd,edf->esf", expert_rows, gate_full, preferred_element_type=jnp.float32
    )
    up_val = jnp.einsum("esd,edf->esf", expert_rows, up_full, preferred_element_type=jnp.float32)
    sigmoid_val = jax.nn.sigmoid(gate_val)
    swish_val = gate_val * sigmoid_val
    hidden_low = (swish_val * up_val).astype(jnp.bfloat16)
    hidden_blocks = hidden_low.reshape(local_experts, slot_count, tp_count, ff_part)
    down_blocks = down_full.reshape(local_experts, tp_count, ff_part, model_width)
    expert_out = (
        jnp.einsum(
            "esbf,ebfd->esbd", hidden_blocks, down_blocks, preferred_element_type=jnp.float32
        )
        .astype(jnp.bfloat16)
        .reshape(local_experts, slot_count, tp_count * model_width)
    )
    returned = lax.all_to_all(
        to_sources(expert_out), "fsdp", split_axis=0, concat_axis=0, tiled=True
    )
    picked = pick_rows(returned)
    moe_part = jnp.sum(gate_probs[:, :, None] * picked, axis=1)
    gate_grad_part = jnp.sum(upstream[:, None, :] * picked, axis=-1)
    weighted = (
        (gate_probs[:, :, None] * upstream[:, None, :])
        .astype(jnp.bfloat16)
        .reshape(group_rows * top_count, model_width)
    )
    weighted = jnp.concatenate([weighted, jnp.zeros((1, model_width), jnp.bfloat16)], axis=0)
    grad_arrived = lax.all_to_all(
        weighted[sent_rows], "fsdp", split_axis=0, concat_axis=0, tiled=True
    )
    grad_slots = to_experts(grad_arrived)
    hidden_grad = jnp.einsum(
        "esd,ebfd->esbf", grad_slots, down_blocks, preferred_element_type=jnp.float32
    ).reshape(local_experts, slot_count, tp_count * ff_part)
    swish_slope = sigmoid_val * (1.0 + gate_val * (1.0 - sigmoid_val))
    gate_val_grad = (hidden_grad * up_val * swish_slope).astype(jnp.bfloat16)
    up_val_grad = (hidden_grad * swish_val).astype(jnp.bfloat16)
    grad_w_down = jnp.einsum(
        "esbf,esd->ebfd", hidden_blocks, grad_slots, preferred_element_type=jnp.float32
    ).reshape(local_experts, tp_count * ff_part, model_width)
    grad_w_gate = jnp.einsum(
        "esd,esf->edf", expert_rows, gate_val_grad, preferred_element_type=jnp.float32
    )
    grad_w_up = jnp.einsum(
        "esd,esf->edf", expert_rows, up_val_grad, preferred_element_type=jnp.float32
    )
    gate_blocks = gate_full.reshape(local_experts, model_width, tp_count, ff_part)
    up_blocks = up_full.reshape(local_experts, model_width, tp_count, ff_part)
    entry_grad = (
        (
            jnp.einsum(
                "esbf,edbf->esbd",
                gate_val_grad.reshape(local_experts, slot_count, tp_count, ff_part),
                gate_blocks,
                preferred_element_type=jnp.float32,
            )
            + jnp.einsum(
                "esbf,edbf->esbd",
                up_val_grad.reshape(local_experts, slot_count, tp_count, ff_part),
                up_blocks,
                preferred_element_type=jnp.float32,
            )
        )
        .astype(jnp.bfloat16)
        .reshape(local_experts, slot_count, tp_count * model_width)
    )
    sent_back = lax.all_to_all(
        to_sources(entry_grad), "fsdp", split_axis=0, concat_axis=0, tiled=True
    )
    expert_grad = jnp.sum(pick_rows(sent_back), axis=1)
    grad_w_gate, grad_w_up, grad_w_down = (
        lax.psum_scatter(
            grad_w_gate.astype(jnp.bfloat16), "tp", scatter_dimension=2, tiled=True
        ).astype(jnp.float32),
        lax.psum_scatter(
            grad_w_up.astype(jnp.bfloat16), "tp", scatter_dimension=2, tiled=True
        ).astype(jnp.float32),
        lax.psum_scatter(
            grad_w_down.astype(jnp.bfloat16), "tp", scatter_dimension=1, tiled=True
        ).astype(jnp.float32),
    )
    moe_grad, gate_grad = (
        lax.psum(expert_grad.astype(jnp.bfloat16), "tp").astype(jnp.float32),
        lax.psum(gate_grad_part.astype(jnp.bfloat16), "tp").astype(jnp.float32),
    )
    gate_inner = jnp.sum(gate_probs * gate_grad, axis=-1, keepdims=True)
    selected_grad = gate_probs * (gate_grad - gate_inner)
    logit_grad = jnp.sum(jnp.where(chosen, selected_grad[:, :, None], 0.0), axis=1).astype(
        jnp.bfloat16
    )
    moe_grad = moe_grad + contract_last(logit_grad, w_router)
    router_grad = contract_rows(
        lax.dynamic_slice_in_dim(moe_low, own_start, half_rows, 0),
        lax.dynamic_slice_in_dim(logit_grad, own_start, half_rows, 0),
    )
    residual_from_norm, moe_gain_terms = norm_back(residual, moe_factor, moe_gain, moe_grad)
    residual_grad = upstream + residual_from_norm
    moe_gain_grad = jnp.sum(
        lax.dynamic_slice_in_dim(moe_gain_terms, own_start, half_rows, 0), axis=0
    )
    residual_low = residual_grad.astype(jnp.bfloat16)
    mixed_grad = (
        contract_last(residual_low, out_full)
        .astype(jnp.bfloat16)
        .reshape(group_rows, kv_heads, group_size, head_dim)
    )
    grad_w_out = contract_rows(mixed_low, residual_low)
    scores = (
        jnp.einsum("qkgd,tkd->kgqt", query_low, key_low, preferred_element_type=jnp.float32)
        * score_scale
    )
    scores = jnp.where(allowed, scores, masked_score)
    probs_full = jnp.exp(scores - log_total)
    prob_grad = jnp.einsum(
        "qkgd,tkd->kgqt", mixed_grad, value_low, preferred_element_type=jnp.float32
    )
    prob_inner = jnp.sum(probs_full * prob_grad, axis=-1, keepdims=True)
    score_grad = (probs_full * (prob_grad - prob_inner)).astype(jnp.bfloat16)
    query_grad = (
        jnp.einsum(
            "kgqt,tkd->qkgd", score_grad, key_low, preferred_element_type=jnp.float32
        ).reshape(group_rows, query_heads, head_dim)
        * score_scale
    )
    key_grad = (
        jnp.einsum("kgqt,qkgd->tkd", score_grad, query_low, preferred_element_type=jnp.float32)
        * score_scale
    )
    value_grad = (
        jnp.einsum(
            "kgqt,qkgd->tkd",
            probs_full.astype(jnp.bfloat16),
            mixed_grad,
            preferred_element_type=jnp.float32,
        )
        .astype(jnp.bfloat16)
        .reshape(group_rows, kv_heads * head_dim)
    )
    query_pre_grad, query_gain_terms = norm_back(
        query_pre, query_factor, query_gain, rotate_back(query_grad, cosine_table, sine_table)
    )
    key_pre_grad, key_gain_terms = norm_back(
        key_before_norm, key_factor, key_gain, rotate_back(key_grad, cosine_table, sine_table)
    )
    query_pre_low = query_pre_grad.astype(jnp.bfloat16).reshape(group_rows, query_heads * head_dim)
    key_pre_low = key_pre_grad.astype(jnp.bfloat16).reshape(group_rows, kv_heads * head_dim)
    grad_w_query = contract_rows(normed_all, query_pre_low)
    grad_w_key = contract_rows(normed_all, key_pre_low)
    grad_w_value = contract_rows(normed_all, value_grad)
    normed_grad = (
        contract_last(query_pre_low, query_full)
        + contract_last(key_pre_low, key_full)
        + contract_last(value_grad, value_full)
    )
    normed_grad_own, moe_own = (
        lax.psum_scatter(
            normed_grad.astype(jnp.bfloat16), "tp", scatter_dimension=0, tiled=True
        ).astype(jnp.float32),
        lax.psum_scatter(
            moe_part.astype(jnp.bfloat16), "tp", scatter_dimension=0, tiled=True
        ).astype(jnp.float32),
    )
    tokens_own = lax.dynamic_slice_in_dim(tokens_in, own_start, half_rows, 0)
    factor_own = lax.dynamic_slice_in_dim(attn_factor, own_start, half_rows, 0)
    tokens_from_norm, attn_gain_terms = norm_back(
        tokens_own, factor_own, attn_gain, normed_grad_own
    )
    grad_group = lax.dynamic_slice_in_dim(residual_grad, own_start, half_rows, 0) + tokens_from_norm
    residual_own = lax.dynamic_slice_in_dim(residual, own_start, half_rows, 0)
    output_group = (residual_own + moe_own).astype(jnp.bfloat16)
    back_output, back_grad = (
        lax.all_to_all(
            output_group.astype(jnp.float32)
            .reshape(fsdp_count, slice_rows, model_width)
            .astype(jnp.bfloat16),
            "fsdp",
            split_axis=0,
            concat_axis=0,
            tiled=True,
        ).astype(jnp.float32),
        lax.all_to_all(
            grad_group.reshape(fsdp_count, slice_rows, model_width).astype(jnp.bfloat16),
            "fsdp",
            split_axis=0,
            concat_axis=0,
            tiled=True,
        ).astype(jnp.float32),
    )
    output = (
        jnp.take(back_output, back_pick, axis=0)
        .reshape(half_rows, model_width)
        .astype(jnp.bfloat16)
    )
    grad_input = jnp.take(back_grad, back_pick, axis=0).reshape(half_rows, model_width)
    grad_w_query, grad_w_key, grad_w_value, grad_w_out = (
        lax.psum_scatter(grad_w_query, "fsdp", scatter_dimension=0, tiled=True),
        lax.psum_scatter(grad_w_key, "fsdp", scatter_dimension=0, tiled=True),
        lax.psum_scatter(grad_w_value, "fsdp", scatter_dimension=0, tiled=True),
        lax.psum_scatter(grad_w_out, "fsdp", scatter_dimension=1, tiled=True),
    )
    grad_attn_gain, grad_query_gain, grad_key_gain, grad_moe_gain, grad_w_router = lax.psum(
        (
            jnp.sum(attn_gain_terms, axis=0),
            jnp.sum(query_gain_terms, axis=(0, 1)),
            jnp.sum(key_gain_terms, axis=(0, 1)),
            moe_gain_grad,
            router_grad,
        ),
        ("fsdp", "tp"),
    )
    return (
        output,
        grad_input,
        grad_attn_gain,
        grad_query_gain,
        grad_key_gain,
        grad_moe_gain,
        grad_w_query,
        grad_w_key,
        grad_w_value,
        grad_w_out,
        grad_w_router,
        grad_w_gate,
        grad_w_up,
        grad_w_down,
    )


def link_cost(microseconds):
    return pl.CostEstimate(flops=0, bytes_accessed=microseconds * 3_000_000, transcendentals=0)


def remote(src, dst, send_sem, recv_sem, target):
    return pltpu.make_async_remote_copy(
        src_ref=src,
        dst_ref=dst,
        send_sem=send_sem,
        recv_sem=recv_sem,
        device_id=target,
        device_id_type=pl.DeviceIdType.MESH,
    )


def greet(targets):
    barrier = pltpu.get_barrier_semaphore()
    for target in targets:
        pl.semaphore_signal(
            barrier, inc=1, device_id=target, device_id_type=pl.DeviceIdType.MESH
        )
    pl.semaphore_wait(barrier, len(targets))


class Place:
    def __init__(self):
        self.chips = lax.axis_size("chip")
        self.levels = self.chips // 2
        self.chip = lax.axis_index("chip")
        self.core = lax.axis_index("core")
        self.tp = lax.axis_index("tp")
        self.level = self.chip // 2
        self.side = self.chip % 2
        self.fsdp = self.chip * 2 + self.core
        self.mate = {"core": 1 - self.core}
        self.across = {"tp": 1 - self.tp}
        self.beside = {"chip": self.level * 2 + 1 - self.side}
        self.above = {"chip": lax.rem(self.chip + 2, self.chips)}
        self.below = {"chip": lax.rem(self.chip + self.chips - 2, self.chips)}

    def member(self, offset):
        count = 2 * self.chips
        index = lax.rem(self.fsdp + offset + count, count)
        return {"chip": index // 2, "core": lax.rem(index, 2)}, index

    def plane_targets(self):
        return [self.member(offset)[0] for offset in range(1, 2 * self.chips)]

    def ring_targets(self):
        return [self.above, self.below, self.beside]


class PlaneGather:
    def __init__(self, place, views, sems):
        self.place, self.views = place, views
        (
            self.up_send,
            self.up_recv,
            self.down_send,
            self.down_recv,
            self.side_send,
            self.side_recv,
        ) = sems

    @staticmethod
    def semaphores(items, levels):
        return [pltpu.SemaphoreType.DMA((items, levels - 1))] * 4 + [
            pltpu.SemaphoreType.DMA((items, 2 * levels - 1))
        ] * 2

    def _up(self, item, step, origin_level):
        view = self.views[item](origin_level * 2 + self.place.side)
        return remote(
            view, view, self.up_send.at[item, step], self.up_recv.at[item, step], self.place.above
        )

    def _down(self, item, step, origin_level):
        view = self.views[item](origin_level * 2 + self.place.side)
        return remote(
            view,
            view,
            self.down_send.at[item, step],
            self.down_recv.at[item, step],
            self.place.below,
        )

    def _side(self, item, slot, origin_level, own_side):
        side = self.place.side if own_side else 1 - self.place.side
        view = self.views[item](origin_level * 2 + side)
        return remote(
            view,
            view,
            self.side_send.at[item, slot],
            self.side_recv.at[item, slot],
            self.place.beside,
        )

    def start(self, item):
        place = self.place
        level, top = place.level, place.levels - 1

        @pl.when(level < top)
        def _():
            self._up(item, 0, level).start()

        @pl.when(level > 0)
        def _():
            self._down(item, 0, level).start()

        self._side(item, 0, level, True).start()

    def step(self, item, step):
        place = self.place
        level, top = place.level, place.levels - 1

        @pl.when(level >= step + 1)
        def _():
            origin = level - 1 - step
            self._up(item, step, origin).wait_recv()
            if step + 1 < top:

                @pl.when(level < top)
                def _():
                    self._up(item, step + 1, origin).start()

            self._side(item, 1 + 2 * step, origin, True).start()

        @pl.when(level + step + 1 <= top)
        def _():
            origin = level + 1 + step
            self._down(item, step, origin).wait_recv()
            if step + 1 < top:

                @pl.when(level > 0)
                def _():
                    self._down(item, step + 1, origin).start()

            self._side(item, 2 + 2 * step, origin, True).start()

    def finish_side(self, item, slot):
        place = self.place
        level, top = place.level, place.levels - 1
        if slot == 0:
            self._side(item, 0, level, False).wait_recv()
        elif slot % 2 == 1:
            step = slot // 2

            @pl.when(level >= step + 1)
            def _():
                self._side(item, slot, level - 1 - step, False).wait_recv()

        else:
            step = slot // 2 - 1

            @pl.when(level + step + 1 <= top)
            def _():
                self._side(item, slot, level + 1 + step, False).wait_recv()

    def drain(self, item):
        place = self.place
        level, top = place.level, place.levels - 1
        self._side(item, 0, level, True).wait_send()
        for step in range(top):

            @pl.when((level < top) & (level >= step))
            def _():
                self._up(item, step, level - step).wait_send()

            @pl.when((level > 0) & (level + step <= top))
            def _():
                self._down(item, step, level + step).wait_send()

            @pl.when(level >= step + 1)
            def _():
                self._side(item, 1 + 2 * step, level - 1 - step, True).wait_send()

            @pl.when(level + step + 1 <= top)
            def _():
                self._side(item, 2 + 2 * step, level + 1 + step, True).wait_send()


def open_kernel(
    sequences,
    slices_ref,
    gain_ref,
    lengths_ref,
    frequency_ref,
    query_ref,
    key_ref,
    value_ref,
    out_ref,
    gate_ref,
    up_ref,
    dealt_ref,
    normed_ref,
    cosine_ref,
    sine_ref,
    mask_ref,
    query_all,
    key_all,
    value_all,
    out_all,
    gate_all,
    up_all,
    both_lengths_ref,
    deal_send,
    deal_recv,
    quad_send,
    quad_recv,
    swap_send,
    swap_recv,
    keep_sem,
    pair_send,
    pair_recv,
    pair_keep,
    *ring_sems,
):
    place = Place()
    core, chip = place.core, place.chip
    own_rows = query_ref.shape[0]
    quarter = query_all.shape[2]
    narrow = key_all.shape[2]
    head_rows = out_all.shape[0]
    lanes = out_ref.shape[1]
    members = 2 * place.chips
    greet(place.plane_targets() + [place.across])

    def deal_copy(offset, sending):
        target, index = place.member(offset if sending else -offset)
        return remote(
            slices_ref.at[index],
            dealt_ref.at[place.fsdp if sending else index],
            deal_send.at[offset - 1],
            deal_recv.at[offset - 1],
            target,
        )

    for offset in range(1, members):
        deal_copy(offset, True).start()

    def rows(who):
        return pl.ds(pl.multiple_of(who * own_rows, own_rows), own_rows)

    def columns(who, width):
        return pl.ds(pl.multiple_of(who * width, width), width)

    def spots(who):
        lane_start = pl.multiple_of((2 * chip + core) * lanes, lanes)
        return [
            (query_ref.at[:, columns(who, quarter)], query_all.at[chip, rows(core)]),
            (key_ref.at[:, columns(who, narrow)], key_all.at[chip, rows(core)]),
            (value_ref.at[:, columns(who, narrow)], value_all.at[chip, rows(core)]),
            (
                out_ref.at[pl.ds(pl.multiple_of(who * head_rows, head_rows), head_rows)],
                out_all.at[:, pl.ds(lane_start, lanes)],
            ),
        ]

    def arrivals():
        lane_start = pl.multiple_of((2 * chip + 1 - core) * lanes, lanes)
        return [
            query_all.at[chip, rows(1 - core)],
            key_all.at[chip, rows(1 - core)],
            value_all.at[chip, rows(1 - core)],
            out_all.at[:, pl.ds(lane_start, lanes)],
        ]

    sends = [
        remote(src, dst, swap_send.at[i], swap_recv.at[i], place.mate)
        for i, (src, dst) in enumerate(spots(1 - core))
    ]
    keeps = [
        pltpu.make_async_copy(src, dst, keep_sem.at[i])
        for i, (src, dst) in enumerate(spots(core))
    ]
    mate_lengths = remote(
        lengths_ref, both_lengths_ref.at[core], swap_send.at[4], swap_recv.at[4], place.mate
    )
    own_lengths = pltpu.make_async_copy(lengths_ref, both_lengths_ref.at[core], keep_sem.at[4])
    own_slice = pltpu.make_async_copy(
        slices_ref.at[place.fsdp], dealt_ref.at[place.fsdp], keep_sem.at[5]
    )
    own_slice.start()
    units = gate_ref.shape[1]

    def halves(who):
        at = pl.ds(pl.multiple_of(who * units, units), units)
        return [gate_all.at[:, at], up_all.at[:, at]]

    shards = (gate_ref, up_ref)
    pair_copies = []
    for i, (src, dst) in enumerate(zip(shards, halves(place.tp))):
        pair_copies.append(
            (
                remote(src, dst, pair_send.at[i], pair_recv.at[i], place.across),
                pltpu.make_async_copy(src, dst, pair_keep.at[i]),
            )
        )
    for i in range(4):
        sends[i].start()
        keeps[i].start()
    mate_lengths.start()
    own_lengths.start()

    out_lanes = 2 * lanes
    ring = PlaneGather(
        place,
        [
            lambda who: query_all.at[who],
            lambda who: key_all.at[who],
            lambda who: value_all.at[who],
            lambda who: out_all.at[
                :, pl.ds(pl.multiple_of(who * out_lanes, out_lanes), out_lanes)
            ],
        ],
        ring_sems,
    )
    landed = arrivals()
    for i in range(4):
        keeps[i].wait()
        sends[i].wait_send()
        remote(landed[i], landed[i], swap_send.at[i], swap_recv.at[i], place.mate).wait_recv()
        ring.start(i)

    own_slice.wait()
    for offset in range(1, members):
        deal_copy(offset, False).wait_recv()
    tp = place.tp
    half = slices_ref.shape[1] // 2
    step_rows = 4
    for start in range(0, members, step_rows):
        x = dealt_ref[start : start + step_rows].astype(jnp.float32)[:, :half]
        x = x.reshape(step_rows * half, x.shape[2])
        factor = lax.rsqrt(jnp.mean(x * x, axis=-1, keepdims=True) + epsilon)
        normed_ref[core, tp, start * half : (start + step_rows) * half, :] = (
            x * factor * gain_ref[...]
        ).astype(jnp.bfloat16)
    mine = normed_ref.at[core, tp]
    to_mate = remote(mine, mine, quad_send.at[0], quad_recv.at[0], place.mate)
    to_across = remote(mine, mine, quad_send.at[1], quad_recv.at[1], place.across)
    to_across.start()
    to_mate.start()
    for both in pair_copies:
        both[0].start()
        both[1].start()
    levels = place.levels
    own_lengths.wait()
    mate_lengths.wait_send()
    theirs = both_lengths_ref.at[1 - core]
    remote(theirs, theirs, swap_send.at[4], swap_recv.at[4], place.mate).wait_recv()
    group = mask_ref.shape[1]
    head = cosine_ref.shape[1]
    across_sign = jnp.where(
        lax.broadcasted_iota(jnp.int32, (group, head), 1) < head // 2, -1.0, 1.0
    )
    for which in range(2):
        ends = []
        for at in range(sequences):
            length = both_lengths_ref[which, 0:1, at : at + 1]
            ends.append(length if at == 0 else ends[-1] + length)

        def segment_start(place_ids):
            start = jnp.zeros_like(place_ids)
            for end in ends:
                start = jnp.where(place_ids >= end, end, start)
            return start

        at_rows = pl.ds(which * group, group)
        row_ids = lax.broadcasted_iota(jnp.int32, (group, head), 0)
        position = (row_ids - segment_start(row_ids)).astype(jnp.float32)
        angles = position * frequency_ref[...]
        cosine_ref[at_rows, :] = jnp.cos(angles)
        sine_ref[at_rows, :] = jnp.sin(angles) * across_sign
        row_ids = lax.broadcasted_iota(jnp.int32, (group, group), 0)
        key_ids = lax.broadcasted_iota(jnp.int32, (group, group), 1)
        allowed = (key_ids <= row_ids) & (key_ids >= segment_start(row_ids))
        mask_ref[which] = jnp.where(allowed, 0.0, masked_score)
    for i in range(4):
        ring.step(i, 0)
    other = normed_ref.at[core, 1 - tp]
    remote(other, other, quad_send.at[1], quad_recv.at[1], place.across).wait_recv()
    passed = remote(other, other, quad_send.at[2], quad_recv.at[2], place.mate)
    passed.start()
    for step in range(1, levels - 1):
        for i in range(4):
            ring.step(i, step)
    for slot in range(2 * levels - 1):
        for i in range(4):
            ring.finish_side(i, slot)
    for i in range(4):
        ring.drain(i)
    for offset in range(1, members):
        deal_copy(offset, True).wait_send()
    to_mate.wait_send()
    to_across.wait_send()
    passed.wait_send()
    for slot, piece in ((0, normed_ref.at[1 - core, tp]), (2, normed_ref.at[1 - core, 1 - tp])):
        remote(piece, piece, quad_send.at[slot], quad_recv.at[slot], place.mate).wait_recv()
    for i, dst in enumerate(halves(1 - place.tp)):
        pair_copies[i][1].wait()
        pair_copies[i][0].wait_send()
        remote(dst, dst, pair_send.at[i], pair_recv.at[i], place.across).wait_recv()


def open_layer(
    slices, gain_vec, lengths, sequences, frequency, w_query, w_key, w_value, w_out, w_gate, w_up
):
    members, pack, model_width = slices.shape
    chips = members // 2
    own_rows = w_query.shape[0]
    low = jnp.bfloat16
    vmem = pl.BlockSpec(memory_space=pltpu.VMEM)
    anywhere = pl.BlockSpec(memory_space=pl.ANY)
    dma = pltpu.SemaphoreType.DMA
    group, head = 2 * own_rows, frequency.shape[1]
    return pl.pallas_call(
        functools.partial(open_kernel, sequences),
        name="open_layer",
        out_shape=[
            jax.ShapeDtypeStruct(slices.shape, low),
            jax.ShapeDtypeStruct((2, 2, own_rows, model_width), low),
            jax.ShapeDtypeStruct((2 * group, head), jnp.float32),
            jax.ShapeDtypeStruct((2 * group, head), jnp.float32),
            jax.ShapeDtypeStruct((2, group, group), jnp.float32),
            jax.ShapeDtypeStruct((chips, 2 * own_rows, w_query.shape[1] // 2), low),
            jax.ShapeDtypeStruct((chips, 2 * own_rows, w_key.shape[1] // 2), low),
            jax.ShapeDtypeStruct((chips, 2 * own_rows, w_value.shape[1] // 2), low),
            jax.ShapeDtypeStruct((w_out.shape[0] // 2, members * w_out.shape[1]), low),
            jax.ShapeDtypeStruct((model_width, 2 * w_gate.shape[1]), low),
            jax.ShapeDtypeStruct((model_width, 2 * w_up.shape[1]), low),
        ],
        in_specs=[vmem] * 4 + [anywhere] * 6,
        out_specs=[vmem] * 5 + [anywhere] * 6,
        scratch_shapes=[
            pltpu.VMEM((2,) + lengths.shape, jnp.int32),
            dma((members - 1,)),
            dma((members - 1,)),
            dma((3,)),
            dma((3,)),
            dma((5,)),
            dma((5,)),
            dma((6,)),
            dma((2,)),
            dma((2,)),
            dma((2,)),
        ]
        + PlaneGather.semaphores(4, chips // 2),
        compiler_params=pltpu.CompilerParams(
            collective_id=0, has_side_effects=True, vmem_limit_bytes=40 << 20
        ),
        cost_estimate=link_cost(110),
    )(slices, gain_vec, lengths, frequency, w_query, w_key, w_value, w_out, w_gate, w_up)


def quad_share_kernel(own_ref, all_ref, send, recv, keep_sem):
    place = Place()
    core, tp = place.core, place.tp
    greet([place.mate, place.across])
    to_across = remote(own_ref, all_ref.at[core, tp], send.at[1], recv.at[1], place.across)
    to_mate = remote(own_ref, all_ref.at[core, tp], send.at[0], recv.at[0], place.mate)
    to_across.start()
    to_mate.start()
    keep = pltpu.make_async_copy(own_ref, all_ref.at[core, tp], keep_sem)
    keep.start()
    other = all_ref.at[core, 1 - tp]
    remote(other, other, send.at[1], recv.at[1], place.across).wait_recv()
    passed = remote(other, other, send.at[2], recv.at[2], place.mate)
    passed.start()
    keep.wait()
    to_mate.wait_send()
    to_across.wait_send()
    passed.wait_send()
    for slot, piece in ((0, all_ref.at[1 - core, tp]), (2, all_ref.at[1 - core, 1 - tp])):
        remote(piece, piece, send.at[slot], recv.at[slot], place.mate).wait_recv()


def quad_share(own, collective_id):
    vmem = pl.BlockSpec(memory_space=pltpu.VMEM)
    dma = pltpu.SemaphoreType.DMA
    return pl.pallas_call(
        quad_share_kernel,
        name="quad_share",
        out_shape=jax.ShapeDtypeStruct((2, 2) + own.shape, own.dtype),
        in_specs=[vmem],
        out_specs=vmem,
        scratch_shapes=[dma((3,)), dma((3,)), dma],
        compiler_params=pltpu.CompilerParams(
            collective_id=collective_id, has_side_effects=True, vmem_limit_bytes=16 << 20
        ),
        cost_estimate=link_cost(16),
    )(own)


def quad_sum_kernel(parts_ref, sum_ref, near, far, pair, send, recv):
    place = Place()
    core, tp = place.core, place.tp
    greet([place.mate, place.across])
    to_mate = [
        remote(parts_ref.at[1 - core, half], near.at[half], send.at[half], recv.at[half], place.mate)
        for half in (1 - tp, tp)
    ]
    for copy in to_mate:
        copy.start()
    wide = jnp.float32

    def landed(half):
        return remote(near.at[half], near.at[half], send.at[half], recv.at[half], place.mate)

    landed(1 - tp).wait_recv()
    pair[...] = (
        parts_ref[core, 1 - tp].astype(wide) + near[1 - tp].astype(wide)
    ).astype(jnp.bfloat16)
    to_across = remote(pair, far, send.at[2], recv.at[2], place.across)
    to_across.start()
    landed(tp).wait_recv()
    sum_ref[...] = parts_ref[core, tp].astype(wide) + near[tp].astype(wide)
    to_across.wait_recv()
    sum_ref[...] += far[...].astype(wide)
    for copy in to_mate:
        copy.wait_send()
    to_across.wait_send()


def quad_sum(parts, collective_id):
    _, _, rows, width = parts.shape
    vmem = pl.BlockSpec(memory_space=pltpu.VMEM)
    dma = pltpu.SemaphoreType.DMA
    low = jnp.bfloat16
    return pl.pallas_call(
        quad_sum_kernel,
        name="quad_sum",
        out_shape=jax.ShapeDtypeStruct((rows, width), jnp.float32),
        in_specs=[vmem],
        out_specs=vmem,
        scratch_shapes=[
            pltpu.VMEM((2, rows, width), low),
            pltpu.VMEM((rows, width), low),
            pltpu.VMEM((rows, width), low),
            dma((3,)),
            dma((3,)),
        ],
        compiler_params=pltpu.CompilerParams(
            collective_id=collective_id, has_side_effects=True, vmem_limit_bytes=24 << 20
        ),
        cost_estimate=link_cost(16),
    )(parts)


class PlaneSum:
    def __init__(self, place, parts, side_bufs, up_bufs, down_bufs, sems):
        self.place, self.parts = place, parts
        self.side_bufs, self.up_bufs, self.down_bufs = side_bufs, up_bufs, down_bufs
        (
            self.up_send,
            self.up_recv,
            self.down_send,
            self.down_recv,
            self.side_send,
            self.side_recv,
        ) = sems

    @staticmethod
    def semaphores(items, levels):
        return [pltpu.SemaphoreType.DMA((items, levels))] * 6

    def target(self, turn):
        place = self.place
        far, near = place.levels - 1 - turn // 2, turn // 2
        low_half = [far, near][turn % 2]
        high_half = [near, far][turn % 2]
        upper = place.level // (place.levels // 2)
        return low_half * (1 - upper) + high_half * upper

    def _side(self, item, goal):
        return remote(
            self.parts[item](goal * 2 + 1 - self.place.side),
            self.side_bufs[item].at[goal],
            self.side_send.at[item, goal],
            self.side_recv.at[item, goal],
            self.place.beside,
        )

    def _up(self, item, goal):
        source = self.side_bufs[item].at[goal]
        return remote(
            source,
            self.up_bufs[item].at[goal],
            self.up_send.at[item, goal],
            self.up_recv.at[item, goal],
            self.place.above,
        )

    def _down(self, item, goal):
        source = self.side_bufs[item].at[goal]
        return remote(
            source,
            self.down_bufs[item].at[goal],
            self.down_send.at[item, goal],
            self.down_recv.at[item, goal],
            self.place.below,
        )

    def start(self, item, turn):
        self._side(item, self.target(turn)).start()

    def add(self, item, goal, ref):
        held = self.side_bufs[item]
        held[goal] = (held[goal].astype(jnp.float32) + ref.astype(jnp.float32)).astype(held.dtype)

    def turn(self, item, turn):
        place = self.place
        goal = self.target(turn)
        level, top = place.level, place.levels - 1
        self._side(item, goal).wait_recv()
        self.add(item, goal, self.parts[item](goal * 2 + place.side)[...])

        @pl.when(goal > level)
        def _():
            @pl.when(level > 0)
            def _():
                self._up(item, goal).wait_recv()
                self.add(item, goal, self.up_bufs[item][goal])

            self._up(item, goal).start()

        @pl.when(goal < level)
        def _():
            @pl.when(level < top)
            def _():
                self._down(item, goal).wait_recv()
                self.add(item, goal, self.down_bufs[item][goal])

            self._down(item, goal).start()

    def close(self, item):
        place = self.place
        level, top = place.level, place.levels - 1

        @pl.when(level > 0)
        def _():
            self._up(item, level).wait_recv()
            self.add(item, level, self.up_bufs[item][level])

        @pl.when(level < top)
        def _():
            self._down(item, level).wait_recv()
            self.add(item, level, self.down_bufs[item][level])

    def drain(self, item):
        place = self.place
        for turn in range(place.levels):
            goal = self.target(turn)
            self._side(item, goal).wait_send()

            @pl.when(goal > place.level)
            def _():
                self._up(item, goal).wait_send()

            @pl.when(goal < place.level)
            def _():
                self._down(item, goal).wait_send()


def close_kernel(
    slices_ref,
    gain_ref,
    query_ref,
    key_ref,
    value_ref,
    down_ref,
    dealt_ref,
    gain_sum_ref,
    query_own,
    key_own,
    value_own,
    down_arrived,
    gain_near,
    gain_pair,
    gain_parts,
    *rest,
):
    side_bufs, up_bufs, down_bufs = rest[0:3], rest[3:6], rest[6:9]
    deal_send, deal_recv, gain_send, gain_recv, swap_send, swap_recv, keep_sem = rest[9:16]
    pair_send, pair_recv, total_send, total_recv = rest[16:20]
    place = Place()
    core = place.core
    members = 2 * place.chips
    own_rows = query_own.shape[0]
    greet(place.plane_targets() + [place.across])
    blocks = 2 * own_rows

    def by_rows(ref):
        return lambda chip: ref.at[pl.ds(pl.multiple_of(chip * blocks, blocks), blocks)]

    sums = PlaneSum(
        place,
        [by_rows(query_ref), by_rows(key_ref), by_rows(value_ref)],
        side_bufs,
        up_bufs,
        down_bufs,
        rest[20:],
    )

    def deal_copy(offset, sending):
        target, index = place.member(offset if sending else -offset)
        return remote(
            slices_ref.at[index],
            dealt_ref.at[place.fsdp if sending else index],
            deal_send.at[offset - 1],
            deal_recv.at[offset - 1],
            target,
        )

    def gain_copy(offset, sending):
        target, index = place.member(offset if sending else -offset)
        return remote(
            gain_pair.at[index],
            gain_parts.at[place.fsdp if sending else index],
            gain_send.at[offset],
            gain_recv.at[offset],
            target,
        )

    def total_copy(offset, sending):
        target, index = place.member(offset if sending else -offset)
        piece = gain_sum_ref.at[place.fsdp if sending else index]
        return remote(piece, piece, total_send.at[offset], total_recv.at[offset], target)

    units = down_arrived.shape[0]
    theirs = down_ref.at[pl.ds(pl.multiple_of((1 - place.tp) * units, units), units)]
    pair_copy = remote(theirs, down_arrived, pair_send, pair_recv, place.across)
    across = remote(gain_ref, gain_near, gain_send.at[0], gain_recv.at[0], place.across)
    across.start()
    across.wait_recv()
    gain_pair[...] = gain_ref[...] + gain_near[...]
    for offset in range(1, members):
        gain_copy(offset, True).start()
    pair_copy.start()
    for item in range(3):
        sums.start(item, 0)
    for offset in range(1, members):
        gain_copy(offset, False).wait_recv()
    gain_parts[place.fsdp] = gain_pair[place.fsdp]
    total = gain_parts[0]
    for member in range(1, members):
        total += gain_parts[member]
    gain_sum_ref[place.fsdp] = total
    for offset in range(1, members):
        total_copy(offset, True).start()
    for offset in range(1, members):
        deal_copy(offset, True).start()
    own_slice = pltpu.make_async_copy(
        slices_ref.at[place.fsdp], dealt_ref.at[place.fsdp], keep_sem
    )
    own_slice.start()
    for item in range(3):
        sums.start(item, 1)
    for turn in range(place.levels):
        for item in range(3):
            sums.turn(item, turn)
            if turn + 2 < place.levels:
                sums.start(item, turn + 2)

    def rows(who):
        return pl.ds(pl.multiple_of(who * own_rows, own_rows), own_rows)

    def columns(who, width):
        return pl.ds(pl.multiple_of(who * width, width), width)

    level = place.level
    spots = []
    for held, own in zip(side_bufs, (query_own, key_own, value_own)):
        width = held.shape[2]
        spots.append(
            (
                held.at[level, rows(core)],
                held.at[level, rows(1 - core)],
                own.at[:, columns(core, width)],
                own.at[:, columns(1 - core, width)],
            )
        )
    keeps, swaps = {}, {}
    for item in range(3):
        sums.close(item)
        mine, theirs, here, there = spots[item]
        keeps[item] = pltpu.make_async_copy(mine, here, keep_sem_of(item, swap_send, 4))
        keeps[item].start()
        swaps[item] = remote(
            theirs, here, swap_send.at[item], swap_recv.at[item], place.mate
        )
        swaps[item].start()
    for item in range(3):
        keeps[item].wait()
        swaps[item].wait_send()
        _, _, _, there = spots[item]
        remote(there, there, swap_send.at[item], swap_recv.at[item], place.mate).wait_recv()
        sums.drain(item)
    across.wait_send()
    pair_copy.wait()
    own_slice.wait()
    for offset in range(1, members):
        deal_copy(offset, False).wait_recv()
        deal_copy(offset, True).wait_send()
        gain_copy(offset, True).wait_send()
        total_copy(offset, True).wait_send()
        total_copy(offset, False).wait_recv()


def keep_sem_of(item, sems, start):
    return sems.at[start + item]


def close_layer(
    slices, gain_part, query_grad, key_grad, value_grad, down_grad
):
    members = slices.shape[0]
    levels = members // 4
    own_rows = query_grad.shape[0] // members
    low = jnp.bfloat16
    vmem = pl.BlockSpec(memory_space=pltpu.VMEM)
    anywhere = pl.BlockSpec(memory_space=pl.ANY)
    dma = pltpu.SemaphoreType.DMA
    blocks = [
        (2 * own_rows, query_grad.shape[1]),
        (2 * own_rows, key_grad.shape[1]),
        (2 * own_rows, value_grad.shape[1]),
    ]
    buffers = [pltpu.VMEM((levels,) + block, low) for block in blocks]
    return pl.pallas_call(
        close_kernel,
        name="close_layer",
        out_shape=[
            jax.ShapeDtypeStruct(slices.shape, low),
            jax.ShapeDtypeStruct(gain_part.shape, jnp.float32),
            jax.ShapeDtypeStruct((own_rows, 2 * query_grad.shape[1]), low),
            jax.ShapeDtypeStruct((own_rows, 2 * key_grad.shape[1]), low),
            jax.ShapeDtypeStruct((own_rows, 2 * value_grad.shape[1]), low),
        ]
        + [jax.ShapeDtypeStruct((down_grad.shape[0] // 2, down_grad.shape[1]), low)],
        in_specs=[vmem] * 5 + [anywhere],
        out_specs=[vmem] * 5 + [anywhere],
        scratch_shapes=[
            pltpu.VMEM(gain_part.shape, jnp.float32),
            pltpu.VMEM(gain_part.shape, jnp.float32),
            pltpu.VMEM(gain_part.shape, jnp.float32),
        ]
        + buffers * 3
        + [
            dma((members - 1,)),
            dma((members - 1,)),
            dma((members,)),
            dma((members,)),
            dma((8,)),
            dma((4,)),
            dma,
            dma,
            dma,
            dma((members,)),
            dma((members,)),
        ]
        + PlaneSum.semaphores(3, levels),
        compiler_params=pltpu.CompilerParams(
            collective_id=1, has_side_effects=True, vmem_limit_bytes=56 << 20
        ),
        cost_estimate=link_cost(90),
    )(
        slices,
        gain_part,
        query_grad,
        key_grad,
        value_grad,
        down_grad,
    )


class RowGather:
    def __init__(self, place, block, sems):
        self.place, self.block = place, block
        (
            self.up_send,
            self.up_recv,
            self.down_send,
            self.down_recv,
            self.side_send,
            self.side_recv,
            self.hand_send,
            self.hand_recv,
        ) = sems

    @staticmethod
    def semaphores(levels):
        dma = pltpu.SemaphoreType.DMA
        return [dma((levels,))] * 6 + [dma((2 * levels,))] * 2

    def climb(self, origin):
        piece, at = self.block(origin, self.place.core), origin // 2
        return remote(piece, piece, self.up_send.at[at], self.up_recv.at[at], self.place.above)

    def sink(self, origin):
        piece, at = self.block(origin, self.place.core), origin // 2
        return remote(piece, piece, self.down_send.at[at], self.down_recv.at[at], self.place.below)

    def cross(self, origin):
        piece, at = self.block(origin, self.place.core), origin // 2
        return remote(piece, piece, self.side_send.at[at], self.side_recv.at[at], self.place.beside)

    def hand(self, origin, whose):
        piece = self.block(origin, whose)
        return remote(
            piece, piece, self.hand_send.at[origin], self.hand_recv.at[origin], self.place.mate
        )

    def start(self):
        place = self.place

        @pl.when(place.level < place.levels - 1)
        def _():
            self.climb(place.chip).start()

        @pl.when(place.level > 0)
        def _():
            self.sink(place.chip).start()

        self.cross(place.chip).start()
        self.hand(place.chip, place.core).start()

    def step(self, n):
        place = self.place
        level, side, top = place.level, place.side, place.levels - 1
        under, over = level - n, level + n

        @pl.when((n > 0) & (under >= 0))
        def _():
            origin = under * 2 + side
            self.climb(origin).wait_recv()

            @pl.when(level < top)
            def _():
                self.climb(origin).start()

            self.cross(origin).start()
            self.hand(origin, place.core).start()

        @pl.when((n > 0) & (over <= top))
        def _():
            origin = over * 2 + side
            self.sink(origin).wait_recv()

            @pl.when(level > 0)
            def _():
                self.sink(origin).start()

            self.cross(origin).start()
            self.hand(origin, place.core).start()

        def crossed(origin_level):
            origin = origin_level * 2 + 1 - side
            self.cross(origin).wait_recv()
            self.hand(origin, place.core).start()

        @pl.when((n > 0) & (under + 1 >= 0))
        def _():
            crossed(under + 1)

        @pl.when((n > 1) & (over - 1 <= top))
        def _():
            crossed(over - 1)

    def take_hands(self):
        place = self.place

        def taken(origin, carry):
            self.hand(origin, 1 - place.core).wait_recv()
            return carry

        lax.fori_loop(0, place.chips, taken, 0)

    def drain(self):
        place = self.place
        level, side, top = place.level, place.side, place.levels - 1

        def handed(origin, carry):
            self.hand(origin, place.core).wait_send()
            return carry

        lax.fori_loop(0, place.chips, handed, 0)

        def sent(at, carry):
            self.cross(at * 2 + side).wait_send()

            @pl.when((level < top) & (at <= level))
            def _():
                self.climb(at * 2 + side).wait_send()

            @pl.when((level > 0) & (at >= level))
            def _():
                self.sink(at * 2 + side).wait_send()

            return carry

        lax.fori_loop(0, place.levels, sent, 0)


class QuadSum:
    def __init__(self, place, parts, near, pair, far, send, recv):
        self.place, self.parts = place, parts
        self.near, self.pair, self.far = near, pair, far
        self.send, self.recv = send, recv

    @staticmethod
    def scratch(rows, width):
        low, dma = jnp.bfloat16, pltpu.SemaphoreType.DMA
        return [
            pltpu.VMEM((2, rows, width), low),
            pltpu.VMEM((rows, width), low),
            pltpu.VMEM((rows, width), low),
            dma((3,)),
            dma((3,)),
        ]

    def to_mate(self, half):
        return remote(
            self.parts.at[1 - self.place.core, half],
            self.near.at[half],
            self.send.at[half],
            self.recv.at[half],
            self.place.mate,
        )

    def to_across(self):
        return remote(self.pair, self.far, self.send.at[2], self.recv.at[2], self.place.across)

    def start(self):
        self.to_mate(1 - self.place.tp).start()
        self.to_mate(self.place.tp).start()

    def relay(self):
        core, tp, wide = self.place.core, self.place.tp, jnp.float32
        self.to_mate(1 - tp).wait_recv()
        self.pair[...] = (
            self.parts[core, 1 - tp].astype(wide) + self.near[1 - tp].astype(wide)
        ).astype(jnp.bfloat16)
        self.to_across().start()

    def total(self):
        core, tp, wide = self.place.core, self.place.tp, jnp.float32
        self.to_mate(tp).wait_recv()
        total = self.parts[core, tp].astype(wide) + self.near[tp].astype(wide)
        self.to_across().wait_recv()
        return total + self.far[...].astype(wide)

    def drain(self):
        for half in range(2):
            self.to_mate(half).wait_send()
        self.to_across().wait_send()


def nt_dot(left, right):
    return lax.dot_general(
        left, right, (((1,), (1,)), ((), ())), preferred_element_type=jnp.float32
    )


def tn_dot(left, right):
    return lax.dot_general(
        left, right, (((0,), (0,)), ((), ())), preferred_element_type=jnp.float32
    )


def lanes_at(index, width):
    return pl.ds(pl.multiple_of(index * width, width), width)


def attend_kernel(
    experts,
    normed_ref,
    query_w,
    key_w,
    value_w,
    out_w,
    cosine_ref,
    sine_ref,
    mask_ref,
    dealt_ref,
    query_gain,
    key_gain,
    moe_gain,
    router_ref,
    chosen_ref,
    upstream_all,
    moe_ext,
    residual_ref,
    gates_ref,
    query_pre,
    query_low,
    key_pre,
    key_low,
    value_low,
    probs_ref,
    mixed_ref,
    upstream_own,
    parts,
    near,
    pair,
    far,
    quad_send,
    quad_recv,
    keep_sem,
    *ring_sems,
):
    place = Place()
    core = place.core
    wide, low = jnp.float32, jnp.bfloat16
    own_rows, width = residual_ref.shape
    group = 2 * own_rows
    head = query_gain.shape[1]
    heads = query_w.shape[1] // head
    members = dealt_ref.shape[0]
    half = dealt_ref.shape[1] // 2
    step_rows = 4

    def dealt_rows(start, second):
        block = dealt_ref[start : start + step_rows].astype(wide)
        block = block[:, half:] if second else block[:, :half]
        return block.reshape(step_rows * half, width)

    for start in range(0, members, step_rows):
        upstream_own[start * half : (start + step_rows) * half, :] = dealt_rows(
            start, True
        ).astype(low)
    keep = pltpu.make_async_copy(upstream_own, upstream_all.at[place.chip, core], keep_sem)
    keep.start()
    greet(place.ring_targets() + [place.mate, place.across])
    gather = RowGather(place, lambda origin, whose: upstream_all.at[origin, whose], ring_sems)
    keep.wait()
    gather.start()

    def turned(values, gain_ref):
        factor = lax.rsqrt(jnp.mean(values * values, axis=-1, keepdims=True) + epsilon)
        scaled = values * factor * gain_ref[...]
        return (scaled * cosine_ref[...] + pltpu.roll(scaled, head // 2, 1) * sine_ref[...]).astype(
            low
        )

    x = normed_ref[...].reshape(2 * group, width)

    def project(index, carry):
        both = jnp.dot(
            normed_ref[...].reshape(2 * group, width),
            query_w[:, lanes_at(index, 2 * head)],
            preferred_element_type=wide,
        )
        query_pre[:, lanes_at(index, 2 * head)] = both
        for which in range(2):
            one = both[:, which * head : (which + 1) * head]
            query_low[:, lanes_at(2 * index + which, head)] = turned(one, query_gain)
        return carry

    lax.fori_loop(0, heads // 2, project, 0)
    key_values = jnp.dot(x, key_w[...], preferred_element_type=wide)
    key_pre[...] = key_values
    key_low[...] = turned(key_values, key_gain)
    value_low[...] = jnp.dot(x, value_w[...], preferred_element_type=wide).astype(low)
    gather.step(1)
    scale = head ** (-0.5)
    batch = 4

    def attend(index, carry):
        which = index // (heads // batch)
        first = (index % (heads // batch)) * batch
        rows = lanes_at(which, group)
        key = key_low[rows, :]
        value = value_low[rows, :]
        mask = mask_ref[which]
        for offset in range(batch):
            at = lanes_at(first + offset, head)
            scores = nt_dot(query_low[rows, at], key) * scale + mask
            peak = jnp.max(scores, axis=-1, keepdims=True)
            exponent = jnp.exp(scores - peak)
            probs = (exponent * (1.0 / jnp.sum(exponent, axis=-1, keepdims=True))).astype(low)
            probs_ref[which * heads + first + offset] = probs
            mixed_ref[rows, at] = jnp.dot(probs, value, preferred_element_type=wide).astype(low)
        return carry

    lax.fori_loop(0, heads // batch, attend, 0)
    gather.step(2)
    lax.fori_loop(heads // batch, 2 * heads // batch, attend, 0)

    def out_rows(whose):
        left = mixed_ref[lanes_at(whose, group), :]

        def out_lanes(index, carry):
            at = lanes_at(index, 512)
            product = jnp.dot(left, out_w[:, at], preferred_element_type=wide).astype(low)
            parts[whose, :, :, at] = product.reshape(2, own_rows, 512)
            return carry

        lax.fori_loop(0, width // 512, out_lanes, 0)

    sums = QuadSum(place, parts, near, pair, far, quad_send, quad_recv)
    out_rows(1 - core)
    sums.start()
    out_rows(core)
    sums.relay()
    gather.step(3)
    total = sums.total()
    tokens = jnp.concatenate(
        [dealt_rows(start, False) for start in range(0, members, step_rows)], axis=0
    )
    residual = tokens + total
    residual_ref[...] = residual
    factor = lax.rsqrt(jnp.mean(residual * residual, axis=-1, keepdims=True) + epsilon)
    moe_low = (residual * factor * moe_gain[...]).astype(low)
    moe_ext[:, :width] = moe_low
    logits = jnp.dot(moe_low, router_ref[...], preferred_element_type=wide)
    chosen = chosen_ref[...] > 0.0
    logits = jnp.where(chosen, logits, masked_score)
    exponent = jnp.exp(logits - jnp.max(logits, axis=-1, keepdims=True))
    exponent = jnp.where(chosen, exponent, 0.0)
    gates = exponent / jnp.sum(exponent, axis=-1, keepdims=True)
    gates_ref[...] = gates
    high = gates.astype(low).astype(wide)
    middle = (gates - high).astype(low).astype(wide)
    rest = gates - high - middle
    moe_ext[:, width:] = (
        high + pltpu.roll(middle, experts, 1) + pltpu.roll(rest, 2 * experts, 1)
    ).astype(low)
    for n in range(4, place.levels + 1):
        gather.step(n)
    gather.take_hands()
    gather.drain()
    sums.drain()


def attend_layer(
    experts, normed, query_w, key_w, value_w, out_w, tables, dealt, gain_vecs, router, chosen
):
    own_rows, width = normed.shape[2:]
    rows = 4 * own_rows
    members = dealt.shape[0]
    chips = members // 2
    heads_width, head = query_w.shape[1], key_w.shape[1]
    group = 2 * own_rows
    wide, low = jnp.float32, jnp.bfloat16
    vmem = pl.BlockSpec(memory_space=pltpu.VMEM)
    anywhere = pl.BlockSpec(memory_space=pl.ANY)
    shape = jax.ShapeDtypeStruct
    return pl.pallas_call(
        functools.partial(attend_kernel, experts),
        name="attend_layer",
        out_shape=[
            shape((chips, 2, own_rows, width), low),
            shape((own_rows, width + 128), low),
            shape((own_rows, width), wide),
            shape((own_rows, 128), wide),
            shape((rows, heads_width), wide),
            shape((rows, heads_width), low),
            shape((rows, head), wide),
            shape((rows, head), low),
            shape((rows, head), low),
            shape((2 * heads_width // head, group, group), low),
            shape((rows, heads_width), low),
        ],
        in_specs=[vmem] * 14,
        out_specs=[anywhere] + [vmem] * 10,
        scratch_shapes=[
            pltpu.VMEM((own_rows, width), low),
            pltpu.VMEM((2, 2, own_rows, width), low),
        ]
        + QuadSum.scratch(own_rows, width)
        + [pltpu.SemaphoreType.DMA]
        + RowGather.semaphores(chips // 2),
        compiler_params=pltpu.CompilerParams(
            collective_id=2, has_side_effects=True, vmem_limit_bytes=56 << 20
        ),
        cost_estimate=link_cost(60),
    )(normed, query_w, key_w, value_w, out_w, *tables, dealt, *gain_vecs, router, chosen)


class ChainSum:
    def __init__(self, place, parts, side_buf, chain_buf, sems):
        self.place, self.parts = place, parts
        self.side_buf, self.chain_buf = side_buf, chain_buf
        (
            self.up_send,
            self.up_recv,
            self.down_send,
            self.down_recv,
            self.side_send,
            self.side_recv,
        ) = sems

    @staticmethod
    def semaphores(levels):
        return [pltpu.SemaphoreType.DMA((levels,))] * 6

    def target(self, turn):
        place = self.place
        far, near = place.levels - 1 - turn // 2, turn // 2
        odd = turn % 2
        low_half = far * (1 - odd) + near * odd
        high_half = near * (1 - odd) + far * odd
        upper = place.level // (place.levels // 2)
        return low_half * (1 - upper) + high_half * upper

    def from_under(self, goal):
        return self.chain_buf.at[goal + 1]

    def from_over(self, goal):
        return self.chain_buf.at[goal]

    def side(self, goal):
        return remote(
            self.parts(goal * 2 + 1 - self.place.side),
            self.side_buf.at[goal],
            self.side_send.at[goal],
            self.side_recv.at[goal],
            self.place.beside,
        )

    def up(self, goal):
        return remote(
            self.side_buf.at[goal],
            self.from_under(goal),
            self.up_send.at[goal],
            self.up_recv.at[goal],
            self.place.above,
        )

    def down(self, goal):
        return remote(
            self.side_buf.at[goal],
            self.from_over(goal),
            self.down_send.at[goal],
            self.down_recv.at[goal],
            self.place.below,
        )

    def add(self, goal, ref):
        held = self.side_buf
        total = held[goal].astype(jnp.float32) + ref[...].astype(jnp.float32)
        held[goal] = total.astype(held.dtype)

    def take_side(self, turn):
        place = self.place
        goal = self.target(turn)
        level, top = place.level, place.levels - 1
        self.side(goal).wait_recv()
        self.add(goal, self.parts(goal * 2 + place.side))

        @pl.when((goal > level) & (level == 0))
        def _():
            self.up(goal).start()

        @pl.when((goal < level) & (level == top))
        def _():
            self.down(goal).start()

    def take_chain(self, turn):
        place = self.place
        goal = self.target(turn)
        level, top = place.level, place.levels - 1

        @pl.when((goal > level) & (level > 0))
        def _():
            self.up(goal).wait_recv()
            self.add(goal, self.from_under(goal))
            self.up(goal).start()

        @pl.when((goal < level) & (level < top))
        def _():
            self.down(goal).wait_recv()
            self.add(goal, self.from_over(goal))
            self.down(goal).start()

    def close(self):
        place = self.place
        level, top = place.level, place.levels - 1

        @pl.when(level > 0)
        def _():
            self.up(level).wait_recv()
            self.add(level, self.from_under(level))

        @pl.when(level < top)
        def _():
            self.down(level).wait_recv()
            self.add(level, self.from_over(level))

    def drain(self):
        place = self.place

        def turn_done(turn, carry):
            goal = self.target(turn)
            self.side(goal).wait_send()

            @pl.when(goal > place.level)
            def _():
                self.up(goal).wait_send()

            @pl.when(goal < place.level)
            def _():
                self.down(goal).wait_send()

            return carry

        lax.fori_loop(0, place.levels, turn_done, 0)


def expert_kernel(
    experts,
    x_own,
    upstream_ref,
    gate_ref,
    up_ref,
    down_ref,
    entry_own,
    out_part,
    gate_grad_ref,
    up_grad_ref,
    down_grad_ref,
    x_all,
    u_all,
    gate_w,
    up_w,
    down_w,
    hidden,
    gate_val_grad,
    up_val_grad,
    scores,
    sums,
    mate_out,
    mate_in,
    side_buf,
    chain_buf,
    staged,
    load_sem,
    store_sem,
    both_sem,
    ring_up_send,
    ring_up_recv,
    ring_down_send,
    ring_down_recv,
    ring_side_send,
    ring_side_recv,
    pass_send,
    pass_recv,
    mate_send,
    mate_recv,
    *sum_sems,
):
    place = Place()
    core, chip, level, side = place.core, place.chip, place.level, place.side
    levels, top = place.levels, place.levels - 1
    rows = x_own.shape[0]
    tile = 2 * rows
    width = upstream_ref.shape[1]
    units = down_ref.shape[0]
    wide = jnp.float32
    low = jnp.bfloat16
    loads = [
        pltpu.make_async_copy(x_own, x_all.at[chip, core], load_sem.at[0]),
        pltpu.make_async_copy(gate_ref, gate_w, load_sem.at[1]),
        pltpu.make_async_copy(up_ref, up_w, load_sem.at[2]),
        pltpu.make_async_copy(down_ref, down_w, load_sem.at[3]),
        pltpu.make_async_copy(upstream_ref, u_all, load_sem.at[4]),
    ]
    for load in loads:
        load.start()
    greet(place.ring_targets() + [place.mate])

    def block(origin):
        return x_all.at[origin, core]

    def climb(origin):
        return remote(
            block(origin),
            block(origin),
            ring_up_send.at[origin // 2],
            ring_up_recv.at[origin // 2],
            place.above,
        )

    def sink(origin):
        return remote(
            block(origin),
            block(origin),
            ring_down_send.at[origin // 2],
            ring_down_recv.at[origin // 2],
            place.below,
        )

    def cross(origin):
        return remote(
            block(origin),
            block(origin),
            ring_side_send.at[origin // 2],
            ring_side_recv.at[origin // 2],
            place.beside,
        )

    def hand(origin, whose):
        piece = x_all.at[origin, whose]
        return remote(piece, piece, pass_send.at[origin], pass_recv.at[origin], place.mate)

    loads[0].wait()

    @pl.when(level < top)
    def _():
        climb(chip).start()

    @pl.when(level > 0)
    def _():
        sink(chip).start()

    cross(chip).start()
    hand(chip, core).start()
    for load in loads[1:]:
        load.wait()

    lane = lax.broadcasted_iota(jnp.int32, (128, 128), 0)
    select = (
        (lane == place.fsdp)
        | (lane == place.fsdp + experts)
        | (lane == place.fsdp + 2 * experts)
    ).astype(low)
    cut = 256
    across_lanes = lax.broadcasted_iota(jnp.int32, (tile, 128), 1)

    def forward_tile(origin):
        x = x_all[origin].reshape(tile, x_all.shape[3])
        gate_lanes = jnp.dot(x[:, width:], select, preferred_element_type=wide)
        gate = jnp.concatenate([gate_lanes] * (cut // 128), axis=1)
        x = x[:, :width]
        start = pl.multiple_of(origin * tile, tile)
        u = u_all[pl.ds(start, tile), :]
        score = jnp.zeros((tile, 1), wide)
        for part in range(units // cut):
            lanes = slice(part * cut, (part + 1) * cut)
            gate_val = jnp.dot(x, gate_w[:, lanes], preferred_element_type=wide)
            up_val = jnp.dot(x, up_w[:, lanes], preferred_element_type=wide)
            back = lax.dot_general(
                u, down_w[lanes, :], (((1,), (1,)), ((), ())), preferred_element_type=wide
            )
            sigmoid = 1.0 / (1.0 + jnp.exp(-gate_val))
            swish = gate_val * sigmoid
            out = (swish * up_val).astype(low).astype(wide)
            score += jnp.sum(out * back, axis=1, keepdims=True)
            back = back * gate
            slope = sigmoid * (1.0 + gate_val * (1.0 - sigmoid))
            hidden[pl.ds(start, tile), lanes] = (out * gate).astype(low)
            gate_val_grad[pl.ds(start, tile), lanes] = (back * up_val * slope).astype(low)
            up_val_grad[pl.ds(start, tile), lanes] = (back * swish).astype(low)
        high = score.astype(low).astype(wide)
        packed = jnp.where(
            across_lanes == place.fsdp,
            high,
            jnp.where(across_lanes == place.fsdp + experts, score - high, 0.0),
        )
        scores[origin] = packed.astype(low)

    def gather_step(n, carry):
        step = n - 1
        under, over = level - n, level + n

        @pl.when((n > 0) & (under >= 0))
        def _():
            origin = under * 2 + side
            climb(origin).wait_recv()

            @pl.when(level < top)
            def _():
                climb(origin).start()

            cross(origin).start()
            hand(origin, core).start()

        @pl.when((n > 0) & (over <= top))
        def _():
            origin = over * 2 + side
            sink(origin).wait_recv()

            @pl.when(level > 0)
            def _():
                sink(origin).start()

            cross(origin).start()
            hand(origin, core).start()

        def crossed(origin_level):
            origin = origin_level * 2 + 1 - side
            cross(origin).wait_recv()
            hand(origin, core).start()

        @pl.when((n > 0) & (level - step >= 0))
        def _():
            crossed(level - step)

        @pl.when((n > 1) & (level + step <= top))
        def _():
            crossed(level + step)

        def candidate(which, carried):
            upward = which % 2
            facing = which // 2
            distance = n - 1 + facing
            at = level + distance * (2 * upward - 1)
            origin = at * 2 + side * facing + (1 - side) * (1 - facing)

            @pl.when(
                (at >= 0) & (at <= top) & (distance >= 0) & ((distance > 0) | (upward == 0))
            )
            def _():
                hand(origin, 1 - core).wait_recv()
                forward_tile(origin)

            return carried

        return lax.fori_loop(0, 4, candidate, carry)

    lax.fori_loop(0, levels + 1, gather_step, 0)

    plane_sum = ChainSum(place, lambda chip: sums.at[chip], side_buf, chain_buf, sum_sems)

    def to_mate(goal_chip, slot):
        return remote(
            mate_out.at[slot],
            mate_in.at[goal_chip],
            mate_send.at[slot],
            mate_recv.at[goal_chip],
            place.mate,
        )

    def backward_tile(goal_chip, slot, reuse):
        start = pl.multiple_of(goal_chip * tile, tile)
        own_start = pl.multiple_of(goal_chip * tile + core * rows, rows)
        mate_start = pl.multiple_of(goal_chip * tile + (1 - core) * rows, rows)

        @pl.when(reuse)
        def _():
            to_mate(goal_chip, slot).wait_send()

        grads = gate_val_grad[pl.ds(start, tile), :]
        up_grads = up_val_grad[pl.ds(start, tile), :]
        piece = 512
        for first in range(0, width, piece):
            lanes = slice(first, first + piece)
            whole = lax.dot_general(
                grads, gate_w[lanes, :], (((1,), (1,)), ((), ())), preferred_element_type=wide
            ) + lax.dot_general(
                up_grads, up_w[lanes, :], (((1,), (1,)), ((), ())), preferred_element_type=wide
            )
            halves = whole.astype(low).reshape(2, rows, piece)
            sums[goal_chip, :, lanes] = jnp.where(core == 0, halves[0], halves[1])
            mate_out[slot, :, lanes] = jnp.where(core == 0, halves[1], halves[0])
        sums[goal_chip, :, width:] = scores[goal_chip, pl.ds(pl.multiple_of(core * rows, rows), rows)]
        mate_out[slot, :, width:] = scores[
            goal_chip, pl.ds(pl.multiple_of((1 - core) * rows, rows), rows)
        ]
        to_mate(goal_chip, slot).start()

    def joined(goal_chip, slot):
        to_mate(goal_chip, slot).wait_recv()
        sums[goal_chip] = (
            sums[goal_chip].astype(wide) + mate_in[goal_chip].astype(wide)
        ).astype(low)

    def backward_turn(turn, carry):
        goal = plane_sum.target(turn)
        backward_tile(goal * 2 + 1 - side, 0, turn > 0)
        backward_tile(goal * 2 + side, 1, turn > 0)
        joined(goal * 2 + 1 - side, 0)
        plane_sum.side(goal).start()
        joined(goal * 2 + side, 1)
        return carry

    lax.fori_loop(0, levels, backward_turn, 0)

    def store(target, start, slot):
        return pltpu.make_async_copy(
            staged.at[slot], target.at[pl.ds(start, tile)], store_sem.at[slot]
        )

    def output_tile(origin, carry):
        start = pl.multiple_of(origin * tile, tile)
        slot = origin % 2

        @pl.when(origin > 1)
        def _():
            store(out_part, start, slot).wait()

        left = hidden[pl.ds(start, tile), :]
        for first in range(0, width, 512):
            lanes = slice(first, first + 512)
            staged[slot, :, lanes] = jnp.dot(
                left, down_w[:, lanes], preferred_element_type=wide
            ).astype(low)
        store(out_part, start, slot).start()
        return carry

    def down_grads(index, carry):
        start = pl.multiple_of(index * tile, tile)
        slot = index % 2
        store(down_grad_ref, start, slot).wait()
        left = hidden[:, pl.ds(start, tile)]
        for first in range(0, width, 512):
            lanes = slice(first, first + 512)
            staged[slot, :, lanes] = lax.dot_general(
                left, u_all[:, lanes], (((0,), (0,)), ((), ())), preferred_element_type=wide
            ).astype(low)
        store(down_grad_ref, start, slot).start()
        return carry

    def store_both(index):
        slot = index % 2
        start = pl.multiple_of(index * tile, tile)
        return [
            pltpu.make_async_copy(
                staged.at[slot, :, i * units : (i + 1) * units],
                target.at[pl.ds(start, tile)],
                both_sem.at[slot, i],
            )
            for i, target in enumerate((gate_grad_ref, up_grad_ref))
        ]

    def entry_weight_grads(index, carry):
        slot = index % 2

        @pl.when(index > 1)
        def _():
            for copy in store_both(index):
                copy.wait()

        left = x_all[:, :, :, pl.ds(pl.multiple_of(index * tile, tile), tile)]
        left = left.reshape(u_all.shape[0], tile)
        for i, right in enumerate((gate_val_grad, up_val_grad)):
            staged[slot, :, i * units : (i + 1) * units] = lax.dot_general(
                left, right[...], (((0,), (0,)), ((), ())), preferred_element_type=wide
            ).astype(low)
        for copy in store_both(index):
            copy.start()
        return carry

    plane_sum.take_side(0)
    lax.fori_loop(0, place.chips, output_tile, 0)
    plane_sum.take_chain(0)
    plane_sum.take_side(1)
    lax.fori_loop(0, units // tile, down_grads, 0)
    for slot in range(2):
        store(down_grad_ref, 0, slot).wait()
    plane_sum.take_chain(1)
    plane_sum.take_side(2)
    chunks = width // tile
    lax.fori_loop(0, chunks // 2, entry_weight_grads, 0)
    plane_sum.take_chain(2)
    plane_sum.take_side(3)
    lax.fori_loop(chunks // 2, chunks, entry_weight_grads, 0)
    plane_sum.take_chain(3)
    plane_sum.close()
    entry_own[...] = side_buf[level]
    for slot in range(2):
        for copy in store_both(slot):
            copy.wait()
        to_mate(0, slot).wait_send()
    plane_sum.drain()

    def handed(origin, carry):
        hand(origin, core).wait_send()
        return carry

    lax.fori_loop(0, place.chips, handed, 0)

    def sent(at, carry):
        cross(at * 2 + side).wait_send()

        @pl.when((level < top) & (at <= level))
        def _():
            climb(at * 2 + side).wait_send()

        @pl.when((level > 0) & (at >= level))
        def _():
            sink(at * 2 + side).wait_send()

        return carry

    lax.fori_loop(0, levels, sent, 0)


def expert_layer(x_own, upstream_all, gate_all, up_all, down_all, experts):
    rows, span = x_own.shape
    total, width = upstream_all.shape
    units = down_all.shape[0]
    chips = total // (2 * rows)
    levels = chips // 2
    low = jnp.bfloat16
    vmem = pl.BlockSpec(memory_space=pltpu.VMEM)
    anywhere = pl.BlockSpec(memory_space=pl.ANY)
    dma = pltpu.SemaphoreType.DMA
    return pl.pallas_call(
        functools.partial(expert_kernel, experts),
        name="expert_layer",
        out_shape=[
            jax.ShapeDtypeStruct((rows, span), low),
            jax.ShapeDtypeStruct((total, width), low),
            jax.ShapeDtypeStruct((width, units), low),
            jax.ShapeDtypeStruct((width, units), low),
            jax.ShapeDtypeStruct((units, width), low),
        ],
        in_specs=[vmem] + [anywhere] * 4,
        out_specs=[vmem] + [anywhere] * 4,
        scratch_shapes=[
            pltpu.VMEM((chips, 2, rows, span), low),
            pltpu.VMEM((total, width), low),
            pltpu.VMEM((width, units), low),
            pltpu.VMEM((width, units), low),
            pltpu.VMEM((units, width), low),
            pltpu.VMEM((total, units), low),
            pltpu.VMEM((total, units), low),
            pltpu.VMEM((total, units), low),
            pltpu.VMEM((chips, 2 * rows, 128), low),
            pltpu.VMEM((chips, rows, span), low),
            pltpu.VMEM((2, rows, span), low),
            pltpu.VMEM((chips, rows, span), low),
            pltpu.VMEM((levels, rows, span), low),
            pltpu.VMEM((levels + 1, rows, span), low),
            pltpu.VMEM((2, 2 * rows, width), low),
            dma((5,)),
            dma((2,)),
            dma((2, 2)),
        ]
        + [dma((levels,))] * 6
        + [dma((chips,)), dma((chips,)), dma((2,)), dma((chips,))]
        + ChainSum.semaphores(levels),
        compiler_params=pltpu.CompilerParams(
            collective_id=5, has_side_effects=True, vmem_limit_bytes=63 << 20
        ),
        cost_estimate=link_cost(125),
    )(x_own, upstream_all, gate_all, up_all, down_all)


def attend_back_kernel(
    experts,
    entry_ref,
    residual_ref,
    gates_ref,
    dealt_ref,
    router_ref,
    attn_gain,
    moe_gain,
    query_gain,
    key_gain,
    mixed_ref,
    probs_ref,
    query_low,
    key_low,
    value_low,
    query_pre,
    key_pre,
    cosine_ref,
    sine_ref,
    normed_ref,
    query_w,
    key_w,
    value_w,
    out_w,
    out_part,
    gate_part,
    up_part,
    finished_ref,
    out_own,
    query_grad,
    key_grad,
    value_grad,
    router_grad,
    attn_gain_part,
    moe_gain_part,
    query_gain_part,
    key_gain_part,
    gate_arrived,
    up_arrived,
    residual_grad,
    low_all,
    mixed_grad,
    low_grads,
    key_total,
    value_total,
    out_grad,
    out_sums,
    out_mate,
    out_side,
    out_chain,
    weight_side,
    weight_chain,
    staged,
    near,
    pair,
    far,
    quad_send,
    quad_recv,
    share_send,
    share_recv,
    swap_send,
    swap_recv,
    keep_sem,
    store_sem,
    pair_send,
    pair_recv,
    *ring_sems,
):
    place = Place()
    core, tp, level = place.core, place.tp, place.level
    wide, low = jnp.float32, jnp.bfloat16
    own_rows, width = residual_ref.shape
    group = 2 * own_rows
    rows = 2 * group
    head = query_gain.shape[1]
    heads = query_w.shape[1] // head
    members = dealt_ref.shape[0]
    half = dealt_ref.shape[1] // 2
    step_rows = 4
    scale = head ** (-0.5)

    def dealt_rows(second):
        blocks = []
        for start in range(0, members, step_rows):
            block = dealt_ref[start : start + step_rows].astype(wide)
            block = block[:, half:] if second else block[:, :half]
            blocks.append(block.reshape(step_rows * half, width))
        return jnp.concatenate(blocks, axis=0)

    greet(place.ring_targets() + [place.mate, place.across])
    to_mate = remote(
        out_part.at[:, 1 - core], out_mate, swap_send.at[0], swap_recv.at[0], place.mate
    )
    to_mate.start()
    keep = pltpu.make_async_copy(out_part.at[:, core], out_sums, keep_sem.at[0])
    keep.start()

    entry = entry_ref[:, :width].astype(wide)
    extra = entry_ref[:, width:].astype(wide)
    gates = gates_ref[...]
    gate_grad = extra + pltpu.roll(extra, 128 - experts, 1)
    inner = jnp.sum(gates * gate_grad, axis=-1, keepdims=True)
    logit_grad = (gates * (gate_grad - inner)).astype(low)
    residual = residual_ref[...]
    factor = lax.rsqrt(jnp.mean(residual * residual, axis=-1, keepdims=True) + epsilon)
    moe_low = (residual * factor * moe_gain[...]).astype(low)
    moe_grad = entry + nt_dot(logit_grad, router_ref[...])
    router_grad[...] = tn_dot(moe_low, logit_grad)
    scaled = moe_grad * moe_gain[...]
    inner = jnp.mean(scaled * residual, axis=-1, keepdims=True)
    moe_gain_part[...] = jnp.sum(moe_grad * residual * factor, axis=0, keepdims=True)
    residual_grad[...] = dealt_rows(True) + factor * (
        scaled - residual * (factor * factor) * inner
    )
    low_all[core, tp] = residual_grad[...].astype(low)
    mine = low_all.at[core, tp]
    share_mate = remote(mine, mine, share_send.at[0], share_recv.at[0], place.mate)
    share_across = remote(mine, mine, share_send.at[1], share_recv.at[1], place.across)
    share_across.start()
    share_mate.start()
    units = gate_arrived.shape[1]
    pair_copies = [
        remote(
            part.at[:, lanes_at(1 - tp, units)],
            arrived,
            pair_send.at[i],
            pair_recv.at[i],
            place.across,
        )
        for i, (part, arrived) in enumerate(((gate_part, gate_arrived), (up_part, up_arrived)))
    ]
    pair_copies[0].start()

    out_ring = ChainSum(
        place, lambda chip: out_sums.at[chip], out_side, out_chain, ring_sems[:6]
    )
    lanes = out_own.shape[1]
    weight_ring = ChainSum(
        place,
        lambda chip: out_grad.at[:, lanes_at(chip, 2 * lanes)],
        weight_side,
        weight_chain,
        ring_sems[6:],
    )
    keep.wait()
    to_mate.wait_recv()

    def join(turn, carry):
        goal = out_ring.target(turn)
        for origin in (goal * 2 + 1 - place.side, goal * 2 + place.side):
            out_sums[origin] = (
                out_sums[origin].astype(wide) + out_mate[origin].astype(wide)
            ).astype(low)
        out_ring.side(goal).start()
        return carry

    lax.fori_loop(0, place.levels, join, 0)
    other = low_all.at[core, 1 - tp]
    remote(other, other, share_send.at[1], share_recv.at[1], place.across).wait_recv()
    passed = remote(other, other, share_send.at[2], share_recv.at[2], place.mate)
    passed.start()
    for slot, piece in ((0, low_all.at[1 - core, tp]), (2, low_all.at[1 - core, 1 - tp])):
        remote(piece, piece, share_send.at[slot], share_recv.at[slot], place.mate).wait_recv()

    def out_grad_rows(index, carry):
        at = lanes_at(index, 256)
        left = mixed_ref[:, at]
        for first in range(0, width, 512):
            out_grad[at, first : first + 512] = tn_dot(
                left, low_all[:, :, :, first : first + 512].reshape(rows, 512)
            ).astype(low)
        return carry

    lax.fori_loop(0, mixed_ref.shape[1] // 256, out_grad_rows, 0)
    for turn in range(min(2, place.levels)):
        weight_ring.side(weight_ring.target(turn)).start()

    def mixed_lanes(index, carry):
        at = lanes_at(index, 256)
        mixed_grad[:, at] = nt_dot(low_all[...].reshape(rows, width), out_w[at, :]).astype(low)
        return carry

    lax.fori_loop(0, mixed_ref.shape[1] // 256, mixed_lanes, 0)
    key_total[...] = jnp.zeros_like(key_total)
    value_total[...] = jnp.zeros_like(value_total)
    query_gain_part[...] = jnp.zeros_like(query_gain_part)

    def pre_back(grad, values, gain_ref, cosine, sine):
        grad = grad * cosine - pltpu.roll(grad, head // 2, 1) * sine
        factor = lax.rsqrt(jnp.mean(values * values, axis=-1, keepdims=True) + epsilon)
        scaled = grad * gain_ref[...]
        inner = jnp.mean(scaled * values, axis=-1, keepdims=True)
        back = factor * (scaled - values * (factor * factor) * inner)
        return back.astype(low), jnp.sum(grad * values * factor, axis=0, keepdims=True)

    batch = 4

    def attend_back(index, carry):
        which = index // (heads // batch)
        first = (index % (heads // batch)) * batch
        at_rows = lanes_at(which, group)
        key = key_low[at_rows, :]
        value = value_low[at_rows, :]
        cosine, sine = cosine_ref[at_rows, :], sine_ref[at_rows, :]
        key_sum = key_total[at_rows, :]
        value_sum = value_total[at_rows, :]
        gain_sum = query_gain_part[...]
        for offset in range(batch):
            at = lanes_at(first + offset, head)
            probs = probs_ref[which * heads + first + offset]
            grads = mixed_grad[at_rows, at]
            prob_grad = nt_dot(grads, value)
            probs_wide = probs.astype(wide)
            inner = jnp.sum(probs_wide * prob_grad, axis=-1, keepdims=True)
            score_grad = (probs_wide * (prob_grad - inner)).astype(low)
            query = jnp.dot(score_grad, key, preferred_element_type=wide) * scale
            key_sum += tn_dot(score_grad, query_low[at_rows, at])
            value_sum += tn_dot(probs, grads)
            back, terms = pre_back(query, query_pre[at_rows, at], query_gain, cosine, sine)
            low_grads[at_rows, at] = back
            gain_sum += terms
        key_total[at_rows, :] = key_sum
        value_total[at_rows, :] = value_sum
        query_gain_part[...] = gain_sum
        return carry

    count = 2 * heads // batch
    share = -(-count // place.levels)
    for turn in range(place.levels):
        out_ring.take_side(turn)
        lax.fori_loop(min(turn * share, count), min((turn + 1) * share, count), attend_back, 0)
        out_ring.take_chain(turn)

    back, terms = pre_back(
        key_total[...] * scale, key_pre[...], key_gain, cosine_ref[...], sine_ref[...]
    )
    key_gain_part[...] = terms
    low_grads[:, heads * head : (heads + 1) * head] = back
    low_grads[:, (heads + 1) * head :] = value_total[...].astype(low)

    def normed_grad_rows(whose):
        at_rows = lanes_at(whose, group)

        def normed_grad_lanes(index, carry):
            at = lanes_at(index, 512)
            grads = low_grads[at_rows, :]
            product = (
                nt_dot(grads[:, : heads * head], query_w[at, :])
                + nt_dot(grads[:, heads * head : (heads + 1) * head], key_w[at, :])
                + nt_dot(grads[:, (heads + 1) * head :], value_w[at, :])
            )
            low_all[whose, :, :, at] = product.astype(low).reshape(2, own_rows, 512)
            return carry

        lax.fori_loop(0, width // 512, normed_grad_lanes, 0)

    share_mate.wait_send()
    share_across.wait_send()
    passed.wait_send()
    sums = QuadSum(place, low_all, near, pair, far, quad_send, quad_recv)
    normed_grad_rows(1 - core)
    sums.start()
    normed_grad_rows(core)
    sums.relay()
    pair_copies[1].start()

    def store(index):
        slot = index % 2
        return pltpu.make_async_copy(
            staged.at[slot], query_grad.at[lanes_at(index, 256)], store_sem.at[slot]
        )

    def weight_grad_rows(index, carry):
        at = lanes_at(index, 256)
        left = normed_ref[:, :, :, at].reshape(rows, 256)

        @pl.when(index > 1)
        def _():
            store(index).wait()

        for first in range(0, heads * head, 512):
            staged[index % 2, :, first : first + 512] = tn_dot(
                left, low_grads[:, first : first + 512]
            ).astype(low)
        store(index).start()
        both = tn_dot(left, low_grads[:, heads * head :]).astype(low)
        key_grad[at, :] = both[:, :head]
        value_grad[at, :] = both[:, head:]
        return carry

    lax.fori_loop(0, width // 256, weight_grad_rows, 0)
    for index in range(2):
        store(index).wait()
    out_ring.close()
    moe_own = out_side[level].astype(wide)
    normed_grad = sums.total()
    tokens = dealt_rows(False)
    factor = lax.rsqrt(jnp.mean(tokens * tokens, axis=-1, keepdims=True) + epsilon)
    scaled = normed_grad * attn_gain[...]
    inner = jnp.mean(scaled * tokens, axis=-1, keepdims=True)
    attn_gain_part[...] = jnp.sum(normed_grad * tokens * factor, axis=0, keepdims=True)
    token_grad = residual_grad[...] + factor * (scaled - tokens * (factor * factor) * inner)
    finished_ref[:, :half] = (residual_ref[...] + moe_own).reshape(members, half, width).astype(low)
    finished_ref[:, half:] = token_grad.reshape(members, half, width).astype(low)

    for turn in range(place.levels):
        weight_ring.take_side(turn)
        if turn + 2 < place.levels:
            weight_ring.side(weight_ring.target(turn + 2)).start()
        weight_ring.take_chain(turn)
    weight_ring.close()
    head_rows = out_grad.shape[0]
    here = out_own.at[lanes_at(core, head_rows)]
    there = out_own.at[lanes_at(1 - core, head_rows)]
    kept = pltpu.make_async_copy(
        weight_side.at[level, :, lanes_at(core, lanes)], here, keep_sem.at[1]
    )
    swap = remote(
        weight_side.at[level, :, lanes_at(1 - core, lanes)],
        here,
        swap_send.at[1],
        swap_recv.at[1],
        place.mate,
    )
    swap.start()
    kept.start()
    kept.wait()
    remote(there, there, swap_send.at[1], swap_recv.at[1], place.mate).wait_recv()
    swap.wait_send()
    for copy in pair_copies:
        copy.wait()
    to_mate.wait_send()
    sums.drain()
    out_ring.drain()
    weight_ring.drain()


def attend_back_layer(
    experts,
    entry,
    residual,
    gates,
    dealt,
    router,
    gain_vecs,
    mixed,
    probs,
    query_low,
    key_low,
    value_low,
    query_pre,
    key_pre,
    tables,
    normed,
    query_w,
    key_w,
    value_w,
    out_w,
    out_part,
    gate_part,
    up_part,
):
    own_rows, width = residual.shape
    members = dealt.shape[0]
    levels = members // 4
    rows = 4 * own_rows
    heads_width, head = query_w.shape[1], key_w.shape[1]
    lanes = width // members
    wide, low = jnp.float32, jnp.bfloat16
    vmem = pl.BlockSpec(memory_space=pltpu.VMEM)
    anywhere = pl.BlockSpec(memory_space=pl.ANY)
    shape = jax.ShapeDtypeStruct
    dma = pltpu.SemaphoreType.DMA
    return pl.pallas_call(
        functools.partial(attend_back_kernel, experts),
        name="attend_back_layer",
        out_shape=[
            shape(dealt.shape, low),
            shape((2 * heads_width, lanes), low),
            shape((width, heads_width), low),
            shape((width, head), low),
            shape((width, head), low),
            shape((width, 128), wide),
            shape((1, width), wide),
            shape((1, width), wide),
            shape((1, head), wide),
            shape((1, head), wide),
            shape((width, gate_part.shape[1] // 2), low),
            shape((width, up_part.shape[1] // 2), low),
        ],
        in_specs=[vmem] * 23 + [anywhere] * 3,
        out_specs=[vmem] * 2 + [anywhere] + [vmem] * 7 + [anywhere] * 2,
        scratch_shapes=[
            pltpu.VMEM((own_rows, width), wide),
            pltpu.VMEM((2, 2, own_rows, width), low),
            pltpu.VMEM((rows, heads_width), low),
            pltpu.VMEM((rows, heads_width + 2 * head), low),
            pltpu.VMEM((rows, head), wide),
            pltpu.VMEM((rows, head), wide),
            pltpu.VMEM((heads_width, width), low),
            pltpu.VMEM((members // 2, own_rows, width), low),
            pltpu.VMEM((members // 2, own_rows, width), low),
            pltpu.VMEM((levels, own_rows, width), low),
            pltpu.VMEM((levels + 1, own_rows, width), low),
            pltpu.VMEM((levels, heads_width, 2 * lanes), low),
            pltpu.VMEM((levels + 1, heads_width, 2 * lanes), low),
            pltpu.VMEM((2, 256, heads_width), low),
        ]
        + QuadSum.scratch(own_rows, width)
        + [dma((3,)), dma((3,)), dma((2,)), dma((2,)), dma((2,)), dma((2,)), dma((2,)), dma((2,))]
        + ChainSum.semaphores(levels) * 2,
        compiler_params=pltpu.CompilerParams(
            collective_id=3, has_side_effects=True, vmem_limit_bytes=65_400_000
        ),
        cost_estimate=link_cost(120),
    )(
        entry,
        residual,
        gates,
        dealt,
        router,
        *gain_vecs,
        mixed,
        probs,
        query_low,
        key_low,
        value_low,
        query_pre,
        key_pre,
        *tables,
        normed,
        query_w,
        key_w,
        value_w,
        out_w,
        out_part,
        gate_part,
        up_part,
    )


def fast_body(
    tokens,
    lengths,
    routes,
    deal_order,
    cotangent,
    attn_gain,
    query_gain,
    key_gain,
    moe_gain,
    w_query,
    key_projection_matrix,
    value_projection_matrix,
    w_out,
    w_router,
    w_gate,
    w_up,
    w_down,
):
    own_rows, model_width = tokens.shape
    head_dim = query_gain.shape[0]
    chip_count = lax.axis_size("chip")
    core_count = lax.axis_size("core")
    tp_count = lax.axis_size("tp")
    core_index = lax.axis_index("core")
    tp_index = lax.axis_index("tp")
    fsdp_count = chip_count * core_count
    fsdp_index = lax.axis_index("chip") * core_count + core_index
    slice_rows = own_rows // fsdp_count
    group_rows = tp_count * own_rows
    quad_rows = core_count * group_rows
    plane = ("chip", "core")
    quad = ("core", "tp")
    peer_ids = jnp.arange(fsdp_count, dtype=jnp.int32)
    wanted = (peer_ids - fsdp_index) % fsdp_count
    send_pick = jnp.sum(
        jnp.where(deal_order[None, :] == wanted[:, None], peer_ids[None, :], 0), axis=1
    )
    back_pick = (deal_order + fsdp_index) % fsdp_count

    def slices_of(values):
        return values.reshape(fsdp_count, slice_rows, model_width)

    def two_of(dealt):
        return (
            dealt[:, :slice_rows].reshape(own_rows, model_width),
            dealt[:, slice_rows:].reshape(own_rows, model_width),
        )

    outgoing = jnp.take(
        jnp.concatenate([slices_of(tokens), slices_of(cotangent)], axis=1), send_pick, axis=0
    )
    down_full = lax.all_gather(w_down[0], "tp", axis=0, tiled=True)
    frequency = rope_base ** (-(jnp.arange(head_dim // 2, dtype=jnp.float32) * (2.0 / head_dim)))
    frequency = jnp.concatenate([frequency, frequency])[None, :]
    padded_lengths = jnp.pad(lengths, ((0, 7), (0, 128 - lengths.shape[1])))
    (
        dealt,
        normed,
        cosine_wide,
        sine_wide,
        mask,
        query_part,
        key_part,
        value_part,
        out_part,
        gate_full,
        up_full,
    ) = open_layer(
        outgoing,
        attn_gain[None, :],
        padded_lengths,
        lengths.shape[1],
        frequency,
        w_query,
        key_projection_matrix,
        value_projection_matrix,
        w_out,
        w_gate[0],
        w_up[0],
    )
    query_part = query_part.reshape(model_width, -1)
    key_part = key_part.reshape(model_width, -1)
    value_part = value_part.reshape(model_width, -1)
    experts = w_router.shape[1]
    own_routes = lax.dynamic_slice_in_dim(routes, tp_index * own_rows, own_rows, 0)
    chosen = jnp.any(
        own_routes[:, :, None] == jnp.arange(128, dtype=jnp.int32)[None, None, :], axis=1
    ).astype(jnp.float32)
    router_wide = jnp.pad(w_router, ((0, 0), (0, 128 - experts)))
    (
        upstream_all,
        moe_ext,
        residual,
        gates,
        query_pre,
        query_low,
        key_before_norm,
        key_low,
        value_low,
        probs_low,
        mixed_low,
    ) = attend_layer(
        experts,
        normed,
        query_part,
        key_part,
        value_part,
        out_part,
        (cosine_wide, sine_wide, mask),
        dealt,
        (query_gain[None, :], key_gain[None, :], moe_gain[None, :]),
        router_wide,
        chosen,
    )
    upstream_all = upstream_all.reshape(fsdp_count * own_rows, model_width)
    entry_ext, moe_out, grad_w_gate, grad_w_up, grad_w_down = expert_layer(
        moe_ext, upstream_all, gate_full, up_full, down_full, experts
    )
    (
        finished,
        grad_w_out,
        grad_w_query,
        grad_w_key,
        grad_w_value,
        router_grad,
        attn_gain_part,
        moe_gain_part,
        query_gain_part,
        key_gain_part,
        gate_arrived,
        up_arrived,
    ) = attend_back_layer(
        experts,
        entry_ext,
        residual,
        gates,
        dealt,
        router_wide,
        (attn_gain[None, :], moe_gain[None, :], query_gain[None, :], key_gain[None, :]),
        mixed_low,
        probs_low,
        query_low,
        key_low,
        value_low,
        query_pre,
        key_before_norm,
        (cosine_wide, sine_wide),
        normed,
        query_part,
        key_part,
        value_part,
        out_part,
        moe_out.reshape(chip_count, core_count, own_rows, model_width),
        grad_w_gate,
        grad_w_up,
    )
    router_grad = router_grad[:, :experts]
    small = jnp.concatenate(
        [
            attn_gain_part[0],
            moe_gain_part[0],
            query_gain_part[0],
            key_gain_part[0],
            router_grad.reshape(-1),
        ]
    )
    small_rows = -(-small.shape[0] // (fsdp_count * 8 * 128)) * 8
    small = jnp.pad(small, (0, fsdp_count * small_rows * 128 - small.shape[0]))
    (
        returned,
        small,
        grad_w_query,
        grad_w_key,
        grad_w_value,
        down_arrived,
    ) = close_layer(
        finished,
        small.reshape(fsdp_count, small_rows, 128),
        grad_w_query,
        grad_w_key,
        grad_w_value,
        grad_w_down,
    )

    def pair_sum(parts, arrived, dim):
        size = arrived.shape[dim]
        mine = lax.dynamic_slice_in_dim(parts, tp_index * size, size, dim)
        return mine.astype(jnp.float32) + arrived.astype(jnp.float32)

    output, grad_input = two_of(jnp.take(returned, back_pick, axis=0))
    grad_input = grad_input.astype(jnp.float32)
    bounds = [model_width, 2 * model_width, 2 * model_width + head_dim]
    bounds += [bounds[2] + head_dim, bounds[2] + head_dim + router_grad.size]
    grad_attn_gain, grad_moe_gain, grad_query_gain, grad_key_gain, grad_w_router, _ = jnp.split(
        small.reshape(-1), bounds
    )
    grad_w_router = grad_w_router.reshape(model_width, experts)
    return (
        output,
        grad_input,
        grad_attn_gain,
        grad_query_gain,
        grad_key_gain,
        grad_moe_gain,
        grad_w_query.astype(jnp.float32),
        grad_w_key.astype(jnp.float32),
        grad_w_value.astype(jnp.float32),
        grad_w_out.astype(jnp.float32),
        grad_w_router,
        pair_sum(grad_w_gate, gate_arrived, 1)[None],
        pair_sum(grad_w_up, up_arrived, 1)[None],
        pair_sum(grad_w_down, down_arrived, 0)[None],
    )


def solution(mesh):
    fsdp_count, tp_count = mesh.shape["fsdp"], mesh.shape["tp"]
    chips = Mesh(mesh.devices.reshape(fsdp_count // 2, 2, tp_count), ("chip", "core", "tp"))
    dense = fsdp_count <= 16
    fsdp = ("chip", "core") if dense else "fsdp"
    every = ("chip", "core", "tp") if dense else ("fsdp", "tp")
    return jax.shard_map(
        fast_body if dense else body,
        mesh=chips if dense else mesh,
        in_specs=(
            P(every, None),
            P(fsdp, None),
            P(fsdp, None),
            P(),
            P(every, None),
            P(),
            P(),
            P(),
            P(),
            P(fsdp, "tp"),
            P(fsdp, "tp"),
            P(fsdp, "tp"),
            P("tp", fsdp),
            P(),
            P(fsdp, None, "tp"),
            P(fsdp, None, "tp"),
            P(fsdp, "tp", None),
        ),
        out_specs=(
            P(every, None),
            P(every, None),
            P(),
            P(),
            P(),
            P(),
            P(fsdp, "tp"),
            P(fsdp, "tp"),
            P(fsdp, "tp"),
            P("tp", fsdp),
            P(),
            P(fsdp, None, "tp"),
            P(fsdp, None, "tp"),
            P(fsdp, "tp", None),
        ),
        check_vma=False,
    )
```

```python
import functools

import jax
import jax.numpy as jnp
from jax import lax
from jax.experimental import pallas as pl
from jax.experimental.pallas import tpu as pltpu
from jax.sharding import Mesh
from jax.sharding import PartitionSpec as P

epsilon = 1e-06
rope_base = 1000000.0
masked_score = -1e30


def row_norm(values, gain_vec):
    factor = lax.rsqrt(jnp.mean(values * values, axis=-1, keepdims=True) + epsilon)
    return (values * factor * gain_vec, factor)


def norm_back(values, factor, gain_vec, upstream):
    scaled = upstream * gain_vec
    inner_term = jnp.mean(scaled * values, axis=-1, keepdims=True)
    return (factor * (scaled - values * (factor * factor) * inner_term), upstream * values * factor)


def seq_layout(seq_lengths, row_count):
    seq_ends = jnp.cumsum(seq_lengths)
    row_ids = jnp.arange(row_count, dtype=jnp.int32)
    segment = jnp.sum((row_ids[:, None] >= seq_ends[None, :]).astype(jnp.int32), axis=1)
    seq_starts = seq_ends - seq_lengths
    chosen = segment[:, None] == jnp.arange(seq_lengths.shape[0], dtype=jnp.int32)[None, :]
    position = row_ids - jnp.sum(jnp.where(chosen, seq_starts[None, :], 0), axis=1)
    return (segment, position)


def rotary(position, head_width):
    half_width = head_width // 2
    inverse_freq = rope_base ** (-(jnp.arange(half_width, dtype=jnp.float32) * (2.0 / head_width)))
    angles = position.astype(jnp.float32)[:, None] * inverse_freq[None, :]
    return (jnp.cos(angles)[:, None, :], jnp.sin(angles)[:, None, :])


def rotate(values, cosine_table, sine_table):
    half_width = values.shape[-1] // 2
    front_half = values[..., :half_width]
    back_half = values[..., half_width:]
    return jnp.concatenate(
        [
            front_half * cosine_table - back_half * sine_table,
            back_half * cosine_table + front_half * sine_table,
        ],
        axis=-1,
    )


def rotate_back(upstream, cosine_table, sine_table):
    half_width = upstream.shape[-1] // 2
    front_half = upstream[..., :half_width]
    back_half = upstream[..., half_width:]
    return jnp.concatenate(
        [
            front_half * cosine_table + back_half * sine_table,
            back_half * cosine_table - front_half * sine_table,
        ],
        axis=-1,
    )


def slot_table(route_rows, expert_count, capacity):
    row_count = route_rows.shape[0] * route_rows.shape[1]
    flat_routes = route_rows.reshape(row_count)
    expert_hits = (
        flat_routes[:, None] == jnp.arange(expert_count, dtype=jnp.int32)[None, :]
    ).astype(jnp.int32)
    earlier = jnp.cumsum(expert_hits, axis=0) - expert_hits
    slot_index = jnp.sum(earlier * expert_hits, axis=1)
    slot_place = flat_routes * capacity + slot_index
    slot_rows = jnp.full((expert_count * capacity,), row_count, jnp.int32)
    slot_rows = slot_rows.at[slot_place].set(jnp.arange(row_count, dtype=jnp.int32))
    return (slot_place, slot_rows.reshape(expert_count, capacity))


def contract_rows(left, right):
    return lax.dot_general(
        left, right, (((0,), (0,)), ((), ())), preferred_element_type=jnp.float32
    )


def contract_last(left, right):
    return lax.dot_general(
        left, right, (((1,), (1,)), ((), ())), preferred_element_type=jnp.float32
    )


def body(
    tokens,
    lengths,
    routes,
    deal_order,
    cotangent,
    attn_gain,
    query_gain,
    key_gain,
    moe_gain,
    w_query,
    key_projection_matrix,
    value_projection_matrix,
    w_out,
    w_router,
    w_gate,
    w_up,
    w_down,
):
    half_rows = tokens.shape[0]
    model_width = tokens.shape[1]
    head_dim = query_gain.shape[0]
    score_scale = head_dim ** (-0.5)
    fsdp_count = lax.axis_size("fsdp")
    tp_count = lax.axis_size("tp")
    fsdp_index = lax.axis_index("fsdp")
    tp_index = lax.axis_index("tp")
    slice_rows = half_rows // fsdp_count
    group_rows = tp_count * half_rows
    own_start = tp_index * half_rows
    peer_ids = jnp.arange(fsdp_count, dtype=jnp.int32)
    wanted = (peer_ids - fsdp_index) % fsdp_count
    send_pick = jnp.sum(
        jnp.where(deal_order[None, :] == wanted[:, None], peer_ids[None, :], 0), axis=1
    )
    back_pick = (deal_order + fsdp_index) % fsdp_count

    def deal_copies(values):
        slices = jnp.take(values.reshape(fsdp_count, slice_rows, model_width), send_pick, axis=0)
        return jnp.broadcast_to(slices[None], (tp_count, fsdp_count, slice_rows, model_width))

    tokens_all, cotangent_all = (
        lax.all_to_all(
            lax.all_to_all(deal_copies(tokens), "tp", split_axis=0, concat_axis=0, tiled=True),
            "fsdp",
            split_axis=1,
            concat_axis=1,
            tiled=True,
        ),
        lax.all_to_all(
            lax.all_to_all(deal_copies(cotangent), "tp", split_axis=0, concat_axis=0, tiled=True),
            "fsdp",
            split_axis=1,
            concat_axis=1,
            tiled=True,
        ),
    )
    tokens_in = tokens_all.reshape(group_rows, model_width).astype(jnp.float32)
    upstream = cotangent_all.reshape(group_rows, model_width).astype(jnp.float32)
    attn_in, attn_factor = row_norm(tokens_in, attn_gain)
    normed_all = attn_in.astype(jnp.bfloat16)
    query_full, key_full, value_full, out_full = (
        lax.all_gather(w_query, "fsdp", axis=0, tiled=True),
        lax.all_gather(key_projection_matrix, "fsdp", axis=0, tiled=True),
        lax.all_gather(value_projection_matrix, "fsdp", axis=0, tiled=True),
        lax.all_gather(w_out, "fsdp", axis=1, tiled=True),
    )
    query_heads = query_full.shape[1] // head_dim
    kv_heads = key_full.shape[1] // head_dim
    group_size = query_heads // kv_heads
    segment, position = seq_layout(lengths[0], group_rows)
    cosine_table, sine_table = rotary(position, head_dim)
    row_ids = jnp.arange(group_rows)
    allowed = (segment[:, None] == segment[None, :]) & (row_ids[None, :] <= row_ids[:, None])
    query_pre = jnp.dot(normed_all, query_full, preferred_element_type=jnp.float32).reshape(
        group_rows, query_heads, head_dim
    )
    query_normed, query_factor = row_norm(query_pre, query_gain)
    query_low = (
        rotate(query_normed, cosine_table, sine_table)
        .astype(jnp.bfloat16)
        .reshape(group_rows, kv_heads, group_size, head_dim)
    )
    key_before_norm = jnp.dot(normed_all, key_full, preferred_element_type=jnp.float32).reshape(
        group_rows, kv_heads, head_dim
    )
    key_normed, key_factor = row_norm(key_before_norm, key_gain)
    key_low = rotate(key_normed, cosine_table, sine_table).astype(jnp.bfloat16)
    value_low = (
        jnp.dot(normed_all, value_full, preferred_element_type=jnp.float32)
        .astype(jnp.bfloat16)
        .reshape(group_rows, kv_heads, head_dim)
    )
    scores = (
        jnp.einsum("qkgd,tkd->kgqt", query_low, key_low, preferred_element_type=jnp.float32)
        * score_scale
    )
    scores = jnp.where(allowed, scores, masked_score)
    row_peak = jnp.max(scores, axis=-1, keepdims=True)
    exponent = jnp.exp(scores - row_peak)
    totals = jnp.sum(exponent, axis=-1, keepdims=True)
    log_total = row_peak + jnp.log(totals)
    attn_probs = (exponent / totals).astype(jnp.bfloat16)
    attn_mixed = jnp.einsum(
        "kgqt,tkd->qkgd", attn_probs, value_low, preferred_element_type=jnp.float32
    )
    mixed_low = attn_mixed.reshape(group_rows, query_heads * head_dim).astype(jnp.bfloat16)
    attn_part = jnp.dot(mixed_low, out_full, preferred_element_type=jnp.float32)
    residual = tokens_in + lax.psum(attn_part, "tp")
    moe_in, moe_factor = row_norm(residual, moe_gain)
    moe_low = moe_in.astype(jnp.bfloat16)
    logits = jnp.dot(moe_low, w_router, preferred_element_type=jnp.float32)
    experts = w_router.shape[1]
    top_count = routes.shape[1]
    chosen = routes[:, :, None] == jnp.arange(experts, dtype=jnp.int32)[None, None, :]
    selected = jnp.sum(jnp.where(chosen, logits[:, None, :], 0.0), axis=-1)
    gate_peak = jnp.max(selected, axis=-1, keepdims=True)
    gate_exp = jnp.exp(selected - gate_peak)
    gate_probs = gate_exp / jnp.sum(gate_exp, axis=-1, keepdims=True)
    capacity = max(2, 3 * group_rows * top_count // (2 * experts))
    slot_place, slot_rows = slot_table(routes, experts, capacity)
    part_cap = capacity // tp_count
    slot_start = tp_index * part_cap
    gate_full, up_full, down_full = (
        lax.all_gather(w_gate, "tp", axis=2, tiled=True),
        lax.all_gather(w_up, "tp", axis=2, tiled=True),
        lax.all_gather(w_down, "tp", axis=1, tiled=True),
    )
    sent_rows = lax.dynamic_slice_in_dim(slot_rows, slot_start, part_cap, 1)
    slot_expert = slot_place // capacity
    slot_offset = slot_place % capacity - slot_start
    in_half = (slot_offset >= 0) & (slot_offset < part_cap)
    local_place = jnp.where(in_half, slot_expert * part_cap + slot_offset, experts * part_cap)
    padded = jnp.concatenate([moe_low, jnp.zeros((1, model_width), jnp.bfloat16)], axis=0)
    arrived = lax.all_to_all(
        padded[sent_rows // top_count], "fsdp", split_axis=0, concat_axis=0, tiled=True
    )
    local_experts = w_gate.shape[0]
    sources = experts // local_experts
    slot_count = sources * part_cap
    ff_part = w_gate.shape[2]

    def to_experts(values):
        return jnp.transpose(
            values.reshape(sources, local_experts, part_cap, model_width), (1, 0, 2, 3)
        ).reshape(local_experts, slot_count, model_width)

    def to_sources(values):
        width = values.shape[-1]
        return jnp.transpose(
            values.reshape(local_experts, sources, part_cap, width), (1, 0, 2, 3)
        ).reshape(experts, part_cap, width)

    def pick_rows(values):
        flat = values.reshape(experts * part_cap, tp_count * model_width)
        flat = jnp.concatenate([flat, jnp.zeros((1, tp_count * model_width), jnp.bfloat16)], axis=0)
        gathered = flat[local_place].reshape(group_rows, top_count, tp_count, model_width)
        return jnp.sum(gathered.astype(jnp.float32), axis=2)

    expert_rows = to_experts(arrived)
    gate_val = jnp.einsum(
        "esd,edf->esf", expert_rows, gate_full, preferred_element_type=jnp.float32
    )
    up_val = jnp.einsum("esd,edf->esf", expert_rows, up_full, preferred_element_type=jnp.float32)
    sigmoid_val = jax.nn.sigmoid(gate_val)
    swish_val = gate_val * sigmoid_val
    hidden_low = (swish_val * up_val).astype(jnp.bfloat16)
    hidden_blocks = hidden_low.reshape(local_experts, slot_count, tp_count, ff_part)
    down_blocks = down_full.reshape(local_experts, tp_count, ff_part, model_width)
    expert_out = (
        jnp.einsum(
            "esbf,ebfd->esbd", hidden_blocks, down_blocks, preferred_element_type=jnp.float32
        )
        .astype(jnp.bfloat16)
        .reshape(local_experts, slot_count, tp_count * model_width)
    )
    returned = lax.all_to_all(
        to_sources(expert_out), "fsdp", split_axis=0, concat_axis=0, tiled=True
    )
    picked = pick_rows(returned)
    moe_part = jnp.sum(gate_probs[:, :, None] * picked, axis=1)
    gate_grad_part = jnp.sum(upstream[:, None, :] * picked, axis=-1)
    weighted = (
        (gate_probs[:, :, None] * upstream[:, None, :])
        .astype(jnp.bfloat16)
        .reshape(group_rows * top_count, model_width)
    )
    weighted = jnp.concatenate([weighted, jnp.zeros((1, model_width), jnp.bfloat16)], axis=0)
    grad_arrived = lax.all_to_all(
        weighted[sent_rows], "fsdp", split_axis=0, concat_axis=0, tiled=True
    )
    grad_slots = to_experts(grad_arrived)
    hidden_grad = jnp.einsum(
        "esd,ebfd->esbf", grad_slots, down_blocks, preferred_element_type=jnp.float32
    ).reshape(local_experts, slot_count, tp_count * ff_part)
    swish_slope = sigmoid_val * (1.0 + gate_val * (1.0 - sigmoid_val))
    gate_val_grad = (hidden_grad * up_val * swish_slope).astype(jnp.bfloat16)
    up_val_grad = (hidden_grad * swish_val).astype(jnp.bfloat16)
    grad_w_down = jnp.einsum(
        "esbf,esd->ebfd", hidden_blocks, grad_slots, preferred_element_type=jnp.float32
    ).reshape(local_experts, tp_count * ff_part, model_width)
    grad_w_gate = jnp.einsum(
        "esd,esf->edf", expert_rows, gate_val_grad, preferred_element_type=jnp.float32
    )
    grad_w_up = jnp.einsum(
        "esd,esf->edf", expert_rows, up_val_grad, preferred_element_type=jnp.float32
    )
    gate_blocks = gate_full.reshape(local_experts, model_width, tp_count, ff_part)
    up_blocks = up_full.reshape(local_experts, model_width, tp_count, ff_part)
    entry_grad = (
        (
            jnp.einsum(
                "esbf,edbf->esbd",
                gate_val_grad.reshape(local_experts, slot_count, tp_count, ff_part),
                gate_blocks,
                preferred_element_type=jnp.float32,
            )
            + jnp.einsum(
                "esbf,edbf->esbd",
                up_val_grad.reshape(local_experts, slot_count, tp_count, ff_part),
                up_blocks,
                preferred_element_type=jnp.float32,
            )
        )
        .astype(jnp.bfloat16)
        .reshape(local_experts, slot_count, tp_count * model_width)
    )
    sent_back = lax.all_to_all(
        to_sources(entry_grad), "fsdp", split_axis=0, concat_axis=0, tiled=True
    )
    expert_grad = jnp.sum(pick_rows(sent_back), axis=1)
    grad_w_gate, grad_w_up, grad_w_down = (
        lax.psum_scatter(
            grad_w_gate.astype(jnp.bfloat16), "tp", scatter_dimension=2, tiled=True
        ).astype(jnp.float32),
        lax.psum_scatter(
            grad_w_up.astype(jnp.bfloat16), "tp", scatter_dimension=2, tiled=True
        ).astype(jnp.float32),
        lax.psum_scatter(
            grad_w_down.astype(jnp.bfloat16), "tp", scatter_dimension=1, tiled=True
        ).astype(jnp.float32),
    )
    moe_grad, gate_grad = (
        lax.psum(expert_grad.astype(jnp.bfloat16), "tp").astype(jnp.float32),
        lax.psum(gate_grad_part.astype(jnp.bfloat16), "tp").astype(jnp.float32),
    )
    gate_inner = jnp.sum(gate_probs * gate_grad, axis=-1, keepdims=True)
    selected_grad = gate_probs * (gate_grad - gate_inner)
    logit_grad = jnp.sum(jnp.where(chosen, selected_grad[:, :, None], 0.0), axis=1).astype(
        jnp.bfloat16
    )
    moe_grad = moe_grad + contract_last(logit_grad, w_router)
    router_grad = contract_rows(
        lax.dynamic_slice_in_dim(moe_low, own_start, half_rows, 0),
        lax.dynamic_slice_in_dim(logit_grad, own_start, half_rows, 0),
    )
    residual_from_norm, moe_gain_terms = norm_back(residual, moe_factor, moe_gain, moe_grad)
    residual_grad = upstream + residual_from_norm
    moe_gain_grad = jnp.sum(
        lax.dynamic_slice_in_dim(moe_gain_terms, own_start, half_rows, 0), axis=0
    )
    residual_low = residual_grad.astype(jnp.bfloat16)
    mixed_grad = (
        contract_last(residual_low, out_full)
        .astype(jnp.bfloat16)
        .reshape(group_rows, kv_heads, group_size, head_dim)
    )
    grad_w_out = contract_rows(mixed_low, residual_low)
    scores = (
        jnp.einsum("qkgd,tkd->kgqt", query_low, key_low, preferred_element_type=jnp.float32)
        * score_scale
    )
    scores = jnp.where(allowed, scores, masked_score)
    probs_full = jnp.exp(scores - log_total)
    prob_grad = jnp.einsum(
        "qkgd,tkd->kgqt", mixed_grad, value_low, preferred_element_type=jnp.float32
    )
    prob_inner = jnp.sum(probs_full * prob_grad, axis=-1, keepdims=True)
    score_grad = (probs_full * (prob_grad - prob_inner)).astype(jnp.bfloat16)
    query_grad = (
        jnp.einsum(
            "kgqt,tkd->qkgd", score_grad, key_low, preferred_element_type=jnp.float32
        ).reshape(group_rows, query_heads, head_dim)
        * score_scale
    )
    key_grad = (
        jnp.einsum("kgqt,qkgd->tkd", score_grad, query_low, preferred_element_type=jnp.float32)
        * score_scale
    )
    value_grad = (
        jnp.einsum(
            "kgqt,qkgd->tkd",
            probs_full.astype(jnp.bfloat16),
            mixed_grad,
            preferred_element_type=jnp.float32,
        )
        .astype(jnp.bfloat16)
        .reshape(group_rows, kv_heads * head_dim)
    )
    query_pre_grad, query_gain_terms = norm_back(
        query_pre, query_factor, query_gain, rotate_back(query_grad, cosine_table, sine_table)
    )
    key_pre_grad, key_gain_terms = norm_back(
        key_before_norm, key_factor, key_gain, rotate_back(key_grad, cosine_table, sine_table)
    )
    query_pre_low = query_pre_grad.astype(jnp.bfloat16).reshape(group_rows, query_heads * head_dim)
    key_pre_low = key_pre_grad.astype(jnp.bfloat16).reshape(group_rows, kv_heads * head_dim)
    grad_w_query = contract_rows(normed_all, query_pre_low)
    grad_w_key = contract_rows(normed_all, key_pre_low)
    grad_w_value = contract_rows(normed_all, value_grad)
    normed_grad = (
        contract_last(query_pre_low, query_full)
        + contract_last(key_pre_low, key_full)
        + contract_last(value_grad, value_full)
    )
    normed_grad_own, moe_own = (
        lax.psum_scatter(
            normed_grad.astype(jnp.bfloat16), "tp", scatter_dimension=0, tiled=True
        ).astype(jnp.float32),
        lax.psum_scatter(
            moe_part.astype(jnp.bfloat16), "tp", scatter_dimension=0, tiled=True
        ).astype(jnp.float32),
    )
    tokens_own = lax.dynamic_slice_in_dim(tokens_in, own_start, half_rows, 0)
    factor_own = lax.dynamic_slice_in_dim(attn_factor, own_start, half_rows, 0)
    tokens_from_norm, attn_gain_terms = norm_back(
        tokens_own, factor_own, attn_gain, normed_grad_own
    )
    grad_group = lax.dynamic_slice_in_dim(residual_grad, own_start, half_rows, 0) + tokens_from_norm
    residual_own = lax.dynamic_slice_in_dim(residual, own_start, half_rows, 0)
    output_group = (residual_own + moe_own).astype(jnp.bfloat16)
    back_output, back_grad = (
        lax.all_to_all(
            output_group.astype(jnp.float32)
            .reshape(fsdp_count, slice_rows, model_width)
            .astype(jnp.bfloat16),
            "fsdp",
            split_axis=0,
            concat_axis=0,
            tiled=True,
        ).astype(jnp.float32),
        lax.all_to_all(
            grad_group.reshape(fsdp_count, slice_rows, model_width).astype(jnp.bfloat16),
            "fsdp",
            split_axis=0,
            concat_axis=0,
            tiled=True,
        ).astype(jnp.float32),
    )
    output = (
        jnp.take(back_output, back_pick, axis=0)
        .reshape(half_rows, model_width)
        .astype(jnp.bfloat16)
    )
    grad_input = jnp.take(back_grad, back_pick, axis=0).reshape(half_rows, model_width)
    grad_w_query, grad_w_key, grad_w_value, grad_w_out = (
        lax.psum_scatter(grad_w_query, "fsdp", scatter_dimension=0, tiled=True),
        lax.psum_scatter(grad_w_key, "fsdp", scatter_dimension=0, tiled=True),
        lax.psum_scatter(grad_w_value, "fsdp", scatter_dimension=0, tiled=True),
        lax.psum_scatter(grad_w_out, "fsdp", scatter_dimension=1, tiled=True),
    )
    grad_attn_gain, grad_query_gain, grad_key_gain, grad_moe_gain, grad_w_router = lax.psum(
        (
            jnp.sum(attn_gain_terms, axis=0),
            jnp.sum(query_gain_terms, axis=(0, 1)),
            jnp.sum(key_gain_terms, axis=(0, 1)),
            moe_gain_grad,
            router_grad,
        ),
        ("fsdp", "tp"),
    )
    return (
        output,
        grad_input,
        grad_attn_gain,
        grad_query_gain,
        grad_key_gain,
        grad_moe_gain,
        grad_w_query,
        grad_w_key,
        grad_w_value,
        grad_w_out,
        grad_w_router,
        grad_w_gate,
        grad_w_up,
        grad_w_down,
    )


def remote(src, dst, send_sem, recv_sem, target):
    return pltpu.make_async_remote_copy(
        src_ref=src,
        dst_ref=dst,
        send_sem=send_sem,
        recv_sem=recv_sem,
        device_id=target,
        device_id_type=pl.DeviceIdType.MESH,
    )


def greet(targets):
    barrier = pltpu.get_barrier_semaphore()
    for target in targets:
        pl.semaphore_signal(
            barrier, inc=1, device_id=target, device_id_type=pl.DeviceIdType.MESH
        )
    pl.semaphore_wait(barrier, len(targets))


def link_cost(microseconds):
    return pl.CostEstimate(flops=0, bytes_accessed=microseconds * 3_000_000, transcendentals=0)


class Place:
    def __init__(self):
        self.chips = lax.axis_size("chip")
        self.levels = self.chips // 2
        self.chip = lax.axis_index("chip")
        self.core = lax.axis_index("core")
        self.tp = lax.axis_index("tp")
        self.level = self.chip // 2
        self.side = self.chip % 2
        self.fsdp = self.chip * 2 + self.core
        self.mate = {"core": 1 - self.core}
        self.across = {"tp": 1 - self.tp}
        self.beside = {"chip": self.level * 2 + 1 - self.side}
        self.above = {"chip": lax.rem(self.chip + 2, self.chips)}
        self.below = {"chip": lax.rem(self.chip + self.chips - 2, self.chips)}
        top = self.levels - 1
        self.upper = self.level // (self.levels // 2)
        self.end = top * self.upper
        self.next = self.end + 1 - 2 * self.upper
        self.at_end = self.level == self.end
        self.at_next = self.level == self.next
        outward = self.level * 2 + self.side + 4 * self.upper - 2
        inward = self.level * 2 + self.side + 2 - 4 * self.upper
        self.outward = {"chip": lax.rem(outward + self.chips, self.chips)}
        self.inward = {"chip": lax.rem(inward + self.chips, self.chips)}

    def member(self, offset):
        count = 2 * self.chips
        index = lax.rem(self.fsdp + offset + count, count)
        return {"chip": index // 2, "core": lax.rem(index, 2)}, index

    def plane_targets(self):
        return [self.member(offset)[0] for offset in range(1, 2 * self.chips)]

    def ring_targets(self):
        return [self.above, self.below, self.beside]


def lower_half(ref):
    return ref.at[pl.ds(0, ref.shape[0] // 2)]


def upper_half(ref):
    return ref.at[pl.ds(ref.shape[0] // 2, ref.shape[0] // 2)]


class RowGather:
    def __init__(self, place, block, sems, hands=True):
        self.place, self.block, self.hands = place, block, hands
        (
            self.up_send,
            self.up_recv,
            self.down_send,
            self.down_recv,
            self.side_send,
            self.side_recv,
            self.hop_send,
            self.hop_recv,
        ) = sems[:8]
        if hands:
            self.hand_send, self.hand_recv = sems[8:10]

    @staticmethod
    def semaphores(levels, hands=True):
        dma = pltpu.SemaphoreType.DMA
        return [dma((levels,))] * 6 + [dma, dma] + ([dma((2 * levels,))] * 2 if hands else [])

    def climb(self, origin):
        piece, at = self.block(origin, self.place.core), origin // 2
        return remote(piece, piece, self.up_send.at[at], self.up_recv.at[at], self.place.above)

    def sink(self, origin):
        piece, at = self.block(origin, self.place.core), origin // 2
        return remote(piece, piece, self.down_send.at[at], self.down_recv.at[at], self.place.below)

    def cross(self, origin, half=False):
        piece, at = self.block(origin, self.place.core), origin // 2
        if half:
            piece = upper_half(piece)
        return remote(piece, piece, self.side_send.at[at], self.side_recv.at[at], self.place.beside)

    def hop(self, level, inward):
        piece = self.block(level * 2 + 1 - self.place.side, self.place.core)
        if not inward:
            piece = lower_half(piece)
        target = self.place.inward if inward else self.place.outward
        return remote(piece, piece, self.hop_send, self.hop_recv, target)

    def hand(self, origin, whose):
        piece = self.block(origin, whose)
        return remote(
            piece, piece, self.hand_send.at[origin], self.hand_recv.at[origin], self.place.mate
        )

    def pass_on(self, origin):
        place = self.place
        at = origin // 2
        skipped = place.at_next & (at == place.end)
        halved = place.at_end & (at == place.next)

        @pl.when(halved)
        def _():
            self.cross(origin, True).start()

        @pl.when(~skipped & ~halved)
        def _():
            self.cross(origin).start()

        self.give(origin)

    def give(self, origin):
        if self.hands:
            self.hand(origin, self.place.core).start()

    def start(self):
        place = self.place

        @pl.when(place.level < place.levels - 1)
        def _():
            self.climb(place.chip).start()

        @pl.when(place.level > 0)
        def _():
            self.sink(place.chip).start()

        self.pass_on(place.chip)

    def crossed(self, at):
        place = self.place
        origin = at * 2 + 1 - place.side
        skipped = place.at_next & (at == place.end)
        halved = place.at_end & (at == place.next)

        @pl.when(skipped)
        def _():
            self.hop(place.end, True).wait_recv()

        @pl.when(halved)
        def _():
            self.cross(origin, True).wait_recv()

        @pl.when(~skipped & ~halved)
        def _():
            self.cross(origin).wait_recv()

        @pl.when(place.at_end & (at == place.end))
        def _():
            self.hop(place.end, True).start()

        @pl.when(~halved)
        def _():
            self.give(origin)

    def finish(self):
        place = self.place

        @pl.when(place.at_end)
        def _():
            self.hop(place.next, False).wait_recv()
            self.give(place.next * 2 + 1 - place.side)

    def step(self, n):
        place = self.place
        level, side, top = place.level, place.side, place.levels - 1
        under, over = level - n, level + n

        @pl.when((n > 0) & (under >= 0))
        def _():
            origin = under * 2 + side
            self.climb(origin).wait_recv()

            @pl.when(level < top)
            def _():
                self.climb(origin).start()

            self.pass_on(origin)

        @pl.when((n > 0) & (over <= top))
        def _():
            origin = over * 2 + side
            self.sink(origin).wait_recv()

            @pl.when(level > 0)
            def _():
                self.sink(origin).start()

            self.pass_on(origin)

        @pl.when(place.at_next & (n == place.levels - 2))
        def _():
            self.hop(place.next, False).start()

        @pl.when((n > 0) & (under + 1 >= 0))
        def _():
            self.crossed(under + 1)

        @pl.when((n > 1) & (over - 1 <= top))
        def _():
            self.crossed(over - 1)

    def take_hands(self):
        place = self.place

        def taken(origin, carry):
            self.hand(origin, 1 - place.core).wait_recv()
            return carry

        lax.fori_loop(0, place.chips, taken, 0)

    def drain(self):
        place = self.place
        level, side, top = place.level, place.side, place.levels - 1

        def handed(origin, carry):
            self.hand(origin, place.core).wait_send()
            return carry

        if self.hands:
            lax.fori_loop(0, place.chips, handed, 0)

        def sent(at, carry):
            skipped = place.at_next & (at == place.end)
            halved = place.at_end & (at == place.next)

            @pl.when(halved)
            def _():
                self.cross(at * 2 + side, True).wait_send()

            @pl.when(~skipped & ~halved)
            def _():
                self.cross(at * 2 + side).wait_send()

            @pl.when((level < top) & (at <= level))
            def _():
                self.climb(at * 2 + side).wait_send()

            @pl.when((level > 0) & (at >= level))
            def _():
                self.sink(at * 2 + side).wait_send()

            return carry

        lax.fori_loop(0, place.levels, sent, 0)

        @pl.when(place.at_end)
        def _():
            self.hop(place.end, True).wait_send()

        @pl.when(place.at_next)
        def _():
            self.hop(place.next, False).wait_send()


class RowGathers:
    def __init__(self, place, block, sems):
        count = len(sems) // 10
        self.rings = []
        for i in range(count):

            def piece(origin, whose, i=i):
                whole = block(origin, whose)
                rows = whole.shape[0] // count
                return whole.at[pl.ds(i * rows, rows)]

            self.rings.append(RowGather(place, piece, sems[10 * i : 10 * i + 10]))

    @staticmethod
    def semaphores(levels):
        return RowGather.semaphores(levels) * 2

    def start(self):
        for ring in self.rings:
            ring.start()

    def step(self, n):
        for ring in self.rings:
            ring.step(n)

    def finish(self):
        for ring in self.rings:
            ring.finish()

    def take_hand(self, origin, whose):
        for ring in self.rings:
            ring.hand(origin, whose).wait_recv()

    def take_hands(self):
        for ring in self.rings:
            ring.take_hands()

    def drain(self):
        for ring in self.rings:
            ring.drain()


class ChainSum:
    def __init__(self, place, parts, side_buf, chain_buf, hop_buf, sems):
        self.place, self.parts = place, parts
        self.side_buf, self.chain_buf, self.hop_buf = side_buf, chain_buf, hop_buf
        (
            self.up_send,
            self.up_recv,
            self.down_send,
            self.down_recv,
            self.side_send,
            self.side_recv,
            self.hop_send,
            self.hop_recv,
            self.half_send,
            self.half_recv,
        ) = sems

    @staticmethod
    def semaphores(levels):
        dma = pltpu.SemaphoreType.DMA
        return [dma((levels,))] * 6 + [dma] * 4

    @staticmethod
    def buffers(levels, block, dtype=jnp.bfloat16):
        return [
            pltpu.VMEM((levels,) + block, dtype),
            pltpu.VMEM((levels + 1,) + block, dtype),
            pltpu.VMEM(block, dtype),
        ]

    def target(self, turn):
        place = self.place
        top = place.levels - 1
        far, near = top - turn // 2, turn // 2
        odd = turn % 2
        low_half = far * (1 - odd) + near * odd
        high_half = near * (1 - odd) + far * odd
        inner = low_half * (1 - place.upper) + high_half * place.upper
        outer = (top - turn) * (1 - place.upper) + turn * place.upper
        return jnp.where(place.at_end, outer, inner)

    def from_under(self, goal):
        return self.chain_buf.at[goal + 1]

    def from_over(self, goal):
        return self.chain_buf.at[goal]

    def other(self, goal):
        return self.parts(goal * 2 + 1 - self.place.side)

    def cross(self, source, target, goal):
        return remote(
            source, target, self.side_send.at[goal], self.side_recv.at[goal], self.place.beside
        )

    def whole(self, goal):
        return self.cross(self.other(goal), self.side_buf.at[goal], goal)

    def lifted(self, goal):
        return self.cross(self.hop_buf, self.side_buf.at[goal], goal)

    def upper(self, goal):
        return self.cross(upper_half(self.other(goal)), upper_half(self.side_buf.at[goal]), goal)

    def lower(self, goal):
        return remote(
            lower_half(self.hop_buf),
            lower_half(self.side_buf.at[goal]),
            self.half_send,
            self.half_recv,
            self.place.beside,
        )

    def hop_out(self):
        return remote(
            self.other(self.place.end), self.hop_buf, self.hop_send, self.hop_recv, self.place.outward
        )

    def hop_in(self):
        return remote(
            lower_half(self.other(self.place.next)),
            lower_half(self.hop_buf),
            self.hop_send,
            self.hop_recv,
            self.place.inward,
        )

    def up(self, goal):
        return remote(
            self.side_buf.at[goal],
            self.from_under(goal),
            self.up_send.at[goal],
            self.up_recv.at[goal],
            self.place.above,
        )

    def down(self, goal):
        return remote(
            self.side_buf.at[goal],
            self.from_over(goal),
            self.down_send.at[goal],
            self.down_recv.at[goal],
            self.place.below,
        )

    def cases(self, goal):
        place = self.place
        to_end, to_next = goal == place.end, goal == place.next
        return (
            place.at_end & to_end,
            place.at_end & to_next,
            place.at_next & to_end,
            place.at_next & to_next,
        )

    def send(self, goal):
        end_end, end_next, next_end, next_next = self.cases(goal)

        @pl.when(end_next)
        def _():
            self.hop_in().start()

        @pl.when(next_end)
        def _():
            self.hop_out().start()

        @pl.when(end_next | next_next)
        def _():
            self.upper(goal).start()

        @pl.when(~(end_end | end_next | next_end | next_next))
        def _():
            self.whole(goal).start()

    def send_joined(self):
        place, wide = self.place, jnp.float32
        hop = self.hop_buf

        @pl.when(place.at_end)
        def _():
            self.hop_out().wait_recv()
            total = hop[...].astype(wide) + self.other(place.end)[...].astype(wide)
            hop[...] = total.astype(hop.dtype)
            self.lifted(place.end).start()

        @pl.when(place.at_next)
        def _():
            self.hop_in().wait_recv()
            half = hop.shape[0] // 2
            own = lower_half(self.other(place.next))[...].astype(wide)
            hop[:half] = (hop[:half].astype(wide) + own).astype(hop.dtype)
            self.lower(place.next).start()

    def add(self, goal, ref):
        held = self.side_buf
        total = held[goal].astype(jnp.float32) + ref[...].astype(jnp.float32)
        held[goal] = total.astype(held.dtype)

    def take_side(self, goal):
        place = self.place
        level, top = place.level, place.levels - 1
        end_end, end_next, next_end, next_next = self.cases(goal)
        held = self.side_buf
        own = self.parts(goal * 2 + place.side)
        half = held.shape[1] // 2

        @pl.when(end_next)
        def _():
            self.upper(goal).wait_recv()
            total = held[goal, half:].astype(jnp.float32) + upper_half(own)[...].astype(jnp.float32)
            held[goal, half:] = total.astype(held.dtype)
            held[goal, :half] = lower_half(own)[...]

        @pl.when(next_end)
        def _():
            held[goal] = own[...]

        @pl.when(next_next)
        def _():
            self.upper(goal).wait_recv()
            self.lower(goal).wait_recv()

        @pl.when(~(end_next | next_end | next_next))
        def _():
            self.whole(goal).wait_recv()

        @pl.when(~(end_next | next_end))
        def _():
            self.add(goal, own)

        @pl.when((goal > level) & (level == 0))
        def _():
            self.up(goal).start()

        @pl.when((goal < level) & (level == top))
        def _():
            self.down(goal).start()

    def take_chain(self, goal):
        place = self.place
        level, top = place.level, place.levels - 1

        @pl.when((goal > level) & (level > 0))
        def _():
            self.up(goal).wait_recv()
            self.add(goal, self.from_under(goal))
            self.up(goal).start()

        @pl.when((goal < level) & (level < top))
        def _():
            self.down(goal).wait_recv()
            self.add(goal, self.from_over(goal))
            self.down(goal).start()

    def close(self):
        place = self.place
        level, top = place.level, place.levels - 1

        @pl.when(level > 0)
        def _():
            self.up(level).wait_recv()
            self.add(level, self.from_under(level))

        @pl.when(level < top)
        def _():
            self.down(level).wait_recv()
            self.add(level, self.from_over(level))

    def drain(self):
        place = self.place

        def goal_done(goal, carry):
            end_end, end_next, next_end, next_next = self.cases(goal)

            @pl.when(end_end)
            def _():
                self.lifted(goal).wait_send()

            @pl.when(end_next)
            def _():
                self.hop_in().wait_send()

            @pl.when(next_end)
            def _():
                self.hop_out().wait_send()

            @pl.when(next_next)
            def _():
                self.lower(goal).wait_send()

            @pl.when(end_next | next_next)
            def _():
                self.upper(goal).wait_send()

            @pl.when(~(end_end | end_next | next_end | next_next))
            def _():
                self.whole(goal).wait_send()

            @pl.when(goal > place.level)
            def _():
                self.up(goal).wait_send()

            @pl.when(goal < place.level)
            def _():
                self.down(goal).wait_send()

            return carry

        lax.fori_loop(0, place.levels, goal_done, 0)


def open_kernel(
    sequences,
    slices_ref,
    gain_ref,
    lengths_ref,
    frequency_ref,
    query_ref,
    key_ref,
    value_ref,
    out_ref,
    gate_ref,
    up_ref,
    dealt_ref,
    normed_ref,
    cosine_ref,
    sine_ref,
    mask_ref,
    query_all,
    key_all,
    value_all,
    out_all,
    gate_all,
    up_all,
    both_lengths_ref,
    deal_send,
    deal_recv,
    quad_send,
    quad_recv,
    swap_send,
    swap_recv,
    keep_sem,
    pair_send,
    pair_recv,
    pair_keep,
    *ring_sems,
):
    place = Place()
    core, chip = place.core, place.chip
    own_rows = query_ref.shape[0]
    quarter = query_all.shape[2]
    narrow = key_all.shape[2]
    head_rows = out_all.shape[0]
    lanes = out_ref.shape[1]
    members = 2 * place.chips
    greet(place.plane_targets() + [place.across])

    def deal_copy(offset, sending):
        target, index = place.member(offset if sending else -offset)
        return remote(
            slices_ref.at[index],
            dealt_ref.at[place.fsdp if sending else index],
            deal_send.at[offset - 1],
            deal_recv.at[offset - 1],
            target,
        )

    for offset in range(1, members):
        deal_copy(offset, True).start()

    def rows(who):
        return pl.ds(pl.multiple_of(who * own_rows, own_rows), own_rows)

    def columns(who, width):
        return pl.ds(pl.multiple_of(who * width, width), width)

    def spots(who):
        lane_start = pl.multiple_of((2 * chip + core) * lanes, lanes)
        return [
            (query_ref.at[:, columns(who, quarter)], query_all.at[chip, rows(core)]),
            (key_ref.at[:, columns(who, narrow)], key_all.at[chip, rows(core)]),
            (value_ref.at[:, columns(who, narrow)], value_all.at[chip, rows(core)]),
            (
                out_ref.at[pl.ds(pl.multiple_of(who * head_rows, head_rows), head_rows)],
                out_all.at[:, pl.ds(lane_start, lanes)],
            ),
        ]

    def arrivals():
        lane_start = pl.multiple_of((2 * chip + 1 - core) * lanes, lanes)
        return [
            query_all.at[chip, rows(1 - core)],
            key_all.at[chip, rows(1 - core)],
            value_all.at[chip, rows(1 - core)],
            out_all.at[:, pl.ds(lane_start, lanes)],
        ]

    sends = [
        remote(src, dst, swap_send.at[i], swap_recv.at[i], place.mate)
        for i, (src, dst) in enumerate(spots(1 - core))
    ]
    keeps = [
        pltpu.make_async_copy(src, dst, keep_sem.at[i])
        for i, (src, dst) in enumerate(spots(core))
    ]
    mate_lengths = remote(
        lengths_ref, both_lengths_ref.at[core], swap_send.at[4], swap_recv.at[4], place.mate
    )
    own_lengths = pltpu.make_async_copy(lengths_ref, both_lengths_ref.at[core], keep_sem.at[4])
    own_slice = pltpu.make_async_copy(
        slices_ref.at[place.fsdp], dealt_ref.at[place.fsdp], keep_sem.at[5]
    )
    own_slice.start()
    units = gate_ref.shape[1]

    def halves(who):
        at = pl.ds(pl.multiple_of(who * units, units), units)
        return [gate_all.at[:, at], up_all.at[:, at]]

    shards = (gate_ref, up_ref)
    pair_copies = []
    for i, (src, dst) in enumerate(zip(shards, halves(place.tp))):
        pair_copies.append(
            (
                remote(src, dst, pair_send.at[i], pair_recv.at[i], place.across),
                pltpu.make_async_copy(src, dst, pair_keep.at[i]),
            )
        )
    for i in range(4):
        sends[i].start()
        keeps[i].start()
    mate_lengths.start()
    own_lengths.start()

    out_lanes = 2 * lanes
    views = [
        lambda who, core: query_all.at[who],
        lambda who, core: key_all.at[who],
        lambda who, core: value_all.at[who],
        lambda who, core: out_all.at[:, lanes_at(who, out_lanes)],
    ]
    rings = [
        RowGather(place, view, ring_sems[8 * i : 8 * i + 8], hands=False)
        for i, view in enumerate(views)
    ]
    landed = arrivals()
    for i in range(4):
        keeps[i].wait()
        sends[i].wait_send()
        remote(landed[i], landed[i], swap_send.at[i], swap_recv.at[i], place.mate).wait_recv()
        rings[i].start()

    own_slice.wait()
    for offset in range(1, members):
        deal_copy(offset, False).wait_recv()
    tp = place.tp
    half = slices_ref.shape[1] // 2
    step_rows = 4
    for start in range(0, members, step_rows):
        x = dealt_ref[start : start + step_rows].astype(jnp.float32)[:, :half]
        x = x.reshape(step_rows * half, x.shape[2])
        factor = lax.rsqrt(jnp.mean(x * x, axis=-1, keepdims=True) + epsilon)
        normed_ref[core, tp, start * half : (start + step_rows) * half, :] = (
            x * factor * gain_ref[...]
        ).astype(jnp.bfloat16)
    mine = normed_ref.at[core, tp]
    to_mate = remote(mine, mine, quad_send.at[0], quad_recv.at[0], place.mate)
    to_across = remote(mine, mine, quad_send.at[1], quad_recv.at[1], place.across)
    to_across.start()
    to_mate.start()
    for both in pair_copies:
        both[0].start()
        both[1].start()
    levels = place.levels
    own_lengths.wait()
    mate_lengths.wait_send()
    theirs = both_lengths_ref.at[1 - core]
    remote(theirs, theirs, swap_send.at[4], swap_recv.at[4], place.mate).wait_recv()
    group = mask_ref.shape[1]
    head = cosine_ref.shape[1]
    across_sign = jnp.where(
        lax.broadcasted_iota(jnp.int32, (group, head), 1) < head // 2, -1.0, 1.0
    )
    for which in range(2):
        ends = []
        for at in range(sequences):
            length = both_lengths_ref[which, 0:1, at : at + 1]
            ends.append(length if at == 0 else ends[-1] + length)

        def segment_start(place_ids):
            start = jnp.zeros_like(place_ids)
            for end in ends:
                start = jnp.where(place_ids >= end, end, start)
            return start

        at_rows = pl.ds(which * group, group)
        row_ids = lax.broadcasted_iota(jnp.int32, (group, head), 0)
        position = (row_ids - segment_start(row_ids)).astype(jnp.float32)
        angles = position * frequency_ref[...]
        cosine_ref[at_rows, :] = jnp.cos(angles)
        sine_ref[at_rows, :] = jnp.sin(angles) * across_sign
        row_ids = lax.broadcasted_iota(jnp.int32, (group, group), 0)
        key_ids = lax.broadcasted_iota(jnp.int32, (group, group), 1)
        allowed = (key_ids <= row_ids) & (key_ids >= segment_start(row_ids))
        mask_ref[which] = jnp.where(allowed, 0.0, masked_score)
    for ring in rings:
        ring.step(1)
    other = normed_ref.at[core, 1 - tp]
    remote(other, other, quad_send.at[1], quad_recv.at[1], place.across).wait_recv()
    passed = remote(other, other, quad_send.at[2], quad_recv.at[2], place.mate)
    passed.start()
    for n in range(2, levels + 1):
        for ring in rings:
            ring.step(n)
    for ring in rings:
        ring.finish()
        ring.drain()
    for offset in range(1, members):
        deal_copy(offset, True).wait_send()
    to_mate.wait_send()
    to_across.wait_send()
    passed.wait_send()
    for slot, piece in ((0, normed_ref.at[1 - core, tp]), (2, normed_ref.at[1 - core, 1 - tp])):
        remote(piece, piece, quad_send.at[slot], quad_recv.at[slot], place.mate).wait_recv()
    for i, dst in enumerate(halves(1 - place.tp)):
        pair_copies[i][1].wait()
        pair_copies[i][0].wait_send()
        remote(dst, dst, pair_send.at[i], pair_recv.at[i], place.across).wait_recv()


def open_layer(
    slices, gain_vec, lengths, sequences, frequency, w_query, w_key, w_value, w_out, w_gate, w_up
):
    members, pack, model_width = slices.shape
    chips = members // 2
    own_rows = w_query.shape[0]
    low = jnp.bfloat16
    vmem = pl.BlockSpec(memory_space=pltpu.VMEM)
    anywhere = pl.BlockSpec(memory_space=pl.ANY)
    dma = pltpu.SemaphoreType.DMA
    group, head = 2 * own_rows, frequency.shape[1]
    return pl.pallas_call(
        functools.partial(open_kernel, sequences),
        name="open_layer",
        out_shape=[
            jax.ShapeDtypeStruct(slices.shape, low),
            jax.ShapeDtypeStruct((2, 2, own_rows, model_width), low),
            jax.ShapeDtypeStruct((2 * group, head), jnp.float32),
            jax.ShapeDtypeStruct((2 * group, head), jnp.float32),
            jax.ShapeDtypeStruct((2, group, group), jnp.float32),
            jax.ShapeDtypeStruct((chips, 2 * own_rows, w_query.shape[1] // 2), low),
            jax.ShapeDtypeStruct((chips, 2 * own_rows, w_key.shape[1] // 2), low),
            jax.ShapeDtypeStruct((chips, 2 * own_rows, w_value.shape[1] // 2), low),
            jax.ShapeDtypeStruct((w_out.shape[0] // 2, members * w_out.shape[1]), low),
            jax.ShapeDtypeStruct((model_width, 2 * w_gate.shape[1]), low),
            jax.ShapeDtypeStruct((model_width, 2 * w_up.shape[1]), low),
        ],
        in_specs=[vmem] * 4 + [anywhere] * 6,
        out_specs=[vmem] * 5 + [anywhere] * 6,
        scratch_shapes=[
            pltpu.VMEM((2,) + lengths.shape, jnp.int32),
            dma((members - 1,)),
            dma((members - 1,)),
            dma((3,)),
            dma((3,)),
            dma((5,)),
            dma((5,)),
            dma((6,)),
            dma((2,)),
            dma((2,)),
            dma((2,)),
        ]
        + RowGather.semaphores(chips // 2, hands=False) * 4,
        compiler_params=pltpu.CompilerParams(
            collective_id=0, has_side_effects=True, vmem_limit_bytes=40 << 20
        ),
        cost_estimate=link_cost(110),
    )(slices, gain_vec, lengths, frequency, w_query, w_key, w_value, w_out, w_gate, w_up)


def close_kernel(
    slices_ref,
    gain_ref,
    query_ref,
    key_ref,
    value_ref,
    down_ref,
    dealt_ref,
    gain_sum_ref,
    query_own,
    key_own,
    value_own,
    down_arrived,
    gain_near,
    gain_pair,
    gain_parts,
    *rest,
):
    ring_bufs = [rest[3 * i : 3 * i + 3] for i in range(3)]
    side_bufs = [bufs[0] for bufs in ring_bufs]
    deal_send, deal_recv, gain_send, gain_recv, swap_send, swap_recv, keep_sem = rest[9:16]
    pair_send, pair_recv, total_send, total_recv = rest[16:20]
    place = Place()
    core = place.core
    members = 2 * place.chips
    own_rows = query_own.shape[0]
    greet(place.plane_targets() + [place.across])
    blocks = 2 * own_rows

    def by_rows(ref):
        return lambda chip: ref.at[pl.ds(pl.multiple_of(chip * blocks, blocks), blocks)]

    sums = [
        ChainSum(
            place, by_rows(ref), *ring_bufs[i], rest[20 + 10 * i : 30 + 10 * i]
        )
        for i, ref in enumerate((query_ref, key_ref, value_ref))
    ]

    def deal_copy(offset, sending):
        target, index = place.member(offset if sending else -offset)
        return remote(
            slices_ref.at[index],
            dealt_ref.at[place.fsdp if sending else index],
            deal_send.at[offset - 1],
            deal_recv.at[offset - 1],
            target,
        )

    def gain_copy(offset, sending):
        target, index = place.member(offset if sending else -offset)
        return remote(
            gain_pair.at[index],
            gain_parts.at[place.fsdp if sending else index],
            gain_send.at[offset],
            gain_recv.at[offset],
            target,
        )

    def total_copy(offset, sending):
        target, index = place.member(offset if sending else -offset)
        piece = gain_sum_ref.at[place.fsdp if sending else index]
        return remote(piece, piece, total_send.at[offset], total_recv.at[offset], target)

    units = down_arrived.shape[0]
    theirs = down_ref.at[pl.ds(pl.multiple_of((1 - place.tp) * units, units), units)]
    pair_copy = remote(theirs, down_arrived, pair_send, pair_recv, place.across)
    across = remote(gain_ref, gain_near, gain_send.at[0], gain_recv.at[0], place.across)
    across.start()
    across.wait_recv()
    gain_pair[...] = gain_ref[...] + gain_near[...]
    for offset in range(1, members):
        gain_copy(offset, True).start()
    pair_copy.start()
    for item in sums:
        item.send(item.target(0))
    for offset in range(1, members):
        gain_copy(offset, False).wait_recv()
    gain_parts[place.fsdp] = gain_pair[place.fsdp]
    total = gain_parts[0]
    for member in range(1, members):
        total += gain_parts[member]
    gain_sum_ref[place.fsdp] = total
    for offset in range(1, members):
        total_copy(offset, True).start()
    for offset in range(1, members):
        deal_copy(offset, True).start()
    own_slice = pltpu.make_async_copy(
        slices_ref.at[place.fsdp], dealt_ref.at[place.fsdp], keep_sem
    )
    own_slice.start()
    for turn in range(1, place.levels):
        for item in sums:
            item.send(item.target(turn))
    for item in sums:
        item.send_joined()
    for turn in range(place.levels):
        for item in sums:
            item.take_side(item.target(turn))
            item.take_chain(item.target(turn))

    def rows(who):
        return pl.ds(pl.multiple_of(who * own_rows, own_rows), own_rows)

    def columns(who, width):
        return pl.ds(pl.multiple_of(who * width, width), width)

    level = place.level
    spots = []
    for held, own in zip(side_bufs, (query_own, key_own, value_own)):
        width = held.shape[2]
        spots.append(
            (
                held.at[level, rows(core)],
                held.at[level, rows(1 - core)],
                own.at[:, columns(core, width)],
                own.at[:, columns(1 - core, width)],
            )
        )
    keeps, swaps = {}, {}
    for item in range(3):
        sums[item].close()
        mine, theirs, here, there = spots[item]
        keeps[item] = pltpu.make_async_copy(mine, here, swap_send.at[4 + item])
        keeps[item].start()
        swaps[item] = remote(
            theirs, here, swap_send.at[item], swap_recv.at[item], place.mate
        )
        swaps[item].start()
    for item in range(3):
        keeps[item].wait()
        swaps[item].wait_send()
        _, _, _, there = spots[item]
        remote(there, there, swap_send.at[item], swap_recv.at[item], place.mate).wait_recv()
        sums[item].drain()
    across.wait_send()
    pair_copy.wait()
    own_slice.wait()
    for offset in range(1, members):
        deal_copy(offset, False).wait_recv()
        deal_copy(offset, True).wait_send()
        gain_copy(offset, True).wait_send()
        total_copy(offset, True).wait_send()
        total_copy(offset, False).wait_recv()


def close_layer(
    slices, gain_part, query_grad, key_grad, value_grad, down_grad
):
    members = slices.shape[0]
    levels = members // 4
    own_rows = query_grad.shape[0] // members
    low = jnp.bfloat16
    vmem = pl.BlockSpec(memory_space=pltpu.VMEM)
    anywhere = pl.BlockSpec(memory_space=pl.ANY)
    dma = pltpu.SemaphoreType.DMA
    blocks = [
        (2 * own_rows, query_grad.shape[1]),
        (2 * own_rows, key_grad.shape[1]),
        (2 * own_rows, value_grad.shape[1]),
    ]
    buffers = [buffer for block in blocks for buffer in ChainSum.buffers(levels, block)]
    return pl.pallas_call(
        close_kernel,
        name="close_layer",
        out_shape=[
            jax.ShapeDtypeStruct(slices.shape, low),
            jax.ShapeDtypeStruct(gain_part.shape, jnp.float32),
            jax.ShapeDtypeStruct((own_rows, 2 * query_grad.shape[1]), low),
            jax.ShapeDtypeStruct((own_rows, 2 * key_grad.shape[1]), low),
            jax.ShapeDtypeStruct((own_rows, 2 * value_grad.shape[1]), low),
        ]
        + [jax.ShapeDtypeStruct((down_grad.shape[0] // 2, down_grad.shape[1]), low)],
        in_specs=[vmem] * 5 + [anywhere],
        out_specs=[vmem] * 5 + [anywhere],
        scratch_shapes=[
            pltpu.VMEM(gain_part.shape, jnp.float32),
            pltpu.VMEM(gain_part.shape, jnp.float32),
            pltpu.VMEM(gain_part.shape, jnp.float32),
        ]
        + buffers
        + [
            dma((members - 1,)),
            dma((members - 1,)),
            dma((members,)),
            dma((members,)),
            dma((8,)),
            dma((4,)),
            dma,
            dma,
            dma,
            dma((members,)),
            dma((members,)),
        ]
        + ChainSum.semaphores(levels) * 3,
        compiler_params=pltpu.CompilerParams(
            collective_id=1, has_side_effects=True, vmem_limit_bytes=56 << 20
        ),
        cost_estimate=link_cost(90),
    )(
        slices,
        gain_part,
        query_grad,
        key_grad,
        value_grad,
        down_grad,
    )


class QuadSum:
    def __init__(self, place, parts, near, pair, far, send, recv):
        self.place, self.parts = place, parts
        self.near, self.pair, self.far = near, pair, far
        self.send, self.recv = send, recv

    @staticmethod
    def scratch(rows, width):
        low, dma = jnp.bfloat16, pltpu.SemaphoreType.DMA
        return [
            pltpu.VMEM((2, rows, width), low),
            pltpu.VMEM((rows, width), low),
            pltpu.VMEM((rows, width), low),
            dma((3,)),
            dma((3,)),
        ]

    def to_mate(self, half):
        return remote(
            self.parts.at[1 - self.place.core, half],
            self.near.at[half],
            self.send.at[half],
            self.recv.at[half],
            self.place.mate,
        )

    def to_across(self):
        return remote(self.pair, self.far, self.send.at[2], self.recv.at[2], self.place.across)

    def start(self):
        self.to_mate(1 - self.place.tp).start()
        self.to_mate(self.place.tp).start()

    def relay(self):
        core, tp, wide = self.place.core, self.place.tp, jnp.float32
        self.to_mate(1 - tp).wait_recv()
        self.pair[...] = (
            self.parts[core, 1 - tp].astype(wide) + self.near[1 - tp].astype(wide)
        ).astype(jnp.bfloat16)
        self.to_across().start()

    def total(self):
        core, tp, wide = self.place.core, self.place.tp, jnp.float32
        self.to_mate(tp).wait_recv()
        total = self.parts[core, tp].astype(wide) + self.near[tp].astype(wide)
        self.to_across().wait_recv()
        return total + self.far[...].astype(wide)

    def drain(self):
        for half in range(2):
            self.to_mate(half).wait_send()
        self.to_across().wait_send()


def nt_dot(left, right):
    return lax.dot_general(
        left, right, (((1,), (1,)), ((), ())), preferred_element_type=jnp.float32
    )


def tn_dot(left, right):
    return lax.dot_general(
        left, right, (((0,), (0,)), ((), ())), preferred_element_type=jnp.float32
    )


def lanes_at(index, width):
    return pl.ds(pl.multiple_of(index * width, width), width)


def attend_kernel(
    experts,
    normed_ref,
    query_w,
    key_w,
    value_w,
    out_w,
    cosine_ref,
    sine_ref,
    mask_ref,
    dealt_ref,
    query_gain,
    key_gain,
    moe_gain,
    router_ref,
    chosen_ref,
    upstream_all,
    moe_ext,
    residual_ref,
    gates_ref,
    query_pre,
    query_low,
    key_pre,
    key_low,
    value_low,
    probs_ref,
    mixed_ref,
    upstream_own,
    parts,
    near,
    pair,
    far,
    quad_send,
    quad_recv,
    keep_sem,
    *ring_sems,
):
    place = Place()
    core = place.core
    wide, low = jnp.float32, jnp.bfloat16
    own_rows, width = residual_ref.shape
    group = 2 * own_rows
    head = query_gain.shape[1]
    heads = query_w.shape[1] // head
    members = dealt_ref.shape[0]
    half = dealt_ref.shape[1] // 2
    step_rows = 4

    def dealt_rows(start, second):
        block = dealt_ref[start : start + step_rows].astype(wide)
        block = block[:, half:] if second else block[:, :half]
        return block.reshape(step_rows * half, width)

    for start in range(0, members, step_rows):
        upstream_own[start * half : (start + step_rows) * half, :] = dealt_rows(
            start, True
        ).astype(low)
    keep = pltpu.make_async_copy(upstream_own, upstream_all.at[place.chip, core], keep_sem)
    keep.start()
    greet(place.ring_targets() + [place.mate, place.across])
    gather = RowGathers(place, lambda origin, whose: upstream_all.at[origin, whose], ring_sems)
    keep.wait()
    gather.start()

    def turned(values, gain_ref):
        factor = lax.rsqrt(jnp.mean(values * values, axis=-1, keepdims=True) + epsilon)
        scaled = values * factor * gain_ref[...]
        return (scaled * cosine_ref[...] + pltpu.roll(scaled, head // 2, 1) * sine_ref[...]).astype(
            low
        )

    x = normed_ref[...].reshape(2 * group, width)

    def project(index, carry):
        both = jnp.dot(
            normed_ref[...].reshape(2 * group, width),
            query_w[:, lanes_at(index, 2 * head)],
            preferred_element_type=wide,
        )
        query_pre[:, lanes_at(index, 2 * head)] = both
        for which in range(2):
            one = both[:, which * head : (which + 1) * head]
            query_low[:, lanes_at(2 * index + which, head)] = turned(one, query_gain)
        return carry

    lax.fori_loop(0, heads // 2, project, 0)
    key_values = jnp.dot(x, key_w[...], preferred_element_type=wide)
    key_pre[...] = key_values
    key_low[...] = turned(key_values, key_gain)
    value_low[...] = jnp.dot(x, value_w[...], preferred_element_type=wide).astype(low)
    gather.step(1)
    scale = head ** (-0.5)
    batch = 4

    def attend(index, carry):
        which = index // (heads // batch)
        first = (index % (heads // batch)) * batch
        rows = lanes_at(which, group)
        key = key_low[rows, :]
        value = value_low[rows, :]
        mask = mask_ref[which]
        for offset in range(batch):
            at = lanes_at(first + offset, head)
            scores = nt_dot(query_low[rows, at], key) * scale + mask
            peak = jnp.max(scores, axis=-1, keepdims=True)
            exponent = jnp.exp(scores - peak)
            probs = (exponent * (1.0 / jnp.sum(exponent, axis=-1, keepdims=True))).astype(low)
            probs_ref[which * heads + first + offset] = probs
            mixed_ref[rows, at] = jnp.dot(probs, value, preferred_element_type=wide).astype(low)
        return carry

    lax.fori_loop(0, heads // batch, attend, 0)
    gather.step(2)
    lax.fori_loop(heads // batch, 2 * heads // batch, attend, 0)

    def out_rows(whose):
        left = mixed_ref[lanes_at(whose, group), :]

        def out_lanes(index, carry):
            at = lanes_at(index, 512)
            product = jnp.dot(left, out_w[:, at], preferred_element_type=wide).astype(low)
            parts[whose, :, :, at] = product.reshape(2, own_rows, 512)
            return carry

        lax.fori_loop(0, width // 512, out_lanes, 0)

    sums = QuadSum(place, parts, near, pair, far, quad_send, quad_recv)
    out_rows(1 - core)
    sums.start()
    out_rows(core)
    sums.relay()
    gather.step(3)
    total = sums.total()
    tokens = jnp.concatenate(
        [dealt_rows(start, False) for start in range(0, members, step_rows)], axis=0
    )
    residual = tokens + total
    residual_ref[...] = residual
    factor = lax.rsqrt(jnp.mean(residual * residual, axis=-1, keepdims=True) + epsilon)
    moe_low = (residual * factor * moe_gain[...]).astype(low)
    moe_ext[:, :width] = moe_low
    logits = jnp.dot(moe_low, router_ref[...], preferred_element_type=wide)
    chosen = chosen_ref[...] > 0.0
    logits = jnp.where(chosen, logits, masked_score)
    exponent = jnp.exp(logits - jnp.max(logits, axis=-1, keepdims=True))
    exponent = jnp.where(chosen, exponent, 0.0)
    gates = exponent / jnp.sum(exponent, axis=-1, keepdims=True)
    gates_ref[...] = gates
    high = gates.astype(low).astype(wide)
    middle = (gates - high).astype(low).astype(wide)
    rest = gates - high - middle
    moe_ext[:, width:] = (
        high + pltpu.roll(middle, experts, 1) + pltpu.roll(rest, 2 * experts, 1)
    ).astype(low)
    for n in range(4, place.levels + 1):
        gather.step(n)
    gather.finish()
    gather.take_hands()
    gather.drain()
    sums.drain()


def attend_layer(
    experts, normed, query_w, key_w, value_w, out_w, tables, dealt, gain_vecs, router, chosen
):
    own_rows, width = normed.shape[2:]
    rows = 4 * own_rows
    members = dealt.shape[0]
    chips = members // 2
    heads_width, head = query_w.shape[1], key_w.shape[1]
    group = 2 * own_rows
    wide, low = jnp.float32, jnp.bfloat16
    vmem = pl.BlockSpec(memory_space=pltpu.VMEM)
    anywhere = pl.BlockSpec(memory_space=pl.ANY)
    shape = jax.ShapeDtypeStruct
    return pl.pallas_call(
        functools.partial(attend_kernel, experts),
        name="attend_layer",
        out_shape=[
            shape((chips, 2, own_rows, width), low),
            shape((own_rows, width + 128), low),
            shape((own_rows, width), wide),
            shape((own_rows, 128), wide),
            shape((rows, heads_width), wide),
            shape((rows, heads_width), low),
            shape((rows, head), wide),
            shape((rows, head), low),
            shape((rows, head), low),
            shape((2 * heads_width // head, group, group), low),
            shape((rows, heads_width), low),
        ],
        in_specs=[vmem] * 14,
        out_specs=[anywhere] + [vmem] * 10,
        scratch_shapes=[
            pltpu.VMEM((own_rows, width), low),
            pltpu.VMEM((2, 2, own_rows, width), low),
        ]
        + QuadSum.scratch(own_rows, width)
        + [pltpu.SemaphoreType.DMA]
        + RowGathers.semaphores(chips // 2),
        compiler_params=pltpu.CompilerParams(
            collective_id=2, has_side_effects=True, vmem_limit_bytes=56 << 20
        ),
        cost_estimate=link_cost(60),
    )(normed, query_w, key_w, value_w, out_w, *tables, dealt, *gain_vecs, router, chosen)


def expert_kernel(
    experts,
    x_own,
    upstream_ref,
    gate_ref,
    up_ref,
    down_ref,
    entry_own,
    out_part,
    gate_grad_ref,
    up_grad_ref,
    down_grad_ref,
    x_all,
    u_all,
    gate_w,
    up_w,
    down_w,
    hidden,
    gate_val_grad,
    up_val_grad,
    scores,
    sums,
    mate_out,
    mate_in,
    side_buf,
    chain_buf,
    hop_buf,
    staged,
    load_sem,
    store_sem,
    both_sem,
    mate_send,
    mate_recv,
    *ring_sems,
):
    place = Place()
    core, chip, level, side = place.core, place.chip, place.level, place.side
    levels, top = place.levels, place.levels - 1
    rows = x_own.shape[0]
    tile = 2 * rows
    width = upstream_ref.shape[1]
    units = down_ref.shape[0]
    wide = jnp.float32
    low = jnp.bfloat16
    loads = [
        pltpu.make_async_copy(x_own, x_all.at[chip, core], load_sem.at[0]),
        pltpu.make_async_copy(gate_ref, gate_w, load_sem.at[1]),
        pltpu.make_async_copy(up_ref, up_w, load_sem.at[2]),
        pltpu.make_async_copy(down_ref, down_w, load_sem.at[3]),
        pltpu.make_async_copy(upstream_ref, u_all, load_sem.at[4]),
    ]
    for load in loads:
        load.start()
    greet(place.ring_targets() + [place.mate])

    gather = RowGathers(place, lambda origin, whose: x_all.at[origin, whose], ring_sems[:20])
    loads[0].wait()

    gather.start()
    for load in loads[1:]:
        load.wait()

    lane = lax.broadcasted_iota(jnp.int32, (128, 128), 0)
    select = (
        (lane == place.fsdp)
        | (lane == place.fsdp + experts)
        | (lane == place.fsdp + 2 * experts)
    ).astype(low)
    cut = 256
    across_lanes = lax.broadcasted_iota(jnp.int32, (tile, 128), 1)

    def forward_tile(origin):
        x = x_all[origin].reshape(tile, x_all.shape[3])
        gate_lanes = jnp.dot(x[:, width:], select, preferred_element_type=wide)
        gate = jnp.concatenate([gate_lanes] * (cut // 128), axis=1)
        x = x[:, :width]
        start = pl.multiple_of(origin * tile, tile)
        u = u_all[pl.ds(start, tile), :]
        score = jnp.zeros((tile, 1), wide)
        for part in range(units // cut):
            lanes = slice(part * cut, (part + 1) * cut)
            gate_val = jnp.dot(x, gate_w[:, lanes], preferred_element_type=wide)
            up_val = jnp.dot(x, up_w[:, lanes], preferred_element_type=wide)
            back = lax.dot_general(
                u, down_w[lanes, :], (((1,), (1,)), ((), ())), preferred_element_type=wide
            )
            sigmoid = 1.0 / (1.0 + jnp.exp(-gate_val))
            swish = gate_val * sigmoid
            out = (swish * up_val).astype(low).astype(wide)
            score += jnp.sum(out * back, axis=1, keepdims=True)
            back = back * gate
            slope = sigmoid * (1.0 + gate_val * (1.0 - sigmoid))
            hidden[pl.ds(start, tile), lanes] = (out * gate).astype(low)
            gate_val_grad[pl.ds(start, tile), lanes] = (back * up_val * slope).astype(low)
            up_val_grad[pl.ds(start, tile), lanes] = (back * swish).astype(low)
        high = score.astype(low).astype(wide)
        packed = jnp.where(
            across_lanes == place.fsdp,
            high,
            jnp.where(across_lanes == place.fsdp + experts, score - high, 0.0),
        )
        scores[origin] = packed.astype(low)

    def gather_step(n, carry):
        gather.step(n)

        @pl.when(n == levels)
        def _():
            gather.finish()

        def candidate(which, carried):
            upward = which % 2
            facing = which // 2
            distance = n - 1 + facing
            at = level + distance * (2 * upward - 1)
            late = (n == levels) & (facing == 0) & (upward == place.upper) & place.at_end
            early = (n == 2) & (facing == 0) & place.at_end
            at = jnp.where(late, place.next, at)
            origin = at * 2 + side * facing + (1 - side) * (1 - facing)
            inside = (at >= 0) & (at <= top) & (distance >= 0) & ((distance > 0) | (upward == 0))

            @pl.when(inside & ~early)
            def _():
                gather.take_hand(origin, 1 - core)
                forward_tile(origin)

            return carried

        return lax.fori_loop(0, 4, candidate, carry)

    lax.fori_loop(0, levels + 1, gather_step, 0)

    plane_sum = ChainSum(place, lambda chip: sums.at[chip], side_buf, chain_buf, hop_buf, ring_sems[20:])

    def to_mate(goal_chip, slot):
        return remote(
            mate_out.at[slot],
            mate_in.at[goal_chip],
            mate_send.at[slot],
            mate_recv.at[goal_chip],
            place.mate,
        )

    def backward_tile(goal_chip, slot, reuse):
        start = pl.multiple_of(goal_chip * tile, tile)
        own_start = pl.multiple_of(goal_chip * tile + core * rows, rows)
        mate_start = pl.multiple_of(goal_chip * tile + (1 - core) * rows, rows)

        @pl.when(reuse)
        def _():
            to_mate(goal_chip, slot).wait_send()

        grads = gate_val_grad[pl.ds(start, tile), :]
        up_grads = up_val_grad[pl.ds(start, tile), :]
        piece = 512
        for first in range(0, width, piece):
            lanes = slice(first, first + piece)
            whole = lax.dot_general(
                grads, gate_w[lanes, :], (((1,), (1,)), ((), ())), preferred_element_type=wide
            ) + lax.dot_general(
                up_grads, up_w[lanes, :], (((1,), (1,)), ((), ())), preferred_element_type=wide
            )
            halves = whole.astype(low).reshape(2, rows, piece)
            sums[goal_chip, :, lanes] = jnp.where(core == 0, halves[0], halves[1])
            mate_out[slot, :, lanes] = jnp.where(core == 0, halves[1], halves[0])
        sums[goal_chip, :, width:] = scores[goal_chip, pl.ds(pl.multiple_of(core * rows, rows), rows)]
        mate_out[slot, :, width:] = scores[
            goal_chip, pl.ds(pl.multiple_of((1 - core) * rows, rows), rows)
        ]
        to_mate(goal_chip, slot).start()

    def joined(goal_chip, slot):
        to_mate(goal_chip, slot).wait_recv()
        sums[goal_chip] = (
            sums[goal_chip].astype(wide) + mate_in[goal_chip].astype(wide)
        ).astype(low)

    def backward_turn(turn, carry):
        goal = plane_sum.target(turn)
        backward_tile(goal * 2 + 1 - side, 0, turn > 0)
        backward_tile(goal * 2 + side, 1, turn > 0)
        joined(goal * 2 + 1 - side, 0)
        plane_sum.send(goal)
        joined(goal * 2 + side, 1)
        return carry

    lax.fori_loop(0, levels, backward_turn, 0)
    plane_sum.send_joined()

    def store(target, start, slot):
        return pltpu.make_async_copy(
            staged.at[slot], target.at[pl.ds(start, tile)], store_sem.at[slot]
        )

    def output_tile(origin, carry):
        start = pl.multiple_of(origin * tile, tile)
        slot = origin % 2

        @pl.when(origin > 1)
        def _():
            store(out_part, start, slot).wait()

        left = hidden[pl.ds(start, tile), :]
        for first in range(0, width, 512):
            lanes = slice(first, first + 512)
            staged[slot, :, lanes] = jnp.dot(
                left, down_w[:, lanes], preferred_element_type=wide
            ).astype(low)
        store(out_part, start, slot).start()
        return carry

    def down_grads(index, carry):
        start = pl.multiple_of(index * tile, tile)
        slot = index % 2
        store(down_grad_ref, start, slot).wait()
        left = hidden[:, pl.ds(start, tile)]
        for first in range(0, width, 512):
            lanes = slice(first, first + 512)
            staged[slot, :, lanes] = lax.dot_general(
                left, u_all[:, lanes], (((0,), (0,)), ((), ())), preferred_element_type=wide
            ).astype(low)
        store(down_grad_ref, start, slot).start()
        return carry

    def store_both(index):
        slot = index % 2
        start = pl.multiple_of(index * tile, tile)
        return [
            pltpu.make_async_copy(
                staged.at[slot, :, i * units : (i + 1) * units],
                target.at[pl.ds(start, tile)],
                both_sem.at[slot, i],
            )
            for i, target in enumerate((gate_grad_ref, up_grad_ref))
        ]

    def entry_weight_grads(index, carry):
        slot = index % 2

        @pl.when(index > 1)
        def _():
            for copy in store_both(index):
                copy.wait()

        left = x_all[:, :, :, pl.ds(pl.multiple_of(index * tile, tile), tile)]
        left = left.reshape(u_all.shape[0], tile)
        for i, right in enumerate((gate_val_grad, up_val_grad)):
            staged[slot, :, i * units : (i + 1) * units] = lax.dot_general(
                left, right[...], (((0,), (0,)), ((), ())), preferred_element_type=wide
            ).astype(low)
        for copy in store_both(index):
            copy.start()
        return carry

    plane_sum.take_side(plane_sum.target(0))
    lax.fori_loop(0, place.chips, output_tile, 0)
    plane_sum.take_chain(plane_sum.target(0))
    plane_sum.take_side(plane_sum.target(1))
    lax.fori_loop(0, units // tile, down_grads, 0)
    for slot in range(2):
        store(down_grad_ref, 0, slot).wait()
    plane_sum.take_chain(plane_sum.target(1))
    plane_sum.take_side(plane_sum.target(2))
    chunks = width // tile
    lax.fori_loop(0, chunks // 2, entry_weight_grads, 0)
    plane_sum.take_chain(plane_sum.target(2))
    plane_sum.take_side(plane_sum.target(3))
    lax.fori_loop(chunks // 2, chunks, entry_weight_grads, 0)
    plane_sum.take_chain(plane_sum.target(3))
    plane_sum.close()
    entry_own[...] = side_buf[level]
    for slot in range(2):
        for copy in store_both(slot):
            copy.wait()
        to_mate(0, slot).wait_send()
    plane_sum.drain()

    gather.drain()


def expert_layer(x_own, upstream_all, gate_all, up_all, down_all, experts):
    rows, span = x_own.shape
    total, width = upstream_all.shape
    units = down_all.shape[0]
    chips = total // (2 * rows)
    levels = chips // 2
    low = jnp.bfloat16
    vmem = pl.BlockSpec(memory_space=pltpu.VMEM)
    anywhere = pl.BlockSpec(memory_space=pl.ANY)
    dma = pltpu.SemaphoreType.DMA
    return pl.pallas_call(
        functools.partial(expert_kernel, experts),
        name="expert_layer",
        out_shape=[
            jax.ShapeDtypeStruct((rows, span), low),
            jax.ShapeDtypeStruct((total, width), low),
            jax.ShapeDtypeStruct((width, units), low),
            jax.ShapeDtypeStruct((width, units), low),
            jax.ShapeDtypeStruct((units, width), low),
        ],
        in_specs=[vmem] + [anywhere] * 4,
        out_specs=[vmem] + [anywhere] * 4,
        scratch_shapes=[
            pltpu.VMEM((chips, 2, rows, span), low),
            pltpu.VMEM((total, width), low),
            pltpu.VMEM((width, units), low),
            pltpu.VMEM((width, units), low),
            pltpu.VMEM((units, width), low),
            pltpu.VMEM((total, units), low),
            pltpu.VMEM((total, units), low),
            pltpu.VMEM((total, units), low),
            pltpu.VMEM((chips, 2 * rows, 128), low),
            pltpu.VMEM((chips, rows, span), low),
            pltpu.VMEM((2, rows, span), low),
            pltpu.VMEM((chips, rows, span), low),
            *ChainSum.buffers(levels, (rows, span)),
            pltpu.VMEM((2, 2 * rows, width), low),
            dma((5,)),
            dma((2,)),
            dma((2, 2)),
        ]
        + [dma((2,)), dma((chips,))]
        + RowGathers.semaphores(levels)
        + ChainSum.semaphores(levels),
        compiler_params=pltpu.CompilerParams(
            collective_id=5, has_side_effects=True, vmem_limit_bytes=63 << 20
        ),
        cost_estimate=link_cost(125),
    )(x_own, upstream_all, gate_all, up_all, down_all)


def attend_back_kernel(
    experts,
    entry_ref,
    residual_ref,
    gates_ref,
    dealt_ref,
    router_ref,
    attn_gain,
    moe_gain,
    query_gain,
    key_gain,
    mixed_ref,
    probs_ref,
    query_low,
    key_low,
    value_low,
    query_pre,
    key_pre,
    cosine_ref,
    sine_ref,
    normed_ref,
    query_w,
    key_w,
    value_w,
    out_w,
    out_part,
    gate_part,
    up_part,
    finished_ref,
    out_own,
    query_grad,
    key_grad,
    value_grad,
    router_grad,
    attn_gain_part,
    moe_gain_part,
    query_gain_part,
    key_gain_part,
    gate_arrived,
    up_arrived,
    residual_grad,
    low_all,
    mixed_grad,
    low_grads,
    key_total,
    value_total,
    out_grad,
    out_sums,
    out_mate,
    out_side,
    out_chain,
    out_hop,
    weight_side,
    weight_chain,
    weight_hop,
    staged,
    near,
    pair,
    far,
    quad_send,
    quad_recv,
    share_send,
    share_recv,
    swap_send,
    swap_recv,
    keep_sem,
    store_sem,
    pair_send,
    pair_recv,
    *ring_sems,
):
    place = Place()
    core, tp, level = place.core, place.tp, place.level
    wide, low = jnp.float32, jnp.bfloat16
    own_rows, width = residual_ref.shape
    group = 2 * own_rows
    rows = 2 * group
    head = query_gain.shape[1]
    heads = query_w.shape[1] // head
    members = dealt_ref.shape[0]
    half = dealt_ref.shape[1] // 2
    step_rows = 4
    scale = head ** (-0.5)

    def dealt_rows(second):
        blocks = []
        for start in range(0, members, step_rows):
            block = dealt_ref[start : start + step_rows].astype(wide)
            block = block[:, half:] if second else block[:, :half]
            blocks.append(block.reshape(step_rows * half, width))
        return jnp.concatenate(blocks, axis=0)

    greet(place.ring_targets() + [place.mate, place.across])
    to_mate = remote(
        out_part.at[:, 1 - core], out_mate, swap_send.at[0], swap_recv.at[0], place.mate
    )
    to_mate.start()
    keep = pltpu.make_async_copy(out_part.at[:, core], out_sums, keep_sem.at[0])
    keep.start()

    entry = entry_ref[:, :width].astype(wide)
    extra = entry_ref[:, width:].astype(wide)
    gates = gates_ref[...]
    gate_grad = extra + pltpu.roll(extra, 128 - experts, 1)
    inner = jnp.sum(gates * gate_grad, axis=-1, keepdims=True)
    logit_grad = (gates * (gate_grad - inner)).astype(low)
    residual = residual_ref[...]
    factor = lax.rsqrt(jnp.mean(residual * residual, axis=-1, keepdims=True) + epsilon)
    moe_low = (residual * factor * moe_gain[...]).astype(low)
    moe_grad = entry + nt_dot(logit_grad, router_ref[...])
    router_grad[...] = tn_dot(moe_low, logit_grad)
    scaled = moe_grad * moe_gain[...]
    inner = jnp.mean(scaled * residual, axis=-1, keepdims=True)
    moe_gain_part[...] = jnp.sum(moe_grad * residual * factor, axis=0, keepdims=True)
    residual_grad[...] = dealt_rows(True) + factor * (
        scaled - residual * (factor * factor) * inner
    )
    low_all[core, tp] = residual_grad[...].astype(low)
    mine = low_all.at[core, tp]
    share_mate = remote(mine, mine, share_send.at[0], share_recv.at[0], place.mate)
    share_across = remote(mine, mine, share_send.at[1], share_recv.at[1], place.across)
    share_across.start()
    share_mate.start()
    units = gate_arrived.shape[1]
    pair_copies = [
        remote(
            part.at[:, lanes_at(1 - tp, units)],
            arrived,
            pair_send.at[i],
            pair_recv.at[i],
            place.across,
        )
        for i, (part, arrived) in enumerate(((gate_part, gate_arrived), (up_part, up_arrived)))
    ]
    pair_copies[0].start()

    out_ring = ChainSum(
        place, lambda chip: out_sums.at[chip], out_side, out_chain, out_hop, ring_sems[:10]
    )
    lanes = out_own.shape[1]
    weight_ring = ChainSum(
        place,
        lambda chip: out_grad.at[:, lanes_at(chip, 2 * lanes)],
        weight_side,
        weight_chain,
        weight_hop,
        ring_sems[10:],
    )
    keep.wait()
    to_mate.wait_recv()

    def join(turn, carry):
        goal = out_ring.target(turn)
        for origin in (goal * 2 + 1 - place.side, goal * 2 + place.side):
            out_sums[origin] = (
                out_sums[origin].astype(wide) + out_mate[origin].astype(wide)
            ).astype(low)
        out_ring.send(goal)
        return carry

    lax.fori_loop(0, place.levels, join, 0)
    out_ring.send_joined()
    other = low_all.at[core, 1 - tp]
    remote(other, other, share_send.at[1], share_recv.at[1], place.across).wait_recv()
    passed = remote(other, other, share_send.at[2], share_recv.at[2], place.mate)
    passed.start()
    for slot, piece in ((0, low_all.at[1 - core, tp]), (2, low_all.at[1 - core, 1 - tp])):
        remote(piece, piece, share_send.at[slot], share_recv.at[slot], place.mate).wait_recv()

    def out_grad_rows(index, carry):
        at = lanes_at(index, 256)
        left = mixed_ref[:, at]
        for first in range(0, width, 512):
            out_grad[at, first : first + 512] = tn_dot(
                left, low_all[:, :, :, first : first + 512].reshape(rows, 512)
            ).astype(low)
        return carry

    lax.fori_loop(0, mixed_ref.shape[1] // 256, out_grad_rows, 0)
    for turn in range(place.levels):
        weight_ring.send(weight_ring.target(turn))

    def mixed_lanes(index, carry):
        at = lanes_at(index, 256)
        mixed_grad[:, at] = nt_dot(low_all[...].reshape(rows, width), out_w[at, :]).astype(low)
        return carry

    lax.fori_loop(0, mixed_ref.shape[1] // 256, mixed_lanes, 0)
    key_total[...] = jnp.zeros_like(key_total)
    value_total[...] = jnp.zeros_like(value_total)
    query_gain_part[...] = jnp.zeros_like(query_gain_part)

    def pre_back(grad, values, gain_ref, cosine, sine):
        grad = grad * cosine - pltpu.roll(grad, head // 2, 1) * sine
        factor = lax.rsqrt(jnp.mean(values * values, axis=-1, keepdims=True) + epsilon)
        scaled = grad * gain_ref[...]
        inner = jnp.mean(scaled * values, axis=-1, keepdims=True)
        back = factor * (scaled - values * (factor * factor) * inner)
        return back.astype(low), jnp.sum(grad * values * factor, axis=0, keepdims=True)

    batch = 4

    def attend_back(index, carry):
        which = index // (heads // batch)
        first = (index % (heads // batch)) * batch
        at_rows = lanes_at(which, group)
        key = key_low[at_rows, :]
        value = value_low[at_rows, :]
        cosine, sine = cosine_ref[at_rows, :], sine_ref[at_rows, :]
        key_sum = key_total[at_rows, :]
        value_sum = value_total[at_rows, :]
        gain_sum = query_gain_part[...]
        for offset in range(batch):
            at = lanes_at(first + offset, head)
            probs = probs_ref[which * heads + first + offset]
            grads = mixed_grad[at_rows, at]
            prob_grad = nt_dot(grads, value)
            probs_wide = probs.astype(wide)
            inner = jnp.sum(probs_wide * prob_grad, axis=-1, keepdims=True)
            score_grad = (probs_wide * (prob_grad - inner)).astype(low)
            query = jnp.dot(score_grad, key, preferred_element_type=wide) * scale
            key_sum += tn_dot(score_grad, query_low[at_rows, at])
            value_sum += tn_dot(probs, grads)
            back, terms = pre_back(query, query_pre[at_rows, at], query_gain, cosine, sine)
            low_grads[at_rows, at] = back
            gain_sum += terms
        key_total[at_rows, :] = key_sum
        value_total[at_rows, :] = value_sum
        query_gain_part[...] = gain_sum
        return carry

    count = 2 * heads // batch
    share = -(-count // place.levels)
    for turn in range(place.levels):
        out_ring.take_side(out_ring.target(turn))
        lax.fori_loop(min(turn * share, count), min((turn + 1) * share, count), attend_back, 0)
        out_ring.take_chain(out_ring.target(turn))

    weight_ring.send_joined()
    back, terms = pre_back(
        key_total[...] * scale, key_pre[...], key_gain, cosine_ref[...], sine_ref[...]
    )
    key_gain_part[...] = terms
    low_grads[:, heads * head : (heads + 1) * head] = back
    low_grads[:, (heads + 1) * head :] = value_total[...].astype(low)

    def normed_grad_rows(whose):
        at_rows = lanes_at(whose, group)

        def normed_grad_lanes(index, carry):
            at = lanes_at(index, 512)
            grads = low_grads[at_rows, :]
            product = (
                nt_dot(grads[:, : heads * head], query_w[at, :])
                + nt_dot(grads[:, heads * head : (heads + 1) * head], key_w[at, :])
                + nt_dot(grads[:, (heads + 1) * head :], value_w[at, :])
            )
            low_all[whose, :, :, at] = product.astype(low).reshape(2, own_rows, 512)
            return carry

        lax.fori_loop(0, width // 512, normed_grad_lanes, 0)

    share_mate.wait_send()
    share_across.wait_send()
    passed.wait_send()
    sums = QuadSum(place, low_all, near, pair, far, quad_send, quad_recv)
    normed_grad_rows(1 - core)
    sums.start()
    normed_grad_rows(core)
    sums.relay()
    pair_copies[1].start()

    def store(index):
        slot = index % 2
        return pltpu.make_async_copy(
            staged.at[slot], query_grad.at[lanes_at(index, 256)], store_sem.at[slot]
        )

    def weight_grad_rows(index, carry):
        at = lanes_at(index, 256)
        left = normed_ref[:, :, :, at].reshape(rows, 256)

        @pl.when(index > 1)
        def _():
            store(index).wait()

        for first in range(0, heads * head, 512):
            staged[index % 2, :, first : first + 512] = tn_dot(
                left, low_grads[:, first : first + 512]
            ).astype(low)
        store(index).start()
        both = tn_dot(left, low_grads[:, heads * head :]).astype(low)
        key_grad[at, :] = both[:, :head]
        value_grad[at, :] = both[:, head:]
        return carry

    lax.fori_loop(0, width // 256, weight_grad_rows, 0)
    for index in range(2):
        store(index).wait()
    out_ring.close()
    moe_own = out_side[level].astype(wide)
    normed_grad = sums.total()
    tokens = dealt_rows(False)
    factor = lax.rsqrt(jnp.mean(tokens * tokens, axis=-1, keepdims=True) + epsilon)
    scaled = normed_grad * attn_gain[...]
    inner = jnp.mean(scaled * tokens, axis=-1, keepdims=True)
    attn_gain_part[...] = jnp.sum(normed_grad * tokens * factor, axis=0, keepdims=True)
    token_grad = residual_grad[...] + factor * (scaled - tokens * (factor * factor) * inner)
    finished_ref[:, :half] = (residual_ref[...] + moe_own).reshape(members, half, width).astype(low)
    finished_ref[:, half:] = token_grad.reshape(members, half, width).astype(low)

    for turn in range(place.levels):
        weight_ring.take_side(weight_ring.target(turn))
        weight_ring.take_chain(weight_ring.target(turn))
    weight_ring.close()
    head_rows = out_grad.shape[0]
    here = out_own.at[lanes_at(core, head_rows)]
    there = out_own.at[lanes_at(1 - core, head_rows)]
    kept = pltpu.make_async_copy(
        weight_side.at[level, :, lanes_at(core, lanes)], here, keep_sem.at[1]
    )
    swap = remote(
        weight_side.at[level, :, lanes_at(1 - core, lanes)],
        here,
        swap_send.at[1],
        swap_recv.at[1],
        place.mate,
    )
    swap.start()
    kept.start()
    kept.wait()
    remote(there, there, swap_send.at[1], swap_recv.at[1], place.mate).wait_recv()
    swap.wait_send()
    for copy in pair_copies:
        copy.wait()
    to_mate.wait_send()
    sums.drain()
    out_ring.drain()
    weight_ring.drain()


def attend_back_layer(
    experts,
    entry,
    residual,
    gates,
    dealt,
    router,
    gain_vecs,
    mixed,
    probs,
    query_low,
    key_low,
    value_low,
    query_pre,
    key_pre,
    tables,
    normed,
    query_w,
    key_w,
    value_w,
    out_w,
    out_part,
    gate_part,
    up_part,
):
    own_rows, width = residual.shape
    members = dealt.shape[0]
    levels = members // 4
    rows = 4 * own_rows
    heads_width, head = query_w.shape[1], key_w.shape[1]
    lanes = width // members
    wide, low = jnp.float32, jnp.bfloat16
    vmem = pl.BlockSpec(memory_space=pltpu.VMEM)
    anywhere = pl.BlockSpec(memory_space=pl.ANY)
    shape = jax.ShapeDtypeStruct
    dma = pltpu.SemaphoreType.DMA
    return pl.pallas_call(
        functools.partial(attend_back_kernel, experts),
        name="attend_back_layer",
        out_shape=[
            shape(dealt.shape, low),
            shape((2 * heads_width, lanes), low),
            shape((width, heads_width), low),
            shape((width, head), low),
            shape((width, head), low),
            shape((width, 128), wide),
            shape((1, width), wide),
            shape((1, width), wide),
            shape((1, head), wide),
            shape((1, head), wide),
            shape((width, gate_part.shape[1] // 2), low),
            shape((width, up_part.shape[1] // 2), low),
        ],
        in_specs=[vmem] * 23 + [anywhere] * 3,
        out_specs=[vmem] * 2 + [anywhere] + [vmem] * 7 + [anywhere] * 2,
        scratch_shapes=[
            pltpu.VMEM((own_rows, width), wide),
            pltpu.VMEM((2, 2, own_rows, width), low),
            pltpu.VMEM((rows, heads_width), low),
            pltpu.VMEM((rows, heads_width + 2 * head), low),
            pltpu.VMEM((rows, head), wide),
            pltpu.VMEM((rows, head), wide),
            pltpu.VMEM((heads_width, width), low),
            pltpu.VMEM((members // 2, own_rows, width), low),
            pltpu.VMEM((members // 2, own_rows, width), low),
            *ChainSum.buffers(levels, (own_rows, width)),
            *ChainSum.buffers(levels, (heads_width, 2 * lanes)),
            pltpu.VMEM((2, 256, heads_width), low),
        ]
        + QuadSum.scratch(own_rows, width)
        + [dma((3,)), dma((3,)), dma((2,)), dma((2,)), dma((2,)), dma((2,)), dma((2,)), dma((2,))]
        + ChainSum.semaphores(levels) * 2,
        compiler_params=pltpu.CompilerParams(
            collective_id=3, has_side_effects=True, vmem_limit_bytes=65_400_000
        ),
        cost_estimate=link_cost(120),
    )(
        entry,
        residual,
        gates,
        dealt,
        router,
        *gain_vecs,
        mixed,
        probs,
        query_low,
        key_low,
        value_low,
        query_pre,
        key_pre,
        *tables,
        normed,
        query_w,
        key_w,
        value_w,
        out_w,
        out_part,
        gate_part,
        up_part,
    )


def fast_body(
    tokens,
    lengths,
    routes,
    deal_order,
    cotangent,
    attn_gain,
    query_gain,
    key_gain,
    moe_gain,
    w_query,
    key_projection_matrix,
    value_projection_matrix,
    w_out,
    w_router,
    w_gate,
    w_up,
    w_down,
):
    own_rows, model_width = tokens.shape
    head_dim = query_gain.shape[0]
    chip_count = lax.axis_size("chip")
    core_count = lax.axis_size("core")
    tp_count = lax.axis_size("tp")
    core_index = lax.axis_index("core")
    tp_index = lax.axis_index("tp")
    fsdp_count = chip_count * core_count
    fsdp_index = lax.axis_index("chip") * core_count + core_index
    slice_rows = own_rows // fsdp_count
    group_rows = tp_count * own_rows
    quad_rows = core_count * group_rows
    plane = ("chip", "core")
    quad = ("core", "tp")
    peer_ids = jnp.arange(fsdp_count, dtype=jnp.int32)
    wanted = (peer_ids - fsdp_index) % fsdp_count
    send_pick = jnp.sum(
        jnp.where(deal_order[None, :] == wanted[:, None], peer_ids[None, :], 0), axis=1
    )
    back_pick = (deal_order + fsdp_index) % fsdp_count

    def slices_of(values):
        return values.reshape(fsdp_count, slice_rows, model_width)

    def two_of(dealt):
        return (
            dealt[:, :slice_rows].reshape(own_rows, model_width),
            dealt[:, slice_rows:].reshape(own_rows, model_width),
        )

    outgoing = jnp.take(
        jnp.concatenate([slices_of(tokens), slices_of(cotangent)], axis=1), send_pick, axis=0
    )
    down_full = lax.all_gather(w_down[0], "tp", axis=0, tiled=True)
    frequency = rope_base ** (-(jnp.arange(head_dim // 2, dtype=jnp.float32) * (2.0 / head_dim)))
    frequency = jnp.concatenate([frequency, frequency])[None, :]
    padded_lengths = jnp.pad(lengths, ((0, 7), (0, 128 - lengths.shape[1])))
    (
        dealt,
        normed,
        cosine_wide,
        sine_wide,
        mask,
        query_part,
        key_part,
        value_part,
        out_part,
        gate_full,
        up_full,
    ) = open_layer(
        outgoing,
        attn_gain[None, :],
        padded_lengths,
        lengths.shape[1],
        frequency,
        w_query,
        key_projection_matrix,
        value_projection_matrix,
        w_out,
        w_gate[0],
        w_up[0],
    )
    query_part = query_part.reshape(model_width, -1)
    key_part = key_part.reshape(model_width, -1)
    value_part = value_part.reshape(model_width, -1)
    experts = w_router.shape[1]
    own_routes = lax.dynamic_slice_in_dim(routes, tp_index * own_rows, own_rows, 0)
    chosen = jnp.any(
        own_routes[:, :, None] == jnp.arange(128, dtype=jnp.int32)[None, None, :], axis=1
    ).astype(jnp.float32)
    router_wide = jnp.pad(w_router, ((0, 0), (0, 128 - experts)))
    (
        upstream_all,
        moe_ext,
        residual,
        gates,
        query_pre,
        query_low,
        key_before_norm,
        key_low,
        value_low,
        probs_low,
        mixed_low,
    ) = attend_layer(
        experts,
        normed,
        query_part,
        key_part,
        value_part,
        out_part,
        (cosine_wide, sine_wide, mask),
        dealt,
        (query_gain[None, :], key_gain[None, :], moe_gain[None, :]),
        router_wide,
        chosen,
    )
    upstream_all = upstream_all.reshape(fsdp_count * own_rows, model_width)
    entry_ext, moe_out, grad_w_gate, grad_w_up, grad_w_down = expert_layer(
        moe_ext, upstream_all, gate_full, up_full, down_full, experts
    )
    (
        finished,
        grad_w_out,
        grad_w_query,
        grad_w_key,
        grad_w_value,
        router_grad,
        attn_gain_part,
        moe_gain_part,
        query_gain_part,
        key_gain_part,
        gate_arrived,
        up_arrived,
    ) = attend_back_layer(
        experts,
        entry_ext,
        residual,
        gates,
        dealt,
        router_wide,
        (attn_gain[None, :], moe_gain[None, :], query_gain[None, :], key_gain[None, :]),
        mixed_low,
        probs_low,
        query_low,
        key_low,
        value_low,
        query_pre,
        key_before_norm,
        (cosine_wide, sine_wide),
        normed,
        query_part,
        key_part,
        value_part,
        out_part,
        moe_out.reshape(chip_count, core_count, own_rows, model_width),
        grad_w_gate,
        grad_w_up,
    )
    router_grad = router_grad[:, :experts]
    small = jnp.concatenate(
        [
            attn_gain_part[0],
            moe_gain_part[0],
            query_gain_part[0],
            key_gain_part[0],
            router_grad.reshape(-1),
        ]
    )
    small_rows = -(-small.shape[0] // (fsdp_count * 8 * 128)) * 8
    small = jnp.pad(small, (0, fsdp_count * small_rows * 128 - small.shape[0]))
    (
        returned,
        small,
        grad_w_query,
        grad_w_key,
        grad_w_value,
        down_arrived,
    ) = close_layer(
        finished,
        small.reshape(fsdp_count, small_rows, 128),
        grad_w_query,
        grad_w_key,
        grad_w_value,
        grad_w_down,
    )

    def pair_sum(parts, arrived, dim):
        size = arrived.shape[dim]
        mine = lax.dynamic_slice_in_dim(parts, tp_index * size, size, dim)
        return mine.astype(jnp.float32) + arrived.astype(jnp.float32)

    output, grad_input = two_of(jnp.take(returned, back_pick, axis=0))
    grad_input = grad_input.astype(jnp.float32)
    bounds = [model_width, 2 * model_width, 2 * model_width + head_dim]
    bounds += [bounds[2] + head_dim, bounds[2] + head_dim + router_grad.size]
    grad_attn_gain, grad_moe_gain, grad_query_gain, grad_key_gain, grad_w_router, _ = jnp.split(
        small.reshape(-1), bounds
    )
    grad_w_router = grad_w_router.reshape(model_width, experts)
    return (
        output,
        grad_input,
        grad_attn_gain,
        grad_query_gain,
        grad_key_gain,
        grad_moe_gain,
        grad_w_query.astype(jnp.float32),
        grad_w_key.astype(jnp.float32),
        grad_w_value.astype(jnp.float32),
        grad_w_out.astype(jnp.float32),
        grad_w_router,
        pair_sum(grad_w_gate, gate_arrived, 1)[None],
        pair_sum(grad_w_up, up_arrived, 1)[None],
        pair_sum(grad_w_down, down_arrived, 0)[None],
    )


def solution(mesh):
    fsdp_count, tp_count = mesh.shape["fsdp"], mesh.shape["tp"]
    chips = Mesh(mesh.devices.reshape(fsdp_count // 2, 2, tp_count), ("chip", "core", "tp"))
    dense = fsdp_count <= 16
    fsdp = ("chip", "core") if dense else "fsdp"
    every = ("chip", "core", "tp") if dense else ("fsdp", "tp")
    return jax.shard_map(
        fast_body if dense else body,
        mesh=chips if dense else mesh,
        in_specs=(
            P(every, None),
            P(fsdp, None),
            P(fsdp, None),
            P(),
            P(every, None),
            P(),
            P(),
            P(),
            P(),
            P(fsdp, "tp"),
            P(fsdp, "tp"),
            P(fsdp, "tp"),
            P("tp", fsdp),
            P(),
            P(fsdp, None, "tp"),
            P(fsdp, None, "tp"),
            P(fsdp, "tp", None),
        ),
        out_specs=(
            P(every, None),
            P(every, None),
            P(),
            P(),
            P(),
            P(),
            P(fsdp, "tp"),
            P(fsdp, "tp"),
            P(fsdp, "tp"),
            P("tp", fsdp),
            P(),
            P(fsdp, None, "tp"),
            P(fsdp, None, "tp"),
            P(fsdp, "tp", None),
        ),
        check_vma=False,
    )
```

```python
import functools

import jax
import jax.numpy as jnp
from jax import lax
from jax.experimental import pallas as pl
from jax.experimental.pallas import tpu as pltpu
from jax.sharding import Mesh
from jax.sharding import PartitionSpec as P

epsilon = 1e-06
rope_base = 1000000.0
masked_score = -1e30


def row_norm(values, gain_vec):
    factor = lax.rsqrt(jnp.mean(values * values, axis=-1, keepdims=True) + epsilon)
    return (values * factor * gain_vec, factor)


def norm_back(values, factor, gain_vec, upstream):
    scaled = upstream * gain_vec
    inner_term = jnp.mean(scaled * values, axis=-1, keepdims=True)
    return (factor * (scaled - values * (factor * factor) * inner_term), upstream * values * factor)


def seq_layout(seq_lengths, row_count):
    seq_ends = jnp.cumsum(seq_lengths)
    row_ids = jnp.arange(row_count, dtype=jnp.int32)
    segment = jnp.sum((row_ids[:, None] >= seq_ends[None, :]).astype(jnp.int32), axis=1)
    seq_starts = seq_ends - seq_lengths
    chosen = segment[:, None] == jnp.arange(seq_lengths.shape[0], dtype=jnp.int32)[None, :]
    position = row_ids - jnp.sum(jnp.where(chosen, seq_starts[None, :], 0), axis=1)
    return (segment, position)


def rotary(position, head_width):
    half_width = head_width // 2
    inverse_freq = rope_base ** (-(jnp.arange(half_width, dtype=jnp.float32) * (2.0 / head_width)))
    angles = position.astype(jnp.float32)[:, None] * inverse_freq[None, :]
    return (jnp.cos(angles)[:, None, :], jnp.sin(angles)[:, None, :])


def rotate(values, cosine_table, sine_table):
    half_width = values.shape[-1] // 2
    front_half = values[..., :half_width]
    back_half = values[..., half_width:]
    return jnp.concatenate(
        [
            front_half * cosine_table - back_half * sine_table,
            back_half * cosine_table + front_half * sine_table,
        ],
        axis=-1,
    )


def rotate_back(upstream, cosine_table, sine_table):
    half_width = upstream.shape[-1] // 2
    front_half = upstream[..., :half_width]
    back_half = upstream[..., half_width:]
    return jnp.concatenate(
        [
            front_half * cosine_table + back_half * sine_table,
            back_half * cosine_table - front_half * sine_table,
        ],
        axis=-1,
    )


def slot_table(route_rows, expert_count, capacity):
    row_count = route_rows.shape[0] * route_rows.shape[1]
    flat_routes = route_rows.reshape(row_count)
    expert_hits = (
        flat_routes[:, None] == jnp.arange(expert_count, dtype=jnp.int32)[None, :]
    ).astype(jnp.int32)
    earlier = jnp.cumsum(expert_hits, axis=0) - expert_hits
    slot_index = jnp.sum(earlier * expert_hits, axis=1)
    slot_place = flat_routes * capacity + slot_index
    slot_rows = jnp.full((expert_count * capacity,), row_count, jnp.int32)
    slot_rows = slot_rows.at[slot_place].set(jnp.arange(row_count, dtype=jnp.int32))
    return (slot_place, slot_rows.reshape(expert_count, capacity))


def contract_rows(left, right):
    return lax.dot_general(
        left, right, (((0,), (0,)), ((), ())), preferred_element_type=jnp.float32
    )


def contract_last(left, right):
    return lax.dot_general(
        left, right, (((1,), (1,)), ((), ())), preferred_element_type=jnp.float32
    )


def body(
    tokens,
    lengths,
    routes,
    deal_order,
    cotangent,
    attn_gain,
    query_gain,
    key_gain,
    moe_gain,
    w_query,
    key_projection_matrix,
    value_projection_matrix,
    w_out,
    w_router,
    w_gate,
    w_up,
    w_down,
):
    half_rows = tokens.shape[0]
    model_width = tokens.shape[1]
    head_dim = query_gain.shape[0]
    score_scale = head_dim ** (-0.5)
    fsdp_count = lax.axis_size("fsdp")
    tp_count = lax.axis_size("tp")
    fsdp_index = lax.axis_index("fsdp")
    tp_index = lax.axis_index("tp")
    slice_rows = half_rows // fsdp_count
    group_rows = tp_count * half_rows
    own_start = tp_index * half_rows
    peer_ids = jnp.arange(fsdp_count, dtype=jnp.int32)
    wanted = (peer_ids - fsdp_index) % fsdp_count
    send_pick = jnp.sum(
        jnp.where(deal_order[None, :] == wanted[:, None], peer_ids[None, :], 0), axis=1
    )
    back_pick = (deal_order + fsdp_index) % fsdp_count

    def deal_copies(values):
        slices = jnp.take(values.reshape(fsdp_count, slice_rows, model_width), send_pick, axis=0)
        return jnp.broadcast_to(slices[None], (tp_count, fsdp_count, slice_rows, model_width))

    tokens_all, cotangent_all = (
        lax.all_to_all(
            lax.all_to_all(deal_copies(tokens), "tp", split_axis=0, concat_axis=0, tiled=True),
            "fsdp",
            split_axis=1,
            concat_axis=1,
            tiled=True,
        ),
        lax.all_to_all(
            lax.all_to_all(deal_copies(cotangent), "tp", split_axis=0, concat_axis=0, tiled=True),
            "fsdp",
            split_axis=1,
            concat_axis=1,
            tiled=True,
        ),
    )
    tokens_in = tokens_all.reshape(group_rows, model_width).astype(jnp.float32)
    upstream = cotangent_all.reshape(group_rows, model_width).astype(jnp.float32)
    attn_in, attn_factor = row_norm(tokens_in, attn_gain)
    normed_all = attn_in.astype(jnp.bfloat16)
    query_full, key_full, value_full, out_full = (
        lax.all_gather(w_query, "fsdp", axis=0, tiled=True),
        lax.all_gather(key_projection_matrix, "fsdp", axis=0, tiled=True),
        lax.all_gather(value_projection_matrix, "fsdp", axis=0, tiled=True),
        lax.all_gather(w_out, "fsdp", axis=1, tiled=True),
    )
    query_heads = query_full.shape[1] // head_dim
    kv_heads = key_full.shape[1] // head_dim
    group_size = query_heads // kv_heads
    segment, position = seq_layout(lengths[0], group_rows)
    cosine_table, sine_table = rotary(position, head_dim)
    row_ids = jnp.arange(group_rows)
    allowed = (segment[:, None] == segment[None, :]) & (row_ids[None, :] <= row_ids[:, None])
    query_pre = jnp.dot(normed_all, query_full, preferred_element_type=jnp.float32).reshape(
        group_rows, query_heads, head_dim
    )
    query_normed, query_factor = row_norm(query_pre, query_gain)
    query_low = (
        rotate(query_normed, cosine_table, sine_table)
        .astype(jnp.bfloat16)
        .reshape(group_rows, kv_heads, group_size, head_dim)
    )
    key_before_norm = jnp.dot(normed_all, key_full, preferred_element_type=jnp.float32).reshape(
        group_rows, kv_heads, head_dim
    )
    key_normed, key_factor = row_norm(key_before_norm, key_gain)
    key_low = rotate(key_normed, cosine_table, sine_table).astype(jnp.bfloat16)
    value_low = (
        jnp.dot(normed_all, value_full, preferred_element_type=jnp.float32)
        .astype(jnp.bfloat16)
        .reshape(group_rows, kv_heads, head_dim)
    )
    scores = (
        jnp.einsum("qkgd,tkd->kgqt", query_low, key_low, preferred_element_type=jnp.float32)
        * score_scale
    )
    scores = jnp.where(allowed, scores, masked_score)
    row_peak = jnp.max(scores, axis=-1, keepdims=True)
    exponent = jnp.exp(scores - row_peak)
    totals = jnp.sum(exponent, axis=-1, keepdims=True)
    log_total = row_peak + jnp.log(totals)
    attn_probs = (exponent / totals).astype(jnp.bfloat16)
    attn_mixed = jnp.einsum(
        "kgqt,tkd->qkgd", attn_probs, value_low, preferred_element_type=jnp.float32
    )
    mixed_low = attn_mixed.reshape(group_rows, query_heads * head_dim).astype(jnp.bfloat16)
    attn_part = jnp.dot(mixed_low, out_full, preferred_element_type=jnp.float32)
    residual = tokens_in + lax.psum(attn_part, "tp")
    moe_in, moe_factor = row_norm(residual, moe_gain)
    moe_low = moe_in.astype(jnp.bfloat16)
    logits = jnp.dot(moe_low, w_router, preferred_element_type=jnp.float32)
    experts = w_router.shape[1]
    top_count = routes.shape[1]
    chosen = routes[:, :, None] == jnp.arange(experts, dtype=jnp.int32)[None, None, :]
    selected = jnp.sum(jnp.where(chosen, logits[:, None, :], 0.0), axis=-1)
    gate_peak = jnp.max(selected, axis=-1, keepdims=True)
    gate_exp = jnp.exp(selected - gate_peak)
    gate_probs = gate_exp / jnp.sum(gate_exp, axis=-1, keepdims=True)
    capacity = max(2, 3 * group_rows * top_count // (2 * experts))
    slot_place, slot_rows = slot_table(routes, experts, capacity)
    part_cap = capacity // tp_count
    slot_start = tp_index * part_cap
    gate_full, up_full, down_full = (
        lax.all_gather(w_gate, "tp", axis=2, tiled=True),
        lax.all_gather(w_up, "tp", axis=2, tiled=True),
        lax.all_gather(w_down, "tp", axis=1, tiled=True),
    )
    sent_rows = lax.dynamic_slice_in_dim(slot_rows, slot_start, part_cap, 1)
    slot_expert = slot_place // capacity
    slot_offset = slot_place % capacity - slot_start
    in_half = (slot_offset >= 0) & (slot_offset < part_cap)
    local_place = jnp.where(in_half, slot_expert * part_cap + slot_offset, experts * part_cap)
    padded = jnp.concatenate([moe_low, jnp.zeros((1, model_width), jnp.bfloat16)], axis=0)
    arrived = lax.all_to_all(
        padded[sent_rows // top_count], "fsdp", split_axis=0, concat_axis=0, tiled=True
    )
    local_experts = w_gate.shape[0]
    sources = experts // local_experts
    slot_count = sources * part_cap
    ff_part = w_gate.shape[2]

    def to_experts(values):
        return jnp.transpose(
            values.reshape(sources, local_experts, part_cap, model_width), (1, 0, 2, 3)
        ).reshape(local_experts, slot_count, model_width)

    def to_sources(values):
        width = values.shape[-1]
        return jnp.transpose(
            values.reshape(local_experts, sources, part_cap, width), (1, 0, 2, 3)
        ).reshape(experts, part_cap, width)

    def pick_rows(values):
        flat = values.reshape(experts * part_cap, tp_count * model_width)
        flat = jnp.concatenate([flat, jnp.zeros((1, tp_count * model_width), jnp.bfloat16)], axis=0)
        gathered = flat[local_place].reshape(group_rows, top_count, tp_count, model_width)
        return jnp.sum(gathered.astype(jnp.float32), axis=2)

    expert_rows = to_experts(arrived)
    gate_val = jnp.einsum(
        "esd,edf->esf", expert_rows, gate_full, preferred_element_type=jnp.float32
    )
    up_val = jnp.einsum("esd,edf->esf", expert_rows, up_full, preferred_element_type=jnp.float32)
    sigmoid_val = jax.nn.sigmoid(gate_val)
    swish_val = gate_val * sigmoid_val
    hidden_low = (swish_val * up_val).astype(jnp.bfloat16)
    hidden_blocks = hidden_low.reshape(local_experts, slot_count, tp_count, ff_part)
    down_blocks = down_full.reshape(local_experts, tp_count, ff_part, model_width)
    expert_out = (
        jnp.einsum(
            "esbf,ebfd->esbd", hidden_blocks, down_blocks, preferred_element_type=jnp.float32
        )
        .astype(jnp.bfloat16)
        .reshape(local_experts, slot_count, tp_count * model_width)
    )
    returned = lax.all_to_all(
        to_sources(expert_out), "fsdp", split_axis=0, concat_axis=0, tiled=True
    )
    picked = pick_rows(returned)
    moe_part = jnp.sum(gate_probs[:, :, None] * picked, axis=1)
    gate_grad_part = jnp.sum(upstream[:, None, :] * picked, axis=-1)
    weighted = (
        (gate_probs[:, :, None] * upstream[:, None, :])
        .astype(jnp.bfloat16)
        .reshape(group_rows * top_count, model_width)
    )
    weighted = jnp.concatenate([weighted, jnp.zeros((1, model_width), jnp.bfloat16)], axis=0)
    grad_arrived = lax.all_to_all(
        weighted[sent_rows], "fsdp", split_axis=0, concat_axis=0, tiled=True
    )
    grad_slots = to_experts(grad_arrived)
    hidden_grad = jnp.einsum(
        "esd,ebfd->esbf", grad_slots, down_blocks, preferred_element_type=jnp.float32
    ).reshape(local_experts, slot_count, tp_count * ff_part)
    swish_slope = sigmoid_val * (1.0 + gate_val * (1.0 - sigmoid_val))
    gate_val_grad = (hidden_grad * up_val * swish_slope).astype(jnp.bfloat16)
    up_val_grad = (hidden_grad * swish_val).astype(jnp.bfloat16)
    grad_w_down = jnp.einsum(
        "esbf,esd->ebfd", hidden_blocks, grad_slots, preferred_element_type=jnp.float32
    ).reshape(local_experts, tp_count * ff_part, model_width)
    grad_w_gate = jnp.einsum(
        "esd,esf->edf", expert_rows, gate_val_grad, preferred_element_type=jnp.float32
    )
    grad_w_up = jnp.einsum(
        "esd,esf->edf", expert_rows, up_val_grad, preferred_element_type=jnp.float32
    )
    gate_blocks = gate_full.reshape(local_experts, model_width, tp_count, ff_part)
    up_blocks = up_full.reshape(local_experts, model_width, tp_count, ff_part)
    entry_grad = (
        (
            jnp.einsum(
                "esbf,edbf->esbd",
                gate_val_grad.reshape(local_experts, slot_count, tp_count, ff_part),
                gate_blocks,
                preferred_element_type=jnp.float32,
            )
            + jnp.einsum(
                "esbf,edbf->esbd",
                up_val_grad.reshape(local_experts, slot_count, tp_count, ff_part),
                up_blocks,
                preferred_element_type=jnp.float32,
            )
        )
        .astype(jnp.bfloat16)
        .reshape(local_experts, slot_count, tp_count * model_width)
    )
    sent_back = lax.all_to_all(
        to_sources(entry_grad), "fsdp", split_axis=0, concat_axis=0, tiled=True
    )
    expert_grad = jnp.sum(pick_rows(sent_back), axis=1)
    grad_w_gate, grad_w_up, grad_w_down = (
        lax.psum_scatter(
            grad_w_gate.astype(jnp.bfloat16), "tp", scatter_dimension=2, tiled=True
        ).astype(jnp.float32),
        lax.psum_scatter(
            grad_w_up.astype(jnp.bfloat16), "tp", scatter_dimension=2, tiled=True
        ).astype(jnp.float32),
        lax.psum_scatter(
            grad_w_down.astype(jnp.bfloat16), "tp", scatter_dimension=1, tiled=True
        ).astype(jnp.float32),
    )
    moe_grad, gate_grad = (
        lax.psum(expert_grad.astype(jnp.bfloat16), "tp").astype(jnp.float32),
        lax.psum(gate_grad_part.astype(jnp.bfloat16), "tp").astype(jnp.float32),
    )
    gate_inner = jnp.sum(gate_probs * gate_grad, axis=-1, keepdims=True)
    selected_grad = gate_probs * (gate_grad - gate_inner)
    logit_grad = jnp.sum(jnp.where(chosen, selected_grad[:, :, None], 0.0), axis=1).astype(
        jnp.bfloat16
    )
    moe_grad = moe_grad + contract_last(logit_grad, w_router)
    router_grad = contract_rows(
        lax.dynamic_slice_in_dim(moe_low, own_start, half_rows, 0),
        lax.dynamic_slice_in_dim(logit_grad, own_start, half_rows, 0),
    )
    residual_from_norm, moe_gain_terms = norm_back(residual, moe_factor, moe_gain, moe_grad)
    residual_grad = upstream + residual_from_norm
    moe_gain_grad = jnp.sum(
        lax.dynamic_slice_in_dim(moe_gain_terms, own_start, half_rows, 0), axis=0
    )
    residual_low = residual_grad.astype(jnp.bfloat16)
    mixed_grad = (
        contract_last(residual_low, out_full)
        .astype(jnp.bfloat16)
        .reshape(group_rows, kv_heads, group_size, head_dim)
    )
    grad_w_out = contract_rows(mixed_low, residual_low)
    scores = (
        jnp.einsum("qkgd,tkd->kgqt", query_low, key_low, preferred_element_type=jnp.float32)
        * score_scale
    )
    scores = jnp.where(allowed, scores, masked_score)
    probs_full = jnp.exp(scores - log_total)
    prob_grad = jnp.einsum(
        "qkgd,tkd->kgqt", mixed_grad, value_low, preferred_element_type=jnp.float32
    )
    prob_inner = jnp.sum(probs_full * prob_grad, axis=-1, keepdims=True)
    score_grad = (probs_full * (prob_grad - prob_inner)).astype(jnp.bfloat16)
    query_grad = (
        jnp.einsum(
            "kgqt,tkd->qkgd", score_grad, key_low, preferred_element_type=jnp.float32
        ).reshape(group_rows, query_heads, head_dim)
        * score_scale
    )
    key_grad = (
        jnp.einsum("kgqt,qkgd->tkd", score_grad, query_low, preferred_element_type=jnp.float32)
        * score_scale
    )
    value_grad = (
        jnp.einsum(
            "kgqt,qkgd->tkd",
            probs_full.astype(jnp.bfloat16),
            mixed_grad,
            preferred_element_type=jnp.float32,
        )
        .astype(jnp.bfloat16)
        .reshape(group_rows, kv_heads * head_dim)
    )
    query_pre_grad, query_gain_terms = norm_back(
        query_pre, query_factor, query_gain, rotate_back(query_grad, cosine_table, sine_table)
    )
    key_pre_grad, key_gain_terms = norm_back(
        key_before_norm, key_factor, key_gain, rotate_back(key_grad, cosine_table, sine_table)
    )
    query_pre_low = query_pre_grad.astype(jnp.bfloat16).reshape(group_rows, query_heads * head_dim)
    key_pre_low = key_pre_grad.astype(jnp.bfloat16).reshape(group_rows, kv_heads * head_dim)
    grad_w_query = contract_rows(normed_all, query_pre_low)
    grad_w_key = contract_rows(normed_all, key_pre_low)
    grad_w_value = contract_rows(normed_all, value_grad)
    normed_grad = (
        contract_last(query_pre_low, query_full)
        + contract_last(key_pre_low, key_full)
        + contract_last(value_grad, value_full)
    )
    normed_grad_own, moe_own = (
        lax.psum_scatter(
            normed_grad.astype(jnp.bfloat16), "tp", scatter_dimension=0, tiled=True
        ).astype(jnp.float32),
        lax.psum_scatter(
            moe_part.astype(jnp.bfloat16), "tp", scatter_dimension=0, tiled=True
        ).astype(jnp.float32),
    )
    tokens_own = lax.dynamic_slice_in_dim(tokens_in, own_start, half_rows, 0)
    factor_own = lax.dynamic_slice_in_dim(attn_factor, own_start, half_rows, 0)
    tokens_from_norm, attn_gain_terms = norm_back(
        tokens_own, factor_own, attn_gain, normed_grad_own
    )
    grad_group = lax.dynamic_slice_in_dim(residual_grad, own_start, half_rows, 0) + tokens_from_norm
    residual_own = lax.dynamic_slice_in_dim(residual, own_start, half_rows, 0)
    output_group = (residual_own + moe_own).astype(jnp.bfloat16)
    back_output, back_grad = (
        lax.all_to_all(
            output_group.astype(jnp.float32)
            .reshape(fsdp_count, slice_rows, model_width)
            .astype(jnp.bfloat16),
            "fsdp",
            split_axis=0,
            concat_axis=0,
            tiled=True,
        ).astype(jnp.float32),
        lax.all_to_all(
            grad_group.reshape(fsdp_count, slice_rows, model_width).astype(jnp.bfloat16),
            "fsdp",
            split_axis=0,
            concat_axis=0,
            tiled=True,
        ).astype(jnp.float32),
    )
    output = (
        jnp.take(back_output, back_pick, axis=0)
        .reshape(half_rows, model_width)
        .astype(jnp.bfloat16)
    )
    grad_input = jnp.take(back_grad, back_pick, axis=0).reshape(half_rows, model_width)
    grad_w_query, grad_w_key, grad_w_value, grad_w_out = (
        lax.psum_scatter(grad_w_query, "fsdp", scatter_dimension=0, tiled=True),
        lax.psum_scatter(grad_w_key, "fsdp", scatter_dimension=0, tiled=True),
        lax.psum_scatter(grad_w_value, "fsdp", scatter_dimension=0, tiled=True),
        lax.psum_scatter(grad_w_out, "fsdp", scatter_dimension=1, tiled=True),
    )
    grad_attn_gain, grad_query_gain, grad_key_gain, grad_moe_gain, grad_w_router = lax.psum(
        (
            jnp.sum(attn_gain_terms, axis=0),
            jnp.sum(query_gain_terms, axis=(0, 1)),
            jnp.sum(key_gain_terms, axis=(0, 1)),
            moe_gain_grad,
            router_grad,
        ),
        ("fsdp", "tp"),
    )
    return (
        output,
        grad_input,
        grad_attn_gain,
        grad_query_gain,
        grad_key_gain,
        grad_moe_gain,
        grad_w_query,
        grad_w_key,
        grad_w_value,
        grad_w_out,
        grad_w_router,
        grad_w_gate,
        grad_w_up,
        grad_w_down,
    )


def remote(src, dst, send_sem, recv_sem, target):
    return pltpu.make_async_remote_copy(
        src_ref=src,
        dst_ref=dst,
        send_sem=send_sem,
        recv_sem=recv_sem,
        device_id=target,
        device_id_type=pl.DeviceIdType.MESH,
    )


def greet(targets):
    barrier = pltpu.get_barrier_semaphore()
    for target in targets:
        pl.semaphore_signal(
            barrier, inc=1, device_id=target, device_id_type=pl.DeviceIdType.MESH
        )
    pl.semaphore_wait(barrier, len(targets))


def link_cost(microseconds):
    return pl.CostEstimate(flops=0, bytes_accessed=microseconds * 3_000_000, transcendentals=0)


class Place:
    def __init__(self):
        self.chips = lax.axis_size("chip")
        self.levels = self.chips // 2
        self.chip = lax.axis_index("chip")
        self.core = lax.axis_index("core")
        self.tp = lax.axis_index("tp")
        self.level = self.chip // 2
        self.side = self.chip % 2
        self.fsdp = self.chip * 2 + self.core
        self.mate = {"core": 1 - self.core}
        self.across = {"tp": 1 - self.tp}
        self.beside = {"chip": self.level * 2 + 1 - self.side}
        self.above = {"chip": lax.rem(self.chip + 2, self.chips)}
        self.below = {"chip": lax.rem(self.chip + self.chips - 2, self.chips)}
        top = self.levels - 1
        self.upper = self.level // (self.levels // 2)
        self.end = top * self.upper
        self.next = self.end + 1 - 2 * self.upper
        self.at_end = self.level == self.end
        self.at_next = self.level == self.next
        outward = self.level * 2 + self.side + 4 * self.upper - 2
        inward = self.level * 2 + self.side + 2 - 4 * self.upper
        self.outward = {"chip": lax.rem(outward + self.chips, self.chips)}
        self.inward = {"chip": lax.rem(inward + self.chips, self.chips)}

    def member(self, offset):
        count = 2 * self.chips
        index = lax.rem(self.fsdp + offset + count, count)
        return {"chip": index // 2, "core": lax.rem(index, 2)}, index

    def plane_targets(self):
        return [self.member(offset)[0] for offset in range(1, 2 * self.chips)]

    def ring_targets(self):
        return [self.above, self.below, self.beside]


def lower_half(ref):
    return ref.at[pl.ds(0, ref.shape[0] // 2)]


def upper_half(ref):
    return ref.at[pl.ds(ref.shape[0] // 2, ref.shape[0] // 2)]


class RowGather:
    def __init__(self, place, block, sems, hands=True):
        self.place, self.block, self.hands = place, block, hands
        (
            self.up_send,
            self.up_recv,
            self.down_send,
            self.down_recv,
            self.side_send,
            self.side_recv,
            self.hop_send,
            self.hop_recv,
        ) = sems[:8]
        if hands:
            self.hand_send, self.hand_recv = sems[8:10]

    @staticmethod
    def semaphores(levels, hands=True):
        dma = pltpu.SemaphoreType.DMA
        return [dma((levels,))] * 6 + [dma, dma] + ([dma((2 * levels,))] * 2 if hands else [])

    def climb(self, origin):
        piece, at = self.block(origin, self.place.core), origin // 2
        return remote(piece, piece, self.up_send.at[at], self.up_recv.at[at], self.place.above)

    def sink(self, origin):
        piece, at = self.block(origin, self.place.core), origin // 2
        return remote(piece, piece, self.down_send.at[at], self.down_recv.at[at], self.place.below)

    def cross(self, origin, half=False):
        piece, at = self.block(origin, self.place.core), origin // 2
        if half:
            piece = upper_half(piece)
        return remote(piece, piece, self.side_send.at[at], self.side_recv.at[at], self.place.beside)

    def hop(self, level, inward):
        piece = self.block(level * 2 + 1 - self.place.side, self.place.core)
        if not inward:
            piece = lower_half(piece)
        target = self.place.inward if inward else self.place.outward
        return remote(piece, piece, self.hop_send, self.hop_recv, target)

    def hand(self, origin, whose):
        piece = self.block(origin, whose)
        return remote(
            piece, piece, self.hand_send.at[origin], self.hand_recv.at[origin], self.place.mate
        )

    def pass_on(self, origin):
        place = self.place
        at = origin // 2
        skipped = place.at_next & (at == place.end)
        halved = place.at_end & (at == place.next)

        @pl.when(halved)
        def _():
            self.cross(origin, True).start()

        @pl.when(~skipped & ~halved)
        def _():
            self.cross(origin).start()

        self.give(origin)

    def give(self, origin):
        if self.hands:
            self.hand(origin, self.place.core).start()

    def start(self):
        place = self.place

        @pl.when(place.level < place.levels - 1)
        def _():
            self.climb(place.chip).start()

        @pl.when(place.level > 0)
        def _():
            self.sink(place.chip).start()

        self.pass_on(place.chip)

    def crossed(self, at):
        place = self.place
        origin = at * 2 + 1 - place.side
        skipped = place.at_next & (at == place.end)
        halved = place.at_end & (at == place.next)

        @pl.when(skipped)
        def _():
            self.hop(place.end, True).wait_recv()

        @pl.when(halved)
        def _():
            self.cross(origin, True).wait_recv()

        @pl.when(~skipped & ~halved)
        def _():
            self.cross(origin).wait_recv()

        @pl.when(place.at_end & (at == place.end))
        def _():
            self.hop(place.end, True).start()

        @pl.when(~halved)
        def _():
            self.give(origin)

    def finish(self):
        place = self.place

        @pl.when(place.at_end)
        def _():
            self.hop(place.next, False).wait_recv()
            self.give(place.next * 2 + 1 - place.side)

    def step(self, n):
        place = self.place
        level, side, top = place.level, place.side, place.levels - 1
        under, over = level - n, level + n

        @pl.when((n > 0) & (under >= 0))
        def _():
            origin = under * 2 + side
            self.climb(origin).wait_recv()

            @pl.when(level < top)
            def _():
                self.climb(origin).start()

            self.pass_on(origin)

        @pl.when((n > 0) & (over <= top))
        def _():
            origin = over * 2 + side
            self.sink(origin).wait_recv()

            @pl.when(level > 0)
            def _():
                self.sink(origin).start()

            self.pass_on(origin)

        @pl.when(place.at_next & (n == place.levels - 2))
        def _():
            self.hop(place.next, False).start()

        @pl.when((n > 0) & (under + 1 >= 0))
        def _():
            self.crossed(under + 1)

        @pl.when((n > 1) & (over - 1 <= top))
        def _():
            self.crossed(over - 1)

    def take_hands(self):
        place = self.place

        def taken(origin, carry):
            self.hand(origin, 1 - place.core).wait_recv()
            return carry

        lax.fori_loop(0, place.chips, taken, 0)

    def drain(self):
        place = self.place
        level, side, top = place.level, place.side, place.levels - 1

        def handed(origin, carry):
            self.hand(origin, place.core).wait_send()
            return carry

        if self.hands:
            lax.fori_loop(0, place.chips, handed, 0)

        def sent(at, carry):
            skipped = place.at_next & (at == place.end)
            halved = place.at_end & (at == place.next)

            @pl.when(halved)
            def _():
                self.cross(at * 2 + side, True).wait_send()

            @pl.when(~skipped & ~halved)
            def _():
                self.cross(at * 2 + side).wait_send()

            @pl.when((level < top) & (at <= level))
            def _():
                self.climb(at * 2 + side).wait_send()

            @pl.when((level > 0) & (at >= level))
            def _():
                self.sink(at * 2 + side).wait_send()

            return carry

        lax.fori_loop(0, place.levels, sent, 0)

        @pl.when(place.at_end)
        def _():
            self.hop(place.end, True).wait_send()

        @pl.when(place.at_next)
        def _():
            self.hop(place.next, False).wait_send()


class RowGathers:
    def __init__(self, place, block, sems):
        count = len(sems) // 10
        self.rings = []
        for i in range(count):

            def piece(origin, whose, i=i):
                whole = block(origin, whose)
                rows = whole.shape[0] // count
                return whole.at[pl.ds(i * rows, rows)]

            self.rings.append(RowGather(place, piece, sems[10 * i : 10 * i + 10]))

    @staticmethod
    def semaphores(levels):
        return RowGather.semaphores(levels) * 2

    def start(self):
        for ring in self.rings:
            ring.start()

    def step(self, n):
        for ring in self.rings:
            ring.step(n)

    def finish(self):
        for ring in self.rings:
            ring.finish()

    def take_hand(self, origin, whose):
        for ring in self.rings:
            ring.hand(origin, whose).wait_recv()

    def take_hands(self):
        for ring in self.rings:
            ring.take_hands()

    def drain(self):
        for ring in self.rings:
            ring.drain()


class ChainSum:
    def __init__(self, place, parts, side_buf, chain_buf, hop_buf, sems):
        self.place, self.parts = place, parts
        self.side_buf, self.chain_buf, self.hop_buf = side_buf, chain_buf, hop_buf
        (
            self.up_send,
            self.up_recv,
            self.down_send,
            self.down_recv,
            self.side_send,
            self.side_recv,
            self.hop_send,
            self.hop_recv,
            self.half_send,
            self.half_recv,
        ) = sems

    @staticmethod
    def semaphores(levels):
        dma = pltpu.SemaphoreType.DMA
        return [dma((levels,))] * 6 + [dma] * 4

    @staticmethod
    def buffers(levels, block, dtype=jnp.bfloat16):
        return [
            pltpu.VMEM((levels,) + block, dtype),
            pltpu.VMEM((levels + 1,) + block, dtype),
            pltpu.VMEM(block, dtype),
        ]

    def target(self, turn):
        place = self.place
        top = place.levels - 1
        far, near = top - turn // 2, turn // 2
        odd = turn % 2
        low_half = far * (1 - odd) + near * odd
        high_half = near * (1 - odd) + far * odd
        inner = low_half * (1 - place.upper) + high_half * place.upper
        outer = (top - turn) * (1 - place.upper) + turn * place.upper
        return jnp.where(place.at_end, outer, inner)

    def from_under(self, goal):
        return self.chain_buf.at[goal + 1]

    def from_over(self, goal):
        return self.chain_buf.at[goal]

    def other(self, goal):
        return self.parts(goal * 2 + 1 - self.place.side)

    def cross(self, source, target, goal):
        return remote(
            source, target, self.side_send.at[goal], self.side_recv.at[goal], self.place.beside
        )

    def whole(self, goal):
        return self.cross(self.other(goal), self.side_buf.at[goal], goal)

    def lifted(self, goal):
        return self.cross(self.hop_buf, self.side_buf.at[goal], goal)

    def upper(self, goal):
        return self.cross(upper_half(self.other(goal)), upper_half(self.side_buf.at[goal]), goal)

    def lower(self, goal):
        return remote(
            lower_half(self.hop_buf),
            lower_half(self.side_buf.at[goal]),
            self.half_send,
            self.half_recv,
            self.place.beside,
        )

    def hop_out(self):
        return remote(
            self.other(self.place.end), self.hop_buf, self.hop_send, self.hop_recv, self.place.outward
        )

    def hop_in(self):
        return remote(
            lower_half(self.other(self.place.next)),
            lower_half(self.hop_buf),
            self.hop_send,
            self.hop_recv,
            self.place.inward,
        )

    def up(self, goal):
        return remote(
            self.side_buf.at[goal],
            self.from_under(goal),
            self.up_send.at[goal],
            self.up_recv.at[goal],
            self.place.above,
        )

    def down(self, goal):
        return remote(
            self.side_buf.at[goal],
            self.from_over(goal),
            self.down_send.at[goal],
            self.down_recv.at[goal],
            self.place.below,
        )

    def cases(self, goal):
        place = self.place
        to_end, to_next = goal == place.end, goal == place.next
        return (
            place.at_end & to_end,
            place.at_end & to_next,
            place.at_next & to_end,
            place.at_next & to_next,
        )

    def send(self, goal):
        end_end, end_next, next_end, next_next = self.cases(goal)

        @pl.when(end_next)
        def _():
            self.hop_in().start()

        @pl.when(next_end)
        def _():
            self.hop_out().start()

        @pl.when(end_next | next_next)
        def _():
            self.upper(goal).start()

        @pl.when(~(end_end | end_next | next_end | next_next))
        def _():
            self.whole(goal).start()

    def send_joined(self):
        place, wide = self.place, jnp.float32
        hop = self.hop_buf

        @pl.when(place.at_end)
        def _():
            self.hop_out().wait_recv()
            total = hop[...].astype(wide) + self.other(place.end)[...].astype(wide)
            hop[...] = total.astype(hop.dtype)
            self.lifted(place.end).start()

        @pl.when(place.at_next)
        def _():
            self.hop_in().wait_recv()
            half = hop.shape[0] // 2
            own = lower_half(self.other(place.next))[...].astype(wide)
            hop[:half] = (hop[:half].astype(wide) + own).astype(hop.dtype)
            self.lower(place.next).start()

    def add(self, goal, ref):
        held = self.side_buf
        total = held[goal].astype(jnp.float32) + ref[...].astype(jnp.float32)
        held[goal] = total.astype(held.dtype)

    def take_side(self, goal):
        place = self.place
        level, top = place.level, place.levels - 1
        end_end, end_next, next_end, next_next = self.cases(goal)
        held = self.side_buf
        own = self.parts(goal * 2 + place.side)
        half = held.shape[1] // 2

        @pl.when(end_next)
        def _():
            self.upper(goal).wait_recv()
            total = held[goal, half:].astype(jnp.float32) + upper_half(own)[...].astype(jnp.float32)
            held[goal, half:] = total.astype(held.dtype)
            held[goal, :half] = lower_half(own)[...]

        @pl.when(next_end)
        def _():
            held[goal] = own[...]

        @pl.when(next_next)
        def _():
            self.upper(goal).wait_recv()
            self.lower(goal).wait_recv()

        @pl.when(~(end_next | next_end | next_next))
        def _():
            self.whole(goal).wait_recv()

        @pl.when(~(end_next | next_end))
        def _():
            self.add(goal, own)

        @pl.when((goal > level) & (level == 0))
        def _():
            self.up(goal).start()

        @pl.when((goal < level) & (level == top))
        def _():
            self.down(goal).start()

    def take_chain(self, goal):
        place = self.place
        level, top = place.level, place.levels - 1

        @pl.when((goal > level) & (level > 0))
        def _():
            self.up(goal).wait_recv()
            self.add(goal, self.from_under(goal))
            self.up(goal).start()

        @pl.when((goal < level) & (level < top))
        def _():
            self.down(goal).wait_recv()
            self.add(goal, self.from_over(goal))
            self.down(goal).start()

    def close(self):
        place = self.place
        level, top = place.level, place.levels - 1

        @pl.when(level > 0)
        def _():
            self.up(level).wait_recv()
            self.add(level, self.from_under(level))

        @pl.when(level < top)
        def _():
            self.down(level).wait_recv()
            self.add(level, self.from_over(level))

    def drain(self):
        place = self.place

        def goal_done(goal, carry):
            end_end, end_next, next_end, next_next = self.cases(goal)

            @pl.when(end_end)
            def _():
                self.lifted(goal).wait_send()

            @pl.when(end_next)
            def _():
                self.hop_in().wait_send()

            @pl.when(next_end)
            def _():
                self.hop_out().wait_send()

            @pl.when(next_next)
            def _():
                self.lower(goal).wait_send()

            @pl.when(end_next | next_next)
            def _():
                self.upper(goal).wait_send()

            @pl.when(~(end_end | end_next | next_end | next_next))
            def _():
                self.whole(goal).wait_send()

            @pl.when(goal > place.level)
            def _():
                self.up(goal).wait_send()

            @pl.when(goal < place.level)
            def _():
                self.down(goal).wait_send()

            return carry

        lax.fori_loop(0, place.levels, goal_done, 0)


def open_kernel(
    sequences,
    tokens_ref,
    cotangent_ref,
    pick_ref,
    gain_ref,
    lengths_ref,
    frequency_ref,
    query_ref,
    key_ref,
    value_ref,
    out_ref,
    gate_ref,
    up_ref,
    dealt_ref,
    normed_ref,
    upstream_own,
    cosine_ref,
    sine_ref,
    mask_ref,
    query_all,
    key_all,
    value_all,
    out_all,
    gate_all,
    up_all,
    slices_ref,
    both_lengths_ref,
    deal_send,
    deal_recv,
    quad_send,
    quad_recv,
    swap_send,
    swap_recv,
    keep_sem,
    pair_send,
    pair_recv,
    pair_keep,
    *ring_sems,
):
    place = Place()
    core, chip = place.core, place.chip
    own_rows = query_ref.shape[0]
    quarter = query_all.shape[2]
    narrow = key_all.shape[2]
    head_rows = out_all.shape[0]
    lanes = out_ref.shape[1]
    members = 2 * place.chips
    for index in range(members):
        picked = pick_ref[index]
        both = [ref[picked].astype(jnp.float32) for ref in (tokens_ref, cotangent_ref)]
        slices_ref[index] = jnp.concatenate(both, axis=0).astype(jnp.bfloat16)
    greet(place.plane_targets() + [place.across])

    def deal_copy(offset, sending):
        target, index = place.member(offset if sending else -offset)
        return remote(
            slices_ref.at[index],
            dealt_ref.at[place.fsdp if sending else index],
            deal_send.at[offset - 1],
            deal_recv.at[offset - 1],
            target,
        )

    for offset in range(1, members):
        deal_copy(offset, True).start()

    def rows(who):
        return pl.ds(pl.multiple_of(who * own_rows, own_rows), own_rows)

    def columns(who, width):
        return pl.ds(pl.multiple_of(who * width, width), width)

    def spots(who):
        lane_start = pl.multiple_of((2 * chip + core) * lanes, lanes)
        return [
            (query_ref.at[:, columns(who, quarter)], query_all.at[chip, rows(core)]),
            (key_ref.at[:, columns(who, narrow)], key_all.at[chip, rows(core)]),
            (value_ref.at[:, columns(who, narrow)], value_all.at[chip, rows(core)]),
            (
                out_ref.at[pl.ds(pl.multiple_of(who * head_rows, head_rows), head_rows)],
                out_all.at[:, pl.ds(lane_start, lanes)],
            ),
        ]

    def arrivals():
        lane_start = pl.multiple_of((2 * chip + 1 - core) * lanes, lanes)
        return [
            query_all.at[chip, rows(1 - core)],
            key_all.at[chip, rows(1 - core)],
            value_all.at[chip, rows(1 - core)],
            out_all.at[:, pl.ds(lane_start, lanes)],
        ]

    sends = [
        remote(src, dst, swap_send.at[i], swap_recv.at[i], place.mate)
        for i, (src, dst) in enumerate(spots(1 - core))
    ]
    keeps = [
        pltpu.make_async_copy(src, dst, keep_sem.at[i])
        for i, (src, dst) in enumerate(spots(core))
    ]
    mate_lengths = remote(
        lengths_ref, both_lengths_ref.at[core], swap_send.at[4], swap_recv.at[4], place.mate
    )
    own_lengths = pltpu.make_async_copy(lengths_ref, both_lengths_ref.at[core], keep_sem.at[4])
    own_slice = pltpu.make_async_copy(
        slices_ref.at[place.fsdp], dealt_ref.at[place.fsdp], keep_sem.at[5]
    )
    own_slice.start()
    units = gate_ref.shape[1]

    def halves(who):
        at = pl.ds(pl.multiple_of(who * units, units), units)
        return [gate_all.at[:, at], up_all.at[:, at]]

    shards = (gate_ref, up_ref)
    pair_copies = []
    for i, (src, dst) in enumerate(zip(shards, halves(place.tp))):
        pair_copies.append(
            (
                remote(src, dst, pair_send.at[i], pair_recv.at[i], place.across),
                pltpu.make_async_copy(src, dst, pair_keep.at[i]),
            )
        )
    for i in range(4):
        sends[i].start()
        keeps[i].start()
    mate_lengths.start()
    own_lengths.start()

    out_lanes = 2 * lanes
    views = [
        lambda who, core: query_all.at[who],
        lambda who, core: key_all.at[who],
        lambda who, core: value_all.at[who],
        lambda who, core: out_all.at[:, lanes_at(who, out_lanes)],
    ]
    rings = [
        RowGather(place, view, ring_sems[8 * i : 8 * i + 8], hands=False)
        for i, view in enumerate(views)
    ]
    landed = arrivals()
    for i in range(4):
        keeps[i].wait()
        sends[i].wait_send()
        remote(landed[i], landed[i], swap_send.at[i], swap_recv.at[i], place.mate).wait_recv()
        rings[i].start()

    own_slice.wait()
    for offset in range(1, members):
        deal_copy(offset, False).wait_recv()
    tp = place.tp
    half = slices_ref.shape[1] // 2
    step_rows = 4
    for start in range(0, members, step_rows):
        block = dealt_ref[start : start + step_rows].astype(jnp.float32)
        span = slice(start * half, (start + step_rows) * half)
        upstream_own[span, :] = (
            block[:, half:].reshape(step_rows * half, block.shape[2]).astype(jnp.bfloat16)
        )
        x = block[:, :half].reshape(step_rows * half, block.shape[2])
        factor = lax.rsqrt(jnp.mean(x * x, axis=-1, keepdims=True) + epsilon)
        normed_ref[core, tp, start * half : (start + step_rows) * half, :] = (
            x * factor * gain_ref[...]
        ).astype(jnp.bfloat16)
    mine = normed_ref.at[core, tp]
    to_mate = remote(mine, mine, quad_send.at[0], quad_recv.at[0], place.mate)
    to_across = remote(mine, mine, quad_send.at[1], quad_recv.at[1], place.across)
    to_across.start()
    to_mate.start()
    for both in pair_copies:
        both[0].start()
        both[1].start()
    levels = place.levels
    own_lengths.wait()
    mate_lengths.wait_send()
    theirs = both_lengths_ref.at[1 - core]
    remote(theirs, theirs, swap_send.at[4], swap_recv.at[4], place.mate).wait_recv()
    group = mask_ref.shape[1]
    head = cosine_ref.shape[1]
    across_sign = jnp.where(
        lax.broadcasted_iota(jnp.int32, (group, head), 1) < head // 2, -1.0, 1.0
    )
    for which in range(2):
        ends = []
        for at in range(sequences):
            length = both_lengths_ref[which, 0:1, at : at + 1]
            ends.append(length if at == 0 else ends[-1] + length)

        def segment_start(place_ids):
            start = jnp.zeros_like(place_ids)
            for end in ends:
                start = jnp.where(place_ids >= end, end, start)
            return start

        at_rows = pl.ds(which * group, group)
        row_ids = lax.broadcasted_iota(jnp.int32, (group, head), 0)
        position = (row_ids - segment_start(row_ids)).astype(jnp.float32)
        angles = position * frequency_ref[...]
        cosine_ref[at_rows, :] = jnp.cos(angles)
        sine_ref[at_rows, :] = jnp.sin(angles) * across_sign
        row_ids = lax.broadcasted_iota(jnp.int32, (group, group), 0)
        key_ids = lax.broadcasted_iota(jnp.int32, (group, group), 1)
        allowed = (key_ids <= row_ids) & (key_ids >= segment_start(row_ids))
        mask_ref[which] = jnp.where(allowed, 0.0, masked_score)
    for ring in rings:
        ring.step(1)
    other = normed_ref.at[core, 1 - tp]
    remote(other, other, quad_send.at[1], quad_recv.at[1], place.across).wait_recv()
    passed = remote(other, other, quad_send.at[2], quad_recv.at[2], place.mate)
    passed.start()
    for n in range(2, levels + 1):
        for ring in rings:
            ring.step(n)
    for ring in rings:
        ring.finish()
        ring.drain()
    for offset in range(1, members):
        deal_copy(offset, True).wait_send()
    to_mate.wait_send()
    to_across.wait_send()
    passed.wait_send()
    for slot, piece in ((0, normed_ref.at[1 - core, tp]), (2, normed_ref.at[1 - core, 1 - tp])):
        remote(piece, piece, quad_send.at[slot], quad_recv.at[slot], place.mate).wait_recv()
    for i, dst in enumerate(halves(1 - place.tp)):
        pair_copies[i][1].wait()
        pair_copies[i][0].wait_send()
        remote(dst, dst, pair_send.at[i], pair_recv.at[i], place.across).wait_recv()


def open_layer(
    tokens, cotangent, pick, gain_vec, lengths, sequences, frequency, w_query, w_key, w_value, w_out, w_gate, w_up
):
    members, slice_rows, model_width = tokens.shape
    dealt_shape = (members, 2 * slice_rows, model_width)
    chips = members // 2
    own_rows = w_query.shape[0]
    low = jnp.bfloat16
    vmem = pl.BlockSpec(memory_space=pltpu.VMEM)
    anywhere = pl.BlockSpec(memory_space=pl.ANY)
    dma = pltpu.SemaphoreType.DMA
    group, head = 2 * own_rows, frequency.shape[1]
    return pl.pallas_call(
        functools.partial(open_kernel, sequences),
        name="open_layer",
        out_shape=[
            jax.ShapeDtypeStruct(dealt_shape, low),
            jax.ShapeDtypeStruct((2, 2, own_rows, model_width), low),
            jax.ShapeDtypeStruct((own_rows, model_width), low),
            jax.ShapeDtypeStruct((2 * group, head), jnp.float32),
            jax.ShapeDtypeStruct((2 * group, head), jnp.float32),
            jax.ShapeDtypeStruct((2, group, group), jnp.float32),
            jax.ShapeDtypeStruct((chips, 2 * own_rows, w_query.shape[1] // 2), low),
            jax.ShapeDtypeStruct((chips, 2 * own_rows, w_key.shape[1] // 2), low),
            jax.ShapeDtypeStruct((chips, 2 * own_rows, w_value.shape[1] // 2), low),
            jax.ShapeDtypeStruct((w_out.shape[0] // 2, members * w_out.shape[1]), low),
            jax.ShapeDtypeStruct((model_width, 2 * w_gate.shape[1]), low),
            jax.ShapeDtypeStruct((model_width, 2 * w_up.shape[1]), low),
        ],
        in_specs=[vmem] * 2
        + [pl.BlockSpec(memory_space=pltpu.SMEM)]
        + [vmem] * 3
        + [anywhere] * 6,
        out_specs=[vmem] * 6 + [anywhere] * 6,
        scratch_shapes=[
            pltpu.VMEM(dealt_shape, low),
            pltpu.VMEM((2,) + lengths.shape, jnp.int32),
            dma((members - 1,)),
            dma((members - 1,)),
            dma((3,)),
            dma((3,)),
            dma((5,)),
            dma((5,)),
            dma((6,)),
            dma((2,)),
            dma((2,)),
            dma((2,)),
        ]
        + RowGather.semaphores(chips // 2, hands=False) * 4,
        compiler_params=pltpu.CompilerParams(
            collective_id=0, has_side_effects=True, vmem_limit_bytes=65_400_000
        ),
        cost_estimate=link_cost(110),
    )(tokens, cotangent, pick, gain_vec, lengths, frequency, w_query, w_key, w_value, w_out, w_gate, w_up)


class QuadSum:
    def __init__(self, place, parts, near, pair, far, send, recv):
        self.place, self.parts = place, parts
        self.near, self.pair, self.far = near, pair, far
        self.send, self.recv = send, recv

    @staticmethod
    def scratch(rows, width):
        low, dma = jnp.bfloat16, pltpu.SemaphoreType.DMA
        return [
            pltpu.VMEM((2, rows, width), low),
            pltpu.VMEM((rows, width), low),
            pltpu.VMEM((rows, width), low),
            dma((3,)),
            dma((3,)),
        ]

    def to_mate(self, half):
        return remote(
            self.parts.at[1 - self.place.core, half],
            self.near.at[half],
            self.send.at[half],
            self.recv.at[half],
            self.place.mate,
        )

    def to_across(self):
        return remote(self.pair, self.far, self.send.at[2], self.recv.at[2], self.place.across)

    def start(self):
        self.to_mate(1 - self.place.tp).start()
        self.to_mate(self.place.tp).start()

    def relay(self):
        core, tp, wide = self.place.core, self.place.tp, jnp.float32
        self.to_mate(1 - tp).wait_recv()
        self.pair[...] = (
            self.parts[core, 1 - tp].astype(wide) + self.near[1 - tp].astype(wide)
        ).astype(jnp.bfloat16)
        self.to_across().start()

    def total(self):
        core, tp, wide = self.place.core, self.place.tp, jnp.float32
        self.to_mate(tp).wait_recv()
        total = self.parts[core, tp].astype(wide) + self.near[tp].astype(wide)
        self.to_across().wait_recv()
        return total + self.far[...].astype(wide)

    def drain(self):
        for half in range(2):
            self.to_mate(half).wait_send()
        self.to_across().wait_send()


def nt_dot(left, right):
    return lax.dot_general(
        left, right, (((1,), (1,)), ((), ())), preferred_element_type=jnp.float32
    )


def tn_dot(left, right):
    return lax.dot_general(
        left, right, (((0,), (0,)), ((), ())), preferred_element_type=jnp.float32
    )


def lanes_at(index, width):
    return pl.ds(pl.multiple_of(index * width, width), width)


def attend_kernel(
    experts,
    normed_ref,
    query_ref,
    key_ref,
    value_ref,
    out_ref,
    cosine_ref,
    sine_ref,
    mask_ref,
    dealt_ref,
    query_gain,
    key_gain,
    moe_gain,
    router_ref,
    routes_ref,
    upstream_own,
    upstream_all,
    moe_ext,
    residual_ref,
    gates_ref,
    query_pre,
    query_low,
    key_pre,
    key_low,
    value_low,
    probs_ref,
    mixed_ref,
    query_w,
    key_w,
    value_w,
    out_w,
    router_rows,
    parts,
    near,
    pair,
    far,
    quad_send,
    quad_recv,
    keep_sem,
    load_sem,
    *ring_sems,
):
    place = Place()
    core = place.core
    wide, low = jnp.float32, jnp.bfloat16
    own_rows, width = residual_ref.shape
    group = 2 * own_rows
    head = query_gain.shape[1]
    heads = query_w.shape[1] // head
    members = dealt_ref.shape[0]
    half = dealt_ref.shape[1] // 2
    step_rows = 4

    def token_rows(start):
        block = dealt_ref[start : start + step_rows].astype(wide)[:, :half]
        return block.reshape(step_rows * half, width)

    loads = [
        pltpu.make_async_copy(src, dst, load_sem.at[i])
        for i, (src, dst) in enumerate(
            ((query_ref, query_w), (key_ref, key_w), (value_ref, value_w), (out_ref, out_w))
        )
    ]
    for load in loads:
        load.start()
    keep = pltpu.make_async_copy(upstream_own, upstream_all.at[place.chip, core], keep_sem)
    keep.start()
    greet(place.ring_targets() + [place.mate, place.across])
    gather = RowGathers(place, lambda origin, whose: upstream_all.at[origin, whose], ring_sems)
    keep.wait()
    gather.start()
    router_rows[...] = jnp.zeros_like(router_rows)
    router_rows[:experts, :] = router_ref[...]

    def turned(values, gain_ref):
        factor = lax.rsqrt(jnp.mean(values * values, axis=-1, keepdims=True) + epsilon)
        scaled = values * factor * gain_ref[...]
        return (scaled * cosine_ref[...] + pltpu.roll(scaled, head // 2, 1) * sine_ref[...]).astype(
            low
        )

    x = normed_ref[...].reshape(2 * group, width)
    for load in loads:
        load.wait()

    def project(index, carry):
        both = jnp.dot(
            normed_ref[...].reshape(2 * group, width),
            query_w[:, lanes_at(index, 2 * head)],
            preferred_element_type=wide,
        )
        query_pre[:, lanes_at(index, 2 * head)] = both.astype(low)
        for which in range(2):
            one = both[:, which * head : (which + 1) * head]
            query_low[:, lanes_at(2 * index + which, head)] = turned(one, query_gain)
        return carry

    lax.fori_loop(0, heads // 2, project, 0)
    key_values = jnp.dot(x, key_w[...], preferred_element_type=wide)
    key_pre[...] = key_values
    key_low[...] = turned(key_values, key_gain)
    value_low[...] = jnp.dot(x, value_w[...], preferred_element_type=wide).astype(low)
    gather.step(1)
    scale = head ** (-0.5)
    batch = 4

    def attend(index, carry):
        which = index // (heads // batch)
        first = (index % (heads // batch)) * batch
        rows = lanes_at(which, group)
        key = key_low[rows, :]
        value = value_low[rows, :]
        mask = mask_ref[which]
        for offset in range(batch):
            at = lanes_at(first + offset, head)
            scores = nt_dot(query_low[rows, at], key) * scale + mask
            peak = jnp.max(scores, axis=-1, keepdims=True)
            exponent = jnp.exp(scores - peak)
            probs = (exponent * (1.0 / jnp.sum(exponent, axis=-1, keepdims=True))).astype(low)
            probs_ref[which * heads + first + offset] = probs
            mixed_ref[rows, at] = jnp.dot(probs, value, preferred_element_type=wide).astype(low)
        return carry

    lax.fori_loop(0, heads // batch, attend, 0)
    gather.step(2)
    lax.fori_loop(heads // batch, 2 * heads // batch, attend, 0)

    def out_rows(whose):
        left = mixed_ref[lanes_at(whose, group), :]

        def out_lanes(index, carry):
            at = lanes_at(index, 512)
            product = jnp.dot(left, out_w[:, at], preferred_element_type=wide).astype(low)
            parts[whose, :, :, at] = product.reshape(2, own_rows, 512)
            return carry

        lax.fori_loop(0, width // 512, out_lanes, 0)

    sums = QuadSum(place, parts, near, pair, far, quad_send, quad_recv)
    out_rows(1 - core)
    sums.start()
    out_rows(core)
    sums.relay()
    gather.step(3)
    total = sums.total()
    tokens = jnp.concatenate(
        [token_rows(start) for start in range(0, members, step_rows)], axis=0
    )
    residual = tokens + total
    residual_ref[...] = residual
    factor = lax.rsqrt(jnp.mean(residual * residual, axis=-1, keepdims=True) + epsilon)
    moe_low = (residual * factor * moe_gain[...]).astype(low)
    moe_ext[:, :width] = moe_low
    logits = nt_dot(moe_low, router_rows[...])
    own_routes = routes_ref[lanes_at(place.tp, own_rows), :]
    lane = lax.broadcasted_iota(jnp.int32, (own_rows, 128), 1)
    chosen = own_routes[:, 0:1] == lane
    for choice in range(1, own_routes.shape[1]):
        chosen |= own_routes[:, choice : choice + 1] == lane
    logits = jnp.where(chosen, logits, masked_score)
    exponent = jnp.exp(logits - jnp.max(logits, axis=-1, keepdims=True))
    exponent = jnp.where(chosen, exponent, 0.0)
    gates = exponent / jnp.sum(exponent, axis=-1, keepdims=True)
    gates_ref[...] = gates
    high = gates.astype(low).astype(wide)
    middle = (gates - high).astype(low).astype(wide)
    rest = gates - high - middle
    moe_ext[:, width:] = (
        high + pltpu.roll(middle, experts, 1) + pltpu.roll(rest, 2 * experts, 1)
    ).astype(low)
    for n in range(4, place.levels + 1):
        gather.step(n)
    gather.finish()
    gather.take_hands()
    gather.drain()
    sums.drain()


def attend_layer(
    experts,
    normed,
    query_w,
    key_w,
    value_w,
    out_w,
    tables,
    dealt,
    gain_vecs,
    router,
    routes,
    upstream_own,
):
    own_rows, width = normed.shape[2:]
    rows = 4 * own_rows
    members = dealt.shape[0]
    chips = members // 2
    heads_width, head = query_w.shape[1], key_w.shape[1]
    group = 2 * own_rows
    wide, low = jnp.float32, jnp.bfloat16
    vmem = pl.BlockSpec(memory_space=pltpu.VMEM)
    anywhere = pl.BlockSpec(memory_space=pl.ANY)
    shape = jax.ShapeDtypeStruct
    return pl.pallas_call(
        functools.partial(attend_kernel, experts),
        name="attend_layer",
        out_shape=[
            shape((chips, 2, own_rows, width), low),
            shape((own_rows, width + 128), low),
            shape((own_rows, width), wide),
            shape((own_rows, 128), wide),
            shape((rows, heads_width), low),
            shape((rows, heads_width), low),
            shape((rows, head), wide),
            shape((rows, head), low),
            shape((rows, head), low),
            shape((2 * heads_width // head, group, group), low),
            shape((rows, heads_width), low),
        ],
        in_specs=[vmem] + [anywhere] * 4 + [vmem] * 10,
        out_specs=[anywhere] + [vmem] * 10,
        scratch_shapes=[
            pltpu.VMEM(query_w.shape, low),
            pltpu.VMEM(key_w.shape, low),
            pltpu.VMEM(value_w.shape, low),
            pltpu.VMEM(out_w.shape, low),
            pltpu.VMEM((128, width), low),
            pltpu.VMEM((2, 2, own_rows, width), low),
        ]
        + QuadSum.scratch(own_rows, width)
        + [pltpu.SemaphoreType.DMA, pltpu.SemaphoreType.DMA((4,))]
        + RowGathers.semaphores(chips // 2),
        compiler_params=pltpu.CompilerParams(
            collective_id=2, has_side_effects=True, vmem_limit_bytes=65_400_000
        ),
        cost_estimate=link_cost(60),
    )(
        normed,
        query_w,
        key_w,
        value_w,
        out_w,
        *tables,
        dealt,
        *gain_vecs,
        router,
        routes,
        upstream_own,
    )


def expert_kernel(
    experts,
    x_own,
    upstream_ref,
    gate_ref,
    up_ref,
    down_ref,
    entry_own,
    out_part,
    gate_grad_ref,
    up_grad_ref,
    down_grad_ref,
    x_all,
    u_all,
    gate_w,
    up_w,
    down_w,
    hidden,
    gate_val_grad,
    up_val_grad,
    scores,
    sums,
    mate_out,
    mate_in,
    side_buf,
    chain_buf,
    hop_buf,
    staged,
    load_sem,
    store_sem,
    both_sem,
    mate_send,
    mate_recv,
    *ring_sems,
):
    place = Place()
    core, chip, level, side = place.core, place.chip, place.level, place.side
    levels, top = place.levels, place.levels - 1
    rows = x_own.shape[0]
    tile = 2 * rows
    width = upstream_ref.shape[1]
    units = down_ref.shape[0]
    wide = jnp.float32
    low = jnp.bfloat16
    loads = [
        pltpu.make_async_copy(x_own, x_all.at[chip, core], load_sem.at[0]),
        pltpu.make_async_copy(gate_ref, gate_w, load_sem.at[1]),
        pltpu.make_async_copy(up_ref, up_w, load_sem.at[2]),
        pltpu.make_async_copy(down_ref, down_w, load_sem.at[3]),
        pltpu.make_async_copy(upstream_ref, u_all, load_sem.at[4]),
    ]
    for load in loads:
        load.start()
    greet(place.ring_targets() + [place.mate])

    gather = RowGathers(place, lambda origin, whose: x_all.at[origin, whose], ring_sems[:20])
    loads[0].wait()

    gather.start()
    for load in loads[1:]:
        load.wait()

    lane = lax.broadcasted_iota(jnp.int32, (128, 128), 0)
    select = (
        (lane == place.fsdp)
        | (lane == place.fsdp + experts)
        | (lane == place.fsdp + 2 * experts)
    ).astype(low)
    cut = 256
    across_lanes = lax.broadcasted_iota(jnp.int32, (tile, 128), 1)

    def forward_tile(origin):
        x = x_all[origin].reshape(tile, x_all.shape[3])
        gate_lanes = jnp.dot(x[:, width:], select, preferred_element_type=wide)
        gate = jnp.concatenate([gate_lanes] * (cut // 128), axis=1)
        x = x[:, :width]
        start = pl.multiple_of(origin * tile, tile)
        u = u_all[pl.ds(start, tile), :]
        score = jnp.zeros((tile, 1), wide)
        for part in range(units // cut):
            lanes = slice(part * cut, (part + 1) * cut)
            gate_val = jnp.dot(x, gate_w[:, lanes], preferred_element_type=wide)
            up_val = jnp.dot(x, up_w[:, lanes], preferred_element_type=wide)
            back = lax.dot_general(
                u, down_w[lanes, :], (((1,), (1,)), ((), ())), preferred_element_type=wide
            )
            sigmoid = 1.0 / (1.0 + jnp.exp(-gate_val))
            swish = gate_val * sigmoid
            out = (swish * up_val).astype(low).astype(wide)
            score += jnp.sum(out * back, axis=1, keepdims=True)
            back = back * gate
            slope = sigmoid * (1.0 + gate_val * (1.0 - sigmoid))
            hidden[pl.ds(start, tile), lanes] = (out * gate).astype(low)
            gate_val_grad[pl.ds(start, tile), lanes] = (back * up_val * slope).astype(low)
            up_val_grad[pl.ds(start, tile), lanes] = (back * swish).astype(low)
        high = score.astype(low).astype(wide)
        packed = jnp.where(
            across_lanes == place.fsdp,
            high,
            jnp.where(across_lanes == place.fsdp + experts, score - high, 0.0),
        )
        scores[origin] = packed.astype(low)

    def gather_step(n, carry):
        gather.step(n)

        @pl.when(n == levels)
        def _():
            gather.finish()

        def candidate(which, carried):
            upward = which % 2
            facing = which // 2
            distance = n - 1 + facing
            at = level + distance * (2 * upward - 1)
            late = (n == levels) & (facing == 0) & (upward == place.upper) & place.at_end
            early = (n == 2) & (facing == 0) & place.at_end
            at = jnp.where(late, place.next, at)
            origin = at * 2 + side * facing + (1 - side) * (1 - facing)
            inside = (at >= 0) & (at <= top) & (distance >= 0) & ((distance > 0) | (upward == 0))

            @pl.when(inside & ~early)
            def _():
                gather.take_hand(origin, 1 - core)
                forward_tile(origin)

            return carried

        return lax.fori_loop(0, 4, candidate, carry)

    lax.fori_loop(0, levels + 1, gather_step, 0)

    plane_sum = ChainSum(place, lambda chip: sums.at[chip], side_buf, chain_buf, hop_buf, ring_sems[20:])

    def to_mate(goal_chip, slot):
        return remote(
            mate_out.at[slot],
            mate_in.at[goal_chip],
            mate_send.at[slot],
            mate_recv.at[goal_chip],
            place.mate,
        )

    def backward_tile(goal_chip, slot, reuse):
        start = pl.multiple_of(goal_chip * tile, tile)
        own_start = pl.multiple_of(goal_chip * tile + core * rows, rows)
        mate_start = pl.multiple_of(goal_chip * tile + (1 - core) * rows, rows)

        @pl.when(reuse)
        def _():
            to_mate(goal_chip, slot).wait_send()

        grads = gate_val_grad[pl.ds(start, tile), :]
        up_grads = up_val_grad[pl.ds(start, tile), :]
        piece = 512
        for first in range(0, width, piece):
            lanes = slice(first, first + piece)
            whole = lax.dot_general(
                grads, gate_w[lanes, :], (((1,), (1,)), ((), ())), preferred_element_type=wide
            ) + lax.dot_general(
                up_grads, up_w[lanes, :], (((1,), (1,)), ((), ())), preferred_element_type=wide
            )
            halves = whole.astype(low).reshape(2, rows, piece)
            sums[goal_chip, :, lanes] = jnp.where(core == 0, halves[0], halves[1])
            mate_out[slot, :, lanes] = jnp.where(core == 0, halves[1], halves[0])
        sums[goal_chip, :, width:] = scores[goal_chip, pl.ds(pl.multiple_of(core * rows, rows), rows)]
        mate_out[slot, :, width:] = scores[
            goal_chip, pl.ds(pl.multiple_of((1 - core) * rows, rows), rows)
        ]
        to_mate(goal_chip, slot).start()

    def joined(goal_chip, slot):
        to_mate(goal_chip, slot).wait_recv()
        sums[goal_chip] = (
            sums[goal_chip].astype(wide) + mate_in[goal_chip].astype(wide)
        ).astype(low)

    def backward_turn(turn, carry):
        goal = plane_sum.target(turn)
        backward_tile(goal * 2 + 1 - side, 0, turn > 0)
        backward_tile(goal * 2 + side, 1, turn > 0)
        joined(goal * 2 + 1 - side, 0)
        plane_sum.send(goal)
        joined(goal * 2 + side, 1)
        return carry

    lax.fori_loop(0, levels, backward_turn, 0)
    plane_sum.send_joined()

    def store(target, start, slot):
        return pltpu.make_async_copy(
            staged.at[slot], target.at[pl.ds(start, tile)], store_sem.at[slot]
        )

    def output_tile(origin, carry):
        start = pl.multiple_of(origin * tile, tile)
        slot = origin % 2

        @pl.when(origin > 1)
        def _():
            store(out_part, start, slot).wait()

        left = hidden[pl.ds(start, tile), :]
        for first in range(0, width, 512):
            lanes = slice(first, first + 512)
            staged[slot, :, lanes] = jnp.dot(
                left, down_w[:, lanes], preferred_element_type=wide
            ).astype(low)
        store(out_part, start, slot).start()
        return carry

    def down_grads(index, carry):
        start = pl.multiple_of(index * tile, tile)
        slot = index % 2
        store(down_grad_ref, start, slot).wait()
        left = hidden[:, pl.ds(start, tile)]
        for first in range(0, width, 512):
            lanes = slice(first, first + 512)
            staged[slot, :, lanes] = lax.dot_general(
                left, u_all[:, lanes], (((0,), (0,)), ((), ())), preferred_element_type=wide
            ).astype(low)
        store(down_grad_ref, start, slot).start()
        return carry

    def store_both(index):
        slot = index % 2
        start = pl.multiple_of(index * tile, tile)
        return [
            pltpu.make_async_copy(
                staged.at[slot, :, i * units : (i + 1) * units],
                target.at[pl.ds(start, tile)],
                both_sem.at[slot, i],
            )
            for i, target in enumerate((gate_grad_ref, up_grad_ref))
        ]

    def entry_weight_grads(index, carry):
        slot = index % 2

        @pl.when(index > 1)
        def _():
            for copy in store_both(index):
                copy.wait()

        left = x_all[:, :, :, pl.ds(pl.multiple_of(index * tile, tile), tile)]
        left = left.reshape(u_all.shape[0], tile)
        for i, right in enumerate((gate_val_grad, up_val_grad)):
            staged[slot, :, i * units : (i + 1) * units] = lax.dot_general(
                left, right[...], (((0,), (0,)), ((), ())), preferred_element_type=wide
            ).astype(low)
        for copy in store_both(index):
            copy.start()
        return carry

    plane_sum.take_side(plane_sum.target(0))
    lax.fori_loop(0, place.chips, output_tile, 0)
    plane_sum.take_chain(plane_sum.target(0))
    plane_sum.take_side(plane_sum.target(1))
    lax.fori_loop(0, units // tile, down_grads, 0)
    for slot in range(2):
        store(down_grad_ref, 0, slot).wait()
    plane_sum.take_chain(plane_sum.target(1))
    plane_sum.take_side(plane_sum.target(2))
    chunks = width // tile
    lax.fori_loop(0, chunks // 2, entry_weight_grads, 0)
    plane_sum.take_chain(plane_sum.target(2))
    plane_sum.take_side(plane_sum.target(3))
    lax.fori_loop(chunks // 2, chunks, entry_weight_grads, 0)
    plane_sum.take_chain(plane_sum.target(3))
    plane_sum.close()
    entry_own[...] = side_buf[level]
    for slot in range(2):
        for copy in store_both(slot):
            copy.wait()
        to_mate(0, slot).wait_send()
    plane_sum.drain()

    gather.drain()


def expert_layer(x_own, upstream_all, gate_all, up_all, down_all, experts):
    rows, span = x_own.shape
    total, width = upstream_all.shape
    units = down_all.shape[0]
    chips = total // (2 * rows)
    levels = chips // 2
    low = jnp.bfloat16
    vmem = pl.BlockSpec(memory_space=pltpu.VMEM)
    anywhere = pl.BlockSpec(memory_space=pl.ANY)
    dma = pltpu.SemaphoreType.DMA
    return pl.pallas_call(
        functools.partial(expert_kernel, experts),
        name="expert_layer",
        out_shape=[
            jax.ShapeDtypeStruct((rows, span), low),
            jax.ShapeDtypeStruct((total, width), low),
            jax.ShapeDtypeStruct((width, units), low),
            jax.ShapeDtypeStruct((width, units), low),
            jax.ShapeDtypeStruct((units, width), low),
        ],
        in_specs=[vmem] + [anywhere] * 4,
        out_specs=[vmem] + [anywhere] * 4,
        scratch_shapes=[
            pltpu.VMEM((chips, 2, rows, span), low),
            pltpu.VMEM((total, width), low),
            pltpu.VMEM((width, units), low),
            pltpu.VMEM((width, units), low),
            pltpu.VMEM((units, width), low),
            pltpu.VMEM((total, units), low),
            pltpu.VMEM((total, units), low),
            pltpu.VMEM((total, units), low),
            pltpu.VMEM((chips, 2 * rows, 128), low),
            pltpu.VMEM((chips, rows, span), low),
            pltpu.VMEM((2, rows, span), low),
            pltpu.VMEM((chips, rows, span), low),
            *ChainSum.buffers(levels, (rows, span)),
            pltpu.VMEM((2, 2 * rows, width), low),
            dma((5,)),
            dma((2,)),
            dma((2, 2)),
        ]
        + [dma((2,)), dma((chips,))]
        + RowGathers.semaphores(levels)
        + ChainSum.semaphores(levels),
        compiler_params=pltpu.CompilerParams(
            collective_id=5, has_side_effects=True, vmem_limit_bytes=65_400_000
        ),
        cost_estimate=link_cost(125),
    )(x_own, upstream_all, gate_all, up_all, down_all)


def attend_back_kernel(
    experts,
    entry_ref,
    residual_ref,
    gates_ref,
    dealt_ref,
    back_ref,
    router_ref,
    attn_gain,
    moe_gain,
    query_gain,
    key_gain,
    mixed_ref,
    probs_ref,
    query_low,
    key_low,
    value_low,
    query_pre,
    key_pre,
    cosine_ref,
    sine_ref,
    normed_ref,
    query_w,
    key_w,
    value_w,
    out_w,
    out_part,
    gate_part,
    up_part,
    down_part,
    output_ref,
    token_grad_ref,
    small_ref,
    query_own,
    key_value_own,
    out_own,
    gate_arrived,
    up_arrived,
    down_arrived,
    finished_ref,
    returned_ref,
    small_own,
    small_near,
    small_pair,
    small_parts,
    query_gain_part,
    residual_grad,
    low_all,
    mixed_grad,
    low_grads,
    key_total,
    value_total,
    out_grad,
    out_sums,
    out_mate,
    out_side,
    out_chain,
    out_hop,
    weight_side,
    weight_chain,
    weight_hop,
    narrow_grad,
    narrow_side,
    narrow_chain,
    narrow_hop,
    near,
    pair,
    far,
    quad_send,
    quad_recv,
    share_send,
    share_recv,
    swap_send,
    swap_recv,
    keep_sem,
    pair_send,
    pair_recv,
    deal_send,
    deal_recv,
    small_send,
    small_recv,
    total_send,
    total_recv,
    free_sem,
    *ring_sems,
):
    place = Place()
    core, tp, level = place.core, place.tp, place.level
    wide, low = jnp.float32, jnp.bfloat16
    own_rows, width = residual_ref.shape
    group = 2 * own_rows
    rows = 2 * group
    head = query_gain.shape[1]
    heads = query_w.shape[1] // head
    members = dealt_ref.shape[0]
    half = dealt_ref.shape[1] // 2
    step_rows = 4
    scale = head ** (-0.5)

    def dealt_rows(second):
        blocks = []
        for start in range(0, members, step_rows):
            block = dealt_ref[start : start + step_rows].astype(wide)
            block = block[:, half:] if second else block[:, :half]
            blocks.append(block.reshape(step_rows * half, width))
        return jnp.concatenate(blocks, axis=0)

    greet(place.plane_targets() + [place.across])
    to_mate = remote(
        out_part.at[:, 1 - core], out_mate, swap_send.at[0], swap_recv.at[0], place.mate
    )
    to_mate.start()
    keep = pltpu.make_async_copy(out_part.at[:, core], out_sums, keep_sem.at[0])
    keep.start()

    entry = entry_ref[:, :width].astype(wide)
    extra = entry_ref[:, width:].astype(wide)
    gates = gates_ref[...]
    gate_grad = extra + pltpu.roll(extra, 128 - experts, 1)
    inner = jnp.sum(gates * gate_grad, axis=-1, keepdims=True)
    logit_grad = (gates * (gate_grad - inner)).astype(low)
    residual = residual_ref[...]
    factor = lax.rsqrt(jnp.mean(residual * residual, axis=-1, keepdims=True) + epsilon)
    moe_low = (residual * factor * moe_gain[...]).astype(low)
    router = jnp.concatenate(
        [router_ref[...], jnp.zeros((128 - experts, width), low)], axis=0
    )
    moe_grad = entry + jnp.dot(logit_grad, router, preferred_element_type=wide)
    small_own[:8, :] = jnp.zeros((8, width), wide)
    small_own[8:, :] = tn_dot(logit_grad, moe_low)[: small_own.shape[0] - 8]
    scaled = moe_grad * moe_gain[...]
    inner = jnp.mean(scaled * residual, axis=-1, keepdims=True)
    small_own[1:2, :] = jnp.sum(moe_grad * residual * factor, axis=0, keepdims=True)
    residual_grad[...] = dealt_rows(True) + factor * (
        scaled - residual * (factor * factor) * inner
    )
    low_all[core, tp] = residual_grad[...].astype(low)
    mine = low_all.at[core, tp]
    share_mate = remote(mine, mine, share_send.at[0], share_recv.at[0], place.mate)
    share_across = remote(mine, mine, share_send.at[1], share_recv.at[1], place.across)
    share_across.start()
    share_mate.start()
    units = gate_arrived.shape[1]
    pair_copies = [
        remote(
            part.at[:, lanes_at(1 - tp, units)],
            arrived,
            pair_send.at[i],
            pair_recv.at[i],
            place.across,
        )
        for i, (part, arrived) in enumerate(((gate_part, gate_arrived), (up_part, up_arrived)))
    ]
    pair_copies.append(
        remote(
            down_part.at[lanes_at(1 - tp, units)],
            down_arrived,
            pair_send.at[2],
            pair_recv.at[2],
            place.across,
        )
    )
    pair_copies[0].start()

    out_ring = ChainSum(
        place, lambda chip: out_sums.at[chip], out_side, out_chain, out_hop, ring_sems[:10]
    )
    lanes = out_own.shape[1]
    weight_ring = ChainSum(
        place,
        lambda chip: out_grad.at[:, lanes_at(chip, 2 * lanes)],
        weight_side,
        weight_chain,
        weight_hop,
        ring_sems[10:20],
    )
    query_ring = ChainSum(
        place, lambda chip: out_sums.at[chip], out_side, out_chain, out_hop, ring_sems[20:30]
    )
    narrow_ring = ChainSum(
        place,
        lambda chip: narrow_grad.at[chip],
        narrow_side,
        narrow_chain,
        narrow_hop,
        ring_sems[30:],
    )
    keep.wait()
    to_mate.wait_recv()

    def join(turn, carry):
        goal = out_ring.target(turn)
        for origin in (goal * 2 + 1 - place.side, goal * 2 + place.side):
            out_sums[origin] = (
                out_sums[origin].astype(wide) + out_mate[origin].astype(wide)
            ).astype(low)
        out_ring.send(goal)
        return carry

    lax.fori_loop(0, place.levels, join, 0)
    out_ring.send_joined()
    other = low_all.at[core, 1 - tp]
    remote(other, other, share_send.at[1], share_recv.at[1], place.across).wait_recv()
    passed = remote(other, other, share_send.at[2], share_recv.at[2], place.mate)
    passed.start()
    for slot, piece in ((0, low_all.at[1 - core, tp]), (2, low_all.at[1 - core, 1 - tp])):
        remote(piece, piece, share_send.at[slot], share_recv.at[slot], place.mate).wait_recv()

    def out_grad_rows(index, carry):
        at = lanes_at(index, 256)
        left = mixed_ref[:, at]
        for first in range(0, width, 512):
            out_grad[at, first : first + 512] = tn_dot(
                left, low_all[:, :, :, first : first + 512].reshape(rows, 512)
            ).astype(low)
        return carry

    lax.fori_loop(0, mixed_ref.shape[1] // 256, out_grad_rows, 0)
    for turn in range(place.levels):
        weight_ring.send(weight_ring.target(turn))

    def mixed_lanes(index, carry):
        at = lanes_at(index, 256)
        mixed_grad[:, at] = nt_dot(low_all[...].reshape(rows, width), out_w[at, :]).astype(low)
        return carry

    lax.fori_loop(0, mixed_ref.shape[1] // 256, mixed_lanes, 0)
    key_total[...] = jnp.zeros_like(key_total)
    value_total[...] = jnp.zeros_like(value_total)
    query_gain_part[...] = jnp.zeros_like(query_gain_part)

    def pre_back(grad, values, gain_ref, cosine, sine):
        grad = grad * cosine - pltpu.roll(grad, head // 2, 1) * sine
        factor = lax.rsqrt(jnp.mean(values * values, axis=-1, keepdims=True) + epsilon)
        scaled = grad * gain_ref[...]
        inner = jnp.mean(scaled * values, axis=-1, keepdims=True)
        back = factor * (scaled - values * (factor * factor) * inner)
        return back.astype(low), jnp.sum(grad * values * factor, axis=0, keepdims=True)

    batch = 4

    def attend_back(index, carry):
        which = index // (heads // batch)
        first = (index % (heads // batch)) * batch
        at_rows = lanes_at(which, group)
        key = key_low[at_rows, :]
        value = value_low[at_rows, :]
        cosine, sine = cosine_ref[at_rows, :], sine_ref[at_rows, :]
        key_sum = key_total[at_rows, :]
        value_sum = value_total[at_rows, :]
        gain_sum = query_gain_part[...]
        for offset in range(batch):
            at = lanes_at(first + offset, head)
            probs = probs_ref[which * heads + first + offset]
            grads = mixed_grad[at_rows, at]
            prob_grad = nt_dot(grads, value)
            probs_wide = probs.astype(wide)
            inner = jnp.sum(probs_wide * prob_grad, axis=-1, keepdims=True)
            score_grad = (probs_wide * (prob_grad - inner)).astype(low)
            query = jnp.dot(score_grad, key, preferred_element_type=wide) * scale
            key_sum += tn_dot(score_grad, query_low[at_rows, at])
            value_sum += tn_dot(probs, grads)
            values = query_pre[at_rows, at].astype(wide)
            back, terms = pre_back(query, values, query_gain, cosine, sine)
            low_grads[at_rows, at] = back
            gain_sum += terms
        key_total[at_rows, :] = key_sum
        value_total[at_rows, :] = value_sum
        query_gain_part[...] = gain_sum
        return carry

    count = 2 * heads // batch
    share = -(-count // place.levels)
    for turn in range(place.levels):
        out_ring.take_side(out_ring.target(turn))
        lax.fori_loop(min(turn * share, count), min((turn + 1) * share, count), attend_back, 0)
        out_ring.take_chain(out_ring.target(turn))

    weight_ring.send_joined()
    back, terms = pre_back(
        key_total[...] * scale, key_pre[...], key_gain, cosine_ref[...], sine_ref[...]
    )
    small_own[2:3, :head] = query_gain_part[...]
    small_own[2:3, head : 2 * head] = terms
    low_grads[:, heads * head : (heads + 1) * head] = back
    low_grads[:, (heads + 1) * head :] = value_total[...].astype(low)

    def normed_grad_rows(whose):
        at_rows = lanes_at(whose, group)

        def normed_grad_lanes(index, carry):
            at = lanes_at(index, 512)
            grads = low_grads[at_rows, :]
            product = (
                nt_dot(grads[:, : heads * head], query_w[at, :])
                + nt_dot(grads[:, heads * head : (heads + 1) * head], key_w[at, :])
                + nt_dot(grads[:, (heads + 1) * head :], value_w[at, :])
            )
            low_all[whose, :, :, at] = product.astype(low).reshape(2, own_rows, 512)
            return carry

        lax.fori_loop(0, width // 512, normed_grad_lanes, 0)

    share_mate.wait_send()
    share_across.wait_send()
    passed.wait_send()
    sums = QuadSum(place, low_all, near, pair, far, quad_send, quad_recv)
    normed_grad_rows(1 - core)
    sums.start()
    normed_grad_rows(core)
    sums.relay()
    out_ring.close()
    moe_own = out_side[level].astype(wide)
    finished_ref[:, :half] = (residual_ref[...] + moe_own).reshape(members, half, width).astype(low)
    out_ring.drain()
    for target in place.ring_targets():
        pl.semaphore_signal(
            free_sem, inc=1, device_id=target, device_id_type=pl.DeviceIdType.MESH
        )

    def weight_grad_rows(index, carry):
        left = normed_ref[:, :, :, lanes_at(index, group)].reshape(rows, group)
        for first in range(0, heads * head, 512):
            grads = tn_dot(left, low_grads[:, first : first + 512]).astype(low)
            out_sums[index, :, first : first + 512] = grads[:own_rows]
            second = heads * head + first
            out_sums[index, :, second : second + 512] = grads[own_rows:]
        narrow_grad[index] = tn_dot(left, low_grads[:, heads * head :]).astype(low)
        return carry

    lax.fori_loop(0, place.chips, weight_grad_rows, 0)
    normed_grad = sums.total()
    tokens = dealt_rows(False)
    factor = lax.rsqrt(jnp.mean(tokens * tokens, axis=-1, keepdims=True) + epsilon)
    scaled = normed_grad * attn_gain[...]
    inner = jnp.mean(scaled * tokens, axis=-1, keepdims=True)
    small_own[0:1, :] = jnp.sum(normed_grad * tokens * factor, axis=0, keepdims=True)
    small_across = remote(
        small_own, small_near, small_send.at[0], small_recv.at[0], place.across
    )
    small_across.start()
    pair_copies[1].start()
    pair_copies[2].start()
    token_grad = residual_grad[...] + factor * (scaled - tokens * (factor * factor) * inner)
    finished_ref[:, half:] = token_grad.reshape(members, half, width).astype(low)

    def deal_copy(offset, sending):
        target, index = place.member(offset if sending else -offset)
        return remote(
            finished_ref.at[index],
            returned_ref.at[place.fsdp if sending else index],
            deal_send.at[offset - 1],
            deal_recv.at[offset - 1],
            target,
        )

    share_lanes = width // members

    def small_copy(offset, sending):
        target, index = place.member(offset if sending else -offset)
        return remote(
            small_pair.at[:, lanes_at(index, share_lanes)],
            small_parts.at[place.fsdp if sending else index],
            small_send.at[offset],
            small_recv.at[offset],
            target,
        )

    def total_copy(offset, sending):
        target, index = place.member(offset if sending else -offset)
        piece = small_ref.at[:, lanes_at(place.fsdp if sending else index, share_lanes)]
        return remote(piece, piece, total_send.at[offset], total_recv.at[offset], target)

    small_across.wait_recv()
    small_pair[...] = small_own[...] + small_near[...]
    for offset in range(1, members):
        small_copy(offset, True).start()
    for offset in range(1, members):
        deal_copy(offset, True).start()
    own_slice = pltpu.make_async_copy(
        finished_ref.at[place.fsdp], returned_ref.at[place.fsdp], keep_sem.at[0]
    )
    own_slice.start()
    pl.semaphore_wait(free_sem, len(place.ring_targets()))
    last_rings = (query_ring, narrow_ring)
    for turn in range(place.levels):
        for ring in last_rings:
            ring.send(ring.target(turn))

    for turn in range(place.levels):
        weight_ring.take_side(weight_ring.target(turn))
        weight_ring.take_chain(weight_ring.target(turn))
    weight_ring.close()
    for ring in last_rings:
        ring.send_joined()

    def swap_with_mate(slot, mine, theirs, here, there):
        kept = pltpu.make_async_copy(mine, here, keep_sem.at[slot])
        sent = remote(theirs, here, swap_send.at[slot], swap_recv.at[slot], place.mate)
        sent.start()
        kept.start()

        def finish():
            kept.wait()
            remote(there, there, swap_send.at[slot], swap_recv.at[slot], place.mate).wait_recv()
            sent.wait_send()

        return finish

    head_rows = out_grad.shape[0]
    finish_out = swap_with_mate(
        1,
        weight_side.at[level, :, lanes_at(core, lanes)],
        weight_side.at[level, :, lanes_at(1 - core, lanes)],
        out_own.at[lanes_at(core, head_rows)],
        out_own.at[lanes_at(1 - core, head_rows)],
    )
    for offset in range(1, members):
        small_copy(offset, False).wait_recv()
    small_parts[place.fsdp] = small_pair[:, lanes_at(place.fsdp, share_lanes)]
    total = small_parts[0]
    for member in range(1, members):
        total += small_parts[member]
    small_ref[:, lanes_at(place.fsdp, share_lanes)] = total
    for offset in range(1, members):
        total_copy(offset, True).start()
    for turn in range(place.levels):
        for ring in last_rings:
            ring.take_side(ring.target(turn))
            ring.take_chain(ring.target(turn))
    own_slice.wait()
    for offset in range(1, members):
        deal_copy(offset, False).wait_recv()
    for index in range(members):
        block = returned_ref[back_ref[index]].astype(wide)
        token_grad_ref[index] = block[half:]
        output_ref[index] = block[:half].astype(low)
    for ring in last_rings:
        ring.close()
    span = heads * head
    finish_query = swap_with_mate(
        2,
        out_side.at[level, :, lanes_at(core, span)],
        out_side.at[level, :, lanes_at(1 - core, span)],
        query_own.at[:, lanes_at(core, span)],
        query_own.at[:, lanes_at(1 - core, span)],
    )
    finish_narrow = swap_with_mate(
        3,
        narrow_side.at[level, lanes_at(core, own_rows)],
        narrow_side.at[level, lanes_at(1 - core, own_rows)],
        key_value_own.at[:, lanes_at(core, 2 * head)],
        key_value_own.at[:, lanes_at(1 - core, 2 * head)],
    )
    finish_out()
    finish_query()
    finish_narrow()
    small_across.wait_send()
    for offset in range(1, members):
        deal_copy(offset, True).wait_send()
        small_copy(offset, True).wait_send()
        total_copy(offset, True).wait_send()
        total_copy(offset, False).wait_recv()
    for copy in pair_copies:
        copy.wait()
    to_mate.wait_send()
    sums.drain()
    for ring in (weight_ring, query_ring, narrow_ring):
        ring.drain()


def attend_back_layer(
    experts,
    entry,
    residual,
    gates,
    dealt,
    back_pick,
    router,
    gain_vecs,
    mixed,
    probs,
    query_low,
    key_low,
    value_low,
    query_pre,
    key_pre,
    tables,
    normed,
    query_w,
    key_w,
    value_w,
    out_w,
    out_part,
    gate_part,
    up_part,
    down_part,
):
    own_rows, width = residual.shape
    members = dealt.shape[0]
    levels = members // 4
    rows = 4 * own_rows
    heads_width, head = query_w.shape[1], key_w.shape[1]
    lanes = width // members
    wide, low = jnp.float32, jnp.bfloat16
    vmem = pl.BlockSpec(memory_space=pltpu.VMEM)
    anywhere = pl.BlockSpec(memory_space=pl.ANY)
    shape = jax.ShapeDtypeStruct
    dma = pltpu.SemaphoreType.DMA
    small = (8 + -(-experts // 8) * 8, width)
    return pl.pallas_call(
        functools.partial(attend_back_kernel, experts),
        name="attend_back_layer",
        out_shape=[
            shape((members, dealt.shape[1] // 2, width), low),
            shape((members, dealt.shape[1] // 2, width), wide),
            shape(small, wide),
            shape((own_rows, 2 * heads_width), low),
            shape((own_rows, 4 * head), low),
            shape((2 * heads_width, lanes), low),
            shape((width, gate_part.shape[1] // 2), low),
            shape((width, up_part.shape[1] // 2), low),
            shape((down_part.shape[0] // 2, width), low),
        ],
        in_specs=[vmem] * 4
        + [pl.BlockSpec(memory_space=pltpu.SMEM)]
        + [vmem] * 19
        + [anywhere] * 4,
        out_specs=[vmem] * 6 + [anywhere] * 3,
        scratch_shapes=[
            pltpu.VMEM(dealt.shape, low),
            pltpu.VMEM(dealt.shape, low),
            pltpu.VMEM(small, wide),
            pltpu.VMEM(small, wide),
            pltpu.VMEM(small, wide),
            pltpu.VMEM((members, small[0], width // members), wide),
            pltpu.VMEM((1, head), wide),
            pltpu.VMEM((own_rows, width), wide),
            pltpu.VMEM((2, 2, own_rows, width), low),
            pltpu.VMEM((rows, heads_width), low),
            pltpu.VMEM((rows, heads_width + 2 * head), low),
            pltpu.VMEM((rows, head), wide),
            pltpu.VMEM((rows, head), wide),
            pltpu.VMEM((heads_width, width), low),
            pltpu.VMEM((members // 2, own_rows, width), low),
            pltpu.VMEM((members // 2, own_rows, width), low),
            *ChainSum.buffers(levels, (own_rows, width)),
            *ChainSum.buffers(levels, (heads_width, 2 * lanes)),
            pltpu.VMEM((members // 2, 2 * own_rows, 2 * head), low),
            *ChainSum.buffers(levels, (2 * own_rows, 2 * head)),
        ]
        + QuadSum.scratch(own_rows, width)
        + [dma((3,)), dma((3,)), dma((4,)), dma((4,)), dma((4,)), dma((3,)), dma((3,))]
        + [dma((members,))] * 6
        + [pltpu.SemaphoreType.REGULAR]
        + ChainSum.semaphores(levels) * 4,
        compiler_params=pltpu.CompilerParams(
            collective_id=3, has_side_effects=True, vmem_limit_bytes=65_400_000
        ),
        cost_estimate=link_cost(185),
    )(
        entry,
        residual,
        gates,
        dealt,
        back_pick,
        router,
        *gain_vecs,
        mixed,
        probs,
        query_low,
        key_low,
        value_low,
        query_pre,
        key_pre,
        *tables,
        normed,
        query_w,
        key_w,
        value_w,
        out_w,
        out_part,
        gate_part,
        up_part,
        down_part,
    )


def fast_body(
    tokens,
    lengths,
    routes,
    deal_order,
    cotangent,
    attn_gain,
    query_gain,
    key_gain,
    moe_gain,
    w_query,
    key_projection_matrix,
    value_projection_matrix,
    w_out,
    w_router,
    w_gate,
    w_up,
    w_down,
):
    own_rows, model_width = tokens.shape
    head_dim = query_gain.shape[0]
    chip_count = lax.axis_size("chip")
    core_count = lax.axis_size("core")
    tp_count = lax.axis_size("tp")
    core_index = lax.axis_index("core")
    tp_index = lax.axis_index("tp")
    fsdp_count = chip_count * core_count
    fsdp_index = lax.axis_index("chip") * core_count + core_index
    slice_rows = own_rows // fsdp_count
    group_rows = tp_count * own_rows
    quad_rows = core_count * group_rows
    plane = ("chip", "core")
    quad = ("core", "tp")
    peer_ids = jnp.arange(fsdp_count, dtype=jnp.int32)
    wanted = (peer_ids - fsdp_index) % fsdp_count
    send_pick = jnp.sum(
        jnp.where(deal_order[None, :] == wanted[:, None], peer_ids[None, :], 0), axis=1
    )
    back_pick = (deal_order + fsdp_index) % fsdp_count

    def slices_of(values):
        return values.reshape(fsdp_count, slice_rows, model_width)

    down_full = lax.all_gather(w_down[0], "tp", axis=0, tiled=True)
    frequency = rope_base ** (-(jnp.arange(head_dim // 2, dtype=jnp.float32) * (2.0 / head_dim)))
    frequency = jnp.concatenate([frequency, frequency])[None, :]
    padded_lengths = jnp.pad(lengths, ((0, 7), (0, 128 - lengths.shape[1])))
    (
        dealt,
        normed,
        upstream_own,
        cosine_wide,
        sine_wide,
        mask,
        query_part,
        key_part,
        value_part,
        out_part,
        gate_full,
        up_full,
    ) = open_layer(
        slices_of(tokens),
        slices_of(cotangent),
        send_pick,
        attn_gain[None, :],
        padded_lengths,
        lengths.shape[1],
        frequency,
        w_query,
        key_projection_matrix,
        value_projection_matrix,
        w_out,
        w_gate[0],
        w_up[0],
    )
    query_part = query_part.reshape(model_width, -1)
    key_part = key_part.reshape(model_width, -1)
    value_part = value_part.reshape(model_width, -1)
    experts = w_router.shape[1]
    router_rows = w_router.T
    (
        upstream_all,
        moe_ext,
        residual,
        gates,
        query_pre,
        query_low,
        key_before_norm,
        key_low,
        value_low,
        probs_low,
        mixed_low,
    ) = attend_layer(
        experts,
        normed,
        query_part,
        key_part,
        value_part,
        out_part,
        (cosine_wide, sine_wide, mask),
        dealt,
        (query_gain[None, :], key_gain[None, :], moe_gain[None, :]),
        router_rows,
        routes,
        upstream_own,
    )
    upstream_all = upstream_all.reshape(fsdp_count * own_rows, model_width)
    entry_ext, moe_out, grad_w_gate, grad_w_up, grad_w_down = expert_layer(
        moe_ext, upstream_all, gate_full, up_full, down_full, experts
    )
    (
        output,
        grad_input,
        small,
        grad_w_query,
        grad_w_narrow,
        grad_w_out,
        gate_arrived,
        up_arrived,
        down_arrived,
    ) = attend_back_layer(
        experts,
        entry_ext,
        residual,
        gates,
        dealt,
        back_pick,
        router_rows,
        (attn_gain[None, :], moe_gain[None, :], query_gain[None, :], key_gain[None, :]),
        mixed_low,
        probs_low,
        query_low,
        key_low,
        value_low,
        query_pre,
        key_before_norm,
        (cosine_wide, sine_wide),
        normed,
        query_part,
        key_part,
        value_part,
        out_part,
        moe_out.reshape(chip_count, core_count, own_rows, model_width),
        grad_w_gate,
        grad_w_up,
        grad_w_down,
    )
    def pair_sum(parts, arrived, dim):
        size = arrived.shape[dim]
        mine = lax.dynamic_slice_in_dim(parts, tp_index * size, size, dim)
        return mine.astype(jnp.float32) + arrived.astype(jnp.float32)

    output = output.reshape(own_rows, model_width)
    grad_input = grad_input.reshape(own_rows, model_width)
    grad_w_router = small[8 : 8 + experts].T
    narrow = grad_w_narrow.astype(jnp.float32).reshape(own_rows, core_count, 2, head_dim)
    grad_w_key, grad_w_value = (
        narrow[:, :, which].reshape(own_rows, core_count * head_dim) for which in range(2)
    )
    return (
        output,
        grad_input,
        small[0],
        small[2, :head_dim],
        small[2, head_dim : 2 * head_dim],
        small[1],
        grad_w_query.astype(jnp.float32),
        grad_w_key,
        grad_w_value,
        grad_w_out.astype(jnp.float32),
        grad_w_router,
        pair_sum(grad_w_gate, gate_arrived, 1)[None],
        pair_sum(grad_w_up, up_arrived, 1)[None],
        pair_sum(grad_w_down, down_arrived, 0)[None],
    )


def solution(mesh):
    fsdp_count, tp_count = mesh.shape["fsdp"], mesh.shape["tp"]
    chips = Mesh(mesh.devices.reshape(fsdp_count // 2, 2, tp_count), ("chip", "core", "tp"))
    dense = fsdp_count <= 16
    fsdp = ("chip", "core") if dense else "fsdp"
    every = ("chip", "core", "tp") if dense else ("fsdp", "tp")
    return jax.shard_map(
        fast_body if dense else body,
        mesh=chips if dense else mesh,
        in_specs=(
            P(every, None),
            P(fsdp, None),
            P(fsdp, None),
            P(),
            P(every, None),
            P(),
            P(),
            P(),
            P(),
            P(fsdp, "tp"),
            P(fsdp, "tp"),
            P(fsdp, "tp"),
            P("tp", fsdp),
            P(),
            P(fsdp, None, "tp"),
            P(fsdp, None, "tp"),
            P(fsdp, "tp", None),
        ),
        out_specs=(
            P(every, None),
            P(every, None),
            P(),
            P(),
            P(),
            P(),
            P(fsdp, "tp"),
            P(fsdp, "tp"),
            P(fsdp, "tp"),
            P("tp", fsdp),
            P(),
            P(fsdp, None, "tp"),
            P(fsdp, None, "tp"),
            P(fsdp, "tp", None),
        ),
        check_vma=False,
    )
```

```python
import functools

import jax
import jax.numpy as jnp
from jax import lax
from jax.experimental import pallas as pl
from jax.experimental.pallas import tpu as pltpu
from jax.sharding import Mesh
from jax.sharding import PartitionSpec as P

epsilon = 1e-06
rope_base = 1000000.0
masked_score = -1e30


def row_norm(values, gain_vec):
    factor = lax.rsqrt(jnp.mean(values * values, axis=-1, keepdims=True) + epsilon)
    return (values * factor * gain_vec, factor)


def norm_back(values, factor, gain_vec, upstream):
    scaled = upstream * gain_vec
    inner_term = jnp.mean(scaled * values, axis=-1, keepdims=True)
    return (factor * (scaled - values * (factor * factor) * inner_term), upstream * values * factor)


def seq_layout(seq_lengths, row_count):
    seq_ends = jnp.cumsum(seq_lengths)
    row_ids = jnp.arange(row_count, dtype=jnp.int32)
    segment = jnp.sum((row_ids[:, None] >= seq_ends[None, :]).astype(jnp.int32), axis=1)
    seq_starts = seq_ends - seq_lengths
    chosen = segment[:, None] == jnp.arange(seq_lengths.shape[0], dtype=jnp.int32)[None, :]
    position = row_ids - jnp.sum(jnp.where(chosen, seq_starts[None, :], 0), axis=1)
    return (segment, position)


def rotary(position, head_width):
    half_width = head_width // 2
    inverse_freq = rope_base ** (-(jnp.arange(half_width, dtype=jnp.float32) * (2.0 / head_width)))
    angles = position.astype(jnp.float32)[:, None] * inverse_freq[None, :]
    return (jnp.cos(angles)[:, None, :], jnp.sin(angles)[:, None, :])


def rotate(values, cosine_table, sine_table):
    half_width = values.shape[-1] // 2
    front_half = values[..., :half_width]
    back_half = values[..., half_width:]
    return jnp.concatenate(
        [
            front_half * cosine_table - back_half * sine_table,
            back_half * cosine_table + front_half * sine_table,
        ],
        axis=-1,
    )


def rotate_back(upstream, cosine_table, sine_table):
    half_width = upstream.shape[-1] // 2
    front_half = upstream[..., :half_width]
    back_half = upstream[..., half_width:]
    return jnp.concatenate(
        [
            front_half * cosine_table + back_half * sine_table,
            back_half * cosine_table - front_half * sine_table,
        ],
        axis=-1,
    )


def slot_table(route_rows, expert_count, capacity):
    row_count = route_rows.shape[0] * route_rows.shape[1]
    flat_routes = route_rows.reshape(row_count)
    expert_hits = (
        flat_routes[:, None] == jnp.arange(expert_count, dtype=jnp.int32)[None, :]
    ).astype(jnp.int32)
    earlier = jnp.cumsum(expert_hits, axis=0) - expert_hits
    slot_index = jnp.sum(earlier * expert_hits, axis=1)
    slot_place = flat_routes * capacity + slot_index
    slot_rows = jnp.full((expert_count * capacity,), row_count, jnp.int32)
    slot_rows = slot_rows.at[slot_place].set(jnp.arange(row_count, dtype=jnp.int32))
    return (slot_place, slot_rows.reshape(expert_count, capacity))


def contract_rows(left, right):
    return lax.dot_general(
        left, right, (((0,), (0,)), ((), ())), preferred_element_type=jnp.float32
    )


def contract_last(left, right):
    return lax.dot_general(
        left, right, (((1,), (1,)), ((), ())), preferred_element_type=jnp.float32
    )


def body(
    tokens,
    lengths,
    routes,
    deal_order,
    cotangent,
    attn_gain,
    query_gain,
    key_gain,
    moe_gain,
    w_query,
    key_projection_matrix,
    value_projection_matrix,
    w_out,
    w_router,
    w_gate,
    w_up,
    w_down,
):
    half_rows = tokens.shape[0]
    model_width = tokens.shape[1]
    head_dim = query_gain.shape[0]
    score_scale = head_dim ** (-0.5)
    fsdp_count = lax.axis_size("fsdp")
    tp_count = lax.axis_size("tp")
    fsdp_index = lax.axis_index("fsdp")
    tp_index = lax.axis_index("tp")
    slice_rows = half_rows // fsdp_count
    group_rows = tp_count * half_rows
    own_start = tp_index * half_rows
    peer_ids = jnp.arange(fsdp_count, dtype=jnp.int32)
    wanted = (peer_ids - fsdp_index) % fsdp_count
    send_pick = jnp.sum(
        jnp.where(deal_order[None, :] == wanted[:, None], peer_ids[None, :], 0), axis=1
    )
    back_pick = (deal_order + fsdp_index) % fsdp_count

    def deal_copies(values):
        slices = jnp.take(values.reshape(fsdp_count, slice_rows, model_width), send_pick, axis=0)
        return jnp.broadcast_to(slices[None], (tp_count, fsdp_count, slice_rows, model_width))

    tokens_all, cotangent_all = (
        lax.all_to_all(
            lax.all_to_all(deal_copies(tokens), "tp", split_axis=0, concat_axis=0, tiled=True),
            "fsdp",
            split_axis=1,
            concat_axis=1,
            tiled=True,
        ),
        lax.all_to_all(
            lax.all_to_all(deal_copies(cotangent), "tp", split_axis=0, concat_axis=0, tiled=True),
            "fsdp",
            split_axis=1,
            concat_axis=1,
            tiled=True,
        ),
    )
    tokens_in = tokens_all.reshape(group_rows, model_width).astype(jnp.float32)
    upstream = cotangent_all.reshape(group_rows, model_width).astype(jnp.float32)
    attn_in, attn_factor = row_norm(tokens_in, attn_gain)
    normed_all = attn_in.astype(jnp.bfloat16)
    query_full, key_full, value_full, out_full = (
        lax.all_gather(w_query, "fsdp", axis=0, tiled=True),
        lax.all_gather(key_projection_matrix, "fsdp", axis=0, tiled=True),
        lax.all_gather(value_projection_matrix, "fsdp", axis=0, tiled=True),
        lax.all_gather(w_out, "fsdp", axis=1, tiled=True),
    )
    query_heads = query_full.shape[1] // head_dim
    kv_heads = key_full.shape[1] // head_dim
    group_size = query_heads // kv_heads
    segment, position = seq_layout(lengths[0], group_rows)
    cosine_table, sine_table = rotary(position, head_dim)
    row_ids = jnp.arange(group_rows)
    allowed = (segment[:, None] == segment[None, :]) & (row_ids[None, :] <= row_ids[:, None])
    query_pre = jnp.dot(normed_all, query_full, preferred_element_type=jnp.float32).reshape(
        group_rows, query_heads, head_dim
    )
    query_normed, query_factor = row_norm(query_pre, query_gain)
    query_low = (
        rotate(query_normed, cosine_table, sine_table)
        .astype(jnp.bfloat16)
        .reshape(group_rows, kv_heads, group_size, head_dim)
    )
    key_before_norm = jnp.dot(normed_all, key_full, preferred_element_type=jnp.float32).reshape(
        group_rows, kv_heads, head_dim
    )
    key_normed, key_factor = row_norm(key_before_norm, key_gain)
    key_low = rotate(key_normed, cosine_table, sine_table).astype(jnp.bfloat16)
    value_low = (
        jnp.dot(normed_all, value_full, preferred_element_type=jnp.float32)
        .astype(jnp.bfloat16)
        .reshape(group_rows, kv_heads, head_dim)
    )
    scores = (
        jnp.einsum("qkgd,tkd->kgqt", query_low, key_low, preferred_element_type=jnp.float32)
        * score_scale
    )
    scores = jnp.where(allowed, scores, masked_score)
    row_peak = jnp.max(scores, axis=-1, keepdims=True)
    exponent = jnp.exp(scores - row_peak)
    totals = jnp.sum(exponent, axis=-1, keepdims=True)
    log_total = row_peak + jnp.log(totals)
    attn_probs = (exponent / totals).astype(jnp.bfloat16)
    attn_mixed = jnp.einsum(
        "kgqt,tkd->qkgd", attn_probs, value_low, preferred_element_type=jnp.float32
    )
    mixed_low = attn_mixed.reshape(group_rows, query_heads * head_dim).astype(jnp.bfloat16)
    attn_part = jnp.dot(mixed_low, out_full, preferred_element_type=jnp.float32)
    residual = tokens_in + lax.psum(attn_part, "tp")
    moe_in, moe_factor = row_norm(residual, moe_gain)
    moe_low = moe_in.astype(jnp.bfloat16)
    logits = jnp.dot(moe_low, w_router, preferred_element_type=jnp.float32)
    experts = w_router.shape[1]
    top_count = routes.shape[1]
    chosen = routes[:, :, None] == jnp.arange(experts, dtype=jnp.int32)[None, None, :]
    selected = jnp.sum(jnp.where(chosen, logits[:, None, :], 0.0), axis=-1)
    gate_peak = jnp.max(selected, axis=-1, keepdims=True)
    gate_exp = jnp.exp(selected - gate_peak)
    gate_probs = gate_exp / jnp.sum(gate_exp, axis=-1, keepdims=True)
    capacity = max(2, 3 * group_rows * top_count // (2 * experts))
    slot_place, slot_rows = slot_table(routes, experts, capacity)
    part_cap = capacity // tp_count
    slot_start = tp_index * part_cap
    gate_full, up_full, down_full = (
        lax.all_gather(w_gate, "tp", axis=2, tiled=True),
        lax.all_gather(w_up, "tp", axis=2, tiled=True),
        lax.all_gather(w_down, "tp", axis=1, tiled=True),
    )
    sent_rows = lax.dynamic_slice_in_dim(slot_rows, slot_start, part_cap, 1)
    slot_expert = slot_place // capacity
    slot_offset = slot_place % capacity - slot_start
    in_half = (slot_offset >= 0) & (slot_offset < part_cap)
    local_place = jnp.where(in_half, slot_expert * part_cap + slot_offset, experts * part_cap)
    padded = jnp.concatenate([moe_low, jnp.zeros((1, model_width), jnp.bfloat16)], axis=0)
    arrived = lax.all_to_all(
        padded[sent_rows // top_count], "fsdp", split_axis=0, concat_axis=0, tiled=True
    )
    local_experts = w_gate.shape[0]
    sources = experts // local_experts
    slot_count = sources * part_cap
    ff_part = w_gate.shape[2]

    def to_experts(values):
        return jnp.transpose(
            values.reshape(sources, local_experts, part_cap, model_width), (1, 0, 2, 3)
        ).reshape(local_experts, slot_count, model_width)

    def to_sources(values):
        width = values.shape[-1]
        return jnp.transpose(
            values.reshape(local_experts, sources, part_cap, width), (1, 0, 2, 3)
        ).reshape(experts, part_cap, width)

    def pick_rows(values):
        flat = values.reshape(experts * part_cap, tp_count * model_width)
        flat = jnp.concatenate([flat, jnp.zeros((1, tp_count * model_width), jnp.bfloat16)], axis=0)
        gathered = flat[local_place].reshape(group_rows, top_count, tp_count, model_width)
        return jnp.sum(gathered.astype(jnp.float32), axis=2)

    expert_rows = to_experts(arrived)
    gate_val = jnp.einsum(
        "esd,edf->esf", expert_rows, gate_full, preferred_element_type=jnp.float32
    )
    up_val = jnp.einsum("esd,edf->esf", expert_rows, up_full, preferred_element_type=jnp.float32)
    sigmoid_val = jax.nn.sigmoid(gate_val)
    swish_val = gate_val * sigmoid_val
    hidden_low = (swish_val * up_val).astype(jnp.bfloat16)
    hidden_blocks = hidden_low.reshape(local_experts, slot_count, tp_count, ff_part)
    down_blocks = down_full.reshape(local_experts, tp_count, ff_part, model_width)
    expert_out = (
        jnp.einsum(
            "esbf,ebfd->esbd", hidden_blocks, down_blocks, preferred_element_type=jnp.float32
        )
        .astype(jnp.bfloat16)
        .reshape(local_experts, slot_count, tp_count * model_width)
    )
    returned = lax.all_to_all(
        to_sources(expert_out), "fsdp", split_axis=0, concat_axis=0, tiled=True
    )
    picked = pick_rows(returned)
    moe_part = jnp.sum(gate_probs[:, :, None] * picked, axis=1)
    gate_grad_part = jnp.sum(upstream[:, None, :] * picked, axis=-1)
    weighted = (
        (gate_probs[:, :, None] * upstream[:, None, :])
        .astype(jnp.bfloat16)
        .reshape(group_rows * top_count, model_width)
    )
    weighted = jnp.concatenate([weighted, jnp.zeros((1, model_width), jnp.bfloat16)], axis=0)
    grad_arrived = lax.all_to_all(
        weighted[sent_rows], "fsdp", split_axis=0, concat_axis=0, tiled=True
    )
    grad_slots = to_experts(grad_arrived)
    hidden_grad = jnp.einsum(
        "esd,ebfd->esbf", grad_slots, down_blocks, preferred_element_type=jnp.float32
    ).reshape(local_experts, slot_count, tp_count * ff_part)
    swish_slope = sigmoid_val * (1.0 + gate_val * (1.0 - sigmoid_val))
    gate_val_grad = (hidden_grad * up_val * swish_slope).astype(jnp.bfloat16)
    up_val_grad = (hidden_grad * swish_val).astype(jnp.bfloat16)
    grad_w_down = jnp.einsum(
        "esbf,esd->ebfd", hidden_blocks, grad_slots, preferred_element_type=jnp.float32
    ).reshape(local_experts, tp_count * ff_part, model_width)
    grad_w_gate = jnp.einsum(
        "esd,esf->edf", expert_rows, gate_val_grad, preferred_element_type=jnp.float32
    )
    grad_w_up = jnp.einsum(
        "esd,esf->edf", expert_rows, up_val_grad, preferred_element_type=jnp.float32
    )
    gate_blocks = gate_full.reshape(local_experts, model_width, tp_count, ff_part)
    up_blocks = up_full.reshape(local_experts, model_width, tp_count, ff_part)
    entry_grad = (
        (
            jnp.einsum(
                "esbf,edbf->esbd",
                gate_val_grad.reshape(local_experts, slot_count, tp_count, ff_part),
                gate_blocks,
                preferred_element_type=jnp.float32,
            )
            + jnp.einsum(
                "esbf,edbf->esbd",
                up_val_grad.reshape(local_experts, slot_count, tp_count, ff_part),
                up_blocks,
                preferred_element_type=jnp.float32,
            )
        )
        .astype(jnp.bfloat16)
        .reshape(local_experts, slot_count, tp_count * model_width)
    )
    sent_back = lax.all_to_all(
        to_sources(entry_grad), "fsdp", split_axis=0, concat_axis=0, tiled=True
    )
    expert_grad = jnp.sum(pick_rows(sent_back), axis=1)
    grad_w_gate, grad_w_up, grad_w_down = (
        lax.psum_scatter(
            grad_w_gate.astype(jnp.bfloat16), "tp", scatter_dimension=2, tiled=True
        ).astype(jnp.float32),
        lax.psum_scatter(
            grad_w_up.astype(jnp.bfloat16), "tp", scatter_dimension=2, tiled=True
        ).astype(jnp.float32),
        lax.psum_scatter(
            grad_w_down.astype(jnp.bfloat16), "tp", scatter_dimension=1, tiled=True
        ).astype(jnp.float32),
    )
    moe_grad, gate_grad = (
        lax.psum(expert_grad.astype(jnp.bfloat16), "tp").astype(jnp.float32),
        lax.psum(gate_grad_part.astype(jnp.bfloat16), "tp").astype(jnp.float32),
    )
    gate_inner = jnp.sum(gate_probs * gate_grad, axis=-1, keepdims=True)
    selected_grad = gate_probs * (gate_grad - gate_inner)
    logit_grad = jnp.sum(jnp.where(chosen, selected_grad[:, :, None], 0.0), axis=1).astype(
        jnp.bfloat16
    )
    moe_grad = moe_grad + contract_last(logit_grad, w_router)
    router_grad = contract_rows(
        lax.dynamic_slice_in_dim(moe_low, own_start, half_rows, 0),
        lax.dynamic_slice_in_dim(logit_grad, own_start, half_rows, 0),
    )
    residual_from_norm, moe_gain_terms = norm_back(residual, moe_factor, moe_gain, moe_grad)
    residual_grad = upstream + residual_from_norm
    moe_gain_grad = jnp.sum(
        lax.dynamic_slice_in_dim(moe_gain_terms, own_start, half_rows, 0), axis=0
    )
    residual_low = residual_grad.astype(jnp.bfloat16)
    mixed_grad = (
        contract_last(residual_low, out_full)
        .astype(jnp.bfloat16)
        .reshape(group_rows, kv_heads, group_size, head_dim)
    )
    grad_w_out = contract_rows(mixed_low, residual_low)
    scores = (
        jnp.einsum("qkgd,tkd->kgqt", query_low, key_low, preferred_element_type=jnp.float32)
        * score_scale
    )
    scores = jnp.where(allowed, scores, masked_score)
    probs_full = jnp.exp(scores - log_total)
    prob_grad = jnp.einsum(
        "qkgd,tkd->kgqt", mixed_grad, value_low, preferred_element_type=jnp.float32
    )
    prob_inner = jnp.sum(probs_full * prob_grad, axis=-1, keepdims=True)
    score_grad = (probs_full * (prob_grad - prob_inner)).astype(jnp.bfloat16)
    query_grad = (
        jnp.einsum(
            "kgqt,tkd->qkgd", score_grad, key_low, preferred_element_type=jnp.float32
        ).reshape(group_rows, query_heads, head_dim)
        * score_scale
    )
    key_grad = (
        jnp.einsum("kgqt,qkgd->tkd", score_grad, query_low, preferred_element_type=jnp.float32)
        * score_scale
    )
    value_grad = (
        jnp.einsum(
            "kgqt,qkgd->tkd",
            probs_full.astype(jnp.bfloat16),
            mixed_grad,
            preferred_element_type=jnp.float32,
        )
        .astype(jnp.bfloat16)
        .reshape(group_rows, kv_heads * head_dim)
    )
    query_pre_grad, query_gain_terms = norm_back(
        query_pre, query_factor, query_gain, rotate_back(query_grad, cosine_table, sine_table)
    )
    key_pre_grad, key_gain_terms = norm_back(
        key_before_norm, key_factor, key_gain, rotate_back(key_grad, cosine_table, sine_table)
    )
    query_pre_low = query_pre_grad.astype(jnp.bfloat16).reshape(group_rows, query_heads * head_dim)
    key_pre_low = key_pre_grad.astype(jnp.bfloat16).reshape(group_rows, kv_heads * head_dim)
    grad_w_query = contract_rows(normed_all, query_pre_low)
    grad_w_key = contract_rows(normed_all, key_pre_low)
    grad_w_value = contract_rows(normed_all, value_grad)
    normed_grad = (
        contract_last(query_pre_low, query_full)
        + contract_last(key_pre_low, key_full)
        + contract_last(value_grad, value_full)
    )
    normed_grad_own, moe_own = (
        lax.psum_scatter(
            normed_grad.astype(jnp.bfloat16), "tp", scatter_dimension=0, tiled=True
        ).astype(jnp.float32),
        lax.psum_scatter(
            moe_part.astype(jnp.bfloat16), "tp", scatter_dimension=0, tiled=True
        ).astype(jnp.float32),
    )
    tokens_own = lax.dynamic_slice_in_dim(tokens_in, own_start, half_rows, 0)
    factor_own = lax.dynamic_slice_in_dim(attn_factor, own_start, half_rows, 0)
    tokens_from_norm, attn_gain_terms = norm_back(
        tokens_own, factor_own, attn_gain, normed_grad_own
    )
    grad_group = lax.dynamic_slice_in_dim(residual_grad, own_start, half_rows, 0) + tokens_from_norm
    residual_own = lax.dynamic_slice_in_dim(residual, own_start, half_rows, 0)
    output_group = (residual_own + moe_own).astype(jnp.bfloat16)
    back_output, back_grad = (
        lax.all_to_all(
            output_group.astype(jnp.float32)
            .reshape(fsdp_count, slice_rows, model_width)
            .astype(jnp.bfloat16),
            "fsdp",
            split_axis=0,
            concat_axis=0,
            tiled=True,
        ).astype(jnp.float32),
        lax.all_to_all(
            grad_group.reshape(fsdp_count, slice_rows, model_width).astype(jnp.bfloat16),
            "fsdp",
            split_axis=0,
            concat_axis=0,
            tiled=True,
        ).astype(jnp.float32),
    )
    output = (
        jnp.take(back_output, back_pick, axis=0)
        .reshape(half_rows, model_width)
        .astype(jnp.bfloat16)
    )
    grad_input = jnp.take(back_grad, back_pick, axis=0).reshape(half_rows, model_width)
    grad_w_query, grad_w_key, grad_w_value, grad_w_out = (
        lax.psum_scatter(grad_w_query, "fsdp", scatter_dimension=0, tiled=True),
        lax.psum_scatter(grad_w_key, "fsdp", scatter_dimension=0, tiled=True),
        lax.psum_scatter(grad_w_value, "fsdp", scatter_dimension=0, tiled=True),
        lax.psum_scatter(grad_w_out, "fsdp", scatter_dimension=1, tiled=True),
    )
    grad_attn_gain, grad_query_gain, grad_key_gain, grad_moe_gain, grad_w_router = lax.psum(
        (
            jnp.sum(attn_gain_terms, axis=0),
            jnp.sum(query_gain_terms, axis=(0, 1)),
            jnp.sum(key_gain_terms, axis=(0, 1)),
            moe_gain_grad,
            router_grad,
        ),
        ("fsdp", "tp"),
    )
    return (
        output,
        grad_input,
        grad_attn_gain,
        grad_query_gain,
        grad_key_gain,
        grad_moe_gain,
        grad_w_query,
        grad_w_key,
        grad_w_value,
        grad_w_out,
        grad_w_router,
        grad_w_gate,
        grad_w_up,
        grad_w_down,
    )


def remote(src, dst, send_sem, recv_sem, target):
    return pltpu.make_async_remote_copy(
        src_ref=src,
        dst_ref=dst,
        send_sem=send_sem,
        recv_sem=recv_sem,
        device_id=target,
        device_id_type=pl.DeviceIdType.MESH,
    )


def greet(targets):
    barrier = pltpu.get_barrier_semaphore()
    for target in targets:
        pl.semaphore_signal(
            barrier, inc=1, device_id=target, device_id_type=pl.DeviceIdType.MESH
        )
    pl.semaphore_wait(barrier, len(targets))


def link_cost(microseconds):
    return pl.CostEstimate(flops=0, bytes_accessed=microseconds * 3_000_000, transcendentals=0)


class Place:
    def __init__(self):
        self.chips = lax.axis_size("chip")
        self.levels = self.chips // 2
        self.chip = lax.axis_index("chip")
        self.core = lax.axis_index("core")
        self.tp = lax.axis_index("tp")
        self.level = self.chip // 2
        self.side = self.chip % 2
        self.fsdp = self.chip * 2 + self.core
        self.mate = {"core": 1 - self.core}
        self.across = {"tp": 1 - self.tp}
        self.beside = {"chip": self.level * 2 + 1 - self.side}
        self.above = {"chip": lax.rem(self.chip + 2, self.chips)}
        self.below = {"chip": lax.rem(self.chip + self.chips - 2, self.chips)}
        top = self.levels - 1
        self.upper = self.level // (self.levels // 2)
        self.end = top * self.upper
        self.next = self.end + 1 - 2 * self.upper
        self.at_end = self.level == self.end
        self.at_next = self.level == self.next
        outward = self.level * 2 + self.side + 4 * self.upper - 2
        inward = self.level * 2 + self.side + 2 - 4 * self.upper
        self.outward = {"chip": lax.rem(outward + self.chips, self.chips)}
        self.inward = {"chip": lax.rem(inward + self.chips, self.chips)}

    def member(self, offset):
        count = 2 * self.chips
        index = lax.rem(self.fsdp + offset + count, count)
        return {"chip": index // 2, "core": lax.rem(index, 2)}, index

    def plane_targets(self):
        return [self.member(offset)[0] for offset in range(1, 2 * self.chips)]

    def ring_targets(self):
        return [self.above, self.below, self.beside]


def lower_half(ref):
    return ref.at[pl.ds(0, ref.shape[0] // 2)]


def upper_half(ref):
    return ref.at[pl.ds(ref.shape[0] // 2, ref.shape[0] // 2)]


class RowGather:
    def __init__(self, place, block, sems, hands=True):
        self.place, self.block, self.hands = place, block, hands
        (
            self.up_send,
            self.up_recv,
            self.down_send,
            self.down_recv,
            self.side_send,
            self.side_recv,
            self.hop_send,
            self.hop_recv,
        ) = sems[:8]
        if hands:
            self.hand_send, self.hand_recv = sems[8:10]

    @staticmethod
    def semaphores(levels, hands=True):
        dma = pltpu.SemaphoreType.DMA
        return [dma((levels,))] * 6 + [dma, dma] + ([dma((2 * levels,))] * 2 if hands else [])

    def climb(self, origin):
        piece, at = self.block(origin, self.place.core), origin // 2
        return remote(piece, piece, self.up_send.at[at], self.up_recv.at[at], self.place.above)

    def sink(self, origin):
        piece, at = self.block(origin, self.place.core), origin // 2
        return remote(piece, piece, self.down_send.at[at], self.down_recv.at[at], self.place.below)

    def cross(self, origin, half=False):
        piece, at = self.block(origin, self.place.core), origin // 2
        if half:
            piece = upper_half(piece)
        return remote(piece, piece, self.side_send.at[at], self.side_recv.at[at], self.place.beside)

    def hop(self, level, inward):
        piece = self.block(level * 2 + 1 - self.place.side, self.place.core)
        if not inward:
            piece = lower_half(piece)
        target = self.place.inward if inward else self.place.outward
        return remote(piece, piece, self.hop_send, self.hop_recv, target)

    def hand(self, origin, whose):
        piece = self.block(origin, whose)
        return remote(
            piece, piece, self.hand_send.at[origin], self.hand_recv.at[origin], self.place.mate
        )

    def pass_on(self, origin):
        place = self.place
        at = origin // 2
        skipped = place.at_next & (at == place.end)
        halved = place.at_end & (at == place.next)

        @pl.when(halved)
        def _():
            self.cross(origin, True).start()

        @pl.when(~skipped & ~halved)
        def _():
            self.cross(origin).start()

        self.give(origin)

    def give(self, origin):
        if self.hands:
            self.hand(origin, self.place.core).start()

    def start(self):
        place = self.place

        @pl.when(place.level < place.levels - 1)
        def _():
            self.climb(place.chip).start()

        @pl.when(place.level > 0)
        def _():
            self.sink(place.chip).start()

        self.pass_on(place.chip)

    def crossed(self, at):
        place = self.place
        origin = at * 2 + 1 - place.side
        skipped = place.at_next & (at == place.end)
        halved = place.at_end & (at == place.next)

        @pl.when(skipped)
        def _():
            self.hop(place.end, True).wait_recv()

        @pl.when(halved)
        def _():
            self.cross(origin, True).wait_recv()

        @pl.when(~skipped & ~halved)
        def _():
            self.cross(origin).wait_recv()

        @pl.when(place.at_end & (at == place.end))
        def _():
            self.hop(place.end, True).start()

        @pl.when(~halved)
        def _():
            self.give(origin)

    def finish(self):
        place = self.place

        @pl.when(place.at_end)
        def _():
            self.hop(place.next, False).wait_recv()
            self.give(place.next * 2 + 1 - place.side)

    def step(self, n):
        place = self.place
        level, side, top = place.level, place.side, place.levels - 1
        under, over = level - n, level + n

        @pl.when((n > 0) & (under >= 0))
        def _():
            origin = under * 2 + side
            self.climb(origin).wait_recv()

            @pl.when(level < top)
            def _():
                self.climb(origin).start()

            self.pass_on(origin)

        @pl.when((n > 0) & (over <= top))
        def _():
            origin = over * 2 + side
            self.sink(origin).wait_recv()

            @pl.when(level > 0)
            def _():
                self.sink(origin).start()

            self.pass_on(origin)

        @pl.when(place.at_next & (n == place.levels - 2))
        def _():
            self.hop(place.next, False).start()

        @pl.when((n > 0) & (under + 1 >= 0))
        def _():
            self.crossed(under + 1)

        @pl.when((n > 1) & (over - 1 <= top))
        def _():
            self.crossed(over - 1)

    def take_hands(self):
        place = self.place

        def taken(origin, carry):
            self.hand(origin, 1 - place.core).wait_recv()
            return carry

        lax.fori_loop(0, place.chips, taken, 0)

    def drain(self):
        place = self.place
        level, side, top = place.level, place.side, place.levels - 1

        def handed(origin, carry):
            self.hand(origin, place.core).wait_send()
            return carry

        if self.hands:
            lax.fori_loop(0, place.chips, handed, 0)

        def sent(at, carry):
            skipped = place.at_next & (at == place.end)
            halved = place.at_end & (at == place.next)

            @pl.when(halved)
            def _():
                self.cross(at * 2 + side, True).wait_send()

            @pl.when(~skipped & ~halved)
            def _():
                self.cross(at * 2 + side).wait_send()

            @pl.when((level < top) & (at <= level))
            def _():
                self.climb(at * 2 + side).wait_send()

            @pl.when((level > 0) & (at >= level))
            def _():
                self.sink(at * 2 + side).wait_send()

            return carry

        lax.fori_loop(0, place.levels, sent, 0)

        @pl.when(place.at_end)
        def _():
            self.hop(place.end, True).wait_send()

        @pl.when(place.at_next)
        def _():
            self.hop(place.next, False).wait_send()


class RowGathers:
    def __init__(self, place, block, sems):
        count = len(sems) // 10
        self.rings = []
        for i in range(count):

            def piece(origin, whose, i=i):
                whole = block(origin, whose)
                rows = whole.shape[0] // count
                return whole.at[pl.ds(i * rows, rows)]

            self.rings.append(RowGather(place, piece, sems[10 * i : 10 * i + 10]))

    @staticmethod
    def semaphores(levels):
        return RowGather.semaphores(levels) * 2

    def start(self):
        for ring in self.rings:
            ring.start()

    def step(self, n):
        for ring in self.rings:
            ring.step(n)

    def finish(self):
        for ring in self.rings:
            ring.finish()

    def take_hand(self, origin, whose):
        for ring in self.rings:
            ring.hand(origin, whose).wait_recv()

    def take_hands(self):
        for ring in self.rings:
            ring.take_hands()

    def drain(self):
        for ring in self.rings:
            ring.drain()


class ChainSum:
    def __init__(self, place, parts, side_buf, chain_buf, hop_buf, sems):
        self.place, self.parts = place, parts
        self.side_buf, self.chain_buf, self.hop_buf = side_buf, chain_buf, hop_buf
        (
            self.up_send,
            self.up_recv,
            self.down_send,
            self.down_recv,
            self.side_send,
            self.side_recv,
            self.hop_send,
            self.hop_recv,
            self.half_send,
            self.half_recv,
        ) = sems

    @staticmethod
    def semaphores(levels):
        dma = pltpu.SemaphoreType.DMA
        return [dma((levels,))] * 6 + [dma] * 4

    @staticmethod
    def buffers(levels, block, dtype=jnp.bfloat16):
        return [
            pltpu.VMEM((levels,) + block, dtype),
            pltpu.VMEM((levels + 1,) + block, dtype),
            pltpu.VMEM(block, dtype),
        ]

    def target(self, turn):
        place = self.place
        top = place.levels - 1
        far, near = top - turn // 2, turn // 2
        odd = turn % 2
        low_half = far * (1 - odd) + near * odd
        high_half = near * (1 - odd) + far * odd
        inner = low_half * (1 - place.upper) + high_half * place.upper
        outer = (top - turn) * (1 - place.upper) + turn * place.upper
        return jnp.where(place.at_end, outer, inner)

    def from_under(self, goal):
        return self.chain_buf.at[goal + 1]

    def from_over(self, goal):
        return self.chain_buf.at[goal]

    def other(self, goal):
        return self.parts(goal * 2 + 1 - self.place.side)

    def cross(self, source, target, goal):
        return remote(
            source, target, self.side_send.at[goal], self.side_recv.at[goal], self.place.beside
        )

    def whole(self, goal):
        return self.cross(self.other(goal), self.side_buf.at[goal], goal)

    def lifted(self, goal):
        return self.cross(self.hop_buf, self.side_buf.at[goal], goal)

    def upper(self, goal):
        return self.cross(upper_half(self.other(goal)), upper_half(self.side_buf.at[goal]), goal)

    def lower(self, goal):
        return remote(
            lower_half(self.hop_buf),
            lower_half(self.side_buf.at[goal]),
            self.half_send,
            self.half_recv,
            self.place.beside,
        )

    def hop_out(self):
        return remote(
            self.other(self.place.end), self.hop_buf, self.hop_send, self.hop_recv, self.place.outward
        )

    def hop_in(self):
        return remote(
            lower_half(self.other(self.place.next)),
            lower_half(self.hop_buf),
            self.hop_send,
            self.hop_recv,
            self.place.inward,
        )

    def up(self, goal):
        return remote(
            self.side_buf.at[goal],
            self.from_under(goal),
            self.up_send.at[goal],
            self.up_recv.at[goal],
            self.place.above,
        )

    def down(self, goal):
        return remote(
            self.side_buf.at[goal],
            self.from_over(goal),
            self.down_send.at[goal],
            self.down_recv.at[goal],
            self.place.below,
        )

    def cases(self, goal):
        place = self.place
        to_end, to_next = goal == place.end, goal == place.next
        return (
            place.at_end & to_end,
            place.at_end & to_next,
            place.at_next & to_end,
            place.at_next & to_next,
        )

    def send(self, goal):
        end_end, end_next, next_end, next_next = self.cases(goal)

        @pl.when(end_next)
        def _():
            self.hop_in().start()

        @pl.when(next_end)
        def _():
            self.hop_out().start()

        @pl.when(end_next | next_next)
        def _():
            self.upper(goal).start()

        @pl.when(~(end_end | end_next | next_end | next_next))
        def _():
            self.whole(goal).start()

    def send_joined(self):
        place, wide = self.place, jnp.float32
        hop = self.hop_buf

        @pl.when(place.at_end)
        def _():
            self.hop_out().wait_recv()
            total = hop[...].astype(wide) + self.other(place.end)[...].astype(wide)
            hop[...] = total.astype(hop.dtype)
            self.lifted(place.end).start()

        @pl.when(place.at_next)
        def _():
            self.hop_in().wait_recv()
            half = hop.shape[0] // 2
            own = lower_half(self.other(place.next))[...].astype(wide)
            hop[:half] = (hop[:half].astype(wide) + own).astype(hop.dtype)
            self.lower(place.next).start()

    def add(self, goal, ref):
        held = self.side_buf
        total = held[goal].astype(jnp.float32) + ref[...].astype(jnp.float32)
        held[goal] = total.astype(held.dtype)

    def take_side(self, goal):
        place = self.place
        level, top = place.level, place.levels - 1
        end_end, end_next, next_end, next_next = self.cases(goal)
        held = self.side_buf
        own = self.parts(goal * 2 + place.side)
        half = held.shape[1] // 2

        @pl.when(end_next)
        def _():
            self.upper(goal).wait_recv()
            total = held[goal, half:].astype(jnp.float32) + upper_half(own)[...].astype(jnp.float32)
            held[goal, half:] = total.astype(held.dtype)
            held[goal, :half] = lower_half(own)[...]

        @pl.when(next_end)
        def _():
            held[goal] = own[...]

        @pl.when(next_next)
        def _():
            self.upper(goal).wait_recv()
            self.lower(goal).wait_recv()

        @pl.when(~(end_next | next_end | next_next))
        def _():
            self.whole(goal).wait_recv()

        @pl.when(~(end_next | next_end))
        def _():
            self.add(goal, own)

        @pl.when((goal > level) & (level == 0))
        def _():
            self.up(goal).start()

        @pl.when((goal < level) & (level == top))
        def _():
            self.down(goal).start()

    def take_chain(self, goal):
        place = self.place
        level, top = place.level, place.levels - 1

        @pl.when((goal > level) & (level > 0))
        def _():
            self.up(goal).wait_recv()
            self.add(goal, self.from_under(goal))
            self.up(goal).start()

        @pl.when((goal < level) & (level < top))
        def _():
            self.down(goal).wait_recv()
            self.add(goal, self.from_over(goal))
            self.down(goal).start()

    def close(self):
        place = self.place
        level, top = place.level, place.levels - 1

        @pl.when(level > 0)
        def _():
            self.up(level).wait_recv()
            self.add(level, self.from_under(level))

        @pl.when(level < top)
        def _():
            self.down(level).wait_recv()
            self.add(level, self.from_over(level))

    def drain(self):
        place = self.place

        def goal_done(goal, carry):
            end_end, end_next, next_end, next_next = self.cases(goal)

            @pl.when(end_end)
            def _():
                self.lifted(goal).wait_send()

            @pl.when(end_next)
            def _():
                self.hop_in().wait_send()

            @pl.when(next_end)
            def _():
                self.hop_out().wait_send()

            @pl.when(next_next)
            def _():
                self.lower(goal).wait_send()

            @pl.when(end_next | next_next)
            def _():
                self.upper(goal).wait_send()

            @pl.when(~(end_end | end_next | next_end | next_next))
            def _():
                self.whole(goal).wait_send()

            @pl.when(goal > place.level)
            def _():
                self.up(goal).wait_send()

            @pl.when(goal < place.level)
            def _():
                self.down(goal).wait_send()

            return carry

        lax.fori_loop(0, place.levels, goal_done, 0)


class QuadSum:
    def __init__(self, place, parts, near, pair, far, send, recv):
        self.place, self.parts = place, parts
        self.near, self.pair, self.far = near, pair, far
        self.send, self.recv = send, recv

    @staticmethod
    def scratch(rows, width):
        low, dma = jnp.bfloat16, pltpu.SemaphoreType.DMA
        return [
            pltpu.VMEM((2, rows, width), low),
            pltpu.VMEM((rows, width), low),
            pltpu.VMEM((rows, width), low),
            dma((3,)),
            dma((3,)),
        ]

    def to_mate(self, half):
        return remote(
            self.parts.at[1 - self.place.core, half],
            self.near.at[half],
            self.send.at[half],
            self.recv.at[half],
            self.place.mate,
        )

    def to_across(self):
        return remote(self.pair, self.far, self.send.at[2], self.recv.at[2], self.place.across)

    def start(self):
        self.to_mate(1 - self.place.tp).start()
        self.to_mate(self.place.tp).start()

    def relay(self):
        core, tp, wide = self.place.core, self.place.tp, jnp.float32
        self.to_mate(1 - tp).wait_recv()
        self.pair[...] = (
            self.parts[core, 1 - tp].astype(wide) + self.near[1 - tp].astype(wide)
        ).astype(jnp.bfloat16)
        self.to_across().start()

    def total(self):
        core, tp, wide = self.place.core, self.place.tp, jnp.float32
        self.to_mate(tp).wait_recv()
        total = self.parts[core, tp].astype(wide) + self.near[tp].astype(wide)
        self.to_across().wait_recv()
        return total + self.far[...].astype(wide)

    def drain(self):
        for half in range(2):
            self.to_mate(half).wait_send()
        self.to_across().wait_send()


def nt_dot(left, right):
    return lax.dot_general(
        left, right, (((1,), (1,)), ((), ())), preferred_element_type=jnp.float32
    )


def tn_dot(left, right):
    return lax.dot_general(
        left, right, (((0,), (0,)), ((), ())), preferred_element_type=jnp.float32
    )


def lanes_at(index, width):
    return pl.ds(pl.multiple_of(index * width, width), width)


def front_kernel(
    sequences,
    experts,
    tokens_ref,
    cotangent_ref,
    pick_ref,
    gain_ref,
    lengths_ref,
    frequency_ref,
    query_gain,
    key_gain,
    moe_gain,
    router_ref,
    routes_ref,
    query_ref,
    key_ref,
    value_ref,
    out_ref,
    gate_ref,
    up_ref,
    dealt_ref,
    normed_ref,
    cosine_ref,
    sine_ref,
    moe_ext,
    residual_ref,
    gates_ref,
    query_pre,
    query_low,
    key_pre,
    key_low,
    value_low,
    probs_ref,
    mixed_ref,
    upstream_all,
    query_all,
    key_all,
    value_all,
    out_all,
    gate_all,
    up_all,
    slices_ref,
    both_lengths_ref,
    mask_ref,
    upstream_own,
    query_w,
    key_w,
    value_w,
    out_w,
    router_rows,
    parts,
    near,
    pair,
    far,
    sum_send,
    sum_recv,
    deal_send,
    deal_recv,
    quad_send,
    quad_recv,
    swap_send,
    swap_recv,
    keep_sem,
    pair_send,
    pair_recv,
    pair_keep,
    load_sem,
    *ring_sems,
):
    place = Place()
    core, chip = place.core, place.chip
    wide, low = jnp.float32, jnp.bfloat16
    own_rows = query_ref.shape[0]
    width = dealt_ref.shape[2]
    quarter = query_all.shape[2]
    narrow = key_all.shape[2]
    head_rows = out_all.shape[0]
    lanes = out_ref.shape[1]
    members = 2 * place.chips
    for index in range(members):
        picked = pick_ref[index]
        both = [ref[picked].astype(jnp.float32) for ref in (tokens_ref, cotangent_ref)]
        slices_ref[index] = jnp.concatenate(both, axis=0).astype(jnp.bfloat16)
    greet(place.plane_targets() + [place.across])

    def deal_copy(offset, sending):
        target, index = place.member(offset if sending else -offset)
        return remote(
            slices_ref.at[index],
            dealt_ref.at[place.fsdp if sending else index],
            deal_send.at[offset - 1],
            deal_recv.at[offset - 1],
            target,
        )

    for offset in range(1, members):
        deal_copy(offset, True).start()

    def rows(who):
        return pl.ds(pl.multiple_of(who * own_rows, own_rows), own_rows)

    def columns(who, width):
        return pl.ds(pl.multiple_of(who * width, width), width)

    def spots(who):
        lane_start = pl.multiple_of((2 * chip + core) * lanes, lanes)
        return [
            (query_ref.at[:, columns(who, quarter)], query_all.at[chip, rows(core)]),
            (key_ref.at[:, columns(who, narrow)], key_all.at[chip, rows(core)]),
            (value_ref.at[:, columns(who, narrow)], value_all.at[chip, rows(core)]),
            (
                out_ref.at[pl.ds(pl.multiple_of(who * head_rows, head_rows), head_rows)],
                out_all.at[:, pl.ds(lane_start, lanes)],
            ),
        ]

    def arrivals():
        lane_start = pl.multiple_of((2 * chip + 1 - core) * lanes, lanes)
        return [
            query_all.at[chip, rows(1 - core)],
            key_all.at[chip, rows(1 - core)],
            value_all.at[chip, rows(1 - core)],
            out_all.at[:, pl.ds(lane_start, lanes)],
        ]

    sends = [
        remote(src, dst, swap_send.at[i], swap_recv.at[i], place.mate)
        for i, (src, dst) in enumerate(spots(1 - core))
    ]
    keeps = [
        pltpu.make_async_copy(src, dst, keep_sem.at[i])
        for i, (src, dst) in enumerate(spots(core))
    ]
    mate_lengths = remote(
        lengths_ref, both_lengths_ref.at[core], swap_send.at[4], swap_recv.at[4], place.mate
    )
    own_lengths = pltpu.make_async_copy(lengths_ref, both_lengths_ref.at[core], keep_sem.at[4])
    own_slice = pltpu.make_async_copy(
        slices_ref.at[place.fsdp], dealt_ref.at[place.fsdp], keep_sem.at[5]
    )
    own_slice.start()
    units = gate_ref.shape[1]

    def halves(who):
        at = pl.ds(pl.multiple_of(who * units, units), units)
        return [gate_all.at[:, at], up_all.at[:, at]]

    shards = (gate_ref, up_ref)
    pair_copies = []
    for i, (src, dst) in enumerate(zip(shards, halves(place.tp))):
        pair_copies.append(
            (
                remote(src, dst, pair_send.at[i], pair_recv.at[i], place.across),
                pltpu.make_async_copy(src, dst, pair_keep.at[i]),
            )
        )
    for i in range(4):
        sends[i].start()
        keeps[i].start()
    mate_lengths.start()
    own_lengths.start()

    out_lanes = 2 * lanes
    views = [
        lambda who, core: query_all.at[who],
        lambda who, core: key_all.at[who],
        lambda who, core: value_all.at[who],
        lambda who, core: out_all.at[:, lanes_at(who, out_lanes)],
    ]
    rings = [
        RowGather(place, view, ring_sems[8 * i : 8 * i + 8], hands=False)
        for i, view in enumerate(views)
    ]
    landed = arrivals()
    upstream_ring = RowGathers(
        place, lambda origin, whose: upstream_all.at[origin, whose], ring_sems[32:]
    )
    for i in range(4):
        keeps[i].wait()
        sends[i].wait_send()
        remote(landed[i], landed[i], swap_send.at[i], swap_recv.at[i], place.mate).wait_recv()
        rings[i].start()

    own_slice.wait()
    for offset in range(1, members):
        deal_copy(offset, False).wait_recv()
    tp = place.tp
    half = slices_ref.shape[1] // 2
    step_rows = 4
    width = dealt_ref.shape[2]
    for start in range(0, members, step_rows):
        block = dealt_ref[start : start + step_rows].astype(jnp.float32)
        span = slice(start * half, (start + step_rows) * half)
        upstream_own[span, :] = (
            block[:, half:].reshape(step_rows * half, block.shape[2]).astype(jnp.bfloat16)
        )
        x = block[:, :half].reshape(step_rows * half, block.shape[2])
        factor = lax.rsqrt(jnp.mean(x * x, axis=-1, keepdims=True) + epsilon)
        normed_ref[core, tp, start * half : (start + step_rows) * half, :] = (
            x * factor * gain_ref[...]
        ).astype(jnp.bfloat16)
    mine = normed_ref.at[core, tp]
    to_mate = remote(mine, mine, quad_send.at[0], quad_recv.at[0], place.mate)
    to_across = remote(mine, mine, quad_send.at[1], quad_recv.at[1], place.across)
    to_across.start()
    to_mate.start()
    for both in pair_copies:
        both[0].start()
        both[1].start()
    keep_upstream = pltpu.make_async_copy(upstream_own, upstream_all.at[chip, core], keep_sem.at[6])
    keep_upstream.start()
    levels = place.levels
    own_lengths.wait()
    mate_lengths.wait_send()
    theirs = both_lengths_ref.at[1 - core]
    remote(theirs, theirs, swap_send.at[4], swap_recv.at[4], place.mate).wait_recv()
    group = mask_ref.shape[1]
    head = cosine_ref.shape[1]
    heads = query_w.shape[2] // head
    across_sign = jnp.where(
        lax.broadcasted_iota(jnp.int32, (group, head), 1) < head // 2, -1.0, 1.0
    )
    for which in range(2):
        ends = []
        for at in range(sequences):
            length = both_lengths_ref[which, 0:1, at : at + 1]
            ends.append(length if at == 0 else ends[-1] + length)

        def segment_start(place_ids):
            start = jnp.zeros_like(place_ids)
            for end in ends:
                start = jnp.where(place_ids >= end, end, start)
            return start

        at_rows = pl.ds(which * group, group)
        row_ids = lax.broadcasted_iota(jnp.int32, (group, head), 0)
        position = (row_ids - segment_start(row_ids)).astype(jnp.float32)
        angles = position * frequency_ref[...]
        cosine_ref[at_rows, :] = jnp.cos(angles)
        sine_ref[at_rows, :] = jnp.sin(angles) * across_sign
        row_ids = lax.broadcasted_iota(jnp.int32, (group, group), 0)
        key_ids = lax.broadcasted_iota(jnp.int32, (group, group), 1)
        allowed = (key_ids <= row_ids) & (key_ids >= segment_start(row_ids))
        mask_ref[which] = jnp.where(allowed, 0.0, masked_score)
    early, late = rings[:3], rings[3]
    for ring in rings:
        ring.step(1)
    other = normed_ref.at[core, 1 - tp]
    remote(other, other, quad_send.at[1], quad_recv.at[1], place.across).wait_recv()
    passed = remote(other, other, quad_send.at[2], quad_recv.at[2], place.mate)
    passed.start()
    keep_upstream.wait()
    for n in range(2, levels):
        for ring in rings:
            ring.step(n)
        if n == 2:
            upstream_ring.start()
    for ring in early:
        ring.step(levels)
        ring.finish()
    loads = [
        pltpu.make_async_copy(src, dst, load_sem.at[i])
        for i, (src, dst) in enumerate(
            ((query_all, query_w), (key_all, key_w), (value_all, value_w), (out_all, out_w))
        )
    ]
    for load in loads[:3]:
        load.start()
    router_rows[...] = jnp.zeros_like(router_rows)
    router_rows[:experts, :] = router_ref[...]
    for slot, piece in ((0, normed_ref.at[1 - core, tp]), (2, normed_ref.at[1 - core, 1 - tp])):
        remote(piece, piece, quad_send.at[slot], quad_recv.at[slot], place.mate).wait_recv()
    for load in loads[:3]:
        load.wait()

    def turned(values, gain_ref):
        factor = lax.rsqrt(jnp.mean(values * values, axis=-1, keepdims=True) + epsilon)
        scaled = values * factor * gain_ref[...]
        return (scaled * cosine_ref[...] + pltpu.roll(scaled, head // 2, 1) * sine_ref[...]).astype(
            low
        )

    x = normed_ref[...].reshape(2 * group, width)

    def project(index, carry):
        both = jnp.dot(
            normed_ref[...].reshape(2 * group, width),
            query_w[:, :, lanes_at(index, 2 * head)].reshape(width, 2 * head),
            preferred_element_type=wide,
        )
        query_pre[:, lanes_at(index, 2 * head)] = both.astype(low)
        for which in range(2):
            one = both[:, which * head : (which + 1) * head]
            query_low[:, lanes_at(2 * index + which, head)] = turned(one, query_gain)
        return carry

    lax.fori_loop(0, heads // 2, project, 0)
    key_values = jnp.dot(x, key_w[...].reshape(width, head), preferred_element_type=wide)
    key_pre[...] = key_values
    key_low[...] = turned(key_values, key_gain)
    value_low[...] = jnp.dot(x, value_w[...].reshape(width, head), preferred_element_type=wide).astype(low)
    late.step(levels)
    late.finish()
    loads[3].start()
    upstream_ring.step(1)
    scale = head ** (-0.5)
    batch = 4

    def attend(index, carry):
        which = index // (heads // batch)
        first = (index % (heads // batch)) * batch
        rows = lanes_at(which, group)
        key = key_low[rows, :]
        value = value_low[rows, :]
        mask = mask_ref[which]
        for offset in range(batch):
            at = lanes_at(first + offset, head)
            scores = nt_dot(query_low[rows, at], key) * scale + mask
            peak = jnp.max(scores, axis=-1, keepdims=True)
            exponent = jnp.exp(scores - peak)
            probs = (exponent * (1.0 / jnp.sum(exponent, axis=-1, keepdims=True))).astype(low)
            probs_ref[which * heads + first + offset] = probs
            mixed_ref[rows, at] = jnp.dot(probs, value, preferred_element_type=wide).astype(low)
        return carry

    lax.fori_loop(0, 2 * heads // batch, attend, 0)
    loads[3].wait()

    def out_rows(whose):
        left = mixed_ref[lanes_at(whose, group), :]

        def out_lanes(index, carry):
            at = lanes_at(index, 512)
            product = jnp.dot(left, out_w[:, at], preferred_element_type=wide).astype(low)
            parts[whose, :, :, at] = product.reshape(2, own_rows, 512)
            return carry

        lax.fori_loop(0, width // 512, out_lanes, 0)

    sums = QuadSum(place, parts, near, pair, far, quad_send, quad_recv)
    sums = QuadSum(place, parts, near, pair, far, sum_send, sum_recv)
    out_rows(1 - core)
    sums.start()
    out_rows(core)
    upstream_ring.step(2)
    sums.relay()
    upstream_ring.step(3)
    total = sums.total()

    def token_rows(start):
        block = dealt_ref[start : start + step_rows].astype(wide)[:, :half]
        return block.reshape(step_rows * half, width)

    tokens = jnp.concatenate(
        [token_rows(start) for start in range(0, members, step_rows)], axis=0
    )
    residual = tokens + total
    residual_ref[...] = residual
    factor = lax.rsqrt(jnp.mean(residual * residual, axis=-1, keepdims=True) + epsilon)
    moe_low = (residual * factor * moe_gain[...]).astype(low)
    moe_ext[:, :width] = moe_low
    logits = nt_dot(moe_low, router_rows[...])
    own_routes = routes_ref[lanes_at(place.tp, own_rows), :]
    lane = lax.broadcasted_iota(jnp.int32, (own_rows, 128), 1)
    chosen = own_routes[:, 0:1] == lane
    for choice in range(1, own_routes.shape[1]):
        chosen |= own_routes[:, choice : choice + 1] == lane
    logits = jnp.where(chosen, logits, masked_score)
    exponent = jnp.exp(logits - jnp.max(logits, axis=-1, keepdims=True))
    exponent = jnp.where(chosen, exponent, 0.0)
    gates = exponent / jnp.sum(exponent, axis=-1, keepdims=True)
    gates_ref[...] = gates
    high = gates.astype(low).astype(wide)
    middle = (gates - high).astype(low).astype(wide)
    rest = gates - high - middle
    moe_ext[:, width:] = (
        high + pltpu.roll(middle, experts, 1) + pltpu.roll(rest, 2 * experts, 1)
    ).astype(low)
    for n in range(4, levels + 1):
        upstream_ring.step(n)
    upstream_ring.finish()
    upstream_ring.take_hands()
    upstream_ring.drain()
    sums.drain()
    for ring in rings:
        ring.drain()
    for offset in range(1, members):
        deal_copy(offset, True).wait_send()
    to_mate.wait_send()
    to_across.wait_send()
    passed.wait_send()
    for i, dst in enumerate(halves(1 - place.tp)):
        pair_copies[i][1].wait()
        pair_copies[i][0].wait_send()
        remote(dst, dst, pair_send.at[i], pair_recv.at[i], place.across).wait_recv()


def front_layer(
    experts,
    sequences,
    tokens,
    cotangent,
    pick,
    gain_vec,
    lengths,
    frequency,
    gain_vecs,
    router,
    routes,
    w_query,
    w_key,
    w_value,
    w_out,
    w_gate,
    w_up,
):
    members, slice_rows, width = tokens.shape
    dealt_shape = (members, 2 * slice_rows, width)
    chips = members // 2
    levels = chips // 2
    own_rows = w_query.shape[0]
    wide, low = jnp.float32, jnp.bfloat16
    vmem = pl.BlockSpec(memory_space=pltpu.VMEM)
    anywhere = pl.BlockSpec(memory_space=pl.ANY)
    dma = pltpu.SemaphoreType.DMA
    shape = jax.ShapeDtypeStruct
    group, head = 2 * own_rows, frequency.shape[1]
    rows, heads_width = 2 * group, w_query.shape[1] // 2
    weights = [(chips, 2 * own_rows, w.shape[1] // 2) for w in (w_query, w_key, w_value)]
    weights.append((w_out.shape[0] // 2, members * w_out.shape[1]))
    return pl.pallas_call(
        functools.partial(front_kernel, sequences, experts),
        name="front_layer",
        out_shape=[
            shape(dealt_shape, low),
            shape((2, 2, own_rows, width), low),
            shape((rows, head), wide),
            shape((rows, head), wide),
            shape((own_rows, width + 128), low),
            shape((own_rows, width), wide),
            shape((own_rows, 128), wide),
            shape((rows, heads_width), low),
            shape((rows, heads_width), low),
            shape((rows, head), wide),
            shape((rows, head), low),
            shape((rows, head), low),
            shape((2 * heads_width // head, group, group), low),
            shape((rows, heads_width), low),
            shape((chips, 2, own_rows, width), low),
        ]
        + [shape(weight, low) for weight in weights]
        + [shape((width, 2 * w_gate.shape[1]), low), shape((width, 2 * w_up.shape[1]), low)],
        in_specs=[vmem] * 2
        + [pl.BlockSpec(memory_space=pltpu.SMEM)]
        + [vmem] * 8
        + [anywhere] * 6,
        out_specs=[vmem] * 14 + [anywhere] * 7,
        scratch_shapes=[
            pltpu.VMEM(dealt_shape, low),
            pltpu.VMEM((2,) + lengths.shape, jnp.int32),
            pltpu.VMEM((2, group, group), wide),
            pltpu.VMEM((own_rows, width), low),
        ]
        + [pltpu.VMEM(weight, low) for weight in weights]
        + [pltpu.VMEM((128, width), low), pltpu.VMEM((2, 2, own_rows, width), low)]
        + QuadSum.scratch(own_rows, width)
        + [
            dma((members - 1,)),
            dma((members - 1,)),
            dma((3,)),
            dma((3,)),
            dma((5,)),
            dma((5,)),
            dma((7,)),
            dma((2,)),
            dma((2,)),
            dma((2,)),
            dma((4,)),
        ]
        + RowGather.semaphores(levels, hands=False) * 4
        + RowGathers.semaphores(levels),
        compiler_params=pltpu.CompilerParams(
            collective_id=0, has_side_effects=True, vmem_limit_bytes=65_400_000
        ),
        cost_estimate=link_cost(170),
    )(
        tokens,
        cotangent,
        pick,
        gain_vec,
        lengths,
        frequency,
        *gain_vecs,
        router,
        routes,
        w_query,
        w_key,
        w_value,
        w_out,
        w_gate,
        w_up,
    )


def expert_kernel(
    experts,
    x_own,
    upstream_ref,
    gate_ref,
    up_ref,
    down_ref,
    entry_own,
    out_part,
    gate_grad_ref,
    up_grad_ref,
    down_grad_ref,
    x_all,
    u_all,
    gate_w,
    up_w,
    down_w,
    hidden,
    gate_val_grad,
    up_val_grad,
    scores,
    sums,
    mate_out,
    mate_in,
    side_buf,
    chain_buf,
    hop_buf,
    staged,
    load_sem,
    store_sem,
    both_sem,
    mate_send,
    mate_recv,
    *ring_sems,
):
    place = Place()
    core, chip, level, side = place.core, place.chip, place.level, place.side
    levels, top = place.levels, place.levels - 1
    rows = x_own.shape[0]
    tile = 2 * rows
    width = upstream_ref.shape[1]
    units = down_ref.shape[0]
    wide = jnp.float32
    low = jnp.bfloat16
    loads = [
        pltpu.make_async_copy(x_own, x_all.at[chip, core], load_sem.at[0]),
        pltpu.make_async_copy(gate_ref, gate_w, load_sem.at[1]),
        pltpu.make_async_copy(up_ref, up_w, load_sem.at[2]),
        pltpu.make_async_copy(down_ref, down_w, load_sem.at[3]),
        pltpu.make_async_copy(upstream_ref, u_all, load_sem.at[4]),
    ]
    for load in loads:
        load.start()
    greet(place.ring_targets() + [place.mate])

    gather = RowGathers(place, lambda origin, whose: x_all.at[origin, whose], ring_sems[:20])
    loads[0].wait()

    gather.start()
    for load in loads[1:]:
        load.wait()

    lane = lax.broadcasted_iota(jnp.int32, (128, 128), 0)
    select = (
        (lane == place.fsdp)
        | (lane == place.fsdp + experts)
        | (lane == place.fsdp + 2 * experts)
    ).astype(low)
    cut = 256
    across_lanes = lax.broadcasted_iota(jnp.int32, (tile, 128), 1)

    def forward_tile(origin):
        x = x_all[origin].reshape(tile, x_all.shape[3])
        gate_lanes = jnp.dot(x[:, width:], select, preferred_element_type=wide)
        gate = jnp.concatenate([gate_lanes] * (cut // 128), axis=1)
        x = x[:, :width]
        start = pl.multiple_of(origin * tile, tile)
        u = u_all[pl.ds(start, tile), :]
        score = jnp.zeros((tile, 1), wide)
        for part in range(units // cut):
            lanes = slice(part * cut, (part + 1) * cut)
            gate_val = jnp.dot(x, gate_w[:, lanes], preferred_element_type=wide)
            up_val = jnp.dot(x, up_w[:, lanes], preferred_element_type=wide)
            back = lax.dot_general(
                u, down_w[lanes, :], (((1,), (1,)), ((), ())), preferred_element_type=wide
            )
            sigmoid = 1.0 / (1.0 + jnp.exp(-gate_val))
            swish = gate_val * sigmoid
            out = (swish * up_val).astype(low).astype(wide)
            score += jnp.sum(out * back, axis=1, keepdims=True)
            back = back * gate
            slope = sigmoid * (1.0 + gate_val * (1.0 - sigmoid))
            hidden[pl.ds(start, tile), lanes] = (out * gate).astype(low)
            gate_val_grad[pl.ds(start, tile), lanes] = (back * up_val * slope).astype(low)
            up_val_grad[pl.ds(start, tile), lanes] = (back * swish).astype(low)
        high = score.astype(low).astype(wide)
        packed = jnp.where(
            across_lanes == place.fsdp,
            high,
            jnp.where(across_lanes == place.fsdp + experts, score - high, 0.0),
        )
        scores[origin] = packed.astype(low)

    def gather_step(n, carry):
        gather.step(n)

        @pl.when(n == levels)
        def _():
            gather.finish()

        def candidate(which, carried):
            upward = which % 2
            facing = which // 2
            distance = n - 1 + facing
            at = level + distance * (2 * upward - 1)
            late = (n == levels) & (facing == 0) & (upward == place.upper) & place.at_end
            early = (n == 2) & (facing == 0) & place.at_end
            at = jnp.where(late, place.next, at)
            origin = at * 2 + side * facing + (1 - side) * (1 - facing)
            inside = (at >= 0) & (at <= top) & (distance >= 0) & ((distance > 0) | (upward == 0))

            @pl.when(inside & ~early)
            def _():
                gather.take_hand(origin, 1 - core)
                forward_tile(origin)

            return carried

        return lax.fori_loop(0, 4, candidate, carry)

    lax.fori_loop(0, levels + 1, gather_step, 0)

    plane_sum = ChainSum(place, lambda chip: sums.at[chip], side_buf, chain_buf, hop_buf, ring_sems[20:])

    def to_mate(goal_chip, slot):
        return remote(
            mate_out.at[slot],
            mate_in.at[goal_chip],
            mate_send.at[slot],
            mate_recv.at[goal_chip],
            place.mate,
        )

    def backward_tile(goal_chip, slot, reuse):
        start = pl.multiple_of(goal_chip * tile, tile)
        own_start = pl.multiple_of(goal_chip * tile + core * rows, rows)
        mate_start = pl.multiple_of(goal_chip * tile + (1 - core) * rows, rows)

        @pl.when(reuse)
        def _():
            to_mate(goal_chip, slot).wait_send()

        grads = gate_val_grad[pl.ds(start, tile), :]
        up_grads = up_val_grad[pl.ds(start, tile), :]
        piece = 512
        for first in range(0, width, piece):
            lanes = slice(first, first + piece)
            whole = lax.dot_general(
                grads, gate_w[lanes, :], (((1,), (1,)), ((), ())), preferred_element_type=wide
            ) + lax.dot_general(
                up_grads, up_w[lanes, :], (((1,), (1,)), ((), ())), preferred_element_type=wide
            )
            halves = whole.astype(low).reshape(2, rows, piece)
            sums[goal_chip, :, lanes] = jnp.where(core == 0, halves[0], halves[1])
            mate_out[slot, :, lanes] = jnp.where(core == 0, halves[1], halves[0])
        sums[goal_chip, :, width:] = scores[goal_chip, pl.ds(pl.multiple_of(core * rows, rows), rows)]
        mate_out[slot, :, width:] = scores[
            goal_chip, pl.ds(pl.multiple_of((1 - core) * rows, rows), rows)
        ]
        to_mate(goal_chip, slot).start()

    def joined(goal_chip, slot):
        to_mate(goal_chip, slot).wait_recv()
        sums[goal_chip] = (
            sums[goal_chip].astype(wide) + mate_in[goal_chip].astype(wide)
        ).astype(low)

    def backward_turn(turn, carry):
        goal = plane_sum.target(turn)
        backward_tile(goal * 2 + 1 - side, 0, turn > 0)
        backward_tile(goal * 2 + side, 1, turn > 0)
        joined(goal * 2 + 1 - side, 0)
        plane_sum.send(goal)
        joined(goal * 2 + side, 1)
        return carry

    lax.fori_loop(0, levels, backward_turn, 0)
    plane_sum.send_joined()

    def store(target, start, slot):
        return pltpu.make_async_copy(
            staged.at[slot], target.at[pl.ds(start, tile)], store_sem.at[slot]
        )

    def output_tile(origin, carry):
        start = pl.multiple_of(origin * tile, tile)
        slot = origin % 2

        @pl.when(origin > 1)
        def _():
            store(out_part, start, slot).wait()

        left = hidden[pl.ds(start, tile), :]
        for first in range(0, width, 512):
            lanes = slice(first, first + 512)
            staged[slot, :, lanes] = jnp.dot(
                left, down_w[:, lanes], preferred_element_type=wide
            ).astype(low)
        store(out_part, start, slot).start()
        return carry

    def down_grads(index, carry):
        start = pl.multiple_of(index * tile, tile)
        slot = index % 2
        store(down_grad_ref, start, slot).wait()
        left = hidden[:, pl.ds(start, tile)]
        for first in range(0, width, 512):
            lanes = slice(first, first + 512)
            staged[slot, :, lanes] = lax.dot_general(
                left, u_all[:, lanes], (((0,), (0,)), ((), ())), preferred_element_type=wide
            ).astype(low)
        store(down_grad_ref, start, slot).start()
        return carry

    def store_both(index):
        slot = index % 2
        start = pl.multiple_of(index * tile, tile)
        return [
            pltpu.make_async_copy(
                staged.at[slot, :, i * units : (i + 1) * units],
                target.at[pl.ds(start, tile)],
                both_sem.at[slot, i],
            )
            for i, target in enumerate((gate_grad_ref, up_grad_ref))
        ]

    def entry_weight_grads(index, carry):
        slot = index % 2

        @pl.when(index > 1)
        def _():
            for copy in store_both(index):
                copy.wait()

        left = x_all[:, :, :, pl.ds(pl.multiple_of(index * tile, tile), tile)]
        left = left.reshape(u_all.shape[0], tile)
        for i, right in enumerate((gate_val_grad, up_val_grad)):
            staged[slot, :, i * units : (i + 1) * units] = lax.dot_general(
                left, right[...], (((0,), (0,)), ((), ())), preferred_element_type=wide
            ).astype(low)
        for copy in store_both(index):
            copy.start()
        return carry

    plane_sum.take_side(plane_sum.target(0))
    lax.fori_loop(0, place.chips, output_tile, 0)
    plane_sum.take_chain(plane_sum.target(0))
    plane_sum.take_side(plane_sum.target(1))
    lax.fori_loop(0, units // tile, down_grads, 0)
    for slot in range(2):
        store(down_grad_ref, 0, slot).wait()
    plane_sum.take_chain(plane_sum.target(1))
    plane_sum.take_side(plane_sum.target(2))
    chunks = width // tile
    lax.fori_loop(0, chunks // 2, entry_weight_grads, 0)
    plane_sum.take_chain(plane_sum.target(2))
    plane_sum.take_side(plane_sum.target(3))
    lax.fori_loop(chunks // 2, chunks, entry_weight_grads, 0)
    plane_sum.take_chain(plane_sum.target(3))
    plane_sum.close()
    entry_own[...] = side_buf[level]
    for slot in range(2):
        for copy in store_both(slot):
            copy.wait()
        to_mate(0, slot).wait_send()
    plane_sum.drain()

    gather.drain()


def expert_layer(x_own, upstream_all, gate_all, up_all, down_all, experts):
    rows, span = x_own.shape
    total, width = upstream_all.shape
    units = down_all.shape[0]
    chips = total // (2 * rows)
    levels = chips // 2
    low = jnp.bfloat16
    vmem = pl.BlockSpec(memory_space=pltpu.VMEM)
    anywhere = pl.BlockSpec(memory_space=pl.ANY)
    dma = pltpu.SemaphoreType.DMA
    return pl.pallas_call(
        functools.partial(expert_kernel, experts),
        name="expert_layer",
        out_shape=[
            jax.ShapeDtypeStruct((rows, span), low),
            jax.ShapeDtypeStruct((total, width), low),
            jax.ShapeDtypeStruct((width, units), low),
            jax.ShapeDtypeStruct((width, units), low),
            jax.ShapeDtypeStruct((units, width), low),
        ],
        in_specs=[vmem] + [anywhere] * 4,
        out_specs=[vmem] + [anywhere] * 4,
        scratch_shapes=[
            pltpu.VMEM((chips, 2, rows, span), low),
            pltpu.VMEM((total, width), low),
            pltpu.VMEM((width, units), low),
            pltpu.VMEM((width, units), low),
            pltpu.VMEM((units, width), low),
            pltpu.VMEM((total, units), low),
            pltpu.VMEM((total, units), low),
            pltpu.VMEM((total, units), low),
            pltpu.VMEM((chips, 2 * rows, 128), low),
            pltpu.VMEM((chips, rows, span), low),
            pltpu.VMEM((2, rows, span), low),
            pltpu.VMEM((chips, rows, span), low),
            *ChainSum.buffers(levels, (rows, span)),
            pltpu.VMEM((2, 2 * rows, width), low),
            dma((5,)),
            dma((2,)),
            dma((2, 2)),
        ]
        + [dma((2,)), dma((chips,))]
        + RowGathers.semaphores(levels)
        + ChainSum.semaphores(levels),
        compiler_params=pltpu.CompilerParams(
            collective_id=5, has_side_effects=True, vmem_limit_bytes=65_400_000
        ),
        cost_estimate=link_cost(125),
    )(x_own, upstream_all, gate_all, up_all, down_all)


def attend_back_kernel(
    experts,
    entry_ref,
    residual_ref,
    gates_ref,
    dealt_ref,
    back_ref,
    router_ref,
    attn_gain,
    moe_gain,
    query_gain,
    key_gain,
    key_low,
    value_low,
    key_pre,
    cosine_ref,
    sine_ref,
    mixed_far,
    out_far,
    probs_far,
    query_low_far,
    query_pre_far,
    query_far,
    key_far,
    value_far,
    normed_far,
    out_part,
    gate_part,
    up_part,
    down_part,
    output_ref,
    token_grad_ref,
    small_ref,
    query_own,
    key_own,
    value_own,
    out_own,
    gate_arrived,
    up_arrived,
    down_arrived,
    finished_ref,
    returned_ref,
    small_own,
    small_near,
    small_pair,
    small_parts,
    query_gain_part,
    mixed_ref,
    out_w,
    probs_ref,
    query_low,
    query_pre,
    query_w,
    key_w,
    value_w,
    normed_ref,
    residual_grad,
    low_all,
    mixed_grad,
    low_grads,
    key_total,
    value_total,
    out_grad,
    out_sums,
    out_mate,
    out_side,
    out_chain,
    out_hop,
    weight_side,
    weight_chain,
    weight_hop,
    narrow_grad,
    narrow_side,
    narrow_chain,
    narrow_hop,
    near,
    pair,
    far,
    quad_send,
    quad_recv,
    share_send,
    share_recv,
    swap_send,
    swap_recv,
    keep_sem,
    pair_send,
    pair_recv,
    deal_send,
    deal_recv,
    small_send,
    small_recv,
    total_send,
    total_recv,
    free_sem,
    load_sem,
    join_send,
    join_recv,
    *ring_sems,
):
    place = Place()
    core, tp, level = place.core, place.tp, place.level
    wide, low = jnp.float32, jnp.bfloat16
    own_rows, width = residual_ref.shape
    group = 2 * own_rows
    rows = 2 * group
    head = query_gain.shape[1]
    heads = mixed_grad.shape[1] // head
    members = dealt_ref.shape[0]
    half = dealt_ref.shape[1] // 2
    step_rows = 4
    scale = head ** (-0.5)

    def dealt_rows(second):
        blocks = []
        for start in range(0, members, step_rows):
            block = dealt_ref[start : start + step_rows].astype(wide)
            block = block[:, half:] if second else block[:, :half]
            blocks.append(block.reshape(step_rows * half, width))
        return jnp.concatenate(blocks, axis=0)

    greet(place.plane_targets() + [place.across])

    def to_mate(origin):
        return remote(
            out_part.at[origin, 1 - core],
            out_mate.at[origin],
            join_send.at[origin],
            join_recv.at[origin],
            place.mate,
        )

    out_ring = ChainSum(
        place, lambda chip: out_sums.at[chip], out_side, out_chain, out_hop, ring_sems[:10]
    )

    def joined_at(turn):
        goal = out_ring.target(turn)
        return (goal * 2 + 1 - place.side, goal * 2 + place.side)

    def offer(turn, carry):
        for origin in joined_at(turn):
            to_mate(origin).start()
        return carry

    keep = pltpu.make_async_copy(out_part.at[:, core], out_sums, keep_sem.at[0])
    keep.start()
    lax.fori_loop(0, place.levels, offer, 0)
    loads = [
        pltpu.make_async_copy(src, dst, load_sem.at[i])
        for i, (src, dst) in enumerate(
            (
                (mixed_far, mixed_ref),
                (out_far, out_w),
                (probs_far, probs_ref),
                (query_low_far, query_low),
                (query_pre_far, query_pre),
                (query_far, query_w),
                (key_far, key_w),
                (value_far, value_w),
                (normed_far, normed_ref),
            )
        )
    ]
    for load in loads:
        load.start()

    def join(turn, carry):
        for origin in joined_at(turn):
            to_mate(origin).wait_recv()
            out_sums[origin] = (
                out_sums[origin].astype(wide) + out_mate[origin].astype(wide)
            ).astype(low)
        out_ring.send(out_ring.target(turn))
        return carry

    keep.wait()
    join(0, 0)

    entry = entry_ref[:, :width].astype(wide)
    extra = entry_ref[:, width:].astype(wide)
    gates = gates_ref[...]
    gate_grad = extra + pltpu.roll(extra, 128 - experts, 1)
    inner = jnp.sum(gates * gate_grad, axis=-1, keepdims=True)
    logit_grad = (gates * (gate_grad - inner)).astype(low)
    residual = residual_ref[...]
    factor = lax.rsqrt(jnp.mean(residual * residual, axis=-1, keepdims=True) + epsilon)
    moe_low = (residual * factor * moe_gain[...]).astype(low)
    router = jnp.concatenate(
        [router_ref[...], jnp.zeros((128 - experts, width), low)], axis=0
    )
    moe_grad = entry + jnp.dot(logit_grad, router, preferred_element_type=wide)
    small_own[:8, :] = jnp.zeros((8, width), wide)
    small_own[8:, :] = tn_dot(logit_grad, moe_low)[: small_own.shape[0] - 8]
    scaled = moe_grad * moe_gain[...]
    inner = jnp.mean(scaled * residual, axis=-1, keepdims=True)
    small_own[1:2, :] = jnp.sum(moe_grad * residual * factor, axis=0, keepdims=True)
    residual_grad[...] = dealt_rows(True) + factor * (
        scaled - residual * (factor * factor) * inner
    )
    low_all[core, tp] = residual_grad[...].astype(low)
    mine = low_all.at[core, tp]
    share_mate = remote(mine, mine, share_send.at[0], share_recv.at[0], place.mate)
    share_across = remote(mine, mine, share_send.at[1], share_recv.at[1], place.across)
    share_across.start()
    share_mate.start()
    units = gate_arrived.shape[1]
    pair_copies = [
        remote(
            part.at[:, lanes_at(1 - tp, units)],
            arrived,
            pair_send.at[i],
            pair_recv.at[i],
            place.across,
        )
        for i, (part, arrived) in enumerate(((gate_part, gate_arrived), (up_part, up_arrived)))
    ]
    pair_copies.append(
        remote(
            down_part.at[lanes_at(1 - tp, units)],
            down_arrived,
            pair_send.at[2],
            pair_recv.at[2],
            place.across,
        )
    )
    pair_copies[0].start()

    lanes = out_own.shape[1]
    weight_ring = ChainSum(
        place,
        lambda chip: out_grad.at[:, lanes_at(chip, 2 * lanes)],
        weight_side,
        weight_chain,
        weight_hop,
        ring_sems[10:20],
    )
    query_ring = ChainSum(
        place, lambda chip: out_sums.at[chip], out_side, out_chain, out_hop, ring_sems[20:30]
    )
    narrow_ring = ChainSum(
        place,
        lambda chip: narrow_grad.at[chip],
        narrow_side,
        narrow_chain,
        narrow_hop,
        ring_sems[30:],
    )
    lax.fori_loop(1, place.levels, join, 0)
    out_ring.send_joined()
    other = low_all.at[core, 1 - tp]
    remote(other, other, share_send.at[1], share_recv.at[1], place.across).wait_recv()
    passed = remote(other, other, share_send.at[2], share_recv.at[2], place.mate)
    passed.start()
    for slot, piece in ((0, low_all.at[1 - core, tp]), (2, low_all.at[1 - core, 1 - tp])):
        remote(piece, piece, share_send.at[slot], share_recv.at[slot], place.mate).wait_recv()

    def out_grad_rows(index, carry):
        at = lanes_at(index, 256)
        left = mixed_ref[:, at]
        for first in range(0, width, 512):
            out_grad[at, first : first + 512] = tn_dot(
                left, low_all[:, :, :, first : first + 512].reshape(rows, 512)
            ).astype(low)
        return carry

    loads[0].wait()
    lax.fori_loop(0, mixed_ref.shape[1] // 256, out_grad_rows, 0)
    for turn in range(place.levels):
        weight_ring.send(weight_ring.target(turn))

    def mixed_lanes(index, carry):
        at = lanes_at(index, 256)
        mixed_grad[:, at] = nt_dot(low_all[...].reshape(rows, width), out_w[at, :]).astype(low)
        return carry

    loads[1].wait()
    lax.fori_loop(0, mixed_ref.shape[1] // 256, mixed_lanes, 0)
    for load in loads[2:]:
        load.wait()
    key_total[...] = jnp.zeros_like(key_total)
    value_total[...] = jnp.zeros_like(value_total)
    query_gain_part[...] = jnp.zeros_like(query_gain_part)

    def pre_back(grad, values, gain_ref, cosine, sine):
        grad = grad * cosine - pltpu.roll(grad, head // 2, 1) * sine
        factor = lax.rsqrt(jnp.mean(values * values, axis=-1, keepdims=True) + epsilon)
        scaled = grad * gain_ref[...]
        inner = jnp.mean(scaled * values, axis=-1, keepdims=True)
        back = factor * (scaled - values * (factor * factor) * inner)
        return back.astype(low), jnp.sum(grad * values * factor, axis=0, keepdims=True)

    batch = 4

    def attend_back(index, carry):
        which = index // (heads // batch)
        first = (index % (heads // batch)) * batch
        at_rows = lanes_at(which, group)
        key = key_low[at_rows, :]
        value = value_low[at_rows, :]
        cosine, sine = cosine_ref[at_rows, :], sine_ref[at_rows, :]
        key_sum = key_total[at_rows, :]
        value_sum = value_total[at_rows, :]
        gain_sum = query_gain_part[...]
        for offset in range(batch):
            at = lanes_at(first + offset, head)
            probs = probs_ref[which * heads + first + offset]
            grads = mixed_grad[at_rows, at]
            prob_grad = nt_dot(grads, value)
            probs_wide = probs.astype(wide)
            inner = jnp.sum(probs_wide * prob_grad, axis=-1, keepdims=True)
            score_grad = (probs_wide * (prob_grad - inner)).astype(low)
            query = jnp.dot(score_grad, key, preferred_element_type=wide) * scale
            key_sum += tn_dot(score_grad, query_low[at_rows, at])
            value_sum += tn_dot(probs, grads)
            values = query_pre[at_rows, at].astype(wide)
            back, terms = pre_back(query, values, query_gain, cosine, sine)
            low_grads[at_rows, at] = back
            gain_sum += terms
        key_total[at_rows, :] = key_sum
        value_total[at_rows, :] = value_sum
        query_gain_part[...] = gain_sum
        return carry

    count = 2 * heads // batch
    share = -(-count // place.levels)
    for turn in range(place.levels):
        out_ring.take_side(out_ring.target(turn))
        lax.fori_loop(min(turn * share, count), min((turn + 1) * share, count), attend_back, 0)
        out_ring.take_chain(out_ring.target(turn))

    weight_ring.send_joined()
    back, terms = pre_back(
        key_total[...] * scale, key_pre[...], key_gain, cosine_ref[...], sine_ref[...]
    )
    small_own[2:3, :head] = query_gain_part[...]
    small_own[2:3, head : 2 * head] = terms
    low_grads[:, heads * head : (heads + 1) * head] = back
    low_grads[:, (heads + 1) * head :] = value_total[...].astype(low)

    def normed_grad_rows(whose):
        at_rows = lanes_at(whose, group)

        def normed_grad_lanes(index, carry):
            at = lanes_at(index, 512)
            grads = low_grads[at_rows, :]
            product = (
                nt_dot(grads[:, : heads * head], query_w[at, :])
                + nt_dot(grads[:, heads * head : (heads + 1) * head], key_w[at, :])
                + nt_dot(grads[:, (heads + 1) * head :], value_w[at, :])
            )
            low_all[whose, :, :, at] = product.astype(low).reshape(2, own_rows, 512)
            return carry

        lax.fori_loop(0, width // 512, normed_grad_lanes, 0)

    share_mate.wait_send()
    share_across.wait_send()
    passed.wait_send()
    sums = QuadSum(place, low_all, near, pair, far, quad_send, quad_recv)
    normed_grad_rows(1 - core)
    sums.start()
    normed_grad_rows(core)
    sums.relay()
    out_ring.close()
    moe_own = out_side[level].astype(wide)
    finished_ref[:, :half] = (residual_ref[...] + moe_own).reshape(members, half, width).astype(low)
    out_ring.drain()
    for target in place.ring_targets():
        pl.semaphore_signal(
            free_sem, inc=1, device_id=target, device_id_type=pl.DeviceIdType.MESH
        )

    def weight_grad_rows(index, carry):
        left = normed_ref[:, :, :, lanes_at(index, group)].reshape(rows, group)
        for first in range(0, heads * head, 512):
            grads = tn_dot(left, low_grads[:, first : first + 512]).astype(low)
            out_sums[index, :, first : first + 512] = grads[:own_rows]
            second = heads * head + first
            out_sums[index, :, second : second + 512] = grads[own_rows:]
        narrow_grad[index] = tn_dot(left, low_grads[:, heads * head :]).astype(low)
        return carry

    lax.fori_loop(0, place.chips, weight_grad_rows, 0)
    normed_grad = sums.total()
    tokens = dealt_rows(False)
    factor = lax.rsqrt(jnp.mean(tokens * tokens, axis=-1, keepdims=True) + epsilon)
    scaled = normed_grad * attn_gain[...]
    inner = jnp.mean(scaled * tokens, axis=-1, keepdims=True)
    small_own[0:1, :] = jnp.sum(normed_grad * tokens * factor, axis=0, keepdims=True)
    small_across = remote(
        small_own, small_near, small_send.at[0], small_recv.at[0], place.across
    )
    small_across.start()
    pair_copies[1].start()
    pair_copies[2].start()
    token_grad = residual_grad[...] + factor * (scaled - tokens * (factor * factor) * inner)
    finished_ref[:, half:] = token_grad.reshape(members, half, width).astype(low)

    def deal_copy(offset, sending):
        target, index = place.member(offset if sending else -offset)
        return remote(
            finished_ref.at[index],
            returned_ref.at[place.fsdp if sending else index],
            deal_send.at[offset - 1],
            deal_recv.at[offset - 1],
            target,
        )

    share_lanes = width // members

    def small_copy(offset, sending):
        target, index = place.member(offset if sending else -offset)
        return remote(
            small_pair.at[:, lanes_at(index, share_lanes)],
            small_parts.at[place.fsdp if sending else index],
            small_send.at[offset],
            small_recv.at[offset],
            target,
        )

    def total_copy(offset, sending):
        target, index = place.member(offset if sending else -offset)
        piece = small_ref.at[:, lanes_at(place.fsdp if sending else index, share_lanes)]
        return remote(piece, piece, total_send.at[offset], total_recv.at[offset], target)

    small_across.wait_recv()
    small_pair[...] = small_own[...] + small_near[...]
    for offset in range(1, members):
        small_copy(offset, True).start()
    for offset in range(1, members):
        deal_copy(offset, True).start()
    own_slice = pltpu.make_async_copy(
        finished_ref.at[place.fsdp], returned_ref.at[place.fsdp], keep_sem.at[0]
    )
    own_slice.start()
    pl.semaphore_wait(free_sem, len(place.ring_targets()))
    last_rings = (query_ring, narrow_ring)
    for turn in range(place.levels):
        for ring in last_rings:
            ring.send(ring.target(turn))

    for turn in range(place.levels):
        weight_ring.take_side(weight_ring.target(turn))
        weight_ring.take_chain(weight_ring.target(turn))
    weight_ring.close()
    for ring in last_rings:
        ring.send_joined()

    def swap_with_mate(slot, mine, theirs, here, there):
        kept = pltpu.make_async_copy(mine, here, keep_sem.at[slot])
        sent = remote(theirs, here, swap_send.at[slot], swap_recv.at[slot], place.mate)
        sent.start()
        kept.start()

        def finish():
            kept.wait()
            remote(there, there, swap_send.at[slot], swap_recv.at[slot], place.mate).wait_recv()
            sent.wait_send()

        return finish

    head_rows = out_grad.shape[0]
    finish_out = swap_with_mate(
        1,
        weight_side.at[level, :, lanes_at(core, lanes)],
        weight_side.at[level, :, lanes_at(1 - core, lanes)],
        out_own.at[lanes_at(core, head_rows)],
        out_own.at[lanes_at(1 - core, head_rows)],
    )
    for offset in range(1, members):
        small_copy(offset, False).wait_recv()
    small_parts[place.fsdp] = small_pair[:, lanes_at(place.fsdp, share_lanes)]
    total = small_parts[0]
    for member in range(1, members):
        total += small_parts[member]
    small_ref[:, lanes_at(place.fsdp, share_lanes)] = total
    for offset in range(1, members):
        total_copy(offset, True).start()
    for turn in range(place.levels):
        for ring in last_rings:
            ring.take_side(ring.target(turn))
            ring.take_chain(ring.target(turn))
    own_slice.wait()
    for offset in range(1, members):
        deal_copy(offset, False).wait_recv()
    for index in range(members):
        block = returned_ref[back_ref[index]].astype(wide)
        token_grad_ref[index] = block[half:]
        output_ref[index] = block[:half].astype(low)
    for ring in last_rings:
        ring.close()
    span = heads * head
    finish_query = swap_with_mate(
        2,
        out_side.at[level, :, lanes_at(core, span)],
        out_side.at[level, :, lanes_at(1 - core, span)],
        query_own.at[:, lanes_at(core, span)],
        query_own.at[:, lanes_at(1 - core, span)],
    )
    finish_narrow = [
        swap_with_mate(
            3 + i,
            narrow_side.at[level, lanes_at(core, own_rows), pl.ds(i * head, head)],
            narrow_side.at[level, lanes_at(1 - core, own_rows), pl.ds(i * head, head)],
            own.at[:, lanes_at(core, head)],
            own.at[:, lanes_at(1 - core, head)],
        )
        for i, own in enumerate((key_own, value_own))
    ]
    finish_out()
    finish_query()
    for finish in finish_narrow:
        finish()
    small_across.wait_send()
    for offset in range(1, members):
        deal_copy(offset, True).wait_send()
        small_copy(offset, True).wait_send()
        total_copy(offset, True).wait_send()
        total_copy(offset, False).wait_recv()
    for copy in pair_copies:
        copy.wait()

    def offered(origin, carry):
        to_mate(origin).wait_send()
        return carry

    lax.fori_loop(0, place.chips, offered, 0)
    sums.drain()
    for ring in (weight_ring, query_ring, narrow_ring):
        ring.drain()


def attend_back_layer(
    experts,
    entry,
    residual,
    gates,
    dealt,
    back_pick,
    router,
    gain_vecs,
    mixed,
    probs,
    query_low,
    key_low,
    value_low,
    query_pre,
    key_pre,
    tables,
    normed,
    query_w,
    key_w,
    value_w,
    out_w,
    out_part,
    gate_part,
    up_part,
    down_part,
):
    own_rows, width = residual.shape
    members = dealt.shape[0]
    levels = members // 4
    rows = 4 * own_rows
    heads_width, head = query_w.shape[1], key_w.shape[1]
    lanes = width // members
    wide, low = jnp.float32, jnp.bfloat16
    vmem = pl.BlockSpec(memory_space=pltpu.VMEM)
    anywhere = pl.BlockSpec(memory_space=pl.ANY)
    shape = jax.ShapeDtypeStruct
    dma = pltpu.SemaphoreType.DMA
    small = (8 + -(-experts // 8) * 8, width)
    late = (mixed, out_w, probs, query_low, query_pre, query_w, key_w, value_w, normed)
    return pl.pallas_call(
        functools.partial(attend_back_kernel, experts),
        name="attend_back_layer",
        out_shape=[
            shape((members, dealt.shape[1] // 2, width), low),
            shape((members, dealt.shape[1] // 2, width), wide),
            shape(small, wide),
            shape((own_rows, 2 * heads_width), low),
            shape((own_rows, 2 * head), low),
            shape((own_rows, 2 * head), low),
            shape((2 * heads_width, lanes), low),
            shape((width, gate_part.shape[1] // 2), low),
            shape((width, up_part.shape[1] // 2), low),
            shape((down_part.shape[0] // 2, width), low),
        ],
        in_specs=[vmem] * 4
        + [pl.BlockSpec(memory_space=pltpu.SMEM)]
        + [vmem] * 10
        + [anywhere] * 13,
        out_specs=[vmem] * 7 + [anywhere] * 3,
        scratch_shapes=[
            pltpu.VMEM(dealt.shape, low),
            pltpu.VMEM(dealt.shape, low),
            pltpu.VMEM(small, wide),
            pltpu.VMEM(small, wide),
            pltpu.VMEM(small, wide),
            pltpu.VMEM((members, small[0], width // members), wide),
            pltpu.VMEM((1, head), wide),
        ]
        + [pltpu.VMEM(array.shape, low) for array in late]
        + [
            pltpu.VMEM((own_rows, width), wide),
            pltpu.VMEM((2, 2, own_rows, width), low),
            pltpu.VMEM((rows, heads_width), low),
            pltpu.VMEM((rows, heads_width + 2 * head), low),
            pltpu.VMEM((rows, head), wide),
            pltpu.VMEM((rows, head), wide),
            pltpu.VMEM((heads_width, width), low),
            pltpu.VMEM((members // 2, own_rows, width), low),
            pltpu.VMEM((members // 2, own_rows, width), low),
            *ChainSum.buffers(levels, (own_rows, width)),
            *ChainSum.buffers(levels, (heads_width, 2 * lanes)),
            pltpu.VMEM((members // 2, 2 * own_rows, 2 * head), low),
            *ChainSum.buffers(levels, (2 * own_rows, 2 * head)),
        ]
        + QuadSum.scratch(own_rows, width)
        + [dma((3,)), dma((3,)), dma((5,)), dma((5,)), dma((5,)), dma((3,)), dma((3,))]
        + [dma((members,))] * 6
        + [pltpu.SemaphoreType.REGULAR, dma((9,)), dma((members // 2,)), dma((members // 2,))]
        + ChainSum.semaphores(levels) * 4,
        compiler_params=pltpu.CompilerParams(
            collective_id=3, has_side_effects=True, vmem_limit_bytes=65_400_000
        ),
        cost_estimate=link_cost(185),
    )(
        entry,
        residual,
        gates,
        dealt,
        back_pick,
        router,
        *gain_vecs,
        key_low,
        value_low,
        key_pre,
        *tables,
        *late,
        out_part,
        gate_part,
        up_part,
        down_part,
    )


def fast_body(
    tokens,
    lengths,
    routes,
    deal_order,
    cotangent,
    attn_gain,
    query_gain,
    key_gain,
    moe_gain,
    w_query,
    key_projection_matrix,
    value_projection_matrix,
    w_out,
    w_router,
    w_gate,
    w_up,
    w_down,
):
    own_rows, model_width = tokens.shape
    head_dim = query_gain.shape[0]
    chip_count = lax.axis_size("chip")
    core_count = lax.axis_size("core")
    tp_count = lax.axis_size("tp")
    core_index = lax.axis_index("core")
    tp_index = lax.axis_index("tp")
    fsdp_count = chip_count * core_count
    fsdp_index = lax.axis_index("chip") * core_count + core_index
    slice_rows = own_rows // fsdp_count
    group_rows = tp_count * own_rows
    quad_rows = core_count * group_rows
    plane = ("chip", "core")
    quad = ("core", "tp")
    peer_ids = jnp.arange(fsdp_count, dtype=jnp.int32)
    wanted = (peer_ids - fsdp_index) % fsdp_count
    send_pick = jnp.sum(
        jnp.where(deal_order[None, :] == wanted[:, None], peer_ids[None, :], 0), axis=1
    )
    back_pick = (deal_order + fsdp_index) % fsdp_count

    def slices_of(values):
        return values.reshape(fsdp_count, slice_rows, model_width)

    down_full = lax.all_gather(w_down[0], "tp", axis=0, tiled=True)
    frequency = rope_base ** (-(jnp.arange(head_dim // 2, dtype=jnp.float32) * (2.0 / head_dim)))
    frequency = jnp.concatenate([frequency, frequency])[None, :]
    padded_lengths = jnp.pad(lengths, ((0, 7), (0, 128 - lengths.shape[1])))
    experts = w_router.shape[1]
    router_rows = w_router.T
    (
        dealt,
        normed,
        cosine_wide,
        sine_wide,
        moe_ext,
        residual,
        gates,
        query_pre,
        query_low,
        key_before_norm,
        key_low,
        value_low,
        probs_low,
        mixed_low,
        upstream_all,
        query_part,
        key_part,
        value_part,
        out_part,
        gate_full,
        up_full,
    ) = front_layer(
        experts,
        lengths.shape[1],
        slices_of(tokens),
        slices_of(cotangent),
        send_pick,
        attn_gain[None, :],
        padded_lengths,
        frequency,
        (query_gain[None, :], key_gain[None, :], moe_gain[None, :]),
        router_rows,
        routes,
        w_query,
        key_projection_matrix,
        value_projection_matrix,
        w_out,
        w_gate[0],
        w_up[0],
    )
    query_part = query_part.reshape(model_width, -1)
    key_part = key_part.reshape(model_width, -1)
    value_part = value_part.reshape(model_width, -1)
    upstream_all = upstream_all.reshape(fsdp_count * own_rows, model_width)
    entry_ext, moe_out, grad_w_gate, grad_w_up, grad_w_down = expert_layer(
        moe_ext, upstream_all, gate_full, up_full, down_full, experts
    )
    (
        output,
        grad_input,
        small,
        grad_w_query,
        grad_w_key,
        grad_w_value,
        grad_w_out,
        gate_arrived,
        up_arrived,
        down_arrived,
    ) = attend_back_layer(
        experts,
        entry_ext,
        residual,
        gates,
        dealt,
        back_pick,
        router_rows,
        (attn_gain[None, :], moe_gain[None, :], query_gain[None, :], key_gain[None, :]),
        mixed_low,
        probs_low,
        query_low,
        key_low,
        value_low,
        query_pre,
        key_before_norm,
        (cosine_wide, sine_wide),
        normed,
        query_part,
        key_part,
        value_part,
        out_part,
        moe_out.reshape(chip_count, core_count, own_rows, model_width),
        grad_w_gate,
        grad_w_up,
        grad_w_down,
    )
    def pair_sum(parts, arrived, dim):
        first, second = jnp.split(parts, 2, axis=dim)
        mine = jnp.where(tp_index == 0, first, second)
        return mine.astype(jnp.float32) + arrived.astype(jnp.float32)

    output = output.reshape(own_rows, model_width)
    grad_input = grad_input.reshape(own_rows, model_width)
    grad_w_router = small[8 : 8 + experts].T
    return (
        output,
        grad_input,
        small[0],
        small[2, :head_dim],
        small[2, head_dim : 2 * head_dim],
        small[1],
        grad_w_query.astype(jnp.float32),
        grad_w_key.astype(jnp.float32),
        grad_w_value.astype(jnp.float32),
        grad_w_out.astype(jnp.float32),
        grad_w_router,
        pair_sum(grad_w_gate, gate_arrived, 1)[None],
        pair_sum(grad_w_up, up_arrived, 1)[None],
        pair_sum(grad_w_down, down_arrived, 0)[None],
    )


def solution(mesh):
    fsdp_count, tp_count = mesh.shape["fsdp"], mesh.shape["tp"]
    chips = Mesh(mesh.devices.reshape(fsdp_count // 2, 2, tp_count), ("chip", "core", "tp"))
    dense = fsdp_count <= 16
    fsdp = ("chip", "core") if dense else "fsdp"
    every = ("chip", "core", "tp") if dense else ("fsdp", "tp")
    return jax.shard_map(
        fast_body if dense else body,
        mesh=chips if dense else mesh,
        in_specs=(
            P(every, None),
            P(fsdp, None),
            P(fsdp, None),
            P(),
            P(every, None),
            P(),
            P(),
            P(),
            P(),
            P(fsdp, "tp"),
            P(fsdp, "tp"),
            P(fsdp, "tp"),
            P("tp", fsdp),
            P(),
            P(fsdp, None, "tp"),
            P(fsdp, None, "tp"),
            P(fsdp, "tp", None),
        ),
        out_specs=(
            P(every, None),
            P(every, None),
            P(),
            P(),
            P(),
            P(),
            P(fsdp, "tp"),
            P(fsdp, "tp"),
            P(fsdp, "tp"),
            P("tp", fsdp),
            P(),
            P(fsdp, None, "tp"),
            P(fsdp, None, "tp"),
            P(fsdp, "tp", None),
        ),
        check_vma=False,
    )
```

```python
import functools

import jax
import jax.numpy as jnp
from jax import lax
from jax.experimental import pallas as pl
from jax.experimental.pallas import tpu as pltpu
from jax.sharding import Mesh
from jax.sharding import PartitionSpec as P

epsilon = 1e-06
rope_base = 1000000.0
masked_score = -1e30


def row_norm(values, gain_vec):
    factor = lax.rsqrt(jnp.mean(values * values, axis=-1, keepdims=True) + epsilon)
    return (values * factor * gain_vec, factor)


def norm_back(values, factor, gain_vec, upstream):
    scaled = upstream * gain_vec
    inner_term = jnp.mean(scaled * values, axis=-1, keepdims=True)
    return (factor * (scaled - values * (factor * factor) * inner_term), upstream * values * factor)


def seq_layout(seq_lengths, row_count):
    seq_ends = jnp.cumsum(seq_lengths)
    row_ids = jnp.arange(row_count, dtype=jnp.int32)
    segment = jnp.sum((row_ids[:, None] >= seq_ends[None, :]).astype(jnp.int32), axis=1)
    seq_starts = seq_ends - seq_lengths
    chosen = segment[:, None] == jnp.arange(seq_lengths.shape[0], dtype=jnp.int32)[None, :]
    position = row_ids - jnp.sum(jnp.where(chosen, seq_starts[None, :], 0), axis=1)
    return (segment, position)


def rotary(position, head_width):
    half_width = head_width // 2
    inverse_freq = rope_base ** (-(jnp.arange(half_width, dtype=jnp.float32) * (2.0 / head_width)))
    angles = position.astype(jnp.float32)[:, None] * inverse_freq[None, :]
    return (jnp.cos(angles)[:, None, :], jnp.sin(angles)[:, None, :])


def rotate(values, cosine_table, sine_table):
    half_width = values.shape[-1] // 2
    front_half = values[..., :half_width]
    back_half = values[..., half_width:]
    return jnp.concatenate(
        [
            front_half * cosine_table - back_half * sine_table,
            back_half * cosine_table + front_half * sine_table,
        ],
        axis=-1,
    )


def rotate_back(upstream, cosine_table, sine_table):
    half_width = upstream.shape[-1] // 2
    front_half = upstream[..., :half_width]
    back_half = upstream[..., half_width:]
    return jnp.concatenate(
        [
            front_half * cosine_table + back_half * sine_table,
            back_half * cosine_table - front_half * sine_table,
        ],
        axis=-1,
    )


def slot_table(route_rows, expert_count, capacity):
    row_count = route_rows.shape[0] * route_rows.shape[1]
    flat_routes = route_rows.reshape(row_count)
    expert_hits = (
        flat_routes[:, None] == jnp.arange(expert_count, dtype=jnp.int32)[None, :]
    ).astype(jnp.int32)
    earlier = jnp.cumsum(expert_hits, axis=0) - expert_hits
    slot_index = jnp.sum(earlier * expert_hits, axis=1)
    slot_place = flat_routes * capacity + slot_index
    slot_rows = jnp.full((expert_count * capacity,), row_count, jnp.int32)
    slot_rows = slot_rows.at[slot_place].set(jnp.arange(row_count, dtype=jnp.int32))
    return (slot_place, slot_rows.reshape(expert_count, capacity))


def contract_rows(left, right):
    return lax.dot_general(
        left, right, (((0,), (0,)), ((), ())), preferred_element_type=jnp.float32
    )


def contract_last(left, right):
    return lax.dot_general(
        left, right, (((1,), (1,)), ((), ())), preferred_element_type=jnp.float32
    )


def body(
    tokens,
    lengths,
    routes,
    deal_order,
    cotangent,
    attn_gain,
    query_gain,
    key_gain,
    moe_gain,
    w_query,
    key_projection_matrix,
    value_projection_matrix,
    w_out,
    w_router,
    w_gate,
    w_up,
    w_down,
):
    half_rows = tokens.shape[0]
    model_width = tokens.shape[1]
    head_dim = query_gain.shape[0]
    score_scale = head_dim ** (-0.5)
    fsdp_count = lax.axis_size("fsdp")
    tp_count = lax.axis_size("tp")
    fsdp_index = lax.axis_index("fsdp")
    tp_index = lax.axis_index("tp")
    slice_rows = half_rows // fsdp_count
    group_rows = tp_count * half_rows
    own_start = tp_index * half_rows
    peer_ids = jnp.arange(fsdp_count, dtype=jnp.int32)
    wanted = (peer_ids - fsdp_index) % fsdp_count
    send_pick = jnp.sum(
        jnp.where(deal_order[None, :] == wanted[:, None], peer_ids[None, :], 0), axis=1
    )
    back_pick = (deal_order + fsdp_index) % fsdp_count

    def deal_copies(values):
        slices = jnp.take(values.reshape(fsdp_count, slice_rows, model_width), send_pick, axis=0)
        return jnp.broadcast_to(slices[None], (tp_count, fsdp_count, slice_rows, model_width))

    tokens_all, cotangent_all = (
        lax.all_to_all(
            lax.all_to_all(deal_copies(tokens), "tp", split_axis=0, concat_axis=0, tiled=True),
            "fsdp",
            split_axis=1,
            concat_axis=1,
            tiled=True,
        ),
        lax.all_to_all(
            lax.all_to_all(deal_copies(cotangent), "tp", split_axis=0, concat_axis=0, tiled=True),
            "fsdp",
            split_axis=1,
            concat_axis=1,
            tiled=True,
        ),
    )
    tokens_in = tokens_all.reshape(group_rows, model_width).astype(jnp.float32)
    upstream = cotangent_all.reshape(group_rows, model_width).astype(jnp.float32)
    attn_in, attn_factor = row_norm(tokens_in, attn_gain)
    normed_all = attn_in.astype(jnp.bfloat16)
    query_full, key_full, value_full, out_full = (
        lax.all_gather(w_query, "fsdp", axis=0, tiled=True),
        lax.all_gather(key_projection_matrix, "fsdp", axis=0, tiled=True),
        lax.all_gather(value_projection_matrix, "fsdp", axis=0, tiled=True),
        lax.all_gather(w_out, "fsdp", axis=1, tiled=True),
    )
    query_heads = query_full.shape[1] // head_dim
    kv_heads = key_full.shape[1] // head_dim
    group_size = query_heads // kv_heads
    segment, position = seq_layout(lengths[0], group_rows)
    cosine_table, sine_table = rotary(position, head_dim)
    row_ids = jnp.arange(group_rows)
    allowed = (segment[:, None] == segment[None, :]) & (row_ids[None, :] <= row_ids[:, None])
    query_pre = jnp.dot(normed_all, query_full, preferred_element_type=jnp.float32).reshape(
        group_rows, query_heads, head_dim
    )
    query_normed, query_factor = row_norm(query_pre, query_gain)
    query_low = (
        rotate(query_normed, cosine_table, sine_table)
        .astype(jnp.bfloat16)
        .reshape(group_rows, kv_heads, group_size, head_dim)
    )
    key_before_norm = jnp.dot(normed_all, key_full, preferred_element_type=jnp.float32).reshape(
        group_rows, kv_heads, head_dim
    )
    key_normed, key_factor = row_norm(key_before_norm, key_gain)
    key_low = rotate(key_normed, cosine_table, sine_table).astype(jnp.bfloat16)
    value_low = (
        jnp.dot(normed_all, value_full, preferred_element_type=jnp.float32)
        .astype(jnp.bfloat16)
        .reshape(group_rows, kv_heads, head_dim)
    )
    scores = (
        jnp.einsum("qkgd,tkd->kgqt", query_low, key_low, preferred_element_type=jnp.float32)
        * score_scale
    )
    scores = jnp.where(allowed, scores, masked_score)
    row_peak = jnp.max(scores, axis=-1, keepdims=True)
    exponent = jnp.exp(scores - row_peak)
    totals = jnp.sum(exponent, axis=-1, keepdims=True)
    log_total = row_peak + jnp.log(totals)
    attn_probs = (exponent / totals).astype(jnp.bfloat16)
    attn_mixed = jnp.einsum(
        "kgqt,tkd->qkgd", attn_probs, value_low, preferred_element_type=jnp.float32
    )
    mixed_low = attn_mixed.reshape(group_rows, query_heads * head_dim).astype(jnp.bfloat16)
    attn_part = jnp.dot(mixed_low, out_full, preferred_element_type=jnp.float32)
    residual = tokens_in + lax.psum(attn_part, "tp")
    moe_in, moe_factor = row_norm(residual, moe_gain)
    moe_low = moe_in.astype(jnp.bfloat16)
    logits = jnp.dot(moe_low, w_router, preferred_element_type=jnp.float32)
    experts = w_router.shape[1]
    top_count = routes.shape[1]
    chosen = routes[:, :, None] == jnp.arange(experts, dtype=jnp.int32)[None, None, :]
    selected = jnp.sum(jnp.where(chosen, logits[:, None, :], 0.0), axis=-1)
    gate_peak = jnp.max(selected, axis=-1, keepdims=True)
    gate_exp = jnp.exp(selected - gate_peak)
    gate_probs = gate_exp / jnp.sum(gate_exp, axis=-1, keepdims=True)
    capacity = max(2, 3 * group_rows * top_count // (2 * experts))
    slot_place, slot_rows = slot_table(routes, experts, capacity)
    part_cap = capacity // tp_count
    slot_start = tp_index * part_cap
    gate_full, up_full, down_full = (
        lax.all_gather(w_gate, "tp", axis=2, tiled=True),
        lax.all_gather(w_up, "tp", axis=2, tiled=True),
        lax.all_gather(w_down, "tp", axis=1, tiled=True),
    )
    sent_rows = lax.dynamic_slice_in_dim(slot_rows, slot_start, part_cap, 1)
    slot_expert = slot_place // capacity
    slot_offset = slot_place % capacity - slot_start
    in_half = (slot_offset >= 0) & (slot_offset < part_cap)
    local_place = jnp.where(in_half, slot_expert * part_cap + slot_offset, experts * part_cap)
    padded = jnp.concatenate([moe_low, jnp.zeros((1, model_width), jnp.bfloat16)], axis=0)
    arrived = lax.all_to_all(
        padded[sent_rows // top_count], "fsdp", split_axis=0, concat_axis=0, tiled=True
    )
    local_experts = w_gate.shape[0]
    sources = experts // local_experts
    slot_count = sources * part_cap
    ff_part = w_gate.shape[2]

    def to_experts(values):
        return jnp.transpose(
            values.reshape(sources, local_experts, part_cap, model_width), (1, 0, 2, 3)
        ).reshape(local_experts, slot_count, model_width)

    def to_sources(values):
        width = values.shape[-1]
        return jnp.transpose(
            values.reshape(local_experts, sources, part_cap, width), (1, 0, 2, 3)
        ).reshape(experts, part_cap, width)

    def pick_rows(values):
        flat = values.reshape(experts * part_cap, tp_count * model_width)
        flat = jnp.concatenate([flat, jnp.zeros((1, tp_count * model_width), jnp.bfloat16)], axis=0)
        gathered = flat[local_place].reshape(group_rows, top_count, tp_count, model_width)
        return jnp.sum(gathered.astype(jnp.float32), axis=2)

    expert_rows = to_experts(arrived)
    gate_val = jnp.einsum(
        "esd,edf->esf", expert_rows, gate_full, preferred_element_type=jnp.float32
    )
    up_val = jnp.einsum("esd,edf->esf", expert_rows, up_full, preferred_element_type=jnp.float32)
    sigmoid_val = jax.nn.sigmoid(gate_val)
    swish_val = gate_val * sigmoid_val
    hidden_low = (swish_val * up_val).astype(jnp.bfloat16)
    hidden_blocks = hidden_low.reshape(local_experts, slot_count, tp_count, ff_part)
    down_blocks = down_full.reshape(local_experts, tp_count, ff_part, model_width)
    expert_out = (
        jnp.einsum(
            "esbf,ebfd->esbd", hidden_blocks, down_blocks, preferred_element_type=jnp.float32
        )
        .astype(jnp.bfloat16)
        .reshape(local_experts, slot_count, tp_count * model_width)
    )
    returned = lax.all_to_all(
        to_sources(expert_out), "fsdp", split_axis=0, concat_axis=0, tiled=True
    )
    picked = pick_rows(returned)
    moe_part = jnp.sum(gate_probs[:, :, None] * picked, axis=1)
    gate_grad_part = jnp.sum(upstream[:, None, :] * picked, axis=-1)
    weighted = (
        (gate_probs[:, :, None] * upstream[:, None, :])
        .astype(jnp.bfloat16)
        .reshape(group_rows * top_count, model_width)
    )
    weighted = jnp.concatenate([weighted, jnp.zeros((1, model_width), jnp.bfloat16)], axis=0)
    grad_arrived = lax.all_to_all(
        weighted[sent_rows], "fsdp", split_axis=0, concat_axis=0, tiled=True
    )
    grad_slots = to_experts(grad_arrived)
    hidden_grad = jnp.einsum(
        "esd,ebfd->esbf", grad_slots, down_blocks, preferred_element_type=jnp.float32
    ).reshape(local_experts, slot_count, tp_count * ff_part)
    swish_slope = sigmoid_val * (1.0 + gate_val * (1.0 - sigmoid_val))
    gate_val_grad = (hidden_grad * up_val * swish_slope).astype(jnp.bfloat16)
    up_val_grad = (hidden_grad * swish_val).astype(jnp.bfloat16)
    grad_w_down = jnp.einsum(
        "esbf,esd->ebfd", hidden_blocks, grad_slots, preferred_element_type=jnp.float32
    ).reshape(local_experts, tp_count * ff_part, model_width)
    grad_w_gate = jnp.einsum(
        "esd,esf->edf", expert_rows, gate_val_grad, preferred_element_type=jnp.float32
    )
    grad_w_up = jnp.einsum(
        "esd,esf->edf", expert_rows, up_val_grad, preferred_element_type=jnp.float32
    )
    gate_blocks = gate_full.reshape(local_experts, model_width, tp_count, ff_part)
    up_blocks = up_full.reshape(local_experts, model_width, tp_count, ff_part)
    entry_grad = (
        (
            jnp.einsum(
                "esbf,edbf->esbd",
                gate_val_grad.reshape(local_experts, slot_count, tp_count, ff_part),
                gate_blocks,
                preferred_element_type=jnp.float32,
            )
            + jnp.einsum(
                "esbf,edbf->esbd",
                up_val_grad.reshape(local_experts, slot_count, tp_count, ff_part),
                up_blocks,
                preferred_element_type=jnp.float32,
            )
        )
        .astype(jnp.bfloat16)
        .reshape(local_experts, slot_count, tp_count * model_width)
    )
    sent_back = lax.all_to_all(
        to_sources(entry_grad), "fsdp", split_axis=0, concat_axis=0, tiled=True
    )
    expert_grad = jnp.sum(pick_rows(sent_back), axis=1)
    grad_w_gate, grad_w_up, grad_w_down = (
        lax.psum_scatter(
            grad_w_gate.astype(jnp.bfloat16), "tp", scatter_dimension=2, tiled=True
        ).astype(jnp.float32),
        lax.psum_scatter(
            grad_w_up.astype(jnp.bfloat16), "tp", scatter_dimension=2, tiled=True
        ).astype(jnp.float32),
        lax.psum_scatter(
            grad_w_down.astype(jnp.bfloat16), "tp", scatter_dimension=1, tiled=True
        ).astype(jnp.float32),
    )
    moe_grad, gate_grad = (
        lax.psum(expert_grad.astype(jnp.bfloat16), "tp").astype(jnp.float32),
        lax.psum(gate_grad_part.astype(jnp.bfloat16), "tp").astype(jnp.float32),
    )
    gate_inner = jnp.sum(gate_probs * gate_grad, axis=-1, keepdims=True)
    selected_grad = gate_probs * (gate_grad - gate_inner)
    logit_grad = jnp.sum(jnp.where(chosen, selected_grad[:, :, None], 0.0), axis=1).astype(
        jnp.bfloat16
    )
    moe_grad = moe_grad + contract_last(logit_grad, w_router)
    router_grad = contract_rows(
        lax.dynamic_slice_in_dim(moe_low, own_start, half_rows, 0),
        lax.dynamic_slice_in_dim(logit_grad, own_start, half_rows, 0),
    )
    residual_from_norm, moe_gain_terms = norm_back(residual, moe_factor, moe_gain, moe_grad)
    residual_grad = upstream + residual_from_norm
    moe_gain_grad = jnp.sum(
        lax.dynamic_slice_in_dim(moe_gain_terms, own_start, half_rows, 0), axis=0
    )
    residual_low = residual_grad.astype(jnp.bfloat16)
    mixed_grad = (
        contract_last(residual_low, out_full)
        .astype(jnp.bfloat16)
        .reshape(group_rows, kv_heads, group_size, head_dim)
    )
    grad_w_out = contract_rows(mixed_low, residual_low)
    scores = (
        jnp.einsum("qkgd,tkd->kgqt", query_low, key_low, preferred_element_type=jnp.float32)
        * score_scale
    )
    scores = jnp.where(allowed, scores, masked_score)
    probs_full = jnp.exp(scores - log_total)
    prob_grad = jnp.einsum(
        "qkgd,tkd->kgqt", mixed_grad, value_low, preferred_element_type=jnp.float32
    )
    prob_inner = jnp.sum(probs_full * prob_grad, axis=-1, keepdims=True)
    score_grad = (probs_full * (prob_grad - prob_inner)).astype(jnp.bfloat16)
    query_grad = (
        jnp.einsum(
            "kgqt,tkd->qkgd", score_grad, key_low, preferred_element_type=jnp.float32
        ).reshape(group_rows, query_heads, head_dim)
        * score_scale
    )
    key_grad = (
        jnp.einsum("kgqt,qkgd->tkd", score_grad, query_low, preferred_element_type=jnp.float32)
        * score_scale
    )
    value_grad = (
        jnp.einsum(
            "kgqt,qkgd->tkd",
            probs_full.astype(jnp.bfloat16),
            mixed_grad,
            preferred_element_type=jnp.float32,
        )
        .astype(jnp.bfloat16)
        .reshape(group_rows, kv_heads * head_dim)
    )
    query_pre_grad, query_gain_terms = norm_back(
        query_pre, query_factor, query_gain, rotate_back(query_grad, cosine_table, sine_table)
    )
    key_pre_grad, key_gain_terms = norm_back(
        key_before_norm, key_factor, key_gain, rotate_back(key_grad, cosine_table, sine_table)
    )
    query_pre_low = query_pre_grad.astype(jnp.bfloat16).reshape(group_rows, query_heads * head_dim)
    key_pre_low = key_pre_grad.astype(jnp.bfloat16).reshape(group_rows, kv_heads * head_dim)
    grad_w_query = contract_rows(normed_all, query_pre_low)
    grad_w_key = contract_rows(normed_all, key_pre_low)
    grad_w_value = contract_rows(normed_all, value_grad)
    normed_grad = (
        contract_last(query_pre_low, query_full)
        + contract_last(key_pre_low, key_full)
        + contract_last(value_grad, value_full)
    )
    normed_grad_own, moe_own = (
        lax.psum_scatter(
            normed_grad.astype(jnp.bfloat16), "tp", scatter_dimension=0, tiled=True
        ).astype(jnp.float32),
        lax.psum_scatter(
            moe_part.astype(jnp.bfloat16), "tp", scatter_dimension=0, tiled=True
        ).astype(jnp.float32),
    )
    tokens_own = lax.dynamic_slice_in_dim(tokens_in, own_start, half_rows, 0)
    factor_own = lax.dynamic_slice_in_dim(attn_factor, own_start, half_rows, 0)
    tokens_from_norm, attn_gain_terms = norm_back(
        tokens_own, factor_own, attn_gain, normed_grad_own
    )
    grad_group = lax.dynamic_slice_in_dim(residual_grad, own_start, half_rows, 0) + tokens_from_norm
    residual_own = lax.dynamic_slice_in_dim(residual, own_start, half_rows, 0)
    output_group = (residual_own + moe_own).astype(jnp.bfloat16)
    back_output, back_grad = (
        lax.all_to_all(
            output_group.astype(jnp.float32)
            .reshape(fsdp_count, slice_rows, model_width)
            .astype(jnp.bfloat16),
            "fsdp",
            split_axis=0,
            concat_axis=0,
            tiled=True,
        ).astype(jnp.float32),
        lax.all_to_all(
            grad_group.reshape(fsdp_count, slice_rows, model_width).astype(jnp.bfloat16),
            "fsdp",
            split_axis=0,
            concat_axis=0,
            tiled=True,
        ).astype(jnp.float32),
    )
    output = (
        jnp.take(back_output, back_pick, axis=0)
        .reshape(half_rows, model_width)
        .astype(jnp.bfloat16)
    )
    grad_input = jnp.take(back_grad, back_pick, axis=0).reshape(half_rows, model_width)
    grad_w_query, grad_w_key, grad_w_value, grad_w_out = (
        lax.psum_scatter(grad_w_query, "fsdp", scatter_dimension=0, tiled=True),
        lax.psum_scatter(grad_w_key, "fsdp", scatter_dimension=0, tiled=True),
        lax.psum_scatter(grad_w_value, "fsdp", scatter_dimension=0, tiled=True),
        lax.psum_scatter(grad_w_out, "fsdp", scatter_dimension=1, tiled=True),
    )
    grad_attn_gain, grad_query_gain, grad_key_gain, grad_moe_gain, grad_w_router = lax.psum(
        (
            jnp.sum(attn_gain_terms, axis=0),
            jnp.sum(query_gain_terms, axis=(0, 1)),
            jnp.sum(key_gain_terms, axis=(0, 1)),
            moe_gain_grad,
            router_grad,
        ),
        ("fsdp", "tp"),
    )
    return (
        output,
        grad_input,
        grad_attn_gain,
        grad_query_gain,
        grad_key_gain,
        grad_moe_gain,
        grad_w_query,
        grad_w_key,
        grad_w_value,
        grad_w_out,
        grad_w_router,
        grad_w_gate,
        grad_w_up,
        grad_w_down,
    )


def remote(src, dst, send_sem, recv_sem, target):
    return pltpu.make_async_remote_copy(
        src_ref=src,
        dst_ref=dst,
        send_sem=send_sem,
        recv_sem=recv_sem,
        device_id=target,
        device_id_type=pl.DeviceIdType.MESH,
    )


def greet(targets):
    barrier = pltpu.get_barrier_semaphore()
    for target in targets:
        pl.semaphore_signal(
            barrier, inc=1, device_id=target, device_id_type=pl.DeviceIdType.MESH
        )
    pl.semaphore_wait(barrier, len(targets))


def link_cost(microseconds):
    return pl.CostEstimate(flops=0, bytes_accessed=microseconds * 3_000_000, transcendentals=0)


class Place:
    def __init__(self):
        self.chips = lax.axis_size("chip")
        self.levels = self.chips // 2
        self.chip = lax.axis_index("chip")
        self.core = lax.axis_index("core")
        self.tp = lax.axis_index("tp")
        self.level = self.chip // 2
        self.side = self.chip % 2
        self.fsdp = self.chip * 2 + self.core
        self.mate = {"core": 1 - self.core}
        self.across = {"tp": 1 - self.tp}
        self.beside = {"chip": self.level * 2 + 1 - self.side}
        self.above = {"chip": lax.rem(self.chip + 2, self.chips)}
        self.below = {"chip": lax.rem(self.chip + self.chips - 2, self.chips)}
        top = self.levels - 1
        self.upper = self.level // (self.levels // 2)
        self.end = top * self.upper
        self.next = self.end + 1 - 2 * self.upper
        self.at_end = self.level == self.end
        self.at_next = self.level == self.next
        outward = self.level * 2 + self.side + 4 * self.upper - 2
        inward = self.level * 2 + self.side + 2 - 4 * self.upper
        self.outward = {"chip": lax.rem(outward + self.chips, self.chips)}
        self.inward = {"chip": lax.rem(inward + self.chips, self.chips)}

    def member(self, offset):
        count = 2 * self.chips
        index = lax.rem(self.fsdp + offset + count, count)
        return {"chip": index // 2, "core": lax.rem(index, 2)}, index

    def plane_targets(self):
        return [self.member(offset)[0] for offset in range(1, 2 * self.chips)]

    def ring_targets(self):
        return [self.above, self.below, self.beside]


def lower_half(ref):
    return ref.at[pl.ds(0, ref.shape[0] // 2)]


def upper_half(ref):
    return ref.at[pl.ds(ref.shape[0] // 2, ref.shape[0] // 2)]


class RowGather:
    def __init__(self, place, block, sems, hands=True):
        self.place, self.block, self.hands = place, block, hands
        (
            self.up_send,
            self.up_recv,
            self.down_send,
            self.down_recv,
            self.side_send,
            self.side_recv,
            self.hop_send,
            self.hop_recv,
        ) = sems[:8]
        if hands:
            self.hand_send, self.hand_recv = sems[8:10]

    @staticmethod
    def semaphores(levels, hands=True):
        dma = pltpu.SemaphoreType.DMA
        return [dma((levels,))] * 6 + [dma, dma] + ([dma((2 * levels,))] * 2 if hands else [])

    def climb(self, origin):
        piece, at = self.block(origin, self.place.core), origin // 2
        return remote(piece, piece, self.up_send.at[at], self.up_recv.at[at], self.place.above)

    def sink(self, origin):
        piece, at = self.block(origin, self.place.core), origin // 2
        return remote(piece, piece, self.down_send.at[at], self.down_recv.at[at], self.place.below)

    def cross(self, origin, half=False):
        piece, at = self.block(origin, self.place.core), origin // 2
        if half:
            piece = upper_half(piece)
        return remote(piece, piece, self.side_send.at[at], self.side_recv.at[at], self.place.beside)

    def hop(self, level, inward):
        piece = self.block(level * 2 + 1 - self.place.side, self.place.core)
        if not inward:
            piece = lower_half(piece)
        target = self.place.inward if inward else self.place.outward
        return remote(piece, piece, self.hop_send, self.hop_recv, target)

    def hand(self, origin, whose):
        piece = self.block(origin, whose)
        return remote(
            piece, piece, self.hand_send.at[origin], self.hand_recv.at[origin], self.place.mate
        )

    def pass_on(self, origin):
        place = self.place
        at = origin // 2
        skipped = place.at_next & (at == place.end)
        halved = place.at_end & (at == place.next)

        @pl.when(halved)
        def _():
            self.cross(origin, True).start()

        @pl.when(~skipped & ~halved)
        def _():
            self.cross(origin).start()

        self.give(origin)

    def give(self, origin):
        if self.hands:
            self.hand(origin, self.place.core).start()

    def start(self):
        place = self.place

        @pl.when(place.level < place.levels - 1)
        def _():
            self.climb(place.chip).start()

        @pl.when(place.level > 0)
        def _():
            self.sink(place.chip).start()

        self.pass_on(place.chip)

    def crossed(self, at):
        place = self.place
        origin = at * 2 + 1 - place.side
        skipped = place.at_next & (at == place.end)
        halved = place.at_end & (at == place.next)

        @pl.when(skipped)
        def _():
            self.hop(place.end, True).wait_recv()

        @pl.when(halved)
        def _():
            self.cross(origin, True).wait_recv()

        @pl.when(~skipped & ~halved)
        def _():
            self.cross(origin).wait_recv()

        @pl.when(place.at_end & (at == place.end))
        def _():
            self.hop(place.end, True).start()

        @pl.when(~halved)
        def _():
            self.give(origin)

    def finish(self):
        place = self.place

        @pl.when(place.at_end)
        def _():
            self.hop(place.next, False).wait_recv()
            self.give(place.next * 2 + 1 - place.side)

    def step(self, n):
        place = self.place
        level, side, top = place.level, place.side, place.levels - 1
        under, over = level - n, level + n

        @pl.when((n > 0) & (under >= 0))
        def _():
            origin = under * 2 + side
            self.climb(origin).wait_recv()

            @pl.when(level < top)
            def _():
                self.climb(origin).start()

            self.pass_on(origin)

        @pl.when((n > 0) & (over <= top))
        def _():
            origin = over * 2 + side
            self.sink(origin).wait_recv()

            @pl.when(level > 0)
            def _():
                self.sink(origin).start()

            self.pass_on(origin)

        @pl.when(place.at_next & (n == place.levels - 2))
        def _():
            self.hop(place.next, False).start()

        @pl.when((n > 0) & (under + 1 >= 0))
        def _():
            self.crossed(under + 1)

        @pl.when((n > 1) & (over - 1 <= top))
        def _():
            self.crossed(over - 1)

    def take_hands(self):
        place = self.place

        def taken(origin, carry):
            self.hand(origin, 1 - place.core).wait_recv()
            return carry

        lax.fori_loop(0, place.chips, taken, 0)

    def drain(self):
        place = self.place
        level, side, top = place.level, place.side, place.levels - 1

        def handed(origin, carry):
            self.hand(origin, place.core).wait_send()
            return carry

        if self.hands:
            lax.fori_loop(0, place.chips, handed, 0)

        def sent(at, carry):
            skipped = place.at_next & (at == place.end)
            halved = place.at_end & (at == place.next)

            @pl.when(halved)
            def _():
                self.cross(at * 2 + side, True).wait_send()

            @pl.when(~skipped & ~halved)
            def _():
                self.cross(at * 2 + side).wait_send()

            @pl.when((level < top) & (at <= level))
            def _():
                self.climb(at * 2 + side).wait_send()

            @pl.when((level > 0) & (at >= level))
            def _():
                self.sink(at * 2 + side).wait_send()

            return carry

        lax.fori_loop(0, place.levels, sent, 0)

        @pl.when(place.at_end)
        def _():
            self.hop(place.end, True).wait_send()

        @pl.when(place.at_next)
        def _():
            self.hop(place.next, False).wait_send()


class RowGathers:
    def __init__(self, place, block, sems):
        count = len(sems) // 10
        self.rings = []
        for i in range(count):

            def piece(origin, whose, i=i):
                whole = block(origin, whose)
                rows = whole.shape[0] // count
                return whole.at[pl.ds(i * rows, rows)]

            self.rings.append(RowGather(place, piece, sems[10 * i : 10 * i + 10]))

    @staticmethod
    def semaphores(levels):
        return RowGather.semaphores(levels) * 2

    def start(self):
        for ring in self.rings:
            ring.start()

    def step(self, n):
        for ring in self.rings:
            ring.step(n)

    def finish(self):
        for ring in self.rings:
            ring.finish()

    def take_hand(self, origin, whose):
        for ring in self.rings:
            ring.hand(origin, whose).wait_recv()

    def take_hands(self):
        for ring in self.rings:
            ring.take_hands()

    def drain(self):
        for ring in self.rings:
            ring.drain()


class ChainSum:
    def __init__(self, place, parts, side_buf, chain_buf, hop_buf, sems):
        self.place, self.parts = place, parts
        self.side_buf, self.chain_buf, self.hop_buf = side_buf, chain_buf, hop_buf
        (
            self.up_send,
            self.up_recv,
            self.down_send,
            self.down_recv,
            self.side_send,
            self.side_recv,
            self.hop_send,
            self.hop_recv,
            self.half_send,
            self.half_recv,
        ) = sems

    @staticmethod
    def semaphores(levels):
        dma = pltpu.SemaphoreType.DMA
        return [dma((levels,))] * 6 + [dma] * 4

    @staticmethod
    def buffers(levels, block, dtype=jnp.bfloat16):
        return [
            pltpu.VMEM((levels,) + block, dtype),
            pltpu.VMEM((levels + 1,) + block, dtype),
            pltpu.VMEM(block, dtype),
        ]

    def target(self, turn):
        place = self.place
        top = place.levels - 1
        far, near = top - turn // 2, turn // 2
        odd = turn % 2
        low_half = far * (1 - odd) + near * odd
        high_half = near * (1 - odd) + far * odd
        inner = low_half * (1 - place.upper) + high_half * place.upper
        outer = (top - turn) * (1 - place.upper) + turn * place.upper
        return jnp.where(place.at_end, outer, inner)

    def from_under(self, goal):
        return self.chain_buf.at[goal + 1]

    def from_over(self, goal):
        return self.chain_buf.at[goal]

    def other(self, goal):
        return self.parts(goal * 2 + 1 - self.place.side)

    def cross(self, source, target, goal):
        return remote(
            source, target, self.side_send.at[goal], self.side_recv.at[goal], self.place.beside
        )

    def whole(self, goal):
        return self.cross(self.other(goal), self.side_buf.at[goal], goal)

    def lifted(self, goal):
        return self.cross(self.hop_buf, self.side_buf.at[goal], goal)

    def upper(self, goal):
        return self.cross(upper_half(self.other(goal)), upper_half(self.side_buf.at[goal]), goal)

    def lower(self, goal):
        return remote(
            lower_half(self.hop_buf),
            lower_half(self.side_buf.at[goal]),
            self.half_send,
            self.half_recv,
            self.place.beside,
        )

    def hop_out(self):
        return remote(
            self.other(self.place.end), self.hop_buf, self.hop_send, self.hop_recv, self.place.outward
        )

    def hop_in(self):
        return remote(
            lower_half(self.other(self.place.next)),
            lower_half(self.hop_buf),
            self.hop_send,
            self.hop_recv,
            self.place.inward,
        )

    def up(self, goal):
        return remote(
            self.side_buf.at[goal],
            self.from_under(goal),
            self.up_send.at[goal],
            self.up_recv.at[goal],
            self.place.above,
        )

    def down(self, goal):
        return remote(
            self.side_buf.at[goal],
            self.from_over(goal),
            self.down_send.at[goal],
            self.down_recv.at[goal],
            self.place.below,
        )

    def cases(self, goal):
        place = self.place
        to_end, to_next = goal == place.end, goal == place.next
        return (
            place.at_end & to_end,
            place.at_end & to_next,
            place.at_next & to_end,
            place.at_next & to_next,
        )

    def send(self, goal):
        end_end, end_next, next_end, next_next = self.cases(goal)

        @pl.when(end_next)
        def _():
            self.hop_in().start()

        @pl.when(next_end)
        def _():
            self.hop_out().start()

        @pl.when(end_next | next_next)
        def _():
            self.upper(goal).start()

        @pl.when(~(end_end | end_next | next_end | next_next))
        def _():
            self.whole(goal).start()

    def send_joined(self):
        place, wide = self.place, jnp.float32
        hop = self.hop_buf

        @pl.when(place.at_end)
        def _():
            self.hop_out().wait_recv()
            total = hop[...].astype(wide) + self.other(place.end)[...].astype(wide)
            hop[...] = total.astype(hop.dtype)
            self.lifted(place.end).start()

        @pl.when(place.at_next)
        def _():
            self.hop_in().wait_recv()
            half = hop.shape[0] // 2
            own = lower_half(self.other(place.next))[...].astype(wide)
            hop[:half] = (hop[:half].astype(wide) + own).astype(hop.dtype)
            self.lower(place.next).start()

    def add(self, goal, ref):
        held = self.side_buf
        total = held[goal].astype(jnp.float32) + ref[...].astype(jnp.float32)
        held[goal] = total.astype(held.dtype)

    def take_side(self, goal):
        place = self.place
        level, top = place.level, place.levels - 1
        end_end, end_next, next_end, next_next = self.cases(goal)
        held = self.side_buf
        own = self.parts(goal * 2 + place.side)
        half = held.shape[1] // 2

        @pl.when(end_next)
        def _():
            self.upper(goal).wait_recv()
            total = held[goal, half:].astype(jnp.float32) + upper_half(own)[...].astype(jnp.float32)
            held[goal, half:] = total.astype(held.dtype)
            held[goal, :half] = lower_half(own)[...]

        @pl.when(next_end)
        def _():
            held[goal] = own[...]

        @pl.when(next_next)
        def _():
            self.upper(goal).wait_recv()
            self.lower(goal).wait_recv()

        @pl.when(~(end_next | next_end | next_next))
        def _():
            self.whole(goal).wait_recv()

        @pl.when(~(end_next | next_end))
        def _():
            self.add(goal, own)

        @pl.when((goal > level) & (level == 0))
        def _():
            self.up(goal).start()

        @pl.when((goal < level) & (level == top))
        def _():
            self.down(goal).start()

    def take_chain(self, goal):
        place = self.place
        level, top = place.level, place.levels - 1

        @pl.when((goal > level) & (level > 0))
        def _():
            self.up(goal).wait_recv()
            self.add(goal, self.from_under(goal))
            self.up(goal).start()

        @pl.when((goal < level) & (level < top))
        def _():
            self.down(goal).wait_recv()
            self.add(goal, self.from_over(goal))
            self.down(goal).start()

    def close(self):
        place = self.place
        level, top = place.level, place.levels - 1

        @pl.when(level > 0)
        def _():
            self.up(level).wait_recv()
            self.add(level, self.from_under(level))

        @pl.when(level < top)
        def _():
            self.down(level).wait_recv()
            self.add(level, self.from_over(level))

    def drain(self):
        place = self.place

        def goal_done(goal, carry):
            end_end, end_next, next_end, next_next = self.cases(goal)

            @pl.when(end_end)
            def _():
                self.lifted(goal).wait_send()

            @pl.when(end_next)
            def _():
                self.hop_in().wait_send()

            @pl.when(next_end)
            def _():
                self.hop_out().wait_send()

            @pl.when(next_next)
            def _():
                self.lower(goal).wait_send()

            @pl.when(end_next | next_next)
            def _():
                self.upper(goal).wait_send()

            @pl.when(~(end_end | end_next | next_end | next_next))
            def _():
                self.whole(goal).wait_send()

            @pl.when(goal > place.level)
            def _():
                self.up(goal).wait_send()

            @pl.when(goal < place.level)
            def _():
                self.down(goal).wait_send()

            return carry

        lax.fori_loop(0, place.levels, goal_done, 0)


class QuadSum:
    def __init__(self, place, parts, near, pair, far, send, recv):
        self.place, self.parts = place, parts
        self.near, self.pair, self.far = near, pair, far
        self.send, self.recv = send, recv

    @staticmethod
    def scratch(rows, width):
        low, dma = jnp.bfloat16, pltpu.SemaphoreType.DMA
        return [
            pltpu.VMEM((2, rows, width), low),
            pltpu.VMEM((rows, width), low),
            pltpu.VMEM((rows, width), low),
            dma((3,)),
            dma((3,)),
        ]

    def to_mate(self, half):
        return remote(
            self.parts.at[1 - self.place.core, half],
            self.near.at[half],
            self.send.at[half],
            self.recv.at[half],
            self.place.mate,
        )

    def to_across(self):
        return remote(self.pair, self.far, self.send.at[2], self.recv.at[2], self.place.across)

    def start(self):
        self.to_mate(1 - self.place.tp).start()
        self.to_mate(self.place.tp).start()

    def relay(self):
        core, tp, wide = self.place.core, self.place.tp, jnp.float32
        self.to_mate(1 - tp).wait_recv()
        self.pair[...] = (
            self.parts[core, 1 - tp].astype(wide) + self.near[1 - tp].astype(wide)
        ).astype(jnp.bfloat16)
        self.to_across().start()

    def total(self):
        core, tp, wide = self.place.core, self.place.tp, jnp.float32
        self.to_mate(tp).wait_recv()
        total = self.parts[core, tp].astype(wide) + self.near[tp].astype(wide)
        self.to_across().wait_recv()
        return total + self.far[...].astype(wide)

    def drain(self):
        for half in range(2):
            self.to_mate(half).wait_send()
        self.to_across().wait_send()


def nt_dot(left, right):
    return lax.dot_general(
        left, right, (((1,), (1,)), ((), ())), preferred_element_type=jnp.float32
    )


def tn_dot(left, right):
    return lax.dot_general(
        left, right, (((0,), (0,)), ((), ())), preferred_element_type=jnp.float32
    )


def lanes_at(index, width):
    return pl.ds(pl.multiple_of(index * width, width), width)


def front_kernel(
    sequences,
    experts,
    tokens_ref,
    cotangent_ref,
    pick_ref,
    gain_ref,
    lengths_ref,
    frequency_ref,
    query_gain,
    key_gain,
    moe_gain,
    router_ref,
    routes_ref,
    query_ref,
    key_ref,
    value_ref,
    out_ref,
    gate_ref,
    up_ref,
    dealt_ref,
    normed_ref,
    cosine_ref,
    sine_ref,
    moe_ext,
    residual_ref,
    gates_ref,
    query_pre,
    query_low,
    key_pre,
    key_low,
    value_low,
    probs_ref,
    mixed_ref,
    upstream_all,
    query_all,
    key_all,
    value_all,
    out_all,
    gate_all,
    up_all,
    slices_ref,
    both_lengths_ref,
    mask_ref,
    upstream_own,
    query_w,
    key_w,
    value_w,
    out_w,
    router_rows,
    parts,
    near,
    pair,
    far,
    sum_send,
    sum_recv,
    deal_send,
    deal_recv,
    quad_send,
    quad_recv,
    swap_send,
    swap_recv,
    keep_sem,
    pair_send,
    pair_recv,
    pair_keep,
    load_sem,
    *ring_sems,
):
    place = Place()
    core, chip = place.core, place.chip
    wide, low = jnp.float32, jnp.bfloat16
    own_rows = query_ref.shape[0]
    width = dealt_ref.shape[2]
    quarter = query_all.shape[2]
    narrow = key_all.shape[2]
    head_rows = out_all.shape[0]
    lanes = out_ref.shape[1]
    members = 2 * place.chips
    for index in range(members):
        picked = pick_ref[index]
        both = [ref[picked].astype(jnp.float32) for ref in (tokens_ref, cotangent_ref)]
        slices_ref[index] = jnp.concatenate(both, axis=0).astype(jnp.bfloat16)
    greet(place.plane_targets() + [place.across])

    def deal_copy(offset, sending):
        target, index = place.member(offset if sending else -offset)
        return remote(
            slices_ref.at[index],
            dealt_ref.at[place.fsdp if sending else index],
            deal_send.at[offset - 1],
            deal_recv.at[offset - 1],
            target,
        )

    for offset in range(1, members):
        deal_copy(offset, True).start()

    def rows(who):
        return pl.ds(pl.multiple_of(who * own_rows, own_rows), own_rows)

    def columns(who, width):
        return pl.ds(pl.multiple_of(who * width, width), width)

    def spots(who):
        lane_start = pl.multiple_of((2 * chip + core) * lanes, lanes)
        return [
            (query_ref.at[:, columns(who, quarter)], query_all.at[chip, rows(core)]),
            (key_ref.at[:, columns(who, narrow)], key_all.at[chip, rows(core)]),
            (value_ref.at[:, columns(who, narrow)], value_all.at[chip, rows(core)]),
            (
                out_ref.at[pl.ds(pl.multiple_of(who * head_rows, head_rows), head_rows)],
                out_all.at[:, pl.ds(lane_start, lanes)],
            ),
        ]

    def arrivals():
        lane_start = pl.multiple_of((2 * chip + 1 - core) * lanes, lanes)
        return [
            query_all.at[chip, rows(1 - core)],
            key_all.at[chip, rows(1 - core)],
            value_all.at[chip, rows(1 - core)],
            out_all.at[:, pl.ds(lane_start, lanes)],
        ]

    sends = [
        remote(src, dst, swap_send.at[i], swap_recv.at[i], place.mate)
        for i, (src, dst) in enumerate(spots(1 - core))
    ]
    keeps = [
        pltpu.make_async_copy(src, dst, keep_sem.at[i])
        for i, (src, dst) in enumerate(spots(core))
    ]
    mate_lengths = remote(
        lengths_ref, both_lengths_ref.at[core], swap_send.at[4], swap_recv.at[4], place.mate
    )
    own_lengths = pltpu.make_async_copy(lengths_ref, both_lengths_ref.at[core], keep_sem.at[4])
    own_slice = pltpu.make_async_copy(
        slices_ref.at[place.fsdp], dealt_ref.at[place.fsdp], keep_sem.at[5]
    )
    own_slice.start()
    units = gate_ref.shape[1]

    def halves(who):
        at = pl.ds(pl.multiple_of(who * units, units), units)
        return [gate_all.at[:, at], up_all.at[:, at]]

    shards = (gate_ref, up_ref)
    pair_copies = []
    for i, (src, dst) in enumerate(zip(shards, halves(place.tp))):
        pair_copies.append(
            (
                remote(src, dst, pair_send.at[i], pair_recv.at[i], place.across),
                pltpu.make_async_copy(src, dst, pair_keep.at[i]),
            )
        )
    for i in range(4):
        sends[i].start()
        keeps[i].start()
    mate_lengths.start()
    own_lengths.start()

    out_lanes = 2 * lanes
    views = [
        lambda who, core: query_all.at[who],
        lambda who, core: key_all.at[who],
        lambda who, core: value_all.at[who],
        lambda who, core: out_all.at[:, lanes_at(who, out_lanes)],
    ]
    rings = [
        RowGather(place, view, ring_sems[8 * i : 8 * i + 8], hands=False)
        for i, view in enumerate(views)
    ]
    landed = arrivals()
    upstream_ring = RowGathers(
        place, lambda origin, whose: upstream_all.at[origin, whose], ring_sems[32:]
    )
    for i in range(4):
        keeps[i].wait()
        sends[i].wait_send()
        remote(landed[i], landed[i], swap_send.at[i], swap_recv.at[i], place.mate).wait_recv()
        rings[i].start()

    own_slice.wait()
    for offset in range(1, members):
        deal_copy(offset, False).wait_recv()
    tp = place.tp
    half = slices_ref.shape[1] // 2
    step_rows = 4
    width = dealt_ref.shape[2]
    for start in range(0, members, step_rows):
        block = dealt_ref[start : start + step_rows].astype(jnp.float32)
        span = slice(start * half, (start + step_rows) * half)
        upstream_own[span, :] = (
            block[:, half:].reshape(step_rows * half, block.shape[2]).astype(jnp.bfloat16)
        )
        x = block[:, :half].reshape(step_rows * half, block.shape[2])
        factor = lax.rsqrt(jnp.mean(x * x, axis=-1, keepdims=True) + epsilon)
        normed_ref[core, tp, start * half : (start + step_rows) * half, :] = (
            x * factor * gain_ref[...]
        ).astype(jnp.bfloat16)
    mine = normed_ref.at[core, tp]
    to_mate = remote(mine, mine, quad_send.at[0], quad_recv.at[0], place.mate)
    to_across = remote(mine, mine, quad_send.at[1], quad_recv.at[1], place.across)
    to_across.start()
    to_mate.start()
    for both in pair_copies:
        both[0].start()
        both[1].start()
    keep_upstream = pltpu.make_async_copy(upstream_own, upstream_all.at[chip, core], keep_sem.at[6])
    keep_upstream.start()
    levels = place.levels
    own_lengths.wait()
    mate_lengths.wait_send()
    theirs = both_lengths_ref.at[1 - core]
    remote(theirs, theirs, swap_send.at[4], swap_recv.at[4], place.mate).wait_recv()
    group = mask_ref.shape[1]
    head = cosine_ref.shape[1]
    heads = query_w.shape[2] // head
    across_sign = jnp.where(
        lax.broadcasted_iota(jnp.int32, (group, head), 1) < head // 2, -1.0, 1.0
    )
    for which in range(2):
        ends = []
        for at in range(sequences):
            length = both_lengths_ref[which, 0:1, at : at + 1]
            ends.append(length if at == 0 else ends[-1] + length)

        def segment_start(place_ids):
            start = jnp.zeros_like(place_ids)
            for end in ends:
                start = jnp.where(place_ids >= end, end, start)
            return start

        at_rows = pl.ds(which * group, group)
        row_ids = lax.broadcasted_iota(jnp.int32, (group, head), 0)
        position = (row_ids - segment_start(row_ids)).astype(jnp.float32)
        angles = position * frequency_ref[...]
        cosine_ref[at_rows, :] = jnp.cos(angles)
        sine_ref[at_rows, :] = jnp.sin(angles) * across_sign
        row_ids = lax.broadcasted_iota(jnp.int32, (group, group), 0)
        key_ids = lax.broadcasted_iota(jnp.int32, (group, group), 1)
        allowed = (key_ids <= row_ids) & (key_ids >= segment_start(row_ids))
        mask_ref[which] = jnp.where(allowed, 0.0, masked_score)
    early, late = rings[:3], rings[3]
    for ring in rings:
        ring.step(1)
    other = normed_ref.at[core, 1 - tp]
    remote(other, other, quad_send.at[1], quad_recv.at[1], place.across).wait_recv()
    passed = remote(other, other, quad_send.at[2], quad_recv.at[2], place.mate)
    passed.start()
    keep_upstream.wait()
    for n in range(2, levels):
        for ring in rings:
            ring.step(n)
        if n == 2:
            upstream_ring.start()
    for ring in early:
        ring.step(levels)
        ring.finish()
    loads = [
        pltpu.make_async_copy(src, dst, load_sem.at[i])
        for i, (src, dst) in enumerate(
            ((query_all, query_w), (key_all, key_w), (value_all, value_w), (out_all, out_w))
        )
    ]
    for load in loads[:3]:
        load.start()
    router_rows[...] = jnp.zeros_like(router_rows)
    router_rows[:experts, :] = router_ref[...]
    for slot, piece in ((0, normed_ref.at[1 - core, tp]), (2, normed_ref.at[1 - core, 1 - tp])):
        remote(piece, piece, quad_send.at[slot], quad_recv.at[slot], place.mate).wait_recv()
    for load in loads[:3]:
        load.wait()

    def turned(values, gain_ref):
        factor = lax.rsqrt(jnp.mean(values * values, axis=-1, keepdims=True) + epsilon)
        scaled = values * factor * gain_ref[...]
        return (scaled * cosine_ref[...] + pltpu.roll(scaled, head // 2, 1) * sine_ref[...]).astype(
            low
        )

    x = normed_ref[...].reshape(2 * group, width)

    def project(index, carry):
        both = jnp.dot(
            normed_ref[...].reshape(2 * group, width),
            query_w[:, :, lanes_at(index, 2 * head)].reshape(width, 2 * head),
            preferred_element_type=wide,
        )
        query_pre[:, lanes_at(index, 2 * head)] = both.astype(low)
        for which in range(2):
            one = both[:, which * head : (which + 1) * head]
            query_low[:, lanes_at(2 * index + which, head)] = turned(one, query_gain)
        return carry

    lax.fori_loop(0, heads // 2, project, 0)
    key_values = jnp.dot(x, key_w[...].reshape(width, head), preferred_element_type=wide)
    key_pre[...] = key_values
    key_low[...] = turned(key_values, key_gain)
    value_low[...] = jnp.dot(x, value_w[...].reshape(width, head), preferred_element_type=wide).astype(low)
    late.step(levels)
    late.finish()
    loads[3].start()
    upstream_ring.step(1)
    scale = head ** (-0.5)
    batch = 4

    def attend(index, carry):
        which = index // (heads // batch)
        first = (index % (heads // batch)) * batch
        rows = lanes_at(which, group)
        key = key_low[rows, :]
        value = value_low[rows, :]
        mask = mask_ref[which]
        for offset in range(batch):
            at = lanes_at(first + offset, head)
            scores = nt_dot(query_low[rows, at], key) * scale + mask
            peak = jnp.max(scores, axis=-1, keepdims=True)
            exponent = jnp.exp(scores - peak)
            probs = (exponent * (1.0 / jnp.sum(exponent, axis=-1, keepdims=True))).astype(low)
            probs_ref[which * heads + first + offset] = probs
            mixed_ref[rows, at] = jnp.dot(probs, value, preferred_element_type=wide).astype(low)
        return carry

    lax.fori_loop(0, 2 * heads // batch, attend, 0)
    loads[3].wait()

    def out_rows(whose):
        left = mixed_ref[lanes_at(whose, group), :]

        def out_lanes(index, carry):
            at = lanes_at(index, 512)
            product = jnp.dot(left, out_w[:, at], preferred_element_type=wide).astype(low)
            parts[whose, :, :, at] = product.reshape(2, own_rows, 512)
            return carry

        lax.fori_loop(0, width // 512, out_lanes, 0)

    sums = QuadSum(place, parts, near, pair, far, quad_send, quad_recv)
    sums = QuadSum(place, parts, near, pair, far, sum_send, sum_recv)
    out_rows(1 - core)
    sums.start()
    out_rows(core)
    upstream_ring.step(2)
    sums.relay()
    upstream_ring.step(3)
    total = sums.total()

    def token_rows(start):
        block = dealt_ref[start : start + step_rows].astype(wide)[:, :half]
        return block.reshape(step_rows * half, width)

    tokens = jnp.concatenate(
        [token_rows(start) for start in range(0, members, step_rows)], axis=0
    )
    residual = tokens + total
    residual_ref[...] = residual
    factor = lax.rsqrt(jnp.mean(residual * residual, axis=-1, keepdims=True) + epsilon)
    moe_low = (residual * factor * moe_gain[...]).astype(low)
    moe_ext[:, :width] = moe_low
    logits = nt_dot(moe_low, router_rows[...])
    own_routes = routes_ref[lanes_at(place.tp, own_rows), :]
    lane = lax.broadcasted_iota(jnp.int32, (own_rows, 128), 1)
    chosen = own_routes[:, 0:1] == lane
    for choice in range(1, own_routes.shape[1]):
        chosen |= own_routes[:, choice : choice + 1] == lane
    logits = jnp.where(chosen, logits, masked_score)
    exponent = jnp.exp(logits - jnp.max(logits, axis=-1, keepdims=True))
    exponent = jnp.where(chosen, exponent, 0.0)
    gates = exponent / jnp.sum(exponent, axis=-1, keepdims=True)
    gates_ref[...] = gates
    high = gates.astype(low).astype(wide)
    middle = (gates - high).astype(low).astype(wide)
    rest = gates - high - middle
    moe_ext[:, width:] = (
        high + pltpu.roll(middle, experts, 1) + pltpu.roll(rest, 2 * experts, 1)
    ).astype(low)
    for n in range(4, levels + 1):
        upstream_ring.step(n)
    upstream_ring.finish()
    upstream_ring.take_hands()
    upstream_ring.drain()
    sums.drain()
    for ring in rings:
        ring.drain()
    for offset in range(1, members):
        deal_copy(offset, True).wait_send()
    to_mate.wait_send()
    to_across.wait_send()
    passed.wait_send()
    for i, dst in enumerate(halves(1 - place.tp)):
        pair_copies[i][1].wait()
        pair_copies[i][0].wait_send()
        remote(dst, dst, pair_send.at[i], pair_recv.at[i], place.across).wait_recv()


def front_layer(
    experts,
    sequences,
    tokens,
    cotangent,
    pick,
    gain_vec,
    lengths,
    frequency,
    gain_vecs,
    router,
    routes,
    w_query,
    w_key,
    w_value,
    w_out,
    w_gate,
    w_up,
):
    members, slice_rows, width = tokens.shape
    dealt_shape = (members, 2 * slice_rows, width)
    chips = members // 2
    levels = chips // 2
    own_rows = w_query.shape[0]
    wide, low = jnp.float32, jnp.bfloat16
    vmem = pl.BlockSpec(memory_space=pltpu.VMEM)
    anywhere = pl.BlockSpec(memory_space=pl.ANY)
    dma = pltpu.SemaphoreType.DMA
    shape = jax.ShapeDtypeStruct
    group, head = 2 * own_rows, frequency.shape[1]
    rows, heads_width = 2 * group, w_query.shape[1] // 2
    weights = [(chips, 2 * own_rows, w.shape[1] // 2) for w in (w_query, w_key, w_value)]
    weights.append((w_out.shape[0] // 2, members * w_out.shape[1]))
    return pl.pallas_call(
        functools.partial(front_kernel, sequences, experts),
        name="front_layer",
        out_shape=[
            shape(dealt_shape, low),
            shape((2, 2, own_rows, width), low),
            shape((rows, head), wide),
            shape((rows, head), wide),
            shape((own_rows, width + 128), low),
            shape((own_rows, width), wide),
            shape((own_rows, 128), wide),
            shape((rows, heads_width), low),
            shape((rows, heads_width), low),
            shape((rows, head), wide),
            shape((rows, head), low),
            shape((rows, head), low),
            shape((2 * heads_width // head, group, group), low),
            shape((rows, heads_width), low),
            shape((chips, 2, own_rows, width), low),
        ]
        + [shape(weight, low) for weight in weights]
        + [shape((width, 2 * w_gate.shape[1]), low), shape((width, 2 * w_up.shape[1]), low)],
        in_specs=[vmem] * 2
        + [pl.BlockSpec(memory_space=pltpu.SMEM)]
        + [vmem] * 8
        + [anywhere] * 6,
        out_specs=[vmem] * 14 + [anywhere] * 7,
        scratch_shapes=[
            pltpu.VMEM(dealt_shape, low),
            pltpu.VMEM((2,) + lengths.shape, jnp.int32),
            pltpu.VMEM((2, group, group), wide),
            pltpu.VMEM((own_rows, width), low),
        ]
        + [pltpu.VMEM(weight, low) for weight in weights]
        + [pltpu.VMEM((128, width), low), pltpu.VMEM((2, 2, own_rows, width), low)]
        + QuadSum.scratch(own_rows, width)
        + [
            dma((members - 1,)),
            dma((members - 1,)),
            dma((3,)),
            dma((3,)),
            dma((5,)),
            dma((5,)),
            dma((7,)),
            dma((2,)),
            dma((2,)),
            dma((2,)),
            dma((4,)),
        ]
        + RowGather.semaphores(levels, hands=False) * 4
        + RowGathers.semaphores(levels),
        compiler_params=pltpu.CompilerParams(
            collective_id=0, has_side_effects=True, vmem_limit_bytes=65_400_000
        ),
        cost_estimate=link_cost(170),
    )(
        tokens,
        cotangent,
        pick,
        gain_vec,
        lengths,
        frequency,
        *gain_vecs,
        router,
        routes,
        w_query,
        w_key,
        w_value,
        w_out,
        w_gate,
        w_up,
    )


def expert_kernel(
    experts,
    x_own,
    upstream_ref,
    gate_ref,
    up_ref,
    down_ref,
    entry_own,
    out_part,
    gate_grad_ref,
    up_grad_ref,
    down_grad_ref,
    x_all,
    u_all,
    gate_w,
    up_w,
    down_w,
    hidden,
    gate_val_grad,
    up_val_grad,
    scores,
    sums,
    mate_out,
    mate_in,
    side_buf,
    chain_buf,
    hop_buf,
    staged,
    load_sem,
    store_sem,
    both_sem,
    mate_send,
    mate_recv,
    *ring_sems,
):
    place = Place()
    core, chip, level, side = place.core, place.chip, place.level, place.side
    levels, top = place.levels, place.levels - 1
    rows = x_own.shape[0]
    tile = 2 * rows
    width = upstream_ref.shape[1]
    units = down_ref.shape[0]
    wide = jnp.float32
    low = jnp.bfloat16
    loads = [
        pltpu.make_async_copy(x_own, x_all.at[chip, core], load_sem.at[0]),
        pltpu.make_async_copy(gate_ref, gate_w, load_sem.at[1]),
        pltpu.make_async_copy(up_ref, up_w, load_sem.at[2]),
        pltpu.make_async_copy(down_ref, down_w, load_sem.at[3]),
        pltpu.make_async_copy(upstream_ref, u_all, load_sem.at[4]),
    ]
    for load in loads:
        load.start()
    greet(place.ring_targets() + [place.mate])

    gather = RowGathers(place, lambda origin, whose: x_all.at[origin, whose], ring_sems[:20])
    loads[0].wait()

    gather.start()
    for load in loads[1:]:
        load.wait()

    lane = lax.broadcasted_iota(jnp.int32, (128, 128), 0)
    select = (
        (lane == place.fsdp)
        | (lane == place.fsdp + experts)
        | (lane == place.fsdp + 2 * experts)
    ).astype(low)
    cut = 256
    across_lanes = lax.broadcasted_iota(jnp.int32, (tile, 128), 1)

    def forward_tile(origin):
        x = x_all[origin].reshape(tile, x_all.shape[3])
        gate_lanes = jnp.dot(x[:, width:], select, preferred_element_type=wide)
        gate = jnp.concatenate([gate_lanes] * (cut // 128), axis=1)
        x = x[:, :width]
        start = pl.multiple_of(origin * tile, tile)
        u = u_all[pl.ds(start, tile), :]
        score = jnp.zeros((tile, 1), wide)
        for part in range(units // cut):
            lanes = slice(part * cut, (part + 1) * cut)
            gate_val = jnp.dot(x, gate_w[:, lanes], preferred_element_type=wide)
            up_val = jnp.dot(x, up_w[:, lanes], preferred_element_type=wide)
            back = lax.dot_general(
                u, down_w[lanes, :], (((1,), (1,)), ((), ())), preferred_element_type=wide
            )
            sigmoid = 1.0 / (1.0 + jnp.exp(-gate_val))
            swish = gate_val * sigmoid
            out = (swish * up_val).astype(low).astype(wide)
            score += jnp.sum(out * back, axis=1, keepdims=True)
            back = back * gate
            slope = sigmoid * (1.0 + gate_val * (1.0 - sigmoid))
            hidden[pl.ds(start, tile), lanes] = (out * gate).astype(low)
            gate_val_grad[pl.ds(start, tile), lanes] = (back * up_val * slope).astype(low)
            up_val_grad[pl.ds(start, tile), lanes] = (back * swish).astype(low)
        high = score.astype(low).astype(wide)
        packed = jnp.where(
            across_lanes == place.fsdp,
            high,
            jnp.where(across_lanes == place.fsdp + experts, score - high, 0.0),
        )
        scores[origin] = packed.astype(low)

    def gather_step(n, carry):
        gather.step(n)

        def candidate(which, carried):
            upward = which % 2
            facing = which // 2
            distance = n - 1 + facing
            at = level + distance * (2 * upward - 1)
            early = (n == 2) & (facing == 0) & place.at_end
            origin = at * 2 + side * facing + (1 - side) * (1 - facing)
            inside = (at >= 0) & (at <= top) & (distance >= 0) & ((distance > 0) | (upward == 0))

            @pl.when(inside & ~early)
            def _():
                gather.take_hand(origin, 1 - core)
                forward_tile(origin)

            return carried

        return lax.fori_loop(0, 4, candidate, carry)

    lax.fori_loop(0, levels + 1, gather_step, 0)

    plane_sum = ChainSum(place, lambda chip: sums.at[chip], side_buf, chain_buf, hop_buf, ring_sems[20:])

    def to_mate(goal_chip, slot):
        return remote(
            mate_out.at[slot],
            mate_in.at[goal_chip],
            mate_send.at[slot],
            mate_recv.at[goal_chip],
            place.mate,
        )

    def backward_tile(goal_chip, slot, reuse):
        start = pl.multiple_of(goal_chip * tile, tile)
        own_start = pl.multiple_of(goal_chip * tile + core * rows, rows)
        mate_start = pl.multiple_of(goal_chip * tile + (1 - core) * rows, rows)

        @pl.when(reuse)
        def _():
            to_mate(goal_chip, slot).wait_send()

        grads = gate_val_grad[pl.ds(start, tile), :]
        up_grads = up_val_grad[pl.ds(start, tile), :]
        piece = 512
        for first in range(0, width, piece):
            lanes = slice(first, first + piece)
            whole = lax.dot_general(
                grads, gate_w[lanes, :], (((1,), (1,)), ((), ())), preferred_element_type=wide
            ) + lax.dot_general(
                up_grads, up_w[lanes, :], (((1,), (1,)), ((), ())), preferred_element_type=wide
            )
            halves = whole.astype(low).reshape(2, rows, piece)
            sums[goal_chip, :, lanes] = jnp.where(core == 0, halves[0], halves[1])
            mate_out[slot, :, lanes] = jnp.where(core == 0, halves[1], halves[0])
        sums[goal_chip, :, width:] = scores[goal_chip, pl.ds(pl.multiple_of(core * rows, rows), rows)]
        mate_out[slot, :, width:] = scores[
            goal_chip, pl.ds(pl.multiple_of((1 - core) * rows, rows), rows)
        ]
        to_mate(goal_chip, slot).start()

    def joined(goal_chip, slot):
        to_mate(goal_chip, slot).wait_recv()
        sums[goal_chip] = (
            sums[goal_chip].astype(wide) + mate_in[goal_chip].astype(wide)
        ).astype(low)

    def backward_turn(turn, carry):
        goal = plane_sum.target(turn)

        @pl.when((turn == levels - 2) & place.at_end)
        def _():
            origin = place.next * 2 + 1 - side
            gather.take_hand(origin, 1 - core)
            forward_tile(origin)

        backward_tile(goal * 2 + 1 - side, 0, turn > 0)
        backward_tile(goal * 2 + side, 1, turn > 0)
        joined(goal * 2 + 1 - side, 0)
        plane_sum.send(goal)
        joined(goal * 2 + side, 1)
        return carry

    def first_turns(turn, carry):
        backward_turn(turn, carry)

        @pl.when(turn == 0)
        def _():
            gather.finish()

        return carry

    lax.fori_loop(0, levels, first_turns, 0)
    plane_sum.send_joined()

    def store(target, start, slot):
        return pltpu.make_async_copy(
            staged.at[slot], target.at[pl.ds(start, tile)], store_sem.at[slot]
        )

    def output_tile(origin, carry):
        start = pl.multiple_of(origin * tile, tile)
        slot = origin % 2

        @pl.when(origin > 1)
        def _():
            store(out_part, start, slot).wait()

        left = hidden[pl.ds(start, tile), :]
        for first in range(0, width, 512):
            lanes = slice(first, first + 512)
            staged[slot, :, lanes] = jnp.dot(
                left, down_w[:, lanes], preferred_element_type=wide
            ).astype(low)
        store(out_part, start, slot).start()
        return carry

    def down_grads(index, carry):
        start = pl.multiple_of(index * tile, tile)
        slot = index % 2
        store(down_grad_ref, start, slot).wait()
        left = hidden[:, pl.ds(start, tile)]
        for first in range(0, width, 512):
            lanes = slice(first, first + 512)
            staged[slot, :, lanes] = lax.dot_general(
                left, u_all[:, lanes], (((0,), (0,)), ((), ())), preferred_element_type=wide
            ).astype(low)
        store(down_grad_ref, start, slot).start()
        return carry

    def store_both(index):
        slot = index % 2
        start = pl.multiple_of(index * tile, tile)
        return [
            pltpu.make_async_copy(
                staged.at[slot, :, i * units : (i + 1) * units],
                target.at[pl.ds(start, tile)],
                both_sem.at[slot, i],
            )
            for i, target in enumerate((gate_grad_ref, up_grad_ref))
        ]

    def entry_weight_grads(index, carry):
        slot = index % 2

        @pl.when(index > 1)
        def _():
            for copy in store_both(index):
                copy.wait()

        left = x_all[:, :, :, pl.ds(pl.multiple_of(index * tile, tile), tile)]
        left = left.reshape(u_all.shape[0], tile)
        for i, right in enumerate((gate_val_grad, up_val_grad)):
            staged[slot, :, i * units : (i + 1) * units] = lax.dot_general(
                left, right[...], (((0,), (0,)), ((), ())), preferred_element_type=wide
            ).astype(low)
        for copy in store_both(index):
            copy.start()
        return carry

    plane_sum.take_side(plane_sum.target(0))
    lax.fori_loop(0, place.chips, output_tile, 0)
    plane_sum.take_chain(plane_sum.target(0))
    plane_sum.take_side(plane_sum.target(1))
    lax.fori_loop(0, units // tile, down_grads, 0)
    for slot in range(2):
        store(down_grad_ref, 0, slot).wait()
    plane_sum.take_chain(plane_sum.target(1))
    plane_sum.take_side(plane_sum.target(2))
    chunks = width // tile
    lax.fori_loop(0, chunks // 2, entry_weight_grads, 0)
    plane_sum.take_chain(plane_sum.target(2))
    plane_sum.take_side(plane_sum.target(3))
    lax.fori_loop(chunks // 2, chunks, entry_weight_grads, 0)
    plane_sum.take_chain(plane_sum.target(3))
    plane_sum.close()
    entry_own[...] = side_buf[level]
    for slot in range(2):
        for copy in store_both(slot):
            copy.wait()
        to_mate(0, slot).wait_send()
    plane_sum.drain()

    gather.drain()


def expert_layer(x_own, upstream_all, gate_all, up_all, down_all, experts):
    rows, span = x_own.shape
    total, width = upstream_all.shape
    units = down_all.shape[0]
    chips = total // (2 * rows)
    levels = chips // 2
    low = jnp.bfloat16
    vmem = pl.BlockSpec(memory_space=pltpu.VMEM)
    anywhere = pl.BlockSpec(memory_space=pl.ANY)
    dma = pltpu.SemaphoreType.DMA
    return pl.pallas_call(
        functools.partial(expert_kernel, experts),
        name="expert_layer",
        out_shape=[
            jax.ShapeDtypeStruct((rows, span), low),
            jax.ShapeDtypeStruct((total, width), low),
            jax.ShapeDtypeStruct((width, units), low),
            jax.ShapeDtypeStruct((width, units), low),
            jax.ShapeDtypeStruct((units, width), low),
        ],
        in_specs=[vmem] + [anywhere] * 4,
        out_specs=[vmem] + [anywhere] * 4,
        scratch_shapes=[
            pltpu.VMEM((chips, 2, rows, span), low),
            pltpu.VMEM((total, width), low),
            pltpu.VMEM((width, units), low),
            pltpu.VMEM((width, units), low),
            pltpu.VMEM((units, width), low),
            pltpu.VMEM((total, units), low),
            pltpu.VMEM((total, units), low),
            pltpu.VMEM((total, units), low),
            pltpu.VMEM((chips, 2 * rows, 128), low),
            pltpu.VMEM((chips, rows, span), low),
            pltpu.VMEM((2, rows, span), low),
            pltpu.VMEM((chips, rows, span), low),
            *ChainSum.buffers(levels, (rows, span)),
            pltpu.VMEM((2, 2 * rows, width), low),
            dma((5,)),
            dma((2,)),
            dma((2, 2)),
        ]
        + [dma((2,)), dma((chips,))]
        + RowGathers.semaphores(levels)
        + ChainSum.semaphores(levels),
        compiler_params=pltpu.CompilerParams(
            collective_id=5, has_side_effects=True, vmem_limit_bytes=65_400_000
        ),
        cost_estimate=link_cost(125),
    )(x_own, upstream_all, gate_all, up_all, down_all)


def attend_back_kernel(
    experts,
    entry_ref,
    residual_ref,
    gates_ref,
    dealt_ref,
    back_ref,
    router_ref,
    attn_gain,
    moe_gain,
    query_gain,
    key_gain,
    key_low,
    value_low,
    key_pre,
    cosine_ref,
    sine_ref,
    mixed_far,
    out_far,
    probs_far,
    query_low_far,
    query_pre_far,
    query_far,
    key_far,
    value_far,
    normed_far,
    out_part,
    gate_part,
    up_part,
    down_part,
    output_ref,
    token_grad_ref,
    small_ref,
    query_own,
    key_own,
    value_own,
    out_own,
    gate_arrived,
    up_arrived,
    down_arrived,
    finished_ref,
    returned_ref,
    small_own,
    small_near,
    small_pair,
    small_parts,
    query_gain_part,
    mixed_ref,
    out_w,
    probs_ref,
    query_low,
    query_pre,
    query_w,
    key_w,
    value_w,
    normed_ref,
    residual_grad,
    low_all,
    mixed_grad,
    low_grads,
    key_total,
    value_total,
    out_grad,
    out_sums,
    out_mate,
    out_side,
    out_chain,
    out_hop,
    weight_side,
    weight_chain,
    weight_hop,
    narrow_grad,
    narrow_side,
    narrow_chain,
    narrow_hop,
    near,
    pair,
    far,
    quad_send,
    quad_recv,
    share_send,
    share_recv,
    swap_send,
    swap_recv,
    keep_sem,
    pair_send,
    pair_recv,
    deal_send,
    deal_recv,
    small_send,
    small_recv,
    total_send,
    total_recv,
    free_sem,
    load_sem,
    join_send,
    join_recv,
    *ring_sems,
):
    place = Place()
    core, tp, level = place.core, place.tp, place.level
    wide, low = jnp.float32, jnp.bfloat16
    own_rows, width = residual_ref.shape
    group = 2 * own_rows
    rows = 2 * group
    head = query_gain.shape[1]
    heads = mixed_grad.shape[1] // head
    members = dealt_ref.shape[0]
    half = dealt_ref.shape[1] // 2
    step_rows = 4
    scale = head ** (-0.5)

    def dealt_rows(second):
        blocks = []
        for start in range(0, members, step_rows):
            block = dealt_ref[start : start + step_rows].astype(wide)
            block = block[:, half:] if second else block[:, :half]
            blocks.append(block.reshape(step_rows * half, width))
        return jnp.concatenate(blocks, axis=0)

    greet(place.plane_targets() + [place.across])

    def to_mate(origin):
        return remote(
            out_part.at[origin, 1 - core],
            out_mate.at[origin],
            join_send.at[origin],
            join_recv.at[origin],
            place.mate,
        )

    out_ring = ChainSum(
        place, lambda chip: out_sums.at[chip], out_side, out_chain, out_hop, ring_sems[:10]
    )

    def joined_at(turn):
        goal = out_ring.target(turn)
        return (goal * 2 + 1 - place.side, goal * 2 + place.side)

    def offer(turn, carry):
        for origin in joined_at(turn):
            to_mate(origin).start()
        return carry

    keep = pltpu.make_async_copy(out_part.at[:, core], out_sums, keep_sem.at[0])
    keep.start()
    lax.fori_loop(0, place.levels, offer, 0)
    loads = [
        pltpu.make_async_copy(src, dst, load_sem.at[i])
        for i, (src, dst) in enumerate(
            (
                (mixed_far, mixed_ref),
                (out_far, out_w),
                (probs_far, probs_ref),
                (query_low_far, query_low),
                (query_pre_far, query_pre),
                (query_far, query_w),
                (key_far, key_w),
                (value_far, value_w),
                (normed_far, normed_ref),
            )
        )
    ]
    for load in loads:
        load.start()

    def join(turn, carry):
        for origin in joined_at(turn):
            to_mate(origin).wait_recv()
            out_sums[origin] = (
                out_sums[origin].astype(wide) + out_mate[origin].astype(wide)
            ).astype(low)
        out_ring.send(out_ring.target(turn))
        return carry

    keep.wait()
    join(0, 0)

    entry = entry_ref[:, :width].astype(wide)
    extra = entry_ref[:, width:].astype(wide)
    gates = gates_ref[...]
    gate_grad = extra + pltpu.roll(extra, 128 - experts, 1)
    inner = jnp.sum(gates * gate_grad, axis=-1, keepdims=True)
    logit_grad = (gates * (gate_grad - inner)).astype(low)
    residual = residual_ref[...]
    factor = lax.rsqrt(jnp.mean(residual * residual, axis=-1, keepdims=True) + epsilon)
    moe_low = (residual * factor * moe_gain[...]).astype(low)
    router = jnp.concatenate(
        [router_ref[...], jnp.zeros((128 - experts, width), low)], axis=0
    )
    moe_grad = entry + jnp.dot(logit_grad, router, preferred_element_type=wide)
    small_own[:8, :] = jnp.zeros((8, width), wide)
    small_own[8:, :] = tn_dot(logit_grad, moe_low)[: small_own.shape[0] - 8]
    scaled = moe_grad * moe_gain[...]
    inner = jnp.mean(scaled * residual, axis=-1, keepdims=True)
    small_own[1:2, :] = jnp.sum(moe_grad * residual * factor, axis=0, keepdims=True)
    residual_grad[...] = dealt_rows(True) + factor * (
        scaled - residual * (factor * factor) * inner
    )
    low_all[core, tp] = residual_grad[...].astype(low)
    mine = low_all.at[core, tp]
    share_mate = remote(mine, mine, share_send.at[0], share_recv.at[0], place.mate)
    share_across = remote(mine, mine, share_send.at[1], share_recv.at[1], place.across)
    share_across.start()
    share_mate.start()
    units = gate_arrived.shape[1]
    pair_copies = [
        remote(
            part.at[:, lanes_at(1 - tp, units)],
            arrived,
            pair_send.at[i],
            pair_recv.at[i],
            place.across,
        )
        for i, (part, arrived) in enumerate(((gate_part, gate_arrived), (up_part, up_arrived)))
    ]
    pair_copies.append(
        remote(
            down_part.at[lanes_at(1 - tp, units)],
            down_arrived,
            pair_send.at[2],
            pair_recv.at[2],
            place.across,
        )
    )
    pair_copies[0].start()

    lanes = out_own.shape[1]
    weight_ring = ChainSum(
        place,
        lambda chip: out_grad.at[:, lanes_at(chip, 2 * lanes)],
        weight_side,
        weight_chain,
        weight_hop,
        ring_sems[10:20],
    )
    query_ring = ChainSum(
        place, lambda chip: out_sums.at[chip], out_side, out_chain, out_hop, ring_sems[20:30]
    )
    narrow_ring = ChainSum(
        place,
        lambda chip: narrow_grad.at[chip],
        narrow_side,
        narrow_chain,
        narrow_hop,
        ring_sems[30:],
    )
    lax.fori_loop(1, place.levels, join, 0)
    out_ring.send_joined()
    other = low_all.at[core, 1 - tp]
    remote(other, other, share_send.at[1], share_recv.at[1], place.across).wait_recv()
    passed = remote(other, other, share_send.at[2], share_recv.at[2], place.mate)
    passed.start()
    for slot, piece in ((0, low_all.at[1 - core, tp]), (2, low_all.at[1 - core, 1 - tp])):
        remote(piece, piece, share_send.at[slot], share_recv.at[slot], place.mate).wait_recv()

    def out_grad_rows(index, carry):
        at = lanes_at(index, 256)
        left = mixed_ref[:, at]
        for first in range(0, width, 512):
            out_grad[at, first : first + 512] = tn_dot(
                left, low_all[:, :, :, first : first + 512].reshape(rows, 512)
            ).astype(low)
        return carry

    loads[0].wait()
    lax.fori_loop(0, mixed_ref.shape[1] // 256, out_grad_rows, 0)
    for turn in range(place.levels):
        weight_ring.send(weight_ring.target(turn))

    def mixed_lanes(index, carry):
        at = lanes_at(index, 256)
        mixed_grad[:, at] = nt_dot(low_all[...].reshape(rows, width), out_w[at, :]).astype(low)
        return carry

    loads[1].wait()
    lax.fori_loop(0, mixed_ref.shape[1] // 256, mixed_lanes, 0)
    for load in loads[2:]:
        load.wait()
    key_total[...] = jnp.zeros_like(key_total)
    value_total[...] = jnp.zeros_like(value_total)
    query_gain_part[...] = jnp.zeros_like(query_gain_part)

    def pre_back(grad, values, gain_ref, cosine, sine):
        grad = grad * cosine - pltpu.roll(grad, head // 2, 1) * sine
        factor = lax.rsqrt(jnp.mean(values * values, axis=-1, keepdims=True) + epsilon)
        scaled = grad * gain_ref[...]
        inner = jnp.mean(scaled * values, axis=-1, keepdims=True)
        back = factor * (scaled - values * (factor * factor) * inner)
        return back.astype(low), jnp.sum(grad * values * factor, axis=0, keepdims=True)

    batch = 4

    def attend_back(index, carry):
        which = index // (heads // batch)
        first = (index % (heads // batch)) * batch
        at_rows = lanes_at(which, group)
        key = key_low[at_rows, :]
        value = value_low[at_rows, :]
        cosine, sine = cosine_ref[at_rows, :], sine_ref[at_rows, :]
        key_sum = key_total[at_rows, :]
        value_sum = value_total[at_rows, :]
        gain_sum = query_gain_part[...]
        for offset in range(batch):
            at = lanes_at(first + offset, head)
            probs = probs_ref[which * heads + first + offset]
            grads = mixed_grad[at_rows, at]
            prob_grad = nt_dot(grads, value)
            probs_wide = probs.astype(wide)
            inner = jnp.sum(probs_wide * prob_grad, axis=-1, keepdims=True)
            score_grad = (probs_wide * (prob_grad - inner)).astype(low)
            query = jnp.dot(score_grad, key, preferred_element_type=wide) * scale
            key_sum += tn_dot(score_grad, query_low[at_rows, at])
            value_sum += tn_dot(probs, grads)
            values = query_pre[at_rows, at].astype(wide)
            back, terms = pre_back(query, values, query_gain, cosine, sine)
            low_grads[at_rows, at] = back
            gain_sum += terms
        key_total[at_rows, :] = key_sum
        value_total[at_rows, :] = value_sum
        query_gain_part[...] = gain_sum
        return carry

    count = 2 * heads // batch
    share = -(-count // place.levels)
    for turn in range(place.levels):
        out_ring.take_side(out_ring.target(turn))
        lax.fori_loop(min(turn * share, count), min((turn + 1) * share, count), attend_back, 0)
        out_ring.take_chain(out_ring.target(turn))

    weight_ring.send_joined()
    back, terms = pre_back(
        key_total[...] * scale, key_pre[...], key_gain, cosine_ref[...], sine_ref[...]
    )
    small_own[2:3, :head] = query_gain_part[...]
    small_own[2:3, head : 2 * head] = terms
    low_grads[:, heads * head : (heads + 1) * head] = back
    low_grads[:, (heads + 1) * head :] = value_total[...].astype(low)

    def normed_grad_rows(whose):
        at_rows = lanes_at(whose, group)

        def normed_grad_lanes(index, carry):
            at = lanes_at(index, 512)
            grads = low_grads[at_rows, :]
            product = (
                nt_dot(grads[:, : heads * head], query_w[at, :])
                + nt_dot(grads[:, heads * head : (heads + 1) * head], key_w[at, :])
                + nt_dot(grads[:, (heads + 1) * head :], value_w[at, :])
            )
            low_all[whose, :, :, at] = product.astype(low).reshape(2, own_rows, 512)
            return carry

        lax.fori_loop(0, width // 512, normed_grad_lanes, 0)

    share_mate.wait_send()
    share_across.wait_send()
    passed.wait_send()
    sums = QuadSum(place, low_all, near, pair, far, quad_send, quad_recv)
    normed_grad_rows(1 - core)
    sums.start()
    normed_grad_rows(core)
    sums.relay()
    out_ring.close()
    moe_own = out_side[level].astype(wide)
    finished_ref[:, :half] = (residual_ref[...] + moe_own).reshape(members, half, width).astype(low)
    out_ring.drain()
    for target in place.ring_targets():
        pl.semaphore_signal(
            free_sem, inc=1, device_id=target, device_id_type=pl.DeviceIdType.MESH
        )

    def weight_grad_rows(index, carry):
        left = normed_ref[:, :, :, lanes_at(index, group)].reshape(rows, group)
        for first in range(0, heads * head, 512):
            grads = tn_dot(left, low_grads[:, first : first + 512]).astype(low)
            out_sums[index, :, first : first + 512] = grads[:own_rows]
            second = heads * head + first
            out_sums[index, :, second : second + 512] = grads[own_rows:]
        narrow_grad[index] = tn_dot(left, low_grads[:, heads * head :]).astype(low)
        return carry

    weight_ring.take_side(weight_ring.target(0))
    lax.fori_loop(0, place.chips, weight_grad_rows, 0)
    weight_ring.take_chain(weight_ring.target(0))
    normed_grad = sums.total()
    tokens = dealt_rows(False)
    factor = lax.rsqrt(jnp.mean(tokens * tokens, axis=-1, keepdims=True) + epsilon)
    scaled = normed_grad * attn_gain[...]
    inner = jnp.mean(scaled * tokens, axis=-1, keepdims=True)
    small_own[0:1, :] = jnp.sum(normed_grad * tokens * factor, axis=0, keepdims=True)
    small_across = remote(
        small_own, small_near, small_send.at[0], small_recv.at[0], place.across
    )
    small_across.start()
    pair_copies[1].start()
    pair_copies[2].start()
    token_grad = residual_grad[...] + factor * (scaled - tokens * (factor * factor) * inner)
    finished_ref[:, half:] = token_grad.reshape(members, half, width).astype(low)

    def deal_copy(offset, sending):
        target, index = place.member(offset if sending else -offset)
        return remote(
            finished_ref.at[index],
            returned_ref.at[place.fsdp if sending else index],
            deal_send.at[offset - 1],
            deal_recv.at[offset - 1],
            target,
        )

    share_lanes = width // members

    def small_copy(offset, sending):
        target, index = place.member(offset if sending else -offset)
        return remote(
            small_pair.at[:, lanes_at(index, share_lanes)],
            small_parts.at[place.fsdp if sending else index],
            small_send.at[offset],
            small_recv.at[offset],
            target,
        )

    def total_copy(offset, sending):
        target, index = place.member(offset if sending else -offset)
        piece = small_ref.at[:, lanes_at(place.fsdp if sending else index, share_lanes)]
        return remote(piece, piece, total_send.at[offset], total_recv.at[offset], target)

    weight_ring.take_side(weight_ring.target(1))
    small_across.wait_recv()
    small_pair[...] = small_own[...] + small_near[...]
    for offset in range(1, members):
        small_copy(offset, True).start()
    for offset in range(1, members):
        deal_copy(offset, True).start()
    own_slice = pltpu.make_async_copy(
        finished_ref.at[place.fsdp], returned_ref.at[place.fsdp], keep_sem.at[0]
    )
    own_slice.start()
    pl.semaphore_wait(free_sem, len(place.ring_targets()))
    last_rings = (query_ring, narrow_ring)
    for turn in range(place.levels):
        for ring in last_rings:
            ring.send(ring.target(turn))

    weight_ring.take_chain(weight_ring.target(1))
    for turn in range(2, place.levels):
        weight_ring.take_side(weight_ring.target(turn))
        weight_ring.take_chain(weight_ring.target(turn))
    weight_ring.close()
    for ring in last_rings:
        ring.send_joined()

    def swap_with_mate(slot, mine, theirs, here, there):
        kept = pltpu.make_async_copy(mine, here, keep_sem.at[slot])
        sent = remote(theirs, here, swap_send.at[slot], swap_recv.at[slot], place.mate)
        sent.start()
        kept.start()

        def finish():
            kept.wait()
            remote(there, there, swap_send.at[slot], swap_recv.at[slot], place.mate).wait_recv()
            sent.wait_send()

        return finish

    head_rows = out_grad.shape[0]
    finish_out = swap_with_mate(
        1,
        weight_side.at[level, :, lanes_at(core, lanes)],
        weight_side.at[level, :, lanes_at(1 - core, lanes)],
        out_own.at[lanes_at(core, head_rows)],
        out_own.at[lanes_at(1 - core, head_rows)],
    )
    for offset in range(1, members):
        small_copy(offset, False).wait_recv()
    small_parts[place.fsdp] = small_pair[:, lanes_at(place.fsdp, share_lanes)]
    total = small_parts[0]
    for member in range(1, members):
        total += small_parts[member]
    small_ref[:, lanes_at(place.fsdp, share_lanes)] = total
    for offset in range(1, members):
        total_copy(offset, True).start()
    for turn in range(place.levels):
        for ring in last_rings:
            ring.take_side(ring.target(turn))
            ring.take_chain(ring.target(turn))
    own_slice.wait()
    for offset in range(1, members):
        deal_copy(offset, False).wait_recv()
    for index in range(members):
        block = returned_ref[back_ref[index]].astype(wide)
        token_grad_ref[index] = block[half:]
        output_ref[index] = block[:half].astype(low)
    for ring in last_rings:
        ring.close()
    span = heads * head
    finish_query = swap_with_mate(
        2,
        out_side.at[level, :, lanes_at(core, span)],
        out_side.at[level, :, lanes_at(1 - core, span)],
        query_own.at[:, lanes_at(core, span)],
        query_own.at[:, lanes_at(1 - core, span)],
    )
    finish_narrow = [
        swap_with_mate(
            3 + i,
            narrow_side.at[level, lanes_at(core, own_rows), pl.ds(i * head, head)],
            narrow_side.at[level, lanes_at(1 - core, own_rows), pl.ds(i * head, head)],
            own.at[:, lanes_at(core, head)],
            own.at[:, lanes_at(1 - core, head)],
        )
        for i, own in enumerate((key_own, value_own))
    ]
    finish_out()
    finish_query()
    for finish in finish_narrow:
        finish()
    small_across.wait_send()
    for offset in range(1, members):
        deal_copy(offset, True).wait_send()
        small_copy(offset, True).wait_send()
        total_copy(offset, True).wait_send()
        total_copy(offset, False).wait_recv()
    for copy in pair_copies:
        copy.wait()

    def offered(origin, carry):
        to_mate(origin).wait_send()
        return carry

    lax.fori_loop(0, place.chips, offered, 0)
    sums.drain()
    for ring in (weight_ring, query_ring, narrow_ring):
        ring.drain()


def attend_back_layer(
    experts,
    entry,
    residual,
    gates,
    dealt,
    back_pick,
    router,
    gain_vecs,
    mixed,
    probs,
    query_low,
    key_low,
    value_low,
    query_pre,
    key_pre,
    tables,
    normed,
    query_w,
    key_w,
    value_w,
    out_w,
    out_part,
    gate_part,
    up_part,
    down_part,
):
    own_rows, width = residual.shape
    members = dealt.shape[0]
    levels = members // 4
    rows = 4 * own_rows
    heads_width, head = query_w.shape[1], key_w.shape[1]
    lanes = width // members
    wide, low = jnp.float32, jnp.bfloat16
    vmem = pl.BlockSpec(memory_space=pltpu.VMEM)
    anywhere = pl.BlockSpec(memory_space=pl.ANY)
    shape = jax.ShapeDtypeStruct
    dma = pltpu.SemaphoreType.DMA
    small = (8 + -(-experts // 8) * 8, width)
    late = (mixed, out_w, probs, query_low, query_pre, query_w, key_w, value_w, normed)
    return pl.pallas_call(
        functools.partial(attend_back_kernel, experts),
        name="attend_back_layer",
        out_shape=[
            shape((members, dealt.shape[1] // 2, width), low),
            shape((members, dealt.shape[1] // 2, width), wide),
            shape(small, wide),
            shape((own_rows, 2 * heads_width), low),
            shape((own_rows, 2 * head), low),
            shape((own_rows, 2 * head), low),
            shape((2 * heads_width, lanes), low),
            shape((width, gate_part.shape[1] // 2), low),
            shape((width, up_part.shape[1] // 2), low),
            shape((down_part.shape[0] // 2, width), low),
        ],
        in_specs=[vmem] * 4
        + [pl.BlockSpec(memory_space=pltpu.SMEM)]
        + [vmem] * 10
        + [anywhere] * 13,
        out_specs=[vmem] * 7 + [anywhere] * 3,
        scratch_shapes=[
            pltpu.VMEM(dealt.shape, low),
            pltpu.VMEM(dealt.shape, low),
            pltpu.VMEM(small, wide),
            pltpu.VMEM(small, wide),
            pltpu.VMEM(small, wide),
            pltpu.VMEM((members, small[0], width // members), wide),
            pltpu.VMEM((1, head), wide),
        ]
        + [pltpu.VMEM(array.shape, low) for array in late]
        + [
            pltpu.VMEM((own_rows, width), wide),
            pltpu.VMEM((2, 2, own_rows, width), low),
            pltpu.VMEM((rows, heads_width), low),
            pltpu.VMEM((rows, heads_width + 2 * head), low),
            pltpu.VMEM((rows, head), wide),
            pltpu.VMEM((rows, head), wide),
            pltpu.VMEM((heads_width, width), low),
            pltpu.VMEM((members // 2, own_rows, width), low),
            pltpu.VMEM((members // 2, own_rows, width), low),
            *ChainSum.buffers(levels, (own_rows, width)),
            *ChainSum.buffers(levels, (heads_width, 2 * lanes)),
            pltpu.VMEM((members // 2, 2 * own_rows, 2 * head), low),
            *ChainSum.buffers(levels, (2 * own_rows, 2 * head)),
        ]
        + QuadSum.scratch(own_rows, width)
        + [dma((3,)), dma((3,)), dma((5,)), dma((5,)), dma((5,)), dma((3,)), dma((3,))]
        + [dma((members,))] * 6
        + [pltpu.SemaphoreType.REGULAR, dma((9,)), dma((members // 2,)), dma((members // 2,))]
        + ChainSum.semaphores(levels) * 4,
        compiler_params=pltpu.CompilerParams(
            collective_id=3, has_side_effects=True, vmem_limit_bytes=65_400_000
        ),
        cost_estimate=link_cost(185),
    )(
        entry,
        residual,
        gates,
        dealt,
        back_pick,
        router,
        *gain_vecs,
        key_low,
        value_low,
        key_pre,
        *tables,
        *late,
        out_part,
        gate_part,
        up_part,
        down_part,
    )


def fast_body(
    tokens,
    lengths,
    routes,
    deal_order,
    cotangent,
    attn_gain,
    query_gain,
    key_gain,
    moe_gain,
    w_query,
    key_projection_matrix,
    value_projection_matrix,
    w_out,
    w_router,
    w_gate,
    w_up,
    w_down,
):
    own_rows, model_width = tokens.shape
    head_dim = query_gain.shape[0]
    chip_count = lax.axis_size("chip")
    core_count = lax.axis_size("core")
    tp_count = lax.axis_size("tp")
    core_index = lax.axis_index("core")
    tp_index = lax.axis_index("tp")
    fsdp_count = chip_count * core_count
    fsdp_index = lax.axis_index("chip") * core_count + core_index
    slice_rows = own_rows // fsdp_count
    group_rows = tp_count * own_rows
    quad_rows = core_count * group_rows
    plane = ("chip", "core")
    quad = ("core", "tp")
    peer_ids = jnp.arange(fsdp_count, dtype=jnp.int32)
    wanted = (peer_ids - fsdp_index) % fsdp_count
    send_pick = jnp.sum(
        jnp.where(deal_order[None, :] == wanted[:, None], peer_ids[None, :], 0), axis=1
    )
    back_pick = (deal_order + fsdp_index) % fsdp_count

    def slices_of(values):
        return values.reshape(fsdp_count, slice_rows, model_width)

    down_full = lax.all_gather(w_down[0], "tp", axis=0, tiled=True)
    frequency = rope_base ** (-(jnp.arange(head_dim // 2, dtype=jnp.float32) * (2.0 / head_dim)))
    frequency = jnp.concatenate([frequency, frequency])[None, :]
    padded_lengths = jnp.pad(lengths, ((0, 7), (0, 128 - lengths.shape[1])))
    experts = w_router.shape[1]
    router_rows = w_router.T
    (
        dealt,
        normed,
        cosine_wide,
        sine_wide,
        moe_ext,
        residual,
        gates,
        query_pre,
        query_low,
        key_before_norm,
        key_low,
        value_low,
        probs_low,
        mixed_low,
        upstream_all,
        query_part,
        key_part,
        value_part,
        out_part,
        gate_full,
        up_full,
    ) = front_layer(
        experts,
        lengths.shape[1],
        slices_of(tokens),
        slices_of(cotangent),
        send_pick,
        attn_gain[None, :],
        padded_lengths,
        frequency,
        (query_gain[None, :], key_gain[None, :], moe_gain[None, :]),
        router_rows,
        routes,
        w_query,
        key_projection_matrix,
        value_projection_matrix,
        w_out,
        w_gate[0],
        w_up[0],
    )
    query_part = query_part.reshape(model_width, -1)
    key_part = key_part.reshape(model_width, -1)
    value_part = value_part.reshape(model_width, -1)
    upstream_all = upstream_all.reshape(fsdp_count * own_rows, model_width)
    entry_ext, moe_out, grad_w_gate, grad_w_up, grad_w_down = expert_layer(
        moe_ext, upstream_all, gate_full, up_full, down_full, experts
    )
    (
        output,
        grad_input,
        small,
        grad_w_query,
        grad_w_key,
        grad_w_value,
        grad_w_out,
        gate_arrived,
        up_arrived,
        down_arrived,
    ) = attend_back_layer(
        experts,
        entry_ext,
        residual,
        gates,
        dealt,
        back_pick,
        router_rows,
        (attn_gain[None, :], moe_gain[None, :], query_gain[None, :], key_gain[None, :]),
        mixed_low,
        probs_low,
        query_low,
        key_low,
        value_low,
        query_pre,
        key_before_norm,
        (cosine_wide, sine_wide),
        normed,
        query_part,
        key_part,
        value_part,
        out_part,
        moe_out.reshape(chip_count, core_count, own_rows, model_width),
        grad_w_gate,
        grad_w_up,
        grad_w_down,
    )
    def pair_sum(parts, arrived, dim):
        first, second = jnp.split(parts, 2, axis=dim)
        mine = jnp.where(tp_index == 0, first, second)
        return mine.astype(jnp.float32) + arrived.astype(jnp.float32)

    output = output.reshape(own_rows, model_width)
    grad_input = grad_input.reshape(own_rows, model_width)
    grad_w_router = small[8 : 8 + experts].T
    return (
        output,
        grad_input,
        small[0],
        small[2, :head_dim],
        small[2, head_dim : 2 * head_dim],
        small[1],
        grad_w_query.astype(jnp.float32),
        grad_w_key.astype(jnp.float32),
        grad_w_value.astype(jnp.float32),
        grad_w_out.astype(jnp.float32),
        grad_w_router,
        pair_sum(grad_w_gate, gate_arrived, 1)[None],
        pair_sum(grad_w_up, up_arrived, 1)[None],
        pair_sum(grad_w_down, down_arrived, 0)[None],
    )


def solution(mesh):
    fsdp_count, tp_count = mesh.shape["fsdp"], mesh.shape["tp"]
    chips = Mesh(mesh.devices.reshape(fsdp_count // 2, 2, tp_count), ("chip", "core", "tp"))
    dense = fsdp_count <= 16
    fsdp = ("chip", "core") if dense else "fsdp"
    every = ("chip", "core", "tp") if dense else ("fsdp", "tp")
    return jax.shard_map(
        fast_body if dense else body,
        mesh=chips if dense else mesh,
        in_specs=(
            P(every, None),
            P(fsdp, None),
            P(fsdp, None),
            P(),
            P(every, None),
            P(),
            P(),
            P(),
            P(),
            P(fsdp, "tp"),
            P(fsdp, "tp"),
            P(fsdp, "tp"),
            P("tp", fsdp),
            P(),
            P(fsdp, None, "tp"),
            P(fsdp, None, "tp"),
            P(fsdp, "tp", None),
        ),
        out_specs=(
            P(every, None),
            P(every, None),
            P(),
            P(),
            P(),
            P(),
            P(fsdp, "tp"),
            P(fsdp, "tp"),
            P(fsdp, "tp"),
            P("tp", fsdp),
            P(),
            P(fsdp, None, "tp"),
            P(fsdp, None, "tp"),
            P(fsdp, "tp", None),
        ),
        check_vma=False,
    )
```

```python
import functools

import jax
import jax.numpy as jnp
from jax import lax
from jax.experimental import pallas as pl
from jax.experimental.pallas import tpu as pltpu
from jax.sharding import Mesh
from jax.sharding import PartitionSpec as P

epsilon = 1e-06
rope_base = 1000000.0
masked_score = -1e30


def row_norm(values, gain_vec):
    factor = lax.rsqrt(jnp.mean(values * values, axis=-1, keepdims=True) + epsilon)
    return (values * factor * gain_vec, factor)


def norm_back(values, factor, gain_vec, upstream):
    scaled = upstream * gain_vec
    inner_term = jnp.mean(scaled * values, axis=-1, keepdims=True)
    return (factor * (scaled - values * (factor * factor) * inner_term), upstream * values * factor)


def seq_layout(seq_lengths, row_count):
    seq_ends = jnp.cumsum(seq_lengths)
    row_ids = jnp.arange(row_count, dtype=jnp.int32)
    segment = jnp.sum((row_ids[:, None] >= seq_ends[None, :]).astype(jnp.int32), axis=1)
    seq_starts = seq_ends - seq_lengths
    chosen = segment[:, None] == jnp.arange(seq_lengths.shape[0], dtype=jnp.int32)[None, :]
    position = row_ids - jnp.sum(jnp.where(chosen, seq_starts[None, :], 0), axis=1)
    return (segment, position)


def rotary(position, head_width):
    half_width = head_width // 2
    inverse_freq = rope_base ** (-(jnp.arange(half_width, dtype=jnp.float32) * (2.0 / head_width)))
    angles = position.astype(jnp.float32)[:, None] * inverse_freq[None, :]
    return (jnp.cos(angles)[:, None, :], jnp.sin(angles)[:, None, :])


def rotate(values, cosine_table, sine_table):
    half_width = values.shape[-1] // 2
    front_half = values[..., :half_width]
    back_half = values[..., half_width:]
    return jnp.concatenate(
        [
            front_half * cosine_table - back_half * sine_table,
            back_half * cosine_table + front_half * sine_table,
        ],
        axis=-1,
    )


def rotate_back(upstream, cosine_table, sine_table):
    half_width = upstream.shape[-1] // 2
    front_half = upstream[..., :half_width]
    back_half = upstream[..., half_width:]
    return jnp.concatenate(
        [
            front_half * cosine_table + back_half * sine_table,
            back_half * cosine_table - front_half * sine_table,
        ],
        axis=-1,
    )


def slot_table(route_rows, expert_count, capacity):
    row_count = route_rows.shape[0] * route_rows.shape[1]
    flat_routes = route_rows.reshape(row_count)
    expert_hits = (
        flat_routes[:, None] == jnp.arange(expert_count, dtype=jnp.int32)[None, :]
    ).astype(jnp.int32)
    earlier = jnp.cumsum(expert_hits, axis=0) - expert_hits
    slot_index = jnp.sum(earlier * expert_hits, axis=1)
    slot_place = flat_routes * capacity + slot_index
    slot_rows = jnp.full((expert_count * capacity,), row_count, jnp.int32)
    slot_rows = slot_rows.at[slot_place].set(jnp.arange(row_count, dtype=jnp.int32))
    return (slot_place, slot_rows.reshape(expert_count, capacity))


def contract_rows(left, right):
    return lax.dot_general(
        left, right, (((0,), (0,)), ((), ())), preferred_element_type=jnp.float32
    )


def contract_last(left, right):
    return lax.dot_general(
        left, right, (((1,), (1,)), ((), ())), preferred_element_type=jnp.float32
    )


def body(
    tokens,
    lengths,
    routes,
    deal_order,
    cotangent,
    attn_gain,
    query_gain,
    key_gain,
    moe_gain,
    w_query,
    key_projection_matrix,
    value_projection_matrix,
    w_out,
    w_router,
    w_gate,
    w_up,
    w_down,
):
    half_rows = tokens.shape[0]
    model_width = tokens.shape[1]
    head_dim = query_gain.shape[0]
    score_scale = head_dim ** (-0.5)
    fsdp_count = lax.axis_size("fsdp")
    tp_count = lax.axis_size("tp")
    fsdp_index = lax.axis_index("fsdp")
    tp_index = lax.axis_index("tp")
    slice_rows = half_rows // fsdp_count
    group_rows = tp_count * half_rows
    own_start = tp_index * half_rows
    peer_ids = jnp.arange(fsdp_count, dtype=jnp.int32)
    wanted = (peer_ids - fsdp_index) % fsdp_count
    send_pick = jnp.sum(
        jnp.where(deal_order[None, :] == wanted[:, None], peer_ids[None, :], 0), axis=1
    )
    back_pick = (deal_order + fsdp_index) % fsdp_count

    def deal_copies(values):
        slices = jnp.take(values.reshape(fsdp_count, slice_rows, model_width), send_pick, axis=0)
        return jnp.broadcast_to(slices[None], (tp_count, fsdp_count, slice_rows, model_width))

    tokens_all, cotangent_all = (
        lax.all_to_all(
            lax.all_to_all(deal_copies(tokens), "tp", split_axis=0, concat_axis=0, tiled=True),
            "fsdp",
            split_axis=1,
            concat_axis=1,
            tiled=True,
        ),
        lax.all_to_all(
            lax.all_to_all(deal_copies(cotangent), "tp", split_axis=0, concat_axis=0, tiled=True),
            "fsdp",
            split_axis=1,
            concat_axis=1,
            tiled=True,
        ),
    )
    tokens_in = tokens_all.reshape(group_rows, model_width).astype(jnp.float32)
    upstream = cotangent_all.reshape(group_rows, model_width).astype(jnp.float32)
    attn_in, attn_factor = row_norm(tokens_in, attn_gain)
    normed_all = attn_in.astype(jnp.bfloat16)
    query_full, key_full, value_full, out_full = (
        lax.all_gather(w_query, "fsdp", axis=0, tiled=True),
        lax.all_gather(key_projection_matrix, "fsdp", axis=0, tiled=True),
        lax.all_gather(value_projection_matrix, "fsdp", axis=0, tiled=True),
        lax.all_gather(w_out, "fsdp", axis=1, tiled=True),
    )
    query_heads = query_full.shape[1] // head_dim
    kv_heads = key_full.shape[1] // head_dim
    group_size = query_heads // kv_heads
    segment, position = seq_layout(lengths[0], group_rows)
    cosine_table, sine_table = rotary(position, head_dim)
    row_ids = jnp.arange(group_rows)
    allowed = (segment[:, None] == segment[None, :]) & (row_ids[None, :] <= row_ids[:, None])
    query_pre = jnp.dot(normed_all, query_full, preferred_element_type=jnp.float32).reshape(
        group_rows, query_heads, head_dim
    )
    query_normed, query_factor = row_norm(query_pre, query_gain)
    query_low = (
        rotate(query_normed, cosine_table, sine_table)
        .astype(jnp.bfloat16)
        .reshape(group_rows, kv_heads, group_size, head_dim)
    )
    key_before_norm = jnp.dot(normed_all, key_full, preferred_element_type=jnp.float32).reshape(
        group_rows, kv_heads, head_dim
    )
    key_normed, key_factor = row_norm(key_before_norm, key_gain)
    key_low = rotate(key_normed, cosine_table, sine_table).astype(jnp.bfloat16)
    value_low = (
        jnp.dot(normed_all, value_full, preferred_element_type=jnp.float32)
        .astype(jnp.bfloat16)
        .reshape(group_rows, kv_heads, head_dim)
    )
    scores = (
        jnp.einsum("qkgd,tkd->kgqt", query_low, key_low, preferred_element_type=jnp.float32)
        * score_scale
    )
    scores = jnp.where(allowed, scores, masked_score)
    row_peak = jnp.max(scores, axis=-1, keepdims=True)
    exponent = jnp.exp(scores - row_peak)
    totals = jnp.sum(exponent, axis=-1, keepdims=True)
    log_total = row_peak + jnp.log(totals)
    attn_probs = (exponent / totals).astype(jnp.bfloat16)
    attn_mixed = jnp.einsum(
        "kgqt,tkd->qkgd", attn_probs, value_low, preferred_element_type=jnp.float32
    )
    mixed_low = attn_mixed.reshape(group_rows, query_heads * head_dim).astype(jnp.bfloat16)
    attn_part = jnp.dot(mixed_low, out_full, preferred_element_type=jnp.float32)
    residual = tokens_in + lax.psum(attn_part, "tp")
    moe_in, moe_factor = row_norm(residual, moe_gain)
    moe_low = moe_in.astype(jnp.bfloat16)
    logits = jnp.dot(moe_low, w_router, preferred_element_type=jnp.float32)
    experts = w_router.shape[1]
    top_count = routes.shape[1]
    chosen = routes[:, :, None] == jnp.arange(experts, dtype=jnp.int32)[None, None, :]
    selected = jnp.sum(jnp.where(chosen, logits[:, None, :], 0.0), axis=-1)
    gate_peak = jnp.max(selected, axis=-1, keepdims=True)
    gate_exp = jnp.exp(selected - gate_peak)
    gate_probs = gate_exp / jnp.sum(gate_exp, axis=-1, keepdims=True)
    capacity = max(2, 3 * group_rows * top_count // (2 * experts))
    slot_place, slot_rows = slot_table(routes, experts, capacity)
    part_cap = capacity // tp_count
    slot_start = tp_index * part_cap
    gate_full, up_full, down_full = (
        lax.all_gather(w_gate, "tp", axis=2, tiled=True),
        lax.all_gather(w_up, "tp", axis=2, tiled=True),
        lax.all_gather(w_down, "tp", axis=1, tiled=True),
    )
    sent_rows = lax.dynamic_slice_in_dim(slot_rows, slot_start, part_cap, 1)
    slot_expert = slot_place // capacity
    slot_offset = slot_place % capacity - slot_start
    in_half = (slot_offset >= 0) & (slot_offset < part_cap)
    local_place = jnp.where(in_half, slot_expert * part_cap + slot_offset, experts * part_cap)
    padded = jnp.concatenate([moe_low, jnp.zeros((1, model_width), jnp.bfloat16)], axis=0)
    arrived = lax.all_to_all(
        padded[sent_rows // top_count], "fsdp", split_axis=0, concat_axis=0, tiled=True
    )
    local_experts = w_gate.shape[0]
    sources = experts // local_experts
    slot_count = sources * part_cap
    ff_part = w_gate.shape[2]

    def to_experts(values):
        return jnp.transpose(
            values.reshape(sources, local_experts, part_cap, model_width), (1, 0, 2, 3)
        ).reshape(local_experts, slot_count, model_width)

    def to_sources(values):
        width = values.shape[-1]
        return jnp.transpose(
            values.reshape(local_experts, sources, part_cap, width), (1, 0, 2, 3)
        ).reshape(experts, part_cap, width)

    def pick_rows(values):
        flat = values.reshape(experts * part_cap, tp_count * model_width)
        flat = jnp.concatenate([flat, jnp.zeros((1, tp_count * model_width), jnp.bfloat16)], axis=0)
        gathered = flat[local_place].reshape(group_rows, top_count, tp_count, model_width)
        return jnp.sum(gathered.astype(jnp.float32), axis=2)

    expert_rows = to_experts(arrived)
    gate_val = jnp.einsum(
        "esd,edf->esf", expert_rows, gate_full, preferred_element_type=jnp.float32
    )
    up_val = jnp.einsum("esd,edf->esf", expert_rows, up_full, preferred_element_type=jnp.float32)
    sigmoid_val = jax.nn.sigmoid(gate_val)
    swish_val = gate_val * sigmoid_val
    hidden_low = (swish_val * up_val).astype(jnp.bfloat16)
    hidden_blocks = hidden_low.reshape(local_experts, slot_count, tp_count, ff_part)
    down_blocks = down_full.reshape(local_experts, tp_count, ff_part, model_width)
    expert_out = (
        jnp.einsum(
            "esbf,ebfd->esbd", hidden_blocks, down_blocks, preferred_element_type=jnp.float32
        )
        .astype(jnp.bfloat16)
        .reshape(local_experts, slot_count, tp_count * model_width)
    )
    returned = lax.all_to_all(
        to_sources(expert_out), "fsdp", split_axis=0, concat_axis=0, tiled=True
    )
    picked = pick_rows(returned)
    moe_part = jnp.sum(gate_probs[:, :, None] * picked, axis=1)
    gate_grad_part = jnp.sum(upstream[:, None, :] * picked, axis=-1)
    weighted = (
        (gate_probs[:, :, None] * upstream[:, None, :])
        .astype(jnp.bfloat16)
        .reshape(group_rows * top_count, model_width)
    )
    weighted = jnp.concatenate([weighted, jnp.zeros((1, model_width), jnp.bfloat16)], axis=0)
    grad_arrived = lax.all_to_all(
        weighted[sent_rows], "fsdp", split_axis=0, concat_axis=0, tiled=True
    )
    grad_slots = to_experts(grad_arrived)
    hidden_grad = jnp.einsum(
        "esd,ebfd->esbf", grad_slots, down_blocks, preferred_element_type=jnp.float32
    ).reshape(local_experts, slot_count, tp_count * ff_part)
    swish_slope = sigmoid_val * (1.0 + gate_val * (1.0 - sigmoid_val))
    gate_val_grad = (hidden_grad * up_val * swish_slope).astype(jnp.bfloat16)
    up_val_grad = (hidden_grad * swish_val).astype(jnp.bfloat16)
    grad_w_down = jnp.einsum(
        "esbf,esd->ebfd", hidden_blocks, grad_slots, preferred_element_type=jnp.float32
    ).reshape(local_experts, tp_count * ff_part, model_width)
    grad_w_gate = jnp.einsum(
        "esd,esf->edf", expert_rows, gate_val_grad, preferred_element_type=jnp.float32
    )
    grad_w_up = jnp.einsum(
        "esd,esf->edf", expert_rows, up_val_grad, preferred_element_type=jnp.float32
    )
    gate_blocks = gate_full.reshape(local_experts, model_width, tp_count, ff_part)
    up_blocks = up_full.reshape(local_experts, model_width, tp_count, ff_part)
    entry_grad = (
        (
            jnp.einsum(
                "esbf,edbf->esbd",
                gate_val_grad.reshape(local_experts, slot_count, tp_count, ff_part),
                gate_blocks,
                preferred_element_type=jnp.float32,
            )
            + jnp.einsum(
                "esbf,edbf->esbd",
                up_val_grad.reshape(local_experts, slot_count, tp_count, ff_part),
                up_blocks,
                preferred_element_type=jnp.float32,
            )
        )
        .astype(jnp.bfloat16)
        .reshape(local_experts, slot_count, tp_count * model_width)
    )
    sent_back = lax.all_to_all(
        to_sources(entry_grad), "fsdp", split_axis=0, concat_axis=0, tiled=True
    )
    expert_grad = jnp.sum(pick_rows(sent_back), axis=1)
    grad_w_gate, grad_w_up, grad_w_down = (
        lax.psum_scatter(
            grad_w_gate.astype(jnp.bfloat16), "tp", scatter_dimension=2, tiled=True
        ).astype(jnp.float32),
        lax.psum_scatter(
            grad_w_up.astype(jnp.bfloat16), "tp", scatter_dimension=2, tiled=True
        ).astype(jnp.float32),
        lax.psum_scatter(
            grad_w_down.astype(jnp.bfloat16), "tp", scatter_dimension=1, tiled=True
        ).astype(jnp.float32),
    )
    moe_grad, gate_grad = (
        lax.psum(expert_grad.astype(jnp.bfloat16), "tp").astype(jnp.float32),
        lax.psum(gate_grad_part.astype(jnp.bfloat16), "tp").astype(jnp.float32),
    )
    gate_inner = jnp.sum(gate_probs * gate_grad, axis=-1, keepdims=True)
    selected_grad = gate_probs * (gate_grad - gate_inner)
    logit_grad = jnp.sum(jnp.where(chosen, selected_grad[:, :, None], 0.0), axis=1).astype(
        jnp.bfloat16
    )
    moe_grad = moe_grad + contract_last(logit_grad, w_router)
    router_grad = contract_rows(
        lax.dynamic_slice_in_dim(moe_low, own_start, half_rows, 0),
        lax.dynamic_slice_in_dim(logit_grad, own_start, half_rows, 0),
    )
    residual_from_norm, moe_gain_terms = norm_back(residual, moe_factor, moe_gain, moe_grad)
    residual_grad = upstream + residual_from_norm
    moe_gain_grad = jnp.sum(
        lax.dynamic_slice_in_dim(moe_gain_terms, own_start, half_rows, 0), axis=0
    )
    residual_low = residual_grad.astype(jnp.bfloat16)
    mixed_grad = (
        contract_last(residual_low, out_full)
        .astype(jnp.bfloat16)
        .reshape(group_rows, kv_heads, group_size, head_dim)
    )
    grad_w_out = contract_rows(mixed_low, residual_low)
    scores = (
        jnp.einsum("qkgd,tkd->kgqt", query_low, key_low, preferred_element_type=jnp.float32)
        * score_scale
    )
    scores = jnp.where(allowed, scores, masked_score)
    probs_full = jnp.exp(scores - log_total)
    prob_grad = jnp.einsum(
        "qkgd,tkd->kgqt", mixed_grad, value_low, preferred_element_type=jnp.float32
    )
    prob_inner = jnp.sum(probs_full * prob_grad, axis=-1, keepdims=True)
    score_grad = (probs_full * (prob_grad - prob_inner)).astype(jnp.bfloat16)
    query_grad = (
        jnp.einsum(
            "kgqt,tkd->qkgd", score_grad, key_low, preferred_element_type=jnp.float32
        ).reshape(group_rows, query_heads, head_dim)
        * score_scale
    )
    key_grad = (
        jnp.einsum("kgqt,qkgd->tkd", score_grad, query_low, preferred_element_type=jnp.float32)
        * score_scale
    )
    value_grad = (
        jnp.einsum(
            "kgqt,qkgd->tkd",
            probs_full.astype(jnp.bfloat16),
            mixed_grad,
            preferred_element_type=jnp.float32,
        )
        .astype(jnp.bfloat16)
        .reshape(group_rows, kv_heads * head_dim)
    )
    query_pre_grad, query_gain_terms = norm_back(
        query_pre, query_factor, query_gain, rotate_back(query_grad, cosine_table, sine_table)
    )
    key_pre_grad, key_gain_terms = norm_back(
        key_before_norm, key_factor, key_gain, rotate_back(key_grad, cosine_table, sine_table)
    )
    query_pre_low = query_pre_grad.astype(jnp.bfloat16).reshape(group_rows, query_heads * head_dim)
    key_pre_low = key_pre_grad.astype(jnp.bfloat16).reshape(group_rows, kv_heads * head_dim)
    grad_w_query = contract_rows(normed_all, query_pre_low)
    grad_w_key = contract_rows(normed_all, key_pre_low)
    grad_w_value = contract_rows(normed_all, value_grad)
    normed_grad = (
        contract_last(query_pre_low, query_full)
        + contract_last(key_pre_low, key_full)
        + contract_last(value_grad, value_full)
    )
    normed_grad_own, moe_own = (
        lax.psum_scatter(
            normed_grad.astype(jnp.bfloat16), "tp", scatter_dimension=0, tiled=True
        ).astype(jnp.float32),
        lax.psum_scatter(
            moe_part.astype(jnp.bfloat16), "tp", scatter_dimension=0, tiled=True
        ).astype(jnp.float32),
    )
    tokens_own = lax.dynamic_slice_in_dim(tokens_in, own_start, half_rows, 0)
    factor_own = lax.dynamic_slice_in_dim(attn_factor, own_start, half_rows, 0)
    tokens_from_norm, attn_gain_terms = norm_back(
        tokens_own, factor_own, attn_gain, normed_grad_own
    )
    grad_group = lax.dynamic_slice_in_dim(residual_grad, own_start, half_rows, 0) + tokens_from_norm
    residual_own = lax.dynamic_slice_in_dim(residual, own_start, half_rows, 0)
    output_group = (residual_own + moe_own).astype(jnp.bfloat16)
    back_output, back_grad = (
        lax.all_to_all(
            output_group.astype(jnp.float32)
            .reshape(fsdp_count, slice_rows, model_width)
            .astype(jnp.bfloat16),
            "fsdp",
            split_axis=0,
            concat_axis=0,
            tiled=True,
        ).astype(jnp.float32),
        lax.all_to_all(
            grad_group.reshape(fsdp_count, slice_rows, model_width).astype(jnp.bfloat16),
            "fsdp",
            split_axis=0,
            concat_axis=0,
            tiled=True,
        ).astype(jnp.float32),
    )
    output = (
        jnp.take(back_output, back_pick, axis=0)
        .reshape(half_rows, model_width)
        .astype(jnp.bfloat16)
    )
    grad_input = jnp.take(back_grad, back_pick, axis=0).reshape(half_rows, model_width)
    grad_w_query, grad_w_key, grad_w_value, grad_w_out = (
        lax.psum_scatter(grad_w_query, "fsdp", scatter_dimension=0, tiled=True),
        lax.psum_scatter(grad_w_key, "fsdp", scatter_dimension=0, tiled=True),
        lax.psum_scatter(grad_w_value, "fsdp", scatter_dimension=0, tiled=True),
        lax.psum_scatter(grad_w_out, "fsdp", scatter_dimension=1, tiled=True),
    )
    grad_attn_gain, grad_query_gain, grad_key_gain, grad_moe_gain, grad_w_router = lax.psum(
        (
            jnp.sum(attn_gain_terms, axis=0),
            jnp.sum(query_gain_terms, axis=(0, 1)),
            jnp.sum(key_gain_terms, axis=(0, 1)),
            moe_gain_grad,
            router_grad,
        ),
        ("fsdp", "tp"),
    )
    return (
        output,
        grad_input,
        grad_attn_gain,
        grad_query_gain,
        grad_key_gain,
        grad_moe_gain,
        grad_w_query,
        grad_w_key,
        grad_w_value,
        grad_w_out,
        grad_w_router,
        grad_w_gate,
        grad_w_up,
        grad_w_down,
    )


def remote(src, dst, send_sem, recv_sem, target):
    return pltpu.make_async_remote_copy(
        src_ref=src,
        dst_ref=dst,
        send_sem=send_sem,
        recv_sem=recv_sem,
        device_id=target,
        device_id_type=pl.DeviceIdType.MESH,
    )


def greet(targets):
    barrier = pltpu.get_barrier_semaphore()
    for target in targets:
        pl.semaphore_signal(
            barrier, inc=1, device_id=target, device_id_type=pl.DeviceIdType.MESH
        )
    pl.semaphore_wait(barrier, len(targets))


def link_cost(microseconds):
    return pl.CostEstimate(flops=0, bytes_accessed=microseconds * 3_000_000, transcendentals=0)


class Place:
    def __init__(self):
        self.chips = lax.axis_size("chip")
        self.levels = self.chips // 2
        self.chip = lax.axis_index("chip")
        self.core = lax.axis_index("core")
        self.tp = lax.axis_index("tp")
        self.level = self.chip // 2
        self.side = self.chip % 2
        self.fsdp = self.chip * 2 + self.core
        self.mate = {"core": 1 - self.core}
        self.across = {"tp": 1 - self.tp}
        self.beside = {"chip": self.level * 2 + 1 - self.side}
        self.above = {"chip": lax.rem(self.chip + 2, self.chips)}
        self.below = {"chip": lax.rem(self.chip + self.chips - 2, self.chips)}
        top = self.levels - 1
        self.upper = self.level // (self.levels // 2)
        self.end = top * self.upper
        self.next = self.end + 1 - 2 * self.upper
        self.at_end = self.level == self.end
        self.at_next = self.level == self.next
        outward = self.level * 2 + self.side + 4 * self.upper - 2
        inward = self.level * 2 + self.side + 2 - 4 * self.upper
        self.outward = {"chip": lax.rem(outward + self.chips, self.chips)}
        self.inward = {"chip": lax.rem(inward + self.chips, self.chips)}

    def member(self, offset):
        count = 2 * self.chips
        index = lax.rem(self.fsdp + offset + count, count)
        return {"chip": index // 2, "core": lax.rem(index, 2)}, index

    def plane_targets(self):
        return [self.member(offset)[0] for offset in range(1, 2 * self.chips)]

    def ring_targets(self):
        return [self.above, self.below, self.beside]


def lower_half(ref):
    return ref.at[pl.ds(0, ref.shape[0] // 2)]


def upper_half(ref):
    return ref.at[pl.ds(ref.shape[0] // 2, ref.shape[0] // 2)]


class RowGather:
    def __init__(self, place, block, sems, hands=True):
        self.place, self.block, self.hands = place, block, hands
        (
            self.up_send,
            self.up_recv,
            self.down_send,
            self.down_recv,
            self.side_send,
            self.side_recv,
            self.hop_send,
            self.hop_recv,
        ) = sems[:8]
        if hands:
            self.hand_send, self.hand_recv = sems[8:10]

    @staticmethod
    def semaphores(levels, hands=True):
        dma = pltpu.SemaphoreType.DMA
        return [dma((levels,))] * 6 + [dma, dma] + ([dma((2 * levels,))] * 2 if hands else [])

    def climb(self, origin):
        piece, at = self.block(origin, self.place.core), origin // 2
        return remote(piece, piece, self.up_send.at[at], self.up_recv.at[at], self.place.above)

    def sink(self, origin):
        piece, at = self.block(origin, self.place.core), origin // 2
        return remote(piece, piece, self.down_send.at[at], self.down_recv.at[at], self.place.below)

    def cross(self, origin, half=False):
        piece, at = self.block(origin, self.place.core), origin // 2
        if half:
            piece = upper_half(piece)
        return remote(piece, piece, self.side_send.at[at], self.side_recv.at[at], self.place.beside)

    def hop(self, level, inward):
        piece = self.block(level * 2 + 1 - self.place.side, self.place.core)
        if not inward:
            piece = lower_half(piece)
        target = self.place.inward if inward else self.place.outward
        return remote(piece, piece, self.hop_send, self.hop_recv, target)

    def hand(self, origin, whose):
        piece = self.block(origin, whose)
        return remote(
            piece, piece, self.hand_send.at[origin], self.hand_recv.at[origin], self.place.mate
        )

    def pass_on(self, origin):
        place = self.place
        at = origin // 2
        skipped = place.at_next & (at == place.end)
        halved = place.at_end & (at == place.next)

        @pl.when(halved)
        def _():
            self.cross(origin, True).start()

        @pl.when(~skipped & ~halved)
        def _():
            self.cross(origin).start()

        self.give(origin)

    def give(self, origin):
        if self.hands:
            self.hand(origin, self.place.core).start()

    def start(self):
        place = self.place

        @pl.when(place.level < place.levels - 1)
        def _():
            self.climb(place.chip).start()

        @pl.when(place.level > 0)
        def _():
            self.sink(place.chip).start()

        self.pass_on(place.chip)

    def crossed(self, at):
        place = self.place
        origin = at * 2 + 1 - place.side
        skipped = place.at_next & (at == place.end)
        halved = place.at_end & (at == place.next)

        @pl.when(skipped)
        def _():
            self.hop(place.end, True).wait_recv()

        @pl.when(halved)
        def _():
            self.cross(origin, True).wait_recv()

        @pl.when(~skipped & ~halved)
        def _():
            self.cross(origin).wait_recv()

        @pl.when(place.at_end & (at == place.end))
        def _():
            self.hop(place.end, True).start()

        @pl.when(~halved)
        def _():
            self.give(origin)

    def finish(self):
        place = self.place

        @pl.when(place.at_end)
        def _():
            self.hop(place.next, False).wait_recv()
            self.give(place.next * 2 + 1 - place.side)

    def step(self, n):
        place = self.place
        level, side, top = place.level, place.side, place.levels - 1
        under, over = level - n, level + n

        @pl.when((n > 0) & (under >= 0))
        def _():
            origin = under * 2 + side
            self.climb(origin).wait_recv()

            @pl.when(level < top)
            def _():
                self.climb(origin).start()

            self.pass_on(origin)

        @pl.when((n > 0) & (over <= top))
        def _():
            origin = over * 2 + side
            self.sink(origin).wait_recv()

            @pl.when(level > 0)
            def _():
                self.sink(origin).start()

            self.pass_on(origin)

        @pl.when(place.at_next & (n == place.levels - 2))
        def _():
            self.hop(place.next, False).start()

        @pl.when((n > 0) & (under + 1 >= 0))
        def _():
            self.crossed(under + 1)

        @pl.when((n > 1) & (over - 1 <= top))
        def _():
            self.crossed(over - 1)

    def take_hands(self):
        place = self.place

        def taken(origin, carry):
            self.hand(origin, 1 - place.core).wait_recv()
            return carry

        lax.fori_loop(0, place.chips, taken, 0)

    def drain(self):
        place = self.place
        level, side, top = place.level, place.side, place.levels - 1

        def handed(origin, carry):
            self.hand(origin, place.core).wait_send()
            return carry

        if self.hands:
            lax.fori_loop(0, place.chips, handed, 0)

        def sent(at, carry):
            skipped = place.at_next & (at == place.end)
            halved = place.at_end & (at == place.next)

            @pl.when(halved)
            def _():
                self.cross(at * 2 + side, True).wait_send()

            @pl.when(~skipped & ~halved)
            def _():
                self.cross(at * 2 + side).wait_send()

            @pl.when((level < top) & (at <= level))
            def _():
                self.climb(at * 2 + side).wait_send()

            @pl.when((level > 0) & (at >= level))
            def _():
                self.sink(at * 2 + side).wait_send()

            return carry

        lax.fori_loop(0, place.levels, sent, 0)

        @pl.when(place.at_end)
        def _():
            self.hop(place.end, True).wait_send()

        @pl.when(place.at_next)
        def _():
            self.hop(place.next, False).wait_send()


class RowGathers:
    def __init__(self, place, block, sems):
        count = len(sems) // 10
        self.rings = []
        for i in range(count):

            def piece(origin, whose, i=i):
                whole = block(origin, whose)
                rows = whole.shape[0] // count
                return whole.at[pl.ds(i * rows, rows)]

            self.rings.append(RowGather(place, piece, sems[10 * i : 10 * i + 10]))

    @staticmethod
    def semaphores(levels):
        return RowGather.semaphores(levels) * 2

    def start(self):
        for ring in self.rings:
            ring.start()

    def step(self, n):
        for ring in self.rings:
            ring.step(n)

    def finish(self):
        for ring in self.rings:
            ring.finish()

    def take_hand(self, origin, whose):
        for ring in self.rings:
            ring.hand(origin, whose).wait_recv()

    def take_hands(self):
        for ring in self.rings:
            ring.take_hands()

    def drain(self):
        for ring in self.rings:
            ring.drain()


class ChainSum:
    def __init__(self, place, parts, side_buf, chain_buf, hop_buf, sems):
        self.place, self.parts = place, parts
        self.side_buf, self.chain_buf, self.hop_buf = side_buf, chain_buf, hop_buf
        (
            self.up_send,
            self.up_recv,
            self.down_send,
            self.down_recv,
            self.side_send,
            self.side_recv,
            self.hop_send,
            self.hop_recv,
            self.half_send,
            self.half_recv,
        ) = sems

    @staticmethod
    def semaphores(levels):
        dma = pltpu.SemaphoreType.DMA
        return [dma((levels,))] * 6 + [dma] * 4

    @staticmethod
    def buffers(levels, block, dtype=jnp.bfloat16):
        return [
            pltpu.VMEM((levels,) + block, dtype),
            pltpu.VMEM((levels + 1,) + block, dtype),
            pltpu.VMEM(block, dtype),
        ]

    def target(self, turn):
        place = self.place
        top = place.levels - 1
        far, near = top - turn // 2, turn // 2
        odd = turn % 2
        low_half = far * (1 - odd) + near * odd
        high_half = near * (1 - odd) + far * odd
        inner = low_half * (1 - place.upper) + high_half * place.upper
        outer = (top - turn) * (1 - place.upper) + turn * place.upper
        return jnp.where(place.at_end, outer, inner)

    def from_under(self, goal):
        return self.chain_buf.at[goal + 1]

    def from_over(self, goal):
        return self.chain_buf.at[goal]

    def other(self, goal):
        return self.parts(goal * 2 + 1 - self.place.side)

    def cross(self, source, target, goal):
        return remote(
            source, target, self.side_send.at[goal], self.side_recv.at[goal], self.place.beside
        )

    def whole(self, goal):
        return self.cross(self.other(goal), self.side_buf.at[goal], goal)

    def lifted(self, goal):
        return self.cross(self.hop_buf, self.side_buf.at[goal], goal)

    def upper(self, goal):
        return self.cross(upper_half(self.other(goal)), upper_half(self.side_buf.at[goal]), goal)

    def lower(self, goal):
        return remote(
            lower_half(self.hop_buf),
            lower_half(self.side_buf.at[goal]),
            self.half_send,
            self.half_recv,
            self.place.beside,
        )

    def hop_out(self):
        return remote(
            self.other(self.place.end), self.hop_buf, self.hop_send, self.hop_recv, self.place.outward
        )

    def hop_in(self):
        return remote(
            lower_half(self.other(self.place.next)),
            lower_half(self.hop_buf),
            self.hop_send,
            self.hop_recv,
            self.place.inward,
        )

    def up(self, goal):
        return remote(
            self.side_buf.at[goal],
            self.from_under(goal),
            self.up_send.at[goal],
            self.up_recv.at[goal],
            self.place.above,
        )

    def down(self, goal):
        return remote(
            self.side_buf.at[goal],
            self.from_over(goal),
            self.down_send.at[goal],
            self.down_recv.at[goal],
            self.place.below,
        )

    def cases(self, goal):
        place = self.place
        to_end, to_next = goal == place.end, goal == place.next
        return (
            place.at_end & to_end,
            place.at_end & to_next,
            place.at_next & to_end,
            place.at_next & to_next,
        )

    def send(self, goal):
        end_end, end_next, next_end, next_next = self.cases(goal)

        @pl.when(end_next)
        def _():
            self.hop_in().start()

        @pl.when(next_end)
        def _():
            self.hop_out().start()

        @pl.when(end_next | next_next)
        def _():
            self.upper(goal).start()

        @pl.when(~(end_end | end_next | next_end | next_next))
        def _():
            self.whole(goal).start()

    def send_joined(self):
        place, wide = self.place, jnp.float32
        hop = self.hop_buf

        @pl.when(place.at_end)
        def _():
            self.hop_out().wait_recv()
            total = hop[...].astype(wide) + self.other(place.end)[...].astype(wide)
            hop[...] = total.astype(hop.dtype)
            self.lifted(place.end).start()

        @pl.when(place.at_next)
        def _():
            self.hop_in().wait_recv()
            half = hop.shape[0] // 2
            own = lower_half(self.other(place.next))[...].astype(wide)
            hop[:half] = (hop[:half].astype(wide) + own).astype(hop.dtype)
            self.lower(place.next).start()

    def add(self, goal, ref):
        held = self.side_buf
        total = held[goal].astype(jnp.float32) + ref[...].astype(jnp.float32)
        held[goal] = total.astype(held.dtype)

    def take_side(self, goal):
        place = self.place
        level, top = place.level, place.levels - 1
        end_end, end_next, next_end, next_next = self.cases(goal)
        held = self.side_buf
        own = self.parts(goal * 2 + place.side)
        half = held.shape[1] // 2

        @pl.when(end_next)
        def _():
            self.upper(goal).wait_recv()
            total = held[goal, half:].astype(jnp.float32) + upper_half(own)[...].astype(jnp.float32)
            held[goal, half:] = total.astype(held.dtype)
            held[goal, :half] = lower_half(own)[...]

        @pl.when(next_end)
        def _():
            held[goal] = own[...]

        @pl.when(next_next)
        def _():
            self.upper(goal).wait_recv()
            self.lower(goal).wait_recv()

        @pl.when(~(end_next | next_end | next_next))
        def _():
            self.whole(goal).wait_recv()

        @pl.when(~(end_next | next_end))
        def _():
            self.add(goal, own)

        @pl.when((goal > level) & (level == 0))
        def _():
            self.up(goal).start()

        @pl.when((goal < level) & (level == top))
        def _():
            self.down(goal).start()

    def take_chain(self, goal):
        place = self.place
        level, top = place.level, place.levels - 1

        @pl.when((goal > level) & (level > 0))
        def _():
            self.up(goal).wait_recv()
            self.add(goal, self.from_under(goal))
            self.up(goal).start()

        @pl.when((goal < level) & (level < top))
        def _():
            self.down(goal).wait_recv()
            self.add(goal, self.from_over(goal))
            self.down(goal).start()

    def close(self):
        place = self.place
        level, top = place.level, place.levels - 1

        @pl.when(level > 0)
        def _():
            self.up(level).wait_recv()
            self.add(level, self.from_under(level))

        @pl.when(level < top)
        def _():
            self.down(level).wait_recv()
            self.add(level, self.from_over(level))

    def drain(self):
        place = self.place

        def goal_done(goal, carry):
            end_end, end_next, next_end, next_next = self.cases(goal)

            @pl.when(end_end)
            def _():
                self.lifted(goal).wait_send()

            @pl.when(end_next)
            def _():
                self.hop_in().wait_send()

            @pl.when(next_end)
            def _():
                self.hop_out().wait_send()

            @pl.when(next_next)
            def _():
                self.lower(goal).wait_send()

            @pl.when(end_next | next_next)
            def _():
                self.upper(goal).wait_send()

            @pl.when(~(end_end | end_next | next_end | next_next))
            def _():
                self.whole(goal).wait_send()

            @pl.when(goal > place.level)
            def _():
                self.up(goal).wait_send()

            @pl.when(goal < place.level)
            def _():
                self.down(goal).wait_send()

            return carry

        lax.fori_loop(0, place.levels, goal_done, 0)


class ChainSums:
    count = 2

    def __init__(self, place, parts, rows, buffers, sems):
        self.rings = []
        for i in range(self.count):

            def piece(chip, i=i):
                return parts(chip).at[pl.ds(i * rows // self.count, rows // self.count)]

            self.rings.append(
                ChainSum(place, piece, *buffers[3 * i : 3 * i + 3], sems[10 * i : 10 * i + 10])
            )
        self.target = self.rings[0].target

    @classmethod
    def semaphores(cls, levels):
        return ChainSum.semaphores(levels) * cls.count

    @classmethod
    def buffers(cls, levels, block):
        return ChainSum.buffers(levels, (block[0] // cls.count,) + block[1:]) * cls.count

    def send(self, goal):
        for ring in self.rings:
            ring.send(goal)

    def send_joined(self):
        for ring in self.rings:
            ring.send_joined()

    def take_side(self, goal):
        for ring in self.rings:
            ring.take_side(goal)

    def take_chain(self, goal):
        for ring in self.rings:
            ring.take_chain(goal)

    def close(self):
        for ring in self.rings:
            ring.close()

    def drain(self):
        for ring in self.rings:
            ring.drain()

    def total(self, level):
        return jnp.concatenate([ring.side_buf[level] for ring in self.rings], axis=0)


class QuadSum:
    def __init__(self, place, parts, near, pair, far, send, recv):
        self.place, self.parts = place, parts
        self.near, self.pair, self.far = near, pair, far
        self.send, self.recv = send, recv

    @staticmethod
    def scratch(rows, width):
        low, dma = jnp.bfloat16, pltpu.SemaphoreType.DMA
        return [
            pltpu.VMEM((2, rows, width), low),
            pltpu.VMEM((rows, width), low),
            pltpu.VMEM((rows, width), low),
            dma((3,)),
            dma((3,)),
        ]

    def to_mate(self, half):
        return remote(
            self.parts.at[1 - self.place.core, half],
            self.near.at[half],
            self.send.at[half],
            self.recv.at[half],
            self.place.mate,
        )

    def to_across(self):
        return remote(self.pair, self.far, self.send.at[2], self.recv.at[2], self.place.across)

    def start(self):
        self.to_mate(1 - self.place.tp).start()
        self.to_mate(self.place.tp).start()

    def relay(self):
        core, tp, wide = self.place.core, self.place.tp, jnp.float32
        self.to_mate(1 - tp).wait_recv()
        self.pair[...] = (
            self.parts[core, 1 - tp].astype(wide) + self.near[1 - tp].astype(wide)
        ).astype(jnp.bfloat16)
        self.to_across().start()

    def total(self):
        core, tp, wide = self.place.core, self.place.tp, jnp.float32
        self.to_mate(tp).wait_recv()
        total = self.parts[core, tp].astype(wide) + self.near[tp].astype(wide)
        self.to_across().wait_recv()
        return total + self.far[...].astype(wide)

    def drain(self):
        for half in range(2):
            self.to_mate(half).wait_send()
        self.to_across().wait_send()


def nt_dot(left, right):
    return lax.dot_general(
        left, right, (((1,), (1,)), ((), ())), preferred_element_type=jnp.float32
    )


def tn_dot(left, right):
    return lax.dot_general(
        left, right, (((0,), (0,)), ((), ())), preferred_element_type=jnp.float32
    )


def lanes_at(index, width):
    return pl.ds(pl.multiple_of(index * width, width), width)


def front_kernel(
    sequences,
    experts,
    tokens_ref,
    cotangent_ref,
    order_ref,
    gain_ref,
    lengths_ref,
    frequency_ref,
    query_gain,
    key_gain,
    moe_gain,
    router_ref,
    routes_ref,
    query_ref,
    key_ref,
    value_ref,
    out_ref,
    gate_ref,
    up_ref,
    dealt_ref,
    normed_ref,
    cosine_ref,
    sine_ref,
    moe_ext,
    residual_ref,
    gates_ref,
    query_pre,
    query_low,
    key_pre,
    key_low,
    value_low,
    probs_ref,
    mixed_ref,
    upstream_all,
    query_all,
    key_all,
    value_all,
    out_all,
    gate_all,
    up_all,
    slices_ref,
    both_lengths_ref,
    mask_ref,
    upstream_own,
    query_w,
    key_w,
    value_w,
    out_w,
    router_rows,
    parts,
    near,
    pair,
    far,
    sum_send,
    sum_recv,
    deal_send,
    deal_recv,
    quad_send,
    quad_recv,
    swap_send,
    swap_recv,
    keep_sem,
    pair_send,
    pair_recv,
    pair_keep,
    load_sem,
    *ring_sems,
):
    place = Place()
    core, chip = place.core, place.chip
    wide, low = jnp.float32, jnp.bfloat16
    own_rows = query_ref.shape[0]
    width = dealt_ref.shape[2]
    quarter = query_all.shape[2]
    narrow = key_all.shape[2]
    head_rows = out_all.shape[0]
    lanes = out_ref.shape[1]
    members = 2 * place.chips
    for index in range(members):
        wanted = lax.rem(index - place.fsdp + members, members)
        picked = 0
        for at in range(members):
            picked += jnp.where(order_ref[at] == wanted, at, 0)
        picked = lax.rem(picked, members)
        both = [ref[picked].astype(jnp.float32) for ref in (tokens_ref, cotangent_ref)]
        slices_ref[index] = jnp.concatenate(both, axis=0).astype(jnp.bfloat16)
    greet(place.plane_targets() + [place.across])

    def deal_copy(offset, sending):
        target, index = place.member(offset if sending else -offset)
        return remote(
            slices_ref.at[index],
            dealt_ref.at[place.fsdp if sending else index],
            deal_send.at[offset - 1],
            deal_recv.at[offset - 1],
            target,
        )

    for offset in range(1, members):
        deal_copy(offset, True).start()

    def rows(who):
        return pl.ds(pl.multiple_of(who * own_rows, own_rows), own_rows)

    def columns(who, width):
        return pl.ds(pl.multiple_of(who * width, width), width)

    def spots(who):
        lane_start = pl.multiple_of((2 * chip + core) * lanes, lanes)
        return [
            (query_ref.at[:, columns(who, quarter)], query_all.at[chip, rows(core)]),
            (key_ref.at[:, columns(who, narrow)], key_all.at[chip, rows(core)]),
            (value_ref.at[:, columns(who, narrow)], value_all.at[chip, rows(core)]),
            (
                out_ref.at[pl.ds(pl.multiple_of(who * head_rows, head_rows), head_rows)],
                out_all.at[:, pl.ds(lane_start, lanes)],
            ),
        ]

    def arrivals():
        lane_start = pl.multiple_of((2 * chip + 1 - core) * lanes, lanes)
        return [
            query_all.at[chip, rows(1 - core)],
            key_all.at[chip, rows(1 - core)],
            value_all.at[chip, rows(1 - core)],
            out_all.at[:, pl.ds(lane_start, lanes)],
        ]

    sends = [
        remote(src, dst, swap_send.at[i], swap_recv.at[i], place.mate)
        for i, (src, dst) in enumerate(spots(1 - core))
    ]
    keeps = [
        pltpu.make_async_copy(src, dst, keep_sem.at[i])
        for i, (src, dst) in enumerate(spots(core))
    ]
    mate_lengths = remote(
        lengths_ref, both_lengths_ref.at[core], swap_send.at[4], swap_recv.at[4], place.mate
    )
    own_lengths = pltpu.make_async_copy(lengths_ref, both_lengths_ref.at[core], keep_sem.at[4])
    own_slice = pltpu.make_async_copy(
        slices_ref.at[place.fsdp], dealt_ref.at[place.fsdp], keep_sem.at[5]
    )
    own_slice.start()
    units = gate_ref.shape[1]

    def halves(who):
        at = pl.ds(pl.multiple_of(who * units, units), units)
        return [gate_all.at[:, at], up_all.at[:, at]]

    shards = (gate_ref, up_ref)
    pair_copies = []
    for i, (src, dst) in enumerate(zip(shards, halves(place.tp))):
        pair_copies.append(
            (
                remote(src, dst, pair_send.at[i], pair_recv.at[i], place.across),
                pltpu.make_async_copy(src, dst, pair_keep.at[i]),
            )
        )
    for i in range(4):
        sends[i].start()
        keeps[i].start()
    mate_lengths.start()
    own_lengths.start()

    out_lanes = 2 * lanes
    views = [
        lambda who, core: query_all.at[who],
        lambda who, core: key_all.at[who],
        lambda who, core: value_all.at[who],
        lambda who, core: out_all.at[:, lanes_at(who, out_lanes)],
    ]
    rings = [
        RowGather(place, view, ring_sems[8 * i : 8 * i + 8], hands=False)
        for i, view in enumerate(views)
    ]
    landed = arrivals()
    upstream_ring = RowGathers(
        place, lambda origin, whose: upstream_all.at[origin, whose], ring_sems[32:]
    )
    for i in range(4):
        keeps[i].wait()
        sends[i].wait_send()
        remote(landed[i], landed[i], swap_send.at[i], swap_recv.at[i], place.mate).wait_recv()
        rings[i].start()

    own_slice.wait()
    for offset in range(1, members):
        deal_copy(offset, False).wait_recv()
    tp = place.tp
    half = slices_ref.shape[1] // 2
    step_rows = 4
    width = dealt_ref.shape[2]
    for start in range(0, members, step_rows):
        block = dealt_ref[start : start + step_rows].astype(jnp.float32)
        span = slice(start * half, (start + step_rows) * half)
        upstream_own[span, :] = (
            block[:, half:].reshape(step_rows * half, block.shape[2]).astype(jnp.bfloat16)
        )
        x = block[:, :half].reshape(step_rows * half, block.shape[2])
        factor = lax.rsqrt(jnp.mean(x * x, axis=-1, keepdims=True) + epsilon)
        normed_ref[core, tp, start * half : (start + step_rows) * half, :] = (
            x * factor * gain_ref[...]
        ).astype(jnp.bfloat16)
    mine = normed_ref.at[core, tp]
    to_mate = remote(mine, mine, quad_send.at[0], quad_recv.at[0], place.mate)
    to_across = remote(mine, mine, quad_send.at[1], quad_recv.at[1], place.across)
    to_across.start()
    to_mate.start()
    for both in pair_copies:
        both[0].start()
        both[1].start()
    keep_upstream = pltpu.make_async_copy(upstream_own, upstream_all.at[chip, core], keep_sem.at[6])
    keep_upstream.start()
    levels = place.levels
    own_lengths.wait()
    mate_lengths.wait_send()
    theirs = both_lengths_ref.at[1 - core]
    remote(theirs, theirs, swap_send.at[4], swap_recv.at[4], place.mate).wait_recv()
    group = mask_ref.shape[1]
    head = cosine_ref.shape[1]
    heads = query_w.shape[2] // head
    across_sign = jnp.where(
        lax.broadcasted_iota(jnp.int32, (group, head), 1) < head // 2, -1.0, 1.0
    )
    for which in range(2):
        ends = []
        for at in range(sequences):
            length = both_lengths_ref[which, 0:1, at : at + 1]
            ends.append(length if at == 0 else ends[-1] + length)

        def segment_start(place_ids):
            start = jnp.zeros_like(place_ids)
            for end in ends:
                start = jnp.where(place_ids >= end, end, start)
            return start

        at_rows = pl.ds(which * group, group)
        row_ids = lax.broadcasted_iota(jnp.int32, (group, head), 0)
        position = (row_ids - segment_start(row_ids)).astype(jnp.float32)
        angles = position * frequency_ref[...]
        cosine_ref[at_rows, :] = jnp.cos(angles)
        sine_ref[at_rows, :] = jnp.sin(angles) * across_sign
        row_ids = lax.broadcasted_iota(jnp.int32, (group, group), 0)
        key_ids = lax.broadcasted_iota(jnp.int32, (group, group), 1)
        allowed = (key_ids <= row_ids) & (key_ids >= segment_start(row_ids))
        mask_ref[which] = jnp.where(allowed, 0.0, masked_score)
    early, late = rings[:3], rings[3]
    for ring in rings:
        ring.step(1)
    other = normed_ref.at[core, 1 - tp]
    remote(other, other, quad_send.at[1], quad_recv.at[1], place.across).wait_recv()
    passed = remote(other, other, quad_send.at[2], quad_recv.at[2], place.mate)
    passed.start()
    keep_upstream.wait()
    for n in range(2, levels):
        for ring in rings:
            ring.step(n)
        if n == 2:
            upstream_ring.start()
    for ring in early:
        ring.step(levels)
        ring.finish()
    loads = [
        pltpu.make_async_copy(src, dst, load_sem.at[i])
        for i, (src, dst) in enumerate(
            ((query_all, query_w), (key_all, key_w), (value_all, value_w), (out_all, out_w))
        )
    ]
    for load in loads[:3]:
        load.start()
    router_rows[...] = jnp.zeros_like(router_rows)
    router_rows[:experts, :] = router_ref[...]
    for slot, piece in ((0, normed_ref.at[1 - core, tp]), (2, normed_ref.at[1 - core, 1 - tp])):
        remote(piece, piece, quad_send.at[slot], quad_recv.at[slot], place.mate).wait_recv()
    for load in loads[:3]:
        load.wait()

    def turned(values, gain_ref):
        factor = lax.rsqrt(jnp.mean(values * values, axis=-1, keepdims=True) + epsilon)
        scaled = values * factor * gain_ref[...]
        return (scaled * cosine_ref[...] + pltpu.roll(scaled, head // 2, 1) * sine_ref[...]).astype(
            low
        )

    x = normed_ref[...].reshape(2 * group, width)

    def project(index, carry):
        both = jnp.dot(
            normed_ref[...].reshape(2 * group, width),
            query_w[:, :, lanes_at(index, 2 * head)].reshape(width, 2 * head),
            preferred_element_type=wide,
        )
        query_pre[:, lanes_at(index, 2 * head)] = both.astype(low)
        for which in range(2):
            one = both[:, which * head : (which + 1) * head]
            query_low[:, lanes_at(2 * index + which, head)] = turned(one, query_gain)
        return carry

    lax.fori_loop(0, heads // 2, project, 0)
    key_values = jnp.dot(x, key_w[...].reshape(width, head), preferred_element_type=wide)
    key_pre[...] = key_values
    key_low[...] = turned(key_values, key_gain)
    value_low[...] = jnp.dot(x, value_w[...].reshape(width, head), preferred_element_type=wide).astype(low)
    late.step(levels)
    late.finish()
    loads[3].start()
    upstream_ring.step(1)
    scale = head ** (-0.5)
    batch = 4

    def attend(index, carry):
        which = index // (heads // batch)
        first = (index % (heads // batch)) * batch
        rows = lanes_at(which, group)
        key = key_low[rows, :]
        value = value_low[rows, :]
        mask = mask_ref[which]
        for offset in range(batch):
            at = lanes_at(first + offset, head)
            scores = nt_dot(query_low[rows, at], key) * scale + mask
            peak = jnp.max(scores, axis=-1, keepdims=True)
            exponent = jnp.exp(scores - peak)
            probs = (exponent * (1.0 / jnp.sum(exponent, axis=-1, keepdims=True))).astype(low)
            probs_ref[which * heads + first + offset] = probs
            mixed_ref[rows, at] = jnp.dot(probs, value, preferred_element_type=wide).astype(low)
        return carry

    lax.fori_loop(0, 2 * heads // batch, attend, 0)
    loads[3].wait()

    def out_rows(whose):
        left = mixed_ref[lanes_at(whose, group), :]

        def out_lanes(index, carry):
            at = lanes_at(index, 512)
            product = jnp.dot(left, out_w[:, at], preferred_element_type=wide).astype(low)
            parts[whose, :, :, at] = product.reshape(2, own_rows, 512)
            return carry

        lax.fori_loop(0, width // 512, out_lanes, 0)

    sums = QuadSum(place, parts, near, pair, far, quad_send, quad_recv)
    sums = QuadSum(place, parts, near, pair, far, sum_send, sum_recv)
    out_rows(1 - core)
    sums.start()
    out_rows(core)
    upstream_ring.step(2)
    sums.relay()
    upstream_ring.step(3)
    total = sums.total()

    def token_rows(start):
        block = dealt_ref[start : start + step_rows].astype(wide)[:, :half]
        return block.reshape(step_rows * half, width)

    tokens = jnp.concatenate(
        [token_rows(start) for start in range(0, members, step_rows)], axis=0
    )
    residual = tokens + total
    residual_ref[...] = residual
    factor = lax.rsqrt(jnp.mean(residual * residual, axis=-1, keepdims=True) + epsilon)
    moe_low = (residual * factor * moe_gain[...]).astype(low)
    moe_ext[:, :width] = moe_low
    logits = nt_dot(moe_low, router_rows[...])
    own_routes = routes_ref[:, lanes_at(place.tp, own_rows)]
    expert = lax.broadcasted_iota(jnp.int32, (128, own_rows), 0)
    chosen = jnp.zeros((128, own_rows), wide)
    for choice in range(own_routes.shape[0]):
        chosen += jnp.where(own_routes[choice : choice + 1, :] == expert, 1.0, 0.0)
    chosen = chosen.T > 0.0
    logits = jnp.where(chosen, logits, masked_score)
    exponent = jnp.exp(logits - jnp.max(logits, axis=-1, keepdims=True))
    exponent = jnp.where(chosen, exponent, 0.0)
    gates = exponent / jnp.sum(exponent, axis=-1, keepdims=True)
    gates_ref[...] = gates
    high = gates.astype(low).astype(wide)
    middle = (gates - high).astype(low).astype(wide)
    rest = gates - high - middle
    moe_ext[:, width:] = (
        high + pltpu.roll(middle, experts, 1) + pltpu.roll(rest, 2 * experts, 1)
    ).astype(low)
    for n in range(4, levels + 1):
        upstream_ring.step(n)
    upstream_ring.finish()
    upstream_ring.take_hands()
    upstream_ring.drain()
    sums.drain()
    for ring in rings:
        ring.drain()
    for offset in range(1, members):
        deal_copy(offset, True).wait_send()
    to_mate.wait_send()
    to_across.wait_send()
    passed.wait_send()
    for i, dst in enumerate(halves(1 - place.tp)):
        pair_copies[i][1].wait()
        pair_copies[i][0].wait_send()
        remote(dst, dst, pair_send.at[i], pair_recv.at[i], place.across).wait_recv()


def front_layer(
    experts,
    sequences,
    tokens,
    cotangent,
    deal_order,
    gain_vec,
    lengths,
    frequency,
    gain_vecs,
    router,
    routes,
    w_query,
    w_key,
    w_value,
    w_out,
    w_gate,
    w_up,
):
    members, slice_rows, width = tokens.shape
    dealt_shape = (members, 2 * slice_rows, width)
    chips = members // 2
    levels = chips // 2
    own_rows = w_query.shape[0]
    wide, low = jnp.float32, jnp.bfloat16
    vmem = pl.BlockSpec(memory_space=pltpu.VMEM)
    anywhere = pl.BlockSpec(memory_space=pl.ANY)
    dma = pltpu.SemaphoreType.DMA
    shape = jax.ShapeDtypeStruct
    group, head = 2 * own_rows, frequency.shape[1]
    rows, heads_width = 2 * group, w_query.shape[1] // 2
    weights = [(chips, 2 * own_rows, w.shape[1] // 2) for w in (w_query, w_key, w_value)]
    weights.append((w_out.shape[0] // 2, members * w_out.shape[1]))
    return pl.pallas_call(
        functools.partial(front_kernel, sequences, experts),
        name="front_layer",
        out_shape=[
            shape(dealt_shape, low),
            shape((2, 2, own_rows, width), low),
            shape((rows, head), wide),
            shape((rows, head), wide),
            shape((own_rows, width + 128), low),
            shape((own_rows, width), wide),
            shape((own_rows, 128), wide),
            shape((rows, heads_width), low),
            shape((rows, heads_width), low),
            shape((rows, head), wide),
            shape((rows, head), low),
            shape((rows, head), low),
            shape((2 * heads_width // head, group, group), low),
            shape((rows, heads_width), low),
            shape((chips, 2, own_rows, width), low),
        ]
        + [shape(weight, low) for weight in weights]
        + [shape((width, 2 * w_gate.shape[1]), low), shape((width, 2 * w_up.shape[1]), low)],
        in_specs=[vmem] * 2
        + [pl.BlockSpec(memory_space=pltpu.SMEM)]
        + [vmem] * 8
        + [anywhere] * 6,
        out_specs=[vmem] * 14 + [anywhere] * 7,
        scratch_shapes=[
            pltpu.VMEM(dealt_shape, low),
            pltpu.VMEM((2,) + lengths.shape, jnp.int32),
            pltpu.VMEM((2, group, group), wide),
            pltpu.VMEM((own_rows, width), low),
        ]
        + [pltpu.VMEM(weight, low) for weight in weights]
        + [pltpu.VMEM((128, width), low), pltpu.VMEM((2, 2, own_rows, width), low)]
        + QuadSum.scratch(own_rows, width)
        + [
            dma((members - 1,)),
            dma((members - 1,)),
            dma((3,)),
            dma((3,)),
            dma((5,)),
            dma((5,)),
            dma((7,)),
            dma((2,)),
            dma((2,)),
            dma((2,)),
            dma((4,)),
        ]
        + RowGather.semaphores(levels, hands=False) * 4
        + RowGathers.semaphores(levels),
        compiler_params=pltpu.CompilerParams(
            collective_id=0, has_side_effects=True, vmem_limit_bytes=65_400_000
        ),
        cost_estimate=link_cost(170),
    )(
        tokens,
        cotangent,
        deal_order,
        gain_vec,
        lengths,
        frequency,
        *gain_vecs,
        router,
        routes,
        w_query,
        w_key,
        w_value,
        w_out,
        w_gate,
        w_up,
    )


def expert_kernel(
    experts,
    x_own,
    upstream_ref,
    gate_ref,
    up_ref,
    down_ref,
    entry_own,
    out_part,
    gate_grad_ref,
    up_grad_ref,
    down_grad_ref,
    x_all,
    u_all,
    gate_w,
    up_w,
    down_w,
    hidden,
    gate_val_grad,
    up_val_grad,
    scores,
    sums,
    mate_out,
    mate_in,
    *rest,
):
    buffers, rest = rest[:6], rest[6:]
    staged, load_sem, store_sem, both_sem, mate_send, mate_recv = rest[:6]
    ring_sems = rest[6:]
    place = Place()
    core, chip, level, side = place.core, place.chip, place.level, place.side
    levels, top = place.levels, place.levels - 1
    rows = x_own.shape[0]
    tile = 2 * rows
    width = upstream_ref.shape[1]
    units = down_ref.shape[0]
    wide = jnp.float32
    low = jnp.bfloat16
    loads = [
        pltpu.make_async_copy(x_own, x_all.at[chip, core], load_sem.at[0]),
        pltpu.make_async_copy(gate_ref, gate_w, load_sem.at[1]),
        pltpu.make_async_copy(up_ref, up_w, load_sem.at[2]),
        pltpu.make_async_copy(down_ref, down_w, load_sem.at[3]),
        pltpu.make_async_copy(upstream_ref, u_all, load_sem.at[4]),
    ]
    for load in loads:
        load.start()
    greet(place.ring_targets() + [place.mate])

    gather = RowGathers(place, lambda origin, whose: x_all.at[origin, whose], ring_sems[:20])
    loads[0].wait()

    gather.start()
    for load in loads[1:]:
        load.wait()

    lane = lax.broadcasted_iota(jnp.int32, (128, 128), 0)
    select = (
        (lane == place.fsdp)
        | (lane == place.fsdp + experts)
        | (lane == place.fsdp + 2 * experts)
    ).astype(low)
    cut = 256
    across_lanes = lax.broadcasted_iota(jnp.int32, (tile, 128), 1)

    def forward_tile(origin):
        x = x_all[origin].reshape(tile, x_all.shape[3])
        gate_lanes = jnp.dot(x[:, width:], select, preferred_element_type=wide)
        gate = jnp.concatenate([gate_lanes] * (cut // 128), axis=1)
        x = x[:, :width]
        start = pl.multiple_of(origin * tile, tile)
        u = u_all[pl.ds(start, tile), :]
        score = jnp.zeros((tile, 1), wide)
        for part in range(units // cut):
            lanes = slice(part * cut, (part + 1) * cut)
            gate_val = jnp.dot(x, gate_w[:, lanes], preferred_element_type=wide)
            up_val = jnp.dot(x, up_w[:, lanes], preferred_element_type=wide)
            back = lax.dot_general(
                u, down_w[lanes, :], (((1,), (1,)), ((), ())), preferred_element_type=wide
            )
            sigmoid = 1.0 / (1.0 + jnp.exp(-gate_val))
            swish = gate_val * sigmoid
            out = (swish * up_val).astype(low).astype(wide)
            score += jnp.sum(out * back, axis=1, keepdims=True)
            back = back * gate
            slope = sigmoid * (1.0 + gate_val * (1.0 - sigmoid))
            hidden[pl.ds(start, tile), lanes] = (out * gate).astype(low)
            gate_val_grad[pl.ds(start, tile), lanes] = (back * up_val * slope).astype(low)
            up_val_grad[pl.ds(start, tile), lanes] = (back * swish).astype(low)
        high = score.astype(low).astype(wide)
        packed = jnp.where(
            across_lanes == place.fsdp,
            high,
            jnp.where(across_lanes == place.fsdp + experts, score - high, 0.0),
        )
        scores[origin] = packed.astype(low)

    def gather_step(n, carry):
        gather.step(n)

        def candidate(which, carried):
            upward = which % 2
            facing = which // 2
            distance = n - 1 + facing
            at = level + distance * (2 * upward - 1)
            early = (n == 2) & (facing == 0) & place.at_end
            origin = at * 2 + side * facing + (1 - side) * (1 - facing)
            inside = (at >= 0) & (at <= top) & (distance >= 0) & ((distance > 0) | (upward == 0))

            @pl.when(inside & ~early)
            def _():
                gather.take_hand(origin, 1 - core)
                forward_tile(origin)

            return carried

        return lax.fori_loop(0, 4, candidate, carry)

    lax.fori_loop(0, levels + 1, gather_step, 0)

    plane_sum = ChainSums(place, lambda chip: sums.at[chip], rows, buffers, ring_sems[20:])

    def to_mate(goal_chip, slot):
        return remote(
            mate_out.at[slot],
            mate_in.at[goal_chip],
            mate_send.at[slot],
            mate_recv.at[goal_chip],
            place.mate,
        )

    def backward_tile(goal_chip, slot, reuse):
        start = pl.multiple_of(goal_chip * tile, tile)
        own_start = pl.multiple_of(goal_chip * tile + core * rows, rows)
        mate_start = pl.multiple_of(goal_chip * tile + (1 - core) * rows, rows)

        @pl.when(reuse)
        def _():
            to_mate(goal_chip, slot).wait_send()

        grads = gate_val_grad[pl.ds(start, tile), :]
        up_grads = up_val_grad[pl.ds(start, tile), :]
        piece = 512
        for first in range(0, width, piece):
            lanes = slice(first, first + piece)
            whole = lax.dot_general(
                grads, gate_w[lanes, :], (((1,), (1,)), ((), ())), preferred_element_type=wide
            ) + lax.dot_general(
                up_grads, up_w[lanes, :], (((1,), (1,)), ((), ())), preferred_element_type=wide
            )
            halves = whole.astype(low).reshape(2, rows, piece)
            sums[goal_chip, :, lanes] = jnp.where(core == 0, halves[0], halves[1])
            mate_out[slot, :, lanes] = jnp.where(core == 0, halves[1], halves[0])
        sums[goal_chip, :, width:] = scores[goal_chip, pl.ds(pl.multiple_of(core * rows, rows), rows)]
        mate_out[slot, :, width:] = scores[
            goal_chip, pl.ds(pl.multiple_of((1 - core) * rows, rows), rows)
        ]
        to_mate(goal_chip, slot).start()

    def joined(goal_chip, slot):
        to_mate(goal_chip, slot).wait_recv()
        sums[goal_chip] = (
            sums[goal_chip].astype(wide) + mate_in[goal_chip].astype(wide)
        ).astype(low)

    def backward_turn(turn, carry):
        goal = plane_sum.target(turn)

        @pl.when((turn == levels - 2) & place.at_end)
        def _():
            origin = place.next * 2 + 1 - side
            gather.take_hand(origin, 1 - core)
            forward_tile(origin)

        backward_tile(goal * 2 + 1 - side, 0, turn > 0)
        backward_tile(goal * 2 + side, 1, turn > 0)
        joined(goal * 2 + 1 - side, 0)
        plane_sum.send(goal)
        joined(goal * 2 + side, 1)
        return carry

    def first_turns(turn, carry):
        backward_turn(turn, carry)

        @pl.when(turn == 0)
        def _():
            gather.finish()

        return carry

    lax.fori_loop(0, levels, first_turns, 0)
    plane_sum.send_joined()

    def store(target, start, slot):
        return pltpu.make_async_copy(
            staged.at[slot], target.at[pl.ds(start, tile)], store_sem.at[slot]
        )

    def output_tile(origin, carry):
        start = pl.multiple_of(origin * tile, tile)
        slot = origin % 2

        @pl.when(origin > 1)
        def _():
            store(out_part, start, slot).wait()

        left = hidden[pl.ds(start, tile), :]
        for first in range(0, width, 512):
            lanes = slice(first, first + 512)
            staged[slot, :, lanes] = jnp.dot(
                left, down_w[:, lanes], preferred_element_type=wide
            ).astype(low)
        store(out_part, start, slot).start()
        return carry

    def down_grads(index, carry):
        start = pl.multiple_of(index * tile, tile)
        slot = index % 2
        store(down_grad_ref, start, slot).wait()
        left = hidden[:, pl.ds(start, tile)]
        for first in range(0, width, 512):
            lanes = slice(first, first + 512)
            staged[slot, :, lanes] = lax.dot_general(
                left, u_all[:, lanes], (((0,), (0,)), ((), ())), preferred_element_type=wide
            ).astype(low)
        store(down_grad_ref, start, slot).start()
        return carry

    def store_both(index):
        slot = index % 2
        start = pl.multiple_of(index * tile, tile)
        return [
            pltpu.make_async_copy(
                staged.at[slot, :, i * units : (i + 1) * units],
                target.at[pl.ds(start, tile)],
                both_sem.at[slot, i],
            )
            for i, target in enumerate((gate_grad_ref, up_grad_ref))
        ]

    def entry_weight_grads(index, carry):
        slot = index % 2

        @pl.when(index > 1)
        def _():
            for copy in store_both(index):
                copy.wait()

        left = x_all[:, :, :, pl.ds(pl.multiple_of(index * tile, tile), tile)]
        left = left.reshape(u_all.shape[0], tile)
        for i, right in enumerate((gate_val_grad, up_val_grad)):
            staged[slot, :, i * units : (i + 1) * units] = lax.dot_general(
                left, right[...], (((0,), (0,)), ((), ())), preferred_element_type=wide
            ).astype(low)
        for copy in store_both(index):
            copy.start()
        return carry

    plane_sum.take_side(plane_sum.target(0))
    lax.fori_loop(0, place.chips, output_tile, 0)
    plane_sum.take_chain(plane_sum.target(0))
    plane_sum.take_side(plane_sum.target(1))
    lax.fori_loop(0, units // tile, down_grads, 0)
    for slot in range(2):
        store(down_grad_ref, 0, slot).wait()
    plane_sum.take_chain(plane_sum.target(1))
    plane_sum.take_side(plane_sum.target(2))
    chunks = width // tile
    lax.fori_loop(0, chunks // 2, entry_weight_grads, 0)
    plane_sum.take_chain(plane_sum.target(2))
    plane_sum.take_side(plane_sum.target(3))
    lax.fori_loop(chunks // 2, chunks, entry_weight_grads, 0)
    plane_sum.take_chain(plane_sum.target(3))
    plane_sum.close()
    entry_own[...] = plane_sum.total(level)
    for slot in range(2):
        for copy in store_both(slot):
            copy.wait()
        to_mate(0, slot).wait_send()
    plane_sum.drain()

    gather.drain()


def expert_layer(x_own, upstream_all, gate_all, up_all, down_all, experts):
    rows, span = x_own.shape
    total, width = upstream_all.shape
    units = down_all.shape[0]
    chips = total // (2 * rows)
    levels = chips // 2
    low = jnp.bfloat16
    vmem = pl.BlockSpec(memory_space=pltpu.VMEM)
    anywhere = pl.BlockSpec(memory_space=pl.ANY)
    dma = pltpu.SemaphoreType.DMA
    return pl.pallas_call(
        functools.partial(expert_kernel, experts),
        name="expert_layer",
        out_shape=[
            jax.ShapeDtypeStruct((rows, span), low),
            jax.ShapeDtypeStruct((total, width), low),
            jax.ShapeDtypeStruct((width, units), low),
            jax.ShapeDtypeStruct((width, units), low),
            jax.ShapeDtypeStruct((units, width), low),
        ],
        in_specs=[vmem] + [anywhere] * 4,
        out_specs=[vmem] + [anywhere] * 4,
        scratch_shapes=[
            pltpu.VMEM((chips, 2, rows, span), low),
            pltpu.VMEM((total, width), low),
            pltpu.VMEM((width, units), low),
            pltpu.VMEM((width, units), low),
            pltpu.VMEM((units, width), low),
            pltpu.VMEM((total, units), low),
            pltpu.VMEM((total, units), low),
            pltpu.VMEM((total, units), low),
            pltpu.VMEM((chips, 2 * rows, 128), low),
            pltpu.VMEM((chips, rows, span), low),
            pltpu.VMEM((2, rows, span), low),
            pltpu.VMEM((chips, rows, span), low),
            *ChainSums.buffers(levels, (rows, span)),
            pltpu.VMEM((2, 2 * rows, width), low),
            dma((5,)),
            dma((2,)),
            dma((2, 2)),
        ]
        + [dma((2,)), dma((chips,))]
        + RowGathers.semaphores(levels)
        + ChainSums.semaphores(levels),
        compiler_params=pltpu.CompilerParams(
            collective_id=5, has_side_effects=True, vmem_limit_bytes=65_400_000
        ),
        cost_estimate=link_cost(125),
    )(x_own, upstream_all, gate_all, up_all, down_all)


def attend_back_kernel(
    experts,
    entry_ref,
    residual_ref,
    gates_ref,
    dealt_ref,
    order_ref,
    router_ref,
    attn_gain,
    moe_gain,
    query_gain,
    key_gain,
    key_low,
    value_low,
    key_pre,
    cosine_ref,
    sine_ref,
    mixed_far,
    out_far,
    probs_far,
    query_low_far,
    query_pre_far,
    query_far,
    key_far,
    value_far,
    normed_far,
    out_part,
    gate_part,
    up_part,
    down_part,
    output_ref,
    token_grad_ref,
    small_ref,
    query_own,
    key_own,
    value_own,
    out_own,
    gate_arrived,
    up_arrived,
    down_arrived,
    finished_ref,
    returned_ref,
    small_own,
    small_near,
    small_pair,
    small_parts,
    query_gain_part,
    mixed_ref,
    out_w,
    probs_ref,
    query_low,
    query_pre,
    query_w,
    key_w,
    value_w,
    normed_ref,
    residual_grad,
    low_all,
    mixed_grad,
    low_grads,
    key_total,
    value_total,
    out_grad,
    out_sums,
    out_mate,
    out_side,
    out_chain,
    out_hop,
    out_side_two,
    out_chain_two,
    out_hop_two,
    weight_side,
    weight_chain,
    weight_hop,
    narrow_grad,
    narrow_side,
    narrow_chain,
    narrow_hop,
    near,
    pair,
    far,
    quad_send,
    quad_recv,
    share_send,
    share_recv,
    swap_send,
    swap_recv,
    keep_sem,
    pair_send,
    pair_recv,
    deal_send,
    deal_recv,
    small_send,
    small_recv,
    total_send,
    total_recv,
    free_sem,
    load_sem,
    join_send,
    join_recv,
    *ring_sems,
):
    place = Place()
    core, tp, level = place.core, place.tp, place.level
    wide, low = jnp.float32, jnp.bfloat16
    own_rows, width = residual_ref.shape
    group = 2 * own_rows
    rows = 2 * group
    head = query_gain.shape[1]
    heads = mixed_grad.shape[1] // head
    members = dealt_ref.shape[0]
    half = dealt_ref.shape[1] // 2
    step_rows = 4
    scale = head ** (-0.5)

    def dealt_rows(second):
        blocks = []
        for start in range(0, members, step_rows):
            block = dealt_ref[start : start + step_rows].astype(wide)
            block = block[:, half:] if second else block[:, :half]
            blocks.append(block.reshape(step_rows * half, width))
        return jnp.concatenate(blocks, axis=0)

    greet(place.plane_targets() + [place.across])

    def to_mate(origin):
        return remote(
            out_part.at[origin, 1 - core],
            out_mate.at[origin],
            join_send.at[origin],
            join_recv.at[origin],
            place.mate,
        )

    out_buffers = (out_side, out_chain, out_hop, out_side_two, out_chain_two, out_hop_two)
    out_ring = ChainSums(
        place, lambda chip: out_sums.at[chip], own_rows, out_buffers, ring_sems[:20]
    )

    def joined_at(turn):
        goal = out_ring.target(turn)
        return (goal * 2 + 1 - place.side, goal * 2 + place.side)

    def offer(turn, carry):
        for origin in joined_at(turn):
            to_mate(origin).start()
        return carry

    keep = pltpu.make_async_copy(out_part.at[:, core], out_sums, keep_sem.at[0])
    keep.start()
    lax.fori_loop(0, place.levels, offer, 0)
    loads = [
        pltpu.make_async_copy(src, dst, load_sem.at[i])
        for i, (src, dst) in enumerate(
            (
                (mixed_far, mixed_ref),
                (out_far, out_w),
                (probs_far, probs_ref),
                (query_low_far, query_low),
                (query_pre_far, query_pre),
                (query_far, query_w),
                (key_far, key_w),
                (value_far, value_w),
                (normed_far, normed_ref),
            )
        )
    ]
    for load in loads:
        load.start()

    def join(turn, carry):
        for origin in joined_at(turn):
            to_mate(origin).wait_recv()
            out_sums[origin] = (
                out_sums[origin].astype(wide) + out_mate[origin].astype(wide)
            ).astype(low)
        out_ring.send(out_ring.target(turn))
        return carry

    keep.wait()
    join(0, 0)

    entry = entry_ref[:, :width].astype(wide)
    extra = entry_ref[:, width:].astype(wide)
    gates = gates_ref[...]
    gate_grad = extra + pltpu.roll(extra, 128 - experts, 1)
    inner = jnp.sum(gates * gate_grad, axis=-1, keepdims=True)
    logit_grad = (gates * (gate_grad - inner)).astype(low)
    residual = residual_ref[...]
    factor = lax.rsqrt(jnp.mean(residual * residual, axis=-1, keepdims=True) + epsilon)
    moe_low = (residual * factor * moe_gain[...]).astype(low)
    router = jnp.concatenate(
        [router_ref[...], jnp.zeros((128 - experts, width), low)], axis=0
    )
    moe_grad = entry + jnp.dot(logit_grad, router, preferred_element_type=wide)
    small_own[:8, :] = jnp.zeros((8, width), wide)
    small_own[8:, :] = tn_dot(logit_grad, moe_low)[: small_own.shape[0] - 8]
    scaled = moe_grad * moe_gain[...]
    inner = jnp.mean(scaled * residual, axis=-1, keepdims=True)
    small_own[1:2, :] = jnp.sum(moe_grad * residual * factor, axis=0, keepdims=True)
    residual_grad[...] = dealt_rows(True) + factor * (
        scaled - residual * (factor * factor) * inner
    )
    low_all[core, tp] = residual_grad[...].astype(low)
    mine = low_all.at[core, tp]
    share_mate = remote(mine, mine, share_send.at[0], share_recv.at[0], place.mate)
    share_across = remote(mine, mine, share_send.at[1], share_recv.at[1], place.across)
    share_across.start()
    share_mate.start()
    units = gate_arrived.shape[1]
    pair_copies = [
        remote(
            part.at[:, lanes_at(1 - tp, units)],
            arrived,
            pair_send.at[i],
            pair_recv.at[i],
            place.across,
        )
        for i, (part, arrived) in enumerate(((gate_part, gate_arrived), (up_part, up_arrived)))
    ]
    pair_copies.append(
        remote(
            down_part.at[lanes_at(1 - tp, units)],
            down_arrived,
            pair_send.at[2],
            pair_recv.at[2],
            place.across,
        )
    )
    pair_copies[0].start()

    lanes = out_own.shape[1]
    weight_ring = ChainSum(
        place,
        lambda chip: out_grad.at[:, lanes_at(chip, 2 * lanes)],
        weight_side,
        weight_chain,
        weight_hop,
        ring_sems[20:30],
    )
    query_ring = ChainSums(
        place, lambda chip: out_sums.at[chip], own_rows, out_buffers, ring_sems[30:50]
    )
    narrow_ring = ChainSum(
        place,
        lambda chip: narrow_grad.at[chip],
        narrow_side,
        narrow_chain,
        narrow_hop,
        ring_sems[50:],
    )
    lax.fori_loop(1, place.levels, join, 0)
    out_ring.send_joined()
    other = low_all.at[core, 1 - tp]
    remote(other, other, share_send.at[1], share_recv.at[1], place.across).wait_recv()
    passed = remote(other, other, share_send.at[2], share_recv.at[2], place.mate)
    passed.start()
    for slot, piece in ((0, low_all.at[1 - core, tp]), (2, low_all.at[1 - core, 1 - tp])):
        remote(piece, piece, share_send.at[slot], share_recv.at[slot], place.mate).wait_recv()

    def out_grad_rows(index, carry):
        at = lanes_at(index, 256)
        left = mixed_ref[:, at]
        for first in range(0, width, 512):
            out_grad[at, first : first + 512] = tn_dot(
                left, low_all[:, :, :, first : first + 512].reshape(rows, 512)
            ).astype(low)
        return carry

    loads[0].wait()
    lax.fori_loop(0, mixed_ref.shape[1] // 256, out_grad_rows, 0)
    for turn in range(place.levels):
        weight_ring.send(weight_ring.target(turn))

    def mixed_lanes(index, carry):
        at = lanes_at(index, 256)
        mixed_grad[:, at] = nt_dot(low_all[...].reshape(rows, width), out_w[at, :]).astype(low)
        return carry

    loads[1].wait()
    lax.fori_loop(0, mixed_ref.shape[1] // 256, mixed_lanes, 0)
    for load in loads[2:]:
        load.wait()
    key_total[...] = jnp.zeros_like(key_total)
    value_total[...] = jnp.zeros_like(value_total)
    query_gain_part[...] = jnp.zeros_like(query_gain_part)

    def pre_back(grad, values, gain_ref, cosine, sine):
        grad = grad * cosine - pltpu.roll(grad, head // 2, 1) * sine
        factor = lax.rsqrt(jnp.mean(values * values, axis=-1, keepdims=True) + epsilon)
        scaled = grad * gain_ref[...]
        inner = jnp.mean(scaled * values, axis=-1, keepdims=True)
        back = factor * (scaled - values * (factor * factor) * inner)
        return back.astype(low), jnp.sum(grad * values * factor, axis=0, keepdims=True)

    batch = 4

    def attend_back(index, carry):
        which = index // (heads // batch)
        first = (index % (heads // batch)) * batch
        at_rows = lanes_at(which, group)
        key = key_low[at_rows, :]
        value = value_low[at_rows, :]
        cosine, sine = cosine_ref[at_rows, :], sine_ref[at_rows, :]
        key_sum = key_total[at_rows, :]
        value_sum = value_total[at_rows, :]
        gain_sum = query_gain_part[...]
        for offset in range(batch):
            at = lanes_at(first + offset, head)
            probs = probs_ref[which * heads + first + offset]
            grads = mixed_grad[at_rows, at]
            prob_grad = nt_dot(grads, value)
            probs_wide = probs.astype(wide)
            inner = jnp.sum(probs_wide * prob_grad, axis=-1, keepdims=True)
            score_grad = (probs_wide * (prob_grad - inner)).astype(low)
            query = jnp.dot(score_grad, key, preferred_element_type=wide) * scale
            key_sum += tn_dot(score_grad, query_low[at_rows, at])
            value_sum += tn_dot(probs, grads)
            values = query_pre[at_rows, at].astype(wide)
            back, terms = pre_back(query, values, query_gain, cosine, sine)
            low_grads[at_rows, at] = back
            gain_sum += terms
        key_total[at_rows, :] = key_sum
        value_total[at_rows, :] = value_sum
        query_gain_part[...] = gain_sum
        return carry

    count = 2 * heads // batch
    share = -(-count // place.levels)
    for turn in range(place.levels):
        out_ring.take_side(out_ring.target(turn))
        lax.fori_loop(min(turn * share, count), min((turn + 1) * share, count), attend_back, 0)
        out_ring.take_chain(out_ring.target(turn))

    weight_ring.send_joined()
    back, terms = pre_back(
        key_total[...] * scale, key_pre[...], key_gain, cosine_ref[...], sine_ref[...]
    )
    small_own[2:3, :head] = query_gain_part[...]
    small_own[2:3, head : 2 * head] = terms
    low_grads[:, heads * head : (heads + 1) * head] = back
    low_grads[:, (heads + 1) * head :] = value_total[...].astype(low)

    def normed_grad_rows(whose):
        at_rows = lanes_at(whose, group)

        def normed_grad_lanes(index, carry):
            at = lanes_at(index, 512)
            grads = low_grads[at_rows, :]
            product = (
                nt_dot(grads[:, : heads * head], query_w[at, :])
                + nt_dot(grads[:, heads * head : (heads + 1) * head], key_w[at, :])
                + nt_dot(grads[:, (heads + 1) * head :], value_w[at, :])
            )
            low_all[whose, :, :, at] = product.astype(low).reshape(2, own_rows, 512)
            return carry

        lax.fori_loop(0, width // 512, normed_grad_lanes, 0)

    share_mate.wait_send()
    share_across.wait_send()
    passed.wait_send()
    sums = QuadSum(place, low_all, near, pair, far, quad_send, quad_recv)
    normed_grad_rows(1 - core)
    sums.start()
    normed_grad_rows(core)
    sums.relay()
    out_ring.close()
    moe_own = out_ring.total(level).astype(wide)
    finished_ref[:, :half] = (residual_ref[...] + moe_own).reshape(members, half, width).astype(low)
    out_ring.drain()
    for target in place.ring_targets():
        pl.semaphore_signal(
            free_sem, inc=1, device_id=target, device_id_type=pl.DeviceIdType.MESH
        )

    def weight_grad_rows(index, carry):
        left = normed_ref[:, :, :, lanes_at(index, group)].reshape(rows, group)
        for first in range(0, heads * head, 512):
            grads = tn_dot(left, low_grads[:, first : first + 512]).astype(low)
            out_sums[index, :, first : first + 512] = grads[:own_rows]
            second = heads * head + first
            out_sums[index, :, second : second + 512] = grads[own_rows:]
        narrow_grad[index] = tn_dot(left, low_grads[:, heads * head :]).astype(low)
        return carry

    weight_ring.take_side(weight_ring.target(0))
    lax.fori_loop(0, place.chips, weight_grad_rows, 0)
    weight_ring.take_chain(weight_ring.target(0))
    normed_grad = sums.total()
    tokens = dealt_rows(False)
    factor = lax.rsqrt(jnp.mean(tokens * tokens, axis=-1, keepdims=True) + epsilon)
    scaled = normed_grad * attn_gain[...]
    inner = jnp.mean(scaled * tokens, axis=-1, keepdims=True)
    small_own[0:1, :] = jnp.sum(normed_grad * tokens * factor, axis=0, keepdims=True)
    small_across = remote(
        small_own, small_near, small_send.at[0], small_recv.at[0], place.across
    )
    small_across.start()
    pair_copies[1].start()
    pair_copies[2].start()
    token_grad = residual_grad[...] + factor * (scaled - tokens * (factor * factor) * inner)
    finished_ref[:, half:] = token_grad.reshape(members, half, width).astype(low)

    def deal_copy(offset, sending):
        target, index = place.member(offset if sending else -offset)
        return remote(
            finished_ref.at[index],
            returned_ref.at[place.fsdp if sending else index],
            deal_send.at[offset - 1],
            deal_recv.at[offset - 1],
            target,
        )

    share_lanes = width // members

    def small_copy(offset, sending):
        target, index = place.member(offset if sending else -offset)
        return remote(
            small_pair.at[:, lanes_at(index, share_lanes)],
            small_parts.at[place.fsdp if sending else index],
            small_send.at[offset],
            small_recv.at[offset],
            target,
        )

    def total_copy(offset, sending):
        target, index = place.member(offset if sending else -offset)
        piece = small_ref.at[:, lanes_at(place.fsdp if sending else index, share_lanes)]
        return remote(piece, piece, total_send.at[offset], total_recv.at[offset], target)

    weight_ring.take_side(weight_ring.target(1))
    small_across.wait_recv()
    small_pair[...] = small_own[...] + small_near[...]
    for offset in range(1, members):
        small_copy(offset, True).start()
    for offset in range(1, members):
        deal_copy(offset, True).start()
    own_slice = pltpu.make_async_copy(
        finished_ref.at[place.fsdp], returned_ref.at[place.fsdp], keep_sem.at[0]
    )
    own_slice.start()
    pl.semaphore_wait(free_sem, len(place.ring_targets()))
    last_rings = (query_ring, narrow_ring)
    for turn in range(place.levels):
        for ring in last_rings:
            ring.send(ring.target(turn))

    weight_ring.take_chain(weight_ring.target(1))
    for turn in range(2, place.levels):
        weight_ring.take_side(weight_ring.target(turn))
        weight_ring.take_chain(weight_ring.target(turn))
    weight_ring.close()
    for ring in last_rings:
        ring.send_joined()

    def swap_with_mate(slot, mine, theirs, here, there):
        kept = pltpu.make_async_copy(mine, here, keep_sem.at[slot])
        sent = remote(theirs, here, swap_send.at[slot], swap_recv.at[slot], place.mate)
        sent.start()
        kept.start()

        def finish():
            kept.wait()
            remote(there, there, swap_send.at[slot], swap_recv.at[slot], place.mate).wait_recv()
            sent.wait_send()

        return finish

    head_rows = out_grad.shape[0]
    finish_out = swap_with_mate(
        1,
        weight_side.at[level, :, lanes_at(core, lanes)],
        weight_side.at[level, :, lanes_at(1 - core, lanes)],
        out_own.at[lanes_at(core, head_rows)],
        out_own.at[lanes_at(1 - core, head_rows)],
    )
    for offset in range(1, members):
        small_copy(offset, False).wait_recv()
    small_parts[place.fsdp] = small_pair[:, lanes_at(place.fsdp, share_lanes)]
    total = small_parts[0]
    for member in range(1, members):
        total += small_parts[member]
    small_ref[:, lanes_at(place.fsdp, share_lanes)] = total
    for offset in range(1, members):
        total_copy(offset, True).start()
    for turn in range(place.levels):
        for ring in last_rings:
            ring.take_side(ring.target(turn))
            ring.take_chain(ring.target(turn))
    own_slice.wait()
    for offset in range(1, members):
        deal_copy(offset, False).wait_recv()
    for index in range(members):
        block = returned_ref[lax.rem(order_ref[index] + place.fsdp, members)].astype(wide)
        token_grad_ref[index] = block[half:]
        output_ref[index] = block[:half].astype(low)
    for ring in last_rings:
        ring.close()
    span = heads * head
    cut = own_rows // query_ring.count
    finish_query = [
        swap_with_mate(
            slot,
            ring.side_buf.at[level, :, lanes_at(core, span)],
            ring.side_buf.at[level, :, lanes_at(1 - core, span)],
            query_own.at[pl.ds(i * cut, cut), lanes_at(core, span)],
            query_own.at[pl.ds(i * cut, cut), lanes_at(1 - core, span)],
        )
        for i, (slot, ring) in enumerate(zip((2, 5), query_ring.rings))
    ]
    finish_narrow = [
        swap_with_mate(
            3 + i,
            narrow_side.at[level, lanes_at(core, own_rows), pl.ds(i * head, head)],
            narrow_side.at[level, lanes_at(1 - core, own_rows), pl.ds(i * head, head)],
            own.at[:, lanes_at(core, head)],
            own.at[:, lanes_at(1 - core, head)],
        )
        for i, own in enumerate((key_own, value_own))
    ]
    finish_out()
    for finish in finish_query + finish_narrow:
        finish()
    small_across.wait_send()
    for offset in range(1, members):
        deal_copy(offset, True).wait_send()
        small_copy(offset, True).wait_send()
        total_copy(offset, True).wait_send()
        total_copy(offset, False).wait_recv()
    for copy in pair_copies:
        copy.wait()

    def offered(origin, carry):
        to_mate(origin).wait_send()
        return carry

    lax.fori_loop(0, place.chips, offered, 0)
    sums.drain()
    for ring in (weight_ring, query_ring, narrow_ring):
        ring.drain()


def attend_back_layer(
    experts,
    entry,
    residual,
    gates,
    dealt,
    deal_order,
    router,
    gain_vecs,
    mixed,
    probs,
    query_low,
    key_low,
    value_low,
    query_pre,
    key_pre,
    tables,
    normed,
    query_w,
    key_w,
    value_w,
    out_w,
    out_part,
    gate_part,
    up_part,
    down_part,
):
    own_rows, width = residual.shape
    members = dealt.shape[0]
    levels = members // 4
    rows = 4 * own_rows
    heads_width, head = query_w.shape[1], key_w.shape[1]
    lanes = width // members
    wide, low = jnp.float32, jnp.bfloat16
    vmem = pl.BlockSpec(memory_space=pltpu.VMEM)
    anywhere = pl.BlockSpec(memory_space=pl.ANY)
    shape = jax.ShapeDtypeStruct
    dma = pltpu.SemaphoreType.DMA
    small = (8 + -(-experts // 8) * 8, width)
    late = (mixed, out_w, probs, query_low, query_pre, query_w, key_w, value_w, normed)
    return pl.pallas_call(
        functools.partial(attend_back_kernel, experts),
        name="attend_back_layer",
        out_shape=[
            shape((members, dealt.shape[1] // 2, width), low),
            shape((members, dealt.shape[1] // 2, width), wide),
            shape(small, wide),
            shape((own_rows, 2 * heads_width), low),
            shape((own_rows, 2 * head), low),
            shape((own_rows, 2 * head), low),
            shape((2 * heads_width, lanes), low),
            shape((width, gate_part.shape[1] // 2), low),
            shape((width, up_part.shape[1] // 2), low),
            shape((down_part.shape[0] // 2, width), low),
        ],
        in_specs=[vmem] * 4
        + [pl.BlockSpec(memory_space=pltpu.SMEM)]
        + [vmem] * 10
        + [anywhere] * 13,
        out_specs=[vmem] * 7 + [anywhere] * 3,
        scratch_shapes=[
            pltpu.VMEM(dealt.shape, low),
            pltpu.VMEM(dealt.shape, low),
            pltpu.VMEM(small, wide),
            pltpu.VMEM(small, wide),
            pltpu.VMEM(small, wide),
            pltpu.VMEM((members, small[0], width // members), wide),
            pltpu.VMEM((1, head), wide),
        ]
        + [pltpu.VMEM(array.shape, low) for array in late]
        + [
            pltpu.VMEM((own_rows, width), wide),
            pltpu.VMEM((2, 2, own_rows, width), low),
            pltpu.VMEM((rows, heads_width), low),
            pltpu.VMEM((rows, heads_width + 2 * head), low),
            pltpu.VMEM((rows, head), wide),
            pltpu.VMEM((rows, head), wide),
            pltpu.VMEM((heads_width, width), low),
            pltpu.VMEM((members // 2, own_rows, width), low),
            pltpu.VMEM((members // 2, own_rows, width), low),
            *ChainSums.buffers(levels, (own_rows, width)),
            *ChainSum.buffers(levels, (heads_width, 2 * lanes)),
            pltpu.VMEM((members // 2, 2 * own_rows, 2 * head), low),
            *ChainSum.buffers(levels, (2 * own_rows, 2 * head)),
        ]
        + QuadSum.scratch(own_rows, width)
        + [dma((3,)), dma((3,)), dma((6,)), dma((6,)), dma((6,)), dma((3,)), dma((3,))]
        + [dma((members,))] * 6
        + [pltpu.SemaphoreType.REGULAR, dma((9,)), dma((members // 2,)), dma((members // 2,))]
        + ChainSum.semaphores(levels) * 6,
        compiler_params=pltpu.CompilerParams(
            collective_id=3, has_side_effects=True, vmem_limit_bytes=65_400_000
        ),
        cost_estimate=link_cost(185),
    )(
        entry,
        residual,
        gates,
        dealt,
        deal_order,
        router,
        *gain_vecs,
        key_low,
        value_low,
        key_pre,
        *tables,
        *late,
        out_part,
        gate_part,
        up_part,
        down_part,
    )


def fast_body(
    tokens,
    lengths,
    routes,
    deal_order,
    cotangent,
    attn_gain,
    query_gain,
    key_gain,
    moe_gain,
    w_query,
    key_projection_matrix,
    value_projection_matrix,
    w_out,
    w_router,
    w_gate,
    w_up,
    w_down,
):
    own_rows, model_width = tokens.shape
    head_dim = query_gain.shape[0]
    chip_count = lax.axis_size("chip")
    core_count = lax.axis_size("core")
    tp_count = lax.axis_size("tp")
    core_index = lax.axis_index("core")
    tp_index = lax.axis_index("tp")
    fsdp_count = chip_count * core_count
    fsdp_index = lax.axis_index("chip") * core_count + core_index
    slice_rows = own_rows // fsdp_count
    group_rows = tp_count * own_rows
    quad_rows = core_count * group_rows
    plane = ("chip", "core")
    quad = ("core", "tp")

    def slices_of(values):
        return values.reshape(fsdp_count, slice_rows, model_width)

    down_full = lax.all_gather(w_down[0], "tp", axis=0, tiled=True)
    frequency = rope_base ** (-(jnp.arange(head_dim // 2, dtype=jnp.float32) * (2.0 / head_dim)))
    frequency = jnp.concatenate([frequency, frequency])[None, :]
    padded_lengths = jnp.pad(lengths, ((0, 7), (0, 128 - lengths.shape[1])))
    experts = w_router.shape[1]
    router_rows = w_router.T
    (
        dealt,
        normed,
        cosine_wide,
        sine_wide,
        moe_ext,
        residual,
        gates,
        query_pre,
        query_low,
        key_before_norm,
        key_low,
        value_low,
        probs_low,
        mixed_low,
        upstream_all,
        query_part,
        key_part,
        value_part,
        out_part,
        gate_full,
        up_full,
    ) = front_layer(
        experts,
        lengths.shape[1],
        slices_of(tokens),
        slices_of(cotangent),
        deal_order,
        attn_gain[None, :],
        padded_lengths,
        frequency,
        (query_gain[None, :], key_gain[None, :], moe_gain[None, :]),
        router_rows,
        routes.T,
        w_query,
        key_projection_matrix,
        value_projection_matrix,
        w_out,
        w_gate[0],
        w_up[0],
    )
    query_part = query_part.reshape(model_width, -1)
    key_part = key_part.reshape(model_width, -1)
    value_part = value_part.reshape(model_width, -1)
    upstream_all = upstream_all.reshape(fsdp_count * own_rows, model_width)
    entry_ext, moe_out, grad_w_gate, grad_w_up, grad_w_down = expert_layer(
        moe_ext, upstream_all, gate_full, up_full, down_full, experts
    )
    (
        output,
        grad_input,
        small,
        grad_w_query,
        grad_w_key,
        grad_w_value,
        grad_w_out,
        gate_arrived,
        up_arrived,
        down_arrived,
    ) = attend_back_layer(
        experts,
        entry_ext,
        residual,
        gates,
        dealt,
        deal_order,
        router_rows,
        (attn_gain[None, :], moe_gain[None, :], query_gain[None, :], key_gain[None, :]),
        mixed_low,
        probs_low,
        query_low,
        key_low,
        value_low,
        query_pre,
        key_before_norm,
        (cosine_wide, sine_wide),
        normed,
        query_part,
        key_part,
        value_part,
        out_part,
        moe_out.reshape(chip_count, core_count, own_rows, model_width),
        grad_w_gate,
        grad_w_up,
        grad_w_down,
    )
    def pair_sum(parts, arrived, dim):
        first, second = jnp.split(parts, 2, axis=dim)
        mine = jnp.where(tp_index == 0, first, second)
        return mine.astype(jnp.float32) + arrived.astype(jnp.float32)

    output = output.reshape(own_rows, model_width)
    grad_input = grad_input.reshape(own_rows, model_width)
    grad_w_router = small[8 : 8 + experts].T
    return (
        output,
        grad_input,
        small[0],
        small[2, :head_dim],
        small[2, head_dim : 2 * head_dim],
        small[1],
        grad_w_query.astype(jnp.float32),
        grad_w_key.astype(jnp.float32),
        grad_w_value.astype(jnp.float32),
        grad_w_out.astype(jnp.float32),
        grad_w_router,
        pair_sum(grad_w_gate, gate_arrived, 1)[None],
        pair_sum(grad_w_up, up_arrived, 1)[None],
        pair_sum(grad_w_down, down_arrived, 0)[None],
    )


def solution(mesh):
    fsdp_count, tp_count = mesh.shape["fsdp"], mesh.shape["tp"]
    chips = Mesh(mesh.devices.reshape(fsdp_count // 2, 2, tp_count), ("chip", "core", "tp"))
    dense = fsdp_count <= 16
    fsdp = ("chip", "core") if dense else "fsdp"
    every = ("chip", "core", "tp") if dense else ("fsdp", "tp")
    return jax.shard_map(
        fast_body if dense else body,
        mesh=chips if dense else mesh,
        in_specs=(
            P(every, None),
            P(fsdp, None),
            P(fsdp, None),
            P(),
            P(every, None),
            P(),
            P(),
            P(),
            P(),
            P(fsdp, "tp"),
            P(fsdp, "tp"),
            P(fsdp, "tp"),
            P("tp", fsdp),
            P(),
            P(fsdp, None, "tp"),
            P(fsdp, None, "tp"),
            P(fsdp, "tp", None),
        ),
        out_specs=(
            P(every, None),
            P(every, None),
            P(),
            P(),
            P(),
            P(),
            P(fsdp, "tp"),
            P(fsdp, "tp"),
            P(fsdp, "tp"),
            P("tp", fsdp),
            P(),
            P(fsdp, None, "tp"),
            P(fsdp, None, "tp"),
            P(fsdp, "tp", None),
        ),
        check_vma=False,
    )
```

```python
import functools

import jax
import jax.numpy as jnp
from jax import lax
from jax.experimental import pallas as pl
from jax.experimental.pallas import tpu as pltpu
from jax.sharding import Mesh
from jax.sharding import PartitionSpec as P

epsilon = 1e-06
rope_base = 1000000.0
masked_score = -1e30


def row_norm(values, gain_vec):
    factor = lax.rsqrt(jnp.mean(values * values, axis=-1, keepdims=True) + epsilon)
    return (values * factor * gain_vec, factor)


def norm_back(values, factor, gain_vec, upstream):
    scaled = upstream * gain_vec
    inner_term = jnp.mean(scaled * values, axis=-1, keepdims=True)
    return (factor * (scaled - values * (factor * factor) * inner_term), upstream * values * factor)


def seq_layout(seq_lengths, row_count):
    seq_ends = jnp.cumsum(seq_lengths)
    row_ids = jnp.arange(row_count, dtype=jnp.int32)
    segment = jnp.sum((row_ids[:, None] >= seq_ends[None, :]).astype(jnp.int32), axis=1)
    seq_starts = seq_ends - seq_lengths
    chosen = segment[:, None] == jnp.arange(seq_lengths.shape[0], dtype=jnp.int32)[None, :]
    position = row_ids - jnp.sum(jnp.where(chosen, seq_starts[None, :], 0), axis=1)
    return (segment, position)


def rotary(position, head_width):
    half_width = head_width // 2
    inverse_freq = rope_base ** (-(jnp.arange(half_width, dtype=jnp.float32) * (2.0 / head_width)))
    angles = position.astype(jnp.float32)[:, None] * inverse_freq[None, :]
    return (jnp.cos(angles)[:, None, :], jnp.sin(angles)[:, None, :])


def rotate(values, cosine_table, sine_table):
    half_width = values.shape[-1] // 2
    front_half = values[..., :half_width]
    back_half = values[..., half_width:]
    return jnp.concatenate(
        [
            front_half * cosine_table - back_half * sine_table,
            back_half * cosine_table + front_half * sine_table,
        ],
        axis=-1,
    )


def rotate_back(upstream, cosine_table, sine_table):
    half_width = upstream.shape[-1] // 2
    front_half = upstream[..., :half_width]
    back_half = upstream[..., half_width:]
    return jnp.concatenate(
        [
            front_half * cosine_table + back_half * sine_table,
            back_half * cosine_table - front_half * sine_table,
        ],
        axis=-1,
    )


def slot_table(route_rows, expert_count, capacity):
    row_count = route_rows.shape[0] * route_rows.shape[1]
    flat_routes = route_rows.reshape(row_count)
    expert_hits = (
        flat_routes[:, None] == jnp.arange(expert_count, dtype=jnp.int32)[None, :]
    ).astype(jnp.int32)
    earlier = jnp.cumsum(expert_hits, axis=0) - expert_hits
    slot_index = jnp.sum(earlier * expert_hits, axis=1)
    slot_place = flat_routes * capacity + slot_index
    slot_rows = jnp.full((expert_count * capacity,), row_count, jnp.int32)
    slot_rows = slot_rows.at[slot_place].set(jnp.arange(row_count, dtype=jnp.int32))
    return (slot_place, slot_rows.reshape(expert_count, capacity))


def contract_rows(left, right):
    return lax.dot_general(
        left, right, (((0,), (0,)), ((), ())), preferred_element_type=jnp.float32
    )


def contract_last(left, right):
    return lax.dot_general(
        left, right, (((1,), (1,)), ((), ())), preferred_element_type=jnp.float32
    )


def body(
    tokens,
    lengths,
    routes,
    deal_order,
    cotangent,
    attn_gain,
    query_gain,
    key_gain,
    moe_gain,
    w_query,
    key_projection_matrix,
    value_projection_matrix,
    w_out,
    w_router,
    w_gate,
    w_up,
    w_down,
):
    half_rows = tokens.shape[0]
    model_width = tokens.shape[1]
    head_dim = query_gain.shape[0]
    score_scale = head_dim ** (-0.5)
    fsdp_count = lax.axis_size("fsdp")
    tp_count = lax.axis_size("tp")
    fsdp_index = lax.axis_index("fsdp")
    tp_index = lax.axis_index("tp")
    slice_rows = half_rows // fsdp_count
    group_rows = tp_count * half_rows
    own_start = tp_index * half_rows
    peer_ids = jnp.arange(fsdp_count, dtype=jnp.int32)
    wanted = (peer_ids - fsdp_index) % fsdp_count
    send_pick = jnp.sum(
        jnp.where(deal_order[None, :] == wanted[:, None], peer_ids[None, :], 0), axis=1
    )
    back_pick = (deal_order + fsdp_index) % fsdp_count

    def deal_copies(values):
        slices = jnp.take(values.reshape(fsdp_count, slice_rows, model_width), send_pick, axis=0)
        return jnp.broadcast_to(slices[None], (tp_count, fsdp_count, slice_rows, model_width))

    tokens_all, cotangent_all = (
        lax.all_to_all(
            lax.all_to_all(deal_copies(tokens), "tp", split_axis=0, concat_axis=0, tiled=True),
            "fsdp",
            split_axis=1,
            concat_axis=1,
            tiled=True,
        ),
        lax.all_to_all(
            lax.all_to_all(deal_copies(cotangent), "tp", split_axis=0, concat_axis=0, tiled=True),
            "fsdp",
            split_axis=1,
            concat_axis=1,
            tiled=True,
        ),
    )
    tokens_in = tokens_all.reshape(group_rows, model_width).astype(jnp.float32)
    upstream = cotangent_all.reshape(group_rows, model_width).astype(jnp.float32)
    attn_in, attn_factor = row_norm(tokens_in, attn_gain)
    normed_all = attn_in.astype(jnp.bfloat16)
    query_full, key_full, value_full, out_full = (
        lax.all_gather(w_query, "fsdp", axis=0, tiled=True),
        lax.all_gather(key_projection_matrix, "fsdp", axis=0, tiled=True),
        lax.all_gather(value_projection_matrix, "fsdp", axis=0, tiled=True),
        lax.all_gather(w_out, "fsdp", axis=1, tiled=True),
    )
    query_heads = query_full.shape[1] // head_dim
    kv_heads = key_full.shape[1] // head_dim
    group_size = query_heads // kv_heads
    segment, position = seq_layout(lengths[0], group_rows)
    cosine_table, sine_table = rotary(position, head_dim)
    row_ids = jnp.arange(group_rows)
    allowed = (segment[:, None] == segment[None, :]) & (row_ids[None, :] <= row_ids[:, None])
    query_pre = jnp.dot(normed_all, query_full, preferred_element_type=jnp.float32).reshape(
        group_rows, query_heads, head_dim
    )
    query_normed, query_factor = row_norm(query_pre, query_gain)
    query_low = (
        rotate(query_normed, cosine_table, sine_table)
        .astype(jnp.bfloat16)
        .reshape(group_rows, kv_heads, group_size, head_dim)
    )
    key_before_norm = jnp.dot(normed_all, key_full, preferred_element_type=jnp.float32).reshape(
        group_rows, kv_heads, head_dim
    )
    key_normed, key_factor = row_norm(key_before_norm, key_gain)
    key_low = rotate(key_normed, cosine_table, sine_table).astype(jnp.bfloat16)
    value_low = (
        jnp.dot(normed_all, value_full, preferred_element_type=jnp.float32)
        .astype(jnp.bfloat16)
        .reshape(group_rows, kv_heads, head_dim)
    )
    scores = (
        jnp.einsum("qkgd,tkd->kgqt", query_low, key_low, preferred_element_type=jnp.float32)
        * score_scale
    )
    scores = jnp.where(allowed, scores, masked_score)
    row_peak = jnp.max(scores, axis=-1, keepdims=True)
    exponent = jnp.exp(scores - row_peak)
    totals = jnp.sum(exponent, axis=-1, keepdims=True)
    log_total = row_peak + jnp.log(totals)
    attn_probs = (exponent / totals).astype(jnp.bfloat16)
    attn_mixed = jnp.einsum(
        "kgqt,tkd->qkgd", attn_probs, value_low, preferred_element_type=jnp.float32
    )
    mixed_low = attn_mixed.reshape(group_rows, query_heads * head_dim).astype(jnp.bfloat16)
    attn_part = jnp.dot(mixed_low, out_full, preferred_element_type=jnp.float32)
    residual = tokens_in + lax.psum(attn_part, "tp")
    moe_in, moe_factor = row_norm(residual, moe_gain)
    moe_low = moe_in.astype(jnp.bfloat16)
    logits = jnp.dot(moe_low, w_router, preferred_element_type=jnp.float32)
    experts = w_router.shape[1]
    top_count = routes.shape[1]
    chosen = routes[:, :, None] == jnp.arange(experts, dtype=jnp.int32)[None, None, :]
    selected = jnp.sum(jnp.where(chosen, logits[:, None, :], 0.0), axis=-1)
    gate_peak = jnp.max(selected, axis=-1, keepdims=True)
    gate_exp = jnp.exp(selected - gate_peak)
    gate_probs = gate_exp / jnp.sum(gate_exp, axis=-1, keepdims=True)
    capacity = max(2, 3 * group_rows * top_count // (2 * experts))
    slot_place, slot_rows = slot_table(routes, experts, capacity)
    part_cap = capacity // tp_count
    slot_start = tp_index * part_cap
    gate_full, up_full, down_full = (
        lax.all_gather(w_gate, "tp", axis=2, tiled=True),
        lax.all_gather(w_up, "tp", axis=2, tiled=True),
        lax.all_gather(w_down, "tp", axis=1, tiled=True),
    )
    sent_rows = lax.dynamic_slice_in_dim(slot_rows, slot_start, part_cap, 1)
    slot_expert = slot_place // capacity
    slot_offset = slot_place % capacity - slot_start
    in_half = (slot_offset >= 0) & (slot_offset < part_cap)
    local_place = jnp.where(in_half, slot_expert * part_cap + slot_offset, experts * part_cap)
    padded = jnp.concatenate([moe_low, jnp.zeros((1, model_width), jnp.bfloat16)], axis=0)
    arrived = lax.all_to_all(
        padded[sent_rows // top_count], "fsdp", split_axis=0, concat_axis=0, tiled=True
    )
    local_experts = w_gate.shape[0]
    sources = experts // local_experts
    slot_count = sources * part_cap
    ff_part = w_gate.shape[2]

    def to_experts(values):
        return jnp.transpose(
            values.reshape(sources, local_experts, part_cap, model_width), (1, 0, 2, 3)
        ).reshape(local_experts, slot_count, model_width)

    def to_sources(values):
        width = values.shape[-1]
        return jnp.transpose(
            values.reshape(local_experts, sources, part_cap, width), (1, 0, 2, 3)
        ).reshape(experts, part_cap, width)

    def pick_rows(values):
        flat = values.reshape(experts * part_cap, tp_count * model_width)
        flat = jnp.concatenate([flat, jnp.zeros((1, tp_count * model_width), jnp.bfloat16)], axis=0)
        gathered = flat[local_place].reshape(group_rows, top_count, tp_count, model_width)
        return jnp.sum(gathered.astype(jnp.float32), axis=2)

    expert_rows = to_experts(arrived)
    gate_val = jnp.einsum(
        "esd,edf->esf", expert_rows, gate_full, preferred_element_type=jnp.float32
    )
    up_val = jnp.einsum("esd,edf->esf", expert_rows, up_full, preferred_element_type=jnp.float32)
    sigmoid_val = jax.nn.sigmoid(gate_val)
    swish_val = gate_val * sigmoid_val
    hidden_low = (swish_val * up_val).astype(jnp.bfloat16)
    hidden_blocks = hidden_low.reshape(local_experts, slot_count, tp_count, ff_part)
    down_blocks = down_full.reshape(local_experts, tp_count, ff_part, model_width)
    expert_out = (
        jnp.einsum(
            "esbf,ebfd->esbd", hidden_blocks, down_blocks, preferred_element_type=jnp.float32
        )
        .astype(jnp.bfloat16)
        .reshape(local_experts, slot_count, tp_count * model_width)
    )
    returned = lax.all_to_all(
        to_sources(expert_out), "fsdp", split_axis=0, concat_axis=0, tiled=True
    )
    picked = pick_rows(returned)
    moe_part = jnp.sum(gate_probs[:, :, None] * picked, axis=1)
    gate_grad_part = jnp.sum(upstream[:, None, :] * picked, axis=-1)
    weighted = (
        (gate_probs[:, :, None] * upstream[:, None, :])
        .astype(jnp.bfloat16)
        .reshape(group_rows * top_count, model_width)
    )
    weighted = jnp.concatenate([weighted, jnp.zeros((1, model_width), jnp.bfloat16)], axis=0)
    grad_arrived = lax.all_to_all(
        weighted[sent_rows], "fsdp", split_axis=0, concat_axis=0, tiled=True
    )
    grad_slots = to_experts(grad_arrived)
    hidden_grad = jnp.einsum(
        "esd,ebfd->esbf", grad_slots, down_blocks, preferred_element_type=jnp.float32
    ).reshape(local_experts, slot_count, tp_count * ff_part)
    swish_slope = sigmoid_val * (1.0 + gate_val * (1.0 - sigmoid_val))
    gate_val_grad = (hidden_grad * up_val * swish_slope).astype(jnp.bfloat16)
    up_val_grad = (hidden_grad * swish_val).astype(jnp.bfloat16)
    grad_w_down = jnp.einsum(
        "esbf,esd->ebfd", hidden_blocks, grad_slots, preferred_element_type=jnp.float32
    ).reshape(local_experts, tp_count * ff_part, model_width)
    grad_w_gate = jnp.einsum(
        "esd,esf->edf", expert_rows, gate_val_grad, preferred_element_type=jnp.float32
    )
    grad_w_up = jnp.einsum(
        "esd,esf->edf", expert_rows, up_val_grad, preferred_element_type=jnp.float32
    )
    gate_blocks = gate_full.reshape(local_experts, model_width, tp_count, ff_part)
    up_blocks = up_full.reshape(local_experts, model_width, tp_count, ff_part)
    entry_grad = (
        (
            jnp.einsum(
                "esbf,edbf->esbd",
                gate_val_grad.reshape(local_experts, slot_count, tp_count, ff_part),
                gate_blocks,
                preferred_element_type=jnp.float32,
            )
            + jnp.einsum(
                "esbf,edbf->esbd",
                up_val_grad.reshape(local_experts, slot_count, tp_count, ff_part),
                up_blocks,
                preferred_element_type=jnp.float32,
            )
        )
        .astype(jnp.bfloat16)
        .reshape(local_experts, slot_count, tp_count * model_width)
    )
    sent_back = lax.all_to_all(
        to_sources(entry_grad), "fsdp", split_axis=0, concat_axis=0, tiled=True
    )
    expert_grad = jnp.sum(pick_rows(sent_back), axis=1)
    grad_w_gate, grad_w_up, grad_w_down = (
        lax.psum_scatter(
            grad_w_gate.astype(jnp.bfloat16), "tp", scatter_dimension=2, tiled=True
        ).astype(jnp.float32),
        lax.psum_scatter(
            grad_w_up.astype(jnp.bfloat16), "tp", scatter_dimension=2, tiled=True
        ).astype(jnp.float32),
        lax.psum_scatter(
            grad_w_down.astype(jnp.bfloat16), "tp", scatter_dimension=1, tiled=True
        ).astype(jnp.float32),
    )
    moe_grad, gate_grad = (
        lax.psum(expert_grad.astype(jnp.bfloat16), "tp").astype(jnp.float32),
        lax.psum(gate_grad_part.astype(jnp.bfloat16), "tp").astype(jnp.float32),
    )
    gate_inner = jnp.sum(gate_probs * gate_grad, axis=-1, keepdims=True)
    selected_grad = gate_probs * (gate_grad - gate_inner)
    logit_grad = jnp.sum(jnp.where(chosen, selected_grad[:, :, None], 0.0), axis=1).astype(
        jnp.bfloat16
    )
    moe_grad = moe_grad + contract_last(logit_grad, w_router)
    router_grad = contract_rows(
        lax.dynamic_slice_in_dim(moe_low, own_start, half_rows, 0),
        lax.dynamic_slice_in_dim(logit_grad, own_start, half_rows, 0),
    )
    residual_from_norm, moe_gain_terms = norm_back(residual, moe_factor, moe_gain, moe_grad)
    residual_grad = upstream + residual_from_norm
    moe_gain_grad = jnp.sum(
        lax.dynamic_slice_in_dim(moe_gain_terms, own_start, half_rows, 0), axis=0
    )
    residual_low = residual_grad.astype(jnp.bfloat16)
    mixed_grad = (
        contract_last(residual_low, out_full)
        .astype(jnp.bfloat16)
        .reshape(group_rows, kv_heads, group_size, head_dim)
    )
    grad_w_out = contract_rows(mixed_low, residual_low)
    scores = (
        jnp.einsum("qkgd,tkd->kgqt", query_low, key_low, preferred_element_type=jnp.float32)
        * score_scale
    )
    scores = jnp.where(allowed, scores, masked_score)
    probs_full = jnp.exp(scores - log_total)
    prob_grad = jnp.einsum(
        "qkgd,tkd->kgqt", mixed_grad, value_low, preferred_element_type=jnp.float32
    )
    prob_inner = jnp.sum(probs_full * prob_grad, axis=-1, keepdims=True)
    score_grad = (probs_full * (prob_grad - prob_inner)).astype(jnp.bfloat16)
    query_grad = (
        jnp.einsum(
            "kgqt,tkd->qkgd", score_grad, key_low, preferred_element_type=jnp.float32
        ).reshape(group_rows, query_heads, head_dim)
        * score_scale
    )
    key_grad = (
        jnp.einsum("kgqt,qkgd->tkd", score_grad, query_low, preferred_element_type=jnp.float32)
        * score_scale
    )
    value_grad = (
        jnp.einsum(
            "kgqt,qkgd->tkd",
            probs_full.astype(jnp.bfloat16),
            mixed_grad,
            preferred_element_type=jnp.float32,
        )
        .astype(jnp.bfloat16)
        .reshape(group_rows, kv_heads * head_dim)
    )
    query_pre_grad, query_gain_terms = norm_back(
        query_pre, query_factor, query_gain, rotate_back(query_grad, cosine_table, sine_table)
    )
    key_pre_grad, key_gain_terms = norm_back(
        key_before_norm, key_factor, key_gain, rotate_back(key_grad, cosine_table, sine_table)
    )
    query_pre_low = query_pre_grad.astype(jnp.bfloat16).reshape(group_rows, query_heads * head_dim)
    key_pre_low = key_pre_grad.astype(jnp.bfloat16).reshape(group_rows, kv_heads * head_dim)
    grad_w_query = contract_rows(normed_all, query_pre_low)
    grad_w_key = contract_rows(normed_all, key_pre_low)
    grad_w_value = contract_rows(normed_all, value_grad)
    normed_grad = (
        contract_last(query_pre_low, query_full)
        + contract_last(key_pre_low, key_full)
        + contract_last(value_grad, value_full)
    )
    normed_grad_own, moe_own = (
        lax.psum_scatter(
            normed_grad.astype(jnp.bfloat16), "tp", scatter_dimension=0, tiled=True
        ).astype(jnp.float32),
        lax.psum_scatter(
            moe_part.astype(jnp.bfloat16), "tp", scatter_dimension=0, tiled=True
        ).astype(jnp.float32),
    )
    tokens_own = lax.dynamic_slice_in_dim(tokens_in, own_start, half_rows, 0)
    factor_own = lax.dynamic_slice_in_dim(attn_factor, own_start, half_rows, 0)
    tokens_from_norm, attn_gain_terms = norm_back(
        tokens_own, factor_own, attn_gain, normed_grad_own
    )
    grad_group = lax.dynamic_slice_in_dim(residual_grad, own_start, half_rows, 0) + tokens_from_norm
    residual_own = lax.dynamic_slice_in_dim(residual, own_start, half_rows, 0)
    output_group = (residual_own + moe_own).astype(jnp.bfloat16)
    back_output, back_grad = (
        lax.all_to_all(
            output_group.astype(jnp.float32)
            .reshape(fsdp_count, slice_rows, model_width)
            .astype(jnp.bfloat16),
            "fsdp",
            split_axis=0,
            concat_axis=0,
            tiled=True,
        ).astype(jnp.float32),
        lax.all_to_all(
            grad_group.reshape(fsdp_count, slice_rows, model_width).astype(jnp.bfloat16),
            "fsdp",
            split_axis=0,
            concat_axis=0,
            tiled=True,
        ).astype(jnp.float32),
    )
    output = (
        jnp.take(back_output, back_pick, axis=0)
        .reshape(half_rows, model_width)
        .astype(jnp.bfloat16)
    )
    grad_input = jnp.take(back_grad, back_pick, axis=0).reshape(half_rows, model_width)
    grad_w_query, grad_w_key, grad_w_value, grad_w_out = (
        lax.psum_scatter(grad_w_query, "fsdp", scatter_dimension=0, tiled=True),
        lax.psum_scatter(grad_w_key, "fsdp", scatter_dimension=0, tiled=True),
        lax.psum_scatter(grad_w_value, "fsdp", scatter_dimension=0, tiled=True),
        lax.psum_scatter(grad_w_out, "fsdp", scatter_dimension=1, tiled=True),
    )
    grad_attn_gain, grad_query_gain, grad_key_gain, grad_moe_gain, grad_w_router = lax.psum(
        (
            jnp.sum(attn_gain_terms, axis=0),
            jnp.sum(query_gain_terms, axis=(0, 1)),
            jnp.sum(key_gain_terms, axis=(0, 1)),
            moe_gain_grad,
            router_grad,
        ),
        ("fsdp", "tp"),
    )
    return (
        output,
        grad_input,
        grad_attn_gain,
        grad_query_gain,
        grad_key_gain,
        grad_moe_gain,
        grad_w_query,
        grad_w_key,
        grad_w_value,
        grad_w_out,
        grad_w_router,
        grad_w_gate,
        grad_w_up,
        grad_w_down,
    )


def remote(src, dst, send_sem, recv_sem, target):
    return pltpu.make_async_remote_copy(
        src_ref=src,
        dst_ref=dst,
        send_sem=send_sem,
        recv_sem=recv_sem,
        device_id=target,
        device_id_type=pl.DeviceIdType.MESH,
    )


def greet(targets):
    barrier = pltpu.get_barrier_semaphore()
    for target in targets:
        pl.semaphore_signal(
            barrier, inc=1, device_id=target, device_id_type=pl.DeviceIdType.MESH
        )
    pl.semaphore_wait(barrier, len(targets))


def link_cost(microseconds):
    return pl.CostEstimate(flops=0, bytes_accessed=microseconds * 3_000_000, transcendentals=0)


class Place:
    def __init__(self):
        self.chips = lax.axis_size("chip")
        self.levels = self.chips // 2
        self.chip = lax.axis_index("chip")
        self.core = lax.axis_index("core")
        self.tp = lax.axis_index("tp")
        self.level = self.chip // 2
        self.side = self.chip % 2
        self.fsdp = self.chip * 2 + self.core
        self.mate = {"core": 1 - self.core}
        self.across = {"tp": 1 - self.tp}
        self.beside = {"chip": self.level * 2 + 1 - self.side}
        self.above = {"chip": lax.rem(self.chip + 2, self.chips)}
        self.below = {"chip": lax.rem(self.chip + self.chips - 2, self.chips)}
        top = self.levels - 1
        self.upper = self.level // (self.levels // 2)
        self.end = top * self.upper
        self.next = self.end + 1 - 2 * self.upper
        self.at_end = self.level == self.end
        self.at_next = self.level == self.next
        outward = self.level * 2 + self.side + 4 * self.upper - 2
        inward = self.level * 2 + self.side + 2 - 4 * self.upper
        self.outward = {"chip": lax.rem(outward + self.chips, self.chips)}
        self.inward = {"chip": lax.rem(inward + self.chips, self.chips)}

    def member(self, offset):
        count = 2 * self.chips
        index = lax.rem(self.fsdp + offset + count, count)
        return {"chip": index // 2, "core": lax.rem(index, 2)}, index

    def plane_targets(self):
        return [self.member(offset)[0] for offset in range(1, 2 * self.chips)]

    def ring_targets(self):
        return [self.above, self.below, self.beside]


def lower_half(ref):
    return ref.at[pl.ds(0, ref.shape[0] // 2)]


def upper_half(ref):
    return ref.at[pl.ds(ref.shape[0] // 2, ref.shape[0] // 2)]


class RowGather:
    def __init__(self, place, block, sems, hands=True):
        self.place, self.block, self.hands = place, block, hands
        (
            self.up_send,
            self.up_recv,
            self.down_send,
            self.down_recv,
            self.side_send,
            self.side_recv,
            self.hop_send,
            self.hop_recv,
        ) = sems[:8]
        if hands:
            self.hand_send, self.hand_recv = sems[8:10]

    @staticmethod
    def semaphores(levels, hands=True):
        dma = pltpu.SemaphoreType.DMA
        return [dma((levels,))] * 6 + [dma, dma] + ([dma((2 * levels,))] * 2 if hands else [])

    def climb(self, origin):
        piece, at = self.block(origin, self.place.core), origin // 2
        return remote(piece, piece, self.up_send.at[at], self.up_recv.at[at], self.place.above)

    def sink(self, origin):
        piece, at = self.block(origin, self.place.core), origin // 2
        return remote(piece, piece, self.down_send.at[at], self.down_recv.at[at], self.place.below)

    def cross(self, origin, half=False):
        piece, at = self.block(origin, self.place.core), origin // 2
        if half:
            piece = upper_half(piece)
        return remote(piece, piece, self.side_send.at[at], self.side_recv.at[at], self.place.beside)

    def hop(self, level, inward):
        piece = self.block(level * 2 + 1 - self.place.side, self.place.core)
        if not inward:
            piece = lower_half(piece)
        target = self.place.inward if inward else self.place.outward
        return remote(piece, piece, self.hop_send, self.hop_recv, target)

    def hand(self, origin, whose):
        piece = self.block(origin, whose)
        return remote(
            piece, piece, self.hand_send.at[origin], self.hand_recv.at[origin], self.place.mate
        )

    def pass_on(self, origin):
        place = self.place
        at = origin // 2
        skipped = place.at_next & (at == place.end)
        halved = place.at_end & (at == place.next)

        @pl.when(halved)
        def _():
            self.cross(origin, True).start()

        @pl.when(~skipped & ~halved)
        def _():
            self.cross(origin).start()

        self.give(origin)

    def give(self, origin):
        if self.hands:
            self.hand(origin, self.place.core).start()

    def start(self):
        place = self.place

        @pl.when(place.level < place.levels - 1)
        def _():
            self.climb(place.chip).start()

        @pl.when(place.level > 0)
        def _():
            self.sink(place.chip).start()

        self.pass_on(place.chip)

    def crossed(self, at):
        place = self.place
        origin = at * 2 + 1 - place.side
        skipped = place.at_next & (at == place.end)
        halved = place.at_end & (at == place.next)

        @pl.when(skipped)
        def _():
            self.hop(place.end, True).wait_recv()

        @pl.when(halved)
        def _():
            self.cross(origin, True).wait_recv()

        @pl.when(~skipped & ~halved)
        def _():
            self.cross(origin).wait_recv()

        @pl.when(place.at_end & (at == place.end))
        def _():
            self.hop(place.end, True).start()

        @pl.when(~halved)
        def _():
            self.give(origin)

    def finish(self):
        place = self.place

        @pl.when(place.at_end)
        def _():
            self.hop(place.next, False).wait_recv()
            self.give(place.next * 2 + 1 - place.side)

    def step(self, n):
        place = self.place
        level, side, top = place.level, place.side, place.levels - 1
        under, over = level - n, level + n

        @pl.when((n > 0) & (under >= 0))
        def _():
            origin = under * 2 + side
            self.climb(origin).wait_recv()

            @pl.when(level < top)
            def _():
                self.climb(origin).start()

            self.pass_on(origin)

        @pl.when((n > 0) & (over <= top))
        def _():
            origin = over * 2 + side
            self.sink(origin).wait_recv()

            @pl.when(level > 0)
            def _():
                self.sink(origin).start()

            self.pass_on(origin)

        @pl.when(place.at_next & (n == place.levels - 2))
        def _():
            self.hop(place.next, False).start()

        @pl.when((n > 0) & (under + 1 >= 0))
        def _():
            self.crossed(under + 1)

        @pl.when((n > 1) & (over - 1 <= top))
        def _():
            self.crossed(over - 1)

    def take_hands(self):
        place = self.place

        def taken(origin, carry):
            self.hand(origin, 1 - place.core).wait_recv()
            return carry

        lax.fori_loop(0, place.chips, taken, 0)

    def drain(self):
        place = self.place
        level, side, top = place.level, place.side, place.levels - 1

        def handed(origin, carry):
            self.hand(origin, place.core).wait_send()
            return carry

        if self.hands:
            lax.fori_loop(0, place.chips, handed, 0)

        def sent(at, carry):
            skipped = place.at_next & (at == place.end)
            halved = place.at_end & (at == place.next)

            @pl.when(halved)
            def _():
                self.cross(at * 2 + side, True).wait_send()

            @pl.when(~skipped & ~halved)
            def _():
                self.cross(at * 2 + side).wait_send()

            @pl.when((level < top) & (at <= level))
            def _():
                self.climb(at * 2 + side).wait_send()

            @pl.when((level > 0) & (at >= level))
            def _():
                self.sink(at * 2 + side).wait_send()

            return carry

        lax.fori_loop(0, place.levels, sent, 0)

        @pl.when(place.at_end)
        def _():
            self.hop(place.end, True).wait_send()

        @pl.when(place.at_next)
        def _():
            self.hop(place.next, False).wait_send()


class RowGathers:
    def __init__(self, place, block, sems):
        count = len(sems) // 10
        self.rings = []
        for i in range(count):

            def piece(origin, whose, i=i):
                whole = block(origin, whose)
                rows = whole.shape[0] // count
                return whole.at[pl.ds(i * rows, rows)]

            self.rings.append(RowGather(place, piece, sems[10 * i : 10 * i + 10]))

    @staticmethod
    def semaphores(levels):
        return RowGather.semaphores(levels) * 2

    def start(self):
        for ring in self.rings:
            ring.start()

    def step(self, n):
        for ring in self.rings:
            ring.step(n)

    def finish(self):
        for ring in self.rings:
            ring.finish()

    def take_hand(self, origin, whose):
        for ring in self.rings:
            ring.hand(origin, whose).wait_recv()

    def take_hands(self):
        for ring in self.rings:
            ring.take_hands()

    def drain(self):
        for ring in self.rings:
            ring.drain()


class ChainSum:
    def __init__(self, place, parts, side_buf, chain_buf, hop_buf, sems):
        self.place, self.parts = place, parts
        self.side_buf, self.chain_buf, self.hop_buf = side_buf, chain_buf, hop_buf
        (
            self.up_send,
            self.up_recv,
            self.down_send,
            self.down_recv,
            self.side_send,
            self.side_recv,
            self.hop_send,
            self.hop_recv,
            self.half_send,
            self.half_recv,
        ) = sems

    @staticmethod
    def semaphores(levels):
        dma = pltpu.SemaphoreType.DMA
        return [dma((levels,))] * 6 + [dma] * 4

    @staticmethod
    def buffers(levels, block, dtype=jnp.bfloat16):
        return [
            pltpu.VMEM((levels,) + block, dtype),
            pltpu.VMEM((levels + 1,) + block, dtype),
            pltpu.VMEM(block, dtype),
        ]

    def target(self, turn):
        place = self.place
        top = place.levels - 1
        far, near = top - turn // 2, turn // 2
        odd = turn % 2
        low_half = far * (1 - odd) + near * odd
        high_half = near * (1 - odd) + far * odd
        inner = low_half * (1 - place.upper) + high_half * place.upper
        outer = (top - turn) * (1 - place.upper) + turn * place.upper
        return jnp.where(place.at_end, outer, inner)

    def from_under(self, goal):
        return self.chain_buf.at[goal + 1]

    def from_over(self, goal):
        return self.chain_buf.at[goal]

    def other(self, goal):
        return self.parts(goal * 2 + 1 - self.place.side)

    def cross(self, source, target, goal):
        return remote(
            source, target, self.side_send.at[goal], self.side_recv.at[goal], self.place.beside
        )

    def whole(self, goal):
        return self.cross(self.other(goal), self.side_buf.at[goal], goal)

    def lifted(self, goal):
        return self.cross(self.hop_buf, self.side_buf.at[goal], goal)

    def upper(self, goal):
        return self.cross(upper_half(self.other(goal)), upper_half(self.side_buf.at[goal]), goal)

    def lower(self, goal):
        return remote(
            lower_half(self.hop_buf),
            lower_half(self.side_buf.at[goal]),
            self.half_send,
            self.half_recv,
            self.place.beside,
        )

    def hop_out(self):
        return remote(
            self.other(self.place.end), self.hop_buf, self.hop_send, self.hop_recv, self.place.outward
        )

    def hop_in(self):
        return remote(
            lower_half(self.other(self.place.next)),
            lower_half(self.hop_buf),
            self.hop_send,
            self.hop_recv,
            self.place.inward,
        )

    def up(self, goal):
        return remote(
            self.side_buf.at[goal],
            self.from_under(goal),
            self.up_send.at[goal],
            self.up_recv.at[goal],
            self.place.above,
        )

    def down(self, goal):
        return remote(
            self.side_buf.at[goal],
            self.from_over(goal),
            self.down_send.at[goal],
            self.down_recv.at[goal],
            self.place.below,
        )

    def cases(self, goal):
        place = self.place
        to_end, to_next = goal == place.end, goal == place.next
        return (
            place.at_end & to_end,
            place.at_end & to_next,
            place.at_next & to_end,
            place.at_next & to_next,
        )

    def send(self, goal):
        end_end, end_next, next_end, next_next = self.cases(goal)

        @pl.when(end_next)
        def _():
            self.hop_in().start()

        @pl.when(next_end)
        def _():
            self.hop_out().start()

        @pl.when(end_next | next_next)
        def _():
            self.upper(goal).start()

        @pl.when(~(end_end | end_next | next_end | next_next))
        def _():
            self.whole(goal).start()

    def send_joined(self):
        place, wide = self.place, jnp.float32
        hop = self.hop_buf

        @pl.when(place.at_end)
        def _():
            self.hop_out().wait_recv()
            total = hop[...].astype(wide) + self.other(place.end)[...].astype(wide)
            hop[...] = total.astype(hop.dtype)
            self.lifted(place.end).start()

        @pl.when(place.at_next)
        def _():
            self.hop_in().wait_recv()
            half = hop.shape[0] // 2
            own = lower_half(self.other(place.next))[...].astype(wide)
            hop[:half] = (hop[:half].astype(wide) + own).astype(hop.dtype)
            self.lower(place.next).start()

    def add(self, goal, ref):
        held = self.side_buf
        total = held[goal].astype(jnp.float32) + ref[...].astype(jnp.float32)
        held[goal] = total.astype(held.dtype)

    def take_side(self, goal):
        place = self.place
        level, top = place.level, place.levels - 1
        end_end, end_next, next_end, next_next = self.cases(goal)
        held = self.side_buf
        own = self.parts(goal * 2 + place.side)
        half = held.shape[1] // 2

        @pl.when(end_next)
        def _():
            self.upper(goal).wait_recv()
            total = held[goal, half:].astype(jnp.float32) + upper_half(own)[...].astype(jnp.float32)
            held[goal, half:] = total.astype(held.dtype)
            held[goal, :half] = lower_half(own)[...]

        @pl.when(next_end)
        def _():
            held[goal] = own[...]

        @pl.when(next_next)
        def _():
            self.upper(goal).wait_recv()
            self.lower(goal).wait_recv()

        @pl.when(~(end_next | next_end | next_next))
        def _():
            self.whole(goal).wait_recv()

        @pl.when(~(end_next | next_end))
        def _():
            self.add(goal, own)

        @pl.when((goal > level) & (level == 0))
        def _():
            self.up(goal).start()

        @pl.when((goal < level) & (level == top))
        def _():
            self.down(goal).start()

    def take_chain(self, goal):
        place = self.place
        level, top = place.level, place.levels - 1

        @pl.when((goal > level) & (level > 0))
        def _():
            self.up(goal).wait_recv()
            self.add(goal, self.from_under(goal))
            self.up(goal).start()

        @pl.when((goal < level) & (level < top))
        def _():
            self.down(goal).wait_recv()
            self.add(goal, self.from_over(goal))
            self.down(goal).start()

    def close(self):
        place = self.place
        level, top = place.level, place.levels - 1

        @pl.when(level > 0)
        def _():
            self.up(level).wait_recv()
            self.add(level, self.from_under(level))

        @pl.when(level < top)
        def _():
            self.down(level).wait_recv()
            self.add(level, self.from_over(level))

    def drain(self):
        place = self.place

        def goal_done(goal, carry):
            end_end, end_next, next_end, next_next = self.cases(goal)

            @pl.when(end_end)
            def _():
                self.lifted(goal).wait_send()

            @pl.when(end_next)
            def _():
                self.hop_in().wait_send()

            @pl.when(next_end)
            def _():
                self.hop_out().wait_send()

            @pl.when(next_next)
            def _():
                self.lower(goal).wait_send()

            @pl.when(end_next | next_next)
            def _():
                self.upper(goal).wait_send()

            @pl.when(~(end_end | end_next | next_end | next_next))
            def _():
                self.whole(goal).wait_send()

            @pl.when(goal > place.level)
            def _():
                self.up(goal).wait_send()

            @pl.when(goal < place.level)
            def _():
                self.down(goal).wait_send()

            return carry

        lax.fori_loop(0, place.levels, goal_done, 0)


class ChainSums:
    count = 2

    def __init__(self, place, parts, rows, buffers, sems):
        self.rings = []
        for i in range(self.count):

            def piece(chip, i=i):
                return parts(chip).at[pl.ds(i * rows // self.count, rows // self.count)]

            self.rings.append(
                ChainSum(place, piece, *buffers[3 * i : 3 * i + 3], sems[10 * i : 10 * i + 10])
            )
        self.target = self.rings[0].target

    @classmethod
    def semaphores(cls, levels):
        return ChainSum.semaphores(levels) * cls.count

    @classmethod
    def buffers(cls, levels, block):
        return ChainSum.buffers(levels, (block[0] // cls.count,) + block[1:]) * cls.count

    def send(self, goal):
        for ring in self.rings:
            ring.send(goal)

    def send_joined(self):
        for ring in self.rings:
            ring.send_joined()

    def take_side(self, goal):
        for ring in self.rings:
            ring.take_side(goal)

    def take_chain(self, goal):
        for ring in self.rings:
            ring.take_chain(goal)

    def close(self):
        for ring in self.rings:
            ring.close()

    def drain(self):
        for ring in self.rings:
            ring.drain()

    def total(self, level):
        return jnp.concatenate([ring.side_buf[level] for ring in self.rings], axis=0)


class QuadSum:
    def __init__(self, place, parts, near, pair, far, send, recv):
        self.place, self.parts = place, parts
        self.near, self.pair, self.far = near, pair, far
        self.send, self.recv = send, recv

    @staticmethod
    def scratch(rows, width):
        low, dma = jnp.bfloat16, pltpu.SemaphoreType.DMA
        return [
            pltpu.VMEM((2, rows, width), low),
            pltpu.VMEM((rows, width), low),
            pltpu.VMEM((rows, width), low),
            dma((3,)),
            dma((3,)),
        ]

    def to_mate(self, half):
        return remote(
            self.parts.at[1 - self.place.core, half],
            self.near.at[half],
            self.send.at[half],
            self.recv.at[half],
            self.place.mate,
        )

    def to_across(self):
        return remote(self.pair, self.far, self.send.at[2], self.recv.at[2], self.place.across)

    def start(self):
        self.to_mate(1 - self.place.tp).start()
        self.to_mate(self.place.tp).start()

    def relay(self):
        core, tp, wide = self.place.core, self.place.tp, jnp.float32
        self.to_mate(1 - tp).wait_recv()
        self.pair[...] = (
            self.parts[core, 1 - tp].astype(wide) + self.near[1 - tp].astype(wide)
        ).astype(jnp.bfloat16)
        self.to_across().start()

    def total(self):
        core, tp, wide = self.place.core, self.place.tp, jnp.float32
        self.to_mate(tp).wait_recv()
        total = self.parts[core, tp].astype(wide) + self.near[tp].astype(wide)
        self.to_across().wait_recv()
        return total + self.far[...].astype(wide)

    def drain(self):
        for half in range(2):
            self.to_mate(half).wait_send()
        self.to_across().wait_send()


def nt_dot(left, right):
    return lax.dot_general(
        left, right, (((1,), (1,)), ((), ())), preferred_element_type=jnp.float32
    )


def tn_dot(left, right):
    return lax.dot_general(
        left, right, (((0,), (0,)), ((), ())), preferred_element_type=jnp.float32
    )


def lanes_at(index, width):
    return pl.ds(pl.multiple_of(index * width, width), width)


def front_kernel(
    sequences,
    experts,
    tokens_ref,
    cotangent_ref,
    order_ref,
    gain_ref,
    lengths_ref,
    frequency_ref,
    query_gain,
    key_gain,
    moe_gain,
    router_ref,
    routes_ref,
    query_ref,
    key_ref,
    value_ref,
    out_ref,
    gate_ref,
    up_ref,
    dealt_ref,
    normed_ref,
    cosine_ref,
    sine_ref,
    moe_ext,
    residual_ref,
    gates_ref,
    query_pre,
    query_low,
    key_pre,
    key_low,
    value_low,
    probs_ref,
    mixed_ref,
    upstream_all,
    query_all,
    key_all,
    value_all,
    out_all,
    gate_all,
    up_all,
    slices_ref,
    both_lengths_ref,
    mask_ref,
    upstream_own,
    query_w,
    key_w,
    value_w,
    out_w,
    router_rows,
    parts,
    near,
    pair,
    far,
    sum_send,
    sum_recv,
    deal_send,
    deal_recv,
    quad_send,
    quad_recv,
    swap_send,
    swap_recv,
    keep_sem,
    pair_send,
    pair_recv,
    pair_keep,
    load_sem,
    *ring_sems,
):
    place = Place()
    core, chip = place.core, place.chip
    wide, low = jnp.float32, jnp.bfloat16
    own_rows = query_ref.shape[0]
    width = dealt_ref.shape[2]
    quarter = query_all.shape[2]
    narrow = key_all.shape[2]
    head_rows = out_all.shape[0]
    lanes = out_ref.shape[1]
    members = 2 * place.chips
    for index in range(members):
        wanted = lax.rem(index - place.fsdp + members, members)
        picked = 0
        for at in range(members):
            picked += jnp.where(order_ref[at] == wanted, at, 0)
        picked = lax.rem(picked, members)
        both = [ref[picked].astype(jnp.float32) for ref in (tokens_ref, cotangent_ref)]
        slices_ref[index] = jnp.concatenate(both, axis=0).astype(jnp.bfloat16)
    greet(place.plane_targets() + [place.across])

    def deal_copy(offset, sending):
        target, index = place.member(offset if sending else -offset)
        return remote(
            slices_ref.at[index],
            dealt_ref.at[place.fsdp if sending else index],
            deal_send.at[offset - 1],
            deal_recv.at[offset - 1],
            target,
        )

    for offset in range(1, members):
        deal_copy(offset, True).start()

    def rows(who):
        return pl.ds(pl.multiple_of(who * own_rows, own_rows), own_rows)

    def columns(who, width):
        return pl.ds(pl.multiple_of(who * width, width), width)

    def spots(who):
        lane_start = pl.multiple_of((2 * chip + core) * lanes, lanes)
        return [
            (query_ref.at[:, columns(who, quarter)], query_all.at[chip, rows(core)]),
            (key_ref.at[:, columns(who, narrow)], key_all.at[chip, rows(core)]),
            (value_ref.at[:, columns(who, narrow)], value_all.at[chip, rows(core)]),
            (
                out_ref.at[pl.ds(pl.multiple_of(who * head_rows, head_rows), head_rows)],
                out_all.at[:, pl.ds(lane_start, lanes)],
            ),
        ]

    def arrivals():
        lane_start = pl.multiple_of((2 * chip + 1 - core) * lanes, lanes)
        return [
            query_all.at[chip, rows(1 - core)],
            key_all.at[chip, rows(1 - core)],
            value_all.at[chip, rows(1 - core)],
            out_all.at[:, pl.ds(lane_start, lanes)],
        ]

    sends = [
        remote(src, dst, swap_send.at[i], swap_recv.at[i], place.mate)
        for i, (src, dst) in enumerate(spots(1 - core))
    ]
    keeps = [
        pltpu.make_async_copy(src, dst, keep_sem.at[i])
        for i, (src, dst) in enumerate(spots(core))
    ]
    mate_lengths = remote(
        lengths_ref, both_lengths_ref.at[core], swap_send.at[4], swap_recv.at[4], place.mate
    )
    own_lengths = pltpu.make_async_copy(lengths_ref, both_lengths_ref.at[core], keep_sem.at[4])
    own_slice = pltpu.make_async_copy(
        slices_ref.at[place.fsdp], dealt_ref.at[place.fsdp], keep_sem.at[5]
    )
    own_slice.start()
    units = gate_ref.shape[1]

    def halves(who):
        at = pl.ds(pl.multiple_of(who * units, units), units)
        return [gate_all.at[:, at], up_all.at[:, at]]

    shards = (gate_ref, up_ref)
    pair_copies = []
    for i, (src, dst) in enumerate(zip(shards, halves(place.tp))):
        pair_copies.append(
            (
                remote(src, dst, pair_send.at[i], pair_recv.at[i], place.across),
                pltpu.make_async_copy(src, dst, pair_keep.at[i]),
            )
        )
    for i in range(4):
        sends[i].start()
        keeps[i].start()
    mate_lengths.start()
    own_lengths.start()

    out_lanes = 2 * lanes
    views = [
        lambda who, core: query_all.at[who],
        lambda who, core: key_all.at[who],
        lambda who, core: value_all.at[who],
        lambda who, core: out_all.at[:, lanes_at(who, out_lanes)],
    ]
    rings = [
        RowGather(place, view, ring_sems[8 * i : 8 * i + 8], hands=False)
        for i, view in enumerate(views)
    ]
    landed = arrivals()
    upstream_ring = RowGathers(
        place, lambda origin, whose: upstream_all.at[origin, whose], ring_sems[32:]
    )
    for i in range(4):
        keeps[i].wait()
        sends[i].wait_send()
        remote(landed[i], landed[i], swap_send.at[i], swap_recv.at[i], place.mate).wait_recv()
        rings[i].start()

    own_slice.wait()
    for offset in range(1, members):
        deal_copy(offset, False).wait_recv()
    tp = place.tp
    half = slices_ref.shape[1] // 2
    step_rows = 4
    width = dealt_ref.shape[2]
    for start in range(0, members, step_rows):
        block = dealt_ref[start : start + step_rows].astype(jnp.float32)
        span = slice(start * half, (start + step_rows) * half)
        upstream_own[span, :] = (
            block[:, half:].reshape(step_rows * half, block.shape[2]).astype(jnp.bfloat16)
        )
        x = block[:, :half].reshape(step_rows * half, block.shape[2])
        factor = lax.rsqrt(jnp.mean(x * x, axis=-1, keepdims=True) + epsilon)
        normed_ref[core, tp, start * half : (start + step_rows) * half, :] = (
            x * factor * gain_ref[...]
        ).astype(jnp.bfloat16)
    mine = normed_ref.at[core, tp]
    to_mate = remote(mine, mine, quad_send.at[0], quad_recv.at[0], place.mate)
    to_across = remote(mine, mine, quad_send.at[1], quad_recv.at[1], place.across)
    to_across.start()
    to_mate.start()
    for both in pair_copies:
        both[0].start()
        both[1].start()
    keep_upstream = pltpu.make_async_copy(upstream_own, upstream_all.at[chip, core], keep_sem.at[6])
    keep_upstream.start()
    levels = place.levels
    own_lengths.wait()
    mate_lengths.wait_send()
    theirs = both_lengths_ref.at[1 - core]
    remote(theirs, theirs, swap_send.at[4], swap_recv.at[4], place.mate).wait_recv()
    group = mask_ref.shape[1]
    head = cosine_ref.shape[1]
    heads = query_w.shape[2] // head
    across_sign = jnp.where(
        lax.broadcasted_iota(jnp.int32, (group, head), 1) < head // 2, -1.0, 1.0
    )
    for which in range(2):
        ends = []
        for at in range(sequences):
            length = both_lengths_ref[which, 0:1, at : at + 1]
            ends.append(length if at == 0 else ends[-1] + length)

        def segment_start(place_ids):
            start = jnp.zeros_like(place_ids)
            for end in ends:
                start = jnp.where(place_ids >= end, end, start)
            return start

        at_rows = pl.ds(which * group, group)
        row_ids = lax.broadcasted_iota(jnp.int32, (group, head), 0)
        position = (row_ids - segment_start(row_ids)).astype(jnp.float32)
        angles = position * frequency_ref[...]
        cosine_ref[at_rows, :] = jnp.cos(angles)
        sine_ref[at_rows, :] = jnp.sin(angles) * across_sign
        row_ids = lax.broadcasted_iota(jnp.int32, (group, group), 0)
        key_ids = lax.broadcasted_iota(jnp.int32, (group, group), 1)
        allowed = (key_ids <= row_ids) & (key_ids >= segment_start(row_ids))
        mask_ref[which] = jnp.where(allowed, 0.0, masked_score)
    early, late = rings[:3], rings[3]
    for ring in rings:
        ring.step(1)
    other = normed_ref.at[core, 1 - tp]
    remote(other, other, quad_send.at[1], quad_recv.at[1], place.across).wait_recv()
    passed = remote(other, other, quad_send.at[2], quad_recv.at[2], place.mate)
    passed.start()
    keep_upstream.wait()
    for n in range(2, levels):
        for ring in rings:
            ring.step(n)
        if n == 2:
            upstream_ring.start()
    for ring in early:
        ring.step(levels)
        ring.finish()
    loads = [
        pltpu.make_async_copy(src, dst, load_sem.at[i])
        for i, (src, dst) in enumerate(
            ((query_all, query_w), (key_all, key_w), (value_all, value_w), (out_all, out_w))
        )
    ]
    for load in loads[:3]:
        load.start()
    router_rows[...] = jnp.zeros_like(router_rows)
    router_rows[:experts, :] = router_ref[...]
    for slot, piece in ((0, normed_ref.at[1 - core, tp]), (2, normed_ref.at[1 - core, 1 - tp])):
        remote(piece, piece, quad_send.at[slot], quad_recv.at[slot], place.mate).wait_recv()
    for load in loads[:3]:
        load.wait()

    def turned(values, gain_ref):
        factor = lax.rsqrt(jnp.mean(values * values, axis=-1, keepdims=True) + epsilon)
        scaled = values * factor * gain_ref[...]
        return (scaled * cosine_ref[...] + pltpu.roll(scaled, head // 2, 1) * sine_ref[...]).astype(
            low
        )

    x = normed_ref[...].reshape(2 * group, width)

    def project(index, carry):
        both = jnp.dot(
            normed_ref[...].reshape(2 * group, width),
            query_w[:, :, lanes_at(index, 2 * head)].reshape(width, 2 * head),
            preferred_element_type=wide,
        )
        query_pre[:, lanes_at(index, 2 * head)] = both.astype(low)
        for which in range(2):
            one = both[:, which * head : (which + 1) * head]
            query_low[:, lanes_at(2 * index + which, head)] = turned(one, query_gain)
        return carry

    lax.fori_loop(0, heads // 2, project, 0)
    key_values = jnp.dot(x, key_w[...].reshape(width, head), preferred_element_type=wide)
    key_pre[...] = key_values
    key_low[...] = turned(key_values, key_gain)
    value_low[...] = jnp.dot(x, value_w[...].reshape(width, head), preferred_element_type=wide).astype(low)
    late.step(levels)
    late.finish()
    loads[3].start()
    upstream_ring.step(1)
    scale = head ** (-0.5)
    batch = 4

    def attend(index, carry):
        which = index // (heads // batch)
        first = (index % (heads // batch)) * batch
        rows = lanes_at(which, group)
        key = key_low[rows, :]
        value = value_low[rows, :]
        mask = mask_ref[which]
        for offset in range(batch):
            at = lanes_at(first + offset, head)
            scores = nt_dot(query_low[rows, at], key) * scale + mask
            peak = jnp.max(scores, axis=-1, keepdims=True)
            exponent = jnp.exp(scores - peak)
            probs = (exponent * (1.0 / jnp.sum(exponent, axis=-1, keepdims=True))).astype(low)
            probs_ref[which * heads + first + offset] = probs
            mixed_ref[rows, at] = jnp.dot(probs, value, preferred_element_type=wide).astype(low)
        return carry

    lax.fori_loop(0, 2 * heads // batch, attend, 0)
    loads[3].wait()

    def out_rows(whose):
        left = mixed_ref[lanes_at(whose, group), :]

        def out_lanes(index, carry):
            at = lanes_at(index, 512)
            product = jnp.dot(left, out_w[:, at], preferred_element_type=wide).astype(low)
            parts[whose, :, :, at] = product.reshape(2, own_rows, 512)
            return carry

        lax.fori_loop(0, width // 512, out_lanes, 0)

    sums = QuadSum(place, parts, near, pair, far, quad_send, quad_recv)
    sums = QuadSum(place, parts, near, pair, far, sum_send, sum_recv)
    out_rows(1 - core)
    sums.start()
    out_rows(core)
    upstream_ring.step(2)
    sums.relay()
    upstream_ring.step(3)
    total = sums.total()

    def token_rows(start):
        block = dealt_ref[start : start + step_rows].astype(wide)[:, :half]
        return block.reshape(step_rows * half, width)

    tokens = jnp.concatenate(
        [token_rows(start) for start in range(0, members, step_rows)], axis=0
    )
    residual = tokens + total
    residual_ref[...] = residual
    factor = lax.rsqrt(jnp.mean(residual * residual, axis=-1, keepdims=True) + epsilon)
    moe_low = (residual * factor * moe_gain[...]).astype(low)
    moe_ext[:, :width] = moe_low
    logits = nt_dot(moe_low, router_rows[...])
    own_routes = routes_ref[:, lanes_at(place.tp, own_rows)]
    expert = lax.broadcasted_iota(jnp.int32, (128, own_rows), 0)
    chosen = jnp.zeros((128, own_rows), wide)
    for choice in range(own_routes.shape[0]):
        chosen += jnp.where(own_routes[choice : choice + 1, :] == expert, 1.0, 0.0)
    chosen = chosen.T > 0.0
    logits = jnp.where(chosen, logits, masked_score)
    exponent = jnp.exp(logits - jnp.max(logits, axis=-1, keepdims=True))
    exponent = jnp.where(chosen, exponent, 0.0)
    gates = exponent / jnp.sum(exponent, axis=-1, keepdims=True)
    gates_ref[...] = gates
    high = gates.astype(low).astype(wide)
    middle = (gates - high).astype(low).astype(wide)
    rest = gates - high - middle
    moe_ext[:, width:] = (
        high + pltpu.roll(middle, experts, 1) + pltpu.roll(rest, 2 * experts, 1)
    ).astype(low)
    for n in range(4, levels + 1):
        upstream_ring.step(n)
    upstream_ring.finish()
    upstream_ring.take_hands()
    upstream_ring.drain()
    sums.drain()
    for ring in rings:
        ring.drain()
    for offset in range(1, members):
        deal_copy(offset, True).wait_send()
    to_mate.wait_send()
    to_across.wait_send()
    passed.wait_send()
    for i, dst in enumerate(halves(1 - place.tp)):
        pair_copies[i][1].wait()
        pair_copies[i][0].wait_send()
        remote(dst, dst, pair_send.at[i], pair_recv.at[i], place.across).wait_recv()


def front_layer(
    experts,
    sequences,
    tokens,
    cotangent,
    deal_order,
    gain_vec,
    lengths,
    frequency,
    gain_vecs,
    router,
    routes,
    w_query,
    w_key,
    w_value,
    w_out,
    w_gate,
    w_up,
):
    members, slice_rows, width = tokens.shape
    dealt_shape = (members, 2 * slice_rows, width)
    chips = members // 2
    levels = chips // 2
    own_rows = w_query.shape[0]
    wide, low = jnp.float32, jnp.bfloat16
    vmem = pl.BlockSpec(memory_space=pltpu.VMEM)
    anywhere = pl.BlockSpec(memory_space=pl.ANY)
    dma = pltpu.SemaphoreType.DMA
    shape = jax.ShapeDtypeStruct
    group, head = 2 * own_rows, frequency.shape[1]
    rows, heads_width = 2 * group, w_query.shape[1] // 2
    weights = [(chips, 2 * own_rows, w.shape[1] // 2) for w in (w_query, w_key, w_value)]
    weights.append((w_out.shape[0] // 2, members * w_out.shape[1]))
    return pl.pallas_call(
        functools.partial(front_kernel, sequences, experts),
        name="front_layer",
        out_shape=[
            shape(dealt_shape, low),
            shape((2, 2, own_rows, width), low),
            shape((rows, head), wide),
            shape((rows, head), wide),
            shape((own_rows, width + 128), low),
            shape((own_rows, width), wide),
            shape((own_rows, 128), wide),
            shape((rows, heads_width), low),
            shape((rows, heads_width), low),
            shape((rows, head), wide),
            shape((rows, head), low),
            shape((rows, head), low),
            shape((2 * heads_width // head, group, group), low),
            shape((rows, heads_width), low),
            shape((chips, 2, own_rows, width), low),
        ]
        + [shape(weight, low) for weight in weights]
        + [shape((width, 2 * w_gate.shape[1]), low), shape((width, 2 * w_up.shape[1]), low)],
        in_specs=[vmem] * 2
        + [pl.BlockSpec(memory_space=pltpu.SMEM)]
        + [vmem] * 8
        + [anywhere] * 6,
        out_specs=[vmem] * 14 + [anywhere] * 7,
        scratch_shapes=[
            pltpu.VMEM(dealt_shape, low),
            pltpu.VMEM((2,) + lengths.shape, jnp.int32),
            pltpu.VMEM((2, group, group), wide),
            pltpu.VMEM((own_rows, width), low),
        ]
        + [pltpu.VMEM(weight, low) for weight in weights]
        + [pltpu.VMEM((128, width), low), pltpu.VMEM((2, 2, own_rows, width), low)]
        + QuadSum.scratch(own_rows, width)
        + [
            dma((members - 1,)),
            dma((members - 1,)),
            dma((3,)),
            dma((3,)),
            dma((5,)),
            dma((5,)),
            dma((7,)),
            dma((2,)),
            dma((2,)),
            dma((2,)),
            dma((4,)),
        ]
        + RowGather.semaphores(levels, hands=False) * 4
        + RowGathers.semaphores(levels),
        compiler_params=pltpu.CompilerParams(
            collective_id=0, has_side_effects=True, vmem_limit_bytes=65_400_000
        ),
        cost_estimate=link_cost(170),
    )(
        tokens,
        cotangent,
        deal_order,
        gain_vec,
        lengths,
        frequency,
        *gain_vecs,
        router,
        routes,
        w_query,
        w_key,
        w_value,
        w_out,
        w_gate,
        w_up,
    )


def expert_kernel(
    experts,
    x_own,
    upstream_ref,
    gate_ref,
    up_ref,
    down_ref,
    entry_own,
    out_part,
    gate_grad_ref,
    up_grad_ref,
    down_grad_ref,
    x_all,
    u_all,
    gate_w,
    up_w,
    down_w,
    hidden,
    gate_val_grad,
    up_val_grad,
    scores,
    sums,
    mate_out,
    mate_in,
    *rest,
):
    buffers, rest = rest[:6], rest[6:]
    staged, load_sem, store_sem, both_sem, mate_send, mate_recv = rest[:6]
    ring_sems = rest[6:]
    place = Place()
    core, chip, level, side = place.core, place.chip, place.level, place.side
    levels, top = place.levels, place.levels - 1
    rows = x_own.shape[0]
    tile = 2 * rows
    width = upstream_ref.shape[1]
    units = down_ref.shape[0]
    wide = jnp.float32
    low = jnp.bfloat16
    loads = [
        pltpu.make_async_copy(x_own, x_all.at[chip, core], load_sem.at[0]),
        pltpu.make_async_copy(gate_ref, gate_w, load_sem.at[1]),
        pltpu.make_async_copy(up_ref, up_w, load_sem.at[2]),
        pltpu.make_async_copy(down_ref, down_w, load_sem.at[3]),
        pltpu.make_async_copy(upstream_ref, u_all, load_sem.at[4]),
    ]
    for load in loads:
        load.start()
    greet(place.ring_targets() + [place.mate])

    gather = RowGathers(place, lambda origin, whose: x_all.at[origin, whose], ring_sems[:20])
    loads[0].wait()

    gather.start()
    for load in loads[1:]:
        load.wait()

    lane = lax.broadcasted_iota(jnp.int32, (128, 128), 0)
    select = (
        (lane == place.fsdp)
        | (lane == place.fsdp + experts)
        | (lane == place.fsdp + 2 * experts)
    ).astype(low)
    cut = 256
    across_lanes = lax.broadcasted_iota(jnp.int32, (tile, 128), 1)

    def forward_tile(origin):
        x = x_all[origin].reshape(tile, x_all.shape[3])
        gate_lanes = jnp.dot(x[:, width:], select, preferred_element_type=wide)
        gate = jnp.concatenate([gate_lanes] * (cut // 128), axis=1)
        x = x[:, :width]
        start = pl.multiple_of(origin * tile, tile)
        u = u_all[pl.ds(start, tile), :]
        score = jnp.zeros((tile, 1), wide)
        for part in range(units // cut):
            lanes = slice(part * cut, (part + 1) * cut)
            gate_val = jnp.dot(x, gate_w[:, lanes], preferred_element_type=wide)
            up_val = jnp.dot(x, up_w[:, lanes], preferred_element_type=wide)
            back = lax.dot_general(
                u, down_w[lanes, :], (((1,), (1,)), ((), ())), preferred_element_type=wide
            )
            sigmoid = 1.0 / (1.0 + jnp.exp(-gate_val))
            swish = gate_val * sigmoid
            out = (swish * up_val).astype(low).astype(wide)
            score += jnp.sum(out * back, axis=1, keepdims=True)
            back = back * gate
            slope = sigmoid * (1.0 + gate_val * (1.0 - sigmoid))
            hidden[pl.ds(start, tile), lanes] = (out * gate).astype(low)
            gate_val_grad[pl.ds(start, tile), lanes] = (back * up_val * slope).astype(low)
            up_val_grad[pl.ds(start, tile), lanes] = (back * swish).astype(low)
        high = score.astype(low).astype(wide)
        packed = jnp.where(
            across_lanes == place.fsdp,
            high,
            jnp.where(across_lanes == place.fsdp + experts, score - high, 0.0),
        )
        scores[origin] = packed.astype(low)

    def gather_step(n, carry):
        gather.step(n)

        def candidate(which, carried):
            upward = which % 2
            facing = which // 2
            distance = n - 1 + facing
            at = level + distance * (2 * upward - 1)
            early = (n == 2) & (facing == 0) & place.at_end
            origin = at * 2 + side * facing + (1 - side) * (1 - facing)
            inside = (at >= 0) & (at <= top) & (distance >= 0) & ((distance > 0) | (upward == 0))

            @pl.when(inside & ~early)
            def _():
                gather.take_hand(origin, 1 - core)
                forward_tile(origin)

            return carried

        return lax.fori_loop(0, 4, candidate, carry)

    lax.fori_loop(0, levels + 1, gather_step, 0)

    plane_sum = ChainSums(place, lambda chip: sums.at[chip], rows, buffers, ring_sems[20:])

    def to_mate(goal_chip, slot):
        return remote(
            mate_out.at[slot],
            mate_in.at[goal_chip],
            mate_send.at[slot],
            mate_recv.at[goal_chip],
            place.mate,
        )

    def backward_tile(goal_chip, slot, reuse):
        start = pl.multiple_of(goal_chip * tile, tile)
        own_start = pl.multiple_of(goal_chip * tile + core * rows, rows)
        mate_start = pl.multiple_of(goal_chip * tile + (1 - core) * rows, rows)

        @pl.when(reuse)
        def _():
            to_mate(goal_chip, slot).wait_send()

        grads = gate_val_grad[pl.ds(start, tile), :]
        up_grads = up_val_grad[pl.ds(start, tile), :]
        piece = 512
        for first in range(0, width, piece):
            lanes = slice(first, first + piece)
            whole = lax.dot_general(
                grads, gate_w[lanes, :], (((1,), (1,)), ((), ())), preferred_element_type=wide
            ) + lax.dot_general(
                up_grads, up_w[lanes, :], (((1,), (1,)), ((), ())), preferred_element_type=wide
            )
            halves = whole.astype(low).reshape(2, rows, piece)
            sums[goal_chip, :, lanes] = jnp.where(core == 0, halves[0], halves[1])
            mate_out[slot, :, lanes] = jnp.where(core == 0, halves[1], halves[0])
        sums[goal_chip, :, width:] = scores[goal_chip, pl.ds(pl.multiple_of(core * rows, rows), rows)]
        mate_out[slot, :, width:] = scores[
            goal_chip, pl.ds(pl.multiple_of((1 - core) * rows, rows), rows)
        ]
        to_mate(goal_chip, slot).start()

    def joined(goal_chip, slot):
        to_mate(goal_chip, slot).wait_recv()
        sums[goal_chip] = (
            sums[goal_chip].astype(wide) + mate_in[goal_chip].astype(wide)
        ).astype(low)

    def backward_turn(turn, carry):
        goal = plane_sum.target(turn)

        @pl.when((turn == levels - 2) & place.at_end)
        def _():
            origin = place.next * 2 + 1 - side
            gather.take_hand(origin, 1 - core)
            forward_tile(origin)

        backward_tile(goal * 2 + 1 - side, 0, turn > 0)
        backward_tile(goal * 2 + side, 1, turn > 0)
        joined(goal * 2 + 1 - side, 0)
        plane_sum.send(goal)
        joined(goal * 2 + side, 1)
        return carry

    def first_turns(turn, carry):
        backward_turn(turn, carry)

        @pl.when(turn == 0)
        def _():
            gather.finish()

        return carry

    lax.fori_loop(0, levels, first_turns, 0)
    plane_sum.send_joined()

    def store(target, start, slot):
        return pltpu.make_async_copy(
            staged.at[slot], target.at[pl.ds(start, tile)], store_sem.at[slot]
        )

    def output_tile(origin, carry):
        start = pl.multiple_of(origin * tile, tile)
        slot = origin % 2

        @pl.when(origin > 1)
        def _():
            store(out_part, start, slot).wait()

        left = hidden[pl.ds(start, tile), :]
        for first in range(0, width, 512):
            lanes = slice(first, first + 512)
            staged[slot, :, lanes] = jnp.dot(
                left, down_w[:, lanes], preferred_element_type=wide
            ).astype(low)
        store(out_part, start, slot).start()
        return carry

    def down_grads(index, carry):
        start = pl.multiple_of(index * tile, tile)
        slot = index % 2
        store(down_grad_ref, start, slot).wait()
        left = hidden[:, pl.ds(start, tile)]
        for first in range(0, width, 512):
            lanes = slice(first, first + 512)
            staged[slot, :, lanes] = lax.dot_general(
                left, u_all[:, lanes], (((0,), (0,)), ((), ())), preferred_element_type=wide
            ).astype(low)
        store(down_grad_ref, start, slot).start()
        return carry

    def store_both(index):
        slot = index % 2
        start = pl.multiple_of(index * tile, tile)
        return [
            pltpu.make_async_copy(
                staged.at[slot, :, i * units : (i + 1) * units],
                target.at[pl.ds(start, tile)],
                both_sem.at[slot, i],
            )
            for i, target in enumerate((gate_grad_ref, up_grad_ref))
        ]

    def entry_weight_grads(index, carry):
        slot = index % 2

        @pl.when(index > 1)
        def _():
            for copy in store_both(index):
                copy.wait()

        left = x_all[:, :, :, pl.ds(pl.multiple_of(index * tile, tile), tile)]
        left = left.reshape(u_all.shape[0], tile)
        for i, right in enumerate((gate_val_grad, up_val_grad)):
            staged[slot, :, i * units : (i + 1) * units] = lax.dot_general(
                left, right[...], (((0,), (0,)), ((), ())), preferred_element_type=wide
            ).astype(low)
        for copy in store_both(index):
            copy.start()
        return carry

    plane_sum.take_side(plane_sum.target(0))
    lax.fori_loop(0, place.chips, output_tile, 0)
    plane_sum.take_chain(plane_sum.target(0))
    plane_sum.take_side(plane_sum.target(1))
    lax.fori_loop(0, units // tile, down_grads, 0)
    for slot in range(2):
        store(down_grad_ref, 0, slot).wait()
    plane_sum.take_chain(plane_sum.target(1))
    plane_sum.take_side(plane_sum.target(2))
    chunks = width // tile
    lax.fori_loop(0, chunks // 2, entry_weight_grads, 0)
    plane_sum.take_chain(plane_sum.target(2))
    plane_sum.take_side(plane_sum.target(3))
    lax.fori_loop(chunks // 2, chunks, entry_weight_grads, 0)
    plane_sum.take_chain(plane_sum.target(3))
    plane_sum.close()
    entry_own[...] = plane_sum.total(level)
    for slot in range(2):
        for copy in store_both(slot):
            copy.wait()
        to_mate(0, slot).wait_send()
    plane_sum.drain()

    gather.drain()


def expert_layer(x_own, upstream_all, gate_all, up_all, down_all, experts):
    rows, span = x_own.shape
    total, width = upstream_all.shape
    units = down_all.shape[0]
    chips = total // (2 * rows)
    levels = chips // 2
    low = jnp.bfloat16
    vmem = pl.BlockSpec(memory_space=pltpu.VMEM)
    anywhere = pl.BlockSpec(memory_space=pl.ANY)
    dma = pltpu.SemaphoreType.DMA
    return pl.pallas_call(
        functools.partial(expert_kernel, experts),
        name="expert_layer",
        out_shape=[
            jax.ShapeDtypeStruct((rows, span), low),
            jax.ShapeDtypeStruct((total, width), low),
            jax.ShapeDtypeStruct((width, units), low),
            jax.ShapeDtypeStruct((width, units), low),
            jax.ShapeDtypeStruct((units, width), low),
        ],
        in_specs=[vmem] + [anywhere] * 4,
        out_specs=[vmem] + [anywhere] * 4,
        scratch_shapes=[
            pltpu.VMEM((chips, 2, rows, span), low),
            pltpu.VMEM((total, width), low),
            pltpu.VMEM((width, units), low),
            pltpu.VMEM((width, units), low),
            pltpu.VMEM((units, width), low),
            pltpu.VMEM((total, units), low),
            pltpu.VMEM((total, units), low),
            pltpu.VMEM((total, units), low),
            pltpu.VMEM((chips, 2 * rows, 128), low),
            pltpu.VMEM((chips, rows, span), low),
            pltpu.VMEM((2, rows, span), low),
            pltpu.VMEM((chips, rows, span), low),
            *ChainSums.buffers(levels, (rows, span)),
            pltpu.VMEM((2, 2 * rows, width), low),
            dma((5,)),
            dma((2,)),
            dma((2, 2)),
        ]
        + [dma((2,)), dma((chips,))]
        + RowGathers.semaphores(levels)
        + ChainSums.semaphores(levels),
        compiler_params=pltpu.CompilerParams(
            collective_id=5, has_side_effects=True, vmem_limit_bytes=65_400_000
        ),
        cost_estimate=link_cost(125),
    )(x_own, upstream_all, gate_all, up_all, down_all)


def attend_back_kernel(
    experts,
    entry_ref,
    residual_ref,
    gates_ref,
    dealt_ref,
    order_ref,
    router_ref,
    attn_gain,
    moe_gain,
    query_gain,
    key_gain,
    key_low,
    value_low,
    key_pre,
    cosine_ref,
    sine_ref,
    mixed_far,
    out_far,
    probs_far,
    query_low_far,
    query_pre_far,
    query_far,
    key_far,
    value_far,
    normed_far,
    out_part,
    gate_part,
    up_part,
    down_part,
    output_ref,
    token_grad_ref,
    small_ref,
    query_own,
    key_own,
    value_own,
    out_own,
    gate_arrived,
    up_arrived,
    down_arrived,
    finished_ref,
    returned_ref,
    small_own,
    small_near,
    small_pair,
    small_parts,
    query_gain_part,
    mixed_ref,
    out_w,
    probs_ref,
    query_low,
    query_pre,
    query_w,
    key_w,
    value_w,
    normed_ref,
    residual_grad,
    low_all,
    mixed_grad,
    low_grads,
    key_total,
    value_total,
    out_grad,
    out_sums,
    out_mate,
    out_side,
    out_chain,
    out_hop,
    out_side_two,
    out_chain_two,
    out_hop_two,
    weight_side,
    weight_chain,
    weight_hop,
    narrow_grad,
    narrow_side,
    narrow_chain,
    narrow_hop,
    near,
    pair,
    far,
    quad_send,
    quad_recv,
    share_send,
    share_recv,
    swap_send,
    swap_recv,
    keep_sem,
    pair_send,
    pair_recv,
    deal_send,
    deal_recv,
    small_send,
    small_recv,
    total_send,
    total_recv,
    free_sem,
    load_sem,
    join_send,
    join_recv,
    *ring_sems,
):
    place = Place()
    core, tp, level = place.core, place.tp, place.level
    wide, low = jnp.float32, jnp.bfloat16
    own_rows, width = residual_ref.shape
    group = 2 * own_rows
    rows = 2 * group
    head = query_gain.shape[1]
    heads = mixed_grad.shape[1] // head
    members = dealt_ref.shape[0]
    half = dealt_ref.shape[1] // 2
    step_rows = 4
    scale = head ** (-0.5)

    def dealt_rows(second):
        blocks = []
        for start in range(0, members, step_rows):
            block = dealt_ref[start : start + step_rows].astype(wide)
            block = block[:, half:] if second else block[:, :half]
            blocks.append(block.reshape(step_rows * half, width))
        return jnp.concatenate(blocks, axis=0)

    greet(place.plane_targets() + [place.across])

    def to_mate(origin):
        return remote(
            out_part.at[origin, 1 - core],
            out_mate.at[origin],
            join_send.at[origin],
            join_recv.at[origin],
            place.mate,
        )

    out_buffers = (out_side, out_chain, out_hop, out_side_two, out_chain_two, out_hop_two)
    out_ring = ChainSums(
        place, lambda chip: out_sums.at[chip], own_rows, out_buffers, ring_sems[:20]
    )

    def joined_at(turn):
        goal = out_ring.target(turn)
        return (goal * 2 + 1 - place.side, goal * 2 + place.side)

    def offer(turn, carry):
        for origin in joined_at(turn):
            to_mate(origin).start()
        return carry

    keep = pltpu.make_async_copy(out_part.at[:, core], out_sums, keep_sem.at[0])
    keep.start()
    lax.fori_loop(0, place.levels, offer, 0)
    loads = [
        pltpu.make_async_copy(src, dst, load_sem.at[i])
        for i, (src, dst) in enumerate(
            (
                (mixed_far, mixed_ref),
                (out_far, out_w),
                (probs_far, probs_ref),
                (query_low_far, query_low),
                (query_pre_far, query_pre),
                (query_far, query_w),
                (key_far, key_w),
                (value_far, value_w),
                (normed_far, normed_ref),
            )
        )
    ]
    for load in loads:
        load.start()

    def join(turn, carry):
        for origin in joined_at(turn):
            to_mate(origin).wait_recv()
            out_sums[origin] = (
                out_sums[origin].astype(wide) + out_mate[origin].astype(wide)
            ).astype(low)
        out_ring.send(out_ring.target(turn))
        return carry

    keep.wait()
    join(0, 0)

    entry = entry_ref[:, :width].astype(wide)
    extra = entry_ref[:, width:].astype(wide)
    gates = gates_ref[...]
    gate_grad = extra + pltpu.roll(extra, 128 - experts, 1)
    inner = jnp.sum(gates * gate_grad, axis=-1, keepdims=True)
    logit_grad = (gates * (gate_grad - inner)).astype(low)
    residual = residual_ref[...]
    factor = lax.rsqrt(jnp.mean(residual * residual, axis=-1, keepdims=True) + epsilon)
    moe_low = (residual * factor * moe_gain[...]).astype(low)
    router = jnp.concatenate(
        [router_ref[...], jnp.zeros((128 - experts, width), low)], axis=0
    )
    moe_grad = entry + jnp.dot(logit_grad, router, preferred_element_type=wide)
    small_own[:8, :] = jnp.zeros((8, width), wide)
    small_own[8:, :] = tn_dot(logit_grad, moe_low)[: small_own.shape[0] - 8]
    scaled = moe_grad * moe_gain[...]
    inner = jnp.mean(scaled * residual, axis=-1, keepdims=True)
    small_own[1:2, :] = jnp.sum(moe_grad * residual * factor, axis=0, keepdims=True)
    residual_grad[...] = dealt_rows(True) + factor * (
        scaled - residual * (factor * factor) * inner
    )
    low_all[core, tp] = residual_grad[...].astype(low)
    mine = low_all.at[core, tp]
    share_mate = remote(mine, mine, share_send.at[0], share_recv.at[0], place.mate)
    share_across = remote(mine, mine, share_send.at[1], share_recv.at[1], place.across)
    share_across.start()
    share_mate.start()
    units = gate_arrived.shape[1]
    pair_copies = [
        remote(
            part.at[:, lanes_at(1 - tp, units)],
            arrived,
            pair_send.at[i],
            pair_recv.at[i],
            place.across,
        )
        for i, (part, arrived) in enumerate(((gate_part, gate_arrived), (up_part, up_arrived)))
    ]
    pair_copies.append(
        remote(
            down_part.at[lanes_at(1 - tp, units)],
            down_arrived,
            pair_send.at[2],
            pair_recv.at[2],
            place.across,
        )
    )
    pair_copies[0].start()

    lanes = out_own.shape[1]
    weight_ring = ChainSum(
        place,
        lambda chip: out_grad.at[:, lanes_at(chip, 2 * lanes)],
        weight_side,
        weight_chain,
        weight_hop,
        ring_sems[20:30],
    )
    query_ring = ChainSums(
        place, lambda chip: out_sums.at[chip], own_rows, out_buffers, ring_sems[30:50]
    )
    narrow_ring = ChainSum(
        place,
        lambda chip: narrow_grad.at[chip],
        narrow_side,
        narrow_chain,
        narrow_hop,
        ring_sems[50:],
    )
    lax.fori_loop(1, place.levels, join, 0)
    out_ring.send_joined()
    other = low_all.at[core, 1 - tp]
    remote(other, other, share_send.at[1], share_recv.at[1], place.across).wait_recv()
    passed = remote(other, other, share_send.at[2], share_recv.at[2], place.mate)
    passed.start()
    for slot, piece in ((0, low_all.at[1 - core, tp]), (2, low_all.at[1 - core, 1 - tp])):
        remote(piece, piece, share_send.at[slot], share_recv.at[slot], place.mate).wait_recv()

    def out_grad_rows(index, carry):
        at = lanes_at(index, 256)
        left = mixed_ref[:, at]
        for first in range(0, width, 512):
            out_grad[at, first : first + 512] = tn_dot(
                left, low_all[:, :, :, first : first + 512].reshape(rows, 512)
            ).astype(low)
        return carry

    loads[0].wait()
    lax.fori_loop(0, mixed_ref.shape[1] // 256, out_grad_rows, 0)
    for turn in range(place.levels):
        weight_ring.send(weight_ring.target(turn))

    def mixed_lanes(index, carry):
        at = lanes_at(index, 256)
        mixed_grad[:, at] = nt_dot(low_all[...].reshape(rows, width), out_w[at, :]).astype(low)
        return carry

    loads[1].wait()
    lax.fori_loop(0, mixed_ref.shape[1] // 256, mixed_lanes, 0)
    for load in loads[2:]:
        load.wait()
    key_total[...] = jnp.zeros_like(key_total)
    value_total[...] = jnp.zeros_like(value_total)
    query_gain_part[...] = jnp.zeros_like(query_gain_part)

    def pre_back(grad, values, gain_ref, cosine, sine):
        grad = grad * cosine - pltpu.roll(grad, head // 2, 1) * sine
        factor = lax.rsqrt(jnp.mean(values * values, axis=-1, keepdims=True) + epsilon)
        scaled = grad * gain_ref[...]
        inner = jnp.mean(scaled * values, axis=-1, keepdims=True)
        back = factor * (scaled - values * (factor * factor) * inner)
        return back.astype(low), jnp.sum(grad * values * factor, axis=0, keepdims=True)

    batch = 4

    def attend_back(index, carry):
        which = index // (heads // batch)
        first = (index % (heads // batch)) * batch
        at_rows = lanes_at(which, group)
        key = key_low[at_rows, :]
        value = value_low[at_rows, :]
        cosine, sine = cosine_ref[at_rows, :], sine_ref[at_rows, :]
        key_sum = key_total[at_rows, :]
        value_sum = value_total[at_rows, :]
        gain_sum = query_gain_part[...]
        for offset in range(batch):
            at = lanes_at(first + offset, head)
            probs = probs_ref[which * heads + first + offset]
            grads = mixed_grad[at_rows, at]
            prob_grad = nt_dot(grads, value)
            probs_wide = probs.astype(wide)
            inner = jnp.sum(probs_wide * prob_grad, axis=-1, keepdims=True)
            score_grad = (probs_wide * (prob_grad - inner)).astype(low)
            query = jnp.dot(score_grad, key, preferred_element_type=wide) * scale
            key_sum += tn_dot(score_grad, query_low[at_rows, at])
            value_sum += tn_dot(probs, grads)
            values = query_pre[at_rows, at].astype(wide)
            back, terms = pre_back(query, values, query_gain, cosine, sine)
            low_grads[at_rows, at] = back
            gain_sum += terms
        key_total[at_rows, :] = key_sum
        value_total[at_rows, :] = value_sum
        query_gain_part[...] = gain_sum
        return carry

    count = 2 * heads // batch
    share = -(-count // place.levels)
    for turn in range(place.levels):
        out_ring.take_side(out_ring.target(turn))
        lax.fori_loop(min(turn * share, count), min((turn + 1) * share, count), attend_back, 0)
        out_ring.take_chain(out_ring.target(turn))

    weight_ring.send_joined()
    back, terms = pre_back(
        key_total[...] * scale, key_pre[...], key_gain, cosine_ref[...], sine_ref[...]
    )
    small_own[2:3, :head] = query_gain_part[...]
    small_own[2:3, head : 2 * head] = terms
    low_grads[:, heads * head : (heads + 1) * head] = back
    low_grads[:, (heads + 1) * head :] = value_total[...].astype(low)

    def normed_grad_rows(whose):
        at_rows = lanes_at(whose, group)

        def normed_grad_lanes(index, carry):
            at = lanes_at(index, 512)
            grads = low_grads[at_rows, :]
            product = (
                nt_dot(grads[:, : heads * head], query_w[at, :])
                + nt_dot(grads[:, heads * head : (heads + 1) * head], key_w[at, :])
                + nt_dot(grads[:, (heads + 1) * head :], value_w[at, :])
            )
            low_all[whose, :, :, at] = product.astype(low).reshape(2, own_rows, 512)
            return carry

        lax.fori_loop(0, width // 512, normed_grad_lanes, 0)

    share_mate.wait_send()
    share_across.wait_send()
    passed.wait_send()
    sums = QuadSum(place, low_all, near, pair, far, quad_send, quad_recv)
    normed_grad_rows(1 - core)
    sums.start()
    normed_grad_rows(core)
    sums.relay()
    out_ring.close()
    moe_own = out_ring.total(level).astype(wide)
    out_mate[0] = (residual_ref[...] + moe_own).astype(low)
    out_ring.drain()
    for target in place.ring_targets():
        pl.semaphore_signal(
            free_sem, inc=1, device_id=target, device_id_type=pl.DeviceIdType.MESH
        )

    def weight_grad_rows(index, carry):
        left = normed_ref[:, :, :, lanes_at(index, group)].reshape(rows, group)
        for first in range(0, heads * head, 512):
            grads = tn_dot(left, low_grads[:, first : first + 512]).astype(low)
            out_sums[index, :, first : first + 512] = grads[:own_rows]
            second = heads * head + first
            out_sums[index, :, second : second + 512] = grads[own_rows:]
        narrow_grad[index] = tn_dot(left, low_grads[:, heads * head :]).astype(low)
        return carry

    weight_ring.take_side(weight_ring.target(0))
    lax.fori_loop(0, place.chips, weight_grad_rows, 0)
    weight_ring.take_chain(weight_ring.target(0))
    normed_grad = sums.total()
    tokens = dealt_rows(False)
    factor = lax.rsqrt(jnp.mean(tokens * tokens, axis=-1, keepdims=True) + epsilon)
    scaled = normed_grad * attn_gain[...]
    inner = jnp.mean(scaled * tokens, axis=-1, keepdims=True)
    small_own[0:1, :] = jnp.sum(normed_grad * tokens * factor, axis=0, keepdims=True)
    small_across = remote(
        small_own, small_near, small_send.at[0], small_recv.at[0], place.across
    )
    small_across.start()
    pair_copies[1].start()
    pair_copies[2].start()
    token_grad = residual_grad[...] + factor * (scaled - tokens * (factor * factor) * inner)
    for start in range(0, members, step_rows):
        span = slice(start * half, (start + step_rows) * half)
        both = [
            values.reshape(step_rows, half, width)
            for values in (out_mate[0, span, :].astype(wide), token_grad[span])
        ]
        finished_ref[start : start + step_rows] = jnp.concatenate(both, axis=1).astype(low)

    def deal_copy(offset, sending):
        target, index = place.member(offset if sending else -offset)
        return remote(
            finished_ref.at[index],
            returned_ref.at[place.fsdp if sending else index],
            deal_send.at[offset - 1],
            deal_recv.at[offset - 1],
            target,
        )

    share_lanes = width // members

    def small_copy(offset, sending):
        target, index = place.member(offset if sending else -offset)
        return remote(
            small_pair.at[:, lanes_at(index, share_lanes)],
            small_parts.at[place.fsdp if sending else index],
            small_send.at[offset],
            small_recv.at[offset],
            target,
        )

    def total_copy(offset, sending):
        target, index = place.member(offset if sending else -offset)
        piece = small_ref.at[:, lanes_at(place.fsdp if sending else index, share_lanes)]
        return remote(piece, piece, total_send.at[offset], total_recv.at[offset], target)

    weight_ring.take_side(weight_ring.target(1))
    small_across.wait_recv()
    small_pair[...] = small_own[...] + small_near[...]
    for offset in range(1, members):
        small_copy(offset, True).start()
    for offset in range(1, members):
        deal_copy(offset, True).start()
    own_slice = pltpu.make_async_copy(
        finished_ref.at[place.fsdp], returned_ref.at[place.fsdp], keep_sem.at[0]
    )
    own_slice.start()
    pl.semaphore_wait(free_sem, len(place.ring_targets()))
    last_rings = (query_ring, narrow_ring)
    for turn in range(place.levels):
        for ring in last_rings:
            ring.send(ring.target(turn))

    weight_ring.take_chain(weight_ring.target(1))
    for turn in range(2, place.levels):
        weight_ring.take_side(weight_ring.target(turn))
        weight_ring.take_chain(weight_ring.target(turn))
    weight_ring.close()
    for ring in last_rings:
        ring.send_joined()

    def swap_with_mate(slot, mine, theirs, here, there):
        kept = pltpu.make_async_copy(mine, here, keep_sem.at[slot])
        sent = remote(theirs, here, swap_send.at[slot], swap_recv.at[slot], place.mate)
        sent.start()
        kept.start()

        def finish():
            kept.wait()
            remote(there, there, swap_send.at[slot], swap_recv.at[slot], place.mate).wait_recv()
            sent.wait_send()

        return finish

    head_rows = out_grad.shape[0]
    finish_out = swap_with_mate(
        1,
        weight_side.at[level, :, lanes_at(core, lanes)],
        weight_side.at[level, :, lanes_at(1 - core, lanes)],
        out_own.at[lanes_at(core, head_rows)],
        out_own.at[lanes_at(1 - core, head_rows)],
    )
    for offset in range(1, members):
        small_copy(offset, False).wait_recv()
    small_parts[place.fsdp] = small_pair[:, lanes_at(place.fsdp, share_lanes)]
    total = small_parts[0]
    for member in range(1, members):
        total += small_parts[member]
    small_ref[:, lanes_at(place.fsdp, share_lanes)] = total
    for offset in range(1, members):
        total_copy(offset, True).start()
    for turn in range(place.levels):
        for ring in last_rings:
            ring.take_side(ring.target(turn))
            ring.take_chain(ring.target(turn))
    own_slice.wait()
    for offset in range(1, members):
        deal_copy(offset, False).wait_recv()
    for index in range(members):
        block = returned_ref[lax.rem(order_ref[index] + place.fsdp, members)].astype(wide)
        token_grad_ref[index] = block[half:]
        output_ref[index] = block[:half].astype(low)
    for ring in last_rings:
        ring.close()
    span = heads * head
    cut = own_rows // query_ring.count
    finish_query = [
        swap_with_mate(
            slot,
            ring.side_buf.at[level, :, lanes_at(core, span)],
            ring.side_buf.at[level, :, lanes_at(1 - core, span)],
            query_own.at[pl.ds(i * cut, cut), lanes_at(core, span)],
            query_own.at[pl.ds(i * cut, cut), lanes_at(1 - core, span)],
        )
        for i, (slot, ring) in enumerate(zip((2, 5), query_ring.rings))
    ]
    finish_narrow = [
        swap_with_mate(
            3 + i,
            narrow_side.at[level, lanes_at(core, own_rows), pl.ds(i * head, head)],
            narrow_side.at[level, lanes_at(1 - core, own_rows), pl.ds(i * head, head)],
            own.at[:, lanes_at(core, head)],
            own.at[:, lanes_at(1 - core, head)],
        )
        for i, own in enumerate((key_own, value_own))
    ]
    finish_out()
    for finish in finish_query + finish_narrow:
        finish()
    small_across.wait_send()
    for offset in range(1, members):
        deal_copy(offset, True).wait_send()
        small_copy(offset, True).wait_send()
        total_copy(offset, True).wait_send()
        total_copy(offset, False).wait_recv()
    for copy in pair_copies:
        copy.wait()

    def offered(origin, carry):
        to_mate(origin).wait_send()
        return carry

    lax.fori_loop(0, place.chips, offered, 0)
    sums.drain()
    for ring in (weight_ring, query_ring, narrow_ring):
        ring.drain()


def attend_back_layer(
    experts,
    entry,
    residual,
    gates,
    dealt,
    deal_order,
    router,
    gain_vecs,
    mixed,
    probs,
    query_low,
    key_low,
    value_low,
    query_pre,
    key_pre,
    tables,
    normed,
    query_w,
    key_w,
    value_w,
    out_w,
    out_part,
    gate_part,
    up_part,
    down_part,
):
    own_rows, width = residual.shape
    members = dealt.shape[0]
    levels = members // 4
    rows = 4 * own_rows
    heads_width, head = query_w.shape[1], key_w.shape[1]
    lanes = width // members
    wide, low = jnp.float32, jnp.bfloat16
    vmem = pl.BlockSpec(memory_space=pltpu.VMEM)
    anywhere = pl.BlockSpec(memory_space=pl.ANY)
    shape = jax.ShapeDtypeStruct
    dma = pltpu.SemaphoreType.DMA
    small = (8 + -(-experts // 8) * 8, width)
    late = (mixed, out_w, probs, query_low, query_pre, query_w, key_w, value_w, normed)
    return pl.pallas_call(
        functools.partial(attend_back_kernel, experts),
        name="attend_back_layer",
        out_shape=[
            shape((members, dealt.shape[1] // 2, width), low),
            shape((members, dealt.shape[1] // 2, width), wide),
            shape(small, wide),
            shape((own_rows, 2 * heads_width), low),
            shape((own_rows, 2 * head), low),
            shape((own_rows, 2 * head), low),
            shape((2 * heads_width, lanes), low),
            shape((width, gate_part.shape[1] // 2), low),
            shape((width, up_part.shape[1] // 2), low),
            shape((down_part.shape[0] // 2, width), low),
        ],
        in_specs=[vmem] * 4
        + [pl.BlockSpec(memory_space=pltpu.SMEM)]
        + [vmem] * 10
        + [anywhere] * 13,
        out_specs=[vmem] * 7 + [anywhere] * 3,
        scratch_shapes=[
            pltpu.VMEM(dealt.shape, low),
            pltpu.VMEM(dealt.shape, low),
            pltpu.VMEM(small, wide),
            pltpu.VMEM(small, wide),
            pltpu.VMEM(small, wide),
            pltpu.VMEM((members, small[0], width // members), wide),
            pltpu.VMEM((1, head), wide),
        ]
        + [pltpu.VMEM(array.shape, low) for array in late]
        + [
            pltpu.VMEM((own_rows, width), wide),
            pltpu.VMEM((2, 2, own_rows, width), low),
            pltpu.VMEM((rows, heads_width), low),
            pltpu.VMEM((rows, heads_width + 2 * head), low),
            pltpu.VMEM((rows, head), wide),
            pltpu.VMEM((rows, head), wide),
            pltpu.VMEM((heads_width, width), low),
            pltpu.VMEM((members // 2, own_rows, width), low),
            pltpu.VMEM((members // 2, own_rows, width), low),
            *ChainSums.buffers(levels, (own_rows, width)),
            *ChainSum.buffers(levels, (heads_width, 2 * lanes)),
            pltpu.VMEM((members // 2, 2 * own_rows, 2 * head), low),
            *ChainSum.buffers(levels, (2 * own_rows, 2 * head)),
        ]
        + QuadSum.scratch(own_rows, width)
        + [dma((3,)), dma((3,)), dma((6,)), dma((6,)), dma((6,)), dma((3,)), dma((3,))]
        + [dma((members,))] * 6
        + [pltpu.SemaphoreType.REGULAR, dma((9,)), dma((members // 2,)), dma((members // 2,))]
        + ChainSum.semaphores(levels) * 6,
        compiler_params=pltpu.CompilerParams(
            collective_id=3, has_side_effects=True, vmem_limit_bytes=65_400_000
        ),
        cost_estimate=link_cost(185),
    )(
        entry,
        residual,
        gates,
        dealt,
        deal_order,
        router,
        *gain_vecs,
        key_low,
        value_low,
        key_pre,
        *tables,
        *late,
        out_part,
        gate_part,
        up_part,
        down_part,
    )


def fast_body(
    tokens,
    lengths,
    routes,
    deal_order,
    cotangent,
    attn_gain,
    query_gain,
    key_gain,
    moe_gain,
    w_query,
    key_projection_matrix,
    value_projection_matrix,
    w_out,
    w_router,
    w_gate,
    w_up,
    w_down,
):
    own_rows, model_width = tokens.shape
    head_dim = query_gain.shape[0]
    chip_count = lax.axis_size("chip")
    core_count = lax.axis_size("core")
    tp_count = lax.axis_size("tp")
    core_index = lax.axis_index("core")
    tp_index = lax.axis_index("tp")
    fsdp_count = chip_count * core_count
    fsdp_index = lax.axis_index("chip") * core_count + core_index
    slice_rows = own_rows // fsdp_count
    group_rows = tp_count * own_rows
    quad_rows = core_count * group_rows
    plane = ("chip", "core")
    quad = ("core", "tp")

    def slices_of(values):
        return values.reshape(fsdp_count, slice_rows, model_width)

    down_full = lax.all_gather(w_down[0], "tp", axis=0, tiled=True)
    frequency = rope_base ** (-(jnp.arange(head_dim // 2, dtype=jnp.float32) * (2.0 / head_dim)))
    frequency = jnp.concatenate([frequency, frequency])[None, :]
    padded_lengths = jnp.pad(lengths, ((0, 7), (0, 128 - lengths.shape[1])))
    experts = w_router.shape[1]
    router_rows = w_router.T
    (
        dealt,
        normed,
        cosine_wide,
        sine_wide,
        moe_ext,
        residual,
        gates,
        query_pre,
        query_low,
        key_before_norm,
        key_low,
        value_low,
        probs_low,
        mixed_low,
        upstream_all,
        query_part,
        key_part,
        value_part,
        out_part,
        gate_full,
        up_full,
    ) = front_layer(
        experts,
        lengths.shape[1],
        slices_of(tokens),
        slices_of(cotangent),
        deal_order,
        attn_gain[None, :],
        padded_lengths,
        frequency,
        (query_gain[None, :], key_gain[None, :], moe_gain[None, :]),
        router_rows,
        routes.T,
        w_query,
        key_projection_matrix,
        value_projection_matrix,
        w_out,
        w_gate[0],
        w_up[0],
    )
    query_part = query_part.reshape(model_width, -1)
    key_part = key_part.reshape(model_width, -1)
    value_part = value_part.reshape(model_width, -1)
    upstream_all = upstream_all.reshape(fsdp_count * own_rows, model_width)
    entry_ext, moe_out, grad_w_gate, grad_w_up, grad_w_down = expert_layer(
        moe_ext, upstream_all, gate_full, up_full, down_full, experts
    )
    (
        output,
        grad_input,
        small,
        grad_w_query,
        grad_w_key,
        grad_w_value,
        grad_w_out,
        gate_arrived,
        up_arrived,
        down_arrived,
    ) = attend_back_layer(
        experts,
        entry_ext,
        residual,
        gates,
        dealt,
        deal_order,
        router_rows,
        (attn_gain[None, :], moe_gain[None, :], query_gain[None, :], key_gain[None, :]),
        mixed_low,
        probs_low,
        query_low,
        key_low,
        value_low,
        query_pre,
        key_before_norm,
        (cosine_wide, sine_wide),
        normed,
        query_part,
        key_part,
        value_part,
        out_part,
        moe_out.reshape(chip_count, core_count, own_rows, model_width),
        grad_w_gate,
        grad_w_up,
        grad_w_down,
    )
    def pair_sum(parts, arrived, dim):
        first, second = jnp.split(parts, 2, axis=dim)
        mine = jnp.where(tp_index == 0, first, second)
        return mine.astype(jnp.float32) + arrived.astype(jnp.float32)

    output = output.reshape(own_rows, model_width)
    grad_input = grad_input.reshape(own_rows, model_width)
    grad_w_router = small[8 : 8 + experts].T
    return (
        output,
        grad_input,
        small[0],
        small[2, :head_dim],
        small[2, head_dim : 2 * head_dim],
        small[1],
        grad_w_query.astype(jnp.float32),
        grad_w_key.astype(jnp.float32),
        grad_w_value.astype(jnp.float32),
        grad_w_out.astype(jnp.float32),
        grad_w_router,
        pair_sum(grad_w_gate, gate_arrived, 1)[None],
        pair_sum(grad_w_up, up_arrived, 1)[None],
        pair_sum(grad_w_down, down_arrived, 0)[None],
    )


def solution(mesh):
    fsdp_count, tp_count = mesh.shape["fsdp"], mesh.shape["tp"]
    chips = Mesh(mesh.devices.reshape(fsdp_count // 2, 2, tp_count), ("chip", "core", "tp"))
    dense = fsdp_count <= 16
    fsdp = ("chip", "core") if dense else "fsdp"
    every = ("chip", "core", "tp") if dense else ("fsdp", "tp")
    return jax.shard_map(
        fast_body if dense else body,
        mesh=chips if dense else mesh,
        in_specs=(
            P(every, None),
            P(fsdp, None),
            P(fsdp, None),
            P(),
            P(every, None),
            P(),
            P(),
            P(),
            P(),
            P(fsdp, "tp"),
            P(fsdp, "tp"),
            P(fsdp, "tp"),
            P("tp", fsdp),
            P(),
            P(fsdp, None, "tp"),
            P(fsdp, None, "tp"),
            P(fsdp, "tp", None),
        ),
        out_specs=(
            P(every, None),
            P(every, None),
            P(),
            P(),
            P(),
            P(),
            P(fsdp, "tp"),
            P(fsdp, "tp"),
            P(fsdp, "tp"),
            P("tp", fsdp),
            P(),
            P(fsdp, None, "tp"),
            P(fsdp, None, "tp"),
            P(fsdp, "tp", None),
        ),
        check_vma=False,
    )
```
